32 devices in a mesh: blk: 8 (over z, y), rep: 4 (over x, core).
Axes of the slice: x: 2, y: 2, z: 4, core: 2. Of those that a mesh axis runs over, the one named last changes fastest.
Arguments:
- patches: bfloat16 [4, 4096, 768], P('rep', 'blk'), may hold values from -6 to 6
- queries: bfloat16 [4, 800, 768], P('rep'), may hold values from -6 to 6
- window_valid: int32 [4, 64], P('rep', 'blk'), may hold values from 0 to 1, as said below
- answer_length: int32 [4], P('rep'), may hold values from 200 to 800
- norm_gain: float32 [6, 768], replicated, may hold values from 0.5 to 1.5
- norm_bias: float32 [6, 768], replicated, may hold values from -1.5 to 1.5
- attn_in: bfloat16 [4, 768, 2304], replicated, may hold values from -0.21875 to 0.21875
- attn_out: bfloat16 [4, 768, 768], replicated, may hold values from -0.625 to 0.625
- mlp_in: bfloat16 [2, 768, 3072], replicated, may hold values from -0.21875 to 0.21875
- mlp_out: bfloat16 [2, 3072, 768], replicated, may hold values from -0.109375 to 0.109375
- cot_patches: bfloat16 [4, 4096, 768], P('rep', 'blk'), may hold values from -6 to 6
- cot_queries: bfloat16 [4, 800, 768], P('rep'), may hold values from -6 to 6
Outputs:
- out_patches: bfloat16 [4, 4096, 768], P('rep', 'blk')
- out_queries: bfloat16 [4, 800, 768], P('rep', None, 'blk')
- grad_patches: float32 [4, 4096, 768], P('rep', 'blk')
- grad_queries: float32 [4, 800, 768], P('rep', None, 'blk')
- grad_norm_gain: float32 [6, 768], P(None, 'blk')
- grad_norm_bias: float32 [6, 768], P(None, 'blk')
- grad_attn_in: float32 [4, 768, 2304], P(None, 'blk')
- grad_attn_out: float32 [4, 768, 768], P(None, 'blk')
- grad_mlp_in: float32 [2, 768, 3072], P(None, 'blk')
- grad_mlp_out: float32 [2, 3072, 768], P(None, 'blk')
The draws below stay inside these ranges and needn't reach their ends.
Inputs may be any that keep to these rules, and one draw needn't show every extreme that they name: `window_valid`: in every aligned block of 8 windows at least one window is valid.
All inputs are finite; a program needn't handle non-finite values.
Results may differ from the reference program's by a relative error of at most 0.015.
Values may be sent and summed in bfloat16 or wider, within the bound.
A program may use at most 576 MiB of HBM per device.

```python
import math
import jax
import jax.numpy as jnp
from jax import lax

D = 768
HEADS = 12
HEAD_DIM = 64
FF = 3072
WIN = 64
QLEN = 800
PATCH_DEV = 512
WIN_DEV = 8
PATCHES = 4096
WINDOWS = 64
IMAGES = 4
N_BLK = 8


def draw_window_valid(key, part):
    key = jax.random.fold_in(key, 7)
    portion_key, toss_key, chosen_key = jax.random.split(key, 3)
    portion = jax.random.randint(portion_key, (IMAGES, 1), 3, 10)
    tosses = jax.random.randint(toss_key, (IMAGES, WINDOWS), 0, 10) < portion
    blocks = WINDOWS // WIN_DEV
    chosen = jax.random.randint(chosen_key, (IMAGES, blocks, 1), 0, WIN_DEV)
    marked = jnp.arange(WIN_DEV, dtype=jnp.int32)[None, None, :] == chosen
    return jnp.logical_or(tosses, marked.reshape(IMAGES, WINDOWS)).astype(jnp.int32)


def with_ends(values, key, least, high):
    index_at = [jax.random.randint(jax.random.fold_in(key, axis), (), 0, length) for axis, length in enumerate(values.shape)]
    longest = values.shape.index(max(values.shape))
    neighbour = index_at[:longest] + [(index_at[longest] + 1) % values.shape[longest]] + index_at[longest + 1:]
    return values.at[tuple(index_at)].set(least).at[tuple(neighbour)].set(high)


def block_scale(key, dims, cuts, low, top_value):
    def one(position, parts):
        heights = jax.random.uniform(jax.random.fold_in(jax.random.fold_in(key, 6), position), (parts,), jnp.float32, low / len(cuts), top_value / len(cuts))
        return jnp.repeat(jnp.exp(heights), dims[position] // parts).reshape((-1,) + (1,) * (len(dims) - position - 1))

    factor_of = one(*cuts[0])
    for cut in cuts[1:]:
        factor_of = factor_of * one(*cut)
    return factor_of


def noise(stream_key, extent, width, reach, pieces=(), kind=jnp.bfloat16):
    gain = block_scale(stream_key, extent, pieces, -0.22, 0.18) if pieces else 1.0
    entries = jax.random.normal(stream_key, extent, jnp.float32) * width * gain
    return jnp.minimum(jnp.maximum(entries, -reach), reach).astype(kind)


def setup_inputs(seed: int = 0) -> dict:
    arg_keys = jax.random.split(jax.random.key(seed), 13)
    return {
        "patches": noise(arg_keys[0], (IMAGES, PATCHES, D), 1.0, 6.0, ((0, 4), (1, 8))),
        "queries": noise(arg_keys[1], (IMAGES, QLEN, D), 1.0, 6.0, ((0, 4),)),
        "window_valid": draw_window_valid(jax.random.fold_in(arg_keys[12], 71), 0),
        "answer_length": with_ends(jax.random.randint(arg_keys[3], (IMAGES,), QLEN // 4, QLEN + 1), jax.random.fold_in(arg_keys[3], 1), QLEN // 4, QLEN).astype(jnp.int32),
        "norm_gain": jnp.clip(1.0 + 0.1 * jax.random.normal(arg_keys[4], (6, D), jnp.float32), 0.5, 1.5),
        "norm_bias": noise(arg_keys[5], (6, D), 0.3, 1.5, (), jnp.float32),
        "attn_in": noise(arg_keys[6], (4, D, 3 * D), D ** -0.5, 0.21875),
        "attn_out": noise(arg_keys[7], (4, D, D), (D // 8) ** -0.5, 0.625),
        "mlp_in": noise(arg_keys[8], (2, D, FF), D ** -0.5, 0.21875),
        "mlp_out": noise(arg_keys[9], (2, FF, D), FF ** -0.5, 0.109375),
        "cot_patches": noise(arg_keys[10], (IMAGES, PATCHES, D), 1.0, 6.0, ((0, 4), (1, 8))),
        "cot_queries": noise(arg_keys[11], (IMAGES, QLEN, D), 1.0, 6.0, ((0, 4),)),
    }


EPSILON = 1e-05
MASKED = -1e+30
HIGHEST = lax.Precision.HIGHEST

@jax.custom_vjp
def low(v):
    return lax.optimization_barrier(v.astype(jnp.bfloat16)).astype(jnp.float32)

@jax.custom_vjp
def low_back(v):
    return v

def low_keep(v):
    return (low(v), None)

def low_pass(kept, grad):
    return (grad,)

def back_keep(v):
    return (v, None)

def back_low(kept, grad):
    return (low(grad),)
low.defvjp(low_keep, low_pass)
low_back.defvjp(back_keep, back_low)

def round_both(tensor):
    return low_back(low(tensor))

def matmul(former, latter):
    return jnp.dot(former, latter, precision=HIGHEST)

def layer_norm(tensor, scales, shifts):
    average = lax.optimization_barrier(jnp.mean(tensor, axis=-1, keepdims=True))
    centred = tensor - average
    spread = lax.optimization_barrier(jnp.mean(centred * centred, axis=-1, keepdims=True))
    return centred * lax.rsqrt(spread + EPSILON) * scales + shifts

def split_heads(tensor):
    return tensor.reshape(tensor.shape[:-1] + (HEADS, HEAD_DIM))

def attention(queries_h, keys_h, values_h, allowed):
    scaling = 1.0 / math.sqrt(HEAD_DIM)
    scores = low_back(jnp.einsum('brhe,bkhe->bhrk', queries_h, keys_h, precision=HIGHEST) * scaling)
    scores = jnp.where(allowed, scores, MASKED)
    probabilities = low(jax.nn.softmax(scores, axis=-1))
    attended = jnp.einsum('bhrk,bkhe->brhe', probabilities, values_h, precision=HIGHEST)
    return attended.reshape(attended.shape[:2] + (D,))

def window_branch(normed, w_in, w_out):
    project = round_both(matmul(normed, w_in)).reshape(-1, WIN, 3 * D)
    attended = attention(split_heads(project[..., :D]), split_heads(project[..., D:2 * D]), split_heads(project[..., 2 * D:]), True)
    return low_back(matmul(round_both(attended.reshape(-1, D)), w_out))

def query_branch(normed, w_in, w_out):
    project = round_both(matmul(normed, w_in))[None]
    places = jnp.arange(QLEN, dtype=jnp.int32)
    allowed = (places[None, :] <= places[:, None])[None, None]
    attended = attention(split_heads(project[..., :D]), split_heads(project[..., D:2 * D]), split_heads(project[..., 2 * D:]), allowed)[0]
    return low_back(matmul(round_both(attended), w_out))

def patch_cross_branch(normed_patches, normed_queries, length, w_in, w_out):
    patch_side = round_both(matmul(normed_patches, w_in[:, :D]))
    query_side = round_both(matmul(normed_queries, w_in[:, D:]))
    allowed = (jnp.arange(QLEN, dtype=jnp.int32) < length)[None, None, None, :]
    attended = attention(split_heads(patch_side)[None], split_heads(query_side[:, :D])[None], split_heads(query_side[:, D:])[None], allowed)[0]
    return low_back(matmul(round_both(attended), w_out))

def query_cross_branch(normed_queries, normed_patches, patch_valid, w_in, w_out):
    scaling = 1.0 / math.sqrt(HEAD_DIM)
    query_heads = split_heads(round_both(matmul(normed_queries, w_in[:, :D])))
    key_values = round_both(matmul(normed_patches, w_in[:, D:]))
    key_blocks = split_heads(key_values[:, :D]).reshape(N_BLK, PATCH_DEV, HEADS, HEAD_DIM)
    value_blocks = split_heads(key_values[:, D:]).reshape(N_BLK, PATCH_DEV, HEADS, HEAD_DIM)
    flag_blocks = patch_valid.reshape(N_BLK, PATCH_DEV)

    def one_block(entry):
        key_rows, value_rows, flag_rows = entry
        scores = low_back(jnp.einsum('qhe,khe->hqk', query_heads, key_rows, precision=HIGHEST) * scaling)
        scores = jnp.where(flag_rows[None, None, :] > 0, scores, MASKED)
        peaks = lax.optimization_barrier(jnp.max(scores, axis=-1))
        weights = jnp.exp(scores - peaks[..., None])
        sums = lax.optimization_barrier(jnp.sum(weights, axis=-1))
        partial_out = low_back(jnp.einsum('hqk,khe->hqe', low(weights), value_rows, precision=HIGHEST))
        return (peaks, sums, partial_out)
    peaks, sums, partial_out = lax.map(jax.checkpoint(one_block), (key_blocks, value_blocks, flag_blocks))
    highest = lax.optimization_barrier(jnp.max(peaks, axis=0))
    factors = jnp.exp(peaks - highest)
    denominator = lax.optimization_barrier(jnp.sum(factors * sums, axis=0))
    combined = lax.optimization_barrier(jnp.sum(factors[..., None] * partial_out, axis=0)) / denominator[..., None]
    attended = round_both(jnp.transpose(combined, (1, 0, 2)).reshape(QLEN, D))
    return low_back(matmul(attended, w_out))

def gelu_exact(tensor):
    return jax.nn.gelu(tensor, approximate=False)

def feed_forward(normed, w_up, w_down):
    preact = low_back(matmul(normed, w_up))
    hidden = low(gelu_exact(preact))
    return low_back(matmul(hidden, w_down))

def one_image(patch_rows, query_rows, patch_valid, length, gains, biases, a_in, a_out, m_in, m_out):
    patch_one = patch_rows + window_branch(low(layer_norm(patch_rows, gains[0], biases[0])), a_in[0], a_out[0])
    query_one = query_rows + query_branch(low(layer_norm(query_rows, gains[1], biases[1])), a_in[1], a_out[1])
    normed_q = low(layer_norm(query_one, gains[2], biases[2]))
    normed_x = low(layer_norm(patch_one, gains[3], biases[3]))
    query_two = query_one + query_cross_branch(normed_q, normed_x, patch_valid, a_in[2], a_out[2])
    patch_two = patch_one + patch_cross_branch(normed_x, normed_q, length, a_in[3], a_out[3])
    query_three = query_two + feed_forward(low(layer_norm(query_two, gains[4], biases[4])), m_in[1], m_out[1])
    patch_three = patch_two + feed_forward(low(layer_norm(patch_two, gains[5], biases[5])), m_in[0], m_out[0])
    return (patch_three, query_three)

def reference(patches, queries, window_valid, answer_length, norm_gain, norm_bias, attn_in, attn_out, mlp_in, mlp_out, cot_patches, cot_queries):
    patch_valid = jnp.repeat(window_valid, WIN, axis=1).astype(jnp.float32)

    def forward(patch_all, query_all, gains, biases, a_in, a_out, m_in, m_out):

        def run(entry):
            return one_image(entry[0], entry[1], entry[2], entry[3], gains, biases, a_in, a_out, m_in, m_out)
        return lax.map(jax.checkpoint(run), (patch_all, query_all, patch_valid, answer_length))
    primals = (patches.astype(jnp.float32), queries.astype(jnp.float32), norm_gain, norm_bias, attn_in.astype(jnp.float32), attn_out.astype(jnp.float32), mlp_in.astype(jnp.float32), mlp_out.astype(jnp.float32))
    outputs, pullback = jax.vjp(forward, *primals)
    grads = pullback((cot_patches.astype(jnp.float32), cot_queries.astype(jnp.float32)))
    return (outputs[0].astype(jnp.bfloat16), outputs[1].astype(jnp.bfloat16), grads[0], grads[1], grads[2], grads[3], grads[4], grads[5], grads[6], grads[7])
```

```python
import math

import jax
import jax.numpy as jnp
from jax import lax
from jax.sharding import PartitionSpec as P

HEADS = 12
WIN = 64


EPSILON = 1e-05
MASKED = -1e30
NARROW = jnp.bfloat16
SINGLE = jnp.float32


def bits_of(count):
    return max(count - 1, 0).bit_length()


def swap(tensor, axis, bit):
    count = lax.axis_size(axis)
    return lax.ppermute(tensor, axis, [(i, i ^ (1 << bit)) for i in range(count)])


def pick(tensor, place, dim):
    return lax.dynamic_index_in_dim(tensor, place, dim, keepdims=False)


def fold(tensor, axis, bit, dim):
    own = (lax.axis_index(axis) >> bit) & 1
    arrived = swap(pick(tensor, 1 - own, dim).astype(NARROW), axis, bit)
    return pick(tensor, own, dim).astype(SINGLE) + arrived.astype(SINGLE)


def unfold(tensor, axis, bit, dim):
    own = (lax.axis_index(axis) >> bit) & 1
    arrived = swap(tensor, axis, bit)
    return jnp.where(
        own == 0,
        jnp.stack((tensor, arrived), axis=dim),
        jnp.stack((arrived, tensor), axis=dim),
    )


def scatter_blk(tensor):
    bits = bits_of(lax.axis_size("blk"))
    tensor = tensor.reshape((2,) * bits + tensor.shape[1:])
    for bit in range(bits):
        tensor = fold(tensor, "blk", bit, bits - 1 - bit)
    return tensor


def gather_blk(tensor):
    bits = bits_of(lax.axis_size("blk"))
    tail = tensor.shape
    for bit in reversed(range(bits)):
        tensor = unfold(tensor, "blk", bit, 0)
    order = tuple(reversed(range(bits))) + tuple(range(bits, bits + len(tail)))
    return jnp.transpose(tensor, order).reshape((2**bits,) + tail)


def sum_rep_scatter(tensor, dim):
    bits = bits_of(lax.axis_size("rep"))
    shape = tensor.shape
    tensor = tensor.reshape(
        shape[:dim] + (2,) * bits + (shape[dim] // 2**bits,) + shape[dim + 1 :]
    )
    for bit in range(bits):
        tensor = fold(tensor, "rep", bit, dim)
    return tensor


def gather_rep(tensor, dim):
    bits = bits_of(lax.axis_size("rep"))
    for bit in reversed(range(bits)):
        tensor = unfold(tensor, "rep", bit, dim)
    shape = tensor.shape
    return tensor.reshape(shape[:dim] + (-1,) + shape[dim + bits + 1 :])


def reduce_all(tensor):
    count = lax.axis_size("blk")
    tensor = tensor.reshape(count, tensor.shape[0] // count, tensor.shape[1])
    tensor = sum_rep_scatter(tensor, 1)
    tensor = scatter_blk(tensor).astype(NARROW)
    return gather_rep(tensor, 0)


def reduce_rep(tensor):
    return gather_rep(sum_rep_scatter(tensor, 0).astype(NARROW), 0)


def layer_norm(tensor, scales, shifts):
    average = jnp.mean(tensor, axis=-1, keepdims=True)
    centred = tensor - average
    spread = jnp.mean(centred * centred, axis=-1, keepdims=True)
    return centred * lax.rsqrt(spread + EPSILON) * scales + shifts


def norm_back(tensor, scales, shifts, upstream):
    unused, pullback = jax.vjp(layer_norm, tensor, scales, shifts)
    return pullback(upstream)


def gelu_exact(tensor):
    return jax.nn.gelu(tensor, approximate=False)


def matmul(former, latter):
    return jnp.dot(former, latter, preferred_element_type=SINGLE)


def weight_grad(inputs, upstream):
    return lax.dot_general(
        inputs, upstream, (((0,), (0,)), ((), ())), preferred_element_type=SINGLE
    )


def input_grad(upstream, weight):
    return lax.dot_general(
        upstream, weight, (((1,), (1,)), ((), ())), preferred_element_type=SINGLE
    )


def split_heads(tensor, head_count):
    return tensor.reshape(tensor.shape[:-1] + (head_count, tensor.shape[-1] // head_count))


def masked_scores(queries_h, keys_h, allowed, scaling):
    products = (
        jnp.einsum("brhe,bkhe->bhrk", queries_h, keys_h, preferred_element_type=SINGLE) * scaling
    )
    return jnp.where(allowed, products, MASKED)


def attend_forward(queries_h, keys_h, values_h, allowed, scaling):
    scores = masked_scores(queries_h, keys_h, allowed, scaling)
    probabilities = jax.nn.softmax(scores, axis=-1)
    attended = jnp.einsum(
        "bhrk,bkhe->brhe", probabilities.astype(NARROW), values_h, preferred_element_type=SINGLE
    )
    return (attended, jax.nn.logsumexp(scores, axis=-1))


def attend_backward(queries_h, keys_h, values_h, allowed, scaling, logsum, upstream):
    probabilities = jnp.exp(masked_scores(queries_h, keys_h, allowed, scaling) - logsum[..., None])
    grad_probs = jnp.einsum("brhe,bkhe->bhrk", upstream, values_h, preferred_element_type=SINGLE)
    grad_scores = probabilities * (
        grad_probs - jnp.sum(grad_probs * probabilities, axis=-1, keepdims=True)
    )
    rounded = grad_scores.astype(NARROW)
    grad_queries = (
        jnp.einsum("bhrk,bkhe->brhe", rounded, keys_h, preferred_element_type=SINGLE) * scaling
    )
    grad_keys = (
        jnp.einsum("bhrk,brhe->bkhe", rounded, queries_h, preferred_element_type=SINGLE) * scaling
    )
    grad_values = jnp.einsum(
        "bhrk,brhe->bkhe", probabilities.astype(NARROW), upstream, preferred_element_type=SINGLE
    )
    return (grad_queries, grad_keys, grad_values)


def branch_forward(normed, w_in, w_out, head_count, groups, allowed, scaling):
    row_count, features = normed.shape
    project = matmul(normed, w_in).astype(NARROW)
    columns = project.reshape(groups, row_count // groups, 3, head_count, features // head_count)
    attended, logsum = attend_forward(
        columns[:, :, 0], columns[:, :, 1], columns[:, :, 2], allowed, scaling
    )
    attended = attended.reshape(row_count, features).astype(NARROW)
    return (matmul(attended, w_out), (project, attended, logsum))


def branch_backward(normed, w_in, w_out, head_count, groups, allowed, scaling, stored, upstream):
    project, attended, logsum = stored
    row_count, features = normed.shape
    grad_out_weight = weight_grad(attended, upstream)
    grad_attended = (
        input_grad(upstream, w_out)
        .astype(NARROW)
        .reshape(groups, row_count // groups, head_count, features // head_count)
    )
    columns = project.reshape(groups, row_count // groups, 3, head_count, features // head_count)
    grads = attend_backward(
        columns[:, :, 0],
        columns[:, :, 1],
        columns[:, :, 2],
        allowed,
        scaling,
        logsum,
        grad_attended,
    )
    grad_project = jnp.stack(grads, axis=2).reshape(row_count, 3 * features).astype(NARROW)
    return (input_grad(grad_project, w_in), weight_grad(normed, grad_project), grad_out_weight)


def mlp_forward(normed, w_up, w_down):
    preact = matmul(normed, w_up)
    hidden = gelu_exact(preact).astype(NARROW)
    return (matmul(hidden, w_down), (preact, hidden))


def mlp_backward(normed, w_up, w_down, stored, upstream):
    preact, hidden = stored
    grad_down = weight_grad(hidden, upstream)
    unused, pullback = jax.vjp(gelu_exact, preact)
    grad_preact = pullback(input_grad(upstream, w_down))[0].astype(NARROW)
    return (input_grad(grad_preact, w_up), weight_grad(normed, grad_preact), grad_down)


def block_stats(query_heads, key_rows, value_rows, flag_rows, scaling):
    head_count = query_heads.shape[1]
    scores = (
        jnp.einsum(
            "qhe,khe->hqk",
            query_heads,
            split_heads(key_rows, head_count),
            preferred_element_type=SINGLE,
        )
        * scaling
    )
    scores = jnp.where(flag_rows[None, None, :] > 0, scores, MASKED)
    peak = jnp.max(scores, axis=-1)
    weights = jnp.exp(scores - peak[..., None])
    accumulated = jnp.einsum(
        "hqk,khe->hqe",
        weights.astype(NARROW),
        split_heads(value_rows, head_count),
        preferred_element_type=SINGLE,
    )
    return (peak, jnp.sum(weights, axis=-1), accumulated)


def body(
    patches,
    queries,
    window_valid,
    answer_length,
    norm_gain,
    norm_bias,
    attn_in,
    attn_out,
    mlp_in,
    mlp_out,
    cot_patches,
    cot_queries,
):
    features = patches.shape[2]
    head_count = HEADS
    head_size = features // head_count
    scaling = 1.0 / math.sqrt(head_size)
    blocks = lax.axis_size("blk")
    place = lax.axis_index("blk")
    share = features // blocks
    hidden = mlp_in.shape[2]
    patch_rows = patches[0].astype(SINGLE)
    query_rows = queries[0].astype(SINGLE)
    patch_count = patch_rows.shape[0]
    query_count = query_rows.shape[0]
    part = -(-query_count // (blocks * 8)) * 8
    padded = part * blocks
    length = answer_length[0]
    flag_rows = jnp.repeat(window_valid[0], WIN).astype(NARROW)
    positions = jnp.arange(query_count, dtype=jnp.int32)
    causal = (positions[None, :] <= positions[:, None])[None, None]
    reaching = (positions < length)[None, None, None, :]
    leader = (place == 0).astype(SINGLE)

    def own_columns(tensor, width=share):
        return lax.dynamic_slice_in_dim(tensor, place * width, width, 1)

    def pad_rows(tensor):
        return jnp.pad(tensor, ((0, padded - query_count), (0, 0)))

    def own_rows(tensor):
        return lax.dynamic_slice_in_dim(pad_rows(tensor), place * part, part, 0)

    normed_zero = layer_norm(patch_rows, norm_gain[0], norm_bias[0]).astype(NARROW)
    window_out, window_kept = branch_forward(
        normed_zero, attn_in[0], attn_out[0], head_count, patch_count // WIN, True, scaling
    )
    patch_one = patch_rows + window_out
    normed_one = layer_norm(query_rows, norm_gain[1], norm_bias[1]).astype(NARROW)
    causal_out, causal_kept = branch_forward(
        normed_one, attn_in[1], attn_out[1], head_count, 1, causal, scaling
    )
    query_one = query_rows + causal_out
    normed_q = layer_norm(query_one, norm_gain[2], norm_bias[2]).astype(NARROW)
    normed_x = layer_norm(patch_one, norm_gain[3], norm_bias[3]).astype(NARROW)
    cross_weights = attn_in[2]
    query_heads = split_heads(
        matmul(normed_q, cross_weights[:, :features]).astype(NARROW), head_count
    )
    patch_kv = matmul(normed_x, cross_weights[:, features:]).astype(NARROW)
    key_local = patch_kv[:, :features]
    value_local = patch_kv[:, features:]
    local_peak, local_total, local_out = block_stats(
        query_heads, key_local, value_local, flag_rows, scaling
    )
    local_log = local_peak + jnp.log(local_total)
    local_mean = jnp.transpose(local_out / local_total[..., None], (1, 0, 2)).reshape(
        query_count, features
    )
    logs = lax.all_gather(jnp.transpose(local_log, (1, 0)), "blk")
    cross_logsum = jax.nn.logsumexp(logs, axis=0)
    weighting = jnp.exp(jnp.transpose(local_log, (1, 0)) - cross_logsum)
    weighted = (split_heads(local_mean, head_count) * weighting[..., None]).reshape(
        query_count, features
    )
    cross_share = scatter_blk(pad_rows(weighted.astype(NARROW)).reshape(blocks, part, features))
    cross_out = gather_blk(cross_share.astype(NARROW)).reshape(padded, features)[:query_count]
    cross_logsum = jnp.transpose(cross_logsum, (1, 0))
    cross_mixed = cross_out
    query_two = query_one + matmul(cross_mixed, attn_out[2])
    reverse_weights = attn_in[3]
    patch_query = split_heads(
        matmul(normed_x, reverse_weights[:, :features]).astype(NARROW), head_count
    )[None]
    query_kv = matmul(normed_q, reverse_weights[:, features:]).astype(NARROW)
    reverse_keys = split_heads(query_kv[:, :features], head_count)[None]
    reverse_values = split_heads(query_kv[:, features:], head_count)[None]
    reverse_mixed, reverse_logsum = attend_forward(
        patch_query, reverse_keys, reverse_values, reaching, scaling
    )
    reverse_mixed = reverse_mixed.reshape(patch_count, features).astype(NARROW)
    patch_two = patch_one + matmul(reverse_mixed, attn_out[3])
    normed_five = layer_norm(patch_two, norm_gain[5], norm_bias[5]).astype(NARROW)
    patch_mlp, patch_kept = mlp_forward(normed_five, mlp_in[0], mlp_out[0])
    patch_three = patch_two + patch_mlp
    grad_x_three = cot_patches[0].astype(SINGLE)
    grad_q_three = cot_queries[0].astype(SINGLE)
    normed_grad, up_grad, down_grad = mlp_backward(
        normed_five, mlp_in[0], mlp_out[0], patch_kept, grad_x_three.astype(NARROW)
    )
    patch_up_grad = reduce_all(up_grad.astype(NARROW))
    patch_down_grad = reduce_all(down_grad.astype(NARROW))
    input_part, gain_five, bias_five = norm_back(patch_two, norm_gain[5], norm_bias[5], normed_grad)
    grad_x_two = grad_x_three + input_part
    reverse_upstream = grad_x_two.astype(NARROW)
    reverse_out_grad = weight_grad(reverse_mixed, reverse_upstream)
    reverse_mixed_grad = (
        input_grad(reverse_upstream, attn_out[3])
        .astype(NARROW)
        .reshape(1, patch_count, head_count, head_size)
    )
    patch_q_grad, query_k_grad, query_v_grad = attend_backward(
        patch_query,
        reverse_keys,
        reverse_values,
        reaching,
        scaling,
        reverse_logsum,
        reverse_mixed_grad,
    )
    patch_q_grad = patch_q_grad.reshape(patch_count, features).astype(NARROW)
    reverse_q_weight = weight_grad(normed_x, patch_q_grad)
    normed_x_grad = input_grad(patch_q_grad, reverse_weights[:, :features])
    query_kv_part = jnp.concatenate(
        (query_k_grad.reshape(query_count, features), query_v_grad.reshape(query_count, features)),
        axis=1,
    )
    query_kv_share = scatter_blk(
        pad_rows(query_kv_part.astype(NARROW)).reshape(blocks, part, 2 * features)
    )
    normed_four = layer_norm(query_two, norm_gain[4], norm_bias[4]).astype(NARROW)
    query_mlp, (preact, hidden_q) = mlp_forward(normed_four, mlp_in[1], mlp_out[1])
    query_three = query_two + query_mlp
    upstream = grad_q_three.astype(NARROW)
    unused, pullback = jax.vjp(gelu_exact, preact)
    grad_preact = pullback(input_grad(upstream, mlp_out[1]))[0].astype(NARROW)
    normed_grad = input_grad(grad_preact, mlp_in[1])
    query_up_grad = reduce_rep(weight_grad(own_columns(normed_four), grad_preact))
    query_down_grad = reduce_rep(weight_grad(own_columns(hidden_q, hidden // blocks), upstream))
    input_part, gain_four, bias_four = norm_back(query_two, norm_gain[4], norm_bias[4], normed_grad)
    grad_q_two = grad_q_three + input_part
    cross_upstream = grad_q_two.astype(NARROW)
    cross_out_grad = weight_grad(own_columns(cross_mixed), cross_upstream)
    cross_heads_grad = jnp.transpose(
        split_heads(input_grad(cross_upstream, attn_out[2]).astype(NARROW), head_count), (1, 0, 2)
    )
    key_heads = split_heads(key_local, head_count)
    scores = (
        jnp.einsum("qhe,khe->hqk", query_heads, key_heads, preferred_element_type=SINGLE) * scaling
    )
    scores = jnp.where(flag_rows[None, None, :] > 0, scores, MASKED)
    weights = jnp.exp(scores - local_peak[..., None])
    factor = jnp.exp(local_peak - cross_logsum)
    delta = jnp.sum(
        cross_heads_grad.astype(SINGLE)
        * jnp.transpose(split_heads(cross_out, head_count), (1, 0, 2)).astype(SINGLE),
        axis=-1,
    )
    block_grad = (cross_heads_grad.astype(SINGLE) * factor[..., None]).astype(NARROW)
    weight_upstream = jnp.einsum(
        "hqe,khe->hqk",
        block_grad,
        split_heads(value_local, head_count),
        preferred_element_type=SINGLE,
    )
    score_grad = (weights * weight_upstream - weights * (factor * delta)[..., None]).astype(NARROW)
    query_part = (
        jnp.einsum("hqk,khe->qhe", score_grad, key_heads, preferred_element_type=SINGLE).reshape(
            query_count, features
        )
        * scaling
    )
    query_share = scatter_blk(pad_rows(query_part.astype(NARROW)).reshape(blocks, part, features))
    key_grad = (
        jnp.einsum("hqk,qhe->khe", score_grad, query_heads, preferred_element_type=SINGLE).reshape(
            patch_count, features
        )
        * scaling
    )
    value_grad = jnp.einsum(
        "hqk,hqe->khe", weights.astype(NARROW), block_grad, preferred_element_type=SINGLE
    ).reshape(patch_count, features)
    patch_kv_grad = jnp.concatenate((key_grad, value_grad), axis=1).astype(NARROW)
    cross_kv_weight = weight_grad(normed_x, patch_kv_grad)
    cross_total = reduce_all(
        jnp.concatenate(
            (cross_kv_weight, reverse_q_weight, reverse_out_grad), axis=1
        ).astype(NARROW)
    )
    normed_x_grad = normed_x_grad + input_grad(patch_kv_grad, cross_weights[:, features:])
    input_part, gain_three, bias_three = norm_back(
        patch_one, norm_gain[3], norm_bias[3], normed_x_grad
    )
    grad_x_one = grad_x_two + input_part
    normed_grad, window_in_grad, window_out_grad = branch_backward(
        normed_zero,
        attn_in[0],
        attn_out[0],
        head_count,
        patch_count // WIN,
        True,
        scaling,
        window_kept,
        grad_x_one.astype(NARROW),
    )
    input_part, gain_zero, bias_zero = norm_back(
        patch_rows, norm_gain[0], norm_bias[0], normed_grad
    )
    grad_x_zero = grad_x_one + input_part
    window_total = reduce_all(
        jnp.concatenate((window_in_grad, window_out_grad), axis=1).astype(NARROW)
    )
    query_sum = query_share.astype(NARROW)
    query_kv_sum = query_kv_share.astype(NARROW)
    share_normed = own_rows(normed_q)
    shared_total = reduce_all(
        weight_grad(share_normed, jnp.concatenate((query_sum, query_kv_sum), axis=1)).astype(NARROW)
    )
    normed_q_grad = input_grad(query_sum, cross_weights[:, :features]) + input_grad(
        query_kv_sum, reverse_weights[:, features:]
    )
    input_part, gain_two, bias_two = norm_back(
        own_rows(query_one), norm_gain[2], norm_bias[2], normed_q_grad
    )
    input_part = gather_blk(input_part.astype(NARROW)).reshape(padded, features)[:query_count]
    grad_q_one = grad_q_two + input_part.astype(SINGLE)
    project, attended, logsum = causal_kept
    upstream = grad_q_one.astype(NARROW)
    causal_out_grad = weight_grad(own_columns(attended), upstream)
    grad_attended = (
        input_grad(upstream, attn_out[1])
        .astype(NARROW)
        .reshape(1, query_count, head_count, head_size)
    )
    columns = project.reshape(1, query_count, 3, head_count, head_size)
    grads = attend_backward(
        columns[:, :, 0],
        columns[:, :, 1],
        columns[:, :, 2],
        causal,
        scaling,
        logsum,
        grad_attended,
    )
    grad_project = jnp.stack(grads, axis=2).reshape(query_count, 3 * features).astype(NARROW)
    normed_grad = input_grad(grad_project, attn_in[1])
    causal_in_grad = weight_grad(own_columns(normed_one), grad_project)
    input_part, gain_one, bias_one = norm_back(query_rows, norm_gain[1], norm_bias[1], normed_grad)
    grad_q_zero = grad_q_one + input_part
    query_total = reduce_rep(
        jnp.concatenate((causal_in_grad, causal_out_grad, cross_out_grad), axis=1)
    )
    norms = jnp.stack(
        (
            gain_zero,
            gain_one * leader,
            gain_two,
            gain_three,
            gain_four * leader,
            gain_five,
            bias_zero,
            bias_one * leader,
            bias_two,
            bias_three,
            bias_four * leader,
            bias_five,
        )
    )
    norms = own_columns(lax.psum(norms, ("blk", "rep")))
    wide = 3 * features
    grad_attn_in = jnp.stack(
        (
            window_total[:, :wide],
            query_total[:, :wide],
            jnp.concatenate((shared_total[:, :features], cross_total[:, : 2 * features]), axis=1),
            jnp.concatenate(
                (cross_total[:, 2 * features : wide], shared_total[:, features:]), axis=1
            ),
        )
    )
    grad_attn_out = jnp.stack(
        (
            window_total[:, wide:],
            query_total[:, wide : wide + features],
            query_total[:, wide + features :],
            cross_total[:, wide:],
        )
    )
    return (
        patch_three.astype(NARROW)[None],
        own_columns(query_three).astype(NARROW)[None],
        grad_x_zero[None],
        own_columns(grad_q_zero)[None],
        norms[:6],
        norms[6:],
        grad_attn_in.astype(SINGLE),
        grad_attn_out.astype(SINGLE),
        jnp.stack((patch_up_grad, query_up_grad)).astype(SINGLE),
        jnp.stack((patch_down_grad, query_down_grad)).astype(SINGLE),
    )


def solution(mesh):
    placed = (
        P("rep", "blk", None),
        P("rep", None, None),
        P("rep", "blk"),
        P("rep"),
        P(),
        P(),
        P(),
        P(),
        P(),
        P(),
        P("rep", "blk", None),
        P("rep", None, None),
    )
    return jax.shard_map(
        body,
        mesh=mesh,
        in_specs=placed,
        out_specs=(
            P("rep", "blk", None),
            P("rep", None, "blk"),
            P("rep", "blk", None),
            P("rep", None, "blk"),
            P(None, "blk"),
            P(None, "blk"),
            P(None, "blk", None),
            P(None, "blk", None),
            P(None, "blk", None),
            P(None, "blk", None),
        ),
        check_vma=False,
    )
```

```python
import functools
import math

import jax
import jax.numpy as jnp
from jax import lax
from jax.experimental import pallas as pl
from jax.experimental.pallas import tpu as pltpu
from jax.sharding import PartitionSpec as P

HEADS = 12
WIN = 64
EPSILON = 1e-05
MASKED = -1e30
NARROW = jnp.bfloat16
SINGLE = jnp.float32
EXACT = lax.Precision.HIGHEST
GROUP = 128
PAIR = 128
HEAD = 64
STRIP = 160
CHUNK = 768


def dot(former, latter, ahead, behind, precision=None):
    return lax.dot_general(
        former,
        latter,
        (((ahead,), (behind,)), ((), ())),
        preferred_element_type=SINGLE,
        precision=precision,
    )


def plain(former, latter):
    return dot(former, latter, 1, 0)


def right_t(former, latter):
    return dot(former, latter, 1, 1)


def left_t(former, latter):
    return dot(former, latter, 0, 0)


def loop(count, action):
    def step(index, nothing):
        action(index)
        return nothing

    lax.fori_loop(0, count, step, 0)


def at(index, size):
    return pl.ds(pl.multiple_of(index * size, size), size)


def iota(shape, dim):
    return lax.broadcasted_iota(jnp.int32, shape, dim)


def statistics(tensor):
    average = jnp.mean(tensor, axis=-1, keepdims=True)
    centred = tensor - average
    spread = jnp.mean(centred * centred, axis=-1, keepdims=True)
    return centred, lax.rsqrt(spread + EPSILON)


def norm(tensor, gain, bias):
    centred, inverse = statistics(tensor)
    return centred * inverse * gain + bias


def norm_back(tensor, gain, upstream):
    centred, inverse = statistics(tensor)
    scaled = centred * inverse
    inner = upstream * gain
    grad = inverse * (
        inner
        - jnp.mean(inner, axis=-1, keepdims=True)
        - scaled * jnp.mean(inner * scaled, axis=-1, keepdims=True)
    )
    return (
        grad,
        jnp.sum(upstream * scaled, axis=0, keepdims=True),
        jnp.sum(upstream, axis=0, keepdims=True),
    )


def gelu_both(tensor):
    size = jnp.abs(tensor)
    ratio = 1.0 / (1.0 + (0.3275911 * math.sqrt(0.5)) * size)
    series = ratio * (
        0.254829592
        + ratio * (-0.284496736 + ratio * (1.421413741 + ratio * (-1.453152027 + ratio * 1.061405429)))
    )
    bell = jnp.exp(-0.5 * (tensor * tensor))
    tail = 0.5 * series * bell
    below = jnp.where(tensor >= 0, 1.0 - tail, tail)
    return tensor * below, below + tensor * bell * (1.0 / math.sqrt(2.0 * math.pi))


def half(which, value=1.0):
    return jnp.where(iota((1, PAIR), 1) // HEAD == which, value, 0.0).astype(NARROW)


def lower_lanes():
    return iota((1, PAIR), 1) < HEAD


def attend(queries, keys, values, mask):
    outs, logs = [], []
    for which in range(2):
        scores = mask(right_t(queries * half(which, 1.0 / math.sqrt(HEAD)), keys))
        peak = jnp.max(scores, axis=-1, keepdims=True)
        weights = jnp.exp(scores - peak)
        total = jnp.sum(weights, axis=-1, keepdims=True)
        outs.append(plain(weights.astype(NARROW), values) * (1.0 / total))
        logs.append(peak + jnp.log(total))
    return jnp.where(lower_lanes(), outs[0], outs[1]), logs


def attend_back(queries, keys, values, upstream, logs, deltas, mask):
    scaled = queries * jnp.asarray(1.0 / math.sqrt(HEAD), NARROW)
    grads = []
    for which in range(2):
        lanes = half(which)
        scores = mask(right_t(keys * lanes, scaled))
        if logs is None:
            weights = jnp.exp(scores - jnp.max(scores, axis=0, keepdims=True))
            weights = weights * (1.0 / jnp.sum(weights, axis=0, keepdims=True))
        else:
            weights = jnp.exp(scores - logs[which])
        inner = right_t(values * lanes, upstream)
        slope = (weights * (inner - deltas[which])).astype(NARROW)
        grads.append(
            (
                left_t(slope, keys),
                plain(slope, scaled),
                plain(weights.astype(NARROW), upstream),
            )
        )
    return tuple(jnp.where(lower_lanes(), one, two) for one, two in zip(*grads))


def head_rows(tensor):
    features = tensor.shape[1]
    heads = 16
    chosen = jnp.where(
        iota((heads, features), 1) // HEAD == iota((heads, features), 0), 1.0, 0.0
    ).astype(SINGLE)
    return dot(chosen, tensor, 1, 1, EXACT)


def turn(columns):
    same = jnp.where(iota((16, columns.shape[1]), 0) == iota((16, columns.shape[1]), 1), 1.0, 0.0)
    return dot(same.astype(SINGLE), columns, 1, 1, EXACT)


def row_pair(ref, pair, span):
    tensor = ref[:, span]
    index = iota(tensor.shape, 0)
    return [
        jnp.sum(jnp.where(index == 2 * pair + which, tensor, 0.0), axis=0, keepdims=True)
        for which in range(2)
    ]


def chooser(rows, width, start, count):
    row = iota((rows, width), 0)
    hit = jnp.logical_and(iota((rows, width), 1) == row + start, row < count)
    return jnp.where(hit, 1.0, 0.0).astype(NARROW)


def mark(log_ref, rows, head, value):
    log_ref[rows, :] = jnp.where(iota((1, PAIR), 1) == head, value, log_ref[rows, :])


def copies(semaphores, *pairs):
    made = [
        pltpu.make_async_copy(source, target, semaphores.at[k])
        for k, (source, target) in enumerate(pairs)
    ]
    for one in made:
        one.start()
    return made


def keep(scores):
    return scores


def window_forward(
    x_ref, gain_ref, bias_ref, a_in, a_out,
    n0_ref, pw_ref, mw_ref, x1_ref, nx_ref, vq_ref, ckv_ref,
    w_in, w_out, w_q, w_kv, sem,
):
    rows, features = x_ref.shape
    loads = copies(
        sem,
        (a_in.at[0], w_in),
        (a_out.at[0], w_out),
        (a_in.at[3, :, pl.ds(0, features)], w_q),
        (a_in.at[2, :, pl.ds(features, 2 * features)], w_kv),
    )

    def first(i):
        span = at(i, GROUP)
        n0_ref[span, :] = norm(
            x_ref[span, :].astype(SINGLE), gain_ref[0:1, :], bias_ref[0:1, :]
        ).astype(NARROW)

    loop(rows // GROUP, first)
    loads[0].wait()

    def project(j):
        span = at(j, CHUNK)
        pw_ref[:, span] = plain(n0_ref[...], w_in[:, span]).astype(NARROW)

    loop(3 * features // CHUNK, project)
    window = jnp.where(
        iota((GROUP, GROUP), 0) // WIN == iota((GROUP, GROUP), 1) // WIN, 0.0, MASKED
    )

    def group(i):
        span = at(i, GROUP)
        for pair in range(features // PAIR):
            lane = pair * PAIR
            out, unused = attend(
                pw_ref[span, lane : lane + PAIR],
                pw_ref[span, features + lane : features + lane + PAIR],
                pw_ref[span, 2 * features + lane : 2 * features + lane + PAIR],
                lambda scores: scores + window,
            )
            mw_ref[span, lane : lane + PAIR] = out.astype(NARROW)

    loop(rows // GROUP, group)
    loads[1].wait()

    def second(i):
        span = at(i, GROUP)
        total = x_ref[span, :].astype(SINGLE) + plain(mw_ref[span, :], w_out[...])
        x1_ref[span, :] = total
        nx_ref[span, :] = norm(total, gain_ref[3:4, :], bias_ref[3:4, :]).astype(NARROW)

    loop(rows // GROUP, second)
    loads[2].wait()
    vq_ref[...] = plain(nx_ref[...], w_q[...]).astype(NARROW)
    loads[3].wait()

    def third(j):
        span = at(j, CHUNK)
        ckv_ref[:, span] = plain(nx_ref[...], w_kv[:, span]).astype(NARROW)

    loop(2 * features // CHUNK, third)


def causal_forward(
    q_ref, gain_ref, bias_ref, a_in, a_out,
    n1_ref, pq_ref, mq_ref, q1_ref, nq_ref, cq_ref, vkv_ref, log_ref,
    w_in, w_out, w_q, w_kv, logs, sem,
):
    rows, features = q_ref.shape
    loads = copies(
        sem,
        (a_in.at[1], w_in),
        (a_out.at[1], w_out),
        (a_in.at[2, :, pl.ds(0, features)], w_q),
        (a_in.at[3, :, pl.ds(features, 2 * features)], w_kv),
    )

    def first(i):
        span = at(i, STRIP)
        n1_ref[span, :] = norm(
            q_ref[span, :].astype(SINGLE), gain_ref[1:2, :], bias_ref[1:2, :]
        ).astype(NARROW)

    loop(rows // STRIP, first)
    loads[0].wait()

    def project(j):
        span = at(j, CHUNK)
        pq_ref[:, span] = plain(n1_ref[...], w_in[:, span]).astype(NARROW)

    loop(3 * features // CHUNK, project)
    logs[...] = jnp.zeros_like(logs)

    def pair(p):
        for strip in range(rows // STRIP):
            start, end = strip * STRIP, (strip + 1) * STRIP

            def mask(scores, start=start):
                shape = scores.shape
                return jnp.where(iota(shape, 1) <= iota(shape, 0) + start, scores, MASKED)

            out, sums = attend(
                pq_ref[start:end, at(p, PAIR)],
                pq_ref[0:end, at(p + features // PAIR, PAIR)],
                pq_ref[0:end, at(p + 2 * features // PAIR, PAIR)],
                mask,
            )
            mq_ref[start:end, at(p, PAIR)] = out.astype(NARROW)
            for which in range(2):
                mark(logs, slice(start, end), 2 * p + which, sums[which])

    loop(features // PAIR, pair)
    log_ref[...] = turn(logs[...])
    loads[1].wait()

    def second(i):
        span = at(i, STRIP)
        total = q_ref[span, :].astype(SINGLE) + plain(mq_ref[span, :], w_out[...])
        q1_ref[span, :] = total
        nq_ref[span, :] = norm(total, gain_ref[2:3, :], bias_ref[2:3, :]).astype(NARROW)

    loop(rows // STRIP, second)
    loads[2].wait()
    cq_ref[...] = plain(nq_ref[...], w_q[...]).astype(NARROW)
    loads[3].wait()

    def third(j):
        span = at(j, CHUNK)
        vkv_ref[:, span] = plain(nq_ref[...], w_kv[:, span]).astype(NARROW)

    loop(2 * features // CHUNK, third)


def cross_forward(pieces, order_ref, cq_ref, ckv_ref, valid_ref, *rest):
    out_refs, log_refs, (whole, logs) = rest[:pieces], rest[pieces : 2 * pieces], rest[2 * pieces :]
    rows, features = cq_ref.shape
    part = out_refs[0].shape[0]
    logs[...] = jnp.zeros_like(logs)
    if whole.shape[0] > rows:
        whole[rows:, :] = jnp.zeros((whole.shape[0] - rows, features), NARROW)

    def pair(p):
        for strip in range(rows // STRIP):
            span = slice(strip * STRIP, (strip + 1) * STRIP)
            out, sums = attend(
                cq_ref[span, at(p, PAIR)],
                ckv_ref[:, at(p, PAIR)],
                ckv_ref[:, at(p + features // PAIR, PAIR)],
                lambda scores: scores + valid_ref[...],
            )
            whole[span, at(p, PAIR)] = out.astype(NARROW)
            for which in range(2):
                mark(logs, span, 2 * p + which, sums[which])

    loop(features // PAIR, pair)
    for k in range(pieces):
        out_refs[k][...] = whole[at(order_ref[k], part), :]
        log_refs[k][...] = logs[at(order_ref[k], part), :]


def merge_blocks(pieces, *refs):
    outs, logs = refs[:pieces], refs[pieces : 2 * pieces]
    co_ref, log_ref = refs[2 * pieces :]
    features = co_ref.shape[1]
    peak = functools.reduce(jnp.maximum, [one[...] for one in logs])
    total = peak + jnp.log(functools.reduce(jnp.add, [jnp.exp(one[...] - peak) for one in logs]))
    log_ref[...] = total
    spread = jnp.where(
        iota((PAIR, features), 1) // HEAD == iota((PAIR, features), 0), 1.0, 0.0
    ).astype(NARROW)
    result = jnp.zeros(co_ref.shape, SINGLE)
    for k in range(pieces):
        weight = jnp.exp(logs[k][...] - total)
        high = weight.astype(NARROW)
        low = (weight - high.astype(SINGLE)).astype(NARROW)
        result = result + (plain(high, spread) + plain(low, spread)) * outs[k][...].astype(SINGLE)
    co_ref[...] = result.astype(NARROW)


def reverse_forward(
    length_ref, vq_ref, vkv_ref, x1_ref, a_out,
    mv_ref, x2_ref, log_ref,
    w_out, logs, sem,
):
    rows, features = vq_ref.shape
    keys = vkv_ref.shape[0]
    (load,) = copies(sem, (a_out.at[3], w_out))
    logs[...] = jnp.zeros_like(logs)
    bias = jnp.where(iota((1, keys), 1) < length_ref[0], 0.0, MASKED)

    def pair(p):
        for strip in range(rows // GROUP):
            span = slice(strip * GROUP, (strip + 1) * GROUP)
            out, sums = attend(
                vq_ref[span, at(p, PAIR)],
                vkv_ref[:, at(p, PAIR)],
                vkv_ref[:, at(p + features // PAIR, PAIR)],
                lambda scores: scores + bias,
            )
            mv_ref[span, at(p, PAIR)] = out.astype(NARROW)
            for which in range(2):
                mark(logs, span, 2 * p + which, sums[which])

    loop(features // PAIR, pair)
    log_ref[...] = turn(logs[...])
    load.wait()

    def second(i):
        span = at(i, GROUP)
        x2_ref[span, :] = x1_ref[span, :] + plain(mv_ref[span, :], w_out[...])

    loop(rows // GROUP, second)


def feed_forward_step(block, normed, up, down, cot, hidden, slope, out, grad):
    rows = normed.shape[0]

    def strip(i):
        span = at(i, block)
        value, rise = gelu_both(plain(normed[span, :], up[...]))
        hidden[span, :] = value.astype(NARROW)
        slope[span, :] = (right_t(cot[span, :], down[...]) * rise).astype(NARROW)
        out[span, :] += plain(hidden[span, :], down[...])
        grad[span, :] += right_t(slope[span, :], up[...])

    loop(rows // block, strip)


def patch_feed_forward(
    x2_ref, cot_ref, gain_ref, bias_ref, up_ref, down_ref,
    x3_ref, dx2_ref, up_grad_ref, down_grad_ref, norm_ref,
    normed, hidden, slope, out, grad,
):
    rows = x2_ref.shape[0]
    step = pl.program_id(0)

    @pl.when(step == 0)
    def begin():
        def first(i):
            span = at(i, GROUP)
            normed[span, :] = norm(
                x2_ref[span, :], gain_ref[5:6, :], bias_ref[5:6, :]
            ).astype(NARROW)
            out[span, :] = x2_ref[span, :]
            grad[span, :] = jnp.zeros_like(grad[span, :])

        loop(rows // GROUP, first)

    feed_forward_step(
        256, normed, up_ref.at[0], down_ref.at[0], cot_ref, hidden, slope, out, grad
    )
    up_grad_ref[...] = left_t(normed[...], slope[...]).astype(NARROW)
    down_grad_ref[...] = left_t(hidden[...], cot_ref[...]).astype(NARROW)

    @pl.when(step == pl.num_programs(0) - 1)
    def finish():
        norm_ref[...] = jnp.zeros_like(norm_ref)

        def last(i):
            span = at(i, GROUP)
            x3_ref[span, :] = out[span, :].astype(NARROW)
            part, gain, bias = norm_back(x2_ref[span, :], gain_ref[5:6, :], grad[span, :])
            dx2_ref[span, :] = cot_ref[span, :].astype(SINGLE) + part
            norm_ref[0:1, :] += gain
            norm_ref[1:2, :] += bias

        loop(rows // GROUP, last)


def query_feed_forward(
    pieces, share, hidden_share, place_ref, order_ref, q1_ref, cot_ref, gain_ref, bias_ref,
    w_out, up_ref, down_ref, *rest,
):
    parts, rest = rest[:pieces], rest[pieces:]
    (
        q3_ref, dq2_ref, up_grad_ref, down_grad_ref, norm_ref, co_ref,
        q2, normed, chosen, hidden, slope, out, grad,
    ) = rest
    rows, features = q1_ref.shape
    part = parts[0].shape[0]
    width = up_ref.shape[2]
    step = pl.program_id(0)

    @pl.when(step == 0)
    def begin():
        for k in range(pieces):
            co_ref[at(order_ref[k], part), :] = parts[k][...]

        def first(i):
            span = at(i, STRIP)
            total = q1_ref[span, :] + plain(co_ref[span, :], w_out[0])
            q2[span, :] = total
            out[span, :] = total
            normed[span, :] = norm(total, gain_ref[4:5, :], bias_ref[4:5, :]).astype(NARROW)
            grad[span, :] = jnp.zeros_like(grad[span, :])

        loop(rows // STRIP, first)
        chosen[...] = right_t(
            chooser(chosen.shape[0], features, place_ref[0] * share, share), normed[...]
        ).astype(NARROW)

    feed_forward_step(
        STRIP, normed, up_ref.at[0], down_ref.at[0], cot_ref, hidden, slope, out, grad
    )
    up_grad_ref[...] = plain(chosen[...], slope[...]).astype(NARROW)
    begins = place_ref[0] * hidden_share

    @pl.when(begins // width == step)
    def own_hidden():
        taken = right_t(
            chooser(down_grad_ref.shape[0], width, begins - step * width, hidden_share),
            hidden[...],
        ).astype(NARROW)
        down_grad_ref[...] = plain(taken, cot_ref[...]).astype(NARROW)

    @pl.when(step == pl.num_programs(0) - 1)
    def finish():
        norm_ref[...] = jnp.zeros_like(norm_ref)

        def last(i):
            span = at(i, STRIP)
            q3_ref[span, :] = out[span, :].astype(NARROW)
            piece, gain, bias = norm_back(q2[span, :], gain_ref[4:5, :], grad[span, :])
            dq2_ref[span, :] = cot_ref[span, :].astype(SINGLE) + piece
            norm_ref[0:1, :] += gain
            norm_ref[1:2, :] += bias

        loop(rows // STRIP, last)


def reverse_backward(
    pieces, order_ref, length_ref, dx2_ref, mv_ref, vq_ref, vkv_ref, nx_ref, log_ref, a_out,
    *rest,
):
    dvq_ref, weight_ref, rest = rest[0], rest[1], rest[2:]
    kv_refs, (w_out, rounded, dmv, deltas, dkv, sem) = rest[:pieces], rest[pieces:]
    rows, features = vq_ref.shape
    keys = vkv_ref.shape[0]
    part = kv_refs[0].shape[0]
    (load,) = copies(sem, (a_out.at[3], w_out))
    rounded[...] = dx2_ref[...].astype(NARROW)
    load.wait()
    dmv[...] = right_t(rounded[...], w_out[...]).astype(NARROW)
    weight_ref[:, features:] = left_t(mv_ref[...], rounded[...]).astype(NARROW)
    deltas[...] = head_rows(dmv[...].astype(SINGLE) * mv_ref[...].astype(SINGLE))
    if dkv.shape[0] > keys:
        dkv[keys:, :] = jnp.zeros((dkv.shape[0] - keys, 2 * features), SINGLE)
    size = 256

    def pair(p):
        for strip in range(rows // size):
            span = slice(strip * size, (strip + 1) * size)

            def mask(scores):
                return jnp.where(iota(scores.shape, 0) < length_ref[0], scores, MASKED)

            dq, dk, dv = attend_back(
                vq_ref[span, at(p, PAIR)],
                vkv_ref[:, at(p, PAIR)],
                vkv_ref[:, at(p + features // PAIR, PAIR)],
                dmv[span, at(p, PAIR)],
                row_pair(log_ref, p, span),
                row_pair(deltas, p, span),
                mask,
            )
            dvq_ref[span, at(p, PAIR)] = (dq * (1.0 / math.sqrt(HEAD))).astype(NARROW)
            if strip == 0:
                dkv[0:keys, at(p, PAIR)] = dk
                dkv[0:keys, at(p + features // PAIR, PAIR)] = dv
            else:
                dkv[0:keys, at(p, PAIR)] += dk
                dkv[0:keys, at(p + features // PAIR, PAIR)] += dv

    loop(features // PAIR, pair)
    weight_ref[:, 0:features] = left_t(nx_ref[...], dvq_ref[...]).astype(NARROW)
    for k in range(pieces):
        kv_refs[k][...] = dkv[at(order_ref[k], part), :].astype(NARROW)


def cross_backward(
    pieces, share, place_ref, order_ref, dq2_ref, co_ref, cq_ref, ckv_ref, valid_ref, a_out, *rest
):
    log_parts, rest = rest[:pieces], rest[pieces:]
    dckv_ref, weight_ref, rest = rest[0], rest[1], rest[2:]
    q_refs, (w_out, rounded, dco, deltas, logs, turned, dq_all, dkv, sem) = (
        rest[:pieces],
        rest[pieces:],
    )
    rows, features = cq_ref.shape
    part = log_parts[0].shape[0]
    (load,) = copies(sem, (a_out.at[2], w_out))
    for k in range(pieces):
        logs[at(order_ref[k], part), :] = log_parts[k][...]
    turned[...] = turn(logs[0:rows, :])
    rounded[...] = dq2_ref[...].astype(NARROW)
    load.wait()
    dco[...] = right_t(rounded[...], w_out[...]).astype(NARROW)
    taken = right_t(
        chooser(weight_ref.shape[0], features, place_ref[0] * share, share), co_ref[0:rows, :]
    ).astype(NARROW)
    weight_ref[...] = plain(taken, rounded[...]).astype(NARROW)
    deltas[...] = head_rows(dco[...].astype(SINGLE) * co_ref[0:rows, :].astype(SINGLE))
    if dq_all.shape[0] > rows:
        dq_all[rows:, :] = jnp.zeros((dq_all.shape[0] - rows, features), NARROW)
    edges = [(start, min(start + 256, rows)) for start in range(0, rows, 256)]
    if len(edges) > 1 and edges[-1][1] - edges[-1][0] < 128:
        edges[-2:] = [(edges[-2][0], rows)]

    def pair(p):
        for number, (start, end) in enumerate(edges):
            span = slice(start, end)
            dq, dk, dv = attend_back(
                cq_ref[span, at(p, PAIR)],
                ckv_ref[:, at(p, PAIR)],
                ckv_ref[:, at(p + features // PAIR, PAIR)],
                dco[span, at(p, PAIR)],
                row_pair(turned, p, span),
                row_pair(deltas, p, span),
                lambda scores: scores + valid_ref[...],
            )
            dq_all[span, at(p, PAIR)] = (dq * (1.0 / math.sqrt(HEAD))).astype(NARROW)
            if number == 0:
                dkv[:, at(p, PAIR)] = dk
                dkv[:, at(p + features // PAIR, PAIR)] = dv
            else:
                dkv[:, at(p, PAIR)] += dk
                dkv[:, at(p + features // PAIR, PAIR)] += dv

    loop(features // PAIR, pair)
    dckv_ref[...] = dkv[...].astype(NARROW)
    for k in range(pieces):
        q_refs[k][...] = dq_all[at(order_ref[k], part), :]


def patch_backward(
    x_ref, dx2_ref, x1_ref, nx_ref, n0_ref, pw_ref, mw_ref, dvq_ref, dckv_ref, gain_ref, a_in, a_out,
    kv_weight_ref, weight_ref, grad_ref, norm_ref,
    w_in, w_out, w_q, w_kv, dx1, rounded, dmw, deltas, dpw, sem,
):
    rows, features = x_ref.shape
    loads = copies(
        sem,
        (a_in.at[3, :, pl.ds(0, features)], w_q),
        (a_in.at[2, :, pl.ds(features, 2 * features)], w_kv),
        (a_out.at[0], w_out),
        (a_in.at[0], w_in),
    )
    norm_ref[...] = jnp.zeros_like(norm_ref)

    def kv_weight(j):
        span = at(j, CHUNK)
        kv_weight_ref[:, span] = left_t(nx_ref[...], dckv_ref[:, span]).astype(NARROW)

    loop(2 * features // CHUNK, kv_weight)
    loads[0].wait()
    loads[1].wait()

    def first(i):
        span = at(i, GROUP)
        upstream = right_t(dvq_ref[span, :], w_q[...]) + right_t(dckv_ref[span, :], w_kv[...])
        part, gain, bias = norm_back(x1_ref[span, :], gain_ref[3:4, :], upstream)
        total = dx2_ref[span, :] + part
        dx1[span, :] = total
        rounded[span, :] = total.astype(NARROW)
        norm_ref[0:1, :] += gain
        norm_ref[1:2, :] += bias

    loop(rows // GROUP, first)
    loads[2].wait()
    dmw[...] = right_t(rounded[...], w_out[...]).astype(NARROW)
    weight_ref[:, 3 * features :] = left_t(mw_ref[...], rounded[...]).astype(NARROW)
    deltas[...] = head_rows(dmw[...].astype(SINGLE) * mw_ref[...].astype(SINGLE))
    window = jnp.where(
        iota((GROUP, GROUP), 0) // WIN == iota((GROUP, GROUP), 1) // WIN, 0.0, MASKED
    )

    def group(i):
        span = at(i, GROUP)
        for pair in range(features // PAIR):
            lane = pair * PAIR
            dq, dk, dv = attend_back(
                pw_ref[span, lane : lane + PAIR],
                pw_ref[span, features + lane : features + lane + PAIR],
                pw_ref[span, 2 * features + lane : 2 * features + lane + PAIR],
                dmw[span, lane : lane + PAIR],
                None,
                [deltas[2 * pair + w : 2 * pair + w + 1, span] for w in range(2)],
                lambda scores: scores + window,
            )
            dpw[span, lane : lane + PAIR] = (dq * (1.0 / math.sqrt(HEAD))).astype(NARROW)
            dpw[span, features + lane : features + lane + PAIR] = dk.astype(NARROW)
            dpw[span, 2 * features + lane : 2 * features + lane + PAIR] = dv.astype(NARROW)

    loop(rows // GROUP, group)

    def in_weight(j):
        span = at(j, CHUNK)
        weight_ref[:, span] = left_t(n0_ref[...], dpw[:, span]).astype(NARROW)

    loop(3 * features // CHUNK, in_weight)
    loads[3].wait()

    def last(i):
        span = at(i, GROUP)
        upstream = right_t(dpw[span, :], w_in[...])
        part, gain, bias = norm_back(x_ref[span, :].astype(SINGLE), gain_ref[0:1, :], upstream)
        grad_ref[span, :] = dx1[span, :] + part
        norm_ref[2:3, :] += gain
        norm_ref[3:4, :] += bias

    loop(rows // GROUP, last)


def share_backward(
    pieces, q1_ref, nq_ref, gain_ref, a_in, *rest
):
    q_parts, kv_parts, rest = rest[:pieces], rest[pieces : 2 * pieces], rest[2 * pieces :]
    grad_ref, weight_ref, norm_ref, w_q, w_kv, summed, sem = rest
    features = q1_ref.shape[1]
    loads = copies(
        sem,
        (a_in.at[2, :, pl.ds(0, features)], w_q),
        (a_in.at[3, :, pl.ds(features, 2 * features)], w_kv),
    )
    summed[:, 0:features] = functools.reduce(
        jnp.add, [one[...].astype(SINGLE) for one in q_parts]
    ).astype(NARROW)
    summed[:, features:] = functools.reduce(
        jnp.add, [one[...].astype(SINGLE) for one in kv_parts]
    ).astype(NARROW)

    def weight(j):
        span = at(j, CHUNK)
        weight_ref[:, span] = left_t(nq_ref[...], summed[:, span]).astype(NARROW)

    loop(3 * features // CHUNK, weight)
    for load in loads:
        load.wait()
    upstream = right_t(summed[:, 0:features], w_q[...]) + right_t(summed[:, features:], w_kv[...])
    part, gain, bias = norm_back(q1_ref[...], gain_ref[2:3, :], upstream)
    grad_ref[...] = part.astype(NARROW)
    norm_ref[...] = jnp.zeros_like(norm_ref)
    norm_ref[0:1, :] = gain
    norm_ref[1:2, :] = bias


def causal_backward(
    pieces, share, place_ref, order_ref, q_ref, dq2_ref, n1_ref, pq_ref, mq_ref, log_ref, gain_ref,
    a_in, a_out, *rest
):
    parts, rest = rest[:pieces], rest[pieces:]
    (
        weight_ref, grad_ref, norm_ref,
        w_in, w_out, gathered, dq1, rounded, dmq, deltas, dkv, dpq, sem,
    ) = rest
    rows, features = q_ref.shape
    part = parts[0].shape[0]
    loads = copies(sem, (a_out.at[1], w_out), (a_in.at[1], w_in))
    for k in range(pieces):
        gathered[at(order_ref[k], part), :] = parts[k][...]

    def first(i):
        span = at(i, STRIP)
        total = dq2_ref[span, :] + gathered[span, :].astype(SINGLE)
        dq1[span, :] = total
        rounded[span, :] = total.astype(NARROW)

    loop(rows // STRIP, first)
    loads[0].wait()
    dmq[...] = right_t(rounded[...], w_out[...]).astype(NARROW)
    chosen = chooser(weight_ref.shape[0], features, place_ref[0] * share, share)
    taken = right_t(chosen, mq_ref[...]).astype(NARROW)
    weight_ref[:, 3 * features :] = plain(taken, rounded[...]).astype(NARROW)
    deltas[...] = head_rows(dmq[...].astype(SINGLE) * mq_ref[...].astype(SINGLE))
    edges = [(start, min(start + 256, rows)) for start in range(0, rows, 256)]

    def pair(p):
        for number, (start, end) in reversed(list(enumerate(edges))):
            span = slice(start, end)

            def mask(scores, start=start):
                shape = scores.shape
                return jnp.where(iota(shape, 0) <= iota(shape, 1) + start, scores, MASKED)

            dq, dk, dv = attend_back(
                pq_ref[span, at(p, PAIR)],
                pq_ref[0:end, at(p + features // PAIR, PAIR)],
                pq_ref[0:end, at(p + 2 * features // PAIR, PAIR)],
                dmq[span, at(p, PAIR)],
                row_pair(log_ref, p, span),
                row_pair(deltas, p, span),
                mask,
            )
            dpq[span, at(p, PAIR)] = (dq * (1.0 / math.sqrt(HEAD))).astype(NARROW)
            if end == rows:
                dkv[0:end, 0:PAIR] = dk
                dkv[0:end, PAIR:] = dv
            else:
                dkv[0:end, 0:PAIR] += dk
                dkv[0:end, PAIR:] += dv
        dpq[:, at(p + features // PAIR, PAIR)] = dkv[:, 0:PAIR].astype(NARROW)
        dpq[:, at(p + 2 * features // PAIR, PAIR)] = dkv[:, PAIR:].astype(NARROW)

    loop(features // PAIR, pair)
    taken = right_t(chosen, n1_ref[...]).astype(NARROW)
    weight_ref[:, 0 : 3 * features] = plain(taken, dpq[...]).astype(NARROW)
    loads[1].wait()
    norm_ref[...] = jnp.zeros_like(norm_ref)

    def last(i):
        span = at(i, STRIP)
        upstream = right_t(dpq[span, :], w_in[...])
        piece, gain, bias = norm_back(q_ref[span, :].astype(SINGLE), gain_ref[1:2, :], upstream)
        grad_ref[span, :] = dq1[span, :] + piece
        norm_ref[0:1, :] += gain
        norm_ref[1:2, :] += bias

    loop(rows // STRIP, last)


def bits_of(count):
    return max(count - 1, 0).bit_length()


def swap(tensor, axis, mask):
    return lax.ppermute(tensor, axis, [(i, i ^ mask) for i in range(lax.axis_size(axis))])


def pick(tensor, place, dim):
    return lax.dynamic_index_in_dim(tensor, place, dim, keepdims=False)


def fold(tensor, axis, bit, dim):
    own = (lax.axis_index(axis) >> bit) & 1
    arrived = swap(pick(tensor, 1 - own, dim).astype(NARROW), axis, 1 << bit)
    return pick(tensor, own, dim).astype(SINGLE) + arrived.astype(SINGLE)


def unfold(tensor, axis, bit, dim):
    own = (lax.axis_index(axis) >> bit) & 1
    arrived = swap(tensor, axis, 1 << bit)
    return jnp.where(
        own == 0,
        jnp.stack((tensor, arrived), axis=dim),
        jnp.stack((arrived, tensor), axis=dim),
    )


def scatter_blk(tensor):
    bits = bits_of(lax.axis_size("blk"))
    tensor = tensor.reshape((2,) * bits + tensor.shape[1:])
    for bit in range(bits):
        tensor = fold(tensor, "blk", bit, bits - 1 - bit)
    return tensor


def sum_rep_scatter(tensor, dim):
    bits = bits_of(lax.axis_size("rep"))
    shape = tensor.shape
    tensor = tensor.reshape(
        shape[:dim] + (2,) * bits + (shape[dim] // 2**bits,) + shape[dim + 1 :]
    )
    for bit in range(bits):
        tensor = fold(tensor, "rep", bit, dim)
    return tensor


def gather_rep(tensor, dim):
    bits = bits_of(lax.axis_size("rep"))
    for bit in reversed(range(bits)):
        tensor = unfold(tensor, "rep", bit, dim)
    shape = tensor.shape
    return tensor.reshape(shape[:dim] + (-1,) + shape[dim + bits + 1 :])


def reduce_all(tensor):
    count = lax.axis_size("blk")
    tensor = tensor.reshape(count, tensor.shape[0] // count, tensor.shape[1])
    tensor = sum_rep_scatter(tensor, 1)
    tensor = scatter_blk(tensor).astype(NARROW)
    return gather_rep(tensor, 0)


def reduce_rep(tensor):
    return gather_rep(sum_rep_scatter(tensor, 0).astype(NARROW), 0)


DIRECT = 8


def piece_order():
    count = lax.axis_size("blk")
    numbers = jnp.arange(count, dtype=jnp.int32)
    return numbers ^ lax.axis_index("blk").astype(jnp.int32) if count <= DIRECT else numbers


def exchange(pieces):
    if len(pieces) <= DIRECT:
        return [one if k == 0 else swap(one, "blk", k) for k, one in enumerate(pieces)]
    whole = lax.all_to_all(jnp.stack(pieces), "blk", 0, 0)
    return [whole[k] for k in range(len(pieces))]


def gather(tensor):
    count = lax.axis_size("blk")
    if count <= DIRECT:
        return [tensor if k == 0 else swap(tensor, "blk", k) for k in range(count)]
    whole = lax.all_gather(tensor, "blk")
    return [whole[k] for k in range(count)]


VMEM = pl.BlockSpec(memory_space=pltpu.VMEM)
SMEM = pl.BlockSpec(memory_space=pltpu.SMEM)
ANY = pl.BlockSpec(memory_space=pl.ANY)


def like(*shape, kind=NARROW):
    return jax.ShapeDtypeStruct(shape, kind)


def call(kernel, outs, operands, specs, scratch, flops, grid=None, out_specs=None, semaphores=0):
    scratch = [pltpu.VMEM(shape, kind) for shape, kind in scratch]
    if semaphores:
        scratch.append(pltpu.SemaphoreType.DMA((semaphores,)))
    extra = {} if grid is None else {"grid": grid}
    return pl.pallas_call(
        kernel,
        out_shape=outs,
        in_specs=specs,
        out_specs=[VMEM] * len(outs) if out_specs is None else out_specs,
        scratch_shapes=scratch,
        compiler_params=pltpu.CompilerParams(vmem_limit_bytes=56 * 2**20),
        cost_estimate=pl.CostEstimate(
            flops=int(flops), bytes_accessed=sum(o.size * o.dtype.itemsize for o in operands), transcendentals=0
        ),
        **extra,
    )(*operands)


def body(
    patches,
    queries,
    window_valid,
    answer_length,
    norm_gain,
    norm_bias,
    attn_in,
    attn_out,
    mlp_in,
    mlp_out,
    cot_patches,
    cot_queries,
):
    x, q, cot_x, cot_q = patches[0], queries[0], cot_patches[0], cot_queries[0]
    rows, features = x.shape
    count = q.shape[0]
    hidden = mlp_in.shape[2]
    blocks = lax.axis_size("blk")
    place = lax.axis_index("blk").astype(jnp.int32)
    places = place.reshape(1)
    order = piece_order()
    share = features // blocks
    hidden_share = hidden // blocks
    share_rows = -(-share // 16) * 16
    hidden_rows = -(-hidden_share // 16) * 16
    part = -(-count // (blocks * 16)) * 16
    padded = part * blocks
    wide = 3 * features
    leader = (place == 0).astype(SINGLE)
    valid = jnp.where(jnp.repeat(window_valid[0], WIN) > 0, 0.0, MASKED).astype(SINGLE)

    def own_columns(tensor):
        return lax.dynamic_slice_in_dim(tensor, place * share, share, 1)

    def own_rows(tensor):
        tensor = jnp.pad(tensor, ((0, padded - count), (0, 0)))
        return lax.dynamic_slice_in_dim(tensor, place * part, part, 0)

    square = 2.0 * features * features

    n0, pw, mw, x1, nx, vq, ckv = call(
        window_forward,
        [
            like(rows, features), like(rows, wide), like(rows, features),
            like(rows, features, kind=SINGLE), like(rows, features), like(rows, features),
            like(rows, 2 * features),
        ],
        [x, norm_gain, norm_bias, attn_in, attn_out],
        [VMEM, VMEM, VMEM, ANY, ANY],
        [((features, wide), NARROW), ((features, features), NARROW),
         ((features, features), NARROW), ((features, 2 * features), NARROW)],
        rows * square * 9,
        semaphores=4,
    )
    n1, pq, mq, q1, nq, cq, vkv, log_q = call(
        causal_forward,
        [
            like(count, features), like(count, wide), like(count, features),
            like(count, features, kind=SINGLE), like(count, features), like(count, features),
            like(count, 2 * features), like(16, count, kind=SINGLE),
        ],
        [q, norm_gain, norm_bias, attn_in, attn_out],
        [VMEM, VMEM, VMEM, ANY, ANY],
        [((features, wide), NARROW), ((features, features), NARROW),
         ((features, features), NARROW), ((features, 2 * features), NARROW),
         ((count, PAIR), SINGLE)],
        count * square * 15,
        semaphores=4,
    )
    pieces = call(
        functools.partial(cross_forward, blocks),
        [like(part, features)] * blocks + [like(part, PAIR, kind=SINGLE)] * blocks,
        [order, cq, ckv, valid[None, :]],
        [SMEM, VMEM, VMEM, VMEM],
        [((padded, features), NARROW), ((padded, PAIR), SINGLE)],
        count * square * 6,
    )
    merged = call(
        functools.partial(merge_blocks, blocks),
        [like(part, features), like(part, PAIR, kind=SINGLE)],
        exchange(pieces[:blocks]) + exchange(pieces[blocks:]),
        [VMEM] * (2 * blocks),
        [],
        padded * square,
    )
    co_parts, log_parts = gather(merged[0]), gather(merged[1])
    mv, x2, log_v = call(
        reverse_forward,
        [like(rows, features), like(rows, features, kind=SINGLE), like(16, rows, kind=SINGLE)],
        [answer_length, vq, vkv, x1, attn_out],
        [SMEM, VMEM, VMEM, VMEM, ANY],
        [((features, features), NARROW), ((rows, PAIR), SINGLE)],
        rows * square * 8,
        semaphores=1,
    )
    fixed = lambda *shape: pl.BlockSpec(shape, lambda j: (0,) * len(shape))
    x3, dx2, up_x, down_x, norm_five = call(
        patch_feed_forward,
        [
            like(rows, features), like(rows, features, kind=SINGLE), like(features, hidden),
            like(hidden, features), like(8, features, kind=SINGLE),
        ],
        [x2, cot_x, norm_gain, norm_bias, mlp_in, mlp_out],
        [
            fixed(rows, features), fixed(rows, features), fixed(6, features), fixed(6, features),
            pl.BlockSpec((1, features, CHUNK), lambda j: (0, 0, j)),
            pl.BlockSpec((1, CHUNK, features), lambda j: (0, j, 0)),
        ],
        [((rows, features), NARROW), ((rows, CHUNK), NARROW), ((rows, CHUNK), NARROW),
         ((rows, features), SINGLE), ((rows, features), SINGLE)],
        rows * square * 24,
        grid=(hidden // CHUNK,),
        out_specs=[
            fixed(rows, features), fixed(rows, features),
            pl.BlockSpec((features, CHUNK), lambda j: (0, j)),
            pl.BlockSpec((CHUNK, features), lambda j: (j, 0)),
            fixed(8, features),
        ],
    )
    up_x_total, down_x_total = reduce_all(up_x), reduce_all(down_x)
    dvq, reverse_weight, *kv_pieces = call(
        functools.partial(reverse_backward, blocks),
        [like(rows, features), like(features, 2 * features)] + [like(part, 2 * features)] * blocks,
        [order, answer_length, dx2, mv, vq, vkv, nx, log_v, attn_out],
        [SMEM, SMEM, VMEM, VMEM, VMEM, VMEM, VMEM, VMEM, ANY],
        [((features, features), NARROW), ((rows, features), NARROW), ((rows, features), NARROW),
         ((16, rows), SINGLE), ((padded, 2 * features), SINGLE)],
        rows * square * 16,
        semaphores=1,
    )
    kv_parts = exchange(kv_pieces)
    reverse_total = reduce_all(reverse_weight)
    q3, dq2, up_q, down_q, norm_four, co = call(
        functools.partial(query_feed_forward, blocks, share, hidden_share),
        [
            like(count, features), like(count, features, kind=SINGLE), like(share_rows, hidden),
            like(hidden_rows, features), like(8, features, kind=SINGLE), like(padded, features),
        ],
        [places, order, q1, cot_q, norm_gain, norm_bias, attn_out, mlp_in, mlp_out] + co_parts,
        [
            SMEM, SMEM, fixed(count, features), fixed(count, features), fixed(6, features),
            fixed(6, features), pl.BlockSpec((1, features, features), lambda j: (2, 0, 0)),
            pl.BlockSpec((1, features, CHUNK), lambda j: (1, 0, j)),
            pl.BlockSpec((1, CHUNK, features), lambda j: (1, j, 0)),
        ] + [fixed(part, features)] * blocks,
        [((count, features), SINGLE), ((count, features), NARROW), ((share_rows, count), NARROW),
         ((count, CHUNK), NARROW), ((count, CHUNK), NARROW),
         ((count, features), SINGLE), ((count, features), SINGLE)],
        count * square * 18,
        grid=(hidden // CHUNK,),
        out_specs=[
            fixed(count, features), fixed(count, features),
            pl.BlockSpec((share_rows, CHUNK), lambda j: (0, j)),
            fixed(hidden_rows, features), fixed(8, features), fixed(padded, features),
        ],
    )
    dckv, cross_out_weight, *q_pieces = call(
        functools.partial(cross_backward, blocks, share),
        [like(rows, 2 * features), like(share_rows, features)] + [like(part, features)] * blocks,
        [places, order, dq2, co, cq, ckv, valid[:, None], attn_out] + log_parts,
        [SMEM, SMEM, VMEM, VMEM, VMEM, VMEM, VMEM, ANY] + [VMEM] * blocks,
        [((features, features), NARROW), ((count, features), NARROW), ((count, features), NARROW),
         ((16, count), SINGLE), ((padded, PAIR), SINGLE), ((16, count), SINGLE),
         ((padded, features), NARROW), ((rows, 2 * features), SINGLE)],
        count * square * 12,
        semaphores=1,
    )
    q_parts = exchange(q_pieces)
    up_q_total = reduce_rep(up_q[:share])
    down_q_total = reduce_rep(down_q[:hidden_share])
    kv_weight, window_weight, grad_x, norm_x = call(
        patch_backward,
        [
            like(features, 2 * features), like(features, 4 * features),
            like(rows, features, kind=SINGLE), like(8, features, kind=SINGLE),
        ],
        [x, dx2, x1, nx, n0, pw, mw, dvq, dckv, norm_gain, attn_in, attn_out],
        [VMEM] * 10 + [ANY, ANY],
        [((features, wide), NARROW), ((features, features), NARROW),
         ((features, features), NARROW), ((features, 2 * features), NARROW),
         ((rows, features), SINGLE), ((rows, features), NARROW), ((rows, features), NARROW),
         ((16, rows), SINGLE), ((rows, wide), NARROW)],
        rows * square * 24,
        semaphores=4,
    )
    kv_total, window_total = reduce_all(kv_weight), reduce_all(window_weight)
    dq1_share, share_weight, norm_two = call(
        functools.partial(share_backward, blocks),
        [like(part, features), like(features, wide), like(8, features, kind=SINGLE)],
        [own_rows(q1), own_rows(nq), norm_gain, attn_in] + q_parts + kv_parts,
        [VMEM, VMEM, VMEM, ANY] + [VMEM] * (2 * blocks),
        [((features, features), NARROW), ((features, 2 * features), NARROW),
         ((part, wide), NARROW)],
        part * square * 6,
        semaphores=2,
    )
    share_total = reduce_all(share_weight)
    causal_weight, grad_q, norm_one = call(
        functools.partial(causal_backward, blocks, share),
        [
            like(share_rows, 4 * features), like(count, features, kind=SINGLE),
            like(8, features, kind=SINGLE),
        ],
        [places, order, q, dq2, n1, pq, mq, log_q, norm_gain, attn_in, attn_out]
        + gather(dq1_share),
        [SMEM, SMEM] + [VMEM] * 7 + [ANY, ANY] + [VMEM] * blocks,
        [((features, wide), NARROW), ((features, features), NARROW), ((padded, features), NARROW),
         ((count, features), SINGLE), ((count, features), NARROW), ((count, features), NARROW),
         ((16, count), SINGLE), ((count, 2 * PAIR), SINGLE), ((count, wide), NARROW)],
        count * square * 16,
        semaphores=2,
    )
    query_total = reduce_rep(
        jnp.concatenate((causal_weight[:share], cross_out_weight[:share]), axis=1)
    )
    norms = jnp.stack(
        (
            norm_x[2], norm_one[0] * leader, norm_two[0], norm_x[0], norm_four[0] * leader,
            norm_five[0], norm_x[3], norm_one[1] * leader, norm_two[1], norm_x[1],
            norm_four[1] * leader, norm_five[1],
        )
    )
    norms = own_columns(lax.psum(norms, ("blk", "rep")))
    grad_attn_in = jnp.stack(
        (
            window_total[:, :wide],
            query_total[:, :wide],
            jnp.concatenate((share_total[:, :features], kv_total), axis=1),
            jnp.concatenate((reverse_total[:, :features], share_total[:, features:]), axis=1),
        )
    )
    grad_attn_out = jnp.stack(
        (
            window_total[:, wide:],
            query_total[:, wide : wide + features],
            query_total[:, wide + features :],
            reverse_total[:, features:],
        )
    )
    return (
        x3[None],
        own_columns(q3)[None],
        grad_x[None],
        own_columns(grad_q)[None],
        norms[:6],
        norms[6:],
        grad_attn_in.astype(SINGLE),
        grad_attn_out.astype(SINGLE),
        jnp.stack((up_x_total, up_q_total)).astype(SINGLE),
        jnp.stack((down_x_total, down_q_total)).astype(SINGLE),
    )


def solution(mesh):
    placed = (
        P("rep", "blk", None),
        P("rep", None, None),
        P("rep", "blk"),
        P("rep"),
        P(),
        P(),
        P(),
        P(),
        P(),
        P(),
        P("rep", "blk", None),
        P("rep", None, None),
    )
    return jax.shard_map(
        body,
        mesh=mesh,
        in_specs=placed,
        out_specs=(
            P("rep", "blk", None),
            P("rep", None, "blk"),
            P("rep", "blk", None),
            P("rep", None, "blk"),
            P(None, "blk"),
            P(None, "blk"),
            P(None, "blk", None),
            P(None, "blk", None),
            P(None, "blk", None),
            P(None, "blk", None),
        ),
        check_vma=False,
    )
```

```python
import functools
import math

import jax
import jax.numpy as jnp
from jax import lax
from jax.experimental import pallas as pl
from jax.experimental.pallas import tpu as pltpu
from jax.sharding import PartitionSpec as P

HEADS = 12
WIN = 64
EPSILON = 1e-05
MASKED = -1e30
NARROW = jnp.bfloat16
SINGLE = jnp.float32
EXACT = lax.Precision.HIGHEST
GROUP = 128
PAIR = 128
HEAD = 64
STRIP = 160
CHUNK = 768


def dot(former, latter, ahead, behind, precision=None):
    return lax.dot_general(
        former,
        latter,
        (((ahead,), (behind,)), ((), ())),
        preferred_element_type=SINGLE,
        precision=precision,
    )


def plain(former, latter):
    return dot(former, latter, 1, 0)


def right_t(former, latter):
    return dot(former, latter, 1, 1)


def left_t(former, latter):
    return dot(former, latter, 0, 0)


def loop(count, action):
    def step(index, nothing):
        action(index)
        return nothing

    lax.fori_loop(0, count, step, 0)


def at(index, size):
    return pl.ds(pl.multiple_of(index * size, size), size)


def iota(shape, dim):
    return lax.broadcasted_iota(jnp.int32, shape, dim)


def statistics(tensor):
    average = jnp.mean(tensor, axis=-1, keepdims=True)
    centred = tensor - average
    spread = jnp.mean(centred * centred, axis=-1, keepdims=True)
    return centred, lax.rsqrt(spread + EPSILON)


def norm(tensor, gain, bias):
    centred, inverse = statistics(tensor)
    return centred * inverse * gain + bias


def norm_back(tensor, gain, upstream):
    centred, inverse = statistics(tensor)
    scaled = centred * inverse
    inner = upstream * gain
    grad = inverse * (
        inner
        - jnp.mean(inner, axis=-1, keepdims=True)
        - scaled * jnp.mean(inner * scaled, axis=-1, keepdims=True)
    )
    return (
        grad,
        jnp.sum(upstream * scaled, axis=0, keepdims=True),
        jnp.sum(upstream, axis=0, keepdims=True),
    )


def gelu_both(tensor):
    size = jnp.abs(tensor)
    ratio = 1.0 / (1.0 + (0.3275911 * math.sqrt(0.5)) * size)
    series = ratio * (
        0.254829592
        + ratio * (-0.284496736 + ratio * (1.421413741 + ratio * (-1.453152027 + ratio * 1.061405429)))
    )
    bell = jnp.exp(-0.5 * (tensor * tensor))
    tail = 0.5 * series * bell
    below = jnp.where(tensor >= 0, 1.0 - tail, tail)
    return tensor * below, below + tensor * bell * (1.0 / math.sqrt(2.0 * math.pi))


def half(which, value=1.0):
    return jnp.where(iota((1, PAIR), 1) // HEAD == which, value, 0.0).astype(NARROW)


def lower_lanes():
    return iota((1, PAIR), 1) < HEAD


def attend(queries, keys, values, mask):
    outs, logs = [], []
    for which in range(2):
        scores = mask(right_t(queries * half(which, 1.0 / math.sqrt(HEAD)), keys))
        peak = jnp.max(scores, axis=-1, keepdims=True)
        weights = jnp.exp(scores - peak)
        total = jnp.sum(weights, axis=-1, keepdims=True)
        outs.append(plain(weights.astype(NARROW), values) * (1.0 / total))
        logs.append(peak + jnp.log(total))
    return jnp.where(lower_lanes(), outs[0], outs[1]), logs


def attend_back(queries, keys, values, upstream, logs, deltas, mask):
    scaled = queries * jnp.asarray(1.0 / math.sqrt(HEAD), NARROW)
    grads = []
    for which in range(2):
        lanes = half(which)
        scores = mask(right_t(keys * lanes, scaled))
        if logs is None:
            weights = jnp.exp(scores - jnp.max(scores, axis=0, keepdims=True))
            weights = weights * (1.0 / jnp.sum(weights, axis=0, keepdims=True))
        else:
            weights = jnp.exp(scores - logs[which])
        inner = right_t(values * lanes, upstream)
        slope = (weights * (inner - deltas[which])).astype(NARROW)
        grads.append(
            (
                left_t(slope, keys),
                plain(slope, scaled),
                plain(weights.astype(NARROW), upstream),
            )
        )
    return tuple(jnp.where(lower_lanes(), one, two) for one, two in zip(*grads))


def head_rows(tensor):
    features = tensor.shape[1]
    heads = 16
    chosen = jnp.where(
        iota((heads, features), 1) // HEAD == iota((heads, features), 0), 1.0, 0.0
    ).astype(SINGLE)
    return dot(chosen, tensor, 1, 1, EXACT)


def turn(columns):
    same = jnp.where(iota((16, columns.shape[1]), 0) == iota((16, columns.shape[1]), 1), 1.0, 0.0)
    return dot(same.astype(SINGLE), columns, 1, 1, EXACT)


def row_pair(ref, pair, span):
    tensor = ref[:, span]
    index = iota(tensor.shape, 0)
    return [
        jnp.sum(jnp.where(index == 2 * pair + which, tensor, 0.0), axis=0, keepdims=True)
        for which in range(2)
    ]


def chooser(rows, width, start, count):
    row = iota((rows, width), 0)
    hit = jnp.logical_and(iota((rows, width), 1) == row + start, row < count)
    return jnp.where(hit, 1.0, 0.0).astype(NARROW)


def mark(log_ref, rows, head, value):
    log_ref[rows, :] = jnp.where(iota((1, PAIR), 1) == head, value, log_ref[rows, :])


def copies(semaphores, *pairs):
    made = [
        pltpu.make_async_copy(source, target, semaphores.at[k])
        for k, (source, target) in enumerate(pairs)
    ]
    for one in made:
        one.start()
    return made


DIRECT = 8


def place_of(axis="blk"):
    return lax.axis_index(axis)


def flipped(index, mask, count):
    total, weight = 0, 1
    while weight < count:
        bit = (index // weight) % 2
        total = total + weight * ((1 - bit) if mask & weight else bit)
        weight *= 2
    return total


def piece_at(number, count):
    return flipped(place_of(), number, count) if count <= DIRECT else number


def window_forward(
    x_ref, gain_ref, bias_ref, a_in, a_out,
    n0_ref, pw_ref, mw_ref, x1_ref, nx_ref, vq_ref, ckv_ref,
    w_in, w_out, w_q, w_kv, sem,
):
    rows, features = x_ref.shape
    loads = copies(
        sem,
        (a_in.at[0], w_in),
        (a_out.at[0], w_out),
        (a_in.at[3, :, pl.ds(0, features)], w_q),
        (a_in.at[2, :, pl.ds(features, 2 * features)], w_kv),
    )

    def first(i):
        span = at(i, GROUP)
        n0_ref[span, :] = norm(
            x_ref[span, :].astype(SINGLE), gain_ref[0:1, :], bias_ref[0:1, :]
        ).astype(NARROW)

    loop(rows // GROUP, first)
    loads[0].wait()

    def project(j):
        span = at(j, CHUNK)
        pw_ref[:, span] = plain(n0_ref[...], w_in[:, span]).astype(NARROW)

    loop(3 * features // CHUNK, project)
    window = jnp.where(
        iota((GROUP, GROUP), 0) // WIN == iota((GROUP, GROUP), 1) // WIN, 0.0, MASKED
    )

    def group(i):
        span = at(i, GROUP)
        for pair in range(features // PAIR):
            lane = pair * PAIR
            out, unused = attend(
                pw_ref[span, lane : lane + PAIR],
                pw_ref[span, features + lane : features + lane + PAIR],
                pw_ref[span, 2 * features + lane : 2 * features + lane + PAIR],
                lambda scores: scores + window,
            )
            mw_ref[span, lane : lane + PAIR] = out.astype(NARROW)

    loop(rows // GROUP, group)
    loads[1].wait()

    def second(i):
        span = at(i, GROUP)
        total = x_ref[span, :].astype(SINGLE) + plain(mw_ref[span, :], w_out[...])
        x1_ref[span, :] = total
        nx_ref[span, :] = norm(total, gain_ref[3:4, :], bias_ref[3:4, :]).astype(NARROW)

    loop(rows // GROUP, second)
    loads[2].wait()
    vq_ref[...] = plain(nx_ref[...], w_q[...]).astype(NARROW)
    loads[3].wait()

    def third(j):
        span = at(j, CHUNK)
        ckv_ref[:, span] = plain(nx_ref[...], w_kv[:, span]).astype(NARROW)

    loop(2 * features // CHUNK, third)


def causal_forward(
    q_ref, gain_ref, bias_ref, a_in, a_out,
    n1_ref, pq_ref, mq_ref, q1_ref, nq_ref, cq_ref, vkv_ref, log_ref,
    w_in, w_out, w_q, w_kv, logs, sem,
):
    rows, features = q_ref.shape
    loads = copies(
        sem,
        (a_in.at[1], w_in),
        (a_out.at[1], w_out),
        (a_in.at[2, :, pl.ds(0, features)], w_q),
        (a_in.at[3, :, pl.ds(features, 2 * features)], w_kv),
    )

    def first(i):
        span = at(i, STRIP)
        n1_ref[span, :] = norm(
            q_ref[span, :].astype(SINGLE), gain_ref[1:2, :], bias_ref[1:2, :]
        ).astype(NARROW)

    loop(rows // STRIP, first)
    loads[0].wait()

    def project(j):
        span = at(j, CHUNK)
        pq_ref[:, span] = plain(n1_ref[...], w_in[:, span]).astype(NARROW)

    loop(3 * features // CHUNK, project)
    logs[...] = jnp.zeros_like(logs)

    def pair(p):
        for strip in range(rows // STRIP):
            start, end = strip * STRIP, (strip + 1) * STRIP

            def mask(scores, start=start):
                shape = scores.shape
                return jnp.where(iota(shape, 1) <= iota(shape, 0) + start, scores, MASKED)

            out, sums = attend(
                pq_ref[start:end, at(p, PAIR)],
                pq_ref[0:end, at(p + features // PAIR, PAIR)],
                pq_ref[0:end, at(p + 2 * features // PAIR, PAIR)],
                mask,
            )
            mq_ref[start:end, at(p, PAIR)] = out.astype(NARROW)
            for which in range(2):
                mark(logs, slice(start, end), 2 * p + which, sums[which])

    loop(features // PAIR, pair)
    log_ref[...] = turn(logs[...])
    loads[1].wait()

    def second(i):
        span = at(i, STRIP)
        total = q_ref[span, :].astype(SINGLE) + plain(mq_ref[span, :], w_out[...])
        q1_ref[span, :] = total
        nq_ref[span, :] = norm(total, gain_ref[2:3, :], bias_ref[2:3, :]).astype(NARROW)

    loop(rows // STRIP, second)
    loads[2].wait()
    cq_ref[...] = plain(nq_ref[...], w_q[...]).astype(NARROW)
    loads[3].wait()

    def third(j):
        span = at(j, CHUNK)
        vkv_ref[:, span] = plain(nq_ref[...], w_kv[:, span]).astype(NARROW)

    loop(2 * features // CHUNK, third)


def cross_forward(pieces, cq_ref, ckv_ref, valid_ref, *rest):
    out_refs, log_refs, (whole, logs) = rest[:pieces], rest[pieces : 2 * pieces], rest[2 * pieces :]
    rows, features = cq_ref.shape
    part = out_refs[0].shape[0]
    logs[...] = jnp.zeros_like(logs)
    if whole.shape[0] > rows:
        whole[rows:, :] = jnp.zeros((whole.shape[0] - rows, features), NARROW)

    def pair(p):
        for strip in range(rows // STRIP):
            span = slice(strip * STRIP, (strip + 1) * STRIP)
            out, sums = attend(
                cq_ref[span, at(p, PAIR)],
                ckv_ref[:, at(p, PAIR)],
                ckv_ref[:, at(p + features // PAIR, PAIR)],
                lambda scores: scores + valid_ref[...],
            )
            whole[span, at(p, PAIR)] = out.astype(NARROW)
            for which in range(2):
                mark(logs, span, 2 * p + which, sums[which])

    loop(features // PAIR, pair)
    for k in range(pieces):
        out_refs[k][...] = whole[at(piece_at(k, pieces), part), :]
        log_refs[k][...] = logs[at(piece_at(k, pieces), part), :]


def merge_blocks(pieces, *refs):
    outs, logs = refs[:pieces], refs[pieces : 2 * pieces]
    co_ref, log_ref = refs[2 * pieces :]
    features = co_ref.shape[1]
    peak = functools.reduce(jnp.maximum, [one[...] for one in logs])
    total = peak + jnp.log(functools.reduce(jnp.add, [jnp.exp(one[...] - peak) for one in logs]))
    log_ref[...] = total
    spread = jnp.where(
        iota((PAIR, features), 1) // HEAD == iota((PAIR, features), 0), 1.0, 0.0
    ).astype(NARROW)
    result = jnp.zeros(co_ref.shape, SINGLE)
    for k in range(pieces):
        weight = jnp.exp(logs[k][...] - total)
        high = weight.astype(NARROW)
        low = (weight - high.astype(SINGLE)).astype(NARROW)
        result = result + (plain(high, spread) + plain(low, spread)) * outs[k][...].astype(SINGLE)
    co_ref[...] = result.astype(NARROW)


def reverse_forward(
    length_ref, vq_ref, vkv_ref, x1_ref, a_out,
    mv_ref, x2_ref, log_ref,
    w_out, logs, sem,
):
    rows, features = vq_ref.shape
    keys = vkv_ref.shape[0]
    (load,) = copies(sem, (a_out.at[3], w_out))
    logs[...] = jnp.zeros_like(logs)
    bias = jnp.where(iota((1, keys), 1) < length_ref[0], 0.0, MASKED)

    def pair(p):
        for strip in range(rows // GROUP):
            span = slice(strip * GROUP, (strip + 1) * GROUP)
            out, sums = attend(
                vq_ref[span, at(p, PAIR)],
                vkv_ref[:, at(p, PAIR)],
                vkv_ref[:, at(p + features // PAIR, PAIR)],
                lambda scores: scores + bias,
            )
            mv_ref[span, at(p, PAIR)] = out.astype(NARROW)
            for which in range(2):
                mark(logs, span, 2 * p + which, sums[which])

    loop(features // PAIR, pair)
    log_ref[...] = turn(logs[...])
    load.wait()

    def second(i):
        span = at(i, GROUP)
        x2_ref[span, :] = x1_ref[span, :] + plain(mv_ref[span, :], w_out[...])

    loop(rows // GROUP, second)


def feed_forward_step(block, normed, up, down, cot, hidden, slope, out, grad):
    rows = normed.shape[0]

    def strip(i):
        span = at(i, block)
        value, rise = gelu_both(plain(normed[span, :], up[...]))
        hidden[span, :] = value.astype(NARROW)
        slope[span, :] = (right_t(cot[span, :], down[...]) * rise).astype(NARROW)
        out[span, :] += plain(hidden[span, :], down[...])
        grad[span, :] += right_t(slope[span, :], up[...])

    loop(rows // block, strip)


def patch_feed_forward(
    x2_ref, cot_ref, gain_ref, bias_ref, up_ref, down_ref,
    x3_ref, dx2_ref, up_grad_ref, down_grad_ref, norm_ref,
    normed, hidden, slope, out, grad,
):
    rows = x2_ref.shape[0]
    step = pl.program_id(0)

    @pl.when(step == 0)
    def begin():
        def first(i):
            span = at(i, GROUP)
            normed[span, :] = norm(
                x2_ref[span, :], gain_ref[5:6, :], bias_ref[5:6, :]
            ).astype(NARROW)
            out[span, :] = x2_ref[span, :]
            grad[span, :] = jnp.zeros_like(grad[span, :])

        loop(rows // GROUP, first)

    feed_forward_step(
        256, normed, up_ref.at[0], down_ref.at[0], cot_ref, hidden, slope, out, grad
    )
    up_grad_ref[...] = left_t(normed[...], slope[...]).astype(NARROW)
    down_grad_ref[...] = left_t(hidden[...], cot_ref[...]).astype(NARROW)

    @pl.when(step == pl.num_programs(0) - 1)
    def finish():
        norm_ref[...] = jnp.zeros_like(norm_ref)

        def last(i):
            span = at(i, GROUP)
            x3_ref[span, :] = out[span, :].astype(NARROW)
            part, gain, bias = norm_back(x2_ref[span, :], gain_ref[5:6, :], grad[span, :])
            dx2_ref[span, :] = cot_ref[span, :].astype(SINGLE) + part
            norm_ref[0:1, :] += gain
            norm_ref[1:2, :] += bias

        loop(rows // GROUP, last)


def query_feed_forward(
    pieces, share, hidden_share, q1_ref, cot_ref, gain_ref, bias_ref,
    w_out, up_ref, down_ref, *rest,
):
    parts, rest = rest[:pieces], rest[pieces:]
    (
        q3_ref, dq2_ref, up_grad_ref, down_grad_ref, norm_ref, co_ref,
        q2, normed, chosen, hidden, slope, out, grad,
    ) = rest
    rows, features = q1_ref.shape
    part = parts[0].shape[0]
    width = up_ref.shape[2]
    step = pl.program_id(0)

    @pl.when(step == 0)
    def begin():
        for k in range(pieces):
            co_ref[at(piece_at(k, pieces), part), :] = parts[k][...]

        def first(i):
            span = at(i, STRIP)
            total = q1_ref[span, :] + plain(co_ref[span, :], w_out[0])
            q2[span, :] = total
            out[span, :] = total
            normed[span, :] = norm(total, gain_ref[4:5, :], bias_ref[4:5, :]).astype(NARROW)
            grad[span, :] = jnp.zeros_like(grad[span, :])

        loop(rows // STRIP, first)
        chosen[...] = right_t(
            chooser(chosen.shape[0], features, place_of() * share, share), normed[...]
        ).astype(NARROW)

    feed_forward_step(
        STRIP, normed, up_ref.at[0], down_ref.at[0], cot_ref, hidden, slope, out, grad
    )
    up_grad_ref[...] = plain(chosen[...], slope[...]).astype(NARROW)
    begins = place_of() * hidden_share

    @pl.when(begins // width == step)
    def own_hidden():
        taken = right_t(
            chooser(down_grad_ref.shape[0], width, begins - step * width, hidden_share),
            hidden[...],
        ).astype(NARROW)
        down_grad_ref[...] = plain(taken, cot_ref[...]).astype(NARROW)

    @pl.when(step == pl.num_programs(0) - 1)
    def finish():
        norm_ref[...] = jnp.zeros_like(norm_ref)

        def last(i):
            span = at(i, STRIP)
            q3_ref[span, :] = out[span, :].astype(NARROW)
            piece, gain, bias = norm_back(q2[span, :], gain_ref[4:5, :], grad[span, :])
            dq2_ref[span, :] = cot_ref[span, :].astype(SINGLE) + piece
            norm_ref[0:1, :] += gain
            norm_ref[1:2, :] += bias

        loop(rows // STRIP, last)


def reverse_backward(
    pieces, length_ref, dx2_ref, mv_ref, vq_ref, vkv_ref, nx_ref, log_ref, a_out,
    *rest,
):
    dvq_ref, weight_ref, rest = rest[0], rest[1], rest[2:]
    kv_refs, (w_out, rounded, dmv, deltas, dkv, sem) = rest[:pieces], rest[pieces:]
    rows, features = vq_ref.shape
    keys = vkv_ref.shape[0]
    part = kv_refs[0].shape[0]
    (load,) = copies(sem, (a_out.at[3], w_out))
    rounded[...] = dx2_ref[...].astype(NARROW)
    load.wait()
    dmv[...] = right_t(rounded[...], w_out[...]).astype(NARROW)
    weight_ref[:, features:] = left_t(mv_ref[...], rounded[...]).astype(NARROW)
    deltas[...] = head_rows(dmv[...].astype(SINGLE) * mv_ref[...].astype(SINGLE))
    if dkv.shape[0] > keys:
        dkv[keys:, :] = jnp.zeros((dkv.shape[0] - keys, 2 * features), SINGLE)
    size = 256

    def pair(p):
        for strip in range(rows // size):
            span = slice(strip * size, (strip + 1) * size)

            def mask(scores):
                return jnp.where(iota(scores.shape, 0) < length_ref[0], scores, MASKED)

            dq, dk, dv = attend_back(
                vq_ref[span, at(p, PAIR)],
                vkv_ref[:, at(p, PAIR)],
                vkv_ref[:, at(p + features // PAIR, PAIR)],
                dmv[span, at(p, PAIR)],
                row_pair(log_ref, p, span),
                row_pair(deltas, p, span),
                mask,
            )
            dvq_ref[span, at(p, PAIR)] = (dq * (1.0 / math.sqrt(HEAD))).astype(NARROW)
            if strip == 0:
                dkv[0:keys, at(p, PAIR)] = dk
                dkv[0:keys, at(p + features // PAIR, PAIR)] = dv
            else:
                dkv[0:keys, at(p, PAIR)] += dk
                dkv[0:keys, at(p + features // PAIR, PAIR)] += dv

    loop(features // PAIR, pair)
    weight_ref[:, 0:features] = left_t(nx_ref[...], dvq_ref[...]).astype(NARROW)
    for k in range(pieces):
        kv_refs[k][...] = dkv[at(piece_at(k, pieces), part), :].astype(NARROW)


def cross_backward(
    pieces, share, dq2_ref, co_ref, cq_ref, ckv_ref, valid_ref, a_out, *rest
):
    log_parts, rest = rest[:pieces], rest[pieces:]
    dckv_ref, weight_ref, rest = rest[0], rest[1], rest[2:]
    q_refs, (w_out, rounded, dco, deltas, logs, turned, dq_all, dkv, sem) = (
        rest[:pieces],
        rest[pieces:],
    )
    rows, features = cq_ref.shape
    part = log_parts[0].shape[0]
    (load,) = copies(sem, (a_out.at[2], w_out))
    for k in range(pieces):
        logs[at(piece_at(k, pieces), part), :] = log_parts[k][...]
    turned[...] = turn(logs[0:rows, :])
    rounded[...] = dq2_ref[...].astype(NARROW)
    load.wait()
    dco[...] = right_t(rounded[...], w_out[...]).astype(NARROW)
    taken = right_t(
        chooser(weight_ref.shape[0], features, place_of() * share, share), co_ref[0:rows, :]
    ).astype(NARROW)
    weight_ref[...] = plain(taken, rounded[...]).astype(NARROW)
    deltas[...] = head_rows(dco[...].astype(SINGLE) * co_ref[0:rows, :].astype(SINGLE))
    if dq_all.shape[0] > rows:
        dq_all[rows:, :] = jnp.zeros((dq_all.shape[0] - rows, features), NARROW)
    edges = [(start, min(start + 256, rows)) for start in range(0, rows, 256)]
    if len(edges) > 1 and edges[-1][1] - edges[-1][0] < 128:
        edges[-2:] = [(edges[-2][0], rows)]

    def pair(p):
        for number, (start, end) in enumerate(edges):
            span = slice(start, end)
            dq, dk, dv = attend_back(
                cq_ref[span, at(p, PAIR)],
                ckv_ref[:, at(p, PAIR)],
                ckv_ref[:, at(p + features // PAIR, PAIR)],
                dco[span, at(p, PAIR)],
                row_pair(turned, p, span),
                row_pair(deltas, p, span),
                lambda scores: scores + valid_ref[...],
            )
            dq_all[span, at(p, PAIR)] = (dq * (1.0 / math.sqrt(HEAD))).astype(NARROW)
            if number == 0:
                dkv[:, at(p, PAIR)] = dk
                dkv[:, at(p + features // PAIR, PAIR)] = dv
            else:
                dkv[:, at(p, PAIR)] += dk
                dkv[:, at(p + features // PAIR, PAIR)] += dv

    loop(features // PAIR, pair)
    dckv_ref[...] = dkv[...].astype(NARROW)
    for k in range(pieces):
        q_refs[k][...] = dq_all[at(piece_at(k, pieces), part), :]


def patch_cross_backward(
    dx2_ref, x1_ref, nx_ref, dvq_ref, dckv_ref, gain_ref, a_in,
    kv_weight_ref, dx1_ref, norm_ref,
    w_q, w_kv, sem,
):
    rows, features = dx2_ref.shape
    loads = copies(
        sem,
        (a_in.at[3, :, pl.ds(0, features)], w_q),
        (a_in.at[2, :, pl.ds(features, 2 * features)], w_kv),
    )
    norm_ref[...] = jnp.zeros_like(norm_ref)

    def kv_weight(j):
        span = at(j, CHUNK)
        kv_weight_ref[:, span] = left_t(nx_ref[...], dckv_ref[:, span]).astype(NARROW)

    loop(2 * features // CHUNK, kv_weight)
    loads[0].wait()
    loads[1].wait()

    def first(i):
        span = at(i, GROUP)
        upstream = right_t(dvq_ref[span, :], w_q[...]) + right_t(dckv_ref[span, :], w_kv[...])
        part, gain, bias = norm_back(x1_ref[span, :], gain_ref[3:4, :], upstream)
        dx1_ref[span, :] = dx2_ref[span, :] + part
        norm_ref[0:1, :] += gain
        norm_ref[1:2, :] += bias

    loop(rows // GROUP, first)


def window_backward(
    x_ref, dx1_ref, n0_ref, pw_ref, mw_ref, gain_ref, a_in, a_out,
    weight_ref, grad_ref, norm_ref,
    w_in, w_out, rounded, dmw, deltas, dpw, sem,
):
    rows, features = x_ref.shape
    loads = copies(sem, (a_out.at[0], w_out), (a_in.at[0], w_in))
    norm_ref[...] = jnp.zeros_like(norm_ref)
    rounded[...] = dx1_ref[...].astype(NARROW)
    loads[0].wait()
    dmw[...] = right_t(rounded[...], w_out[...]).astype(NARROW)
    weight_ref[:, 3 * features :] = left_t(mw_ref[...], rounded[...]).astype(NARROW)
    deltas[...] = head_rows(dmw[...].astype(SINGLE) * mw_ref[...].astype(SINGLE))
    window = jnp.where(
        iota((GROUP, GROUP), 0) // WIN == iota((GROUP, GROUP), 1) // WIN, 0.0, MASKED
    )

    def group(i):
        span = at(i, GROUP)
        for pair in range(features // PAIR):
            lane = pair * PAIR
            dq, dk, dv = attend_back(
                pw_ref[span, lane : lane + PAIR],
                pw_ref[span, features + lane : features + lane + PAIR],
                pw_ref[span, 2 * features + lane : 2 * features + lane + PAIR],
                dmw[span, lane : lane + PAIR],
                None,
                [deltas[2 * pair + w : 2 * pair + w + 1, span] for w in range(2)],
                lambda scores: scores + window,
            )
            dpw[span, lane : lane + PAIR] = (dq * (1.0 / math.sqrt(HEAD))).astype(NARROW)
            dpw[span, features + lane : features + lane + PAIR] = dk.astype(NARROW)
            dpw[span, 2 * features + lane : 2 * features + lane + PAIR] = dv.astype(NARROW)

    loop(rows // GROUP, group)

    def in_weight(j):
        span = at(j, CHUNK)
        weight_ref[:, span] = left_t(n0_ref[...], dpw[:, span]).astype(NARROW)

    loop(3 * features // CHUNK, in_weight)
    loads[1].wait()

    def last(i):
        span = at(i, GROUP)
        upstream = right_t(dpw[span, :], w_in[...])
        part, gain, bias = norm_back(x_ref[span, :].astype(SINGLE), gain_ref[0:1, :], upstream)
        grad_ref[span, :] = dx1_ref[span, :] + part
        norm_ref[0:1, :] += gain
        norm_ref[1:2, :] += bias

    loop(rows // GROUP, last)


def share_backward(
    pieces, q1_ref, nq_ref, gain_ref, a_in, *rest
):
    q_parts, kv_parts, rest = rest[:pieces], rest[pieces : 2 * pieces], rest[2 * pieces :]
    grad_ref, weight_ref, norm_ref, w_q, w_kv, summed, sem = rest
    features = q1_ref.shape[1]
    loads = copies(
        sem,
        (a_in.at[2, :, pl.ds(0, features)], w_q),
        (a_in.at[3, :, pl.ds(features, 2 * features)], w_kv),
    )
    summed[:, 0:features] = functools.reduce(
        jnp.add, [one[...].astype(SINGLE) for one in q_parts]
    ).astype(NARROW)
    summed[:, features:] = functools.reduce(
        jnp.add, [one[...].astype(SINGLE) for one in kv_parts]
    ).astype(NARROW)

    def weight(j):
        span = at(j, CHUNK)
        weight_ref[:, span] = left_t(nq_ref[...], summed[:, span]).astype(NARROW)

    loop(3 * features // CHUNK, weight)
    for load in loads:
        load.wait()
    upstream = right_t(summed[:, 0:features], w_q[...]) + right_t(summed[:, features:], w_kv[...])
    part, gain, bias = norm_back(q1_ref[...], gain_ref[2:3, :], upstream)
    grad_ref[...] = part.astype(NARROW)
    norm_ref[...] = jnp.zeros_like(norm_ref)
    norm_ref[0:1, :] = gain
    norm_ref[1:2, :] = bias


def causal_backward(
    pieces, share, q_ref, dq2_ref, n1_ref, pq_ref, mq_ref, log_ref, cross_ref, gain_ref,
    a_in, a_out, *rest
):
    parts, rest = rest[:pieces], rest[pieces:]
    (
        weight_ref, grad_ref, norm_ref,
        w_in, w_out, gathered, dq1, rounded, dmq, deltas, dkv, dpq, sem,
    ) = rest
    rows, features = q_ref.shape
    part = parts[0].shape[0]
    loads = copies(sem, (a_out.at[1], w_out), (a_in.at[1], w_in))
    for k in range(pieces):
        gathered[at(piece_at(k, pieces), part), :] = parts[k][...]

    def first(i):
        span = at(i, STRIP)
        total = dq2_ref[span, :] + gathered[span, :].astype(SINGLE)
        dq1[span, :] = total
        rounded[span, :] = total.astype(NARROW)

    loop(rows // STRIP, first)
    loads[0].wait()
    dmq[...] = right_t(rounded[...], w_out[...]).astype(NARROW)
    chosen = chooser(weight_ref.shape[0], features, place_of() * share, share)
    taken = right_t(chosen, mq_ref[...]).astype(NARROW)
    weight_ref[:, 3 * features : 4 * features] = plain(taken, rounded[...]).astype(NARROW)
    weight_ref[:, 4 * features : 5 * features] = cross_ref[...]
    weight_ref[:, 5 * features :] = jnp.zeros_like(weight_ref[:, 5 * features :])
    deltas[...] = head_rows(dmq[...].astype(SINGLE) * mq_ref[...].astype(SINGLE))
    edges = [(start, min(start + 256, rows)) for start in range(0, rows, 256)]

    def pair(p):
        for number, (start, end) in reversed(list(enumerate(edges))):
            span = slice(start, end)

            def mask(scores, start=start):
                shape = scores.shape
                return jnp.where(iota(shape, 0) <= iota(shape, 1) + start, scores, MASKED)

            dq, dk, dv = attend_back(
                pq_ref[span, at(p, PAIR)],
                pq_ref[0:end, at(p + features // PAIR, PAIR)],
                pq_ref[0:end, at(p + 2 * features // PAIR, PAIR)],
                dmq[span, at(p, PAIR)],
                row_pair(log_ref, p, span),
                row_pair(deltas, p, span),
                mask,
            )
            dpq[span, at(p, PAIR)] = (dq * (1.0 / math.sqrt(HEAD))).astype(NARROW)
            if end == rows:
                dkv[0:end, 0:PAIR] = dk
                dkv[0:end, PAIR:] = dv
            else:
                dkv[0:end, 0:PAIR] += dk
                dkv[0:end, PAIR:] += dv
        dpq[:, at(p + features // PAIR, PAIR)] = dkv[:, 0:PAIR].astype(NARROW)
        dpq[:, at(p + 2 * features // PAIR, PAIR)] = dkv[:, PAIR:].astype(NARROW)

    loop(features // PAIR, pair)
    taken = right_t(chosen, n1_ref[...]).astype(NARROW)
    weight_ref[:, 0 : 3 * features] = plain(taken, dpq[...]).astype(NARROW)
    loads[1].wait()
    norm_ref[...] = jnp.zeros_like(norm_ref)

    def last(i):
        span = at(i, STRIP)
        upstream = right_t(dpq[span, :], w_in[...])
        piece, gain, bias = norm_back(q_ref[span, :].astype(SINGLE), gain_ref[1:2, :], upstream)
        grad_ref[span, :] = dq1[span, :] + piece
        norm_ref[0:1, :] += gain
        norm_ref[1:2, :] += bias

    loop(rows // STRIP, last)


def bits_of(count):
    return max(count - 1, 0).bit_length()


def swap(tensor, axis, mask):
    return lax.ppermute(tensor, axis, [(i, i ^ mask) for i in range(lax.axis_size(axis))])


def pick(tensor, place, dim):
    return lax.dynamic_index_in_dim(tensor, place, dim, keepdims=False)


def fold(tensor, axis, bit, dim):
    own = (lax.axis_index(axis) >> bit) & 1
    arrived = swap(pick(tensor, 1 - own, dim).astype(NARROW), axis, 1 << bit)
    return pick(tensor, own, dim).astype(SINGLE) + arrived.astype(SINGLE)


def unfold(tensor, axis, bit, dim):
    own = (lax.axis_index(axis) >> bit) & 1
    arrived = swap(tensor, axis, 1 << bit)
    return jnp.where(
        own == 0,
        jnp.stack((tensor, arrived), axis=dim),
        jnp.stack((arrived, tensor), axis=dim),
    )


def scatter_blk(tensor):
    bits = bits_of(lax.axis_size("blk"))
    tensor = tensor.reshape((2,) * bits + tensor.shape[1:])
    for bit in range(bits):
        tensor = fold(tensor, "blk", bit, bits - 1 - bit)
    return tensor


def sum_rep_scatter(tensor, dim):
    bits = bits_of(lax.axis_size("rep"))
    shape = tensor.shape
    tensor = tensor.reshape(
        shape[:dim] + (2,) * bits + (shape[dim] // 2**bits,) + shape[dim + 1 :]
    )
    for bit in range(bits):
        tensor = fold(tensor, "rep", bit, dim)
    return tensor


def gather_rep(tensor, dim):
    bits = bits_of(lax.axis_size("rep"))
    for bit in reversed(range(bits)):
        tensor = unfold(tensor, "rep", bit, dim)
    shape = tensor.shape
    return tensor.reshape(shape[:dim] + (-1,) + shape[dim + bits + 1 :])


def reduce_all(tensor):
    count = lax.axis_size("blk")
    tensor = tensor.reshape(count, tensor.shape[0] // count, tensor.shape[1])
    tensor = sum_rep_scatter(tensor, 1)
    tensor = scatter_blk(tensor).astype(NARROW)
    return gather_rep(tensor, 0)


def reduce_rep(tensor):
    return gather_rep(sum_rep_scatter(tensor, 0).astype(NARROW), 0)


def exchange(pieces):
    whole = lax.all_to_all(jnp.stack(pieces), "blk", 0, 0)
    return [whole[k] for k in range(len(pieces))]


def gather(tensor):
    count = lax.axis_size("blk")
    whole = lax.all_gather(tensor, "blk")
    return [whole[k] for k in range(count)]


def whole(ref):
    return ref


class Move:
    def __init__(self, source, shape, axis, flip, take=whole):
        self.source, self.shape, self.axis, self.flip, self.take = source, shape, axis, flip, take


class Reduction:
    def __init__(self, tensor):
        blocks = lax.axis_size("blk")
        height = tensor.shape[0] // blocks
        self.tensor = tensor.reshape(blocks, 2, height // 2, tensor.shape[1])

    def moves(self, stage):
        tensor = self.tensor
        shape = tensor.shape
        if stage == "core":
            return [
                Move(tensor, shape[:1] + shape[2:], "rep", 1,
                     lambda ref: ref.at[:, 1 - place_of("rep") % 2])
            ]
        if stage == "x":
            width = shape[-1] // 2

            def columns(ref):
                span = pl.ds(pl.multiple_of((1 - place_of("rep") // 2) * width, width), width)
                return ref.at[(slice(None),) * (len(shape) - 1) + (span,)]

            return [Move(tensor, shape[:-1] + (width,), "rep", 2, columns)]
        if stage == "y":
            tensor = self.tensor = tensor.reshape((shape[0] // 2, 2) + shape[1:])
            return [
                Move(tensor, tensor.shape[:1] + shape[1:], "blk", 1,
                     lambda ref: ref.at[:, 1 - place_of() % 2])
            ]
        if stage == "z":
            length = shape[0]
            return [
                Move(tensor, shape[1:], "blk", 2 * k,
                     lambda ref, k=k: ref.at[flipped(place_of() // 2, k, length)])
                for k in range(1, length)
            ]
        return [Move(tensor, shape, "rep", 2 if stage == "back_x" else 1)]

    def absorb(self, stage, arrived):
        tensor = self.tensor
        rep, blk = lax.axis_index("rep"), lax.axis_index("blk")
        if stage == "core":
            own = pick(tensor, rep % 2, 1)
        elif stage == "x":
            width = tensor.shape[-1] // 2
            own = lax.dynamic_slice_in_dim(tensor, (rep // 2) * width, width, tensor.ndim - 1)
        elif stage == "y":
            own = pick(tensor, blk % 2, 1)
        elif stage == "z":
            own = pick(tensor, blk // 2, 0)
        else:
            bit, dim = (rep // 2, tensor.ndim - 1) if stage == "back_x" else (rep % 2, 0)
            self.tensor = jnp.where(
                bit == 0,
                jnp.concatenate((tensor, arrived[0]), axis=dim),
                jnp.concatenate((arrived[0], tensor), axis=dim),
            )
            return
        total = own.astype(SINGLE)
        for one in arrived:
            total = total + one.astype(SINGLE)
        self.tensor = total.astype(NARROW)


class RepSum:
    def __init__(self, tensor, dim):
        self.tensor, self.dim = tensor, dim

    def moves(self, stage):
        shape = list(self.tensor.shape)
        if stage == "out":
            size = shape[self.dim] = shape[self.dim] // 4

            def quarter(ref, k):
                span = pl.ds(pl.multiple_of(flipped(place_of("rep"), k, 4) * size, size), size)
                return ref.at[span, :] if self.dim == 0 else ref.at[:, span]

            return [
                Move(self.tensor, tuple(shape), "rep", k, lambda ref, k=k: quarter(ref, k))
                for k in range(1, 4)
            ]
        return [Move(self.tensor, tuple(shape), "rep", k) for k in range(1, 4)]

    def absorb(self, stage, arrived):
        rep = lax.axis_index("rep")
        if stage == "out":
            size = self.tensor.shape[self.dim] // 4
            total = lax.dynamic_slice_in_dim(self.tensor, rep * size, size, self.dim).astype(SINGLE)
            for one in arrived:
                total = total + one.astype(SINGLE)
            self.tensor = total.astype(NARROW)
            return
        held = [self.tensor] + list(arrived)
        for weight in (1, 2):
            flip = (rep // weight) % 2 == 1
            held = [
                jnp.where(flip, held[k ^ weight], held[k]) for k in range(4)
            ]
        self.tensor = jnp.concatenate(held, axis=self.dim)


VMEM = pl.BlockSpec(memory_space=pltpu.VMEM)
SMEM = pl.BlockSpec(memory_space=pltpu.SMEM)
ANY = pl.BlockSpec(memory_space=pl.ANY)


def like(*shape, kind=NARROW):
    return jax.ShapeDtypeStruct(shape, kind)


def call(
    kernel, outs, operands, specs, scratch, flops, grid=None, out_specs=None, semaphores=0,
    moves=(), ident=None,
):
    scratch = [pltpu.VMEM(shape, kind) for shape, kind in scratch]
    if semaphores:
        scratch.append(pltpu.SemaphoreType.DMA((semaphores,)))
    out_specs = [VMEM] * len(outs) if out_specs is None else out_specs
    extra = {} if grid is None else {"grid": grid}
    params = {}
    sources = []
    for move in moves:
        if not any(move.source is one for one in sources):
            sources.append(move.source)
    number = [next(k for k, one in enumerate(sources) if one is move.source) for move in moves]
    fixed_in, fixed_out = len(operands), len(outs)
    partners = sorted({(move.axis, move.flip) for move in moves})
    body_kernel = kernel
    if moves:
        params = {"collective_id": ident, "has_side_effects": True}
        scratch += [pltpu.SemaphoreType.DMA((len(moves),))] * 2

        def body_kernel(*refs):
            ins, refs = refs[:fixed_in], refs[fixed_in:]
            sent, refs = refs[: len(sources)], refs[len(sources) :]
            results, refs = refs[:fixed_out], refs[fixed_out:]
            landed, refs = refs[: len(moves)], refs[len(moves) :]
            rest, (send_sem, recv_sem) = refs[:-2], refs[-2:]

            def target(axis, flip):
                return {axis: flipped(lax.axis_index(axis), flip, lax.axis_size(axis))}

            def made(k):
                move = moves[k]
                return pltpu.make_async_remote_copy(
                    src_ref=move.take(sent[number[k]]),
                    dst_ref=landed[k],
                    send_sem=send_sem.at[k],
                    recv_sem=recv_sem.at[k],
                    device_id=target(move.axis, move.flip),
                    device_id_type=pl.DeviceIdType.MESH,
                )

            def begin():
                barrier = pltpu.get_barrier_semaphore()
                for axis, flip in partners:
                    pl.semaphore_signal(
                        barrier, inc=1, device_id=target(axis, flip),
                        device_id_type=pl.DeviceIdType.MESH,
                    )
                pl.semaphore_wait(barrier, len(partners))
                for k in range(len(moves)):
                    made(k).start()

            def finish():
                for k in range(len(moves)):
                    made(k).wait()

            if grid is None:
                begin()
                kernel(*ins, *results, *rest)
                finish()
            else:
                pl.when(pl.program_id(0) == 0)(begin)
                kernel(*ins, *results, *rest)
                pl.when(pl.program_id(0) == pl.num_programs(0) - 1)(finish)

    result = pl.pallas_call(
        body_kernel,
        out_shape=list(outs) + [like(*m.shape, kind=m.source.dtype) for m in moves],
        in_specs=list(specs) + [ANY] * len(sources),
        out_specs=list(out_specs) + [ANY] * len(moves),
        scratch_shapes=scratch,
        compiler_params=pltpu.CompilerParams(vmem_limit_bytes=56 * 2**20, **params),
        cost_estimate=pl.CostEstimate(
            flops=int(flops),
            bytes_accessed=sum(o.size * o.dtype.itemsize for o in operands),
            transcendentals=0,
        ),
        **extra,
    )(*operands, *sources)
    return list(result[:fixed_out]), list(result[fixed_out:])


def nothing():
    return None


class Courier:
    def __init__(self, active):
        self.active, self.waiting, self.ident = active, [], 0

    def load(self, *jobs):
        self.waiting += jobs

    def run(self, kernel, outs, operands, specs, scratch, flops, **extra):
        jobs, self.waiting = self.waiting, []
        moves, ends = [], []
        for job, stage in jobs:
            moves += job.moves(stage)
            ends.append(len(moves))
        if moves:
            self.ident += 1
        results, arrived = call(
            kernel, outs, operands, specs, scratch, flops, moves=tuple(moves), ident=self.ident, **extra
        )
        start = 0
        for (job, stage), end in zip(jobs, ends):
            job.absorb(stage, arrived[start:end])
            start = end
        return results


class Exchange:
    def __init__(self, pieces):
        self.pieces = pieces

    def moves(self, stage):
        return [Move(one, one.shape, "blk", k) for k, one in enumerate(self.pieces) if k]

    def absorb(self, stage, arrived):
        self.result = self.pieces[:1] + list(arrived)


class Gather:
    def __init__(self, tensor):
        self.tensor = tensor

    def moves(self, stage):
        return [
            Move(self.tensor, self.tensor.shape, "blk", k) for k in range(1, lax.axis_size("blk"))
        ]

    def absorb(self, stage, arrived):
        self.result = [self.tensor] + list(arrived)


class Norms:
    def __init__(self, tensor):
        self.tensor = tensor

    def moves(self, stage):
        axis = "rep" if stage == "out" else "blk"
        return [
            Move(self.tensor, self.tensor.shape, axis, k) for k in range(1, lax.axis_size(axis))
        ]

    def absorb(self, stage, arrived):
        for one in arrived:
            self.tensor = self.tensor + one


def body(
    patches,
    queries,
    window_valid,
    answer_length,
    norm_gain,
    norm_bias,
    attn_in,
    attn_out,
    mlp_in,
    mlp_out,
    cot_patches,
    cot_queries,
):
    x, q, cot_x, cot_q = patches[0], queries[0], cot_patches[0], cot_queries[0]
    rows, features = x.shape
    count = q.shape[0]
    hidden = mlp_in.shape[2]
    blocks = lax.axis_size("blk")
    place = lax.axis_index("blk").astype(jnp.int32)
    share = features // blocks
    hidden_share = hidden // blocks
    share_rows = -(-share // 16) * 16
    hidden_rows = -(-hidden_share // 16) * 16
    part = -(-count // (blocks * 16)) * 16
    padded = part * blocks
    wide = 3 * features
    last = wide + features + features
    causal_columns = -(-last // 512) * 512
    leader = (place == 0).astype(SINGLE)
    valid = jnp.where(jnp.repeat(window_valid[0], WIN) > 0, 0.0, MASKED).astype(SINGLE)
    carried = blocks == DIRECT and lax.axis_size("rep") == 4 and share % 32 == 0
    courier = Courier(carried)

    def own_columns(tensor):
        return lax.dynamic_slice_in_dim(tensor, place * share, share, 1)

    def own_rows(tensor):
        tensor = jnp.pad(tensor, ((0, padded - count), (0, 0)))
        return lax.dynamic_slice_in_dim(tensor, place * part, part, 0)

    square = 2.0 * features * features
    run = courier.run

    n0, pw, mw, x1, nx, vq, ckv = run(
        window_forward,
        [
            like(rows, features), like(rows, wide), like(rows, features),
            like(rows, features, kind=SINGLE), like(rows, features), like(rows, features),
            like(rows, 2 * features),
        ],
        [x, norm_gain, norm_bias, attn_in, attn_out],
        [VMEM, VMEM, VMEM, ANY, ANY],
        [((features, wide), NARROW), ((features, features), NARROW),
         ((features, features), NARROW), ((features, 2 * features), NARROW)],
        rows * square * 9,
        semaphores=4,
    )
    n1, pq, mq, q1, nq, cq, vkv, log_q = run(
        causal_forward,
        [
            like(count, features), like(count, wide), like(count, features),
            like(count, features, kind=SINGLE), like(count, features), like(count, features),
            like(count, 2 * features), like(16, count, kind=SINGLE),
        ],
        [q, norm_gain, norm_bias, attn_in, attn_out],
        [VMEM, VMEM, VMEM, ANY, ANY],
        [((features, wide), NARROW), ((features, features), NARROW),
         ((features, features), NARROW), ((features, 2 * features), NARROW),
         ((count, PAIR), SINGLE)],
        count * square * 15,
        semaphores=4,
    )
    pieces = run(
        functools.partial(cross_forward, blocks),
        [like(part, features)] * blocks + [like(part, PAIR, kind=SINGLE)] * blocks,
        [cq, ckv, valid[None, :]],
        [VMEM, VMEM, VMEM],
        [((padded, features), NARROW), ((padded, PAIR), SINGLE)],
        count * square * 6,
    )
    outs, logs = Exchange(pieces[:blocks]), Exchange(pieces[blocks:])
    if carried:
        courier.load((outs, ""), (logs, ""))
    mv, x2, log_v = run(
        reverse_forward,
        [like(rows, features), like(rows, features, kind=SINGLE), like(16, rows, kind=SINGLE)],
        [answer_length, vq, vkv, x1, attn_out],
        [SMEM, VMEM, VMEM, VMEM, ANY],
        [((features, features), NARROW), ((rows, PAIR), SINGLE)],
        rows * square * 8,
        semaphores=1,
    )
    if not carried:
        outs.result, logs.result = exchange(outs.pieces), exchange(logs.pieces)
    merged = run(
        functools.partial(merge_blocks, blocks),
        [like(part, features), like(part, PAIR, kind=SINGLE)],
        outs.result + logs.result,
        [VMEM] * (2 * blocks),
        [],
        padded * square,
    )
    co_parts, log_parts = Gather(merged[0]), Gather(merged[1])
    if carried:
        courier.load((co_parts, ""), (log_parts, ""))
    else:
        co_parts.result, log_parts.result = gather(merged[0]), gather(merged[1])
    fixed = lambda *shape: pl.BlockSpec(shape, lambda j: (0,) * len(shape))
    x3, dx2, up_x, down_x, norm_five = run(
        patch_feed_forward,
        [
            like(rows, features), like(rows, features, kind=SINGLE), like(features, hidden),
            like(hidden, features), like(8, features, kind=SINGLE),
        ],
        [x2, cot_x, norm_gain, norm_bias, mlp_in, mlp_out],
        [
            fixed(rows, features), fixed(rows, features), fixed(6, features), fixed(6, features),
            pl.BlockSpec((1, features, CHUNK), lambda j: (0, 0, j)),
            pl.BlockSpec((1, CHUNK, features), lambda j: (0, j, 0)),
        ],
        [((rows, features), NARROW), ((rows, CHUNK), NARROW), ((rows, CHUNK), NARROW),
         ((rows, features), SINGLE), ((rows, features), SINGLE)],
        rows * square * 24,
        grid=(hidden // CHUNK,),
        out_specs=[
            fixed(rows, features), fixed(rows, features),
            pl.BlockSpec((features, CHUNK), lambda j: (0, j)),
            pl.BlockSpec((CHUNK, features), lambda j: (j, 0)),
            fixed(8, features),
        ],
    )
    if carried:
        up_x, down_x = Reduction(up_x), Reduction(down_x)
        courier.load((up_x, "core"), (down_x, "core"))
    dvq, reverse_weight, *kv_pieces = run(
        functools.partial(reverse_backward, blocks),
        [like(rows, features), like(features, 2 * features)] + [like(part, 2 * features)] * blocks,
        [answer_length, dx2, mv, vq, vkv, nx, log_v, attn_out],
        [SMEM, VMEM, VMEM, VMEM, VMEM, VMEM, VMEM, ANY],
        [((features, features), NARROW), ((rows, features), NARROW), ((rows, features), NARROW),
         ((16, rows), SINGLE), ((padded, 2 * features), SINGLE)],
        rows * square * 16,
        semaphores=1,
    )
    kv_parts = Exchange(kv_pieces)
    if carried:
        reverse_weight = Reduction(reverse_weight)
        courier.load((up_x, "x"), (down_x, "x"), (reverse_weight, "core"), (kv_parts, ""))
    else:
        kv_parts.result = exchange(kv_pieces)
    q3, dq2, up_q, down_q, norm_four, co = run(
        functools.partial(query_feed_forward, blocks, share, hidden_share),
        [
            like(count, features), like(count, features, kind=SINGLE), like(share_rows, hidden),
            like(hidden_rows, features), like(8, features, kind=SINGLE), like(padded, features),
        ],
        [q1, cot_q, norm_gain, norm_bias, attn_out, mlp_in, mlp_out] + co_parts.result,
        [
            fixed(count, features), fixed(count, features), fixed(6, features),
            fixed(6, features), pl.BlockSpec((1, features, features), lambda j: (2, 0, 0)),
            pl.BlockSpec((1, features, CHUNK), lambda j: (1, 0, j)),
            pl.BlockSpec((1, CHUNK, features), lambda j: (1, j, 0)),
        ] + [fixed(part, features)] * blocks,
        [((count, features), SINGLE), ((count, features), NARROW), ((share_rows, count), NARROW),
         ((count, CHUNK), NARROW), ((count, CHUNK), NARROW),
         ((count, features), SINGLE), ((count, features), SINGLE)],
        count * square * 18,
        grid=(hidden // CHUNK,),
        out_specs=[
            fixed(count, features), fixed(count, features),
            pl.BlockSpec((share_rows, CHUNK), lambda j: (0, j)),
            fixed(hidden_rows, features), fixed(8, features), fixed(padded, features),
        ],
    )
    if carried:
        up_q, down_q = RepSum(up_q, 1), RepSum(down_q, 0)
        courier.load(
            (up_x, "y"), (down_x, "y"), (reverse_weight, "x"), (up_q, "out"), (down_q, "out")
        )
    dckv, cross_out_weight, *q_pieces = run(
        functools.partial(cross_backward, blocks, share),
        [like(rows, 2 * features), like(share_rows, features)] + [like(part, features)] * blocks,
        [dq2, co, cq, ckv, valid[:, None], attn_out] + log_parts.result,
        [VMEM, VMEM, VMEM, VMEM, VMEM, ANY] + [VMEM] * blocks,
        [((features, features), NARROW), ((count, features), NARROW), ((count, features), NARROW),
         ((16, count), SINGLE), ((padded, PAIR), SINGLE), ((16, count), SINGLE),
         ((padded, features), NARROW), ((rows, 2 * features), SINGLE)],
        count * square * 12,
        semaphores=1,
    )
    q_parts = Exchange(q_pieces)
    if carried:
        courier.load((q_parts, ""), (reverse_weight, "y"), (up_q, "back"), (down_q, "back"))
    else:
        q_parts.result = exchange(q_pieces)
    kv_weight, dx1, norm_three = run(
        patch_cross_backward,
        [
            like(features, 2 * features), like(rows, features, kind=SINGLE),
            like(8, features, kind=SINGLE),
        ],
        [dx2, x1, nx, dvq, dckv, norm_gain, attn_in],
        [VMEM] * 6 + [ANY],
        [((features, features), NARROW), ((features, 2 * features), NARROW)],
        rows * square * 12,
        semaphores=2,
    )
    dq1_share, share_weight, norm_two = run(
        functools.partial(share_backward, blocks),
        [like(part, features), like(features, wide), like(8, features, kind=SINGLE)],
        [own_rows(q1), own_rows(nq), norm_gain, attn_in] + q_parts.result + kv_parts.result,
        [VMEM, VMEM, VMEM, ANY] + [VMEM] * (2 * blocks),
        [((features, features), NARROW), ((features, 2 * features), NARROW),
         ((part, wide), NARROW)],
        part * square * 6,
        semaphores=2,
    )
    dq1_parts = Gather(dq1_share)
    if carried:
        kv_weight, share_weight = Reduction(kv_weight), Reduction(share_weight)
        courier.load(
            (dq1_parts, ""), (up_x, "z"), (down_x, "z"), (reverse_weight, "z"),
            (kv_weight, "core"), (share_weight, "core"),
        )
    else:
        dq1_parts.result = gather(dq1_share)
    window_weight, grad_x, norm_zero = run(
        window_backward,
        [
            like(features, 4 * features), like(rows, features, kind=SINGLE),
            like(8, features, kind=SINGLE),
        ],
        [x, dx1, n0, pw, mw, norm_gain, attn_in, attn_out],
        [VMEM] * 6 + [ANY, ANY],
        [((features, wide), NARROW), ((features, features), NARROW),
         ((rows, features), NARROW), ((rows, features), NARROW),
         ((16, rows), SINGLE), ((rows, wide), NARROW)],
        rows * square * 16,
        semaphores=2,
    )
    if carried:
        window_weight = Reduction(window_weight)
        courier.load(
            (window_weight, "core"), (kv_weight, "x"), (share_weight, "y"),
            (up_x, "back_x"), (down_x, "back_x"), (reverse_weight, "back_x"),
        )
    causal_weight, grad_q, norm_one = run(
        functools.partial(causal_backward, blocks, share),
        [
            like(share_rows, causal_columns), like(count, features, kind=SINGLE),
            like(8, features, kind=SINGLE),
        ],
        [q, dq2, n1, pq, mq, log_q, cross_out_weight, norm_gain, attn_in, attn_out]
        + dq1_parts.result,
        [VMEM] * 8 + [ANY, ANY] + [VMEM] * blocks,
        [((features, wide), NARROW), ((features, features), NARROW), ((padded, features), NARROW),
         ((count, features), SINGLE), ((count, features), NARROW), ((count, features), NARROW),
         ((16, count), SINGLE), ((count, 2 * PAIR), SINGLE), ((count, wide), NARROW)],
        count * square * 16,
        semaphores=2,
    )
    norms = jnp.stack(
        (
            norm_zero[0], norm_one[0] * leader, norm_two[0], norm_three[0], norm_four[0] * leader,
            norm_five[0], norm_zero[1], norm_one[1] * leader, norm_two[1], norm_three[1],
            norm_four[1] * leader, norm_five[1],
        )
    )
    if carried:
        norms = Norms(jnp.pad(norms, ((0, 4), (0, 0))))
        causal_weight = RepSum(causal_weight, 1)
        arrive = lambda *jobs: (courier.load(*jobs), run(nothing, [], [], [], [], 0))
        arrive(
            (window_weight, "x"), (share_weight, "x"), (kv_weight, "y"), (norms, "out"),
            (causal_weight, "out"), (up_x, "back_core"), (down_x, "back_core"),
            (reverse_weight, "back_core"),
        )
        arrive(
            (window_weight, "y"), (share_weight, "z"), (kv_weight, "z"), (norms, "back"),
            (causal_weight, "back"),
        )
        arrive((window_weight, "z"), (share_weight, "back_x"), (kv_weight, "back_x"))
        arrive((window_weight, "back_x"), (share_weight, "back_core"), (kv_weight, "back_core"))
        arrive((window_weight, "back_core"))
        up_x, down_x, reverse_weight, window_weight, kv_weight, share_weight, causal_weight = (
            one.tensor
            for one in (
                up_x, down_x, reverse_weight, window_weight, kv_weight, share_weight, causal_weight
            )
        )
        up_q, down_q, norms = up_q.tensor, down_q.tensor, norms.tensor[:12]
    else:
        up_x, down_x, reverse_weight, window_weight, kv_weight, share_weight = (
            reduce_all(one)
            for one in (up_x, down_x, reverse_weight, window_weight, kv_weight, share_weight)
        )
        up_q, down_q = reduce_rep(up_q[:share]), reduce_rep(down_q[:hidden_share])
        causal_weight = reduce_rep(causal_weight[:share])
        norms = lax.psum(norms, ("blk", "rep"))
    norms = own_columns(norms)
    grad_attn_in = jnp.stack(
        (
            window_weight[:, :wide],
            causal_weight[:, :wide],
            jnp.concatenate((share_weight[:, :features], kv_weight), axis=1),
            jnp.concatenate((reverse_weight[:, :features], share_weight[:, features:]), axis=1),
        )
    )
    grad_attn_out = jnp.stack(
        (
            window_weight[:, wide:],
            causal_weight[:, wide : wide + features],
            causal_weight[:, wide + features : last],
            reverse_weight[:, features:],
        )
    )
    return (
        x3[None],
        own_columns(q3)[None],
        grad_x[None],
        own_columns(grad_q)[None],
        norms[:6],
        norms[6:],
        grad_attn_in.astype(SINGLE),
        grad_attn_out.astype(SINGLE),
        jnp.stack((up_x, up_q)).astype(SINGLE),
        jnp.stack((down_x, down_q)).astype(SINGLE),
    )


def solution(mesh):
    placed = (
        P("rep", "blk", None),
        P("rep", None, None),
        P("rep", "blk"),
        P("rep"),
        P(),
        P(),
        P(),
        P(),
        P(),
        P(),
        P("rep", "blk", None),
        P("rep", None, None),
    )
    return jax.shard_map(
        body,
        mesh=mesh,
        in_specs=placed,
        out_specs=(
            P("rep", "blk", None),
            P("rep", None, "blk"),
            P("rep", "blk", None),
            P("rep", None, "blk"),
            P(None, "blk"),
            P(None, "blk"),
            P(None, "blk", None),
            P(None, "blk", None),
            P(None, "blk", None),
            P(None, "blk", None),
        ),
        check_vma=False,
    )
```

```python
import functools
import math

import jax
import jax.numpy as jnp
from jax import lax
from jax.experimental import pallas as pl
from jax.experimental.pallas import tpu as pltpu
from jax.sharding import PartitionSpec as P

HEADS = 12
WIN = 64
EPSILON = 1e-05
MASKED = -1e30
NARROW = jnp.bfloat16
SINGLE = jnp.float32
EXACT = lax.Precision.HIGHEST
GROUP = 128
WINDOWS = 256
PAIR = 128
HEAD = 64
STRIP = 160
LONG = 400
CHUNK = 768


def dot(former, latter, ahead, behind, precision=None):
    return lax.dot_general(
        former,
        latter,
        (((ahead,), (behind,)), ((), ())),
        preferred_element_type=SINGLE,
        precision=precision,
    )


def plain(former, latter):
    return dot(former, latter, 1, 0)


def right_t(former, latter):
    return dot(former, latter, 1, 1)


def left_t(former, latter):
    return dot(former, latter, 0, 0)


def loop(count, action):
    def step(index, nothing):
        action(index)
        return nothing

    lax.fori_loop(0, count, step, 0)


def at(index, size):
    return pl.ds(pl.multiple_of(index * size, size), size)


def iota(shape, dim):
    return lax.broadcasted_iota(jnp.int32, shape, dim)


def statistics(tensor):
    average = jnp.mean(tensor, axis=-1, keepdims=True)
    centred = tensor - average
    spread = jnp.mean(centred * centred, axis=-1, keepdims=True)
    return centred, lax.rsqrt(spread + EPSILON)


def norm(tensor, gain, bias):
    centred, inverse = statistics(tensor)
    return centred * inverse * gain + bias


def norm_back(tensor, gain, upstream):
    centred, inverse = statistics(tensor)
    scaled = centred * inverse
    inner = upstream * gain
    grad = inverse * (
        inner
        - jnp.mean(inner, axis=-1, keepdims=True)
        - scaled * jnp.mean(inner * scaled, axis=-1, keepdims=True)
    )
    return (
        grad,
        jnp.sum(upstream * scaled, axis=0, keepdims=True),
        jnp.sum(upstream, axis=0, keepdims=True),
    )


def gelu_both(tensor):
    size = jnp.abs(tensor)
    ratio = 1.0 / (1.0 + (0.3275911 * math.sqrt(0.5)) * size)
    series = ratio * (
        0.254829592
        + ratio * (-0.284496736 + ratio * (1.421413741 + ratio * (-1.453152027 + ratio * 1.061405429)))
    )
    bell = jnp.exp(-0.5 * (tensor * tensor))
    tail = 0.5 * series * bell
    below = jnp.where(tensor >= 0, 1.0 - tail, tail)
    return tensor * below, below + tensor * bell * (1.0 / math.sqrt(2.0 * math.pi))


def half(which, value=1.0):
    return jnp.where(iota((1, PAIR), 1) // HEAD == which, value, 0.0).astype(NARROW)


def lower_lanes():
    return iota((1, PAIR), 1) < HEAD


def both(tensor, value=1.0):
    return jnp.concatenate((tensor * half(0, value), tensor * half(1, value)), axis=0)


def attend(queries, keys, values, mask):
    rows = queries.shape[0]
    scores = right_t(both(queries, 1.0 / math.sqrt(HEAD)), keys)
    weights, totals, logs = [], [], []
    for which in range(2):
        part = mask(scores[which * rows : (which + 1) * rows])
        peak = jnp.max(part, axis=-1, keepdims=True)
        part = jnp.exp(part - peak)
        total = jnp.sum(part, axis=-1, keepdims=True)
        weights.append(part.astype(NARROW))
        totals.append(1.0 / total)
        logs.append(peak + jnp.log(total))
    out = plain(jnp.concatenate(weights, axis=0), values)
    return jnp.where(lower_lanes(), out[:rows] * totals[0], out[rows:] * totals[1]), logs


def attend_back(queries, keys, values, upstream, logs, deltas, mask):
    scaled = queries * jnp.asarray(1.0 / math.sqrt(HEAD), NARROW)
    count = keys.shape[0]
    keys = both(keys)
    turned_keys = keys.T
    scores = right_t(keys, scaled)
    inner = right_t(both(values), upstream)
    weights, slopes = [], []
    for which in range(2):
        span = slice(which * count, (which + 1) * count)
        part = mask(scores[span])
        if logs is None:
            part = jnp.exp(part - jnp.max(part, axis=0, keepdims=True))
            part = part * (1.0 / jnp.sum(part, axis=0, keepdims=True))
        else:
            part = jnp.exp(part - logs[which])
        weights.append(part.astype(NARROW))
        slopes.append((part * (inner[span] - deltas[which])).astype(NARROW))
    slope = jnp.concatenate(slopes, axis=0)
    query_grad = plain(turned_keys, slope).T
    key_grad = plain(slope, scaled)
    value_grad = plain(jnp.concatenate(weights, axis=0), upstream)
    lanes = lower_lanes()
    return (
        query_grad,
        jnp.where(lanes, key_grad[:count], key_grad[count:]),
        jnp.where(lanes, value_grad[:count], value_grad[count:]),
    )


def head_rows(tensor):
    features = tensor.shape[1]
    heads = 16
    chosen = jnp.where(
        iota((heads, features), 1) // HEAD == iota((heads, features), 0), 1.0, 0.0
    ).astype(SINGLE)
    return dot(chosen, tensor, 1, 1, EXACT)


def turn(columns):
    same = jnp.where(iota((16, columns.shape[1]), 0) == iota((16, columns.shape[1]), 1), 1.0, 0.0)
    return dot(same.astype(SINGLE), columns, 1, 1, EXACT)


def row_pair(ref, pair, span):
    tensor = ref[:, span]
    index = iota(tensor.shape, 0)
    return [
        jnp.sum(jnp.where(index == 2 * pair + which, tensor, 0.0), axis=0, keepdims=True)
        for which in range(2)
    ]


def chooser(rows, width, start, count):
    row = iota((rows, width), 0)
    hit = jnp.logical_and(iota((rows, width), 1) == row + start, row < count)
    return jnp.where(hit, 1.0, 0.0).astype(NARROW)


def spans(rows, size):
    edges = [(start, min(start + size, rows)) for start in range(0, rows, size)]
    if len(edges) > 1 and edges[-1][1] - edges[-1][0] < PAIR:
        edges[-2:] = [(edges[-2][0], rows)]
    return edges


def mark(log_ref, rows, head, value):
    log_ref[rows, :] = jnp.where(iota((1, PAIR), 1) == head, value, log_ref[rows, :])


def store_rows(ref, columns, value):
    ref[(slice(None),) * (len(ref.shape) - 1) + (columns,)] = value.astype(ref.dtype).reshape(
        ref.shape[:-1] + value.shape[1:]
    )


def nothing(*unused):
    return None


def copies(semaphores, *pairs):
    made = [
        pltpu.make_async_copy(source, target, semaphores.at[k])
        for k, (source, target) in enumerate(pairs)
    ]
    for one in made:
        one.start()
    return made


DIRECT = 8


def place_of(axis="blk"):
    return lax.axis_index(axis)


def flipped(index, mask, count):
    total, weight = 0, 1
    while weight < count:
        bit = (index // weight) % 2
        total = total + weight * ((1 - bit) if mask & weight else bit)
        weight *= 2
    return total


def piece_at(number, count):
    return flipped(place_of(), number, count) if count <= DIRECT else number


def window_forward(
    x_ref, gain_ref, bias_ref, a_in, a_out,
    n0_ref, pw_ref, mw_ref, x1_ref, nx_ref, vq_ref, ckv_ref,
    w_in, w_out, w_q, w_kv, sem,
):
    rows, features = x_ref.shape
    loads = copies(
        sem,
        (a_in.at[0], w_in),
        (a_out.at[0], w_out),
        (a_in.at[3, :, pl.ds(0, features)], w_q),
        (a_in.at[2, :, pl.ds(features, 2 * features)], w_kv),
    )

    def first(i):
        span = at(i, GROUP)
        n0_ref[span, :] = norm(
            x_ref[span, :].astype(SINGLE), gain_ref[0:1, :], bias_ref[0:1, :]
        ).astype(NARROW)

    loop(rows // GROUP, first)
    loads[0].wait()

    def project(j):
        span = at(j, CHUNK)
        pw_ref[:, span] = plain(n0_ref[...], w_in[:, span]).astype(NARROW)

    loop(3 * features // CHUNK, project)
    window = jnp.where(
        iota((WINDOWS, WINDOWS), 0) // WIN == iota((WINDOWS, WINDOWS), 1) // WIN, 0.0, MASKED
    )

    def group(i):
        span = at(i, WINDOWS)
        for pair in range(features // PAIR):
            lane = pair * PAIR
            out, unused = attend(
                pw_ref[span, lane : lane + PAIR],
                pw_ref[span, features + lane : features + lane + PAIR],
                pw_ref[span, 2 * features + lane : 2 * features + lane + PAIR],
                lambda scores: scores + window,
            )
            mw_ref[span, lane : lane + PAIR] = out.astype(NARROW)

    loop(rows // WINDOWS, group)
    loads[1].wait()

    def second(i):
        span = at(i, GROUP)
        total = x_ref[span, :].astype(SINGLE) + plain(mw_ref[span, :], w_out[...])
        x1_ref[span, :] = total
        nx_ref[span, :] = norm(total, gain_ref[3:4, :], bias_ref[3:4, :]).astype(NARROW)

    loop(rows // GROUP, second)
    loads[2].wait()
    vq_ref[...] = plain(nx_ref[...], w_q[...]).astype(NARROW)
    loads[3].wait()

    def third(j):
        span = at(j, CHUNK)
        ckv_ref[:, span] = plain(nx_ref[...], w_kv[:, span]).astype(NARROW)

    loop(2 * features // CHUNK, third)


def causal_forward(
    q_ref, gain_ref, bias_ref, a_in, a_out,
    n1_ref, pq_ref, mq_ref, q1_ref, nq_ref, cq_ref, vkv_ref, log_ref,
    w_in, w_out, w_q, w_kv, logs, sem,
):
    rows, features = q_ref.shape
    loads = copies(
        sem,
        (a_in.at[1], w_in),
        (a_out.at[1], w_out),
        (a_in.at[2, :, pl.ds(0, features)], w_q),
        (a_in.at[3, :, pl.ds(features, 2 * features)], w_kv),
    )

    def first(i):
        span = at(i, STRIP)
        n1_ref[span, :] = norm(
            q_ref[span, :].astype(SINGLE), gain_ref[1:2, :], bias_ref[1:2, :]
        ).astype(NARROW)

    loop(rows // STRIP, first)
    loads[0].wait()

    def project(j):
        span = at(j, CHUNK)
        pq_ref[:, span] = plain(n1_ref[...], w_in[:, span]).astype(NARROW)

    loop(3 * features // CHUNK, project)
    logs[...] = jnp.zeros_like(logs)

    def pair(p):
        for start in range(0, rows, LONG):
            end = min(start + LONG, rows)

            def mask(scores, start=start):
                shape = scores.shape
                return jnp.where(iota(shape, 1) <= iota(shape, 0) + start, scores, MASKED)

            out, sums = attend(
                pq_ref[start:end, at(p, PAIR)],
                pq_ref[0:end, at(p + features // PAIR, PAIR)],
                pq_ref[0:end, at(p + 2 * features // PAIR, PAIR)],
                mask,
            )
            mq_ref[start:end, at(p, PAIR)] = out.astype(NARROW)
            for which in range(2):
                mark(logs, slice(start, end), 2 * p + which, sums[which])

    loop(features // PAIR, pair)
    log_ref[...] = turn(logs[...])
    loads[1].wait()

    def second(i):
        span = at(i, STRIP)
        total = q_ref[span, :].astype(SINGLE) + plain(mq_ref[span, :], w_out[...])
        q1_ref[span, :] = total
        nq_ref[span, :] = norm(total, gain_ref[2:3, :], bias_ref[2:3, :]).astype(NARROW)

    loop(rows // STRIP, second)
    loads[2].wait()
    cq_ref[...] = plain(nq_ref[...], w_q[...]).astype(NARROW)
    loads[3].wait()

    def third(j):
        span = at(j, CHUNK)
        vkv_ref[:, span] = plain(nq_ref[...], w_kv[:, span]).astype(NARROW)

    loop(2 * features // CHUNK, third)


def cross_forward(pieces, cq_ref, ckv_ref, valid_ref, whole, *rest):
    log_refs, (logs,) = rest[:pieces], rest[pieces:]
    rows, features = cq_ref.shape
    part = log_refs[0].shape[1]
    logs[...] = jnp.zeros_like(logs)
    if whole.shape[0] > rows:
        whole[rows:, :] = jnp.zeros((whole.shape[0] - rows, features), NARROW)

    def pair(p):
        for start in range(0, rows, LONG):
            span = slice(start, min(start + LONG, rows))
            out, sums = attend(
                cq_ref[span, at(p, PAIR)],
                ckv_ref[:, at(p, PAIR)],
                ckv_ref[:, at(p + features // PAIR, PAIR)],
                lambda scores: scores + valid_ref[...],
            )
            whole[span, at(p, PAIR)] = out.astype(NARROW)
            for which in range(2):
                mark(logs, span, 2 * p + which, sums[which])

    loop(features // PAIR, pair)
    for k in range(pieces):
        log_refs[k][...] = turn(logs[at(piece_at(k, pieces), part), :])


def untwist(rows):
    same = jnp.where(iota((16, PAIR), 0) == iota((16, PAIR), 1), 1.0, 0.0)
    return dot(rows, same.astype(SINGLE), 0, 0, EXACT)


def merge_blocks(pieces, own_ref, *refs):
    logs, refs = refs[:pieces], refs[pieces:]
    halves, (co_ref, log_ref) = (refs[: pieces - 1], refs[pieces - 1 : -2]), refs[-2:]
    part, features = co_ref.shape
    width = features // 2
    peak = functools.reduce(jnp.maximum, [one[...] for one in logs])
    total = peak + jnp.log(functools.reduce(jnp.add, [jnp.exp(one[...] - peak) for one in logs]))
    log_ref[...] = total
    spread = jnp.where(
        iota((PAIR, features), 1) // HEAD == iota((PAIR, features), 0), 1.0, 0.0
    ).astype(NARROW)
    result = jnp.zeros(co_ref.shape, SINGLE)
    for k in range(pieces):
        weight = untwist(jnp.exp(logs[k][...] - total))
        high = weight.astype(NARROW)
        low = (weight - high.astype(SINGLE)).astype(NARROW)
        if k == 0:
            block = own_ref[at(place_of(), part), :]
        else:
            block = jnp.concatenate((halves[0][k - 1][...], halves[1][k - 1][...]), axis=1)
        result = result + (plain(high, spread) + plain(low, spread)) * block.astype(SINGLE)
    co_ref[...] = result.astype(NARROW)


def reverse_forward(
    length_ref, vq_ref, vkv_ref, x1_ref, a_out,
    mv_ref, x2_ref, log_ref,
    w_out, logs, sem,
):
    rows, features = vq_ref.shape
    keys = vkv_ref.shape[0]
    (load,) = copies(sem, (a_out.at[3], w_out))
    logs[...] = jnp.zeros_like(logs)
    bias = jnp.where(iota((1, keys), 1) < length_ref[0], 0.0, MASKED)

    def pair(p):
        for start in range(0, rows, WINDOWS):
            span = slice(start, start + WINDOWS)
            out, sums = attend(
                vq_ref[span, at(p, PAIR)],
                vkv_ref[:, at(p, PAIR)],
                vkv_ref[:, at(p + features // PAIR, PAIR)],
                lambda scores: scores + bias,
            )
            mv_ref[span, at(p, PAIR)] = out.astype(NARROW)
            for which in range(2):
                mark(logs, span, 2 * p + which, sums[which])

    loop(features // PAIR, pair)
    log_ref[...] = turn(logs[...])
    load.wait()

    def second(i):
        span = at(i, GROUP)
        x2_ref[span, :] = x1_ref[span, :] + plain(mv_ref[span, :], w_out[...])

    loop(rows // GROUP, second)


def feed_forward_step(block, normed, up, down, cot, hidden, slope, out, grad):
    rows = normed.shape[0]

    def strip(i):
        span = at(i, block)
        value, rise = gelu_both(plain(normed[span, :], up[...]))
        hidden[span, :] = value.astype(NARROW)
        slope[span, :] = (right_t(cot[span, :], down[...]) * rise).astype(NARROW)
        out[span, :] += plain(hidden[span, :], down[...])
        grad[span, :] += right_t(slope[span, :], up[...])

    loop(rows // block, strip)


def patch_feed_forward(
    x2_ref, cot_ref, gain_ref, bias_ref, up_ref, down_ref,
    x3_ref, dx2_ref, up_grad_ref, down_grad_ref, norm_ref,
    normed, hidden, slope, out, grad,
):
    rows = x2_ref.shape[0]
    step = pl.program_id(0)

    @pl.when(step == 0)
    def begin():
        def first(i):
            span = at(i, GROUP)
            normed[span, :] = norm(
                x2_ref[span, :], gain_ref[5:6, :], bias_ref[5:6, :]
            ).astype(NARROW)
            out[span, :] = x2_ref[span, :]
            grad[span, :] = jnp.zeros_like(grad[span, :])

        loop(rows // GROUP, first)

    feed_forward_step(
        512, normed, up_ref.at[0], down_ref.at[0], cot_ref, hidden, slope, out, grad
    )
    up_grad_ref[...] = left_t(normed[...], slope[...]).astype(NARROW)
    down_grad_ref[...] = left_t(hidden[...], cot_ref[...]).astype(NARROW)

    @pl.when(step == pl.num_programs(0) - 1)
    def finish():
        norm_ref[...] = jnp.zeros_like(norm_ref)

        def last(i):
            span = at(i, GROUP)
            x3_ref[span, :] = out[span, :].astype(NARROW)
            part, gain, bias = norm_back(x2_ref[span, :], gain_ref[5:6, :], grad[span, :])
            dx2_ref[span, :] = cot_ref[span, :].astype(SINGLE) + part
            norm_ref[0:1, :] += gain
            norm_ref[1:2, :] += bias

        loop(rows // GROUP, last)


def query_feed_forward(
    pieces, share, hidden_share, q1_ref, cot_ref, gain_ref, bias_ref,
    w_out, up_ref, down_ref, *rest,
):
    parts, rest = rest[:pieces], rest[pieces:]
    (
        q3_ref, dq2_ref, up_grad_ref, down_grad_ref, norm_ref, co_ref,
        q2, normed, chosen, hidden, slope, out, grad,
    ) = rest
    rows, features = q1_ref.shape
    part = parts[0].shape[0]
    width = up_ref.shape[2]
    step = pl.program_id(0)

    @pl.when(step == 0)
    def begin():
        for k in range(pieces):
            co_ref[at(piece_at(k, pieces), part), :] = parts[k][...]

        def first(i):
            span = at(i, STRIP)
            total = q1_ref[span, :] + plain(co_ref[span, :], w_out[0])
            q2[span, :] = total
            out[span, :] = total
            normed[span, :] = norm(total, gain_ref[4:5, :], bias_ref[4:5, :]).astype(NARROW)
            grad[span, :] = jnp.zeros_like(grad[span, :])

        loop(rows // STRIP, first)
        chosen[...] = right_t(
            chooser(chosen.shape[0], features, place_of() * share, share), normed[...]
        ).astype(NARROW)

    feed_forward_step(
        LONG, normed, up_ref.at[0], down_ref.at[0], cot_ref, hidden, slope, out, grad
    )
    up_grad_ref[...] = plain(chosen[...], slope[...]).astype(NARROW)
    begins = place_of() * hidden_share

    @pl.when(begins // width == step)
    def own_hidden():
        taken = right_t(
            chooser(down_grad_ref.shape[0], width, begins - step * width, hidden_share),
            hidden[...],
        ).astype(NARROW)
        down_grad_ref[...] = plain(taken, cot_ref[...]).astype(NARROW)

    @pl.when(step == pl.num_programs(0) - 1)
    def finish():
        norm_ref[...] = jnp.zeros_like(norm_ref)

        def last(i):
            span = at(i, STRIP)
            q3_ref[span, :] = out[span, :].astype(NARROW)
            piece, gain, bias = norm_back(q2[span, :], gain_ref[4:5, :], grad[span, :])
            dq2_ref[span, :] = cot_ref[span, :].astype(SINGLE) + piece
            norm_ref[0:1, :] += gain
            norm_ref[1:2, :] += bias

        loop(rows // STRIP, last)


def reverse_backward(
    pieces, length_ref, dx2_ref, mv_ref, vq_ref, vkv_ref, nx_ref, log_ref, a_out,
    *rest, launch=nothing,
):
    dvq_ref, weight_ref, rest = rest[0], rest[1], rest[2:]
    k_refs, v_refs, rest = rest[:pieces], rest[pieces : 2 * pieces], rest[2 * pieces :]
    w_out, rounded, dmv, deltas, dkv, sem = rest
    rows, features = vq_ref.shape
    keys = vkv_ref.shape[0]
    part = k_refs[0].shape[0]
    (load,) = copies(sem, (a_out.at[3], w_out))
    rounded[...] = dx2_ref[...].astype(NARROW)
    load.wait()
    dmv[...] = right_t(rounded[...], w_out[...]).astype(NARROW)
    store_rows(
        weight_ref, slice(features, 2 * features), left_t(mv_ref[...], rounded[...])
    )
    deltas[...] = head_rows(dmv[...].astype(SINGLE) * mv_ref[...].astype(SINGLE))
    if dkv.shape[0] > keys:
        dkv[keys:, :] = jnp.zeros((dkv.shape[0] - keys, 2 * features), SINGLE)
    size = 256

    def pair(p):
        for strip in range(rows // size):
            span = slice(strip * size, (strip + 1) * size)

            def mask(scores):
                return jnp.where(iota(scores.shape, 0) < length_ref[0], scores, MASKED)

            dq, dk, dv = attend_back(
                vq_ref[span, at(p, PAIR)],
                vkv_ref[:, at(p, PAIR)],
                vkv_ref[:, at(p + features // PAIR, PAIR)],
                dmv[span, at(p, PAIR)],
                row_pair(log_ref, p, span),
                row_pair(deltas, p, span),
                mask,
            )
            dvq_ref[span, at(p, PAIR)] = (dq * (1.0 / math.sqrt(HEAD))).astype(NARROW)
            if strip == 0:
                dkv[0:keys, at(p, PAIR)] = dk
                dkv[0:keys, at(p + features // PAIR, PAIR)] = dv
            else:
                dkv[0:keys, at(p, PAIR)] += dk
                dkv[0:keys, at(p + features // PAIR, PAIR)] += dv

    loop(features // PAIR, pair)
    store_rows(weight_ref, slice(0, features), left_t(nx_ref[...], dvq_ref[...]))
    launch(1)
    for k in range(pieces):
        span = at(piece_at(k, pieces), part)
        k_refs[k][...] = dkv[span, 0:features].astype(NARROW)
        v_refs[k][...] = dkv[span, features:].astype(NARROW)


def cross_backward(
    pieces, share, dq2_ref, co_ref, cq_ref, ckv_ref, valid_ref, a_out, *rest
):
    log_parts, rest = rest[:pieces], rest[pieces:]
    dckv_ref, weight_ref, rest = rest[0], rest[1], rest[2:]
    q_refs, (w_out, rounded, dco, deltas, logs, turned, dq_all, dkv, sem) = (
        rest[:pieces],
        rest[pieces:],
    )
    rows, features = cq_ref.shape
    part = log_parts[0].shape[1]
    (load,) = copies(sem, (a_out.at[2], w_out))
    for k in range(pieces):
        logs[at(piece_at(k, pieces), part), :] = untwist(log_parts[k][...])
    turned[...] = turn(logs[0:rows, :])
    rounded[...] = dq2_ref[...].astype(NARROW)
    load.wait()
    dco[...] = right_t(rounded[...], w_out[...]).astype(NARROW)
    taken = right_t(
        chooser(weight_ref.shape[0], features, place_of() * share, share), co_ref[0:rows, :]
    ).astype(NARROW)
    weight_ref[...] = plain(taken, rounded[...]).astype(NARROW)
    deltas[...] = head_rows(dco[...].astype(SINGLE) * co_ref[0:rows, :].astype(SINGLE))
    if dq_all.shape[0] > rows:
        dq_all[rows:, :] = jnp.zeros((dq_all.shape[0] - rows, features), NARROW)
    edges = spans(rows, 512)

    def pair(p):
        for number, (start, end) in enumerate(edges):
            span = slice(start, end)
            dq, dk, dv = attend_back(
                cq_ref[span, at(p, PAIR)],
                ckv_ref[:, at(p, PAIR)],
                ckv_ref[:, at(p + features // PAIR, PAIR)],
                dco[span, at(p, PAIR)],
                row_pair(turned, p, span),
                row_pair(deltas, p, span),
                lambda scores: scores + valid_ref[...],
            )
            dq_all[span, at(p, PAIR)] = (dq * (1.0 / math.sqrt(HEAD))).astype(NARROW)
            if number == 0:
                dkv[:, at(p, PAIR)] = dk
                dkv[:, at(p + features // PAIR, PAIR)] = dv
            else:
                dkv[:, at(p, PAIR)] += dk
                dkv[:, at(p + features // PAIR, PAIR)] += dv

    loop(features // PAIR, pair)
    dckv_ref[...] = dkv[...].astype(NARROW)
    for k in range(pieces):
        q_refs[k][...] = dq_all[at(piece_at(k, pieces), part), :]


def patch_backward(
    x_ref, dx2_ref, x1_ref, nx_ref, n0_ref, pw_ref, mw_ref, dvq_ref, dckv_ref, gain_ref, a_in, a_out,
    kv_weight_ref, weight_ref, grad_ref, norm_ref,
    w_in, w_out, w_q, w_kv, dx1, rounded, dmw, deltas, dpw, sem,
    launch=nothing,
):
    rows, features = x_ref.shape
    loads = copies(
        sem,
        (a_in.at[3, :, pl.ds(0, features)], w_q),
        (a_in.at[2, :, pl.ds(features, 2 * features)], w_kv),
        (a_out.at[0], w_out),
        (a_in.at[0], w_in),
    )
    norm_ref[...] = jnp.zeros_like(norm_ref)
    for start in range(0, 2 * features, CHUNK):
        span = slice(start, start + CHUNK)
        store_rows(kv_weight_ref, span, left_t(nx_ref[...], dckv_ref[:, span]))
    launch(0)
    loads[0].wait()
    loads[1].wait()

    def first(i):
        span = at(i, GROUP)
        upstream = right_t(dvq_ref[span, :], w_q[...]) + right_t(dckv_ref[span, :], w_kv[...])
        part, gain, bias = norm_back(x1_ref[span, :], gain_ref[3:4, :], upstream)
        total = dx2_ref[span, :] + part
        dx1[span, :] = total
        rounded[span, :] = total.astype(NARROW)
        norm_ref[0:1, :] += gain
        norm_ref[1:2, :] += bias

    loop(rows // GROUP, first)
    loads[2].wait()
    dmw[...] = right_t(rounded[...], w_out[...]).astype(NARROW)
    store_rows(
        weight_ref, slice(3 * features, 4 * features), left_t(mw_ref[...], rounded[...])
    )
    deltas[...] = head_rows(dmw[...].astype(SINGLE) * mw_ref[...].astype(SINGLE))
    window = jnp.where(
        iota((WINDOWS, WINDOWS), 0) // WIN == iota((WINDOWS, WINDOWS), 1) // WIN, 0.0, MASKED
    )

    def group(i):
        span = at(i, WINDOWS)
        for pair in range(features // PAIR):
            lane = pair * PAIR
            dq, dk, dv = attend_back(
                pw_ref[span, lane : lane + PAIR],
                pw_ref[span, features + lane : features + lane + PAIR],
                pw_ref[span, 2 * features + lane : 2 * features + lane + PAIR],
                dmw[span, lane : lane + PAIR],
                None,
                [deltas[2 * pair + w : 2 * pair + w + 1, span] for w in range(2)],
                lambda scores: scores + window,
            )
            dpw[span, lane : lane + PAIR] = (dq * (1.0 / math.sqrt(HEAD))).astype(NARROW)
            dpw[span, features + lane : features + lane + PAIR] = dk.astype(NARROW)
            dpw[span, 2 * features + lane : 2 * features + lane + PAIR] = dv.astype(NARROW)

    loop(rows // WINDOWS, group)
    for start in range(0, 3 * features, CHUNK):
        span = slice(start, start + CHUNK)
        store_rows(weight_ref, span, left_t(n0_ref[...], dpw[:, span]))
    launch(1)
    loads[3].wait()

    def last(i):
        span = at(i, GROUP)
        upstream = right_t(dpw[span, :], w_in[...])
        part, gain, bias = norm_back(x_ref[span, :].astype(SINGLE), gain_ref[0:1, :], upstream)
        grad_ref[span, :] = dx1[span, :] + part
        norm_ref[2:3, :] += gain
        norm_ref[3:4, :] += bias

    loop(rows // GROUP, last)


def share_backward(
    pieces, q1_ref, nq_ref, gain_ref, a_in, *rest, launch=nothing
):
    parts = [rest[k * pieces : (k + 1) * pieces] for k in range(3)]
    rest = rest[3 * pieces :]
    grad_ref, weight_ref, norm_ref, w_q, w_kv, summed, sem = rest
    features = q1_ref.shape[1]
    loads = copies(
        sem,
        (a_in.at[2, :, pl.ds(0, features)], w_q),
        (a_in.at[3, :, pl.ds(features, 2 * features)], w_kv),
    )
    for k in range(3):
        span = slice(k * features, (k + 1) * features)
        total = functools.reduce(jnp.add, [one[...].astype(SINGLE) for one in parts[k]])
        summed[:, span] = total.astype(NARROW)
        store_rows(weight_ref, span, left_t(nq_ref[...], summed[:, span]))
    launch(1)
    for load in loads:
        load.wait()
    upstream = right_t(summed[:, 0:features], w_q[...]) + right_t(summed[:, features:], w_kv[...])
    part, gain, bias = norm_back(q1_ref[...], gain_ref[2:3, :], upstream)
    grad_ref[...] = part.astype(NARROW)
    norm_ref[...] = jnp.zeros_like(norm_ref)
    norm_ref[0:1, :] = gain
    norm_ref[1:2, :] = bias


def causal_backward(
    pieces, share, q_ref, dq2_ref, n1_ref, pq_ref, mq_ref, log_ref, cross_ref, gain_ref,
    a_in, a_out, *rest
):
    parts, rest = rest[:pieces], rest[pieces:]
    (
        weight_ref, grad_ref, norm_ref,
        w_in, w_out, gathered, dq1, rounded, dmq, deltas, dkv, dpq, sem,
    ) = rest
    rows, features = q_ref.shape
    part = parts[0].shape[0]
    loads = copies(sem, (a_out.at[1], w_out), (a_in.at[1], w_in))
    for k in range(pieces):
        gathered[at(piece_at(k, pieces), part), :] = parts[k][...]

    def first(i):
        span = at(i, STRIP)
        total = dq2_ref[span, :] + gathered[span, :].astype(SINGLE)
        dq1[span, :] = total
        rounded[span, :] = total.astype(NARROW)

    loop(rows // STRIP, first)
    loads[0].wait()
    dmq[...] = right_t(rounded[...], w_out[...]).astype(NARROW)
    chosen = chooser(weight_ref.shape[0], features, place_of() * share, share)
    taken = right_t(chosen, mq_ref[...]).astype(NARROW)
    weight_ref[:, 3 * features : 4 * features] = plain(taken, rounded[...]).astype(NARROW)
    weight_ref[:, 4 * features : 5 * features] = cross_ref[...]
    weight_ref[:, 5 * features :] = jnp.zeros_like(weight_ref[:, 5 * features :])
    deltas[...] = head_rows(dmq[...].astype(SINGLE) * mq_ref[...].astype(SINGLE))
    edges = spans(rows, 256)

    def pair(p):
        for number, (start, end) in reversed(list(enumerate(edges))):
            span = slice(start, end)

            def mask(scores, start=start):
                shape = scores.shape
                return jnp.where(iota(shape, 0) <= iota(shape, 1) + start, scores, MASKED)

            dq, dk, dv = attend_back(
                pq_ref[span, at(p, PAIR)],
                pq_ref[0:end, at(p + features // PAIR, PAIR)],
                pq_ref[0:end, at(p + 2 * features // PAIR, PAIR)],
                dmq[span, at(p, PAIR)],
                row_pair(log_ref, p, span),
                row_pair(deltas, p, span),
                mask,
            )
            dpq[span, at(p, PAIR)] = (dq * (1.0 / math.sqrt(HEAD))).astype(NARROW)
            if end == rows:
                dkv[0:end, 0:PAIR] = dk
                dkv[0:end, PAIR:] = dv
            else:
                dkv[0:end, 0:PAIR] += dk
                dkv[0:end, PAIR:] += dv
        dpq[:, at(p + features // PAIR, PAIR)] = dkv[:, 0:PAIR].astype(NARROW)
        dpq[:, at(p + 2 * features // PAIR, PAIR)] = dkv[:, PAIR:].astype(NARROW)

    loop(features // PAIR, pair)
    taken = right_t(chosen, n1_ref[...]).astype(NARROW)
    weight_ref[:, 0 : 3 * features] = plain(taken, dpq[...]).astype(NARROW)
    loads[1].wait()
    norm_ref[...] = jnp.zeros_like(norm_ref)

    def last(i):
        span = at(i, STRIP)
        upstream = right_t(dpq[span, :], w_in[...])
        piece, gain, bias = norm_back(q_ref[span, :].astype(SINGLE), gain_ref[1:2, :], upstream)
        grad_ref[span, :] = dq1[span, :] + piece
        norm_ref[0:1, :] += gain
        norm_ref[1:2, :] += bias

    loop(rows // STRIP, last)


def bits_of(count):
    return max(count - 1, 0).bit_length()


def swap(tensor, axis, mask):
    return lax.ppermute(tensor, axis, [(i, i ^ mask) for i in range(lax.axis_size(axis))])


def pick(tensor, place, dim):
    return lax.dynamic_index_in_dim(tensor, place, dim, keepdims=False)


def fold(tensor, axis, bit, dim):
    own = (lax.axis_index(axis) >> bit) & 1
    arrived = swap(pick(tensor, 1 - own, dim).astype(NARROW), axis, 1 << bit)
    return pick(tensor, own, dim).astype(SINGLE) + arrived.astype(SINGLE)


def unfold(tensor, axis, bit, dim):
    own = (lax.axis_index(axis) >> bit) & 1
    arrived = swap(tensor, axis, 1 << bit)
    return jnp.where(
        own == 0,
        jnp.stack((tensor, arrived), axis=dim),
        jnp.stack((arrived, tensor), axis=dim),
    )


def scatter_blk(tensor):
    bits = bits_of(lax.axis_size("blk"))
    tensor = tensor.reshape((2,) * bits + tensor.shape[1:])
    for bit in range(bits):
        tensor = fold(tensor, "blk", bit, bits - 1 - bit)
    return tensor


def sum_rep_scatter(tensor, dim):
    bits = bits_of(lax.axis_size("rep"))
    shape = tensor.shape
    tensor = tensor.reshape(
        shape[:dim] + (2,) * bits + (shape[dim] // 2**bits,) + shape[dim + 1 :]
    )
    for bit in range(bits):
        tensor = fold(tensor, "rep", bit, dim)
    return tensor


def gather_rep(tensor, dim):
    bits = bits_of(lax.axis_size("rep"))
    for bit in reversed(range(bits)):
        tensor = unfold(tensor, "rep", bit, dim)
    shape = tensor.shape
    return tensor.reshape(shape[:dim] + (-1,) + shape[dim + bits + 1 :])


def reduce_all(tensor):
    count = lax.axis_size("blk")
    tensor = tensor.reshape(count, tensor.shape[0] // count, tensor.shape[1])
    tensor = sum_rep_scatter(tensor, 1)
    tensor = scatter_blk(tensor).astype(NARROW)
    return gather_rep(tensor, 0)


def reduce_rep(tensor):
    return gather_rep(sum_rep_scatter(tensor, 0).astype(NARROW), 0)


def exchange(pieces):
    whole = lax.all_to_all(jnp.stack(pieces), "blk", 0, 0)
    return [whole[k] for k in range(len(pieces))]


def gather(tensor):
    count = lax.axis_size("blk")
    whole = lax.all_gather(tensor, "blk")
    return [whole[k] for k in range(count)]


def whole(ref):
    return ref


class Move:
    late = None

    def __init__(self, source, shape, axis, flip, take=whole):
        self.source, self.shape, self.axis, self.flip, self.take = source, shape, axis, flip, take


def in_order(held, rep):
    for weight in (1, 2):
        flip = (rep // weight) % 2 == 1
        held = [jnp.where(flip, held[k ^ weight], held[k]) for k in range(4)]
    return held


class Reduction:
    def __init__(self, tensor):
        if len(tensor.shape) == 2:
            blocks = lax.axis_size("blk")
            height = tensor.shape[0] // blocks
            tensor = tensor.reshape(blocks, 2, height // 2, tensor.shape[1])
        self.tensor = tensor

    def moves(self, stage):
        tensor = self.tensor
        shape = tensor.shape
        if stage == "core":
            return [
                Move(tensor, shape[:1] + shape[2:], "rep", 1,
                     lambda ref: ref.at[:, 1 - place_of("rep") % 2])
            ]
        if stage == "x":
            width = shape[-1] // 2

            def columns(ref):
                span = pl.ds(pl.multiple_of((1 - place_of("rep") // 2) * width, width), width)
                return ref.at[(slice(None),) * (len(shape) - 1) + (span,)]

            return [Move(tensor, shape[:-1] + (width,), "rep", 2, columns)]
        if stage == "y":
            tensor = self.tensor = tensor.reshape((shape[0] // 2, 2) + shape[1:])
            return [
                Move(tensor, tensor.shape[:1] + shape[1:], "blk", 1,
                     lambda ref: ref.at[:, 1 - place_of() % 2])
            ]
        if stage == "z":
            length = shape[0]
            return [
                Move(tensor, shape[1:], "blk", 2 * k,
                     lambda ref, k=k: ref.at[flipped(place_of() // 2, k, length)])
                for k in range(1, length)
            ]
        return [Move(tensor, shape, "rep", k) for k in range(1, 4)]

    def absorb(self, stage, arrived):
        tensor = self.tensor
        rep, blk = lax.axis_index("rep"), lax.axis_index("blk")
        if stage == "core":
            own = pick(tensor, rep % 2, 1)
        elif stage == "x":
            width = tensor.shape[-1] // 2
            own = lax.dynamic_slice_in_dim(tensor, (rep // 2) * width, width, tensor.ndim - 1)
        elif stage == "y":
            own = pick(tensor, blk % 2, 1)
        elif stage == "z":
            own = pick(tensor, blk // 2, 0)
        else:
            held = in_order([tensor] + list(arrived), rep)
            self.tensor = jnp.concatenate(
                [jnp.concatenate((held[k], held[k + 2]), axis=1) for k in range(2)], axis=0
            )
            return
        total = own.astype(SINGLE)
        for one in arrived:
            total = total + one.astype(SINGLE)
        self.tensor = total.astype(NARROW)


class RepSum:
    def __init__(self, tensor, dim):
        self.tensor, self.dim = tensor, dim

    def moves(self, stage):
        shape = list(self.tensor.shape)
        if stage == "out":
            size = shape[self.dim] = shape[self.dim] // 4

            def quarter(ref, k):
                span = pl.ds(pl.multiple_of(flipped(place_of("rep"), k, 4) * size, size), size)
                return ref.at[span, :] if self.dim == 0 else ref.at[:, span]

            return [
                Move(self.tensor, tuple(shape), "rep", k, lambda ref, k=k: quarter(ref, k))
                for k in range(1, 4)
            ]
        return [Move(self.tensor, tuple(shape), "rep", k) for k in range(1, 4)]

    def absorb(self, stage, arrived):
        rep = lax.axis_index("rep")
        if stage == "out":
            size = self.tensor.shape[self.dim] // 4
            total = lax.dynamic_slice_in_dim(self.tensor, rep * size, size, self.dim).astype(SINGLE)
            for one in arrived:
                total = total + one.astype(SINGLE)
            self.tensor = total.astype(NARROW)
            return
        held = in_order([self.tensor] + list(arrived), rep)
        self.tensor = jnp.concatenate(held, axis=self.dim)


VMEM = pl.BlockSpec(memory_space=pltpu.VMEM)
SMEM = pl.BlockSpec(memory_space=pltpu.SMEM)
ANY = pl.BlockSpec(memory_space=pl.ANY)


def like(*shape, kind=NARROW):
    return jax.ShapeDtypeStruct(shape, kind)


def call(
    kernel, outs, operands, specs, scratch, flops, grid=None, out_specs=None, semaphores=0,
    moves=(), ident=None,
):
    scratch = [pltpu.VMEM(shape, kind) for shape, kind in scratch]
    if semaphores:
        scratch.append(pltpu.SemaphoreType.DMA((semaphores,)))
    out_specs = [VMEM] * len(outs) if out_specs is None else out_specs
    extra = {} if grid is None else {"grid": grid}
    params = {}
    sources = []
    for move in moves:
        if move.late is None and not any(move.source is one for one in sources):
            sources.append(move.source)
    number = [
        next((k for k, one in enumerate(sources) if one is move.source), None) for move in moves
    ]
    fixed_in, fixed_out = len(operands), len(outs)
    partners = sorted({(move.axis, move.flip) for move in moves})
    body_kernel = kernel
    if moves:
        params = {"collective_id": ident, "has_side_effects": True}
        scratch += [pltpu.SemaphoreType.DMA((len(moves),))] * 2

        def body_kernel(*refs):
            ins, refs = refs[:fixed_in], refs[fixed_in:]
            sent, refs = refs[: len(sources)], refs[len(sources) :]
            results, refs = refs[:fixed_out], refs[fixed_out:]
            landed, refs = refs[: len(moves)], refs[len(moves) :]
            rest, (send_sem, recv_sem) = refs[:-2], refs[-2:]

            def target(axis, flip):
                return {axis: flipped(lax.axis_index(axis), flip, lax.axis_size(axis))}

            def made(k):
                move = moves[k]
                late = move.late is not None
                return pltpu.make_async_remote_copy(
                    src_ref=move.take(results[move.late] if late else sent[number[k]]),
                    dst_ref=landed[k],
                    send_sem=send_sem.at[k],
                    recv_sem=recv_sem.at[k],
                    device_id=target(move.axis, move.flip),
                    device_id_type=pl.DeviceIdType.MESH,
                )

            def begin():
                barrier = pltpu.get_barrier_semaphore()
                for axis, flip in partners:
                    pl.semaphore_signal(
                        barrier, inc=1, device_id=target(axis, flip),
                        device_id_type=pl.DeviceIdType.MESH,
                    )
                pl.semaphore_wait(barrier, len(partners))
                launch(None)

            def launch(which):
                for k in range(len(moves)):
                    if moves[k].late == which:
                        made(k).start()

            def finish():
                for k in range(len(moves)):
                    made(k).wait()

            if grid is None:
                begin()
                if any(move.late is not None for move in moves):
                    kernel(*ins, *results, *rest, launch=launch)
                else:
                    kernel(*ins, *results, *rest)
                finish()
            else:
                pl.when(pl.program_id(0) == 0)(begin)
                kernel(*ins, *results, *rest)
                pl.when(pl.program_id(0) == pl.num_programs(0) - 1)(finish)

    result = pl.pallas_call(
        body_kernel,
        out_shape=list(outs) + [like(*m.shape, kind=m.source.dtype) for m in moves],
        in_specs=list(specs) + [ANY] * len(sources),
        out_specs=list(out_specs) + [ANY] * len(moves),
        scratch_shapes=scratch,
        compiler_params=pltpu.CompilerParams(vmem_limit_bytes=56 * 2**20, **params),
        cost_estimate=pl.CostEstimate(
            flops=int(flops),
            bytes_accessed=sum(o.size * o.dtype.itemsize for o in operands),
            transcendentals=0,
        ),
        **extra,
    )(*operands, *sources)
    return list(result[:fixed_out]), list(result[fixed_out:])


class Courier:
    def __init__(self, active):
        self.active, self.waiting, self.ident = active, [], 0

    def load(self, *jobs):
        self.waiting += jobs

    def run(self, kernel, outs, operands, specs, scratch, flops, **extra):
        jobs, self.waiting = self.waiting, []
        moves, ends = [], []
        for job, stage, *late in jobs:
            added = job.moves(stage)
            for move in added:
                move.late = late[0] if late else None
            moves += added
            ends.append(len(moves))
        if moves:
            self.ident += 1
        results, arrived = call(
            kernel, outs, operands, specs, scratch, flops, moves=tuple(moves), ident=self.ident, **extra
        )
        start = 0
        for (job, stage, *late), end in zip(jobs, ends):
            if late:
                job.tensor = results[late[0]]
            job.absorb(stage, arrived[start:end])
            start = end
        return results


class Exchange:
    def __init__(self, pieces):
        self.pieces = pieces

    def moves(self, stage):
        return [Move(one, one.shape, "blk", k) for k, one in enumerate(self.pieces) if k]

    def absorb(self, stage, arrived):
        self.result = self.pieces[:1] + list(arrived)


class Pieces:
    def __init__(self, tensor, part, start, width):
        self.tensor, self.part, self.start, self.width = tensor, part, start, width

    def moves(self, stage):
        part, span = self.part, slice(self.start, self.start + self.width)
        count = lax.axis_size("blk")
        return [
            Move(self.tensor, (part, self.width), "blk", k,
                 lambda ref, k=k: ref.at[at(flipped(place_of(), k, count), part), span])
            for k in range(1, count)
        ]

    def absorb(self, stage, arrived):
        self.result = list(arrived)


class Gather:
    def __init__(self, tensor):
        self.tensor = tensor

    def moves(self, stage):
        return [
            Move(self.tensor, self.tensor.shape, "blk", k) for k in range(1, lax.axis_size("blk"))
        ]

    def absorb(self, stage, arrived):
        self.result = [self.tensor] + list(arrived)


class Norms:
    def __init__(self, tensor):
        self.tensor = tensor

    def moves(self, stage):
        axis = "rep" if stage == "out" else "blk"
        return [
            Move(self.tensor, self.tensor.shape, axis, k) for k in range(1, lax.axis_size(axis))
        ]

    def absorb(self, stage, arrived):
        for one in arrived:
            self.tensor = self.tensor + one


def body(
    patches,
    queries,
    window_valid,
    answer_length,
    norm_gain,
    norm_bias,
    attn_in,
    attn_out,
    mlp_in,
    mlp_out,
    cot_patches,
    cot_queries,
):
    x, q, cot_x, cot_q = patches[0], queries[0], cot_patches[0], cot_queries[0]
    rows, features = x.shape
    count = q.shape[0]
    hidden = mlp_in.shape[2]
    blocks = lax.axis_size("blk")
    place = lax.axis_index("blk").astype(jnp.int32)
    share = features // blocks
    hidden_share = hidden // blocks
    share_rows = -(-share // 16) * 16
    hidden_rows = -(-hidden_share // 16) * 16
    part = -(-count // (blocks * 16)) * 16
    padded = part * blocks
    wide = 3 * features
    last = wide + features + features
    causal_columns = -(-last // 512) * 512
    leader = (place == 0).astype(SINGLE)
    valid = jnp.where(jnp.repeat(window_valid[0], WIN) > 0, 0.0, MASKED).astype(SINGLE)
    carried = blocks == DIRECT and lax.axis_size("rep") == 4 and share % 32 == 0
    courier = Courier(carried)

    def own_columns(tensor):
        return lax.dynamic_slice_in_dim(tensor, place * share, share, 1)

    def own_rows(tensor):
        tensor = jnp.pad(tensor, ((0, padded - count), (0, 0)))
        return lax.dynamic_slice_in_dim(tensor, place * part, part, 0)

    square = 2.0 * features * features
    run = courier.run

    n0, pw, mw, x1, nx, vq, ckv = run(
        window_forward,
        [
            like(rows, features), like(rows, wide), like(rows, features),
            like(rows, features, kind=SINGLE), like(rows, features), like(rows, features),
            like(rows, 2 * features),
        ],
        [x, norm_gain, norm_bias, attn_in, attn_out],
        [VMEM, VMEM, VMEM, ANY, ANY],
        [((features, wide), NARROW), ((features, features), NARROW),
         ((features, features), NARROW), ((features, 2 * features), NARROW)],
        rows * square * 9,
        semaphores=4,
    )
    n1, pq, mq, q1, nq, cq, vkv, log_q = run(
        causal_forward,
        [
            like(count, features), like(count, wide), like(count, features),
            like(count, features, kind=SINGLE), like(count, features), like(count, features),
            like(count, 2 * features), like(16, count, kind=SINGLE),
        ],
        [q, norm_gain, norm_bias, attn_in, attn_out],
        [VMEM, VMEM, VMEM, ANY, ANY],
        [((features, wide), NARROW), ((features, features), NARROW),
         ((features, features), NARROW), ((features, 2 * features), NARROW),
         ((count, PAIR), SINGLE)],
        count * square * 15,
        semaphores=4,
    )
    outs, *log_pieces = run(
        functools.partial(cross_forward, blocks),
        [like(padded, features)] + [like(16, part, kind=SINGLE)] * blocks,
        [cq, ckv, valid[None, :]],
        [VMEM, VMEM, VMEM],
        [((padded, PAIR), SINGLE)],
        count * square * 6,
    )
    logs = Exchange(log_pieces)
    halves = [Pieces(outs, part, k * features // 2, features // 2) for k in range(2)]
    if carried:
        courier.load((logs, ""), (halves[0], ""))
    mv, x2, log_v = run(
        reverse_forward,
        [like(rows, features), like(rows, features, kind=SINGLE), like(16, rows, kind=SINGLE)],
        [answer_length, vq, vkv, x1, attn_out],
        [SMEM, VMEM, VMEM, VMEM, ANY],
        [((features, features), NARROW), ((rows, PAIR), SINGLE)],
        rows * square * 8,
        semaphores=1,
    )
    if carried:
        courier.load((halves[1], ""))
    fixed = lambda *shape: pl.BlockSpec(shape, lambda j: (0,) * len(shape))
    x3, dx2, up_x, down_x, norm_five = run(
        patch_feed_forward,
        [
            like(rows, features), like(rows, features, kind=SINGLE), like(features, hidden),
            like(hidden, features), like(8, features, kind=SINGLE),
        ],
        [x2, cot_x, norm_gain, norm_bias, mlp_in, mlp_out],
        [
            fixed(rows, features), fixed(rows, features), fixed(6, features), fixed(6, features),
            pl.BlockSpec((1, features, CHUNK), lambda j: (0, 0, j)),
            pl.BlockSpec((1, CHUNK, features), lambda j: (0, j, 0)),
        ],
        [((rows, features), NARROW), ((rows, CHUNK), NARROW), ((rows, CHUNK), NARROW),
         ((rows, features), SINGLE), ((rows, features), SINGLE)],
        rows * square * 24,
        grid=(hidden // CHUNK,),
        out_specs=[
            fixed(rows, features), fixed(rows, features),
            pl.BlockSpec((features, CHUNK), lambda j: (0, j)),
            pl.BlockSpec((CHUNK, features), lambda j: (j, 0)),
            fixed(8, features),
        ],
    )
    if carried:
        merged = run(
            functools.partial(merge_blocks, blocks),
            [like(part, features), like(16, part, kind=SINGLE)],
            [outs] + logs.result + halves[0].result + halves[1].result,
            [VMEM] * (3 * blocks - 1),
            [],
            padded * square,
        )
        co_parts, log_parts = Gather(merged[0]), Gather(merged[1])
        up_x, down_x = Reduction(up_x), Reduction(down_x)
        reverse_weight = Reduction(like(blocks, 2, share // 2, 2 * features))
        courier.load(
            (co_parts, ""), (log_parts, ""), (up_x, "core"), (down_x, "core"),
            (reverse_weight, "core", 1),
        )
    else:
        whole_logs = jnp.stack(exchange(log_pieces))
        merged_log = jax.nn.logsumexp(whole_logs, axis=0)
        weights = jnp.transpose(jnp.exp(whole_logs - merged_log)[:, :HEADS], (0, 2, 1))
        shares = lax.all_to_all(outs.reshape(blocks, part, features), "blk", 0, 0)
        merged_out = jnp.sum(jnp.repeat(weights, HEAD, axis=2) * shares.astype(SINGLE), axis=0)
        co_parts, log_parts = Gather(None), Gather(None)
        co_parts.result, log_parts.result = gather(merged_out.astype(NARROW)), gather(merged_log)
    folded = (blocks, 2, share // 2) if carried else (features,)
    dvq, reverse_grad, *kv_pieces = run(
        functools.partial(reverse_backward, blocks),
        [like(rows, features), like(*folded, 2 * features)]
        + [like(part, features)] * (2 * blocks),
        [answer_length, dx2, mv, vq, vkv, nx, log_v, attn_out],
        [SMEM, VMEM, VMEM, VMEM, VMEM, VMEM, VMEM, ANY],
        [((features, features), NARROW), ((rows, features), NARROW), ((rows, features), NARROW),
         ((16, rows), SINGLE), ((padded, 2 * features), SINGLE)],
        rows * square * 16,
        semaphores=1,
    )
    k_parts, v_parts = Exchange(kv_pieces[:blocks]), Exchange(kv_pieces[blocks:])
    if carried:
        courier.load((up_x, "x"), (k_parts, ""))
    else:
        k_parts.result, v_parts.result = exchange(k_parts.pieces), exchange(v_parts.pieces)
    q3, dq2, up_q, down_q, norm_four, co = run(
        functools.partial(query_feed_forward, blocks, share, hidden_share),
        [
            like(count, features), like(count, features, kind=SINGLE), like(share_rows, hidden),
            like(hidden_rows, features), like(8, features, kind=SINGLE), like(padded, features),
        ],
        [q1, cot_q, norm_gain, norm_bias, attn_out, mlp_in, mlp_out] + co_parts.result,
        [
            fixed(count, features), fixed(count, features), fixed(6, features),
            fixed(6, features), pl.BlockSpec((1, features, features), lambda j: (2, 0, 0)),
            pl.BlockSpec((1, features, CHUNK), lambda j: (1, 0, j)),
            pl.BlockSpec((1, CHUNK, features), lambda j: (1, j, 0)),
        ] + [fixed(part, features)] * blocks,
        [((count, features), SINGLE), ((count, features), NARROW), ((share_rows, count), NARROW),
         ((count, CHUNK), NARROW), ((count, CHUNK), NARROW),
         ((count, features), SINGLE), ((count, features), SINGLE)],
        count * square * 18,
        grid=(hidden // CHUNK,),
        out_specs=[
            fixed(count, features), fixed(count, features),
            pl.BlockSpec((share_rows, CHUNK), lambda j: (0, j)),
            fixed(hidden_rows, features), fixed(8, features), fixed(padded, features),
        ],
    )
    if carried:
        up_q, down_q = RepSum(up_q, 1), RepSum(down_q, 0)
        courier.load((down_x, "x"), (v_parts, ""), (up_x, "y"))
    dckv, cross_out_weight, *q_pieces = run(
        functools.partial(cross_backward, blocks, share),
        [like(rows, 2 * features), like(share_rows, features)] + [like(part, features)] * blocks,
        [dq2, co, cq, ckv, valid[:, None], attn_out] + log_parts.result,
        [VMEM, VMEM, VMEM, VMEM, VMEM, ANY] + [VMEM] * blocks,
        [((features, features), NARROW), ((count, features), NARROW), ((count, features), NARROW),
         ((16, count), SINGLE), ((padded, PAIR), SINGLE), ((16, count), SINGLE),
         ((padded, features), NARROW), ((rows, 2 * features), SINGLE)],
        count * square * 12,
        semaphores=1,
    )
    q_parts = Exchange(q_pieces)
    if carried:
        kv_weight = Reduction(like(blocks, 2, share // 2, 2 * features))
        window_weight = Reduction(like(blocks, 2, share // 2, 4 * features))
        courier.load(
            (q_parts, ""), (down_x, "y"), (reverse_weight, "x"), (up_q, "out"), (down_q, "out"),
            (kv_weight, "core", 0), (window_weight, "core", 1),
        )
    else:
        q_parts.result = exchange(q_pieces)
    kv_grad, window_grad, grad_x, norm_x = run(
        patch_backward,
        [
            like(*folded, 2 * features), like(*folded, 4 * features),
            like(rows, features, kind=SINGLE), like(8, features, kind=SINGLE),
        ],
        [x, dx2, x1, nx, n0, pw, mw, dvq, dckv, norm_gain, attn_in, attn_out],
        [VMEM] * 10 + [ANY, ANY],
        [((features, wide), NARROW), ((features, features), NARROW),
         ((features, features), NARROW), ((features, 2 * features), NARROW),
         ((rows, features), SINGLE), ((rows, features), NARROW), ((rows, features), NARROW),
         ((16, rows), SINGLE), ((rows, wide), NARROW)],
        rows * square * 24,
        semaphores=4,
    )
    if carried:
        share_weight = Reduction(like(blocks, 2, share // 2, wide))
        courier.load((share_weight, "core", 1))
    dq1_share, share_grad, norm_two = run(
        functools.partial(share_backward, blocks),
        [like(part, features), like(*folded, wide), like(8, features, kind=SINGLE)],
        [own_rows(q1), own_rows(nq), norm_gain, attn_in]
        + q_parts.result + k_parts.result + v_parts.result,
        [VMEM, VMEM, VMEM, ANY] + [VMEM] * (3 * blocks),
        [((features, features), NARROW), ((features, 2 * features), NARROW),
         ((part, wide), NARROW)],
        part * square * 6,
        semaphores=2,
    )
    dq1_parts = Gather(dq1_share)

    def arrive(*jobs):
        courier.load(*jobs)
        run(nothing, [], [], [], [], 0)

    if carried:
        arrive((dq1_parts, ""), (window_weight, "x"), (reverse_weight, "y"))
        courier.load(
            (up_x, "z"), (down_x, "z"), (reverse_weight, "z"), (window_weight, "y"),
            (share_weight, "y"), (kv_weight, "x"), (up_q, "back"), (down_q, "back"),
        )
    else:
        dq1_parts.result = gather(dq1_share)
    causal_weight, grad_q, norm_one = run(
        functools.partial(causal_backward, blocks, share),
        [
            like(share_rows, causal_columns), like(count, features, kind=SINGLE),
            like(8, features, kind=SINGLE),
        ],
        [q, dq2, n1, pq, mq, log_q, cross_out_weight, norm_gain, attn_in, attn_out]
        + dq1_parts.result,
        [VMEM] * 8 + [ANY, ANY] + [VMEM] * blocks,
        [((features, wide), NARROW), ((features, features), NARROW), ((padded, features), NARROW),
         ((count, features), SINGLE), ((count, features), NARROW), ((count, features), NARROW),
         ((16, count), SINGLE), ((count, 2 * PAIR), SINGLE), ((count, wide), NARROW)],
        count * square * 16,
        semaphores=2,
    )
    norms = jnp.stack(
        (
            norm_x[2], norm_one[0] * leader, norm_two[0], norm_x[0], norm_four[0] * leader,
            norm_five[0], norm_x[3], norm_one[1] * leader, norm_two[1], norm_x[1],
            norm_four[1] * leader, norm_five[1],
        )
    )
    if carried:
        norms = Norms(jnp.pad(norms, ((0, 4), (0, 0))))
        causal_weight = RepSum(causal_weight, 1)
        arrive(
            (share_weight, "x"), (causal_weight, "out"), (norms, "out"), (kv_weight, "y"),
            (window_weight, "z"),
        )
        arrive(
            (share_weight, "z"), (kv_weight, "z"), (causal_weight, "back"), (norms, "back"),
            (up_x, "back"), (down_x, "back"), (reverse_weight, "back"), (window_weight, "back"),
        )
        arrive((share_weight, "back"), (kv_weight, "back"))
        up_x, down_x, reverse_weight, window_weight, kv_weight, share_weight, causal_weight = (
            one.tensor
            for one in (
                up_x, down_x, reverse_weight, window_weight, kv_weight, share_weight, causal_weight
            )
        )
        up_q, down_q, norms = up_q.tensor, down_q.tensor, norms.tensor[:12]
    else:
        up_x, down_x, reverse_weight, window_weight, kv_weight, share_weight = (
            reduce_all(one)
            for one in (up_x, down_x, reverse_grad, window_grad, kv_grad, share_grad)
        )
        up_q, down_q = reduce_rep(up_q[:share]), reduce_rep(down_q[:hidden_share])
        causal_weight = reduce_rep(causal_weight[:share])
        norms = lax.psum(norms, ("blk", "rep"))
    norms = own_columns(norms)
    grad_attn_in = jnp.stack(
        (
            window_weight[:, :wide],
            causal_weight[:, :wide],
            jnp.concatenate((share_weight[:, :features], kv_weight), axis=1),
            jnp.concatenate((reverse_weight[:, :features], share_weight[:, features:]), axis=1),
        )
    )
    grad_attn_out = jnp.stack(
        (
            window_weight[:, wide:],
            causal_weight[:, wide : wide + features],
            causal_weight[:, wide + features : last],
            reverse_weight[:, features:],
        )
    )
    return (
        x3[None],
        own_columns(q3)[None],
        grad_x[None],
        own_columns(grad_q)[None],
        norms[:6],
        norms[6:],
        grad_attn_in.astype(SINGLE),
        grad_attn_out.astype(SINGLE),
        jnp.stack((up_x, up_q)).astype(SINGLE),
        jnp.stack((down_x, down_q)).astype(SINGLE),
    )


def solution(mesh):
    placed = (
        P("rep", "blk", None),
        P("rep", None, None),
        P("rep", "blk"),
        P("rep"),
        P(),
        P(),
        P(),
        P(),
        P(),
        P(),
        P("rep", "blk", None),
        P("rep", None, None),
    )
    return jax.shard_map(
        body,
        mesh=mesh,
        in_specs=placed,
        out_specs=(
            P("rep", "blk", None),
            P("rep", None, "blk"),
            P("rep", "blk", None),
            P("rep", None, "blk"),
            P(None, "blk"),
            P(None, "blk"),
            P(None, "blk", None),
            P(None, "blk", None),
            P(None, "blk", None),
            P(None, "blk", None),
        ),
        check_vma=False,
    )
```

```python
import functools
import math

import jax
import jax.numpy as jnp
from jax import lax
from jax.experimental import pallas as pl
from jax.experimental.pallas import tpu as pltpu
from jax.sharding import PartitionSpec as P

HEADS = 12
WIN = 64
EPSILON = 1e-05
MASKED = -1e30
NARROW = jnp.bfloat16
SINGLE = jnp.float32
EXACT = lax.Precision.HIGHEST
GROUP = 128
WINDOWS = 256
PAIR = 128
HEAD = 64
STRIP = 160
LONG = 400
CHUNK = 768


def dot(former, latter, ahead, behind, precision=None):
    return lax.dot_general(
        former,
        latter,
        (((ahead,), (behind,)), ((), ())),
        preferred_element_type=SINGLE,
        precision=precision,
    )


def plain(former, latter):
    return dot(former, latter, 1, 0)


def right_t(former, latter):
    return dot(former, latter, 1, 1)


def left_t(former, latter):
    return dot(former, latter, 0, 0)


def loop(count, action):
    def step(index, nothing):
        action(index)
        return nothing

    lax.fori_loop(0, count, step, 0)


def at(index, size):
    return pl.ds(pl.multiple_of(index * size, size), size)


def iota(shape, dim):
    return lax.broadcasted_iota(jnp.int32, shape, dim)


def statistics(tensor):
    average = jnp.mean(tensor, axis=-1, keepdims=True)
    centred = tensor - average
    spread = jnp.mean(centred * centred, axis=-1, keepdims=True)
    return centred, lax.rsqrt(spread + EPSILON)


def norm(tensor, gain, bias):
    centred, inverse = statistics(tensor)
    return centred * inverse * gain + bias


def norm_back(tensor, gain, upstream):
    centred, inverse = statistics(tensor)
    scaled = centred * inverse
    inner = upstream * gain
    grad = inverse * (
        inner
        - jnp.mean(inner, axis=-1, keepdims=True)
        - scaled * jnp.mean(inner * scaled, axis=-1, keepdims=True)
    )
    return (
        grad,
        jnp.sum(upstream * scaled, axis=0, keepdims=True),
        jnp.sum(upstream, axis=0, keepdims=True),
    )


def gelu_both(tensor):
    size = jnp.abs(tensor)
    ratio = 1.0 / (1.0 + (0.3275911 * math.sqrt(0.5)) * size)
    series = ratio * (
        0.254829592
        + ratio * (-0.284496736 + ratio * (1.421413741 + ratio * (-1.453152027 + ratio * 1.061405429)))
    )
    bell = jnp.exp(-0.5 * (tensor * tensor))
    tail = 0.5 * series * bell
    below = jnp.where(tensor >= 0, 1.0 - tail, tail)
    return tensor * below, below + tensor * bell * (1.0 / math.sqrt(2.0 * math.pi))


def half(which, value=1.0):
    return jnp.where(iota((1, PAIR), 1) // HEAD == which, value, 0.0).astype(NARROW)


def lower_lanes():
    return iota((1, PAIR), 1) < HEAD


def both(tensor, value=1.0):
    return jnp.concatenate((tensor * half(0, value), tensor * half(1, value)), axis=0)


def attend(queries, keys, values, mask):
    rows = queries.shape[0]
    scores = right_t(both(queries, 1.0 / math.sqrt(HEAD)), keys)
    weights, totals, logs = [], [], []
    for which in range(2):
        part = mask(scores[which * rows : (which + 1) * rows])
        peak = jnp.max(part, axis=-1, keepdims=True)
        part = jnp.exp(part - peak)
        total = jnp.sum(part, axis=-1, keepdims=True)
        weights.append(part.astype(NARROW))
        totals.append(1.0 / total)
        logs.append(peak + jnp.log(total))
    out = plain(jnp.concatenate(weights, axis=0), values)
    return jnp.where(lower_lanes(), out[:rows] * totals[0], out[rows:] * totals[1]), logs


def attend_back(queries, keys, values, upstream, logs, deltas, mask):
    scaled = queries * jnp.asarray(1.0 / math.sqrt(HEAD), NARROW)
    count = keys.shape[0]
    keys = both(keys)
    turned_keys = keys.T
    scores = right_t(keys, scaled)
    inner = right_t(both(values), upstream)
    weights, slopes = [], []
    for which in range(2):
        span = slice(which * count, (which + 1) * count)
        part = mask(scores[span])
        if logs is None:
            part = jnp.exp(part - jnp.max(part, axis=0, keepdims=True))
            part = part * (1.0 / jnp.sum(part, axis=0, keepdims=True))
        else:
            part = jnp.exp(part - logs[which])
        weights.append(part.astype(NARROW))
        slopes.append((part * (inner[span] - deltas[which])).astype(NARROW))
    slope = jnp.concatenate(slopes, axis=0)
    query_grad = plain(turned_keys, slope).T
    key_grad = plain(slope, scaled)
    value_grad = plain(jnp.concatenate(weights, axis=0), upstream)
    lanes = lower_lanes()
    return (
        query_grad,
        jnp.where(lanes, key_grad[:count], key_grad[count:]),
        jnp.where(lanes, value_grad[:count], value_grad[count:]),
    )


def head_rows(tensor):
    features = tensor.shape[1]
    heads = 16
    chosen = jnp.where(
        iota((heads, features), 1) // HEAD == iota((heads, features), 0), 1.0, 0.0
    ).astype(SINGLE)
    return dot(chosen, tensor, 1, 1, EXACT)


def turn(columns):
    same = jnp.where(iota((16, columns.shape[1]), 0) == iota((16, columns.shape[1]), 1), 1.0, 0.0)
    return dot(same.astype(SINGLE), columns, 1, 1, EXACT)


def row_pair(ref, pair, span):
    tensor = ref[:, span]
    index = iota(tensor.shape, 0)
    return [
        jnp.sum(jnp.where(index == 2 * pair + which, tensor, 0.0), axis=0, keepdims=True)
        for which in range(2)
    ]


def chooser(rows, width, start, count):
    row = iota((rows, width), 0)
    hit = jnp.logical_and(iota((rows, width), 1) == row + start, row < count)
    return jnp.where(hit, 1.0, 0.0).astype(NARROW)


def spans(rows, size):
    edges = [(start, min(start + size, rows)) for start in range(0, rows, size)]
    if len(edges) > 1 and edges[-1][1] - edges[-1][0] < PAIR:
        edges[-2:] = [(edges[-2][0], rows)]
    return edges


def mark(log_ref, rows, head, value):
    log_ref[rows, :] = jnp.where(iota((1, PAIR), 1) == head, value, log_ref[rows, :])


def store_rows(ref, columns, value):
    ref[(slice(None),) * (len(ref.shape) - 1) + (columns,)] = value.astype(ref.dtype).reshape(
        ref.shape[:-1] + value.shape[1:]
    )


def nothing(*unused):
    return None


def copies(semaphores, *pairs):
    made = [
        pltpu.make_async_copy(source, target, semaphores.at[k])
        for k, (source, target) in enumerate(pairs)
    ]
    for one in made:
        one.start()
    return made


DIRECT = 8


def place_of(axis="blk"):
    return lax.axis_index(axis)


def flipped(index, mask, count):
    total, weight = 0, 1
    while weight < count:
        bit = (index // weight) % 2
        total = total + weight * ((1 - bit) if mask & weight else bit)
        weight *= 2
    return total


def piece_at(number, count):
    return flipped(place_of(), number, count) if count <= DIRECT else number


def window_forward(
    x_ref, gain_ref, bias_ref, a_in, a_out,
    n0_ref, pw_ref, mw_ref, x1_ref, nx_ref, vq_ref, ckv_ref,
    w_in, w_out, w_q, w_kv, sem,
):
    rows, features = x_ref.shape
    loads = copies(
        sem,
        (a_in.at[0], w_in),
        (a_out.at[0], w_out),
        (a_in.at[3, :, pl.ds(0, features)], w_q),
        (a_in.at[2, :, pl.ds(features, 2 * features)], w_kv),
    )

    def first(i):
        span = at(i, GROUP)
        n0_ref[span, :] = norm(
            x_ref[span, :].astype(SINGLE), gain_ref[0:1, :], bias_ref[0:1, :]
        ).astype(NARROW)

    loop(rows // GROUP, first)
    loads[0].wait()

    def project(j):
        span = at(j, CHUNK)
        pw_ref[:, span] = plain(n0_ref[...], w_in[:, span]).astype(NARROW)

    loop(3 * features // CHUNK, project)
    window = jnp.where(
        iota((WINDOWS, WINDOWS), 0) // WIN == iota((WINDOWS, WINDOWS), 1) // WIN, 0.0, MASKED
    )

    def group(i):
        span = at(i, WINDOWS)
        for pair in range(features // PAIR):
            lane = pair * PAIR
            out, unused = attend(
                pw_ref[span, lane : lane + PAIR],
                pw_ref[span, features + lane : features + lane + PAIR],
                pw_ref[span, 2 * features + lane : 2 * features + lane + PAIR],
                lambda scores: scores + window,
            )
            mw_ref[span, lane : lane + PAIR] = out.astype(NARROW)

    loop(rows // WINDOWS, group)
    loads[1].wait()

    def second(i):
        span = at(i, GROUP)
        total = x_ref[span, :].astype(SINGLE) + plain(mw_ref[span, :], w_out[...])
        x1_ref[span, :] = total
        nx_ref[span, :] = norm(total, gain_ref[3:4, :], bias_ref[3:4, :]).astype(NARROW)

    loop(rows // GROUP, second)
    loads[2].wait()
    vq_ref[...] = plain(nx_ref[...], w_q[...]).astype(NARROW)
    loads[3].wait()

    def third(j):
        span = at(j, CHUNK)
        ckv_ref[:, span] = plain(nx_ref[...], w_kv[:, span]).astype(NARROW)

    loop(2 * features // CHUNK, third)


def causal_forward(
    q_ref, gain_ref, bias_ref, a_in, a_out,
    n1_ref, pq_ref, mq_ref, q1_ref, nq_ref, cq_ref, vkv_ref, log_ref,
    w_in, w_out, w_q, w_kv, logs, sem,
):
    rows, features = q_ref.shape
    loads = copies(
        sem,
        (a_in.at[1], w_in),
        (a_out.at[1], w_out),
        (a_in.at[2, :, pl.ds(0, features)], w_q),
        (a_in.at[3, :, pl.ds(features, 2 * features)], w_kv),
    )

    def first(i):
        span = at(i, STRIP)
        n1_ref[span, :] = norm(
            q_ref[span, :].astype(SINGLE), gain_ref[1:2, :], bias_ref[1:2, :]
        ).astype(NARROW)

    loop(rows // STRIP, first)
    loads[0].wait()

    def project(j):
        span = at(j, CHUNK)
        pq_ref[:, span] = plain(n1_ref[...], w_in[:, span]).astype(NARROW)

    loop(3 * features // CHUNK, project)
    logs[...] = jnp.zeros_like(logs)

    def pair(p):
        for start in range(0, rows, LONG):
            end = min(start + LONG, rows)

            def mask(scores, start=start):
                shape = scores.shape
                return jnp.where(iota(shape, 1) <= iota(shape, 0) + start, scores, MASKED)

            out, sums = attend(
                pq_ref[start:end, at(p, PAIR)],
                pq_ref[0:end, at(p + features // PAIR, PAIR)],
                pq_ref[0:end, at(p + 2 * features // PAIR, PAIR)],
                mask,
            )
            mq_ref[start:end, at(p, PAIR)] = out.astype(NARROW)
            for which in range(2):
                mark(logs, slice(start, end), 2 * p + which, sums[which])

    loop(features // PAIR, pair)
    log_ref[...] = turn(logs[...])
    loads[1].wait()

    def second(i):
        span = at(i, STRIP)
        total = q_ref[span, :].astype(SINGLE) + plain(mq_ref[span, :], w_out[...])
        q1_ref[span, :] = total
        nq_ref[span, :] = norm(total, gain_ref[2:3, :], bias_ref[2:3, :]).astype(NARROW)

    loop(rows // STRIP, second)
    if q1_ref.shape[0] > rows:
        q1_ref[rows:, :] = jnp.zeros_like(q1_ref[rows:, :])
        nq_ref[rows:, :] = jnp.zeros_like(nq_ref[rows:, :])
    loads[2].wait()
    cq_ref[...] = plain(nq_ref[0:rows, :], w_q[...]).astype(NARROW)
    loads[3].wait()

    def third(j):
        span = at(j, CHUNK)
        vkv_ref[:, span] = plain(nq_ref[0:rows, :], w_kv[:, span]).astype(NARROW)

    loop(2 * features // CHUNK, third)


def cross_forward(pieces, cq_ref, ckv_ref, valid_ref, whole, *rest):
    log_refs, (logs,) = rest[:pieces], rest[pieces:]
    rows, features = cq_ref.shape
    part = log_refs[0].shape[1]
    logs[...] = jnp.zeros_like(logs)
    if whole.shape[0] > rows:
        whole[rows:, :] = jnp.zeros((whole.shape[0] - rows, features), NARROW)

    def pair(p):
        for start in range(0, rows, LONG):
            span = slice(start, min(start + LONG, rows))
            out, sums = attend(
                cq_ref[span, at(p, PAIR)],
                ckv_ref[:, at(p, PAIR)],
                ckv_ref[:, at(p + features // PAIR, PAIR)],
                lambda scores: scores + valid_ref[...],
            )
            whole[span, at(p, PAIR)] = out.astype(NARROW)
            for which in range(2):
                mark(logs, span, 2 * p + which, sums[which])

    loop(features // PAIR, pair)
    for k in range(pieces):
        log_refs[k][...] = turn(logs[at(piece_at(k, pieces), part), :])


def untwist(rows):
    same = jnp.where(iota((16, PAIR), 0) == iota((16, PAIR), 1), 1.0, 0.0)
    return dot(rows, same.astype(SINGLE), 0, 0, EXACT)


def merge_blocks(pieces, own_ref, *refs):
    logs, refs = refs[:pieces], refs[pieces:]
    halves, (co_ref, log_ref) = (refs[: pieces - 1], refs[pieces - 1 : -2]), refs[-2:]
    part, features = co_ref.shape
    width = features // 2
    peak = functools.reduce(jnp.maximum, [one[...] for one in logs])
    total = peak + jnp.log(functools.reduce(jnp.add, [jnp.exp(one[...] - peak) for one in logs]))
    log_ref[...] = total
    spread = jnp.where(
        iota((PAIR, features), 1) // HEAD == iota((PAIR, features), 0), 1.0, 0.0
    ).astype(NARROW)
    result = jnp.zeros(co_ref.shape, SINGLE)
    for k in range(pieces):
        weight = untwist(jnp.exp(logs[k][...] - total))
        high = weight.astype(NARROW)
        low = (weight - high.astype(SINGLE)).astype(NARROW)
        if k == 0:
            block = own_ref[at(place_of(), part), :]
        else:
            block = jnp.concatenate((halves[0][k - 1][...], halves[1][k - 1][...]), axis=1)
        result = result + (plain(high, spread) + plain(low, spread)) * block.astype(SINGLE)
    co_ref[...] = result.astype(NARROW)


def reverse_forward(
    length_ref, vq_ref, vkv_ref, x1_ref, a_out,
    mv_ref, x2_ref, log_ref,
    w_out, logs, sem,
):
    rows, features = vq_ref.shape
    keys = vkv_ref.shape[0]
    (load,) = copies(sem, (a_out.at[3], w_out))
    logs[...] = jnp.zeros_like(logs)
    bias = jnp.where(iota((1, keys), 1) < length_ref[0], 0.0, MASKED)

    def pair(p):
        for start in range(0, rows, WINDOWS):
            span = slice(start, start + WINDOWS)
            out, sums = attend(
                vq_ref[span, at(p, PAIR)],
                vkv_ref[:, at(p, PAIR)],
                vkv_ref[:, at(p + features // PAIR, PAIR)],
                lambda scores: scores + bias,
            )
            mv_ref[span, at(p, PAIR)] = out.astype(NARROW)
            for which in range(2):
                mark(logs, span, 2 * p + which, sums[which])

    loop(features // PAIR, pair)
    log_ref[...] = turn(logs[...])
    load.wait()

    def second(i):
        span = at(i, GROUP)
        x2_ref[span, :] = x1_ref[span, :] + plain(mv_ref[span, :], w_out[...])

    loop(rows // GROUP, second)


def feed_forward_step(block, normed, up, down, cot, hidden, slope, out, grad):
    rows = normed.shape[0]

    def strip(i):
        span = at(i, block)
        value, rise = gelu_both(plain(normed[span, :], up[...]))
        hidden[span, :] = value.astype(NARROW)
        slope[span, :] = (right_t(cot[span, :], down[...]) * rise).astype(NARROW)
        out[span, :] += plain(hidden[span, :], down[...])
        grad[span, :] += right_t(slope[span, :], up[...])

    loop(rows // block, strip)


def patch_feed_forward(
    x2_ref, cot_ref, gain_ref, bias_ref, up_ref, down_ref,
    x3_ref, dx2_ref, up_grad_ref, down_grad_ref, norm_ref,
    normed, hidden, slope, out, grad,
):
    rows = x2_ref.shape[0]
    step = pl.program_id(0)

    @pl.when(step == 0)
    def begin():
        def first(i):
            span = at(i, GROUP)
            normed[span, :] = norm(
                x2_ref[span, :], gain_ref[5:6, :], bias_ref[5:6, :]
            ).astype(NARROW)
            out[span, :] = x2_ref[span, :]
            grad[span, :] = jnp.zeros_like(grad[span, :])

        loop(rows // GROUP, first)

    feed_forward_step(
        512, normed, up_ref.at[0], down_ref.at[0], cot_ref, hidden, slope, out, grad
    )
    up_grad_ref[...] = left_t(normed[...], slope[...]).astype(NARROW)
    down_grad_ref[...] = left_t(hidden[...], cot_ref[...]).astype(NARROW)

    @pl.when(step == pl.num_programs(0) - 1)
    def finish():
        norm_ref[...] = jnp.zeros_like(norm_ref)

        def last(i):
            span = at(i, GROUP)
            x3_ref[span, :] = out[span, :].astype(NARROW)
            part, gain, bias = norm_back(x2_ref[span, :], gain_ref[5:6, :], grad[span, :])
            dx2_ref[span, :] = cot_ref[span, :].astype(SINGLE) + part
            norm_ref[0:1, :] += gain
            norm_ref[1:2, :] += bias

        loop(rows // GROUP, last)


def place_parts(ref, pieces, parts):
    part, features = parts[0].shape
    width = features // 2
    ref[at(piece_at(0, pieces), part), :] = parts[0][...]
    for k in range(1, pieces):
        for number in range(2):
            ref[at(piece_at(k, pieces), part), number * width : (number + 1) * width] = parts[
                number * (pieces - 1) + k
            ][...]


def query_feed_forward(
    pieces, share, hidden_share, q1_ref, cot_ref, gain_ref, bias_ref,
    w_out, up_ref, down_ref, *rest,
):
    parts, rest = rest[: 2 * pieces - 1], rest[2 * pieces - 1 :]
    (
        q3_ref, dq2_ref, up_grad_ref, down_grad_ref, norm_ref, co_ref,
        q2, normed, chosen, hidden, slope, out, grad,
    ) = rest
    rows, features = q1_ref.shape
    width = up_ref.shape[2]
    step = pl.program_id(0)

    @pl.when(step == 0)
    def begin():
        place_parts(co_ref, pieces, parts)

        def first(i):
            span = at(i, STRIP)
            total = q1_ref[span, :] + plain(co_ref[span, :], w_out[0])
            q2[span, :] = total
            out[span, :] = total
            normed[span, :] = norm(total, gain_ref[4:5, :], bias_ref[4:5, :]).astype(NARROW)
            grad[span, :] = jnp.zeros_like(grad[span, :])

        loop(rows // STRIP, first)
        chosen[...] = right_t(
            chooser(chosen.shape[0], features, place_of() * share, share), normed[...]
        ).astype(NARROW)

    feed_forward_step(
        LONG, normed, up_ref.at[0], down_ref.at[0], cot_ref, hidden, slope, out, grad
    )
    up_grad_ref[...] = plain(chosen[...], slope[...]).astype(NARROW)
    begins = place_of() * hidden_share

    @pl.when(begins // width == step)
    def own_hidden():
        taken = right_t(
            chooser(down_grad_ref.shape[0], width, begins - step * width, hidden_share),
            hidden[...],
        ).astype(NARROW)
        down_grad_ref[...] = plain(taken, cot_ref[...]).astype(NARROW)

    @pl.when(step == pl.num_programs(0) - 1)
    def finish():
        norm_ref[...] = jnp.zeros_like(norm_ref)

        def last(i):
            span = at(i, STRIP)
            q3_ref[span, :] = out[span, :].astype(NARROW)
            piece, gain, bias = norm_back(q2[span, :], gain_ref[4:5, :], grad[span, :])
            dq2_ref[span, :] = cot_ref[span, :].astype(SINGLE) + piece
            norm_ref[0:1, :] += gain
            norm_ref[1:2, :] += bias

        loop(rows // STRIP, last)


def reverse_backward(
    pieces, length_ref, dx2_ref, mv_ref, vq_ref, vkv_ref, nx_ref, log_ref, a_out,
    *rest, launch=nothing, tick=nothing,
):
    dvq_ref, weight_ref, rest = rest[0], rest[1], rest[2:]
    k_refs, v_refs, rest = rest[:pieces], rest[pieces : 2 * pieces], rest[2 * pieces :]
    w_out, rounded, dmv, deltas, dkv, sem = rest
    rows, features = vq_ref.shape
    keys = vkv_ref.shape[0]
    part = k_refs[0].shape[0]
    (load,) = copies(sem, (a_out.at[3], w_out))
    rounded[...] = dx2_ref[...].astype(NARROW)
    load.wait()
    dmv[...] = right_t(rounded[...], w_out[...]).astype(NARROW)
    store_rows(
        weight_ref, slice(features, 2 * features), left_t(mv_ref[...], rounded[...])
    )
    deltas[...] = head_rows(dmv[...].astype(SINGLE) * mv_ref[...].astype(SINGLE))
    if dkv.shape[0] > keys:
        dkv[keys:, :] = jnp.zeros((dkv.shape[0] - keys, 2 * features), SINGLE)
    size = 256

    def pair(p):
        pl.when(p == 2)(lambda: tick(1))
        pl.when(p == 4)(lambda: tick(2))
        for strip in range(rows // size):
            span = slice(strip * size, (strip + 1) * size)

            def mask(scores):
                return jnp.where(iota(scores.shape, 0) < length_ref[0], scores, MASKED)

            dq, dk, dv = attend_back(
                vq_ref[span, at(p, PAIR)],
                vkv_ref[:, at(p, PAIR)],
                vkv_ref[:, at(p + features // PAIR, PAIR)],
                dmv[span, at(p, PAIR)],
                row_pair(log_ref, p, span),
                row_pair(deltas, p, span),
                mask,
            )
            dvq_ref[span, at(p, PAIR)] = (dq * (1.0 / math.sqrt(HEAD))).astype(NARROW)
            if strip == 0:
                dkv[0:keys, at(p, PAIR)] = dk
                dkv[0:keys, at(p + features // PAIR, PAIR)] = dv
            else:
                dkv[0:keys, at(p, PAIR)] += dk
                dkv[0:keys, at(p + features // PAIR, PAIR)] += dv

    loop(features // PAIR, pair)
    store_rows(weight_ref, slice(0, features), left_t(nx_ref[...], dvq_ref[...]))
    launch(1)
    for k in range(pieces):
        span = at(piece_at(k, pieces), part)
        k_refs[k][...] = dkv[span, 0:features].astype(NARROW)
        v_refs[k][...] = dkv[span, features:].astype(NARROW)


def cross_backward(
    pieces, share, dq2_ref, co_ref, cq_ref, ckv_ref, valid_ref, a_out, *rest
):
    log_parts, rest = rest[:pieces], rest[pieces:]
    dckv_ref, weight_ref, rest = rest[0], rest[1], rest[2:]
    q_refs, (w_out, rounded, dco, deltas, logs, turned, dq_all, dkv, sem) = (
        rest[:pieces],
        rest[pieces:],
    )
    rows, features = cq_ref.shape
    part = log_parts[0].shape[1]
    (load,) = copies(sem, (a_out.at[2], w_out))
    for k in range(pieces):
        logs[at(piece_at(k, pieces), part), :] = untwist(log_parts[k][...])
    turned[...] = turn(logs[0:rows, :])
    rounded[...] = dq2_ref[...].astype(NARROW)
    load.wait()
    dco[...] = right_t(rounded[...], w_out[...]).astype(NARROW)
    taken = right_t(
        chooser(weight_ref.shape[0], features, place_of() * share, share), co_ref[0:rows, :]
    ).astype(NARROW)
    weight_ref[...] = plain(taken, rounded[...]).astype(NARROW)
    deltas[...] = head_rows(dco[...].astype(SINGLE) * co_ref[0:rows, :].astype(SINGLE))
    if dq_all.shape[0] > rows:
        dq_all[rows:, :] = jnp.zeros((dq_all.shape[0] - rows, features), NARROW)
    edges = spans(rows, 512)

    def pair(p):
        for number, (start, end) in enumerate(edges):
            span = slice(start, end)
            dq, dk, dv = attend_back(
                cq_ref[span, at(p, PAIR)],
                ckv_ref[:, at(p, PAIR)],
                ckv_ref[:, at(p + features // PAIR, PAIR)],
                dco[span, at(p, PAIR)],
                row_pair(turned, p, span),
                row_pair(deltas, p, span),
                lambda scores: scores + valid_ref[...],
            )
            dq_all[span, at(p, PAIR)] = (dq * (1.0 / math.sqrt(HEAD))).astype(NARROW)
            if number == 0:
                dkv[:, at(p, PAIR)] = dk
                dkv[:, at(p + features // PAIR, PAIR)] = dv
            else:
                dkv[:, at(p, PAIR)] += dk
                dkv[:, at(p + features // PAIR, PAIR)] += dv

    loop(features // PAIR, pair)
    dckv_ref[...] = dkv[...].astype(NARROW)
    for k in range(pieces):
        q_refs[k][...] = dq_all[at(piece_at(k, pieces), part), :]


def patch_backward(
    x_ref, dx2_ref, x1_ref, nx_ref, n0_ref, pw_ref, mw_ref, dvq_ref, dckv_ref, gain_ref, a_in, a_out,
    kv_weight_ref, weight_ref, grad_ref, norm_ref,
    w_in, w_out, w_q, w_kv, dx1, rounded, dmw, deltas, dpw, sem,
    launch=nothing,
):
    rows, features = x_ref.shape
    loads = copies(
        sem,
        (a_in.at[3, :, pl.ds(0, features)], w_q),
        (a_in.at[2, :, pl.ds(features, 2 * features)], w_kv),
        (a_out.at[0], w_out),
        (a_in.at[0], w_in),
    )
    norm_ref[...] = jnp.zeros_like(norm_ref)
    for start in range(0, 2 * features, CHUNK):
        span = slice(start, start + CHUNK)
        store_rows(kv_weight_ref, span, left_t(nx_ref[...], dckv_ref[:, span]))
    launch(0)
    loads[0].wait()
    loads[1].wait()

    def first(i):
        span = at(i, GROUP)
        upstream = right_t(dvq_ref[span, :], w_q[...]) + right_t(dckv_ref[span, :], w_kv[...])
        part, gain, bias = norm_back(x1_ref[span, :], gain_ref[3:4, :], upstream)
        total = dx2_ref[span, :] + part
        dx1[span, :] = total
        rounded[span, :] = total.astype(NARROW)
        norm_ref[0:1, :] += gain
        norm_ref[1:2, :] += bias

    loop(rows // GROUP, first)
    loads[2].wait()
    dmw[...] = right_t(rounded[...], w_out[...]).astype(NARROW)
    store_rows(
        weight_ref, slice(3 * features, 4 * features), left_t(mw_ref[...], rounded[...])
    )
    deltas[...] = head_rows(dmw[...].astype(SINGLE) * mw_ref[...].astype(SINGLE))
    window = jnp.where(
        iota((WINDOWS, WINDOWS), 0) // WIN == iota((WINDOWS, WINDOWS), 1) // WIN, 0.0, MASKED
    )

    def group(i):
        span = at(i, WINDOWS)
        for pair in range(features // PAIR):
            lane = pair * PAIR
            dq, dk, dv = attend_back(
                pw_ref[span, lane : lane + PAIR],
                pw_ref[span, features + lane : features + lane + PAIR],
                pw_ref[span, 2 * features + lane : 2 * features + lane + PAIR],
                dmw[span, lane : lane + PAIR],
                None,
                [deltas[2 * pair + w : 2 * pair + w + 1, span] for w in range(2)],
                lambda scores: scores + window,
            )
            dpw[span, lane : lane + PAIR] = (dq * (1.0 / math.sqrt(HEAD))).astype(NARROW)
            dpw[span, features + lane : features + lane + PAIR] = dk.astype(NARROW)
            dpw[span, 2 * features + lane : 2 * features + lane + PAIR] = dv.astype(NARROW)

    loop(rows // WINDOWS, group)
    for start in range(0, 3 * features, CHUNK):
        span = slice(start, start + CHUNK)
        store_rows(weight_ref, span, left_t(n0_ref[...], dpw[:, span]))
    launch(1)
    loads[3].wait()

    def last(i):
        span = at(i, GROUP)
        upstream = right_t(dpw[span, :], w_in[...])
        part, gain, bias = norm_back(x_ref[span, :].astype(SINGLE), gain_ref[0:1, :], upstream)
        grad_ref[span, :] = dx1[span, :] + part
        norm_ref[2:3, :] += gain
        norm_ref[3:4, :] += bias

    loop(rows // GROUP, last)


def share_backward(
    pieces, q1, nq, gain_ref, a_in, *rest, launch=nothing
):
    parts = [rest[k * pieces : (k + 1) * pieces] for k in range(3)]
    rest = rest[3 * pieces :]
    grad_ref, weight_ref, norm_ref, w_q, w_kv, summed, q1_ref, nq_ref, sem = rest
    part, features = q1_ref.shape
    *loads, load_q, load_n = copies(
        sem,
        (a_in.at[2, :, pl.ds(0, features)], w_q),
        (a_in.at[3, :, pl.ds(features, 2 * features)], w_kv),
        (q1.at[at(place_of(), part), :], q1_ref),
        (nq.at[at(place_of(), part), :], nq_ref),
    )
    load_n.wait()
    for k in range(3):
        span = slice(k * features, (k + 1) * features)
        total = functools.reduce(jnp.add, [one[...].astype(SINGLE) for one in parts[k]])
        summed[:, span] = total.astype(NARROW)
        store_rows(weight_ref, span, left_t(nq_ref[...], summed[:, span]))
    launch(1)
    for load in loads:
        load.wait()
    upstream = right_t(summed[:, 0:features], w_q[...]) + right_t(summed[:, features:], w_kv[...])
    load_q.wait()
    piece, gain, bias = norm_back(q1_ref[...], gain_ref[2:3, :], upstream)
    grad_ref[...] = piece.astype(NARROW)
    norm_ref[...] = jnp.zeros_like(norm_ref)
    norm_ref[0:1, :] = gain
    norm_ref[1:2, :] = bias


def causal_backward(
    pieces, share, q_ref, dq2_ref, n1_ref, pq_ref, mq_ref, log_ref, cross_ref, gain_ref,
    a_in, a_out, *rest
):
    parts, rest = rest[: 2 * pieces - 1], rest[2 * pieces - 1 :]
    (
        weight_ref, grad_ref, norm_ref,
        w_in, w_out, gathered, dq1, rounded, dmq, deltas, dkv, dpq, sem,
    ) = rest
    rows, features = q_ref.shape
    loads = copies(sem, (a_out.at[1], w_out), (a_in.at[1], w_in))
    place_parts(gathered, pieces, parts)

    def first(i):
        span = at(i, STRIP)
        total = dq2_ref[span, :] + gathered[span, :].astype(SINGLE)
        dq1[span, :] = total
        rounded[span, :] = total.astype(NARROW)

    loop(rows // STRIP, first)
    loads[0].wait()
    dmq[...] = right_t(rounded[...], w_out[...]).astype(NARROW)
    chosen = chooser(weight_ref.shape[0], features, place_of() * share, share)
    taken = right_t(chosen, mq_ref[...]).astype(NARROW)
    weight_ref[:, 3 * features : 4 * features] = plain(taken, rounded[...]).astype(NARROW)
    weight_ref[:, 4 * features : 5 * features] = cross_ref[...]
    weight_ref[:, 5 * features :] = jnp.zeros_like(weight_ref[:, 5 * features :])
    deltas[...] = head_rows(dmq[...].astype(SINGLE) * mq_ref[...].astype(SINGLE))
    edges = spans(rows, 256)

    def pair(p):
        for number, (start, end) in reversed(list(enumerate(edges))):
            span = slice(start, end)

            def mask(scores, start=start):
                shape = scores.shape
                return jnp.where(iota(shape, 0) <= iota(shape, 1) + start, scores, MASKED)

            dq, dk, dv = attend_back(
                pq_ref[span, at(p, PAIR)],
                pq_ref[0:end, at(p + features // PAIR, PAIR)],
                pq_ref[0:end, at(p + 2 * features // PAIR, PAIR)],
                dmq[span, at(p, PAIR)],
                row_pair(log_ref, p, span),
                row_pair(deltas, p, span),
                mask,
            )
            dpq[span, at(p, PAIR)] = (dq * (1.0 / math.sqrt(HEAD))).astype(NARROW)
            if end == rows:
                dkv[0:end, 0:PAIR] = dk
                dkv[0:end, PAIR:] = dv
            else:
                dkv[0:end, 0:PAIR] += dk
                dkv[0:end, PAIR:] += dv
        dpq[:, at(p + features // PAIR, PAIR)] = dkv[:, 0:PAIR].astype(NARROW)
        dpq[:, at(p + 2 * features // PAIR, PAIR)] = dkv[:, PAIR:].astype(NARROW)

    loop(features // PAIR, pair)
    taken = right_t(chosen, n1_ref[...]).astype(NARROW)
    weight_ref[:, 0 : 3 * features] = plain(taken, dpq[...]).astype(NARROW)
    loads[1].wait()
    norm_ref[...] = jnp.zeros_like(norm_ref)

    def last(i):
        span = at(i, STRIP)
        upstream = right_t(dpq[span, :], w_in[...])
        piece, gain, bias = norm_back(q_ref[span, :].astype(SINGLE), gain_ref[1:2, :], upstream)
        grad_ref[span, :] = dq1[span, :] + piece
        norm_ref[0:1, :] += gain
        norm_ref[1:2, :] += bias

    loop(rows // STRIP, last)


def bits_of(count):
    return max(count - 1, 0).bit_length()


def swap(tensor, axis, mask):
    return lax.ppermute(tensor, axis, [(i, i ^ mask) for i in range(lax.axis_size(axis))])


def pick(tensor, place, dim):
    return lax.dynamic_index_in_dim(tensor, place, dim, keepdims=False)


def fold(tensor, axis, bit, dim):
    own = (lax.axis_index(axis) >> bit) & 1
    arrived = swap(pick(tensor, 1 - own, dim).astype(NARROW), axis, 1 << bit)
    return pick(tensor, own, dim).astype(SINGLE) + arrived.astype(SINGLE)


def unfold(tensor, axis, bit, dim):
    own = (lax.axis_index(axis) >> bit) & 1
    arrived = swap(tensor, axis, 1 << bit)
    return jnp.where(
        own == 0,
        jnp.stack((tensor, arrived), axis=dim),
        jnp.stack((arrived, tensor), axis=dim),
    )


def scatter_blk(tensor):
    bits = bits_of(lax.axis_size("blk"))
    tensor = tensor.reshape((2,) * bits + tensor.shape[1:])
    for bit in range(bits):
        tensor = fold(tensor, "blk", bit, bits - 1 - bit)
    return tensor


def sum_rep_scatter(tensor, dim):
    bits = bits_of(lax.axis_size("rep"))
    shape = tensor.shape
    tensor = tensor.reshape(
        shape[:dim] + (2,) * bits + (shape[dim] // 2**bits,) + shape[dim + 1 :]
    )
    for bit in range(bits):
        tensor = fold(tensor, "rep", bit, dim)
    return tensor


def gather_rep(tensor, dim):
    bits = bits_of(lax.axis_size("rep"))
    for bit in reversed(range(bits)):
        tensor = unfold(tensor, "rep", bit, dim)
    shape = tensor.shape
    return tensor.reshape(shape[:dim] + (-1,) + shape[dim + bits + 1 :])


def reduce_all(tensor):
    count = lax.axis_size("blk")
    tensor = tensor.reshape(count, tensor.shape[0] // count, tensor.shape[1])
    tensor = sum_rep_scatter(tensor, 1)
    tensor = scatter_blk(tensor).astype(NARROW)
    return gather_rep(tensor, 0)


def reduce_rep(tensor):
    return gather_rep(sum_rep_scatter(tensor, 0).astype(NARROW), 0)


def exchange(pieces):
    whole = lax.all_to_all(jnp.stack(pieces), "blk", 0, 0)
    return [whole[k] for k in range(len(pieces))]


def gather(tensor):
    count = lax.axis_size("blk")
    whole = lax.all_gather(tensor, "blk")
    return [whole[k] for k in range(count)]


def whole(ref):
    return ref


class Fold:
    def __init__(self, own, take, arrived, shape, keep=whole, keep_shape=None):
        self.own, self.take, self.arrived, self.shape = own, take, arrived, shape
        self.keep, self.keep_shape = keep, keep_shape or shape


class Move:
    late = None

    def __init__(self, source, shape, axis, flip, take=whole, phase=0):
        self.source, self.shape, self.axis, self.flip, self.take = source, shape, axis, flip, take
        self.phase = phase


def in_order(held, rep):
    for weight in (1, 2):
        flip = (rep // weight) % 2 == 1
        held = [jnp.where(flip, held[k ^ weight], held[k]) for k in range(4)]
    return held


def lanes_of(ref, start, width):
    return ref.at[(slice(None),) * (len(ref.shape) - 1) + (pl.ds(start, width),)]


class Reduction:
    def __init__(self, tensor):
        if len(tensor.shape) == 2:
            blocks = lax.axis_size("blk")
            height = tensor.shape[0] // blocks
            tensor = tensor.reshape(blocks // 2, 2, 2, height // 2, tensor.shape[1])
        self.tensor, self.take, self.arrived, self.shape = tensor, whole, [], tensor.shape

    def fold(self, keep=whole, keep_shape=None):
        return Fold(self.tensor, self.take, self.arrived, self.shape, keep, keep_shape)

    def moves(self, stage):
        shape = self.shape
        if stage == "core":
            self.next = shape[:2] + shape[3:]
            return [
                Move(self.tensor, self.next, "rep", 1,
                     lambda ref: ref.at[:, :, 1 - place_of("rep") % 2])
            ]
        if stage == "x":
            width = shape[-1] // 2
            self.next = shape[:-1] + (width,)

            def own(ref):
                return lanes_of(ref, pl.multiple_of((place_of("rep") // 2) * width, width), width)

            def other(ref):
                start = (1 - place_of("rep") // 2) * width
                return lanes_of(ref, pl.multiple_of(start, width), width)

            return [Move(self.fold(own, self.next), self.next, "rep", 2, other)]
        if stage == "y":
            self.next = shape[:1] + shape[2:]
            fold = self.fold(lambda ref: ref.at[:, place_of() % 2], self.next)
            return [Move(fold, self.next, "blk", 1, lambda ref: ref.at[:, 1 - place_of() % 2])]
        if stage == "z":
            length = shape[0]
            self.next = shape[1:]
            fold = self.fold(lambda ref: ref.at[place_of() // 2], self.next)
            return [
                Move(fold, self.next, "blk", 2 * k,
                     lambda ref, k=k: ref.at[flipped(place_of() // 2, k, length)])
                for k in range(1, length)
            ]
        if stage == "back":
            fold = self.fold()
            return [Move(fold, shape, "rep", k) for k in range(1, 4)]
        if stage == "back_x":
            return [Move(self.fold(), shape, "rep", 2)]
        return [Move(self.tensor, shape, "rep", 1), Move(self.other, shape, "rep", 1)]

    def absorb(self, stage, arrived, kept):
        if stage == "core":
            self.take = lambda ref: ref.at[:, :, place_of("rep") % 2]
        else:
            self.take = whole
        if kept:
            self.tensor = kept[0]
        if stage in ("back", "back_x", "back_core"):
            if stage == "back_x":
                self.other = arrived[0]
                return
            rep = lax.axis_index("rep")
            if stage == "back":
                held = [self.tensor] + list(arrived)
            else:
                held = [self.tensor, arrived[0], self.other, arrived[1]]
            held = in_order(held, rep)
            self.tensor = jnp.concatenate(
                [jnp.concatenate((held[k], held[k + 2]), axis=1) for k in range(2)], axis=0
            )
            return
        self.shape, self.arrived = self.next, list(arrived)


class RepSum:
    def __init__(self, tensor, dim):
        self.tensor, self.dim = tensor, dim

    def moves(self, stage):
        if stage == "out":
            self.shape = list(self.tensor.shape)
            size = self.shape[self.dim] = self.shape[self.dim] // 4

            def quarter(ref, k):
                span = pl.ds(pl.multiple_of(flipped(place_of("rep"), k, 4) * size, size), size)
                return ref.at[span, :] if self.dim == 0 else ref.at[:, span]

            self.quarter = quarter
            return [
                Move(self.tensor, tuple(self.shape), "rep", k, lambda ref, k=k: quarter(ref, k))
                for k in range(1, 4)
            ]
        fold = Fold(
            self.tensor, lambda ref: self.quarter(ref, 0), self.arrived, tuple(self.shape)
        )
        return [Move(fold, tuple(self.shape), "rep", k) for k in range(1, 4)]

    def absorb(self, stage, arrived, kept):
        if stage == "out":
            self.arrived = list(arrived)
            return
        held = in_order([kept[0]] + list(arrived), lax.axis_index("rep"))
        self.tensor = jnp.concatenate(held, axis=self.dim)


class Exchange:
    def __init__(self, pieces):
        self.pieces = pieces

    def moves(self, stage):
        return [Move(one, one.shape, "blk", k) for k, one in enumerate(self.pieces) if k]

    def absorb(self, stage, arrived, kept):
        self.result = self.pieces[:1] + list(arrived)


class Pieces:
    def __init__(self, tensor, part, start, width):
        self.tensor, self.part, self.start, self.width = tensor, part, start, width

    def moves(self, stage):
        part, span = self.part, slice(self.start, self.start + self.width)
        count = lax.axis_size("blk")
        return [
            Move(self.tensor, (part, self.width), "blk", k,
                 lambda ref, k=k: ref.at[at(flipped(place_of(), k, count), part), span])
            for k in range(1, count)
        ]

    def absorb(self, stage, arrived, kept):
        self.result = list(arrived)


class Gather:
    def __init__(self, tensor):
        self.tensor = tensor

    def moves(self, stage):
        return [
            Move(self.tensor, self.tensor.shape, "blk", k) for k in range(1, lax.axis_size("blk"))
        ]

    def absorb(self, stage, arrived, kept):
        self.result = [self.tensor] + list(arrived)


class Spread:
    def __init__(self, tensor):
        self.tensor = tensor

    def moves(self, stage):
        count = lax.axis_size("blk")
        rows, width = self.tensor.shape[0], self.tensor.shape[1] // 2
        moves, self.places = [], []
        for number in range(2):
            span = slice(number * width, (number + 1) * width)
            own = lambda ref, span=span: ref.at[:, span]
            along = []
            for k in range(2, count, 2):
                along.append(Move(self.tensor, (rows, width), "blk", k, own, number))
                self.places.append((number, k))
            moves += along
            moves.append(Move(self.tensor, (rows, width), "blk", 1, own, number + 1))
            self.places.append((number, 1))
            for one in along:
                moves.append(Move(one, (rows, width), "blk", 1, whole, number + 1))
                self.places.append((number, one.flip + 1))
        return moves

    def absorb(self, stage, arrived, kept):
        found = dict(zip(self.places, arrived))
        count = lax.axis_size("blk")
        self.result = [found[number, k] for number in range(2) for k in range(1, count)]


class Norms:
    def __init__(self, tensor):
        self.tensor = tensor

    def moves(self, stage):
        axis = "rep" if stage == "out" else "blk"
        return [
            Move(self.tensor, self.tensor.shape, axis, k) for k in range(1, lax.axis_size(axis))
        ]

    def absorb(self, stage, arrived, kept):
        for one in arrived:
            self.tensor = self.tensor + one


VMEM = pl.BlockSpec(memory_space=pltpu.VMEM)
SMEM = pl.BlockSpec(memory_space=pltpu.SMEM)
ANY = pl.BlockSpec(memory_space=pl.ANY)


def like(*shape, kind=NARROW):
    return jax.ShapeDtypeStruct(shape, kind)


def index_of(items, item):
    return next(k for k, one in enumerate(items) if one is item)


def call(
    kernel, outs, operands, specs, scratch, flops, grid=None, out_specs=None, semaphores=0,
    moves=(), ident=None, ticking=False,
):
    scratch = [pltpu.VMEM(shape, kind) for shape, kind in scratch]
    if semaphores:
        scratch.append(pltpu.SemaphoreType.DMA((semaphores,)))
    out_specs = [VMEM] * len(outs) if out_specs is None else out_specs
    extra = {} if grid is None else {"grid": grid}
    params = {}
    sources, folds = [], []

    def need(array):
        if not any(array is one for one in sources):
            sources.append(array)

    for move in moves:
        if isinstance(move.source, Fold):
            if not any(move.source is one for one in folds):
                folds.append(move.source)
                for array in [move.source.own] + move.source.arrived:
                    need(array)
        elif move.late is None and not isinstance(move.source, Move):
            need(move.source)
    fixed_in, fixed_out = len(operands), len(outs)
    partners = sorted({(move.axis, move.flip) for move in moves})
    body_kernel = kernel
    lasts = max([move.phase for move in moves], default=0)
    if moves:
        params = {"collective_id": ident, "has_side_effects": True}
        terms = sum(1 + len(fold.arrived) for fold in folds)
        for fold in folds:
            scratch += [pltpu.VMEM(fold.shape, NARROW)] * (1 + len(fold.arrived))
        scratch += [
            pltpu.SemaphoreType.DMA((max(terms, 1),)),
            pltpu.SemaphoreType.DMA((max(len(folds), 1),)),
        ]
        scratch += [pltpu.SemaphoreType.DMA((len(moves),))] * 2

        def body_kernel(*refs):
            ins, refs = refs[:fixed_in], refs[fixed_in:]
            sent, refs = refs[: len(sources)], refs[len(sources) :]
            results, refs = refs[:fixed_out], refs[fixed_out:]
            landed, refs = refs[: len(moves)], refs[len(moves) :]
            kept, refs = refs[: len(folds)], refs[len(folds) :]
            rest, refs = refs[: len(refs) - 4 - terms], refs[len(refs) - 4 - terms :]
            buffers, (load_sem, keep_sem, send_sem, recv_sem) = refs[:terms], refs[terms:]
            before = {}
            for move in moves:
                if isinstance(move.source, Move):
                    number = index_of(moves, move.source)
                    before[number] = min(move.phase, before.get(number, move.phase))

            def target(axis, flip):
                return {axis: flipped(lax.axis_index(axis), flip, lax.axis_size(axis))}

            def buffers_of(fold):
                start = sum(1 + len(one.arrived) for one in folds[: index_of(folds, fold)])
                return start, buffers[start : start + 1 + len(fold.arrived)]

            def made(k):
                move = moves[k]
                if move.late is not None:
                    source = results[move.late]
                elif isinstance(move.source, Fold):
                    source = buffers_of(move.source)[1][0]
                elif isinstance(move.source, Move):
                    source = landed[index_of(moves, move.source)]
                else:
                    source = sent[index_of(sources, move.source)]
                return pltpu.make_async_remote_copy(
                    src_ref=move.take(source),
                    dst_ref=landed[k],
                    send_sem=send_sem.at[k],
                    recv_sem=recv_sem.at[k],
                    device_id=target(move.axis, move.flip),
                    device_id_type=pl.DeviceIdType.MESH,
                )

            def loads(fold):
                start, held = buffers_of(fold)
                return [
                    pltpu.make_async_copy(
                        (fold.take if k == 0 else whole)(sent[index_of(sources, array)]),
                        held[k],
                        load_sem.at[start + k],
                    )
                    for k, array in enumerate([fold.own] + fold.arrived)
                ]

            def keeping(k):
                fold = folds[k]
                return pltpu.make_async_copy(
                    fold.keep(buffers_of(fold)[1][0]), kept[k], keep_sem.at[k]
                )

            def add(fold):
                held = buffers_of(fold)[1]

                def one(index):
                    if len(held) == 2:
                        held[0][index] = held[0][index] + held[1][index]
                    elif len(held) > 2:
                        held[0][index] = functools.reduce(
                            jnp.add, [part[index].astype(SINGLE) for part in held]
                        ).astype(NARROW)

                if len(fold.shape) == 2:
                    one((slice(None), slice(None)))
                else:
                    loop(fold.shape[0], one)

            def begin():
                for fold in folds:
                    for load in loads(fold):
                        load.start()
                barrier = pltpu.get_barrier_semaphore()
                for axis, flip in partners:
                    pl.semaphore_signal(
                        barrier, inc=1, device_id=target(axis, flip),
                        device_id_type=pl.DeviceIdType.MESH,
                    )
                pl.semaphore_wait(barrier, len(partners))
                for k, move in enumerate(moves):
                    if move.phase == 0 and move.late is None and not isinstance(move.source, Fold):
                        made(k).start()
                for number, fold in enumerate(folds):
                    for load in loads(fold):
                        load.wait()
                    add(fold)
                    for k, move in enumerate(moves):
                        if move.source is fold:
                            made(k).start()
                    keeping(number).start()

            def launch(which):
                for k in range(len(moves)):
                    if moves[k].late == which:
                        made(k).start()

            def tick(phase):
                for k, needed in before.items():
                    if needed == phase:
                        made(k).wait_recv()
                for k, move in enumerate(moves):
                    if move.phase == phase:
                        made(k).start()

            def finish():
                if not ticking:
                    for phase in range(1, lasts + 1):
                        tick(phase)
                for k in range(len(moves)):
                    made(k).wait_send()
                    if k not in before:
                        made(k).wait_recv()
                for k in range(len(folds)):
                    keeping(k).wait()

            options = {}
            if any(move.late is not None for move in moves):
                options["launch"] = launch
            if ticking:
                options["tick"] = tick
            if grid is None:
                begin()
                kernel(*ins, *results, *rest, **options)
                finish()
            else:
                pl.when(pl.program_id(0) == 0)(begin)
                kernel(*ins, *results, *rest, **options)
                pl.when(pl.program_id(0) == pl.num_programs(0) - 1)(finish)

    result = pl.pallas_call(
        body_kernel,
        out_shape=list(outs)
        + [
            like(*m.shape, kind=m.source.dtype if hasattr(m.source, "dtype") else NARROW)
            for m in moves
        ]
        + [like(*fold.keep_shape) for fold in folds],
        in_specs=list(specs) + [ANY] * len(sources),
        out_specs=list(out_specs) + [ANY] * (len(moves) + len(folds)),
        scratch_shapes=scratch,
        compiler_params=pltpu.CompilerParams(vmem_limit_bytes=60 * 2**20, **params),
        cost_estimate=pl.CostEstimate(
            flops=int(flops),
            bytes_accessed=sum(o.size * o.dtype.itemsize for o in operands),
            transcendentals=0,
        ),
        **extra,
    )(*operands, *sources)
    end = fixed_out + len(moves)
    return list(result[:fixed_out]), list(result[fixed_out:end]), (folds, list(result[end:]))


class Courier:
    def __init__(self, active):
        self.active, self.waiting, self.ident = active, [], 0

    def load(self, *jobs):
        self.waiting += jobs

    def run(self, kernel, outs, operands, specs, scratch, flops, **extra):
        jobs, self.waiting = self.waiting, []
        moves, ends = [], []
        for job, stage, *late in jobs:
            added = job.moves(stage)
            for move in added:
                move.late = late[0] if late else None
            moves += added
            ends.append(len(moves))
        if moves:
            self.ident += 1
        results, arrived, (folds, kept) = call(
            kernel, outs, operands, specs, scratch, flops, moves=tuple(moves), ident=self.ident, **extra
        )
        start = 0
        for (job, stage, *late), end in zip(jobs, ends):
            if late:
                job.tensor = results[late[0]]
            own = [
                kept[k]
                for k, fold in enumerate(folds)
                if any(move.source is fold for move in moves[start:end])
            ]
            job.absorb(stage, arrived[start:end], own)
            start = end
        return results


def in_halves(arrays):
    width = arrays[0].shape[1] // 2
    return (
        arrays[:1] + [one[:, :width] for one in arrays[1:]] + [one[:, width:] for one in arrays[1:]]
    )


def body(
    patches,
    queries,
    window_valid,
    answer_length,
    norm_gain,
    norm_bias,
    attn_in,
    attn_out,
    mlp_in,
    mlp_out,
    cot_patches,
    cot_queries,
):
    x, q, cot_x, cot_q = patches[0], queries[0], cot_patches[0], cot_queries[0]
    rows, features = x.shape
    count = q.shape[0]
    hidden = mlp_in.shape[2]
    blocks = lax.axis_size("blk")
    place = lax.axis_index("blk").astype(jnp.int32)
    share = features // blocks
    hidden_share = hidden // blocks
    share_rows = -(-share // 16) * 16
    hidden_rows = -(-hidden_share // 16) * 16
    part = -(-count // (blocks * 16)) * 16
    padded = part * blocks
    wide = 3 * features
    last = wide + features + features
    causal_columns = -(-last // 512) * 512
    leader = (place == 0).astype(SINGLE)
    valid = jnp.where(jnp.repeat(window_valid[0], WIN) > 0, 0.0, MASKED).astype(SINGLE)
    carried = blocks == DIRECT and lax.axis_size("rep") == 4 and share % 32 == 0
    courier = Courier(carried)

    def own_columns(tensor):
        return lax.dynamic_slice_in_dim(tensor, place * share, share, 1)

    square = 2.0 * features * features
    run = courier.run

    n0, pw, mw, x1, nx, vq, ckv = run(
        window_forward,
        [
            like(rows, features), like(rows, wide), like(rows, features),
            like(rows, features, kind=SINGLE), like(rows, features), like(rows, features),
            like(rows, 2 * features),
        ],
        [x, norm_gain, norm_bias, attn_in, attn_out],
        [VMEM, VMEM, VMEM, ANY, ANY],
        [((features, wide), NARROW), ((features, features), NARROW),
         ((features, features), NARROW), ((features, 2 * features), NARROW)],
        rows * square * 9,
        semaphores=4,
    )
    n1, pq, mq, q1, nq, cq, vkv, log_q = run(
        causal_forward,
        [
            like(count, features), like(count, wide), like(count, features),
            like(padded, features, kind=SINGLE), like(padded, features), like(count, features),
            like(count, 2 * features), like(16, count, kind=SINGLE),
        ],
        [q, norm_gain, norm_bias, attn_in, attn_out],
        [VMEM, VMEM, VMEM, ANY, ANY],
        [((features, wide), NARROW), ((features, features), NARROW),
         ((features, features), NARROW), ((features, 2 * features), NARROW),
         ((count, PAIR), SINGLE)],
        count * square * 15,
        semaphores=4,
    )
    outs, *log_pieces = run(
        functools.partial(cross_forward, blocks),
        [like(padded, features)] + [like(16, part, kind=SINGLE)] * blocks,
        [cq, ckv, valid[None, :]],
        [VMEM, VMEM, VMEM],
        [((padded, PAIR), SINGLE)],
        count * square * 6,
    )
    logs = Exchange(log_pieces)
    halves = [Pieces(outs, part, k * features // 2, features // 2) for k in range(2)]
    if carried:
        courier.load((logs, ""), (halves[0], ""))
    mv, x2, log_v = run(
        reverse_forward,
        [like(rows, features), like(rows, features, kind=SINGLE), like(16, rows, kind=SINGLE)],
        [answer_length, vq, vkv, x1, attn_out],
        [SMEM, VMEM, VMEM, VMEM, ANY],
        [((features, features), NARROW), ((rows, PAIR), SINGLE)],
        rows * square * 8,
        semaphores=1,
    )
    if carried:
        courier.load((halves[1], ""))
    fixed = lambda *shape: pl.BlockSpec(shape, lambda j: (0,) * len(shape))
    x3, dx2, up_x, down_x, norm_five = run(
        patch_feed_forward,
        [
            like(rows, features), like(rows, features, kind=SINGLE), like(features, hidden),
            like(hidden, features), like(8, features, kind=SINGLE),
        ],
        [x2, cot_x, norm_gain, norm_bias, mlp_in, mlp_out],
        [
            fixed(rows, features), fixed(rows, features), fixed(6, features), fixed(6, features),
            pl.BlockSpec((1, features, CHUNK), lambda j: (0, 0, j)),
            pl.BlockSpec((1, CHUNK, features), lambda j: (0, j, 0)),
        ],
        [((rows, features), NARROW), ((rows, CHUNK), NARROW), ((rows, CHUNK), NARROW),
         ((rows, features), SINGLE), ((rows, features), SINGLE)],
        rows * square * 24,
        grid=(hidden // CHUNK,),
        out_specs=[
            fixed(rows, features), fixed(rows, features),
            pl.BlockSpec((features, CHUNK), lambda j: (0, j)),
            pl.BlockSpec((CHUNK, features), lambda j: (j, 0)),
            fixed(8, features),
        ],
    )
    if carried:
        merged = run(
            functools.partial(merge_blocks, blocks),
            [like(part, features), like(16, part, kind=SINGLE)],
            [outs] + logs.result + halves[0].result + halves[1].result,
            [VMEM] * (3 * blocks - 1),
            [],
            padded * square,
        )
        co_parts, log_parts = Spread(merged[0]), Gather(merged[1])
        up_x, down_x = Reduction(up_x), Reduction(down_x)
        reverse_weight = Reduction(like(blocks // 2, 2, 2, share // 2, 2 * features))
        courier.load(
            (co_parts, ""), (log_parts, ""), (up_x, "core"), (down_x, "core"),
            (reverse_weight, "core", 1),
        )
    else:
        whole_logs = jnp.stack(exchange(log_pieces))
        merged_log = jax.nn.logsumexp(whole_logs, axis=0)
        weights = jnp.transpose(jnp.exp(whole_logs - merged_log)[:, :HEADS], (0, 2, 1))
        shares = lax.all_to_all(outs.reshape(blocks, part, features), "blk", 0, 0)
        merged_out = jnp.sum(jnp.repeat(weights, HEAD, axis=2) * shares.astype(SINGLE), axis=0)
        co_parts, log_parts = Spread(None), Gather(None)
        co_parts.tensor, *co_parts.result = in_halves(gather(merged_out.astype(NARROW)))
        log_parts.result = gather(merged_log)
    folded = (blocks // 2, 2, 2, share // 2) if carried else (features,)
    dvq, reverse_grad, *kv_pieces = run(
        functools.partial(reverse_backward, blocks),
        [like(rows, features), like(*folded, 2 * features)]
        + [like(part, features)] * (2 * blocks),
        [answer_length, dx2, mv, vq, vkv, nx, log_v, attn_out],
        [SMEM, VMEM, VMEM, VMEM, VMEM, VMEM, VMEM, ANY],
        [((features, features), NARROW), ((rows, features), NARROW), ((rows, features), NARROW),
         ((16, rows), SINGLE), ((padded, 2 * features), SINGLE)],
        rows * square * 16,
        semaphores=1,
        ticking=carried,
    )
    k_parts, v_parts = Exchange(kv_pieces[:blocks]), Exchange(kv_pieces[blocks:])
    if carried:
        courier.load((k_parts, ""), (up_x, "x"), (reverse_weight, "x"))
    else:
        k_parts.result, v_parts.result = exchange(k_parts.pieces), exchange(v_parts.pieces)
    q3, dq2, up_q, down_q, norm_four, co = run(
        functools.partial(query_feed_forward, blocks, share, hidden_share),
        [
            like(count, features), like(count, features, kind=SINGLE), like(share_rows, hidden),
            like(hidden_rows, features), like(8, features, kind=SINGLE), like(padded, features),
        ],
        [q1, cot_q, norm_gain, norm_bias, attn_out, mlp_in, mlp_out, co_parts.tensor]
        + co_parts.result,
        [
            fixed(count, features), fixed(count, features), fixed(6, features),
            fixed(6, features), pl.BlockSpec((1, features, features), lambda j: (2, 0, 0)),
            pl.BlockSpec((1, features, CHUNK), lambda j: (1, 0, j)),
            pl.BlockSpec((1, CHUNK, features), lambda j: (1, j, 0)),
            fixed(part, features),
        ] + [fixed(part, features // 2)] * (2 * blocks - 2),
        [((count, features), SINGLE), ((count, features), NARROW), ((share_rows, count), NARROW),
         ((count, CHUNK), NARROW), ((count, CHUNK), NARROW),
         ((count, features), SINGLE), ((count, features), SINGLE)],
        count * square * 18,
        grid=(hidden // CHUNK,),
        out_specs=[
            fixed(count, features), fixed(count, features),
            pl.BlockSpec((share_rows, CHUNK), lambda j: (0, j)),
            fixed(hidden_rows, features), fixed(8, features), fixed(padded, features),
        ],
    )
    if carried:
        up_q, down_q = RepSum(up_q, 1), RepSum(down_q, 0)
        courier.load((v_parts, ""), (down_x, "x"), (up_x, "y"))
    dckv, cross_out_weight, *q_pieces = run(
        functools.partial(cross_backward, blocks, share),
        [like(rows, 2 * features), like(share_rows, features)] + [like(part, features)] * blocks,
        [dq2, co, cq, ckv, valid[:, None], attn_out] + log_parts.result,
        [VMEM, VMEM, VMEM, VMEM, VMEM, ANY] + [VMEM] * blocks,
        [((features, features), NARROW), ((count, features), NARROW), ((count, features), NARROW),
         ((16, count), SINGLE), ((padded, PAIR), SINGLE), ((16, count), SINGLE),
         ((padded, features), NARROW), ((rows, 2 * features), SINGLE)],
        count * square * 12,
        semaphores=1,
    )
    q_parts = Exchange(q_pieces)
    if carried:
        kv_weight = Reduction(like(blocks // 2, 2, 2, share // 2, 2 * features))
        window_weight = Reduction(like(blocks // 2, 2, 2, share // 2, 4 * features))
        courier.load(
            (q_parts, ""), (down_x, "y"), (reverse_weight, "y"), (up_q, "out"), (down_q, "out"),
            (kv_weight, "core", 0), (window_weight, "core", 1),
        )
    else:
        q_parts.result = exchange(q_pieces)
    kv_grad, window_grad, grad_x, norm_x = run(
        patch_backward,
        [
            like(*folded, 2 * features), like(*folded, 4 * features),
            like(rows, features, kind=SINGLE), like(8, features, kind=SINGLE),
        ],
        [x, dx2, x1, nx, n0, pw, mw, dvq, dckv, norm_gain, attn_in, attn_out],
        [VMEM] * 10 + [ANY, ANY],
        [((features, wide), NARROW), ((features, features), NARROW),
         ((features, features), NARROW), ((features, 2 * features), NARROW),
         ((rows, features), SINGLE), ((rows, features), NARROW), ((rows, features), NARROW),
         ((16, rows), SINGLE), ((rows, wide), NARROW)],
        rows * square * 24,
        semaphores=4,
    )
    if carried:
        share_weight = Reduction(like(blocks // 2, 2, 2, share // 2, wide))
        courier.load((share_weight, "core", 1))
    dq1_share, share_grad, norm_two = run(
        functools.partial(share_backward, blocks),
        [like(part, features), like(*folded, wide), like(8, features, kind=SINGLE)],
        [q1, nq, norm_gain, attn_in]
        + q_parts.result + k_parts.result + v_parts.result,
        [ANY, ANY, VMEM, ANY] + [VMEM] * (3 * blocks),
        [((features, features), NARROW), ((features, 2 * features), NARROW),
         ((part, wide), NARROW), ((part, features), SINGLE), ((part, features), NARROW)],
        part * square * 6,
        semaphores=4,
    )
    dq1_parts = Spread(dq1_share)

    def arrive(*jobs):
        courier.load(*jobs)
        run(nothing, [], [], [], [], 0)

    if carried:
        arrive((dq1_parts, ""), (window_weight, "x"))
        courier.load(
            (up_x, "z"), (down_x, "z"), (reverse_weight, "z"), (window_weight, "y"),
            (share_weight, "y"), (kv_weight, "x"), (up_q, "back"), (down_q, "back"),
        )
    else:
        dq1_parts.tensor, *dq1_parts.result = in_halves(gather(dq1_share))
    causal_weight, grad_q, norm_one = run(
        functools.partial(causal_backward, blocks, share),
        [
            like(share_rows, causal_columns), like(count, features, kind=SINGLE),
            like(8, features, kind=SINGLE),
        ],
        [q, dq2, n1, pq, mq, log_q, cross_out_weight, norm_gain, attn_in, attn_out]
        + [dq1_parts.tensor] + dq1_parts.result,
        [VMEM] * 8 + [ANY, ANY] + [VMEM] * (2 * blocks - 1),
        [((features, wide), NARROW), ((features, features), NARROW), ((padded, features), NARROW),
         ((count, features), SINGLE), ((count, features), NARROW), ((count, features), NARROW),
         ((16, count), SINGLE), ((count, 2 * PAIR), SINGLE), ((count, wide), NARROW)],
        count * square * 16,
        semaphores=2,
    )
    norms = jnp.stack(
        (
            norm_x[2], norm_one[0] * leader, norm_two[0], norm_x[0], norm_four[0] * leader,
            norm_five[0], norm_x[3], norm_one[1] * leader, norm_two[1], norm_x[1],
            norm_four[1] * leader, norm_five[1],
        )
    )
    if carried:
        norms = Norms(jnp.pad(norms, ((0, 4), (0, 0))))
        causal_weight = RepSum(causal_weight, 1)
        arrive(
            (share_weight, "x"), (causal_weight, "out"), (norms, "out"), (kv_weight, "y"),
            (window_weight, "z"), (up_x, "back_x"), (down_x, "back_x"), (reverse_weight, "back_x"),
        )
        arrive(
            (share_weight, "z"), (kv_weight, "z"), (causal_weight, "back"), (norms, "back"),
            (up_x, "back_core"), (down_x, "back_core"), (reverse_weight, "back_core"),
            (window_weight, "back"),
        )
        arrive((share_weight, "back"), (kv_weight, "back"))
        up_x, down_x, reverse_weight, window_weight, kv_weight, share_weight, causal_weight = (
            one.tensor
            for one in (
                up_x, down_x, reverse_weight, window_weight, kv_weight, share_weight, causal_weight
            )
        )
        up_q, down_q, norms = up_q.tensor, down_q.tensor, norms.tensor[:12]
    else:
        up_x, down_x, reverse_weight, window_weight, kv_weight, share_weight = (
            reduce_all(one)
            for one in (up_x, down_x, reverse_grad, window_grad, kv_grad, share_grad)
        )
        up_q, down_q = reduce_rep(up_q[:share]), reduce_rep(down_q[:hidden_share])
        causal_weight = reduce_rep(causal_weight[:share])
        norms = lax.psum(norms, ("blk", "rep"))
    norms = own_columns(norms)
    grad_attn_in = jnp.stack(
        (
            window_weight[:, :wide],
            causal_weight[:, :wide],
            jnp.concatenate((share_weight[:, :features], kv_weight), axis=1),
            jnp.concatenate((reverse_weight[:, :features], share_weight[:, features:]), axis=1),
        )
    )
    grad_attn_out = jnp.stack(
        (
            window_weight[:, wide:],
            causal_weight[:, wide : wide + features],
            causal_weight[:, wide + features : last],
            reverse_weight[:, features:],
        )
    )
    return (
        x3[None],
        own_columns(q3)[None],
        grad_x[None],
        own_columns(grad_q)[None],
        norms[:6],
        norms[6:],
        grad_attn_in.astype(SINGLE),
        grad_attn_out.astype(SINGLE),
        jnp.stack((up_x, up_q)).astype(SINGLE),
        jnp.stack((down_x, down_q)).astype(SINGLE),
    )


def solution(mesh):
    placed = (
        P("rep", "blk", None),
        P("rep", None, None),
        P("rep", "blk"),
        P("rep"),
        P(),
        P(),
        P(),
        P(),
        P(),
        P(),
        P("rep", "blk", None),
        P("rep", None, None),
    )
    return jax.shard_map(
        body,
        mesh=mesh,
        in_specs=placed,
        out_specs=(
            P("rep", "blk", None),
            P("rep", None, "blk"),
            P("rep", "blk", None),
            P("rep", None, "blk"),
            P(None, "blk"),
            P(None, "blk"),
            P(None, "blk", None),
            P(None, "blk", None),
            P(None, "blk", None),
            P(None, "blk", None),
        ),
        check_vma=False,
    )
```

```python
import functools
import math

import jax
import jax.numpy as jnp
from jax import lax
from jax.experimental import pallas as pl
from jax.experimental.pallas import tpu as pltpu
from jax.sharding import PartitionSpec as P

HEADS = 12
WIN = 64
EPSILON = 1e-05
MASKED = -1e30
NARROW = jnp.bfloat16
SINGLE = jnp.float32
EXACT = lax.Precision.HIGHEST
GROUP = 128
WINDOWS = 256
PAIR = 128
HEAD = 64
STRIP = 160
LONG = 400
CHUNK = 768


def dot(former, latter, ahead, behind, precision=None):
    return lax.dot_general(
        former,
        latter,
        (((ahead,), (behind,)), ((), ())),
        preferred_element_type=SINGLE,
        precision=precision,
    )


def plain(former, latter):
    return dot(former, latter, 1, 0)


def right_t(former, latter):
    return dot(former, latter, 1, 1)


def left_t(former, latter):
    return dot(former, latter, 0, 0)


def loop(count, action):
    def step(index, nothing):
        action(index)
        return nothing

    lax.fori_loop(0, count, step, 0)


def at(index, size):
    return pl.ds(pl.multiple_of(index * size, size), size)


def iota(shape, dim):
    return lax.broadcasted_iota(jnp.int32, shape, dim)


def statistics(tensor):
    average = jnp.mean(tensor, axis=-1, keepdims=True)
    centred = tensor - average
    spread = jnp.mean(centred * centred, axis=-1, keepdims=True)
    return centred, lax.rsqrt(spread + EPSILON)


def norm(tensor, gain, bias):
    centred, inverse = statistics(tensor)
    return centred * inverse * gain + bias


def norm_back(tensor, gain, upstream):
    centred, inverse = statistics(tensor)
    scaled = centred * inverse
    inner = upstream * gain
    grad = inverse * (
        inner
        - jnp.mean(inner, axis=-1, keepdims=True)
        - scaled * jnp.mean(inner * scaled, axis=-1, keepdims=True)
    )
    return (
        grad,
        jnp.sum(upstream * scaled, axis=0, keepdims=True),
        jnp.sum(upstream, axis=0, keepdims=True),
    )


def gelu_both(tensor):
    size = jnp.abs(tensor)
    ratio = 1.0 / (1.0 + (0.3275911 * math.sqrt(0.5)) * size)
    series = ratio * (
        0.254829592
        + ratio * (-0.284496736 + ratio * (1.421413741 + ratio * (-1.453152027 + ratio * 1.061405429)))
    )
    bell = jnp.exp(-0.5 * (tensor * tensor))
    tail = 0.5 * series * bell
    below = jnp.where(tensor >= 0, 1.0 - tail, tail)
    return tensor * below, below + tensor * bell * (1.0 / math.sqrt(2.0 * math.pi))


def half(which, value=1.0):
    return jnp.where(iota((1, PAIR), 1) // HEAD == which, value, 0.0).astype(NARROW)


def lower_lanes():
    return iota((1, PAIR), 1) < HEAD


def both(tensor, value=1.0):
    return jnp.concatenate((tensor * half(0, value), tensor * half(1, value)), axis=0)


def attend(queries, keys, values, mask):
    rows = queries.shape[0]
    scores = right_t(both(queries, 1.0 / math.sqrt(HEAD)), keys)
    weights, totals, logs = [], [], []
    for which in range(2):
        part = mask(scores[which * rows : (which + 1) * rows])
        peak = jnp.max(part, axis=-1, keepdims=True)
        part = jnp.exp(part - peak)
        total = jnp.sum(part, axis=-1, keepdims=True)
        weights.append(part.astype(NARROW))
        totals.append(1.0 / total)
        logs.append(peak + jnp.log(total))
    out = plain(jnp.concatenate(weights, axis=0), values)
    return jnp.where(lower_lanes(), out[:rows] * totals[0], out[rows:] * totals[1]), logs


def attend_back(queries, keys, values, upstream, logs, deltas, mask):
    scaled = queries * jnp.asarray(1.0 / math.sqrt(HEAD), NARROW)
    count = keys.shape[0]
    keys = both(keys)
    turned_keys = keys.T
    scores = right_t(keys, scaled)
    inner = right_t(both(values), upstream)
    weights, slopes = [], []
    for which in range(2):
        span = slice(which * count, (which + 1) * count)
        part = mask(scores[span])
        if logs is None:
            part = jnp.exp(part - jnp.max(part, axis=0, keepdims=True))
            part = part * (1.0 / jnp.sum(part, axis=0, keepdims=True))
        else:
            part = jnp.exp(part - logs[which])
        weights.append(part.astype(NARROW))
        slopes.append((part * (inner[span] - deltas[which])).astype(NARROW))
    slope = jnp.concatenate(slopes, axis=0)
    query_grad = plain(turned_keys, slope).T
    key_grad = plain(slope, scaled)
    value_grad = plain(jnp.concatenate(weights, axis=0), upstream)
    lanes = lower_lanes()
    return (
        query_grad,
        jnp.where(lanes, key_grad[:count], key_grad[count:]),
        jnp.where(lanes, value_grad[:count], value_grad[count:]),
    )


def head_rows(tensor):
    features = tensor.shape[1]
    heads = 16
    chosen = jnp.where(
        iota((heads, features), 1) // HEAD == iota((heads, features), 0), 1.0, 0.0
    ).astype(SINGLE)
    return dot(chosen, tensor, 1, 1, EXACT)


def turn(columns):
    same = jnp.where(iota((16, columns.shape[1]), 0) == iota((16, columns.shape[1]), 1), 1.0, 0.0)
    return dot(same.astype(SINGLE), columns, 1, 1, EXACT)


def row_pair(ref, pair, span):
    tensor = ref[:, span]
    index = iota(tensor.shape, 0)
    return [
        jnp.sum(jnp.where(index == 2 * pair + which, tensor, 0.0), axis=0, keepdims=True)
        for which in range(2)
    ]


def chooser(rows, width, start, count):
    row = iota((rows, width), 0)
    hit = jnp.logical_and(iota((rows, width), 1) == row + start, row < count)
    return jnp.where(hit, 1.0, 0.0).astype(NARROW)


def spans(rows, size):
    edges = [(start, min(start + size, rows)) for start in range(0, rows, size)]
    if len(edges) > 1 and edges[-1][1] - edges[-1][0] < PAIR:
        edges[-2:] = [(edges[-2][0], rows)]
    return edges


def mark(log_ref, rows, head, value):
    log_ref[rows, :] = jnp.where(iota((1, PAIR), 1) == head, value, log_ref[rows, :])


def store_rows(ref, columns, value):
    ref[(slice(None),) * (len(ref.shape) - 1) + (columns,)] = value.astype(ref.dtype).reshape(
        ref.shape[:-1] + value.shape[1:]
    )


def nothing(*unused):
    return None


def copies(semaphores, *pairs):
    made = [
        pltpu.make_async_copy(source, target, semaphores.at[k])
        for k, (source, target) in enumerate(pairs)
    ]
    for one in made:
        one.start()
    return made


DIRECT = 8


def place_of(axis="blk"):
    return lax.axis_index(axis)


def flipped(index, mask, count):
    total, weight = 0, 1
    while weight < count:
        bit = (index // weight) % 2
        total = total + weight * ((1 - bit) if mask & weight else bit)
        weight *= 2
    return total


def piece_at(number, count):
    return flipped(place_of(), number, count) if count <= DIRECT else number


def window_forward(
    x_ref, gain_ref, bias_ref, a_in, a_out,
    n0_ref, pw_ref, mw_ref, x1_ref, nx_ref, vq_ref, ckv_ref,
    w_in, w_out, w_q, w_kv, sem,
    flush=nothing,
):
    rows, features = x_ref.shape
    loads = copies(
        sem,
        (a_in.at[0], w_in),
        (a_out.at[0], w_out),
        (a_in.at[3, :, pl.ds(0, features)], w_q),
        (a_in.at[2, :, pl.ds(features, 2 * features)], w_kv),
    )

    def first(i):
        span = at(i, GROUP)
        n0_ref[span, :] = norm(
            x_ref[span, :].astype(SINGLE), gain_ref[0:1, :], bias_ref[0:1, :]
        ).astype(NARROW)

    loop(rows // GROUP, first)
    loads[0].wait()

    def project(j):
        span = at(j, CHUNK)
        pw_ref[:, span] = plain(n0_ref[...], w_in[:, span]).astype(NARROW)

    loop(3 * features // CHUNK, project)
    flush(0)
    flush(1)
    window = jnp.where(
        iota((WINDOWS, WINDOWS), 0) // WIN == iota((WINDOWS, WINDOWS), 1) // WIN, 0.0, MASKED
    )

    def group(i):
        span = at(i, WINDOWS)
        for pair in range(features // PAIR):
            lane = pair * PAIR
            out, unused = attend(
                pw_ref[span, lane : lane + PAIR],
                pw_ref[span, features + lane : features + lane + PAIR],
                pw_ref[span, 2 * features + lane : 2 * features + lane + PAIR],
                lambda scores: scores + window,
            )
            mw_ref[span, lane : lane + PAIR] = out.astype(NARROW)

    loop(rows // WINDOWS, group)
    flush(2)
    loads[1].wait()

    def second(i):
        span = at(i, GROUP)
        total = x_ref[span, :].astype(SINGLE) + plain(mw_ref[span, :], w_out[...])
        x1_ref[span, :] = total
        nx_ref[span, :] = norm(total, gain_ref[3:4, :], bias_ref[3:4, :]).astype(NARROW)

    loop(rows // GROUP, second)
    flush(3)
    flush(4)
    loads[2].wait()
    vq_ref[...] = plain(nx_ref[...], w_q[...]).astype(NARROW)
    flush(5)
    loads[3].wait()

    def third(j):
        span = at(j, CHUNK)
        ckv_ref[:, span] = plain(nx_ref[...], w_kv[:, span]).astype(NARROW)

    loop(2 * features // CHUNK, third)


def causal_forward(
    q_ref, gain_ref, bias_ref, a_in, a_out,
    n1_ref, pq_ref, mq_ref, q1_ref, nq_ref, cq_ref, vkv_ref, log_ref,
    w_in, w_out, w_q, w_kv, logs, sem,
    flush=nothing,
):
    rows, features = q_ref.shape
    loads = copies(
        sem,
        (a_in.at[1], w_in),
        (a_out.at[1], w_out),
        (a_in.at[2, :, pl.ds(0, features)], w_q),
        (a_in.at[3, :, pl.ds(features, 2 * features)], w_kv),
    )

    def first(i):
        span = at(i, STRIP)
        n1_ref[span, :] = norm(
            q_ref[span, :].astype(SINGLE), gain_ref[1:2, :], bias_ref[1:2, :]
        ).astype(NARROW)

    loop(rows // STRIP, first)
    loads[0].wait()

    def project(j):
        span = at(j, CHUNK)
        pq_ref[:, span] = plain(n1_ref[...], w_in[:, span]).astype(NARROW)

    loop(3 * features // CHUNK, project)
    flush(0)
    flush(1)
    logs[...] = jnp.zeros_like(logs)

    def pair(p):
        for start in range(0, rows, LONG):
            end = min(start + LONG, rows)

            def mask(scores, start=start):
                shape = scores.shape
                return jnp.where(iota(shape, 1) <= iota(shape, 0) + start, scores, MASKED)

            out, sums = attend(
                pq_ref[start:end, at(p, PAIR)],
                pq_ref[0:end, at(p + features // PAIR, PAIR)],
                pq_ref[0:end, at(p + 2 * features // PAIR, PAIR)],
                mask,
            )
            mq_ref[start:end, at(p, PAIR)] = out.astype(NARROW)
            for which in range(2):
                mark(logs, slice(start, end), 2 * p + which, sums[which])

    loop(features // PAIR, pair)
    flush(2)
    log_ref[...] = turn(logs[...])
    loads[1].wait()

    def second(i):
        span = at(i, STRIP)
        total = q_ref[span, :].astype(SINGLE) + plain(mq_ref[span, :], w_out[...])
        q1_ref[span, :] = total
        nq_ref[span, :] = norm(total, gain_ref[2:3, :], bias_ref[2:3, :]).astype(NARROW)

    loop(rows // STRIP, second)
    if q1_ref.shape[0] > rows:
        q1_ref[rows:, :] = jnp.zeros_like(q1_ref[rows:, :])
        nq_ref[rows:, :] = jnp.zeros_like(nq_ref[rows:, :])
    flush(3)
    flush(4)
    loads[2].wait()
    cq_ref[...] = plain(nq_ref[0:rows, :], w_q[...]).astype(NARROW)
    flush(5)
    loads[3].wait()

    def third(j):
        span = at(j, CHUNK)
        vkv_ref[:, span] = plain(nq_ref[0:rows, :], w_kv[:, span]).astype(NARROW)

    loop(2 * features // CHUNK, third)


def cross_forward(pieces, cq_ref, ckv_ref, valid_ref, whole, *rest):
    log_refs, (logs,) = rest[:pieces], rest[pieces:]
    rows, features = cq_ref.shape
    part = log_refs[0].shape[1]
    logs[...] = jnp.zeros_like(logs)
    if whole.shape[0] > rows:
        whole[rows:, :] = jnp.zeros((whole.shape[0] - rows, features), NARROW)

    def pair(p):
        for start in range(0, rows, LONG):
            span = slice(start, min(start + LONG, rows))
            out, sums = attend(
                cq_ref[span, at(p, PAIR)],
                ckv_ref[:, at(p, PAIR)],
                ckv_ref[:, at(p + features // PAIR, PAIR)],
                lambda scores: scores + valid_ref[...],
            )
            whole[span, at(p, PAIR)] = out.astype(NARROW)
            for which in range(2):
                mark(logs, span, 2 * p + which, sums[which])

    loop(features // PAIR, pair)
    for k in range(pieces):
        log_refs[k][...] = turn(logs[at(piece_at(k, pieces), part), :])


def untwist(rows):
    same = jnp.where(iota((16, PAIR), 0) == iota((16, PAIR), 1), 1.0, 0.0)
    return dot(rows, same.astype(SINGLE), 0, 0, EXACT)


def merge_blocks(pieces, own_ref, *refs):
    logs, refs = refs[:pieces], refs[pieces:]
    halves, (co_ref, log_ref) = (refs[: pieces - 1], refs[pieces - 1 : -2]), refs[-2:]
    part, features = co_ref.shape
    width = features // 2
    peak = functools.reduce(jnp.maximum, [one[...] for one in logs])
    total = peak + jnp.log(functools.reduce(jnp.add, [jnp.exp(one[...] - peak) for one in logs]))
    log_ref[...] = total
    spread = jnp.where(
        iota((PAIR, features), 1) // HEAD == iota((PAIR, features), 0), 1.0, 0.0
    ).astype(NARROW)
    result = jnp.zeros(co_ref.shape, SINGLE)
    for k in range(pieces):
        weight = untwist(jnp.exp(logs[k][...] - total))
        high = weight.astype(NARROW)
        low = (weight - high.astype(SINGLE)).astype(NARROW)
        if k == 0:
            block = own_ref[at(place_of(), part), :]
        else:
            block = jnp.concatenate((halves[0][k - 1][...], halves[1][k - 1][...]), axis=1)
        result = result + (plain(high, spread) + plain(low, spread)) * block.astype(SINGLE)
    co_ref[...] = result.astype(NARROW)


def reverse_forward(
    length_ref, vq_ref, vkv_ref, x1_ref, a_out,
    mv_ref, x2_ref, log_ref,
    w_out, logs, sem,
):
    rows, features = vq_ref.shape
    keys = vkv_ref.shape[0]
    (load,) = copies(sem, (a_out.at[3], w_out))
    logs[...] = jnp.zeros_like(logs)
    bias = jnp.where(iota((1, keys), 1) < length_ref[0], 0.0, MASKED)

    def pair(p):
        for start in range(0, rows, WINDOWS):
            span = slice(start, start + WINDOWS)
            out, sums = attend(
                vq_ref[span, at(p, PAIR)],
                vkv_ref[:, at(p, PAIR)],
                vkv_ref[:, at(p + features // PAIR, PAIR)],
                lambda scores: scores + bias,
            )
            mv_ref[span, at(p, PAIR)] = out.astype(NARROW)
            for which in range(2):
                mark(logs, span, 2 * p + which, sums[which])

    loop(features // PAIR, pair)
    log_ref[...] = turn(logs[...])
    load.wait()

    def second(i):
        span = at(i, GROUP)
        x2_ref[span, :] = x1_ref[span, :] + plain(mv_ref[span, :], w_out[...])

    loop(rows // GROUP, second)


def feed_forward_step(block, normed, up, down, cot, hidden, slope, out, grad):
    rows = normed.shape[0]

    def strip(i):
        span = at(i, block)
        value, rise = gelu_both(plain(normed[span, :], up[...]))
        hidden[span, :] = value.astype(NARROW)
        slope[span, :] = (right_t(cot[span, :], down[...]) * rise).astype(NARROW)
        out[span, :] += plain(hidden[span, :], down[...])
        grad[span, :] += right_t(slope[span, :], up[...])

    loop(rows // block, strip)


def patch_feed_forward(
    x2_ref, cot_ref, gain_ref, bias_ref, up_ref, down_ref,
    x3_ref, dx2_ref, up_grad_ref, down_grad_ref, norm_ref,
    normed, hidden, slope, out, grad,
):
    rows = x2_ref.shape[0]
    step = pl.program_id(0)

    @pl.when(step == 0)
    def begin():
        def first(i):
            span = at(i, GROUP)
            normed[span, :] = norm(
                x2_ref[span, :], gain_ref[5:6, :], bias_ref[5:6, :]
            ).astype(NARROW)
            out[span, :] = x2_ref[span, :]
            grad[span, :] = jnp.zeros_like(grad[span, :])

        loop(rows // GROUP, first)

    feed_forward_step(
        512, normed, up_ref.at[0], down_ref.at[0], cot_ref, hidden, slope, out, grad
    )
    up_grad_ref[...] = left_t(normed[...], slope[...]).astype(NARROW)
    down_grad_ref[...] = left_t(hidden[...], cot_ref[...]).astype(NARROW)

    @pl.when(step == pl.num_programs(0) - 1)
    def finish():
        norm_ref[...] = jnp.zeros_like(norm_ref)

        def last(i):
            span = at(i, GROUP)
            x3_ref[span, :] = out[span, :].astype(NARROW)
            part, gain, bias = norm_back(x2_ref[span, :], gain_ref[5:6, :], grad[span, :])
            dx2_ref[span, :] = cot_ref[span, :].astype(SINGLE) + part
            norm_ref[0:1, :] += gain
            norm_ref[1:2, :] += bias

        loop(rows // GROUP, last)


def place_parts(ref, pieces, parts, sem):
    part, features = parts[0].shape
    width = features // 2
    pairs = [(parts[0], ref.at[at(piece_at(0, pieces), part), :])]
    for number in range(2):
        for k in range(1, pieces):
            pairs.append(
                (
                    parts[number * (pieces - 1) + k],
                    ref.at[at(piece_at(k, pieces), part), pl.ds(number * width, width)],
                )
            )
    return copies(sem, *pairs)


def query_feed_forward(
    pieces, share, hidden_share, q1_ref, cot_ref, gain_ref, bias_ref,
    w_out, up_ref, down_ref, *rest,
):
    parts, rest = rest[: 2 * pieces - 1], rest[2 * pieces - 1 :]
    (
        q3_ref, dq2_ref, up_grad_ref, down_grad_ref, norm_ref, co_ref,
        q2, normed, chosen, hidden, slope, out, grad, sem,
    ) = rest
    rows, features = cot_ref.shape
    width = up_ref.shape[2]
    step = pl.program_id(0)

    @pl.when(step == 0)
    def begin():
        for one in place_parts(co_ref, pieces, parts, sem):
            one.wait()

        def first(i):
            span = at(i, STRIP)
            total = q1_ref[span, :] + plain(co_ref[span, :], w_out[0])
            q2[span, :] = total
            out[span, :] = total
            normed[span, :] = norm(total, gain_ref[4:5, :], bias_ref[4:5, :]).astype(NARROW)
            grad[span, :] = jnp.zeros_like(grad[span, :])

        loop(rows // STRIP, first)
        chosen[...] = right_t(
            chooser(chosen.shape[0], features, place_of() * share, share), normed[...]
        ).astype(NARROW)

    feed_forward_step(
        LONG, normed, up_ref.at[0], down_ref.at[0], cot_ref, hidden, slope, out, grad
    )
    up_grad_ref[...] = plain(chosen[...], slope[...]).astype(NARROW)
    begins = place_of() * hidden_share

    @pl.when(begins // width == step)
    def own_hidden():
        taken = right_t(
            chooser(down_grad_ref.shape[0], width, begins - step * width, hidden_share),
            hidden[...],
        ).astype(NARROW)
        down_grad_ref[...] = plain(taken, cot_ref[...]).astype(NARROW)

    @pl.when(step == pl.num_programs(0) - 1)
    def finish():
        norm_ref[...] = jnp.zeros_like(norm_ref)

        def last(i):
            span = at(i, STRIP)
            q3_ref[span, :] = out[span, :].astype(NARROW)
            piece, gain, bias = norm_back(q2[span, :], gain_ref[4:5, :], grad[span, :])
            dq2_ref[span, :] = cot_ref[span, :].astype(SINGLE) + piece
            norm_ref[0:1, :] += gain
            norm_ref[1:2, :] += bias

        loop(rows // STRIP, last)


def reverse_backward(
    pieces, length_ref, dx2_ref, mv_ref, vq_ref, vkv_ref, nx_ref, log_ref, a_out,
    *rest, launch=nothing, tick=nothing,
):
    dvq_ref, weight_ref, rest = rest[0], rest[1], rest[2:]
    k_refs, v_refs, rest = rest[:pieces], rest[pieces : 2 * pieces], rest[2 * pieces :]
    w_out, rounded, dmv, deltas, dkv, sem = rest
    rows, features = vq_ref.shape
    keys = vkv_ref.shape[0]
    part = k_refs[0].shape[0]
    (load,) = copies(sem, (a_out.at[3], w_out))
    rounded[...] = dx2_ref[...].astype(NARROW)
    load.wait()
    dmv[...] = right_t(rounded[...], w_out[...]).astype(NARROW)
    store_rows(
        weight_ref, slice(features, 2 * features), left_t(mv_ref[...], rounded[...])
    )
    deltas[...] = head_rows(dmv[...].astype(SINGLE) * mv_ref[...].astype(SINGLE))
    if dkv.shape[0] > keys:
        dkv[keys:, :] = jnp.zeros((dkv.shape[0] - keys, 2 * features), SINGLE)
    size = 256

    def pair(p):
        pl.when(p == 2)(lambda: tick(1))
        pl.when(p == 4)(lambda: tick(2))
        for strip in range(rows // size):
            span = slice(strip * size, (strip + 1) * size)

            def mask(scores):
                return jnp.where(iota(scores.shape, 0) < length_ref[0], scores, MASKED)

            dq, dk, dv = attend_back(
                vq_ref[span, at(p, PAIR)],
                vkv_ref[:, at(p, PAIR)],
                vkv_ref[:, at(p + features // PAIR, PAIR)],
                dmv[span, at(p, PAIR)],
                row_pair(log_ref, p, span),
                row_pair(deltas, p, span),
                mask,
            )
            dvq_ref[span, at(p, PAIR)] = (dq * (1.0 / math.sqrt(HEAD))).astype(NARROW)
            if strip == 0:
                dkv[0:keys, at(p, PAIR)] = dk
                dkv[0:keys, at(p + features // PAIR, PAIR)] = dv
            else:
                dkv[0:keys, at(p, PAIR)] += dk
                dkv[0:keys, at(p + features // PAIR, PAIR)] += dv

    loop(features // PAIR, pair)
    store_rows(weight_ref, slice(0, features), left_t(nx_ref[...], dvq_ref[...]))
    launch(1)
    for k in range(pieces):
        span = at(piece_at(k, pieces), part)
        k_refs[k][...] = dkv[span, 0:features].astype(NARROW)
        v_refs[k][...] = dkv[span, features:].astype(NARROW)


def cross_backward(
    pieces, share, dq2_ref, co_ref, cq_ref, ckv_ref, valid_ref, a_out, *rest
):
    log_parts, rest = rest[:pieces], rest[pieces:]
    dckv_ref, weight_ref, rest = rest[0], rest[1], rest[2:]
    q_refs, (w_out, rounded, dco, deltas, logs, turned, dq_all, dkv, sem) = (
        rest[:pieces],
        rest[pieces:],
    )
    rows, features = cq_ref.shape
    part = log_parts[0].shape[1]
    (load,) = copies(sem, (a_out.at[2], w_out))
    for k in range(pieces):
        logs[at(piece_at(k, pieces), part), :] = untwist(log_parts[k][...])
    turned[...] = turn(logs[0:rows, :])
    rounded[...] = dq2_ref[...].astype(NARROW)
    load.wait()
    dco[...] = right_t(rounded[...], w_out[...]).astype(NARROW)
    taken = right_t(
        chooser(weight_ref.shape[0], features, place_of() * share, share), co_ref[0:rows, :]
    ).astype(NARROW)
    weight_ref[...] = plain(taken, rounded[...]).astype(NARROW)
    deltas[...] = head_rows(dco[...].astype(SINGLE) * co_ref[0:rows, :].astype(SINGLE))
    if dq_all.shape[0] > rows:
        dq_all[rows:, :] = jnp.zeros((dq_all.shape[0] - rows, features), NARROW)
    edges = spans(rows, 512)

    def pair(p):
        for number, (start, end) in enumerate(edges):
            span = slice(start, end)
            dq, dk, dv = attend_back(
                cq_ref[span, at(p, PAIR)],
                ckv_ref[:, at(p, PAIR)],
                ckv_ref[:, at(p + features // PAIR, PAIR)],
                dco[span, at(p, PAIR)],
                row_pair(turned, p, span),
                row_pair(deltas, p, span),
                lambda scores: scores + valid_ref[...],
            )
            dq_all[span, at(p, PAIR)] = (dq * (1.0 / math.sqrt(HEAD))).astype(NARROW)
            if number == 0:
                dkv[:, at(p, PAIR)] = dk
                dkv[:, at(p + features // PAIR, PAIR)] = dv
            else:
                dkv[:, at(p, PAIR)] += dk
                dkv[:, at(p + features // PAIR, PAIR)] += dv

    loop(features // PAIR, pair)
    dckv_ref[...] = dkv[...].astype(NARROW)
    for k in range(pieces):
        q_refs[k][...] = dq_all[at(piece_at(k, pieces), part), :]


def patch_backward(
    x_ref, dx2_ref, x1_ref, nx_ref, n0_ref, pw_ref, mw_ref, dvq_ref, dckv_ref, gain_ref, a_in, a_out,
    kv_weight_ref, weight_ref, grad_ref, norm_ref,
    w_in, w_out, w_q, w_kv, dx1, rounded, dmw, deltas, dpw, sem,
    launch=nothing, ready=nothing, flush=nothing,
):
    rows, features = x_ref.shape
    loads = copies(
        sem,
        (a_in.at[3, :, pl.ds(0, features)], w_q),
        (a_in.at[2, :, pl.ds(features, 2 * features)], w_kv),
        (a_out.at[0], w_out),
        (a_in.at[0], w_in),
    )
    norm_ref[...] = jnp.zeros_like(norm_ref)
    for start in range(0, 2 * features, CHUNK):
        span = slice(start, start + CHUNK)
        store_rows(kv_weight_ref, span, left_t(nx_ref[...], dckv_ref[:, span]))
    launch(0)
    flush(0)
    loads[0].wait()
    loads[1].wait()

    def first(i):
        span = at(i, GROUP)
        upstream = right_t(dvq_ref[span, :], w_q[...]) + right_t(dckv_ref[span, :], w_kv[...])
        part, gain, bias = norm_back(x1_ref[span, :], gain_ref[3:4, :], upstream)
        total = dx2_ref[span, :] + part
        dx1[span, :] = total
        rounded[span, :] = total.astype(NARROW)
        norm_ref[0:1, :] += gain
        norm_ref[1:2, :] += bias

    loop(rows // GROUP, first)
    loads[2].wait()
    ready(6)
    dmw[...] = right_t(rounded[...], w_out[...]).astype(NARROW)
    store_rows(
        weight_ref, slice(3 * features, 4 * features), left_t(mw_ref[...], rounded[...])
    )
    deltas[...] = head_rows(dmw[...].astype(SINGLE) * mw_ref[...].astype(SINGLE))
    ready(5)
    window = jnp.where(
        iota((WINDOWS, WINDOWS), 0) // WIN == iota((WINDOWS, WINDOWS), 1) // WIN, 0.0, MASKED
    )

    def group(i):
        span = at(i, WINDOWS)
        for pair in range(features // PAIR):
            lane = pair * PAIR
            dq, dk, dv = attend_back(
                pw_ref[span, lane : lane + PAIR],
                pw_ref[span, features + lane : features + lane + PAIR],
                pw_ref[span, 2 * features + lane : 2 * features + lane + PAIR],
                dmw[span, lane : lane + PAIR],
                None,
                [deltas[2 * pair + w : 2 * pair + w + 1, span] for w in range(2)],
                lambda scores: scores + window,
            )
            dpw[span, lane : lane + PAIR] = (dq * (1.0 / math.sqrt(HEAD))).astype(NARROW)
            dpw[span, features + lane : features + lane + PAIR] = dk.astype(NARROW)
            dpw[span, 2 * features + lane : 2 * features + lane + PAIR] = dv.astype(NARROW)

    loop(rows // WINDOWS, group)
    ready(4)
    for start in range(0, 3 * features, CHUNK):
        span = slice(start, start + CHUNK)
        store_rows(weight_ref, span, left_t(n0_ref[...], dpw[:, span]))
    launch(1)
    flush(1)
    ready(0)
    loads[3].wait()

    def last(i):
        span = at(i, GROUP)
        upstream = right_t(dpw[span, :], w_in[...])
        part, gain, bias = norm_back(x_ref[span, :].astype(SINGLE), gain_ref[0:1, :], upstream)
        grad_ref[span, :] = dx1[span, :] + part
        norm_ref[2:3, :] += gain
        norm_ref[3:4, :] += bias

    loop(rows // GROUP, last)


def share_backward(
    pieces, q1, nq, gain_ref, a_in, *rest, launch=nothing
):
    parts = [rest[k * pieces : (k + 1) * pieces] for k in range(3)]
    rest = rest[3 * pieces :]
    grad_ref, weight_ref, norm_ref, w_q, w_kv, summed, q1_ref, nq_ref, sem = rest
    part, features = q1_ref.shape
    *loads, load_q, load_n = copies(
        sem,
        (a_in.at[2, :, pl.ds(0, features)], w_q),
        (a_in.at[3, :, pl.ds(features, 2 * features)], w_kv),
        (q1.at[at(place_of(), part), :], q1_ref),
        (nq.at[at(place_of(), part), :], nq_ref),
    )
    for k in range(3):
        span = slice(k * features, (k + 1) * features)
        total = functools.reduce(jnp.add, [one[...].astype(SINGLE) for one in parts[k]])
        summed[:, span] = total.astype(NARROW)
    for load in loads:
        load.wait()
    upstream = right_t(summed[:, 0:features], w_q[...]) + right_t(summed[:, features:], w_kv[...])
    load_q.wait()
    piece, gain, bias = norm_back(q1_ref[...], gain_ref[2:3, :], upstream)
    grad_ref[...] = piece.astype(NARROW)
    launch(0)
    load_n.wait()
    for k in range(3):
        span = slice(k * features, (k + 1) * features)
        store_rows(weight_ref, span, left_t(nq_ref[...], summed[:, span]))
    launch(1)
    norm_ref[...] = jnp.zeros_like(norm_ref)
    norm_ref[0:1, :] = gain
    norm_ref[1:2, :] = bias


def causal_backward(
    pieces, share, q_ref, dq2_ref, n1_ref, pq_ref, mq_ref, log_ref, cross_ref, gain_ref,
    a_in, a_out, *rest, ready=nothing
):
    parts, rest = rest[: 2 * pieces - 1], rest[2 * pieces - 1 :]
    (
        weight_ref, grad_ref, norm_ref,
        w_in, w_out, gathered, dq1, rounded, dmq, deltas, dkv, dpq, sem,
    ) = rest
    rows, features = q_ref.shape
    placed = place_parts(gathered, pieces, parts, sem)
    loads = copies(sem.at[pl.ds(len(placed), 2)], (a_out.at[1], w_out), (a_in.at[1], w_in))
    for one in placed:
        one.wait()

    def first(i):
        span = at(i, STRIP)
        total = dq2_ref[span, :] + gathered[span, :].astype(SINGLE)
        dq1[span, :] = total
        rounded[span, :] = total.astype(NARROW)

    loop(rows // STRIP, first)
    loads[0].wait()
    dmq[...] = right_t(rounded[...], w_out[...]).astype(NARROW)
    ready(4)
    chosen = chooser(weight_ref.shape[0], features, place_of() * share, share)
    taken = right_t(chosen, mq_ref[...]).astype(NARROW)
    weight_ref[:, 3 * features : 4 * features] = plain(taken, rounded[...]).astype(NARROW)
    weight_ref[:, 4 * features : 5 * features] = cross_ref[...]
    weight_ref[:, 5 * features :] = jnp.zeros_like(weight_ref[:, 5 * features :])
    deltas[...] = head_rows(dmq[...].astype(SINGLE) * mq_ref[...].astype(SINGLE))
    edges = spans(rows, 256)
    ready(3)
    ready(5)

    def pair(p):
        for number, (start, end) in reversed(list(enumerate(edges))):
            span = slice(start, end)

            def mask(scores, start=start):
                shape = scores.shape
                return jnp.where(iota(shape, 0) <= iota(shape, 1) + start, scores, MASKED)

            dq, dk, dv = attend_back(
                pq_ref[span, at(p, PAIR)],
                pq_ref[0:end, at(p + features // PAIR, PAIR)],
                pq_ref[0:end, at(p + 2 * features // PAIR, PAIR)],
                dmq[span, at(p, PAIR)],
                row_pair(log_ref, p, span),
                row_pair(deltas, p, span),
                mask,
            )
            dpq[span, at(p, PAIR)] = (dq * (1.0 / math.sqrt(HEAD))).astype(NARROW)
            if end == rows:
                dkv[0:end, 0:PAIR] = dk
                dkv[0:end, PAIR:] = dv
            else:
                dkv[0:end, 0:PAIR] += dk
                dkv[0:end, PAIR:] += dv
        dpq[:, at(p + features // PAIR, PAIR)] = dkv[:, 0:PAIR].astype(NARROW)
        dpq[:, at(p + 2 * features // PAIR, PAIR)] = dkv[:, PAIR:].astype(NARROW)

    loop(features // PAIR, pair)
    ready(2)
    taken = right_t(chosen, n1_ref[...]).astype(NARROW)
    weight_ref[:, 0 : 3 * features] = plain(taken, dpq[...]).astype(NARROW)
    loads[1].wait()
    norm_ref[...] = jnp.zeros_like(norm_ref)

    def last(i):
        span = at(i, STRIP)
        upstream = right_t(dpq[span, :], w_in[...])
        piece, gain, bias = norm_back(q_ref[span, :].astype(SINGLE), gain_ref[1:2, :], upstream)
        grad_ref[span, :] = dq1[span, :] + piece
        norm_ref[0:1, :] += gain
        norm_ref[1:2, :] += bias

    loop(rows // STRIP, last)


def assemble(pairs, quarters, count, *refs):
    parts, refs = refs[: 4 * (pairs + quarters)], refs[4 * (pairs + quarters) :]
    norms, refs = refs[:count], refs[count:]
    in_ref, out_ref, up_ref, down_ref, gain_ref, bias_ref, share, causal = refs
    features = down_ref.shape[2]
    rep = place_of("rep")

    def corners(group, write):
        for k in range(4):
            owner = flipped(rep, k, 4)
            piece = group[k][...].astype(SINGLE)
            height, width = piece.shape
            write(
                pl.ds(pl.multiple_of((owner % 2) * height, height), height),
                pl.multiple_of((owner // 2) * width, width), width, piece,
            )

    def into(ref, index, start=0):
        def write(rows, column, width, piece):
            ref[index, rows, pl.ds(column + start, width)] = piece

        return write

    groups = [parts[4 * k : 4 * k + 4] for k in range(pairs + quarters)]
    up_x, down_x, reverse, window, kv, shared, up_q, down_q, rest = groups
    corners(up_x, into(up_ref, 0))
    corners(down_x, into(down_ref, 0))
    corners(kv, into(in_ref, 2, features))

    def keep_share(rows, column, width, piece):
        share[rows, pl.ds(column, width)] = piece

    corners(shared, keep_share)
    in_ref[2, :, 0:features] = share[:, 0:features]
    in_ref[3, :, features:] = share[:, features : 3 * features]
    corners(reverse, keep_share)
    in_ref[3, :, 0:features] = share[:, 0:features]
    out_ref[3, :, :] = share[:, features : 2 * features]
    corners(window, keep_share)
    in_ref[0, :, :] = share[:, 0 : 3 * features]
    out_ref[0, :, :] = share[:, 3 * features :]
    for k in range(4):
        owner = flipped(rep, k, 4)
        width = up_q[k].shape[1]
        up_ref[1, :, at(owner, width)] = up_q[k][...].astype(SINGLE)
        down_ref[1, at(owner, down_q[k].shape[0]), :] = down_q[k][...].astype(SINGLE)
        causal[:, at(owner, rest[k].shape[1])] = rest[k][...].astype(SINGLE)
    in_ref[1, :, :] = causal[:, 0 : 3 * features]
    out_ref[1, :, :] = causal[:, 3 * features : 4 * features]
    out_ref[2, :, :] = causal[:, 4 * features : 5 * features]
    total = functools.reduce(jnp.add, [one[...] for one in norms])
    columns = gain_ref.shape[1]
    gain_ref[...] = total[0:6, 0:columns]
    bias_ref[...] = total[8:14, 0:columns]


def bits_of(count):
    return max(count - 1, 0).bit_length()


def swap(tensor, axis, mask):
    return lax.ppermute(tensor, axis, [(i, i ^ mask) for i in range(lax.axis_size(axis))])


def pick(tensor, place, dim):
    return lax.dynamic_index_in_dim(tensor, place, dim, keepdims=False)


def fold(tensor, axis, bit, dim):
    own = (lax.axis_index(axis) >> bit) & 1
    arrived = swap(pick(tensor, 1 - own, dim).astype(NARROW), axis, 1 << bit)
    return pick(tensor, own, dim).astype(SINGLE) + arrived.astype(SINGLE)


def unfold(tensor, axis, bit, dim):
    own = (lax.axis_index(axis) >> bit) & 1
    arrived = swap(tensor, axis, 1 << bit)
    return jnp.where(
        own == 0,
        jnp.stack((tensor, arrived), axis=dim),
        jnp.stack((arrived, tensor), axis=dim),
    )


def scatter_blk(tensor):
    bits = bits_of(lax.axis_size("blk"))
    tensor = tensor.reshape((2,) * bits + tensor.shape[1:])
    for bit in range(bits):
        tensor = fold(tensor, "blk", bit, bits - 1 - bit)
    return tensor


def sum_rep_scatter(tensor, dim):
    bits = bits_of(lax.axis_size("rep"))
    shape = tensor.shape
    tensor = tensor.reshape(
        shape[:dim] + (2,) * bits + (shape[dim] // 2**bits,) + shape[dim + 1 :]
    )
    for bit in range(bits):
        tensor = fold(tensor, "rep", bit, dim)
    return tensor


def gather_rep(tensor, dim):
    bits = bits_of(lax.axis_size("rep"))
    for bit in reversed(range(bits)):
        tensor = unfold(tensor, "rep", bit, dim)
    shape = tensor.shape
    return tensor.reshape(shape[:dim] + (-1,) + shape[dim + bits + 1 :])


def reduce_all(tensor):
    count = lax.axis_size("blk")
    tensor = tensor.reshape(count, tensor.shape[0] // count, tensor.shape[1])
    tensor = sum_rep_scatter(tensor, 1)
    tensor = scatter_blk(tensor).astype(NARROW)
    return gather_rep(tensor, 0)


def reduce_rep(tensor):
    return gather_rep(sum_rep_scatter(tensor, 0).astype(NARROW), 0)


def exchange(pieces):
    whole = lax.all_to_all(jnp.stack(pieces), "blk", 0, 0)
    return [whole[k] for k in range(len(pieces))]


def gather(tensor):
    count = lax.axis_size("blk")
    whole = lax.all_gather(tensor, "blk")
    return [whole[k] for k in range(count)]


def whole(ref):
    return ref


class Fold:
    def __init__(self, own, take, arrived, shape, keep=whole, keep_shape=None):
        self.own, self.take, self.arrived, self.shape = own, take, arrived, shape
        self.keep, self.keep_shape = keep, keep_shape or shape


class Move:
    late = None

    def __init__(self, source, shape, axis, flip, take=whole, phase=0):
        self.source, self.shape, self.axis, self.flip, self.take = source, shape, axis, flip, take
        self.phase = phase


def lanes_of(ref, start, width):
    return ref.at[(slice(None),) * (len(ref.shape) - 1) + (pl.ds(start, width),)]


class Reduction:
    def __init__(self, tensor):
        if len(tensor.shape) == 2:
            blocks = lax.axis_size("blk")
            height = tensor.shape[0] // blocks
            tensor = tensor.reshape(blocks // 2, 2, 2, height // 2, tensor.shape[1])
        self.tensor, self.take, self.arrived, self.shape = tensor, whole, [], tensor.shape

    def fold(self, keep=whole, keep_shape=None):
        return Fold(self.tensor, self.take, self.arrived, self.shape, keep, keep_shape)

    def moves(self, stage):
        shape = self.shape
        if stage == "core":
            self.next = shape[:2] + shape[3:]
            return [
                Move(self.tensor, self.next, "rep", 1,
                     lambda ref: ref.at[:, :, 1 - place_of("rep") % 2])
            ]
        if stage == "x":
            width = shape[-1] // 2
            self.next = shape[:-1] + (width,)

            def own(ref):
                return lanes_of(ref, pl.multiple_of((place_of("rep") // 2) * width, width), width)

            def other(ref):
                start = (1 - place_of("rep") // 2) * width
                return lanes_of(ref, pl.multiple_of(start, width), width)

            return [Move(self.fold(own, self.next), self.next, "rep", 2, other)]
        if stage == "y":
            self.next = shape[:1] + shape[2:]
            fold = self.fold(lambda ref: ref.at[:, place_of() % 2], self.next)
            return [Move(fold, self.next, "blk", 1, lambda ref: ref.at[:, 1 - place_of() % 2])]
        if stage == "z":
            length = shape[0]
            self.next = shape[1:]
            fold = self.fold(lambda ref: ref.at[place_of() // 2], self.next)
            return [
                Move(fold, self.next, "blk", 2 * k,
                     lambda ref, k=k: ref.at[flipped(place_of() // 2, k, length)])
                for k in range(1, length)
            ]
        if stage == "back":
            fold = self.fold()
            return [Move(fold, shape, "rep", k) for k in range(1, 4)]
        if stage == "back_x":
            return [Move(self.fold(), shape, "rep", 2)]
        return [Move(self.tensor, shape, "rep", 1), Move(self.other, shape, "rep", 1)]

    def absorb(self, stage, arrived, kept):
        if stage == "core":
            self.take = lambda ref: ref.at[:, :, place_of("rep") % 2]
        else:
            self.take = whole
        if kept:
            self.tensor = kept[0]
        if stage in ("back", "back_x", "back_core"):
            if stage == "back_x":
                self.other = arrived[0]
                return
            if stage == "back":
                self.result = [self.tensor] + list(arrived)
            else:
                self.result = [self.tensor, arrived[0], self.other, arrived[1]]
            return
        self.shape, self.arrived = self.next, list(arrived)


class RepSum:
    def __init__(self, tensor, dim):
        self.tensor, self.dim = tensor, dim

    def moves(self, stage):
        if stage == "out":
            self.shape = list(self.tensor.shape)
            size = self.shape[self.dim] = self.shape[self.dim] // 4

            def quarter(ref, k):
                span = pl.ds(pl.multiple_of(flipped(place_of("rep"), k, 4) * size, size), size)
                return ref.at[span, :] if self.dim == 0 else ref.at[:, span]

            self.quarter = quarter
            return [
                Move(self.tensor, tuple(self.shape), "rep", k, lambda ref, k=k: quarter(ref, k))
                for k in range(1, 4)
            ]
        fold = Fold(
            self.tensor, lambda ref: self.quarter(ref, 0), self.arrived, tuple(self.shape)
        )
        return [Move(fold, tuple(self.shape), "rep", k) for k in range(1, 4)]

    def absorb(self, stage, arrived, kept):
        if stage == "out":
            self.arrived = list(arrived)
            return
        self.result = [kept[0]] + list(arrived)


class Exchange:
    def __init__(self, pieces):
        self.pieces = pieces

    def moves(self, stage):
        return [Move(one, one.shape, "blk", k) for k, one in enumerate(self.pieces) if k]

    def absorb(self, stage, arrived, kept):
        self.result = self.pieces[:1] + list(arrived)


class Pieces:
    def __init__(self, tensor, part, start, width):
        self.tensor, self.part, self.start, self.width = tensor, part, start, width

    def moves(self, stage):
        part, span = self.part, slice(self.start, self.start + self.width)
        count = lax.axis_size("blk")
        return [
            Move(self.tensor, (part, self.width), "blk", k,
                 lambda ref, k=k: ref.at[at(flipped(place_of(), k, count), part), span])
            for k in range(1, count)
        ]

    def absorb(self, stage, arrived, kept):
        self.result = list(arrived)


class Gather:
    def __init__(self, tensor):
        self.tensor = tensor

    def moves(self, stage):
        return [
            Move(self.tensor, self.tensor.shape, "blk", k) for k in range(1, lax.axis_size("blk"))
        ]

    def absorb(self, stage, arrived, kept):
        self.result = [self.tensor] + list(arrived)


class Spread:
    def __init__(self, tensor):
        self.tensor = tensor

    def moves(self, stage):
        count = lax.axis_size("blk")
        rows, width = self.tensor.shape[0], self.tensor.shape[1] // 2
        moves, self.places = [], []
        for number in range(2):
            span = slice(number * width, (number + 1) * width)
            own = lambda ref, span=span: ref.at[:, span]
            along = []
            for k in range(2, count, 2):
                along.append(Move(self.tensor, (rows, width), "blk", k, own, number))
                self.places.append((number, k))
            moves += along
            moves.append(Move(self.tensor, (rows, width), "blk", 1, own, number + 1))
            self.places.append((number, 1))
            for one in along:
                moves.append(Move(one, (rows, width), "blk", 1, whole, number + 1))
                self.places.append((number, one.flip + 1))
        return moves

    def absorb(self, stage, arrived, kept):
        found = dict(zip(self.places, arrived))
        count = lax.axis_size("blk")
        self.result = [found[number, k] for number in range(2) for k in range(1, count)]


class Norms:
    def __init__(self, tensor):
        self.tensor = tensor

    def moves(self, stage):
        axis = "rep" if stage == "out" else "blk"
        count = lax.axis_size(axis)
        shape = self.tensor.shape
        if stage == "out":
            return [Move(self.tensor, shape, axis, k) for k in range(1, count)]
        return [
            Move(self.tensor, shape[1:], axis, k,
                 lambda ref, k=k: ref.at[flipped(place_of(), k, count)])
            for k in range(1, count)
        ]

    def absorb(self, stage, arrived, kept):
        if stage == "out":
            for one in arrived:
                self.tensor = self.tensor + one
        else:
            self.result = [pick(self.tensor, lax.axis_index("blk"), 0)] + list(arrived)


VMEM = pl.BlockSpec(memory_space=pltpu.VMEM)
SMEM = pl.BlockSpec(memory_space=pltpu.SMEM)
ANY = pl.BlockSpec(memory_space=pl.ANY)


def like(*shape, kind=NARROW):
    return jax.ShapeDtypeStruct(shape, kind)


def index_of(items, item):
    return next(k for k, one in enumerate(items) if one is item)


def call(
    kernel, outs, operands, specs, scratch, flops, grid=None, out_specs=None, semaphores=0,
    moves=(), ident=None, ticking=False, lazy=(), early=(),
):
    scratch = [pltpu.VMEM(shape, kind) for shape, kind in scratch]
    if semaphores:
        scratch.append(pltpu.SemaphoreType.DMA((semaphores,)))
    out_specs = [VMEM] * len(outs) if out_specs is None else out_specs
    extra = {} if grid is None else {"grid": grid}
    params = {}
    sources, folds = [], []

    def need(array):
        if not any(array is one for one in sources):
            sources.append(array)

    for move in moves:
        if isinstance(move.source, Fold):
            if not any(move.source is one for one in folds):
                folds.append(move.source)
                for array in [move.source.own] + move.source.arrived:
                    need(array)
        elif move.late is None and not isinstance(move.source, Move):
            need(move.source)
    fixed_in, fixed_out = len(operands), len(outs)
    partners = sorted({(move.axis, move.flip) for move in moves})
    lasts = max([move.phase for move in moves], default=0)
    held_in = [k for k, spec in enumerate(specs) if spec is VMEM]
    held_out = [k for k, spec in enumerate(out_specs) if spec is VMEM]
    own_scratch = len(scratch)
    scratch += [pltpu.VMEM(operands[k].shape, operands[k].dtype) for k in held_in]
    scratch += [pltpu.VMEM(outs[k].shape, outs[k].dtype) for k in held_out]
    terms = sum(1 + len(fold.arrived) for fold in folds)
    for fold in folds:
        scratch += [pltpu.VMEM(fold.shape, NARROW)] * (1 + len(fold.arrived))
    for number in (len(held_in), len(held_out), terms, len(folds), len(moves), len(moves)):
        scratch.append(pltpu.SemaphoreType.DMA((max(number, 1),)))
    if moves:
        params = {"collective_id": ident, "has_side_effects": True}
    before = {}
    for move in moves:
        if isinstance(move.source, Move):
            number = index_of(moves, move.source)
            before[number] = min(move.phase, before.get(number, move.phase))

    def body_kernel(*refs):
        ins, refs = list(refs[:fixed_in]), refs[fixed_in:]
        sent, refs = refs[: len(sources)], refs[len(sources) :]
        results, refs = list(refs[:fixed_out]), refs[fixed_out:]
        landed, refs = refs[: len(moves)], refs[len(moves) :]
        kept, refs = refs[: len(folds)], refs[len(folds) :]
        rest, refs = refs[:own_scratch], refs[own_scratch:]
        inner, refs = refs[: len(held_in)], refs[len(held_in) :]
        outer, refs = refs[: len(held_out)], refs[len(held_out) :]
        buffers, (in_sem, out_sem, load_sem, keep_sem, send_sem, recv_sem) = refs[:terms], refs[terms:]
        fetches, stores = {}, {}
        for number, k in enumerate(held_in):
            fetches[k] = pltpu.make_async_copy(ins[k], inner[number], in_sem.at[number])
            ins[k] = inner[number]
        for number, k in enumerate(held_out):
            stores[k] = pltpu.make_async_copy(outer[number], results[k], out_sem.at[number])
            results[k] = outer[number]

        def target(axis, flip):
            return {axis: flipped(lax.axis_index(axis), flip, lax.axis_size(axis))}

        def buffers_of(fold):
            start = sum(1 + len(one.arrived) for one in folds[: index_of(folds, fold)])
            return start, buffers[start : start + 1 + len(fold.arrived)]

        def made(k):
            move = moves[k]
            if move.late is not None:
                source = results[move.late]
            elif isinstance(move.source, Fold):
                source = buffers_of(move.source)[1][0]
            elif isinstance(move.source, Move):
                source = landed[index_of(moves, move.source)]
            else:
                source = sent[index_of(sources, move.source)]
            return pltpu.make_async_remote_copy(
                src_ref=move.take(source),
                dst_ref=landed[k],
                send_sem=send_sem.at[k],
                recv_sem=recv_sem.at[k],
                device_id=target(move.axis, move.flip),
                device_id_type=pl.DeviceIdType.MESH,
            )

        def loads(fold):
            start, held = buffers_of(fold)
            return [
                pltpu.make_async_copy(
                    (fold.take if k == 0 else whole)(sent[index_of(sources, array)]),
                    held[k],
                    load_sem.at[start + k],
                )
                for k, array in enumerate([fold.own] + fold.arrived)
            ]

        def keeping(k):
            fold = folds[k]
            return pltpu.make_async_copy(
                fold.keep(buffers_of(fold)[1][0]), kept[k], keep_sem.at[k]
            )

        def add(fold):
            held = buffers_of(fold)[1]

            def one(index):
                if len(held) == 2:
                    held[0][index] = held[0][index] + held[1][index]
                elif len(held) > 2:
                    held[0][index] = functools.reduce(
                        jnp.add, [part[index].astype(SINGLE) for part in held]
                    ).astype(NARROW)

            if len(fold.shape) == 2:
                one((slice(None), slice(None)))
            else:
                loop(fold.shape[0], one)

        def begin():
            for fold in folds:
                for load in loads(fold):
                    load.start()
            for fetch in fetches.values():
                fetch.start()
            if moves:
                barrier = pltpu.get_barrier_semaphore()
                for axis, flip in partners:
                    pl.semaphore_signal(
                        barrier, inc=1, device_id=target(axis, flip),
                        device_id_type=pl.DeviceIdType.MESH,
                    )
                pl.semaphore_wait(barrier, len(partners))
            for k, move in enumerate(moves):
                if move.phase == 0 and move.late is None and not isinstance(move.source, Fold):
                    made(k).start()
            for number, fold in enumerate(folds):
                for load in loads(fold):
                    load.wait()
                add(fold)
                for k, move in enumerate(moves):
                    if move.source is fold:
                        made(k).start()
                keeping(number).start()
            for k, fetch in fetches.items():
                if k not in lazy:
                    fetch.wait()

        def launch(which):
            for k in range(len(moves)):
                if moves[k].late == which and moves[k].phase == 0:
                    made(k).start()

        def tick(phase):
            for k, needed in before.items():
                if needed == phase:
                    made(k).wait_recv()
            for k, move in enumerate(moves):
                if move.phase == phase:
                    made(k).start()

        def finish():
            for k, store in stores.items():
                if k not in early:
                    store.start()
            if not ticking:
                for phase in range(1, lasts + 1):
                    tick(phase)
            for k in range(len(moves)):
                made(k).wait_send()
                if k not in before:
                    made(k).wait_recv()
            for k in range(len(folds)):
                keeping(k).wait()
            for store in stores.values():
                store.wait()

        options = {}
        if any(move.late is not None for move in moves):
            options["launch"] = launch
        if ticking:
            options["tick"] = tick
        if lazy:
            options["ready"] = lambda k: fetches[k].wait()
        if early:
            options["flush"] = lambda k: stores[k].start()
        if grid is None:
            begin()
            kernel(*ins, *results, *rest, **options)
            finish()
        else:
            pl.when(pl.program_id(0) == 0)(begin)
            kernel(*ins, *results, *rest, **options)
            pl.when(pl.program_id(0) == pl.num_programs(0) - 1)(finish)

    result = pl.pallas_call(
        body_kernel,
        out_shape=list(outs)
        + [
            like(*m.shape, kind=m.source.dtype if hasattr(m.source, "dtype") else NARROW)
            for m in moves
        ]
        + [like(*fold.keep_shape) for fold in folds],
        in_specs=[ANY if spec is VMEM else spec for spec in specs] + [ANY] * len(sources),
        out_specs=[ANY if spec is VMEM else spec for spec in out_specs]
        + [ANY] * (len(moves) + len(folds)),
        scratch_shapes=scratch,
        compiler_params=pltpu.CompilerParams(vmem_limit_bytes=60 * 2**20, **params),
        cost_estimate=pl.CostEstimate(
            flops=int(flops),
            bytes_accessed=sum(o.size * o.dtype.itemsize for o in operands),
            transcendentals=0,
        ),
        **extra,
    )(*operands, *sources)
    end = fixed_out + len(moves)
    return list(result[:fixed_out]), list(result[fixed_out:end]), (folds, list(result[end:]))


class Courier:
    def __init__(self, active):
        self.active, self.waiting, self.ident = active, [], 0

    def load(self, *jobs):
        self.waiting += jobs

    def run(self, kernel, outs, operands, specs, scratch, flops, **extra):
        jobs, self.waiting = self.waiting, []
        moves, ends = [], []
        for job, stage, *late in jobs:
            added = job.moves(stage)
            for move in added:
                if late and not isinstance(move.source, Move):
                    move.late = late[0]
            moves += added
            ends.append(len(moves))
        if moves:
            self.ident += 1
        results, arrived, (folds, kept) = call(
            kernel, outs, operands, specs, scratch, flops, moves=tuple(moves), ident=self.ident, **extra
        )
        start = 0
        for (job, stage, *late), end in zip(jobs, ends):
            if late:
                job.tensor = results[late[0]]
            own = [
                kept[k]
                for k, fold in enumerate(folds)
                if any(move.source is fold for move in moves[start:end])
            ]
            job.absorb(stage, arrived[start:end], own)
            start = end
        return results


def in_halves(arrays):
    width = arrays[0].shape[1] // 2
    return (
        arrays[:1] + [one[:, :width] for one in arrays[1:]] + [one[:, width:] for one in arrays[1:]]
    )


def body(
    patches,
    queries,
    window_valid,
    answer_length,
    norm_gain,
    norm_bias,
    attn_in,
    attn_out,
    mlp_in,
    mlp_out,
    cot_patches,
    cot_queries,
):
    x, q, cot_x, cot_q = patches[0], queries[0], cot_patches[0], cot_queries[0]
    rows, features = x.shape
    count = q.shape[0]
    hidden = mlp_in.shape[2]
    blocks = lax.axis_size("blk")
    place = lax.axis_index("blk").astype(jnp.int32)
    share = features // blocks
    hidden_share = hidden // blocks
    share_rows = -(-share // 16) * 16
    hidden_rows = -(-hidden_share // 16) * 16
    part = -(-count // (blocks * 16)) * 16
    padded = part * blocks
    wide = 3 * features
    last = wide + features + features
    causal_columns = -(-last // 512) * 512
    leader = (place == 0).astype(SINGLE)
    valid = jnp.where(jnp.repeat(window_valid[0], WIN) > 0, 0.0, MASKED).astype(SINGLE)
    carried = blocks == DIRECT and lax.axis_size("rep") == 4 and share % 32 == 0
    courier = Courier(carried)

    def own_columns(tensor):
        return lax.dynamic_slice_in_dim(tensor, place * share, share, 1)

    square = 2.0 * features * features
    run = courier.run

    n0, pw, mw, x1, nx, vq, ckv = run(
        window_forward,
        [
            like(rows, features), like(rows, wide), like(rows, features),
            like(rows, features, kind=SINGLE), like(rows, features), like(rows, features),
            like(rows, 2 * features),
        ],
        [x, norm_gain, norm_bias, attn_in, attn_out],
        [VMEM, VMEM, VMEM, ANY, ANY],
        [((features, wide), NARROW), ((features, features), NARROW),
         ((features, features), NARROW), ((features, 2 * features), NARROW)],
        rows * square * 9,
        semaphores=4,
        early=(0, 1, 2, 3, 4, 5),
    )
    n1, pq, mq, q1, nq, cq, vkv, log_q = run(
        causal_forward,
        [
            like(count, features), like(count, wide), like(count, features),
            like(padded, features, kind=SINGLE), like(padded, features), like(count, features),
            like(count, 2 * features), like(16, count, kind=SINGLE),
        ],
        [q, norm_gain, norm_bias, attn_in, attn_out],
        [VMEM, VMEM, VMEM, ANY, ANY],
        [((features, wide), NARROW), ((features, features), NARROW),
         ((features, features), NARROW), ((features, 2 * features), NARROW),
         ((count, PAIR), SINGLE)],
        count * square * 15,
        semaphores=4,
        early=(0, 1, 2, 3, 4, 5),
    )
    outs, *log_pieces = run(
        functools.partial(cross_forward, blocks),
        [like(padded, features)] + [like(16, part, kind=SINGLE)] * blocks,
        [cq, ckv, valid[None, :]],
        [VMEM, VMEM, VMEM],
        [((padded, PAIR), SINGLE)],
        count * square * 6,
    )
    logs = Exchange(log_pieces)
    halves = [Pieces(outs, part, k * features // 2, features // 2) for k in range(2)]
    if carried:
        courier.load((logs, ""), (halves[0], ""))
    mv, x2, log_v = run(
        reverse_forward,
        [like(rows, features), like(rows, features, kind=SINGLE), like(16, rows, kind=SINGLE)],
        [answer_length, vq, vkv, x1, attn_out],
        [SMEM, VMEM, VMEM, VMEM, ANY],
        [((features, features), NARROW), ((rows, PAIR), SINGLE)],
        rows * square * 8,
        semaphores=1,
    )
    if carried:
        courier.load((halves[1], ""))
    x3, dx2, up_x, down_x, norm_five = run(
        patch_feed_forward,
        [
            like(rows, features), like(rows, features, kind=SINGLE), like(features, hidden),
            like(hidden, features), like(8, features, kind=SINGLE),
        ],
        [x2, cot_x, norm_gain, norm_bias, mlp_in, mlp_out],
        [
            VMEM, VMEM, VMEM, VMEM,
            pl.BlockSpec((1, features, CHUNK), lambda j: (0, 0, j)),
            pl.BlockSpec((1, CHUNK, features), lambda j: (0, j, 0)),
        ],
        [((rows, features), NARROW), ((rows, CHUNK), NARROW), ((rows, CHUNK), NARROW),
         ((rows, features), SINGLE), ((rows, features), SINGLE)],
        rows * square * 24,
        grid=(hidden // CHUNK,),
        out_specs=[
            VMEM, VMEM,
            pl.BlockSpec((features, CHUNK), lambda j: (0, j)),
            pl.BlockSpec((CHUNK, features), lambda j: (j, 0)),
            VMEM,
        ],
    )
    if carried:
        merged = run(
            functools.partial(merge_blocks, blocks),
            [like(part, features), like(16, part, kind=SINGLE)],
            [outs] + logs.result + halves[0].result + halves[1].result,
            [VMEM] * (3 * blocks - 1),
            [],
            padded * square,
        )
        co_parts, log_parts = Spread(merged[0]), Gather(merged[1])
        up_x, down_x = Reduction(up_x), Reduction(down_x)
        reverse_weight = Reduction(like(blocks // 2, 2, 2, share // 2, 2 * features))
        courier.load(
            (co_parts, ""), (log_parts, ""), (up_x, "core"), (down_x, "core"),
            (reverse_weight, "core", 1),
        )
    else:
        whole_logs = jnp.stack(exchange(log_pieces))
        merged_log = jax.nn.logsumexp(whole_logs, axis=0)
        weights = jnp.transpose(jnp.exp(whole_logs - merged_log)[:, :HEADS], (0, 2, 1))
        shares = lax.all_to_all(outs.reshape(blocks, part, features), "blk", 0, 0)
        merged_out = jnp.sum(jnp.repeat(weights, HEAD, axis=2) * shares.astype(SINGLE), axis=0)
        co_parts, log_parts = Spread(None), Gather(None)
        co_parts.tensor, *co_parts.result = in_halves(gather(merged_out.astype(NARROW)))
        log_parts.result = gather(merged_log)
    folded = (blocks // 2, 2, 2, share // 2) if carried else (features,)
    dvq, reverse_grad, *kv_pieces = run(
        functools.partial(reverse_backward, blocks),
        [like(rows, features), like(*folded, 2 * features)]
        + [like(part, features)] * (2 * blocks),
        [answer_length, dx2, mv, vq, vkv, nx, log_v, attn_out],
        [SMEM, VMEM, VMEM, VMEM, VMEM, VMEM, VMEM, ANY],
        [((features, features), NARROW), ((rows, features), NARROW), ((rows, features), NARROW),
         ((16, rows), SINGLE), ((padded, 2 * features), SINGLE)],
        rows * square * 16,
        semaphores=1,
        ticking=carried,
    )
    k_parts, v_parts = Exchange(kv_pieces[:blocks]), Exchange(kv_pieces[blocks:])
    if carried:
        courier.load((k_parts, ""), (up_x, "x"))
    else:
        k_parts.result, v_parts.result = exchange(k_parts.pieces), exchange(v_parts.pieces)
    q3, dq2, up_q, down_q, norm_four, co = run(
        functools.partial(query_feed_forward, blocks, share, hidden_share),
        [
            like(count, features), like(count, features, kind=SINGLE), like(share_rows, hidden),
            like(hidden_rows, features), like(8, features, kind=SINGLE), like(padded, features),
        ],
        [q1, cot_q, norm_gain, norm_bias, attn_out, mlp_in, mlp_out, co_parts.tensor]
        + co_parts.result,
        [
            VMEM, VMEM, VMEM, VMEM, pl.BlockSpec((1, features, features), lambda j: (2, 0, 0)),
            pl.BlockSpec((1, features, CHUNK), lambda j: (1, 0, j)),
            pl.BlockSpec((1, CHUNK, features), lambda j: (1, j, 0)),
        ] + [ANY] * (2 * blocks - 1),
        [((count, features), SINGLE), ((count, features), NARROW), ((share_rows, count), NARROW),
         ((count, CHUNK), NARROW), ((count, CHUNK), NARROW),
         ((count, features), SINGLE), ((count, features), SINGLE)],
        count * square * 18,
        semaphores=2 * blocks - 1,
        grid=(hidden // CHUNK,),
        out_specs=[
            VMEM, VMEM,
            pl.BlockSpec((share_rows, CHUNK), lambda j: (0, j)),
            VMEM, VMEM, VMEM,
        ],
    )
    if carried:
        up_q, down_q = RepSum(up_q, 1), RepSum(down_q, 0)
        courier.load((v_parts, ""), (down_x, "x"), (up_x, "y"))
    dckv, cross_out_weight, *q_pieces = run(
        functools.partial(cross_backward, blocks, share),
        [like(rows, 2 * features), like(share_rows, features)] + [like(part, features)] * blocks,
        [dq2, co, cq, ckv, valid[:, None], attn_out] + log_parts.result,
        [VMEM, VMEM, VMEM, VMEM, VMEM, ANY] + [VMEM] * blocks,
        [((features, features), NARROW), ((count, features), NARROW), ((count, features), NARROW),
         ((16, count), SINGLE), ((padded, PAIR), SINGLE), ((16, count), SINGLE),
         ((padded, features), NARROW), ((rows, 2 * features), SINGLE)],
        count * square * 12,
        semaphores=1,
    )
    q_parts = Exchange(q_pieces)
    if carried:
        kv_weight = Reduction(like(blocks // 2, 2, 2, share // 2, 2 * features))
        window_weight = Reduction(like(blocks // 2, 2, 2, share // 2, 4 * features))
        courier.load(
            (q_parts, ""), (down_x, "y"), (reverse_weight, "x"), (up_q, "out"), (down_q, "out"),
            (kv_weight, "core", 0), (window_weight, "core", 1),
        )
    else:
        q_parts.result = exchange(q_pieces)
    kv_grad, window_grad, grad_x, norm_x = run(
        patch_backward,
        [
            like(*folded, 2 * features), like(*folded, 4 * features),
            like(rows, features, kind=SINGLE), like(8, features, kind=SINGLE),
        ],
        [x, dx2, x1, nx, n0, pw, mw, dvq, dckv, norm_gain, attn_in, attn_out],
        [VMEM] * 10 + [ANY, ANY],
        [((features, wide), NARROW), ((features, features), NARROW),
         ((features, features), NARROW), ((features, 2 * features), NARROW),
         ((rows, features), SINGLE), ((rows, features), NARROW), ((rows, features), NARROW),
         ((16, rows), SINGLE), ((rows, wide), NARROW)],
        rows * square * 24,
        semaphores=4,
        lazy=(0, 4, 5, 6),
        early=(0, 1),
    )
    if carried:
        share_weight = Reduction(like(blocks // 2, 2, 2, share // 2, wide))
        dq1_parts = Spread(like(part, features))
        courier.load(
            (share_weight, "core", 1), (dq1_parts, "", 0), (window_weight, "x"),
            (reverse_weight, "y"),
        )
    dq1_share, share_grad, norm_two = run(
        functools.partial(share_backward, blocks),
        [like(part, features), like(*folded, wide), like(8, features, kind=SINGLE)],
        [q1, nq, norm_gain, attn_in]
        + q_parts.result + k_parts.result + v_parts.result,
        [ANY, ANY, VMEM, ANY] + [VMEM] * (3 * blocks),
        [((features, features), NARROW), ((features, 2 * features), NARROW),
         ((part, wide), NARROW), ((part, features), SINGLE), ((part, features), NARROW)],
        part * square * 6,
        semaphores=4,
    )
    def arrive(*jobs):
        courier.load(*jobs)
        run(nothing, [], [], [], [], 0)

    if carried:
        courier.load(
            (window_weight, "y"), (share_weight, "y"), (kv_weight, "x"), (down_x, "z"),
            (reverse_weight, "z"), (up_q, "back"), (down_q, "back"), (up_x, "z"),
        )
    else:
        dq1_parts = Spread(None)
        dq1_parts.tensor, *dq1_parts.result = in_halves(gather(dq1_share))
    causal_weight, grad_q, norm_one = run(
        functools.partial(causal_backward, blocks, share),
        [
            like(share_rows, causal_columns), like(count, features, kind=SINGLE),
            like(8, features, kind=SINGLE),
        ],
        [q, dq2, n1, pq, mq, log_q, cross_out_weight, norm_gain, attn_in, attn_out]
        + [dq1_parts.tensor] + dq1_parts.result,
        [VMEM] * 8 + [ANY] * (2 * blocks + 1),
        [((features, wide), NARROW), ((features, features), NARROW), ((padded, features), NARROW),
         ((count, features), SINGLE), ((count, features), NARROW), ((count, features), NARROW),
         ((16, count), SINGLE), ((count, 2 * PAIR), SINGLE), ((count, wide), NARROW)],
        count * square * 16,
        semaphores=2 * blocks + 1,
        lazy=(2, 3, 4, 5),
    )
    gains = jnp.stack(
        (norm_x[2], norm_one[0] * leader, norm_two[0], norm_x[0], norm_four[0] * leader, norm_five[0])
    )
    biases = jnp.stack(
        (norm_x[3], norm_one[1] * leader, norm_two[1], norm_x[1], norm_four[1] * leader, norm_five[1])
    )
    rest = (
        x3[None],
        own_columns(q3)[None],
        grad_x[None],
        own_columns(grad_q)[None],
    )
    if carried:
        norms = jnp.concatenate((jnp.pad(gains, ((0, 2), (0, 0))), jnp.pad(biases, ((0, 2), (0, 0)))))
        norms = jnp.transpose(norms.reshape(16, blocks, share), (1, 0, 2))
        norms = Norms(jnp.pad(norms, ((0, 0), (0, 0), (0, -share % PAIR))))
        causal_weight = RepSum(causal_weight, 1)
        arrive(
            (share_weight, "x"), (causal_weight, "out"), (norms, "out"), (kv_weight, "y"),
            (window_weight, "z"), (down_x, "back_x"), (reverse_weight, "back_x"),
            (up_x, "back_x"),
        )
        arrive(
            (share_weight, "z"), (kv_weight, "z"), (causal_weight, "back"), (norms, "back"),
            (down_x, "back_core"), (reverse_weight, "back_core"), (window_weight, "back_x"),
            (up_x, "back_core"),
        )
        arrive((share_weight, "back"), (kv_weight, "back"), (window_weight, "back_core"))
        sums = [up_x, down_x, reverse_weight, window_weight, kv_weight, share_weight]
        quarters = [up_q, down_q, causal_weight]
        operands = sum([one.result for one in sums + quarters], []) + norms.result
        grads = run(
            functools.partial(assemble, len(sums), len(quarters), blocks),
            [
                like(4, share, wide, kind=SINGLE), like(4, share, features, kind=SINGLE),
                like(2, share, hidden, kind=SINGLE), like(2, hidden_share, features, kind=SINGLE),
                like(6, share, kind=SINGLE), like(6, share, kind=SINGLE),
            ],
            operands,
            [VMEM] * len(operands),
            [((share, 4 * features), SINGLE), ((share, causal_columns), SINGLE)],
            0,
        )
        return rest + (grads[4], grads[5], grads[0], grads[1], grads[2], grads[3])
    up_x, down_x, reverse_weight, window_weight, kv_weight, share_weight = (
        reduce_all(one) for one in (up_x, down_x, reverse_grad, window_grad, kv_grad, share_grad)
    )
    up_q, down_q = reduce_rep(up_q[:share]), reduce_rep(down_q[:hidden_share])
    causal_weight = reduce_rep(causal_weight[:share])
    gains, biases = (
        own_columns(one) for one in lax.psum((gains, biases), ("blk", "rep"))
    )
    grad_attn_in = jnp.stack(
        (
            window_weight[:, :wide],
            causal_weight[:, :wide],
            jnp.concatenate((share_weight[:, :features], kv_weight), axis=1),
            jnp.concatenate((reverse_weight[:, :features], share_weight[:, features:]), axis=1),
        )
    )
    grad_attn_out = jnp.stack(
        (
            window_weight[:, wide:],
            causal_weight[:, wide : wide + features],
            causal_weight[:, wide + features : last],
            reverse_weight[:, features:],
        )
    )
    return rest + (
        gains,
        biases,
        grad_attn_in.astype(SINGLE),
        grad_attn_out.astype(SINGLE),
        jnp.stack((up_x, up_q)).astype(SINGLE),
        jnp.stack((down_x, down_q)).astype(SINGLE),
    )


def solution(mesh):
    placed = (
        P("rep", "blk", None),
        P("rep", None, None),
        P("rep", "blk"),
        P("rep"),
        P(),
        P(),
        P(),
        P(),
        P(),
        P(),
        P("rep", "blk", None),
        P("rep", None, None),
    )
    return jax.shard_map(
        body,
        mesh=mesh,
        in_specs=placed,
        out_specs=(
            P("rep", "blk", None),
            P("rep", None, "blk"),
            P("rep", "blk", None),
            P("rep", None, "blk"),
            P(None, "blk"),
            P(None, "blk"),
            P(None, "blk", None),
            P(None, "blk", None),
            P(None, "blk", None),
            P(None, "blk", None),
        ),
        check_vma=False,
    )
```

```python
import functools
import math

import jax
import jax.numpy as jnp
from jax import lax
from jax.experimental import pallas as pl
from jax.experimental.pallas import tpu as pltpu
from jax.sharding import PartitionSpec as P

HEADS = 12
WIN = 64
EPSILON = 1e-05
MASKED = -1e30
NARROW = jnp.bfloat16
SINGLE = jnp.float32
EXACT = lax.Precision.HIGHEST
GROUP = 128
WINDOWS = 256
PAIR = 128
HEAD = 64
STRIP = 160
LONG = 400
CHUNK = 768


def dot(former, latter, ahead, behind, precision=None):
    return lax.dot_general(
        former,
        latter,
        (((ahead,), (behind,)), ((), ())),
        preferred_element_type=SINGLE,
        precision=precision,
    )


def plain(former, latter):
    return dot(former, latter, 1, 0)


def right_t(former, latter):
    return dot(former, latter, 1, 1)


def left_t(former, latter):
    return dot(former, latter, 0, 0)


def loop(count, action):
    def step(index, nothing):
        action(index)
        return nothing

    lax.fori_loop(0, count, step, 0)


def at(index, size):
    return pl.ds(pl.multiple_of(index * size, size), size)


def iota(shape, dim):
    return lax.broadcasted_iota(jnp.int32, shape, dim)


def statistics(tensor):
    average = jnp.mean(tensor, axis=-1, keepdims=True)
    centred = tensor - average
    spread = jnp.mean(centred * centred, axis=-1, keepdims=True)
    return centred, lax.rsqrt(spread + EPSILON)


def norm(tensor, gain, bias):
    centred, inverse = statistics(tensor)
    return centred * inverse * gain + bias


def norm_back(tensor, gain, upstream):
    centred, inverse = statistics(tensor)
    scaled = centred * inverse
    inner = upstream * gain
    grad = inverse * (
        inner
        - jnp.mean(inner, axis=-1, keepdims=True)
        - scaled * jnp.mean(inner * scaled, axis=-1, keepdims=True)
    )
    return (
        grad,
        jnp.sum(upstream * scaled, axis=0, keepdims=True),
        jnp.sum(upstream, axis=0, keepdims=True),
    )


def gelu_both(tensor):
    size = jnp.abs(tensor)
    ratio = 1.0 / (1.0 + (0.3275911 * math.sqrt(0.5)) * size)
    series = ratio * (
        0.254829592
        + ratio * (-0.284496736 + ratio * (1.421413741 + ratio * (-1.453152027 + ratio * 1.061405429)))
    )
    bell = jnp.exp(-0.5 * (tensor * tensor))
    tail = 0.5 * series * bell
    below = jnp.where(tensor >= 0, 1.0 - tail, tail)
    return tensor * below, below + tensor * bell * (1.0 / math.sqrt(2.0 * math.pi))


def half(which, value=1.0):
    return jnp.where(iota((1, PAIR), 1) // HEAD == which, value, 0.0).astype(NARROW)


def lower_lanes():
    return iota((1, PAIR), 1) < HEAD


def both(tensor, value=1.0):
    return jnp.concatenate((tensor * half(0, value), tensor * half(1, value)), axis=0)


def attend(queries, keys, values, mask):
    rows = queries.shape[0]
    scores = right_t(both(queries, 1.0 / math.sqrt(HEAD)), keys)
    weights, totals, logs = [], [], []
    for which in range(2):
        part = mask(scores[which * rows : (which + 1) * rows])
        peak = jnp.max(part, axis=-1, keepdims=True)
        part = jnp.exp(part - peak)
        total = jnp.sum(part, axis=-1, keepdims=True)
        weights.append(part.astype(NARROW))
        totals.append(1.0 / total)
        logs.append(peak + jnp.log(total))
    out = plain(jnp.concatenate(weights, axis=0), values)
    return jnp.where(lower_lanes(), out[:rows] * totals[0], out[rows:] * totals[1]), logs


def attend_back(queries, keys, values, upstream, logs, deltas, mask):
    scaled = queries * jnp.asarray(1.0 / math.sqrt(HEAD), NARROW)
    count = keys.shape[0]
    keys = both(keys)
    turned_keys = keys.T
    scores = right_t(keys, scaled)
    inner = right_t(both(values), upstream)
    weights, slopes = [], []
    for which in range(2):
        span = slice(which * count, (which + 1) * count)
        part = mask(scores[span])
        if logs is None:
            part = jnp.exp(part - jnp.max(part, axis=0, keepdims=True))
            part = part * (1.0 / jnp.sum(part, axis=0, keepdims=True))
        else:
            part = jnp.exp(part - logs[which])
        weights.append(part.astype(NARROW))
        slopes.append((part * (inner[span] - deltas[which])).astype(NARROW))
    slope = jnp.concatenate(slopes, axis=0)
    query_grad = plain(turned_keys, slope).T
    key_grad = plain(slope, scaled)
    value_grad = plain(jnp.concatenate(weights, axis=0), upstream)
    lanes = lower_lanes()
    return (
        query_grad,
        jnp.where(lanes, key_grad[:count], key_grad[count:]),
        jnp.where(lanes, value_grad[:count], value_grad[count:]),
    )


def head_rows(tensor):
    features = tensor.shape[1]
    heads = 16
    chosen = jnp.where(
        iota((heads, features), 1) // HEAD == iota((heads, features), 0), 1.0, 0.0
    ).astype(SINGLE)
    return dot(chosen, tensor, 1, 1, EXACT)


def turn(columns):
    same = jnp.where(iota((16, columns.shape[1]), 0) == iota((16, columns.shape[1]), 1), 1.0, 0.0)
    return dot(same.astype(SINGLE), columns, 1, 1, EXACT)


def row_pair(ref, pair, span):
    tensor = ref[:, span]
    index = iota(tensor.shape, 0)
    return [
        jnp.sum(jnp.where(index == 2 * pair + which, tensor, 0.0), axis=0, keepdims=True)
        for which in range(2)
    ]


def chooser(rows, width, start, count):
    row = iota((rows, width), 0)
    hit = jnp.logical_and(iota((rows, width), 1) == row + start, row < count)
    return jnp.where(hit, 1.0, 0.0).astype(NARROW)


def spans(rows, size):
    edges = [(start, min(start + size, rows)) for start in range(0, rows, size)]
    if len(edges) > 1 and edges[-1][1] - edges[-1][0] < PAIR:
        edges[-2:] = [(edges[-2][0], rows)]
    return edges


def mark(log_ref, rows, head, value):
    log_ref[rows, :] = jnp.where(iota((1, PAIR), 1) == head, value, log_ref[rows, :])


def store_rows(ref, columns, value):
    ref[(slice(None),) * (len(ref.shape) - 1) + (columns,)] = value.astype(ref.dtype).reshape(
        ref.shape[:-1] + value.shape[1:]
    )


def nothing(*unused):
    return None


def copies(semaphores, *pairs):
    made = [
        pltpu.make_async_copy(source, target, semaphores.at[k])
        for k, (source, target) in enumerate(pairs)
    ]
    for one in made:
        one.start()
    return made


DIRECT = 8


def place_of(axis="blk"):
    return lax.axis_index(axis)


def flipped(index, mask, count):
    total, weight = 0, 1
    while weight < count:
        bit = (index // weight) % 2
        total = total + weight * ((1 - bit) if mask & weight else bit)
        weight *= 2
    return total


def piece_at(number, count):
    return flipped(place_of(), number, count) if count <= DIRECT else number


def window_forward(
    x_ref, gain_ref, bias_ref, a_in, a_out,
    n0_ref, pw_ref, mw_ref, x1_ref, nx_ref, vq_ref, ckv_ref,
    w_in, w_out, w_q, w_kv, sem,
    flush=nothing,
):
    rows, features = x_ref.shape
    loads = copies(
        sem,
        (a_in.at[0], w_in),
        (a_out.at[0], w_out),
        (a_in.at[3, :, pl.ds(0, features)], w_q),
        (a_in.at[2, :, pl.ds(features, 2 * features)], w_kv),
    )

    def first(i):
        span = at(i, GROUP)
        n0_ref[span, :] = norm(
            x_ref[span, :].astype(SINGLE), gain_ref[0:1, :], bias_ref[0:1, :]
        ).astype(NARROW)

    loop(rows // GROUP, first)
    loads[0].wait()

    def project(j):
        span = at(j, CHUNK)
        pw_ref[:, span] = plain(n0_ref[...], w_in[:, span]).astype(NARROW)

    loop(3 * features // CHUNK, project)
    flush(0)
    flush(1)
    window = jnp.where(
        iota((WINDOWS, WINDOWS), 0) // WIN == iota((WINDOWS, WINDOWS), 1) // WIN, 0.0, MASKED
    )

    def group(i):
        span = at(i, WINDOWS)
        for pair in range(features // PAIR):
            lane = pair * PAIR
            out, unused = attend(
                pw_ref[span, lane : lane + PAIR],
                pw_ref[span, features + lane : features + lane + PAIR],
                pw_ref[span, 2 * features + lane : 2 * features + lane + PAIR],
                lambda scores: scores + window,
            )
            mw_ref[span, lane : lane + PAIR] = out.astype(NARROW)

    loop(rows // WINDOWS, group)
    flush(2)
    loads[1].wait()

    def second(i):
        span = at(i, GROUP)
        total = x_ref[span, :].astype(SINGLE) + plain(mw_ref[span, :], w_out[...])
        x1_ref[span, :] = total
        nx_ref[span, :] = norm(total, gain_ref[3:4, :], bias_ref[3:4, :]).astype(NARROW)

    loop(rows // GROUP, second)
    flush(3)
    flush(4)
    loads[2].wait()
    vq_ref[...] = plain(nx_ref[...], w_q[...]).astype(NARROW)
    flush(5)
    loads[3].wait()

    def third(j):
        span = at(j, CHUNK)
        ckv_ref[:, span] = plain(nx_ref[...], w_kv[:, span]).astype(NARROW)

    loop(2 * features // CHUNK, third)


def causal_forward(
    q_ref, gain_ref, bias_ref, a_in, a_out,
    n1_ref, pq_ref, mq_ref, q1_ref, nq_ref, cq_ref, vkv_ref, log_ref,
    w_in, w_out, w_q, w_kv, logs, sem,
    flush=nothing,
):
    rows, features = q_ref.shape
    loads = copies(
        sem,
        (a_in.at[1], w_in),
        (a_out.at[1], w_out),
        (a_in.at[2, :, pl.ds(0, features)], w_q),
        (a_in.at[3, :, pl.ds(features, 2 * features)], w_kv),
    )

    def first(i):
        span = at(i, STRIP)
        n1_ref[span, :] = norm(
            q_ref[span, :].astype(SINGLE), gain_ref[1:2, :], bias_ref[1:2, :]
        ).astype(NARROW)

    loop(rows // STRIP, first)
    loads[0].wait()

    def project(j):
        span = at(j, CHUNK)
        pq_ref[:, span] = plain(n1_ref[...], w_in[:, span]).astype(NARROW)

    loop(3 * features // CHUNK, project)
    flush(0)
    flush(1)
    logs[...] = jnp.zeros_like(logs)

    def pair(p):
        for start in range(0, rows, LONG):
            end = min(start + LONG, rows)

            def mask(scores, start=start):
                shape = scores.shape
                return jnp.where(iota(shape, 1) <= iota(shape, 0) + start, scores, MASKED)

            out, sums = attend(
                pq_ref[start:end, at(p, PAIR)],
                pq_ref[0:end, at(p + features // PAIR, PAIR)],
                pq_ref[0:end, at(p + 2 * features // PAIR, PAIR)],
                mask,
            )
            mq_ref[start:end, at(p, PAIR)] = out.astype(NARROW)
            for which in range(2):
                mark(logs, slice(start, end), 2 * p + which, sums[which])

    loop(features // PAIR, pair)
    flush(2)
    log_ref[...] = turn(logs[...])
    loads[1].wait()

    def second(i):
        span = at(i, STRIP)
        total = q_ref[span, :].astype(SINGLE) + plain(mq_ref[span, :], w_out[...])
        q1_ref[span, :] = total
        nq_ref[span, :] = norm(total, gain_ref[2:3, :], bias_ref[2:3, :]).astype(NARROW)

    loop(rows // STRIP, second)
    if q1_ref.shape[0] > rows:
        q1_ref[rows:, :] = jnp.zeros_like(q1_ref[rows:, :])
        nq_ref[rows:, :] = jnp.zeros_like(nq_ref[rows:, :])
    flush(3)
    flush(4)
    loads[2].wait()
    cq_ref[...] = plain(nq_ref[0:rows, :], w_q[...]).astype(NARROW)
    flush(5)
    loads[3].wait()

    def third(j):
        span = at(j, CHUNK)
        vkv_ref[:, span] = plain(nq_ref[0:rows, :], w_kv[:, span]).astype(NARROW)

    loop(2 * features // CHUNK, third)


def cross_forward(pieces, cq_ref, ckv_ref, valid_ref, whole, *rest):
    log_refs, (logs,) = rest[:pieces], rest[pieces:]
    rows, features = cq_ref.shape
    part = log_refs[0].shape[1]
    logs[...] = jnp.zeros_like(logs)
    if whole.shape[0] > rows:
        whole[rows:, :] = jnp.zeros((whole.shape[0] - rows, features), NARROW)

    def pair(p):
        for start in range(0, rows, LONG):
            span = slice(start, min(start + LONG, rows))
            out, sums = attend(
                cq_ref[span, at(p, PAIR)],
                ckv_ref[:, at(p, PAIR)],
                ckv_ref[:, at(p + features // PAIR, PAIR)],
                lambda scores: scores + valid_ref[...],
            )
            whole[span, at(p, PAIR)] = out.astype(NARROW)
            for which in range(2):
                mark(logs, span, 2 * p + which, sums[which])

    loop(features // PAIR, pair)
    for k in range(pieces):
        log_refs[k][...] = turn(logs[at(piece_at(k, pieces), part), :])


def untwist(rows):
    same = jnp.where(iota((16, PAIR), 0) == iota((16, PAIR), 1), 1.0, 0.0)
    return dot(rows, same.astype(SINGLE), 0, 0, EXACT)


def merge_blocks(pieces, own_ref, *refs):
    logs, refs = refs[:pieces], refs[pieces:]
    halves, (co_ref, log_ref) = (refs[: pieces - 1], refs[pieces - 1 : -2]), refs[-2:]
    part, features = co_ref.shape
    width = features // 2
    peak = functools.reduce(jnp.maximum, [one[...] for one in logs])
    total = peak + jnp.log(functools.reduce(jnp.add, [jnp.exp(one[...] - peak) for one in logs]))
    log_ref[...] = total
    spread = jnp.where(
        iota((PAIR, features), 1) // HEAD == iota((PAIR, features), 0), 1.0, 0.0
    ).astype(NARROW)
    result = jnp.zeros(co_ref.shape, SINGLE)
    for k in range(pieces):
        weight = untwist(jnp.exp(logs[k][...] - total))
        high = weight.astype(NARROW)
        low = (weight - high.astype(SINGLE)).astype(NARROW)
        if k == 0:
            block = own_ref[at(place_of(), part), :]
        else:
            block = jnp.concatenate((halves[0][k - 1][...], halves[1][k - 1][...]), axis=1)
        result = result + (plain(high, spread) + plain(low, spread)) * block.astype(SINGLE)
    co_ref[...] = result.astype(NARROW)


def reverse_forward(
    length_ref, vq_ref, vkv_ref, x1_ref, a_out,
    mv_ref, x2_ref, log_ref,
    w_out, logs, sem,
):
    rows, features = vq_ref.shape
    keys = vkv_ref.shape[0]
    (load,) = copies(sem, (a_out.at[3], w_out))
    logs[...] = jnp.zeros_like(logs)
    bias = jnp.where(iota((1, keys), 1) < length_ref[0], 0.0, MASKED)

    def pair(p):
        for start in range(0, rows, WINDOWS):
            span = slice(start, start + WINDOWS)
            out, sums = attend(
                vq_ref[span, at(p, PAIR)],
                vkv_ref[:, at(p, PAIR)],
                vkv_ref[:, at(p + features // PAIR, PAIR)],
                lambda scores: scores + bias,
            )
            mv_ref[span, at(p, PAIR)] = out.astype(NARROW)
            for which in range(2):
                mark(logs, span, 2 * p + which, sums[which])

    loop(features // PAIR, pair)
    log_ref[...] = turn(logs[...])
    load.wait()

    def second(i):
        span = at(i, GROUP)
        x2_ref[span, :] = x1_ref[span, :] + plain(mv_ref[span, :], w_out[...])

    loop(rows // GROUP, second)


def feed_forward_step(block, normed, up, down, cot, hidden, slope, out, grad):
    rows = normed.shape[0]

    def strip(i):
        span = at(i, block)
        value, rise = gelu_both(plain(normed[span, :], up[...]))
        hidden[span, :] = value.astype(NARROW)
        slope[span, :] = (right_t(cot[span, :], down[...]) * rise).astype(NARROW)
        out[span, :] += plain(hidden[span, :], down[...])
        grad[span, :] += right_t(slope[span, :], up[...])

    loop(rows // block, strip)


def patch_feed_forward(
    x2_ref, cot_ref, gain_ref, bias_ref, up_ref, down_ref,
    x3_ref, dx2_ref, up_grad_ref, down_grad_ref, norm_ref,
    normed, hidden, slope, out, grad,
):
    rows = x2_ref.shape[0]
    step = pl.program_id(0)

    @pl.when(step == 0)
    def begin():
        def first(i):
            span = at(i, GROUP)
            normed[span, :] = norm(
                x2_ref[span, :], gain_ref[5:6, :], bias_ref[5:6, :]
            ).astype(NARROW)
            out[span, :] = x2_ref[span, :]
            grad[span, :] = jnp.zeros_like(grad[span, :])

        loop(rows // GROUP, first)

    feed_forward_step(
        512, normed, up_ref.at[0], down_ref.at[0], cot_ref, hidden, slope, out, grad
    )
    up_grad_ref[...] = left_t(normed[...], slope[...]).astype(NARROW)
    down_grad_ref[...] = left_t(hidden[...], cot_ref[...]).astype(NARROW)

    @pl.when(step == pl.num_programs(0) - 1)
    def finish():
        norm_ref[...] = jnp.zeros_like(norm_ref)

        def last(i):
            span = at(i, GROUP)
            x3_ref[span, :] = out[span, :].astype(NARROW)
            part, gain, bias = norm_back(x2_ref[span, :], gain_ref[5:6, :], grad[span, :])
            dx2_ref[span, :] = cot_ref[span, :].astype(SINGLE) + part
            norm_ref[0:1, :] += gain
            norm_ref[1:2, :] += bias

        loop(rows // GROUP, last)


def place_parts(ref, pieces, parts, sem):
    part, features = parts[0].shape
    width = features // 2
    pairs = [(parts[0], ref.at[at(piece_at(0, pieces), part), :])]
    for number in range(2):
        for k in range(1, pieces):
            pairs.append(
                (
                    parts[number * (pieces - 1) + k],
                    ref.at[at(piece_at(k, pieces), part), pl.ds(number * width, width)],
                )
            )
    return copies(sem, *pairs)


def query_feed_forward(
    pieces, share, hidden_share, q1_ref, cot_ref, gain_ref, bias_ref,
    w_out, up_ref, down_ref, *rest,
):
    parts, rest = rest[: 2 * pieces - 1], rest[2 * pieces - 1 :]
    (
        q3_ref, dq2_ref, up_grad_ref, down_grad_ref, norm_ref, co_ref,
        q2, normed, chosen, hidden, slope, out, grad, sem,
    ) = rest
    rows, features = cot_ref.shape
    width = up_ref.shape[2]
    step = pl.program_id(0)

    @pl.when(step == 0)
    def begin():
        for one in place_parts(co_ref, pieces, parts, sem):
            one.wait()

        def first(i):
            span = at(i, STRIP)
            total = q1_ref[span, :] + plain(co_ref[span, :], w_out[0])
            q2[span, :] = total
            out[span, :] = total
            normed[span, :] = norm(total, gain_ref[4:5, :], bias_ref[4:5, :]).astype(NARROW)
            grad[span, :] = jnp.zeros_like(grad[span, :])

        loop(rows // STRIP, first)
        chosen[...] = right_t(
            chooser(chosen.shape[0], features, place_of() * share, share), normed[...]
        ).astype(NARROW)

    feed_forward_step(
        LONG, normed, up_ref.at[0], down_ref.at[0], cot_ref, hidden, slope, out, grad
    )
    up_grad_ref[...] = plain(chosen[...], slope[...]).astype(NARROW)
    begins = place_of() * hidden_share

    @pl.when(begins // width == step)
    def own_hidden():
        taken = right_t(
            chooser(down_grad_ref.shape[0], width, begins - step * width, hidden_share),
            hidden[...],
        ).astype(NARROW)
        down_grad_ref[...] = plain(taken, cot_ref[...]).astype(NARROW)

    @pl.when(step == pl.num_programs(0) - 1)
    def finish():
        norm_ref[...] = jnp.zeros_like(norm_ref)

        def last(i):
            span = at(i, STRIP)
            q3_ref[span, :] = out[span, :].astype(NARROW)
            piece, gain, bias = norm_back(q2[span, :], gain_ref[4:5, :], grad[span, :])
            dq2_ref[span, :] = cot_ref[span, :].astype(SINGLE) + piece
            norm_ref[0:1, :] += gain
            norm_ref[1:2, :] += bias

        loop(rows // STRIP, last)


def reverse_backward(
    pieces, length_ref, dx2_ref, mv_ref, vq_ref, vkv_ref, nx_ref, log_ref, a_out,
    *rest, launch=nothing, tick=nothing,
):
    dvq_ref, weight_ref, rest = rest[0], rest[1], rest[2:]
    k_refs, v_refs, rest = rest[:pieces], rest[pieces : 2 * pieces], rest[2 * pieces :]
    w_out, rounded, dmv, deltas, dkv, sem = rest
    rows, features = vq_ref.shape
    keys = vkv_ref.shape[0]
    part = k_refs[0].shape[0]
    (load,) = copies(sem, (a_out.at[3], w_out))
    rounded[...] = dx2_ref[...].astype(NARROW)
    load.wait()
    dmv[...] = right_t(rounded[...], w_out[...]).astype(NARROW)
    store_rows(
        weight_ref, slice(features, 2 * features), left_t(mv_ref[...], rounded[...])
    )
    deltas[...] = head_rows(dmv[...].astype(SINGLE) * mv_ref[...].astype(SINGLE))
    if dkv.shape[0] > keys:
        dkv[keys:, :] = jnp.zeros((dkv.shape[0] - keys, 2 * features), SINGLE)
    size = 256

    def pair(p):
        pl.when(p == 2)(lambda: tick(1))
        pl.when(p == 4)(lambda: tick(2))
        for strip in range(rows // size):
            span = slice(strip * size, (strip + 1) * size)

            def mask(scores):
                return jnp.where(iota(scores.shape, 0) < length_ref[0], scores, MASKED)

            dq, dk, dv = attend_back(
                vq_ref[span, at(p, PAIR)],
                vkv_ref[:, at(p, PAIR)],
                vkv_ref[:, at(p + features // PAIR, PAIR)],
                dmv[span, at(p, PAIR)],
                row_pair(log_ref, p, span),
                row_pair(deltas, p, span),
                mask,
            )
            dvq_ref[span, at(p, PAIR)] = (dq * (1.0 / math.sqrt(HEAD))).astype(NARROW)
            if strip == 0:
                dkv[0:keys, at(p, PAIR)] = dk
                dkv[0:keys, at(p + features // PAIR, PAIR)] = dv
            else:
                dkv[0:keys, at(p, PAIR)] += dk
                dkv[0:keys, at(p + features // PAIR, PAIR)] += dv

    loop(features // PAIR, pair)
    store_rows(weight_ref, slice(0, features), left_t(nx_ref[...], dvq_ref[...]))
    launch(1)
    for k in range(pieces):
        span = at(piece_at(k, pieces), part)
        k_refs[k][...] = dkv[span, 0:features].astype(NARROW)
        v_refs[k][...] = dkv[span, features:].astype(NARROW)


def cross_backward(
    pieces, share, dq2_ref, co_ref, cq_ref, ckv_ref, valid_ref, a_out, *rest
):
    log_parts, rest = rest[:pieces], rest[pieces:]
    dckv_ref, weight_ref, rest = rest[0], rest[1], rest[2:]
    q_refs, (w_out, rounded, dco, deltas, logs, turned, dq_all, dkv, sem) = (
        rest[:pieces],
        rest[pieces:],
    )
    rows, features = cq_ref.shape
    part = log_parts[0].shape[1]
    (load,) = copies(sem, (a_out.at[2], w_out))
    for k in range(pieces):
        logs[at(piece_at(k, pieces), part), :] = untwist(log_parts[k][...])
    turned[...] = turn(logs[0:rows, :])
    rounded[...] = dq2_ref[...].astype(NARROW)
    load.wait()
    dco[...] = right_t(rounded[...], w_out[...]).astype(NARROW)
    taken = right_t(
        chooser(weight_ref.shape[0], features, place_of() * share, share), co_ref[0:rows, :]
    ).astype(NARROW)
    weight_ref[...] = plain(taken, rounded[...]).astype(NARROW)
    deltas[...] = head_rows(dco[...].astype(SINGLE) * co_ref[0:rows, :].astype(SINGLE))
    if dq_all.shape[0] > rows:
        dq_all[rows:, :] = jnp.zeros((dq_all.shape[0] - rows, features), NARROW)
    edges = spans(rows, 512)

    def pair(p):
        for number, (start, end) in enumerate(edges):
            span = slice(start, end)
            dq, dk, dv = attend_back(
                cq_ref[span, at(p, PAIR)],
                ckv_ref[:, at(p, PAIR)],
                ckv_ref[:, at(p + features // PAIR, PAIR)],
                dco[span, at(p, PAIR)],
                row_pair(turned, p, span),
                row_pair(deltas, p, span),
                lambda scores: scores + valid_ref[...],
            )
            dq_all[span, at(p, PAIR)] = (dq * (1.0 / math.sqrt(HEAD))).astype(NARROW)
            if number == 0:
                dkv[:, at(p, PAIR)] = dk
                dkv[:, at(p + features // PAIR, PAIR)] = dv
            else:
                dkv[:, at(p, PAIR)] += dk
                dkv[:, at(p + features // PAIR, PAIR)] += dv

    loop(features // PAIR, pair)
    dckv_ref[...] = dkv[...].astype(NARROW)
    for k in range(pieces):
        q_refs[k][...] = dq_all[at(piece_at(k, pieces), part), :]


def patch_backward(
    x_ref, dx2_ref, x1_ref, nx_ref, n0_ref, pw_ref, mw_ref, dvq_ref, dckv_ref, gain_ref, a_in, a_out,
    kv_weight_ref, weight_ref, grad_ref, norm_ref,
    w_in, w_out, w_q, w_kv, dx1, rounded, dmw, deltas, dpw, sem,
    launch=nothing, ready=nothing, flush=nothing,
):
    rows, features = x_ref.shape
    loads = copies(
        sem,
        (a_in.at[3, :, pl.ds(0, features)], w_q),
        (a_in.at[2, :, pl.ds(features, 2 * features)], w_kv),
        (a_out.at[0], w_out),
        (a_in.at[0], w_in),
    )
    norm_ref[...] = jnp.zeros_like(norm_ref)
    for start in range(0, 2 * features, CHUNK):
        span = slice(start, start + CHUNK)
        store_rows(kv_weight_ref, span, left_t(nx_ref[...], dckv_ref[:, span]))
    launch(0)
    flush(0)
    loads[0].wait()
    loads[1].wait()

    def first(i):
        span = at(i, GROUP)
        upstream = right_t(dvq_ref[span, :], w_q[...]) + right_t(dckv_ref[span, :], w_kv[...])
        part, gain, bias = norm_back(x1_ref[span, :], gain_ref[3:4, :], upstream)
        total = dx2_ref[span, :] + part
        dx1[span, :] = total
        rounded[span, :] = total.astype(NARROW)
        norm_ref[0:1, :] += gain
        norm_ref[1:2, :] += bias

    loop(rows // GROUP, first)
    loads[2].wait()
    ready(6)
    dmw[...] = right_t(rounded[...], w_out[...]).astype(NARROW)
    store_rows(
        weight_ref, slice(3 * features, 4 * features), left_t(mw_ref[...], rounded[...])
    )
    deltas[...] = head_rows(dmw[...].astype(SINGLE) * mw_ref[...].astype(SINGLE))
    ready(5)
    window = jnp.where(
        iota((WINDOWS, WINDOWS), 0) // WIN == iota((WINDOWS, WINDOWS), 1) // WIN, 0.0, MASKED
    )

    def group(i):
        span = at(i, WINDOWS)
        for pair in range(features // PAIR):
            lane = pair * PAIR
            dq, dk, dv = attend_back(
                pw_ref[span, lane : lane + PAIR],
                pw_ref[span, features + lane : features + lane + PAIR],
                pw_ref[span, 2 * features + lane : 2 * features + lane + PAIR],
                dmw[span, lane : lane + PAIR],
                None,
                [deltas[2 * pair + w : 2 * pair + w + 1, span] for w in range(2)],
                lambda scores: scores + window,
            )
            dpw[span, lane : lane + PAIR] = (dq * (1.0 / math.sqrt(HEAD))).astype(NARROW)
            dpw[span, features + lane : features + lane + PAIR] = dk.astype(NARROW)
            dpw[span, 2 * features + lane : 2 * features + lane + PAIR] = dv.astype(NARROW)

    loop(rows // WINDOWS, group)
    ready(4)
    for start in range(0, 3 * features, CHUNK):
        span = slice(start, start + CHUNK)
        store_rows(weight_ref, span, left_t(n0_ref[...], dpw[:, span]))
    launch(1)
    flush(1)
    ready(0)
    loads[3].wait()

    def last(i):
        span = at(i, GROUP)
        upstream = right_t(dpw[span, :], w_in[...])
        part, gain, bias = norm_back(x_ref[span, :].astype(SINGLE), gain_ref[0:1, :], upstream)
        grad_ref[span, :] = dx1[span, :] + part
        norm_ref[2:3, :] += gain
        norm_ref[3:4, :] += bias

    loop(rows // GROUP, last)


def share_backward(
    pieces, q1, nq, gain_ref, a_in, *rest, launch=nothing
):
    parts = [rest[k * pieces : (k + 1) * pieces] for k in range(3)]
    rest = rest[3 * pieces :]
    grad_ref, weight_ref, norm_ref, w_q, w_kv, summed, q1_ref, nq_ref, sem = rest
    part, features = q1_ref.shape
    *loads, load_q, load_n = copies(
        sem,
        (a_in.at[2, :, pl.ds(0, features)], w_q),
        (a_in.at[3, :, pl.ds(features, 2 * features)], w_kv),
        (q1.at[at(place_of(), part), :], q1_ref),
        (nq.at[at(place_of(), part), :], nq_ref),
    )
    for k in range(3):
        span = slice(k * features, (k + 1) * features)
        total = functools.reduce(jnp.add, [one[...].astype(SINGLE) for one in parts[k]])
        summed[:, span] = total.astype(NARROW)
    for load in loads:
        load.wait()
    upstream = right_t(summed[:, 0:features], w_q[...]) + right_t(summed[:, features:], w_kv[...])
    load_q.wait()
    piece, gain, bias = norm_back(q1_ref[...], gain_ref[2:3, :], upstream)
    grad_ref[...] = piece.astype(NARROW)
    launch(0)
    load_n.wait()
    for k in range(3):
        span = slice(k * features, (k + 1) * features)
        store_rows(weight_ref, span, left_t(nq_ref[...], summed[:, span]))
    launch(1)
    norm_ref[...] = jnp.zeros_like(norm_ref)
    norm_ref[0:1, :] = gain
    norm_ref[1:2, :] = bias


def causal_backward(
    pieces, share, q_ref, dq2_ref, n1_ref, pq_ref, mq_ref, log_ref, cross_ref, gain_ref,
    a_in, a_out, *rest, ready=nothing
):
    parts, rest = rest[: 2 * pieces - 1], rest[2 * pieces - 1 :]
    (
        weight_ref, grad_ref, norm_ref,
        w_in, w_out, gathered, dq1, rounded, dmq, deltas, dkv, dpq, sem,
    ) = rest
    rows, features = q_ref.shape
    placed = place_parts(gathered, pieces, parts, sem)
    loads = copies(sem.at[pl.ds(len(placed), 2)], (a_out.at[1], w_out), (a_in.at[1], w_in))
    for one in placed:
        one.wait()

    def first(i):
        span = at(i, STRIP)
        total = dq2_ref[span, :] + gathered[span, :].astype(SINGLE)
        dq1[span, :] = total
        rounded[span, :] = total.astype(NARROW)

    loop(rows // STRIP, first)
    loads[0].wait()
    dmq[...] = right_t(rounded[...], w_out[...]).astype(NARROW)
    ready(4)
    chosen = chooser(weight_ref.shape[0], features, place_of() * share, share)
    taken = right_t(chosen, mq_ref[...]).astype(NARROW)
    weight_ref[:, 3 * features : 4 * features] = plain(taken, rounded[...]).astype(NARROW)
    weight_ref[:, 4 * features : 5 * features] = cross_ref[...]
    weight_ref[:, 5 * features :] = jnp.zeros_like(weight_ref[:, 5 * features :])
    deltas[...] = head_rows(dmq[...].astype(SINGLE) * mq_ref[...].astype(SINGLE))
    edges = spans(rows, 256)
    ready(3)
    ready(5)

    def pair(p):
        for number, (start, end) in reversed(list(enumerate(edges))):
            span = slice(start, end)

            def mask(scores, start=start):
                shape = scores.shape
                return jnp.where(iota(shape, 0) <= iota(shape, 1) + start, scores, MASKED)

            dq, dk, dv = attend_back(
                pq_ref[span, at(p, PAIR)],
                pq_ref[0:end, at(p + features // PAIR, PAIR)],
                pq_ref[0:end, at(p + 2 * features // PAIR, PAIR)],
                dmq[span, at(p, PAIR)],
                row_pair(log_ref, p, span),
                row_pair(deltas, p, span),
                mask,
            )
            dpq[span, at(p, PAIR)] = (dq * (1.0 / math.sqrt(HEAD))).astype(NARROW)
            if end == rows:
                dkv[0:end, 0:PAIR] = dk
                dkv[0:end, PAIR:] = dv
            else:
                dkv[0:end, 0:PAIR] += dk
                dkv[0:end, PAIR:] += dv
        dpq[:, at(p + features // PAIR, PAIR)] = dkv[:, 0:PAIR].astype(NARROW)
        dpq[:, at(p + 2 * features // PAIR, PAIR)] = dkv[:, PAIR:].astype(NARROW)

    loop(features // PAIR, pair)
    ready(2)
    taken = right_t(chosen, n1_ref[...]).astype(NARROW)
    weight_ref[:, 0 : 3 * features] = plain(taken, dpq[...]).astype(NARROW)
    loads[1].wait()
    norm_ref[...] = jnp.zeros_like(norm_ref)

    def last(i):
        span = at(i, STRIP)
        upstream = right_t(dpq[span, :], w_in[...])
        piece, gain, bias = norm_back(q_ref[span, :].astype(SINGLE), gain_ref[1:2, :], upstream)
        grad_ref[span, :] = dq1[span, :] + piece
        norm_ref[0:1, :] += gain
        norm_ref[1:2, :] += bias

    loop(rows // STRIP, last)


def assemble(pairs, quarters, count, *refs, ready=nothing, flush=nothing):
    parts, refs = refs[: 4 * (pairs + quarters)], refs[4 * (pairs + quarters) :]
    norms, refs = refs[:count], refs[count:]
    in_ref, out_ref, up_ref, down_ref, gain_ref, bias_ref, share, causal = refs
    features = down_ref.shape[2]
    rep = place_of("rep")

    def corners(number, write):
        for k in range(4):
            ready(4 * number + k)
            owner = flipped(rep, k, 4)
            piece = parts[4 * number + k][...]
            height, width = piece.shape
            write(
                pl.ds(pl.multiple_of((owner % 2) * height, height), height),
                pl.multiple_of((owner // 2) * width, width), width, piece,
            )

    def into(ref, index, start=0):
        def write(rows, column, width, piece):
            ref[index, rows, pl.ds(column + start, width)] = piece

        return write

    up_x, down_x, reverse, window, kv, shared, up_q, down_q, rest = range(pairs + quarters)

    def quarter(number, write):
        for k in range(4):
            ready(4 * number + k)
            piece = parts[4 * number + k][...]
            write(flipped(rep, k, 4), piece)

    def up_part(owner, piece):
        up_ref[1, :, at(owner, piece.shape[1])] = piece

    def down_part(owner, piece):
        down_ref[1, at(owner, piece.shape[0]), :] = piece

    def causal_part(owner, piece):
        causal[:, at(owner, piece.shape[1])] = piece

    def keep_share(rows, column, width, piece):
        share[rows, pl.ds(column, width)] = piece

    quarter(up_q, up_part)
    quarter(down_q, down_part)
    corners(up_x, into(up_ref, 0))
    flush(2)
    corners(down_x, into(down_ref, 0))
    flush(3)
    first = 4 * (pairs + quarters)
    for k in range(count):
        ready(first + k)
    terms = [norms[0][place_of()]] + [one[...] for one in norms[1:]]
    total = functools.reduce(jnp.add, terms)
    columns = gain_ref.shape[1]
    gain_ref[...] = total[0:6, 0:columns]
    bias_ref[...] = total[8:14, 0:columns]
    flush(4)
    flush(5)
    quarter(rest, causal_part)
    in_ref[1, :, :] = causal[:, 0 : 3 * features]
    out_ref[1, :, :] = causal[:, 3 * features : 4 * features]
    out_ref[2, :, :] = causal[:, 4 * features : 5 * features]
    corners(reverse, keep_share)
    in_ref[3, :, 0:features] = share[:, 0:features]
    out_ref[3, :, :] = share[:, features : 2 * features]
    corners(window, keep_share)
    in_ref[0, :, :] = share[:, 0 : 3 * features]
    out_ref[0, :, :] = share[:, 3 * features :]
    flush(1)
    corners(kv, into(in_ref, 2, features))
    corners(shared, keep_share)
    in_ref[2, :, 0:features] = share[:, 0:features]
    in_ref[3, :, features:] = share[:, features : 3 * features]
    flush(0)


def bits_of(count):
    return max(count - 1, 0).bit_length()


def swap(tensor, axis, mask):
    return lax.ppermute(tensor, axis, [(i, i ^ mask) for i in range(lax.axis_size(axis))])


def pick(tensor, place, dim):
    return lax.dynamic_index_in_dim(tensor, place, dim, keepdims=False)


def fold(tensor, axis, bit, dim):
    own = (lax.axis_index(axis) >> bit) & 1
    arrived = swap(pick(tensor, 1 - own, dim).astype(NARROW), axis, 1 << bit)
    return pick(tensor, own, dim).astype(SINGLE) + arrived.astype(SINGLE)


def unfold(tensor, axis, bit, dim):
    own = (lax.axis_index(axis) >> bit) & 1
    arrived = swap(tensor, axis, 1 << bit)
    return jnp.where(
        own == 0,
        jnp.stack((tensor, arrived), axis=dim),
        jnp.stack((arrived, tensor), axis=dim),
    )


def scatter_blk(tensor):
    bits = bits_of(lax.axis_size("blk"))
    tensor = tensor.reshape((2,) * bits + tensor.shape[1:])
    for bit in range(bits):
        tensor = fold(tensor, "blk", bit, bits - 1 - bit)
    return tensor


def sum_rep_scatter(tensor, dim):
    bits = bits_of(lax.axis_size("rep"))
    shape = tensor.shape
    tensor = tensor.reshape(
        shape[:dim] + (2,) * bits + (shape[dim] // 2**bits,) + shape[dim + 1 :]
    )
    for bit in range(bits):
        tensor = fold(tensor, "rep", bit, dim)
    return tensor


def gather_rep(tensor, dim):
    bits = bits_of(lax.axis_size("rep"))
    for bit in reversed(range(bits)):
        tensor = unfold(tensor, "rep", bit, dim)
    shape = tensor.shape
    return tensor.reshape(shape[:dim] + (-1,) + shape[dim + bits + 1 :])


def reduce_all(tensor):
    count = lax.axis_size("blk")
    tensor = tensor.reshape(count, tensor.shape[0] // count, tensor.shape[1])
    tensor = sum_rep_scatter(tensor, 1)
    tensor = scatter_blk(tensor).astype(NARROW)
    return gather_rep(tensor, 0)


def reduce_rep(tensor):
    return gather_rep(sum_rep_scatter(tensor, 0).astype(NARROW), 0)


def exchange(pieces):
    whole = lax.all_to_all(jnp.stack(pieces), "blk", 0, 0)
    return [whole[k] for k in range(len(pieces))]


def gather(tensor):
    count = lax.axis_size("blk")
    whole = lax.all_gather(tensor, "blk")
    return [whole[k] for k in range(count)]


def whole(ref):
    return ref


class Fold:
    def __init__(self, own, take, arrived, shape, keep=whole, keep_shape=None):
        self.own, self.take, self.arrived, self.shape = own, take, arrived, shape
        self.keep, self.keep_shape = keep, keep_shape or shape
        self.dtype = own.dtype


class Move:
    late = None

    def __init__(self, source, shape, axis, flip, take=whole, phase=0):
        self.source, self.shape, self.axis, self.flip, self.take = source, shape, axis, flip, take
        self.phase = phase
        self.dtype = source.dtype


def lanes_of(ref, start, width):
    return ref.at[(slice(None),) * (len(ref.shape) - 1) + (pl.ds(start, width),)]


class Reduction:
    def __init__(self, tensor):
        if len(tensor.shape) == 2:
            blocks = lax.axis_size("blk")
            height = tensor.shape[0] // blocks
            tensor = tensor.reshape(blocks // 2, 2, 2, height // 2, tensor.shape[1])
        self.tensor, self.take, self.arrived, self.shape = tensor, whole, [], tensor.shape

    def fold(self, keep=whole, keep_shape=None):
        return Fold(self.tensor, self.take, self.arrived, self.shape, keep, keep_shape)

    def moves(self, stage):
        shape = self.shape
        if stage == "core":
            self.next = shape[:2] + shape[3:]
            return [
                Move(self.tensor, self.next, "rep", 1,
                     lambda ref: ref.at[:, :, 1 - place_of("rep") % 2])
            ]
        if stage == "x":
            width = shape[-1] // 2
            self.next = shape[:-1] + (width,)

            def own(ref):
                return lanes_of(ref, pl.multiple_of((place_of("rep") // 2) * width, width), width)

            def other(ref):
                start = (1 - place_of("rep") // 2) * width
                return lanes_of(ref, pl.multiple_of(start, width), width)

            return [Move(self.fold(own, self.next), self.next, "rep", 2, other)]
        if stage == "y":
            self.next = shape[:1] + shape[2:]
            fold = self.fold(lambda ref: ref.at[:, place_of() % 2], self.next)
            return [Move(fold, self.next, "blk", 1, lambda ref: ref.at[:, 1 - place_of() % 2])]
        if stage == "z":
            length = shape[0]
            self.next = shape[1:]
            fold = self.fold(lambda ref: ref.at[place_of() // 2], self.next)
            return [
                Move(fold, self.next, "blk", 2 * k,
                     lambda ref, k=k: ref.at[flipped(place_of() // 2, k, length)])
                for k in range(1, length)
            ]
        if stage == "back":
            fold = self.fold()
            return [Move(fold, shape, "rep", k) for k in range(1, 4)]
        if stage == "back_x":
            return [Move(self.fold(), shape, "rep", 2)]
        return [Move(self.tensor, shape, "rep", 1), Move(self.other, shape, "rep", 1)]

    def absorb(self, stage, arrived, kept):
        if stage == "core":
            self.take = lambda ref: ref.at[:, :, place_of("rep") % 2]
        else:
            self.take = whole
        if kept:
            self.tensor = kept[0]
        if stage in ("back", "back_x", "back_core"):
            if stage == "back_x":
                self.other = arrived[0]
                return
            if stage == "back":
                self.result = [self.tensor] + list(arrived)
            else:
                self.result = [self.tensor, arrived[0], self.other, arrived[1]]
            return
        self.shape, self.arrived = self.next, list(arrived)


class RepSum:
    def __init__(self, tensor, dim):
        self.tensor, self.dim = tensor, dim

    def moves(self, stage):
        if stage == "out":
            self.shape = list(self.tensor.shape)
            size = self.shape[self.dim] = self.shape[self.dim] // 4

            def quarter(ref, k):
                span = pl.ds(pl.multiple_of(flipped(place_of("rep"), k, 4) * size, size), size)
                return ref.at[span, :] if self.dim == 0 else ref.at[:, span]

            self.quarter = quarter
            return [
                Move(self.tensor, tuple(self.shape), "rep", k, lambda ref, k=k: quarter(ref, k))
                for k in range(1, 4)
            ]
        fold = Fold(
            self.tensor, lambda ref: self.quarter(ref, 0), self.arrived, tuple(self.shape)
        )
        return [Move(fold, tuple(self.shape), "rep", k) for k in range(1, 4)]

    def absorb(self, stage, arrived, kept):
        if stage == "out":
            self.arrived = list(arrived)
            return
        self.result = [kept[0]] + list(arrived)


class Exchange:
    def __init__(self, pieces):
        self.pieces = pieces

    def moves(self, stage):
        return [Move(one, one.shape, "blk", k) for k, one in enumerate(self.pieces) if k]

    def absorb(self, stage, arrived, kept):
        self.result = self.pieces[:1] + list(arrived)


class Pieces:
    def __init__(self, tensor, part, start, width):
        self.tensor, self.part, self.start, self.width = tensor, part, start, width

    def moves(self, stage):
        part, span = self.part, slice(self.start, self.start + self.width)
        count = lax.axis_size("blk")
        return [
            Move(self.tensor, (part, self.width), "blk", k,
                 lambda ref, k=k: ref.at[at(flipped(place_of(), k, count), part), span])
            for k in range(1, count)
        ]

    def absorb(self, stage, arrived, kept):
        self.result = list(arrived)


class Gather:
    def __init__(self, tensor):
        self.tensor = tensor

    def moves(self, stage):
        return [
            Move(self.tensor, self.tensor.shape, "blk", k) for k in range(1, lax.axis_size("blk"))
        ]

    def absorb(self, stage, arrived, kept):
        self.result = [self.tensor] + list(arrived)


class Spread:
    def __init__(self, tensor):
        self.tensor = tensor

    def moves(self, stage):
        count = lax.axis_size("blk")
        rows, width = self.tensor.shape[0], self.tensor.shape[1] // 2
        moves, self.places = [], []
        for number in range(2):
            span = slice(number * width, (number + 1) * width)
            own = lambda ref, span=span: ref.at[:, span]
            along = []
            for k in range(2, count, 2):
                along.append(Move(self.tensor, (rows, width), "blk", k, own, number))
                self.places.append((number, k))
            moves += along
            moves.append(Move(self.tensor, (rows, width), "blk", 1, own, number + 1))
            self.places.append((number, 1))
            for one in along:
                moves.append(Move(one, (rows, width), "blk", 1, whole, number + 1))
                self.places.append((number, one.flip + 1))
        return moves

    def absorb(self, stage, arrived, kept):
        found = dict(zip(self.places, arrived))
        count = lax.axis_size("blk")
        self.result = [found[number, k] for number in range(2) for k in range(1, count)]


class Norms:
    def __init__(self, tensor):
        self.tensor = tensor

    def moves(self, stage):
        axis = "rep" if stage == "out" else "blk"
        count = lax.axis_size(axis)
        shape = self.tensor.shape
        if stage == "out":
            return [Move(self.tensor, shape, axis, k) for k in range(1, count)]
        fold = Fold(self.tensor, whole, self.arrived, shape)
        return [
            Move(fold, shape[1:], axis, k,
                 lambda ref, k=k: ref.at[flipped(place_of(), k, count)])
            for k in range(1, count)
        ]

    def absorb(self, stage, arrived, kept):
        if stage == "out":
            self.arrived = list(arrived)
        else:
            self.result = [kept[0]] + list(arrived)


VMEM = pl.BlockSpec(memory_space=pltpu.VMEM)
SMEM = pl.BlockSpec(memory_space=pltpu.SMEM)
ANY = pl.BlockSpec(memory_space=pl.ANY)


def like(*shape, kind=NARROW):
    return jax.ShapeDtypeStruct(shape, kind)


def index_of(items, item):
    return next(k for k, one in enumerate(items) if one is item)


def call(
    kernel, outs, operands, specs, scratch, flops, grid=None, out_specs=None, semaphores=0,
    moves=(), ident=None, ticking=False, lazy=(), early=(),
):
    scratch = [pltpu.VMEM(shape, kind) for shape, kind in scratch]
    if semaphores:
        scratch.append(pltpu.SemaphoreType.DMA((semaphores,)))
    out_specs = [VMEM] * len(outs) if out_specs is None else out_specs
    extra = {} if grid is None else {"grid": grid}
    params = {}
    sources, folds = [], []

    def need(array):
        if not any(array is one for one in sources):
            sources.append(array)

    for move in moves:
        if isinstance(move.source, Fold):
            if not any(move.source is one for one in folds):
                folds.append(move.source)
                for array in [move.source.own] + move.source.arrived:
                    need(array)
        elif move.late is None and not isinstance(move.source, Move):
            need(move.source)
    fixed_in, fixed_out = len(operands), len(outs)
    partners = sorted({(move.axis, move.flip) for move in moves})
    lasts = max([move.phase for move in moves], default=0)
    held_in = [k for k, spec in enumerate(specs) if spec is VMEM]
    held_out = [k for k, spec in enumerate(out_specs) if spec is VMEM]
    own_scratch = len(scratch)
    scratch += [pltpu.VMEM(operands[k].shape, operands[k].dtype) for k in held_in]
    scratch += [pltpu.VMEM(outs[k].shape, outs[k].dtype) for k in held_out]
    terms = sum(1 + len(fold.arrived) for fold in folds)
    for fold in folds:
        scratch += [pltpu.VMEM(fold.shape, NARROW)] * (1 + len(fold.arrived))
    for number in (len(held_in), len(held_out), terms, len(folds), len(moves), len(moves)):
        scratch.append(pltpu.SemaphoreType.DMA((max(number, 1),)))
    if moves:
        params = {"collective_id": ident, "has_side_effects": True}
    before = {}
    for move in moves:
        if isinstance(move.source, Move):
            number = index_of(moves, move.source)
            before[number] = min(move.phase, before.get(number, move.phase))

    def body_kernel(*refs):
        ins, refs = list(refs[:fixed_in]), refs[fixed_in:]
        sent, refs = refs[: len(sources)], refs[len(sources) :]
        results, refs = list(refs[:fixed_out]), refs[fixed_out:]
        landed, refs = refs[: len(moves)], refs[len(moves) :]
        kept, refs = refs[: len(folds)], refs[len(folds) :]
        rest, refs = refs[:own_scratch], refs[own_scratch:]
        inner, refs = refs[: len(held_in)], refs[len(held_in) :]
        outer, refs = refs[: len(held_out)], refs[len(held_out) :]
        buffers, (in_sem, out_sem, load_sem, keep_sem, send_sem, recv_sem) = refs[:terms], refs[terms:]
        fetches, stores = {}, {}
        for number, k in enumerate(held_in):
            fetches[k] = pltpu.make_async_copy(ins[k], inner[number], in_sem.at[number])
            ins[k] = inner[number]
        for number, k in enumerate(held_out):
            stores[k] = pltpu.make_async_copy(outer[number], results[k], out_sem.at[number])
            results[k] = outer[number]

        def target(axis, flip):
            return {axis: flipped(lax.axis_index(axis), flip, lax.axis_size(axis))}

        def buffers_of(fold):
            start = sum(1 + len(one.arrived) for one in folds[: index_of(folds, fold)])
            return start, buffers[start : start + 1 + len(fold.arrived)]

        def made(k):
            move = moves[k]
            if move.late is not None:
                source = results[move.late]
            elif isinstance(move.source, Fold):
                source = buffers_of(move.source)[1][0]
            elif isinstance(move.source, Move):
                source = landed[index_of(moves, move.source)]
            else:
                source = sent[index_of(sources, move.source)]
            return pltpu.make_async_remote_copy(
                src_ref=move.take(source),
                dst_ref=landed[k],
                send_sem=send_sem.at[k],
                recv_sem=recv_sem.at[k],
                device_id=target(move.axis, move.flip),
                device_id_type=pl.DeviceIdType.MESH,
            )

        def loads(fold):
            start, held = buffers_of(fold)
            return [
                pltpu.make_async_copy(
                    (fold.take if k == 0 else whole)(sent[index_of(sources, array)]),
                    held[k],
                    load_sem.at[start + k],
                )
                for k, array in enumerate([fold.own] + fold.arrived)
            ]

        def keeping(k):
            fold = folds[k]
            return pltpu.make_async_copy(
                fold.keep(buffers_of(fold)[1][0]), kept[k], keep_sem.at[k]
            )

        def add(fold):
            held = buffers_of(fold)[1]

            def one(index):
                if len(held) == 2:
                    held[0][index] = held[0][index] + held[1][index]
                elif len(held) > 2:
                    held[0][index] = functools.reduce(
                        jnp.add, [part[index].astype(SINGLE) for part in held]
                    ).astype(NARROW)

            if len(fold.shape) == 2:
                one((slice(None), slice(None)))
            else:
                loop(fold.shape[0], one)

        def begin():
            for fold in folds:
                for load in loads(fold):
                    load.start()
            for fetch in fetches.values():
                fetch.start()
            if moves:
                barrier = pltpu.get_barrier_semaphore()
                for axis, flip in partners:
                    pl.semaphore_signal(
                        barrier, inc=1, device_id=target(axis, flip),
                        device_id_type=pl.DeviceIdType.MESH,
                    )
                pl.semaphore_wait(barrier, len(partners))
            for k, move in enumerate(moves):
                if move.phase == 0 and move.late is None and not isinstance(move.source, Fold):
                    made(k).start()
            for number, fold in enumerate(folds):
                for load in loads(fold):
                    load.wait()
                add(fold)
                for k, move in enumerate(moves):
                    if move.source is fold:
                        made(k).start()
                keeping(number).start()
            for k, fetch in fetches.items():
                if k not in lazy:
                    fetch.wait()

        def launch(which):
            for k in range(len(moves)):
                if moves[k].late == which and moves[k].phase == 0:
                    made(k).start()

        def tick(phase):
            for k, needed in before.items():
                if needed == phase:
                    made(k).wait_recv()
            for k, move in enumerate(moves):
                if move.phase == phase:
                    made(k).start()

        def finish():
            for k, store in stores.items():
                if k not in early:
                    store.start()
            if not ticking:
                for phase in range(1, lasts + 1):
                    tick(phase)
            for k in range(len(moves)):
                made(k).wait_send()
                if k not in before:
                    made(k).wait_recv()
            for k in range(len(folds)):
                keeping(k).wait()
            for store in stores.values():
                store.wait()

        options = {}
        if any(move.late is not None for move in moves):
            options["launch"] = launch
        if ticking:
            options["tick"] = tick
        if lazy:
            options["ready"] = lambda k: fetches[k].wait()
        if early:
            options["flush"] = lambda k: stores[k].start()
        if grid is None:
            begin()
            kernel(*ins, *results, *rest, **options)
            finish()
        else:
            pl.when(pl.program_id(0) == 0)(begin)
            kernel(*ins, *results, *rest, **options)
            pl.when(pl.program_id(0) == pl.num_programs(0) - 1)(finish)

    result = pl.pallas_call(
        body_kernel,
        out_shape=list(outs)
        + [
            like(*m.shape, kind=m.dtype)
            for m in moves
        ]
        + [like(*fold.keep_shape) for fold in folds],
        in_specs=[ANY if spec is VMEM else spec for spec in specs] + [ANY] * len(sources),
        out_specs=[ANY if spec is VMEM else spec for spec in out_specs]
        + [ANY] * (len(moves) + len(folds)),
        scratch_shapes=scratch,
        compiler_params=pltpu.CompilerParams(vmem_limit_bytes=60 * 2**20, **params),
        cost_estimate=pl.CostEstimate(
            flops=int(flops),
            bytes_accessed=sum(o.size * o.dtype.itemsize for o in operands),
            transcendentals=0,
        ),
        **extra,
    )(*operands, *sources)
    end = fixed_out + len(moves)
    return list(result[:fixed_out]), list(result[fixed_out:end]), (folds, list(result[end:]))


def finale(kernel, outs, stages, results, scratch, ident):
    plan = []
    for stage in stages:
        for job, name in stage:
            moves = job.moves(name)
            folds = []
            for move in moves:
                known = folds + [fold for part, _ in plan for fold in part]
                if isinstance(move.source, Fold) and not any(move.source is one for one in known):
                    folds.append(move.source)
            job.absorb(name, moves, folds)
            plan.append((folds, moves))
    items = results()
    moves = [move for _, part in plan for move in part]
    folds = [fold for part, _ in plan for fold in part]
    sources, fetched = [], []

    def need(item):
        if not isinstance(item, (Fold, Move)) and not any(item is one for one in sources):
            sources.append(item)

    for fold in folds:
        for item in [fold.own] + fold.arrived:
            need(item)
            if not isinstance(item, (Fold, Move)):
                fetched.append((fold, item))
    for move in moves:
        need(move.source)
    plain_items = []
    for item in items:
        need(item)
        if not isinstance(item, (Fold, Move)):
            plain_items.append(item)
    partners = sorted({(move.axis, move.flip) for move in moves})
    shapes = [pltpu.VMEM(one.shape, one.dtype) for one in scratch]
    shapes += [pltpu.VMEM(move.shape, move.dtype) for move in moves]
    shapes += [pltpu.VMEM(fold.shape, fold.dtype) for fold in folds]
    shapes += [pltpu.VMEM(fold.shape, fold.dtype) for fold, _ in fetched]
    shapes += [pltpu.VMEM(item.shape, item.dtype) for item in plain_items]
    shapes += [pltpu.VMEM(one.shape, one.dtype) for one in outs]
    for number in (len(moves), len(moves), len(fetched), len(plain_items), len(outs)):
        shapes.append(pltpu.SemaphoreType.DMA((max(number, 1),)))

    def body_kernel(*refs):
        def take(count):
            nonlocal refs
            some, refs = refs[:count], refs[count:]
            return some

        sent, finals = take(len(sources)), take(len(outs))
        rest, landed, sums = take(len(scratch)), take(len(moves)), take(len(folds))
        brought, held, outer = take(len(fetched)), take(len(plain_items)), take(len(outs))
        send_sem, recv_sem, load_sem, item_sem, out_sem = refs
        arrived = set()

        def target(axis, flip):
            return {axis: flipped(lax.axis_index(axis), flip, lax.axis_size(axis))}

        def place(item):
            if isinstance(item, Fold):
                return sums[index_of(folds, item)]
            if isinstance(item, Move):
                return landed[index_of(moves, item)]
            return sent[index_of(sources, item)]

        def made(move):
            k = index_of(moves, move)
            source = place(move.source)
            return pltpu.make_async_remote_copy(
                src_ref=move.take(source),
                dst_ref=landed[k],
                send_sem=send_sem.at[k],
                recv_sem=recv_sem.at[k],
                device_id=target(move.axis, move.flip),
                device_id_type=pl.DeviceIdType.MESH,
            )

        def arrival(item):
            if isinstance(item, Move) and index_of(moves, item) not in arrived:
                arrived.add(index_of(moves, item))
                made(item).wait_recv()

        loads = [
            pltpu.make_async_copy(
                (fold.take if item is fold.own else whole)(place(item)), brought[k], load_sem.at[k]
            )
            for k, (fold, item) in enumerate(fetched)
        ]
        fetches = [
            pltpu.make_async_copy(place(item), held[k], item_sem.at[k])
            for k, item in enumerate(plain_items)
        ]
        stores = [
            pltpu.make_async_copy(outer[k], finals[k], out_sem.at[k]) for k in range(len(outs))
        ]
        for load in loads:
            load.start()
        barrier = pltpu.get_barrier_semaphore()
        for axis, flip in partners:
            pl.semaphore_signal(
                barrier, inc=1, device_id=target(axis, flip), device_id_type=pl.DeviceIdType.MESH
            )
        pl.semaphore_wait(barrier, len(partners))

        def total(fold):
            terms = []
            for item in [fold.own] + fold.arrived:
                if isinstance(item, (Fold, Move)):
                    arrival(item)
                    term = place(item)
                    if item is fold.own:
                        term = fold.take(item.keep(term) if isinstance(item, Fold) else term)
                else:
                    k = next(
                        k for k, (one, other) in enumerate(fetched) if one is fold and other is item
                    )
                    loads[k].wait()
                    term = brought[k]
                terms.append(term)
            goal = place(fold)

            def one(index):
                goal[index] = functools.reduce(
                    jnp.add, [term[index].astype(SINGLE) for term in terms]
                ).astype(goal.dtype)

            if len(fold.shape) == 2:
                one((slice(None), slice(None)))
            else:
                loop(fold.shape[0], one)

        for number, (some, part) in enumerate(plan):
            for fold in some:
                total(fold)
            for move in part:
                arrival(move.source)
                made(move).start()
            if number == 0:
                for fetch in fetches:
                    fetch.start()
        operands = []
        for item in items:
            if isinstance(item, (Fold, Move)):
                operands.append(place(item))
            else:
                operands.append(held[next(k for k, one in enumerate(plain_items) if one is item)])
        for fetch in fetches:
            fetch.wait()

        def ready(k):
            arrival(items[k])

        kernel(*operands, *outer, *rest, ready=ready, flush=lambda k: stores[k].start())
        for move in moves:
            made(move).wait_send()
            arrival(move)
        for store in stores:
            store.wait()

    return pl.pallas_call(
        body_kernel,
        out_shape=list(outs),
        in_specs=[ANY] * len(sources),
        out_specs=[ANY] * len(outs),
        scratch_shapes=shapes,
        compiler_params=pltpu.CompilerParams(
            vmem_limit_bytes=60 * 2**20, collective_id=ident, has_side_effects=True
        ),
    )(*sources)


class Courier:
    def __init__(self, active):
        self.active, self.waiting, self.ident = active, [], 0

    def load(self, *jobs):
        self.waiting += jobs

    def run(self, kernel, outs, operands, specs, scratch, flops, **extra):
        jobs, self.waiting = self.waiting, []
        moves, ends = [], []
        for job, stage, *late in jobs:
            added = job.moves(stage)
            for move in added:
                if late and not isinstance(move.source, Move):
                    move.late = late[0]
            moves += added
            ends.append(len(moves))
        if moves:
            self.ident += 1
        results, arrived, (folds, kept) = call(
            kernel, outs, operands, specs, scratch, flops, moves=tuple(moves), ident=self.ident, **extra
        )
        start = 0
        for (job, stage, *late), end in zip(jobs, ends):
            if late:
                job.tensor = results[late[0]]
            own = [
                kept[k]
                for k, fold in enumerate(folds)
                if any(move.source is fold for move in moves[start:end])
            ]
            job.absorb(stage, arrived[start:end], own)
            start = end
        return results


def in_halves(arrays):
    width = arrays[0].shape[1] // 2
    return (
        arrays[:1] + [one[:, :width] for one in arrays[1:]] + [one[:, width:] for one in arrays[1:]]
    )


def body(
    patches,
    queries,
    window_valid,
    answer_length,
    norm_gain,
    norm_bias,
    attn_in,
    attn_out,
    mlp_in,
    mlp_out,
    cot_patches,
    cot_queries,
):
    x, q, cot_x, cot_q = patches[0], queries[0], cot_patches[0], cot_queries[0]
    rows, features = x.shape
    count = q.shape[0]
    hidden = mlp_in.shape[2]
    blocks = lax.axis_size("blk")
    place = lax.axis_index("blk").astype(jnp.int32)
    share = features // blocks
    hidden_share = hidden // blocks
    share_rows = -(-share // 16) * 16
    hidden_rows = -(-hidden_share // 16) * 16
    part = -(-count // (blocks * 16)) * 16
    padded = part * blocks
    wide = 3 * features
    last = wide + features + features
    causal_columns = -(-last // 512) * 512
    leader = (place == 0).astype(SINGLE)
    valid = jnp.where(jnp.repeat(window_valid[0], WIN) > 0, 0.0, MASKED).astype(SINGLE)
    carried = blocks == DIRECT and lax.axis_size("rep") == 4 and share % 32 == 0
    courier = Courier(carried)

    def own_columns(tensor):
        return lax.dynamic_slice_in_dim(tensor, place * share, share, 1)

    square = 2.0 * features * features
    run = courier.run

    n0, pw, mw, x1, nx, vq, ckv = run(
        window_forward,
        [
            like(rows, features), like(rows, wide), like(rows, features),
            like(rows, features, kind=SINGLE), like(rows, features), like(rows, features),
            like(rows, 2 * features),
        ],
        [x, norm_gain, norm_bias, attn_in, attn_out],
        [VMEM, VMEM, VMEM, ANY, ANY],
        [((features, wide), NARROW), ((features, features), NARROW),
         ((features, features), NARROW), ((features, 2 * features), NARROW)],
        rows * square * 9,
        semaphores=4,
        early=(0, 1, 2, 3, 4, 5),
    )
    n1, pq, mq, q1, nq, cq, vkv, log_q = run(
        causal_forward,
        [
            like(count, features), like(count, wide), like(count, features),
            like(padded, features, kind=SINGLE), like(padded, features), like(count, features),
            like(count, 2 * features), like(16, count, kind=SINGLE),
        ],
        [q, norm_gain, norm_bias, attn_in, attn_out],
        [VMEM, VMEM, VMEM, ANY, ANY],
        [((features, wide), NARROW), ((features, features), NARROW),
         ((features, features), NARROW), ((features, 2 * features), NARROW),
         ((count, PAIR), SINGLE)],
        count * square * 15,
        semaphores=4,
        early=(0, 1, 2, 3, 4, 5),
    )
    outs, *log_pieces = run(
        functools.partial(cross_forward, blocks),
        [like(padded, features)] + [like(16, part, kind=SINGLE)] * blocks,
        [cq, ckv, valid[None, :]],
        [VMEM, VMEM, VMEM],
        [((padded, PAIR), SINGLE)],
        count * square * 6,
    )
    logs = Exchange(log_pieces)
    halves = [Pieces(outs, part, k * features // 2, features // 2) for k in range(2)]
    if carried:
        courier.load((logs, ""), (halves[0], ""))
    mv, x2, log_v = run(
        reverse_forward,
        [like(rows, features), like(rows, features, kind=SINGLE), like(16, rows, kind=SINGLE)],
        [answer_length, vq, vkv, x1, attn_out],
        [SMEM, VMEM, VMEM, VMEM, ANY],
        [((features, features), NARROW), ((rows, PAIR), SINGLE)],
        rows * square * 8,
        semaphores=1,
    )
    if carried:
        courier.load((halves[1], ""))
    x3, dx2, up_x, down_x, norm_five = run(
        patch_feed_forward,
        [
            like(rows, features), like(rows, features, kind=SINGLE), like(features, hidden),
            like(hidden, features), like(8, features, kind=SINGLE),
        ],
        [x2, cot_x, norm_gain, norm_bias, mlp_in, mlp_out],
        [
            VMEM, VMEM, VMEM, VMEM,
            pl.BlockSpec((1, features, CHUNK), lambda j: (0, 0, j)),
            pl.BlockSpec((1, CHUNK, features), lambda j: (0, j, 0)),
        ],
        [((rows, features), NARROW), ((rows, CHUNK), NARROW), ((rows, CHUNK), NARROW),
         ((rows, features), SINGLE), ((rows, features), SINGLE)],
        rows * square * 24,
        grid=(hidden // CHUNK,),
        out_specs=[
            VMEM, VMEM,
            pl.BlockSpec((features, CHUNK), lambda j: (0, j)),
            pl.BlockSpec((CHUNK, features), lambda j: (j, 0)),
            VMEM,
        ],
    )
    if carried:
        merged = run(
            functools.partial(merge_blocks, blocks),
            [like(part, features), like(16, part, kind=SINGLE)],
            [outs] + logs.result + halves[0].result + halves[1].result,
            [VMEM] * (3 * blocks - 1),
            [],
            padded * square,
        )
        co_parts, log_parts = Spread(merged[0]), Gather(merged[1])
        up_x, down_x = Reduction(up_x), Reduction(down_x)
        reverse_weight = Reduction(like(blocks // 2, 2, 2, share // 2, 2 * features))
        courier.load(
            (co_parts, ""), (log_parts, ""), (up_x, "core"), (down_x, "core"),
            (reverse_weight, "core", 1),
        )
    else:
        whole_logs = jnp.stack(exchange(log_pieces))
        merged_log = jax.nn.logsumexp(whole_logs, axis=0)
        weights = jnp.transpose(jnp.exp(whole_logs - merged_log)[:, :HEADS], (0, 2, 1))
        shares = lax.all_to_all(outs.reshape(blocks, part, features), "blk", 0, 0)
        merged_out = jnp.sum(jnp.repeat(weights, HEAD, axis=2) * shares.astype(SINGLE), axis=0)
        co_parts, log_parts = Spread(None), Gather(None)
        co_parts.tensor, *co_parts.result = in_halves(gather(merged_out.astype(NARROW)))
        log_parts.result = gather(merged_log)
    folded = (blocks // 2, 2, 2, share // 2) if carried else (features,)
    dvq, reverse_grad, *kv_pieces = run(
        functools.partial(reverse_backward, blocks),
        [like(rows, features), like(*folded, 2 * features)]
        + [like(part, features)] * (2 * blocks),
        [answer_length, dx2, mv, vq, vkv, nx, log_v, attn_out],
        [SMEM, VMEM, VMEM, VMEM, VMEM, VMEM, VMEM, ANY],
        [((features, features), NARROW), ((rows, features), NARROW), ((rows, features), NARROW),
         ((16, rows), SINGLE), ((padded, 2 * features), SINGLE)],
        rows * square * 16,
        semaphores=1,
        ticking=carried,
    )
    k_parts, v_parts = Exchange(kv_pieces[:blocks]), Exchange(kv_pieces[blocks:])
    if carried:
        courier.load((k_parts, ""), (up_x, "x"))
    else:
        k_parts.result, v_parts.result = exchange(k_parts.pieces), exchange(v_parts.pieces)
    q3, dq2, up_q, down_q, norm_four, co = run(
        functools.partial(query_feed_forward, blocks, share, hidden_share),
        [
            like(count, features), like(count, features, kind=SINGLE), like(share_rows, hidden),
            like(hidden_rows, features), like(8, features, kind=SINGLE), like(padded, features),
        ],
        [q1, cot_q, norm_gain, norm_bias, attn_out, mlp_in, mlp_out, co_parts.tensor]
        + co_parts.result,
        [
            VMEM, VMEM, VMEM, VMEM, pl.BlockSpec((1, features, features), lambda j: (2, 0, 0)),
            pl.BlockSpec((1, features, CHUNK), lambda j: (1, 0, j)),
            pl.BlockSpec((1, CHUNK, features), lambda j: (1, j, 0)),
        ] + [ANY] * (2 * blocks - 1),
        [((count, features), SINGLE), ((count, features), NARROW), ((share_rows, count), NARROW),
         ((count, CHUNK), NARROW), ((count, CHUNK), NARROW),
         ((count, features), SINGLE), ((count, features), SINGLE)],
        count * square * 18,
        semaphores=2 * blocks - 1,
        grid=(hidden // CHUNK,),
        out_specs=[
            VMEM, VMEM,
            pl.BlockSpec((share_rows, CHUNK), lambda j: (0, j)),
            VMEM, VMEM, VMEM,
        ],
    )
    if carried:
        up_q, down_q = RepSum(up_q, 1), RepSum(down_q, 0)
        courier.load((v_parts, ""), (down_x, "x"), (up_x, "y"))
    dckv, cross_out_weight, *q_pieces = run(
        functools.partial(cross_backward, blocks, share),
        [like(rows, 2 * features), like(share_rows, features)] + [like(part, features)] * blocks,
        [dq2, co, cq, ckv, valid[:, None], attn_out] + log_parts.result,
        [VMEM, VMEM, VMEM, VMEM, VMEM, ANY] + [VMEM] * blocks,
        [((features, features), NARROW), ((count, features), NARROW), ((count, features), NARROW),
         ((16, count), SINGLE), ((padded, PAIR), SINGLE), ((16, count), SINGLE),
         ((padded, features), NARROW), ((rows, 2 * features), SINGLE)],
        count * square * 12,
        semaphores=1,
    )
    q_parts = Exchange(q_pieces)
    if carried:
        kv_weight = Reduction(like(blocks // 2, 2, 2, share // 2, 2 * features))
        window_weight = Reduction(like(blocks // 2, 2, 2, share // 2, 4 * features))
        courier.load(
            (q_parts, ""), (down_x, "y"), (reverse_weight, "x"), (up_q, "out"), (down_q, "out"),
            (kv_weight, "core", 0), (window_weight, "core", 1),
        )
    else:
        q_parts.result = exchange(q_pieces)
    kv_grad, window_grad, grad_x, norm_x = run(
        patch_backward,
        [
            like(*folded, 2 * features), like(*folded, 4 * features),
            like(rows, features, kind=SINGLE), like(8, features, kind=SINGLE),
        ],
        [x, dx2, x1, nx, n0, pw, mw, dvq, dckv, norm_gain, attn_in, attn_out],
        [VMEM] * 10 + [ANY, ANY],
        [((features, wide), NARROW), ((features, features), NARROW),
         ((features, features), NARROW), ((features, 2 * features), NARROW),
         ((rows, features), SINGLE), ((rows, features), NARROW), ((rows, features), NARROW),
         ((16, rows), SINGLE), ((rows, wide), NARROW)],
        rows * square * 24,
        semaphores=4,
        lazy=(0, 4, 5, 6),
        early=(0, 1),
    )
    if carried:
        share_weight = Reduction(like(blocks // 2, 2, 2, share // 2, wide))
        dq1_parts = Spread(like(part, features))
        courier.load(
            (share_weight, "core", 1), (dq1_parts, "", 0), (window_weight, "x"),
            (reverse_weight, "y"),
        )
    dq1_share, share_grad, norm_two = run(
        functools.partial(share_backward, blocks),
        [like(part, features), like(*folded, wide), like(8, features, kind=SINGLE)],
        [q1, nq, norm_gain, attn_in]
        + q_parts.result + k_parts.result + v_parts.result,
        [ANY, ANY, VMEM, ANY] + [VMEM] * (3 * blocks),
        [((features, features), NARROW), ((features, 2 * features), NARROW),
         ((part, wide), NARROW), ((part, features), SINGLE), ((part, features), NARROW)],
        part * square * 6,
        semaphores=4,
    )
    if carried:
        courier.load(
            (window_weight, "y"), (share_weight, "y"), (kv_weight, "x"), (down_x, "z"),
            (reverse_weight, "z"), (up_q, "back"), (down_q, "back"), (up_x, "z"),
        )
    else:
        dq1_parts = Spread(None)
        dq1_parts.tensor, *dq1_parts.result = in_halves(gather(dq1_share))
    causal_weight, grad_q, norm_one = run(
        functools.partial(causal_backward, blocks, share),
        [
            like(share_rows, causal_columns), like(count, features, kind=SINGLE),
            like(8, features, kind=SINGLE),
        ],
        [q, dq2, n1, pq, mq, log_q, cross_out_weight, norm_gain, attn_in, attn_out]
        + [dq1_parts.tensor] + dq1_parts.result,
        [VMEM] * 8 + [ANY] * (2 * blocks + 1),
        [((features, wide), NARROW), ((features, features), NARROW), ((padded, features), NARROW),
         ((count, features), SINGLE), ((count, features), NARROW), ((count, features), NARROW),
         ((16, count), SINGLE), ((count, 2 * PAIR), SINGLE), ((count, wide), NARROW)],
        count * square * 16,
        semaphores=2 * blocks + 1,
        lazy=(2, 3, 4, 5),
    )
    gains = jnp.stack(
        (norm_x[2], norm_one[0] * leader, norm_two[0], norm_x[0], norm_four[0] * leader, norm_five[0])
    )
    biases = jnp.stack(
        (norm_x[3], norm_one[1] * leader, norm_two[1], norm_x[1], norm_four[1] * leader, norm_five[1])
    )
    rest = (
        x3[None],
        own_columns(q3)[None],
        grad_x[None],
        own_columns(grad_q)[None],
    )
    if carried:
        norms = jnp.concatenate((jnp.pad(gains, ((0, 2), (0, 0))), jnp.pad(biases, ((0, 2), (0, 0)))))
        norms = jnp.transpose(norms.reshape(16, blocks, share), (1, 0, 2))
        norms = Norms(jnp.pad(norms, ((0, 0), (0, 0), (0, -share % PAIR))))
        causal_weight = RepSum(causal_weight, 1)
        sums = [up_x, down_x, reverse_weight, window_weight, kv_weight, share_weight]
        quarters = [up_q, down_q, causal_weight]
        grads = finale(
            functools.partial(assemble, len(sums), len(quarters), blocks),
            [
                like(4, share, wide), like(4, share, features), like(2, share, hidden),
                like(2, hidden_share, features),
                like(6, share, kind=SINGLE), like(6, share, kind=SINGLE),
            ],
            [
                [
                    (causal_weight, "out"), (norms, "out"), (share_weight, "x"), (kv_weight, "y"),
                    (window_weight, "z"), (up_x, "back_x"), (down_x, "back_x"),
                    (reverse_weight, "back_x"),
                ],
                [
                    (norms, "back"), (kv_weight, "z"), (causal_weight, "back"), (share_weight, "z"),
                    (window_weight, "back_x"), (up_x, "back_core"), (down_x, "back_core"),
                    (reverse_weight, "back_core"),
                ],
                [(kv_weight, "back_x"), (share_weight, "back_x"), (window_weight, "back_core")],
                [(kv_weight, "back_core"), (share_weight, "back_core")],
            ],
            lambda: sum([one.result for one in sums + quarters], []) + norms.result,
            [like(share, 4 * features), like(share, causal_columns)],
            courier.ident + 1,
        )
        return rest + (grads[4], grads[5]) + tuple(one.astype(SINGLE) for one in grads[:4])
    up_x, down_x, reverse_weight, window_weight, kv_weight, share_weight = (
        reduce_all(one) for one in (up_x, down_x, reverse_grad, window_grad, kv_grad, share_grad)
    )
    up_q, down_q = reduce_rep(up_q[:share]), reduce_rep(down_q[:hidden_share])
    causal_weight = reduce_rep(causal_weight[:share])
    gains, biases = (
        own_columns(one) for one in lax.psum((gains, biases), ("blk", "rep"))
    )
    grad_attn_in = jnp.stack(
        (
            window_weight[:, :wide],
            causal_weight[:, :wide],
            jnp.concatenate((share_weight[:, :features], kv_weight), axis=1),
            jnp.concatenate((reverse_weight[:, :features], share_weight[:, features:]), axis=1),
        )
    )
    grad_attn_out = jnp.stack(
        (
            window_weight[:, wide:],
            causal_weight[:, wide : wide + features],
            causal_weight[:, wide + features : last],
            reverse_weight[:, features:],
        )
    )
    return rest + (
        gains,
        biases,
        grad_attn_in.astype(SINGLE),
        grad_attn_out.astype(SINGLE),
        jnp.stack((up_x, up_q)).astype(SINGLE),
        jnp.stack((down_x, down_q)).astype(SINGLE),
    )


def solution(mesh):
    placed = (
        P("rep", "blk", None),
        P("rep", None, None),
        P("rep", "blk"),
        P("rep"),
        P(),
        P(),
        P(),
        P(),
        P(),
        P(),
        P("rep", "blk", None),
        P("rep", None, None),
    )
    return jax.shard_map(
        body,
        mesh=mesh,
        in_specs=placed,
        out_specs=(
            P("rep", "blk", None),
            P("rep", None, "blk"),
            P("rep", "blk", None),
            P("rep", None, "blk"),
            P(None, "blk"),
            P(None, "blk"),
            P(None, "blk", None),
            P(None, "blk", None),
            P(None, "blk", None),
            P(None, "blk", None),
        ),
        check_vma=False,
    )
```

```python
import functools
import math

import jax
import jax.numpy as jnp
from jax import lax
from jax.experimental import pallas as pl
from jax.experimental.pallas import tpu as pltpu
from jax.sharding import PartitionSpec as P

HEADS = 12
WIN = 64
EPSILON = 1e-05
MASKED = -1e30
NARROW = jnp.bfloat16
SINGLE = jnp.float32
GROUP = 128
WINDOWS = 256
PAIR = 128
HEAD = 64
STRIP = 160
LONG = 400
CHUNK = 768


def dot(former, latter, ahead, behind, precision=None):
    return lax.dot_general(
        former,
        latter,
        (((ahead,), (behind,)), ((), ())),
        preferred_element_type=SINGLE,
        precision=precision,
    )


def plain(former, latter):
    return dot(former, latter, 1, 0)


def right_t(former, latter):
    return dot(former, latter, 1, 1)


def left_t(former, latter):
    return dot(former, latter, 0, 0)


def loop(count, action):
    def step(index, nothing):
        action(index)
        return nothing

    lax.fori_loop(0, count, step, 0)


def at(index, size):
    return pl.ds(pl.multiple_of(index * size, size), size)


def iota(shape, dim):
    return lax.broadcasted_iota(jnp.int32, shape, dim)


def statistics(tensor):
    average = jnp.mean(tensor, axis=-1, keepdims=True)
    centred = tensor - average
    spread = jnp.mean(centred * centred, axis=-1, keepdims=True)
    return centred, lax.rsqrt(spread + EPSILON)


def norm(tensor, gain, bias):
    centred, inverse = statistics(tensor)
    return centred * inverse * gain + bias


def norm_back(tensor, gain, upstream):
    centred, inverse = statistics(tensor)
    scaled = centred * inverse
    inner = upstream * gain
    grad = inverse * (
        inner
        - jnp.mean(inner, axis=-1, keepdims=True)
        - scaled * jnp.mean(inner * scaled, axis=-1, keepdims=True)
    )
    return (
        grad,
        jnp.sum(upstream * scaled, axis=0, keepdims=True),
        jnp.sum(upstream, axis=0, keepdims=True),
    )


def gelu_both(tensor):
    size = jnp.abs(tensor)
    ratio = 1.0 / (1.0 + (0.3275911 * math.sqrt(0.5)) * size)
    series = ratio * (
        0.254829592
        + ratio * (-0.284496736 + ratio * (1.421413741 + ratio * (-1.453152027 + ratio * 1.061405429)))
    )
    bell = jnp.exp(-0.5 * (tensor * tensor))
    tail = 0.5 * series * bell
    below = jnp.where(tensor >= 0, 1.0 - tail, tail)
    return tensor * below, below + tensor * bell * (1.0 / math.sqrt(2.0 * math.pi))


def half(which, value=1.0):
    return jnp.where(iota((1, PAIR), 1) // HEAD == which, value, 0.0).astype(NARROW)


def lower_lanes():
    return iota((1, PAIR), 1) < HEAD


def both(tensor, value=1.0):
    return jnp.concatenate((tensor * half(0, value), tensor * half(1, value)), axis=0)


def attend(queries, keys, values, mask):
    rows = queries.shape[0]
    scores = right_t(both(queries, 1.0 / math.sqrt(HEAD)), keys)
    weights, totals, logs = [], [], []
    for which in range(2):
        part = mask(scores[which * rows : (which + 1) * rows])
        peak = jnp.max(part, axis=-1, keepdims=True)
        part = jnp.exp(part - peak)
        total = jnp.sum(part, axis=-1, keepdims=True)
        weights.append(part.astype(NARROW))
        totals.append(1.0 / total)
        logs.append(peak + jnp.log(total))
    out = plain(jnp.concatenate(weights, axis=0), values)
    return jnp.where(lower_lanes(), out[:rows] * totals[0], out[rows:] * totals[1]), logs


def attend_back(queries, keys, values, upstream, logs, deltas, mask):
    scaled = queries * jnp.asarray(1.0 / math.sqrt(HEAD), NARROW)
    count = keys.shape[0]
    keys = both(keys)
    turned_keys = keys.T
    scores = right_t(keys, scaled)
    inner = right_t(both(values), upstream)
    weights, slopes = [], []
    for which in range(2):
        span = slice(which * count, (which + 1) * count)
        part = mask(scores[span])
        if logs is None:
            part = jnp.exp(part - jnp.max(part, axis=0, keepdims=True))
            part = part * (1.0 / jnp.sum(part, axis=0, keepdims=True))
        else:
            part = jnp.exp(part - logs[which])
        weights.append(part.astype(NARROW))
        slopes.append((part * (inner[span] - deltas[which])).astype(NARROW))
    slope = jnp.concatenate(slopes, axis=0)
    query_grad = plain(turned_keys, slope).T
    key_grad = plain(slope, scaled)
    value_grad = plain(jnp.concatenate(weights, axis=0), upstream)
    lanes = lower_lanes()
    return (
        query_grad,
        jnp.where(lanes, key_grad[:count], key_grad[count:]),
        jnp.where(lanes, value_grad[:count], value_grad[count:]),
    )


def exact_parts(tensor, count):
    parts = []
    for _ in range(count):
        parts.append(tensor.astype(NARROW))
        tensor = tensor - parts[-1].astype(SINGLE)
    return parts


def head_rows(tensor):
    features = tensor.shape[1]
    heads = 16
    chosen = jnp.where(
        iota((heads, features), 1) // HEAD == iota((heads, features), 0), 1.0, 0.0
    ).astype(NARROW)
    return functools.reduce(jnp.add, [right_t(chosen, part) for part in exact_parts(tensor, 2)])


def turn(columns):
    same = jnp.where(iota((16, columns.shape[1]), 0) == iota((16, columns.shape[1]), 1), 1.0, 0.0)
    same = same.astype(NARROW)
    return functools.reduce(jnp.add, [right_t(same, part) for part in exact_parts(columns, 3)])


def row_pair(ref, pair, span):
    tensor = ref[:, span]
    index = iota(tensor.shape, 0)
    return [
        jnp.sum(jnp.where(index == 2 * pair + which, tensor, 0.0), axis=0, keepdims=True)
        for which in range(2)
    ]


def chooser(rows, width, start, count):
    row = iota((rows, width), 0)
    hit = jnp.logical_and(iota((rows, width), 1) == row + start, row < count)
    return jnp.where(hit, 1.0, 0.0).astype(NARROW)


def spans(rows, size):
    edges = [(start, min(start + size, rows)) for start in range(0, rows, size)]
    if len(edges) > 1 and edges[-1][1] - edges[-1][0] < PAIR:
        edges[-2:] = [(edges[-2][0], rows)]
    return edges


def mark(log_ref, rows, head, value):
    log_ref[rows, :] = jnp.where(iota((1, PAIR), 1) == head, value, log_ref[rows, :])


def store_rows(ref, columns, value):
    ref[(slice(None),) * (len(ref.shape) - 1) + (columns,)] = value.astype(ref.dtype).reshape(
        ref.shape[:-1] + value.shape[1:]
    )


def nothing(*unused):
    return None


def copies(semaphores, *pairs):
    made = [
        pltpu.make_async_copy(source, target, semaphores.at[k])
        for k, (source, target) in enumerate(pairs)
    ]
    for one in made:
        one.start()
    return made


DIRECT = 8


def place_of(axis="blk"):
    return lax.axis_index(axis)


def flipped(index, mask, count):
    total, weight = 0, 1
    while weight < count:
        bit = (index // weight) % 2
        total = total + weight * ((1 - bit) if mask & weight else bit)
        weight *= 2
    return total


def piece_at(number, count):
    return flipped(place_of(), number, count) if count <= DIRECT else number


def window_forward(
    x_ref, gain_ref, bias_ref, a_in, a_out,
    n0_ref, pw_ref, mw_ref, x1_ref, nx_ref, vq_ref, ckv_ref,
    w_in, w_out, w_q, w_kv, sem,
    flush=nothing,
):
    rows, features = x_ref.shape
    loads = copies(
        sem,
        (a_in.at[0], w_in),
        (a_out.at[0], w_out),
        (a_in.at[3, :, pl.ds(0, features)], w_q),
        (a_in.at[2, :, pl.ds(features, 2 * features)], w_kv),
    )

    def first(i):
        span = at(i, GROUP)
        n0_ref[span, :] = norm(
            x_ref[span, :].astype(SINGLE), gain_ref[0:1, :], bias_ref[0:1, :]
        ).astype(NARROW)

    loop(rows // GROUP, first)
    loads[0].wait()

    def project(j):
        span = at(j, CHUNK)
        pw_ref[:, span] = plain(n0_ref[...], w_in[:, span]).astype(NARROW)

    loop(3 * features // CHUNK, project)
    flush(0)
    flush(1)
    window = jnp.where(
        iota((WINDOWS, WINDOWS), 0) // WIN == iota((WINDOWS, WINDOWS), 1) // WIN, 0.0, MASKED
    )

    def group(i):
        span = at(i, WINDOWS)
        for pair in range(features // PAIR):
            lane = pair * PAIR
            out, unused = attend(
                pw_ref[span, lane : lane + PAIR],
                pw_ref[span, features + lane : features + lane + PAIR],
                pw_ref[span, 2 * features + lane : 2 * features + lane + PAIR],
                lambda scores: scores + window,
            )
            mw_ref[span, lane : lane + PAIR] = out.astype(NARROW)

    loop(rows // WINDOWS, group)
    flush(2)
    loads[1].wait()

    def second(i):
        span = at(i, GROUP)
        total = x_ref[span, :].astype(SINGLE) + plain(mw_ref[span, :], w_out[...])
        x1_ref[span, :] = total
        nx_ref[span, :] = norm(total, gain_ref[3:4, :], bias_ref[3:4, :]).astype(NARROW)

    loop(rows // GROUP, second)
    flush(3)
    flush(4)
    loads[2].wait()
    vq_ref[...] = plain(nx_ref[...], w_q[...]).astype(NARROW)
    flush(5)
    loads[3].wait()

    def third(j):
        span = at(j, CHUNK)
        ckv_ref[:, span] = plain(nx_ref[...], w_kv[:, span]).astype(NARROW)

    loop(2 * features // CHUNK, third)


def causal_forward(
    q_ref, gain_ref, bias_ref, a_in, a_out,
    n1_ref, pq_ref, mq_ref, q1_ref, nq_ref, cq_ref, vkv_ref, log_ref,
    w_in, w_out, w_q, w_kv, logs, sem,
    flush=nothing,
):
    rows, features = q_ref.shape
    loads = copies(
        sem,
        (a_in.at[1], w_in),
        (a_out.at[1], w_out),
        (a_in.at[2, :, pl.ds(0, features)], w_q),
        (a_in.at[3, :, pl.ds(features, 2 * features)], w_kv),
    )

    def first(i):
        span = at(i, STRIP)
        n1_ref[span, :] = norm(
            q_ref[span, :].astype(SINGLE), gain_ref[1:2, :], bias_ref[1:2, :]
        ).astype(NARROW)

    loop(rows // STRIP, first)
    loads[0].wait()

    def project(j):
        span = at(j, CHUNK)
        pq_ref[:, span] = plain(n1_ref[...], w_in[:, span]).astype(NARROW)

    loop(3 * features // CHUNK, project)
    flush(0)
    flush(1)
    logs[...] = jnp.zeros_like(logs)

    def pair(p):
        for start in range(0, rows, LONG):
            end = min(start + LONG, rows)

            def mask(scores, start=start):
                shape = scores.shape
                return jnp.where(iota(shape, 1) <= iota(shape, 0) + start, scores, MASKED)

            out, sums = attend(
                pq_ref[start:end, at(p, PAIR)],
                pq_ref[0:end, at(p + features // PAIR, PAIR)],
                pq_ref[0:end, at(p + 2 * features // PAIR, PAIR)],
                mask,
            )
            mq_ref[start:end, at(p, PAIR)] = out.astype(NARROW)
            for which in range(2):
                mark(logs, slice(start, end), 2 * p + which, sums[which])

    loop(features // PAIR, pair)
    flush(2)
    log_ref[...] = turn(logs[...])
    loads[1].wait()

    def second(i):
        span = at(i, STRIP)
        total = q_ref[span, :].astype(SINGLE) + plain(mq_ref[span, :], w_out[...])
        q1_ref[span, :] = total
        nq_ref[span, :] = norm(total, gain_ref[2:3, :], bias_ref[2:3, :]).astype(NARROW)

    loop(rows // STRIP, second)
    if q1_ref.shape[0] > rows:
        q1_ref[rows:, :] = jnp.zeros_like(q1_ref[rows:, :])
        nq_ref[rows:, :] = jnp.zeros_like(nq_ref[rows:, :])
    flush(3)
    flush(4)
    loads[2].wait()
    cq_ref[...] = plain(nq_ref[0:rows, :], w_q[...]).astype(NARROW)
    flush(5)
    loads[3].wait()

    def third(j):
        span = at(j, CHUNK)
        vkv_ref[:, span] = plain(nq_ref[0:rows, :], w_kv[:, span]).astype(NARROW)

    loop(2 * features // CHUNK, third)


def cross_forward(pieces, cq_ref, ckv_ref, valid_ref, whole, *rest):
    log_refs, (logs,) = rest[:pieces], rest[pieces:]
    rows, features = cq_ref.shape
    part = log_refs[0].shape[1]
    logs[...] = jnp.zeros_like(logs)
    if whole.shape[0] > rows:
        whole[rows:, :] = jnp.zeros((whole.shape[0] - rows, features), NARROW)

    def pair(p):
        for start in range(0, rows, LONG):
            span = slice(start, min(start + LONG, rows))
            out, sums = attend(
                cq_ref[span, at(p, PAIR)],
                ckv_ref[:, at(p, PAIR)],
                ckv_ref[:, at(p + features // PAIR, PAIR)],
                lambda scores: scores + valid_ref[...],
            )
            whole[span, at(p, PAIR)] = out.astype(NARROW)
            for which in range(2):
                mark(logs, span, 2 * p + which, sums[which])

    loop(features // PAIR, pair)
    for k in range(pieces):
        log_refs[k][...] = turn(logs[at(piece_at(k, pieces), part), :])


def untwist(rows):
    same = jnp.where(iota((16, PAIR), 0) == iota((16, PAIR), 1), 1.0, 0.0).astype(NARROW)
    return functools.reduce(jnp.add, [left_t(part, same) for part in exact_parts(rows, 3)])


def merge_blocks(pieces, own_ref, *refs):
    logs, refs = refs[:pieces], refs[pieces:]
    halves, (co_ref, log_ref) = (refs[: pieces - 1], refs[pieces - 1 : -2]), refs[-2:]
    part, features = co_ref.shape
    width = features // 2
    peak = functools.reduce(jnp.maximum, [one[...] for one in logs])
    total = peak + jnp.log(functools.reduce(jnp.add, [jnp.exp(one[...] - peak) for one in logs]))
    log_ref[...] = total
    spread = jnp.where(
        iota((PAIR, features), 1) // HEAD == iota((PAIR, features), 0), 1.0, 0.0
    ).astype(NARROW)
    result = jnp.zeros(co_ref.shape, SINGLE)
    for k in range(pieces):
        weight = untwist(jnp.exp(logs[k][...] - total))
        high = weight.astype(NARROW)
        low = (weight - high.astype(SINGLE)).astype(NARROW)
        if k == 0:
            block = own_ref[at(place_of(), part), :]
        else:
            block = jnp.concatenate((halves[0][k - 1][...], halves[1][k - 1][...]), axis=1)
        result = result + (plain(high, spread) + plain(low, spread)) * block.astype(SINGLE)
    co_ref[...] = result.astype(NARROW)


def reverse_forward(
    length_ref, vq_ref, vkv_ref, x1_ref, a_out,
    mv_ref, x2_ref, log_ref,
    w_out, logs, sem,
    ready=nothing, flush=nothing,
):
    rows, features = vq_ref.shape
    keys = vkv_ref.shape[0]
    (load,) = copies(sem, (a_out.at[3], w_out))
    logs[...] = jnp.zeros_like(logs)
    bias = jnp.where(iota((1, keys), 1) < length_ref[0], 0.0, MASKED)

    def pair(p):
        for start in range(0, rows, WINDOWS):
            span = slice(start, start + WINDOWS)
            out, sums = attend(
                vq_ref[span, at(p, PAIR)],
                vkv_ref[:, at(p, PAIR)],
                vkv_ref[:, at(p + features // PAIR, PAIR)],
                lambda scores: scores + bias,
            )
            mv_ref[span, at(p, PAIR)] = out.astype(NARROW)
            for which in range(2):
                mark(logs, span, 2 * p + which, sums[which])

    loop(features // PAIR, pair)
    flush(0)
    log_ref[...] = turn(logs[...])
    load.wait()
    ready(3)

    def second(i):
        span = at(i, GROUP)
        x2_ref[span, :] = x1_ref[span, :] + plain(mv_ref[span, :], w_out[...])

    loop(rows // GROUP, second)


def feed_forward_step(block, normed, up, down, cot, hidden, slope, out, grad):
    rows = normed.shape[0]

    def strip(i):
        span = at(i, block)
        value, rise = gelu_both(plain(normed[span, :], up[...]))
        hidden[span, :] = value.astype(NARROW)
        slope[span, :] = (right_t(cot[span, :], down[...]) * rise).astype(NARROW)
        out[span, :] += plain(hidden[span, :], down[...])
        grad[span, :] += right_t(slope[span, :], up[...])

    loop(rows // block, strip)


def patch_feed_forward(
    x2_ref, cot_ref, gain_ref, bias_ref, up_ref, down_ref,
    x3_ref, dx2_ref, up_grad_ref, down_grad_ref, norm_ref,
    normed, hidden, slope, out, grad,
):
    rows = x2_ref.shape[0]
    step = pl.program_id(0)

    @pl.when(step == 0)
    def begin():
        def first(i):
            span = at(i, GROUP)
            normed[span, :] = norm(
                x2_ref[span, :], gain_ref[5:6, :], bias_ref[5:6, :]
            ).astype(NARROW)
            out[span, :] = x2_ref[span, :]
            grad[span, :] = jnp.zeros_like(grad[span, :])

        loop(rows // GROUP, first)

    feed_forward_step(
        512, normed, up_ref.at[0], down_ref.at[0], cot_ref, hidden, slope, out, grad
    )
    up_grad_ref[...] = left_t(normed[...], slope[...]).astype(NARROW)
    down_grad_ref[...] = left_t(hidden[...], cot_ref[...]).astype(NARROW)

    @pl.when(step == pl.num_programs(0) - 1)
    def finish():
        norm_ref[...] = jnp.zeros_like(norm_ref)

        def last(i):
            span = at(i, GROUP)
            x3_ref[span, :] = out[span, :].astype(NARROW)
            part, gain, bias = norm_back(x2_ref[span, :], gain_ref[5:6, :], grad[span, :])
            dx2_ref[span, :] = cot_ref[span, :].astype(SINGLE) + part
            norm_ref[0:1, :] += gain
            norm_ref[1:2, :] += bias

        loop(rows // GROUP, last)


def place_parts(ref, pieces, parts, sem):
    part, features = parts[0].shape
    width = features // 2
    pairs = [(parts[0], ref.at[at(piece_at(0, pieces), part), :])]
    for number in range(2):
        for k in range(1, pieces):
            pairs.append(
                (
                    parts[number * (pieces - 1) + k],
                    ref.at[at(piece_at(k, pieces), part), pl.ds(number * width, width)],
                )
            )
    return copies(sem, *pairs)


def query_feed_forward(
    pieces, share, hidden_share, q1_ref, cot_ref, gain_ref, bias_ref,
    w_out, up_ref, down_ref, *rest,
):
    parts, rest = rest[: 2 * pieces - 1], rest[2 * pieces - 1 :]
    (
        q3_ref, dq2_ref, up_grad_ref, down_grad_ref, norm_ref, co_ref,
        q2, normed, chosen, hidden, slope, out, grad, sem,
    ) = rest
    rows, features = cot_ref.shape
    width = up_ref.shape[2]
    step = pl.program_id(0)

    @pl.when(step == 0)
    def begin():
        for one in place_parts(co_ref, pieces, parts, sem):
            one.wait()

        def first(i):
            span = at(i, STRIP)
            total = q1_ref[span, :] + plain(co_ref[span, :], w_out[0])
            q2[span, :] = total
            out[span, :] = total
            normed[span, :] = norm(total, gain_ref[4:5, :], bias_ref[4:5, :]).astype(NARROW)
            grad[span, :] = jnp.zeros_like(grad[span, :])

        loop(rows // STRIP, first)
        chosen[...] = right_t(
            chooser(chosen.shape[0], features, place_of() * share, share), normed[...]
        ).astype(NARROW)

    feed_forward_step(
        rows, normed, up_ref.at[0], down_ref.at[0], cot_ref, hidden, slope, out, grad
    )
    up_grad_ref[...] = plain(chosen[...], slope[...]).astype(NARROW)
    begins = place_of() * hidden_share

    @pl.when(begins // width == step)
    def own_hidden():
        taken = right_t(
            chooser(down_grad_ref.shape[0], width, begins - step * width, hidden_share),
            hidden[...],
        ).astype(NARROW)
        down_grad_ref[...] = plain(taken, cot_ref[...]).astype(NARROW)

    @pl.when(step == pl.num_programs(0) - 1)
    def finish():
        norm_ref[...] = jnp.zeros_like(norm_ref)

        def last(i):
            span = at(i, STRIP)
            q3_ref[span, :] = out[span, :].astype(NARROW)
            piece, gain, bias = norm_back(q2[span, :], gain_ref[4:5, :], grad[span, :])
            dq2_ref[span, :] = cot_ref[span, :].astype(SINGLE) + piece
            norm_ref[0:1, :] += gain
            norm_ref[1:2, :] += bias

        loop(rows // STRIP, last)


def reverse_backward(
    pieces, length_ref, dx2_ref, mv_ref, vq_ref, vkv_ref, nx_ref, log_ref, a_out,
    *rest, launch=nothing, tick=nothing, ready=nothing,
):
    dvq_ref, weight_ref, rest = rest[0], rest[1], rest[2:]
    k_refs, v_refs, rest = rest[:pieces], rest[pieces : 2 * pieces], rest[2 * pieces :]
    w_out, rounded, dmv, deltas, dkv, sem = rest
    rows, features = vq_ref.shape
    keys = vkv_ref.shape[0]
    part = k_refs[0].shape[0]
    (load,) = copies(sem, (a_out.at[3], w_out))
    rounded[...] = dx2_ref[...].astype(NARROW)
    load.wait()
    dmv[...] = right_t(rounded[...], w_out[...]).astype(NARROW)
    store_rows(
        weight_ref, slice(features, 2 * features), left_t(mv_ref[...], rounded[...])
    )
    deltas[...] = head_rows(dmv[...].astype(SINGLE) * mv_ref[...].astype(SINGLE))
    if dkv.shape[0] > keys:
        dkv[keys:, :] = jnp.zeros((dkv.shape[0] - keys, 2 * features), SINGLE)
    size = 256
    for k in (3, 4, 6):
        ready(k)

    def pair(p):
        pl.when(p == 2)(lambda: tick(1))
        pl.when(p == 4)(lambda: tick(2))
        for strip in range(rows // size):
            span = slice(strip * size, (strip + 1) * size)

            def mask(scores):
                return jnp.where(iota(scores.shape, 0) < length_ref[0], scores, MASKED)

            dq, dk, dv = attend_back(
                vq_ref[span, at(p, PAIR)],
                vkv_ref[:, at(p, PAIR)],
                vkv_ref[:, at(p + features // PAIR, PAIR)],
                dmv[span, at(p, PAIR)],
                row_pair(log_ref, p, span),
                row_pair(deltas, p, span),
                mask,
            )
            dvq_ref[span, at(p, PAIR)] = (dq * (1.0 / math.sqrt(HEAD))).astype(NARROW)
            if strip == 0:
                dkv[0:keys, at(p, PAIR)] = dk
                dkv[0:keys, at(p + features // PAIR, PAIR)] = dv
            else:
                dkv[0:keys, at(p, PAIR)] += dk
                dkv[0:keys, at(p + features // PAIR, PAIR)] += dv

    loop(features // PAIR, pair)
    ready(5)
    store_rows(weight_ref, slice(0, features), left_t(nx_ref[...], dvq_ref[...]))
    launch(1)
    for k in range(pieces):
        span = at(piece_at(k, pieces), part)
        k_refs[k][...] = dkv[span, 0:features].astype(NARROW)
        v_refs[k][...] = dkv[span, features:].astype(NARROW)


def cross_backward(
    pieces, share, dq2_ref, co_ref, cq_ref, ckv_ref, valid_ref, a_out, *rest, ready=nothing
):
    log_parts, rest = rest[:pieces], rest[pieces:]
    dckv_ref, weight_ref, rest = rest[0], rest[1], rest[2:]
    q_refs, (w_out, rounded, dco, deltas, logs, turned, dq_all, dkv, sem) = (
        rest[:pieces],
        rest[pieces:],
    )
    rows, features = cq_ref.shape
    part = log_parts[0].shape[1]
    (load,) = copies(sem, (a_out.at[2], w_out))
    for k in range(pieces):
        logs[at(piece_at(k, pieces), part), :] = untwist(log_parts[k][...])
    turned[...] = turn(logs[0:rows, :])
    rounded[...] = dq2_ref[...].astype(NARROW)
    load.wait()
    dco[...] = right_t(rounded[...], w_out[...]).astype(NARROW)
    taken = right_t(
        chooser(weight_ref.shape[0], features, place_of() * share, share), co_ref[0:rows, :]
    ).astype(NARROW)
    weight_ref[...] = plain(taken, rounded[...]).astype(NARROW)
    deltas[...] = head_rows(dco[...].astype(SINGLE) * co_ref[0:rows, :].astype(SINGLE))
    if dq_all.shape[0] > rows:
        dq_all[rows:, :] = jnp.zeros((dq_all.shape[0] - rows, features), NARROW)
    edges = spans(rows, 512)
    ready(2)
    ready(3)

    def pair(p):
        for number, (start, end) in enumerate(edges):
            span = slice(start, end)
            dq, dk, dv = attend_back(
                cq_ref[span, at(p, PAIR)],
                ckv_ref[:, at(p, PAIR)],
                ckv_ref[:, at(p + features // PAIR, PAIR)],
                dco[span, at(p, PAIR)],
                row_pair(turned, p, span),
                row_pair(deltas, p, span),
                lambda scores: scores + valid_ref[...],
            )
            dq_all[span, at(p, PAIR)] = (dq * (1.0 / math.sqrt(HEAD))).astype(NARROW)
            if number == 0:
                dkv[:, at(p, PAIR)] = dk
                dkv[:, at(p + features // PAIR, PAIR)] = dv
            else:
                dkv[:, at(p, PAIR)] += dk
                dkv[:, at(p + features // PAIR, PAIR)] += dv

    loop(features // PAIR, pair)
    dckv_ref[...] = dkv[...].astype(NARROW)
    for k in range(pieces):
        q_refs[k][...] = dq_all[at(piece_at(k, pieces), part), :]


def patch_backward(
    x_ref, dx2_ref, x1_ref, nx_ref, n0_ref, pw_ref, mw_ref, dvq_ref, dckv_ref, gain_ref, a_in, a_out,
    kv_weight_ref, weight_ref, grad_ref, norm_ref,
    w_in, w_out, w_q, w_kv, dx1, rounded, dmw, deltas, dpw, sem,
    launch=nothing, ready=nothing, flush=nothing,
):
    rows, features = x_ref.shape
    loads = copies(
        sem,
        (a_in.at[3, :, pl.ds(0, features)], w_q),
        (a_in.at[2, :, pl.ds(features, 2 * features)], w_kv),
        (a_out.at[0], w_out),
        (a_in.at[0], w_in),
    )
    norm_ref[...] = jnp.zeros_like(norm_ref)
    for start in range(0, 2 * features, CHUNK):
        span = slice(start, start + CHUNK)
        store_rows(kv_weight_ref, span, left_t(nx_ref[...], dckv_ref[:, span]))
    launch(0)
    flush(0)
    loads[0].wait()
    loads[1].wait()

    def first(i):
        span = at(i, GROUP)
        upstream = right_t(dvq_ref[span, :], w_q[...]) + right_t(dckv_ref[span, :], w_kv[...])
        part, gain, bias = norm_back(x1_ref[span, :], gain_ref[3:4, :], upstream)
        total = dx2_ref[span, :] + part
        dx1[span, :] = total
        rounded[span, :] = total.astype(NARROW)
        norm_ref[0:1, :] += gain
        norm_ref[1:2, :] += bias

    loop(rows // GROUP, first)
    loads[2].wait()
    ready(6)
    dmw[...] = right_t(rounded[...], w_out[...]).astype(NARROW)
    store_rows(
        weight_ref, slice(3 * features, 4 * features), left_t(mw_ref[...], rounded[...])
    )
    deltas[...] = head_rows(dmw[...].astype(SINGLE) * mw_ref[...].astype(SINGLE))
    ready(5)
    window = jnp.where(
        iota((WINDOWS, WINDOWS), 0) // WIN == iota((WINDOWS, WINDOWS), 1) // WIN, 0.0, MASKED
    )

    def group(i):
        span = at(i, WINDOWS)
        for pair in range(features // PAIR):
            lane = pair * PAIR
            dq, dk, dv = attend_back(
                pw_ref[span, lane : lane + PAIR],
                pw_ref[span, features + lane : features + lane + PAIR],
                pw_ref[span, 2 * features + lane : 2 * features + lane + PAIR],
                dmw[span, lane : lane + PAIR],
                None,
                [deltas[2 * pair + w : 2 * pair + w + 1, span] for w in range(2)],
                lambda scores: scores + window,
            )
            dpw[span, lane : lane + PAIR] = (dq * (1.0 / math.sqrt(HEAD))).astype(NARROW)
            dpw[span, features + lane : features + lane + PAIR] = dk.astype(NARROW)
            dpw[span, 2 * features + lane : 2 * features + lane + PAIR] = dv.astype(NARROW)

    loop(rows // WINDOWS, group)
    ready(4)
    for start in range(0, 3 * features, CHUNK):
        span = slice(start, start + CHUNK)
        store_rows(weight_ref, span, left_t(n0_ref[...], dpw[:, span]))
    launch(1)
    flush(1)
    ready(0)
    loads[3].wait()

    def last(i):
        span = at(i, GROUP)
        upstream = right_t(dpw[span, :], w_in[...])
        part, gain, bias = norm_back(x_ref[span, :].astype(SINGLE), gain_ref[0:1, :], upstream)
        grad_ref[span, :] = dx1[span, :] + part
        norm_ref[2:3, :] += gain
        norm_ref[3:4, :] += bias

    loop(rows // GROUP, last)


def share_backward(
    pieces, q1, nq, gain_ref, a_in, *rest, launch=nothing
):
    parts = [rest[k * pieces : (k + 1) * pieces] for k in range(3)]
    rest = rest[3 * pieces :]
    grad_ref, weight_ref, norm_ref, w_q, w_kv, summed, q1_ref, nq_ref, sem = rest
    part, features = q1_ref.shape
    *loads, load_q, load_n = copies(
        sem,
        (a_in.at[2, :, pl.ds(0, features)], w_q),
        (a_in.at[3, :, pl.ds(features, 2 * features)], w_kv),
        (q1.at[at(place_of(), part), :], q1_ref),
        (nq.at[at(place_of(), part), :], nq_ref),
    )
    for k in range(3):
        span = slice(k * features, (k + 1) * features)
        total = functools.reduce(jnp.add, [one[...].astype(SINGLE) for one in parts[k]])
        summed[:, span] = total.astype(NARROW)
    for load in loads:
        load.wait()
    upstream = right_t(summed[:, 0:features], w_q[...]) + right_t(summed[:, features:], w_kv[...])
    load_q.wait()
    piece, gain, bias = norm_back(q1_ref[...], gain_ref[2:3, :], upstream)
    grad_ref[...] = piece.astype(NARROW)
    launch(0)
    load_n.wait()
    for k in range(3):
        span = slice(k * features, (k + 1) * features)
        store_rows(weight_ref, span, left_t(nq_ref[...], summed[:, span]))
    launch(1)
    norm_ref[...] = jnp.zeros_like(norm_ref)
    norm_ref[0:1, :] = gain
    norm_ref[1:2, :] = bias


def causal_backward(
    pieces, share, q_ref, dq2_ref, n1_ref, pq_ref, mq_ref, log_ref, cross_ref, gain_ref,
    a_in, a_out, *rest, ready=nothing
):
    parts, rest = rest[: 2 * pieces - 1], rest[2 * pieces - 1 :]
    (
        weight_ref, grad_ref, norm_ref,
        w_in, w_out, gathered, dq1, rounded, dmq, deltas, dkv, dpq, sem,
    ) = rest
    rows, features = q_ref.shape
    placed = place_parts(gathered, pieces, parts, sem)
    loads = copies(sem.at[pl.ds(len(placed), 2)], (a_out.at[1], w_out), (a_in.at[1], w_in))
    for one in placed:
        one.wait()

    def first(i):
        span = at(i, STRIP)
        total = dq2_ref[span, :] + gathered[span, :].astype(SINGLE)
        dq1[span, :] = total
        rounded[span, :] = total.astype(NARROW)

    loop(rows // STRIP, first)
    loads[0].wait()
    dmq[...] = right_t(rounded[...], w_out[...]).astype(NARROW)
    ready(4)
    chosen = chooser(weight_ref.shape[0], features, place_of() * share, share)
    taken = right_t(chosen, mq_ref[...]).astype(NARROW)
    weight_ref[:, 3 * features : 4 * features] = plain(taken, rounded[...]).astype(NARROW)
    weight_ref[:, 4 * features : 5 * features] = cross_ref[...]
    weight_ref[:, 5 * features :] = jnp.zeros_like(weight_ref[:, 5 * features :])
    deltas[...] = head_rows(dmq[...].astype(SINGLE) * mq_ref[...].astype(SINGLE))
    edges = spans(rows, 256)
    ready(3)
    ready(5)

    def pair(p):
        for number, (start, end) in reversed(list(enumerate(edges))):
            span = slice(start, end)

            def mask(scores, start=start):
                shape = scores.shape
                return jnp.where(iota(shape, 0) <= iota(shape, 1) + start, scores, MASKED)

            dq, dk, dv = attend_back(
                pq_ref[span, at(p, PAIR)],
                pq_ref[0:end, at(p + features // PAIR, PAIR)],
                pq_ref[0:end, at(p + 2 * features // PAIR, PAIR)],
                dmq[span, at(p, PAIR)],
                row_pair(log_ref, p, span),
                row_pair(deltas, p, span),
                mask,
            )
            dpq[span, at(p, PAIR)] = (dq * (1.0 / math.sqrt(HEAD))).astype(NARROW)
            if end == rows:
                dkv[0:end, 0:PAIR] = dk
                dkv[0:end, PAIR:] = dv
            else:
                dkv[0:end, 0:PAIR] += dk
                dkv[0:end, PAIR:] += dv
        dpq[:, at(p + features // PAIR, PAIR)] = dkv[:, 0:PAIR].astype(NARROW)
        dpq[:, at(p + 2 * features // PAIR, PAIR)] = dkv[:, PAIR:].astype(NARROW)

    loop(features // PAIR, pair)
    ready(2)
    taken = right_t(chosen, n1_ref[...]).astype(NARROW)
    weight_ref[:, 0 : 3 * features] = plain(taken, dpq[...]).astype(NARROW)
    loads[1].wait()
    norm_ref[...] = jnp.zeros_like(norm_ref)

    def last(i):
        span = at(i, STRIP)
        upstream = right_t(dpq[span, :], w_in[...])
        piece, gain, bias = norm_back(q_ref[span, :].astype(SINGLE), gain_ref[1:2, :], upstream)
        grad_ref[span, :] = dq1[span, :] + piece
        norm_ref[0:1, :] += gain
        norm_ref[1:2, :] += bias

    loop(rows // STRIP, last)


def assemble(groups, count, *refs, ready=nothing, flush=nothing):
    parts, refs = refs[: 4 * groups], refs[4 * groups :]
    norms, refs = refs[:count], refs[count:]
    in_ref, out_ref, up_ref, down_ref, gain_ref, bias_ref, share, causal = refs
    features = down_ref.shape[2]
    rep = place_of("rep")

    def corners(number, write):
        for k in range(4):
            ready(4 * number + k)
            owner = flipped(rep, k, 4)
            piece = parts[4 * number + k][...]
            height, width = piece.shape[-2:]
            piece = piece.reshape(height, width)
            write(
                pl.ds(pl.multiple_of((owner % 2) * height, height), height),
                pl.multiple_of((owner // 2) * width, width), width, piece,
            )

    def into(ref, index, start=0):
        def write(rows, column, width, piece):
            ref[index, rows, pl.ds(column + start, width)] = piece

        return write

    up_x, down_x, reverse, window, kv, shared, up_q, down_q, rest = range(groups)

    def keep_causal(rows, column, width, piece):
        causal[rows, pl.ds(column, width)] = piece

    def keep_share(rows, column, width, piece):
        share[rows, pl.ds(column, width)] = piece

    corners(up_q, into(up_ref, 1))
    corners(down_q, into(down_ref, 1))
    corners(up_x, into(up_ref, 0))
    flush(2)
    corners(down_x, into(down_ref, 0))
    flush(3)
    first = 4 * groups
    for k in range(count):
        ready(first + k)
    terms = [norms[0][place_of()]] + [one[...] for one in norms[1:]]
    total = functools.reduce(jnp.add, terms)
    columns = gain_ref.shape[1]
    gain_ref[...] = total[0:6, 0:columns]
    bias_ref[...] = total[8:14, 0:columns]
    flush(4)
    flush(5)
    corners(reverse, keep_share)
    in_ref[3, :, 0:features] = share[:, 0:features]
    out_ref[3, :, :] = share[:, features : 2 * features]
    corners(window, keep_share)
    in_ref[0, :, :] = share[:, 0 : 3 * features]
    out_ref[0, :, :] = share[:, 3 * features :]
    corners(rest, keep_causal)
    in_ref[1, :, :] = causal[:, 0 : 3 * features]
    out_ref[1, :, :] = causal[:, 3 * features : 4 * features]
    out_ref[2, :, :] = causal[:, 4 * features : 5 * features]
    flush(1)
    corners(kv, into(in_ref, 2, features))
    corners(shared, keep_share)
    in_ref[2, :, 0:features] = share[:, 0:features]
    in_ref[3, :, features:] = share[:, features : 3 * features]
    flush(0)


def bits_of(count):
    return max(count - 1, 0).bit_length()


def swap(tensor, axis, mask):
    return lax.ppermute(tensor, axis, [(i, i ^ mask) for i in range(lax.axis_size(axis))])


def pick(tensor, place, dim):
    return lax.dynamic_index_in_dim(tensor, place, dim, keepdims=False)


def fold(tensor, axis, bit, dim):
    own = (lax.axis_index(axis) >> bit) & 1
    arrived = swap(pick(tensor, 1 - own, dim).astype(NARROW), axis, 1 << bit)
    return pick(tensor, own, dim).astype(SINGLE) + arrived.astype(SINGLE)


def unfold(tensor, axis, bit, dim):
    own = (lax.axis_index(axis) >> bit) & 1
    arrived = swap(tensor, axis, 1 << bit)
    return jnp.where(
        own == 0,
        jnp.stack((tensor, arrived), axis=dim),
        jnp.stack((arrived, tensor), axis=dim),
    )


def scatter_blk(tensor):
    bits = bits_of(lax.axis_size("blk"))
    tensor = tensor.reshape((2,) * bits + tensor.shape[1:])
    for bit in range(bits):
        tensor = fold(tensor, "blk", bit, bits - 1 - bit)
    return tensor


def sum_rep_scatter(tensor, dim):
    bits = bits_of(lax.axis_size("rep"))
    shape = tensor.shape
    tensor = tensor.reshape(
        shape[:dim] + (2,) * bits + (shape[dim] // 2**bits,) + shape[dim + 1 :]
    )
    for bit in range(bits):
        tensor = fold(tensor, "rep", bit, dim)
    return tensor


def gather_rep(tensor, dim):
    bits = bits_of(lax.axis_size("rep"))
    for bit in reversed(range(bits)):
        tensor = unfold(tensor, "rep", bit, dim)
    shape = tensor.shape
    return tensor.reshape(shape[:dim] + (-1,) + shape[dim + bits + 1 :])


def reduce_all(tensor):
    count = lax.axis_size("blk")
    tensor = tensor.reshape(count, tensor.shape[0] // count, tensor.shape[1])
    tensor = sum_rep_scatter(tensor, 1)
    tensor = scatter_blk(tensor).astype(NARROW)
    return gather_rep(tensor, 0)


def reduce_rep(tensor):
    return gather_rep(sum_rep_scatter(tensor, 0).astype(NARROW), 0)


def exchange(pieces):
    whole = lax.all_to_all(jnp.stack(pieces), "blk", 0, 0)
    return [whole[k] for k in range(len(pieces))]


def gather(tensor):
    count = lax.axis_size("blk")
    whole = lax.all_gather(tensor, "blk")
    return [whole[k] for k in range(count)]


def whole(ref):
    return ref


class Fold:
    def __init__(self, own, take, arrived, shape, keep=whole, keep_shape=None):
        self.own, self.take, self.arrived, self.shape = own, take, arrived, shape
        self.keep, self.keep_shape = keep, keep_shape or shape
        self.dtype = own.dtype


class Move:
    late = None

    def __init__(self, source, shape, axis, flip, take=whole, phase=0):
        self.source, self.shape, self.axis, self.flip, self.take = source, shape, axis, flip, take
        self.phase = phase
        self.dtype = source.dtype


def lanes_of(ref, start, width):
    return ref.at[(slice(None),) * (len(ref.shape) - 1) + (pl.ds(start, width),)]


class Reduction:
    def __init__(self, tensor, blocks=None):
        if blocks == 1:
            tensor = tensor.reshape(1, 1, 2, tensor.shape[0] // 2, tensor.shape[1])
        elif len(tensor.shape) == 2:
            blocks = lax.axis_size("blk")
            height = tensor.shape[0] // blocks
            tensor = tensor.reshape(blocks // 2, 2, 2, height // 2, tensor.shape[1])
        self.tensor, self.take, self.arrived, self.shape = tensor, whole, [], tensor.shape

    def fold(self, keep=whole, keep_shape=None):
        return Fold(self.tensor, self.take, self.arrived, self.shape, keep, keep_shape)

    def moves(self, stage):
        shape = self.shape
        if stage == "core":
            self.next = shape[:2] + shape[3:]
            return [
                Move(self.tensor, self.next, "rep", 1,
                     lambda ref: ref.at[:, :, 1 - place_of("rep") % 2])
            ]
        if stage == "x":
            width = shape[-1] // 2
            self.next = shape[:-1] + (width,)

            def own(ref):
                return lanes_of(ref, pl.multiple_of((place_of("rep") // 2) * width, width), width)

            def other(ref):
                start = (1 - place_of("rep") // 2) * width
                return lanes_of(ref, pl.multiple_of(start, width), width)

            return [Move(self.fold(own, self.next), self.next, "rep", 2, other)]
        if stage == "y":
            self.next = shape[:1] + shape[2:]
            fold = self.fold(lambda ref: ref.at[:, place_of() % 2], self.next)
            return [Move(fold, self.next, "blk", 1, lambda ref: ref.at[:, 1 - place_of() % 2])]
        if stage == "z":
            length = shape[0]
            self.next = shape[1:]
            fold = self.fold(lambda ref: ref.at[place_of() // 2], self.next)
            return [
                Move(fold, self.next, "blk", 2 * k,
                     lambda ref, k=k: ref.at[flipped(place_of() // 2, k, length)])
                for k in range(1, length)
            ]
        if stage == "back":
            fold = self.fold()
            return [Move(fold, shape, "rep", k) for k in range(1, 4)]
        if stage == "back_x":
            return [Move(self.fold(), shape, "rep", 2)]
        return [Move(self.tensor, shape, "rep", 1), Move(self.other, shape, "rep", 1)]

    def absorb(self, stage, arrived, kept):
        if stage == "core":
            self.take = lambda ref: ref.at[:, :, place_of("rep") % 2]
        else:
            self.take = whole
        if kept:
            self.tensor = kept[0]
        if stage in ("back", "back_x", "back_core"):
            if stage == "back_x":
                self.other = arrived[0]
                return
            if stage == "back":
                self.result = [self.tensor] + list(arrived)
            else:
                self.result = [self.tensor, arrived[0], self.other, arrived[1]]
            return
        self.shape, self.arrived = self.next, list(arrived)


class Exchange:
    def __init__(self, pieces):
        self.pieces = pieces

    def moves(self, stage):
        return [Move(one, one.shape, "blk", k) for k, one in enumerate(self.pieces) if k]

    def absorb(self, stage, arrived, kept):
        self.result = self.pieces[:1] + list(arrived)


class Pieces:
    def __init__(self, tensor, part, start, width):
        self.tensor, self.part, self.start, self.width = tensor, part, start, width

    def moves(self, stage):
        part, span = self.part, slice(self.start, self.start + self.width)
        count = lax.axis_size("blk")
        return [
            Move(self.tensor, (part, self.width), "blk", k,
                 lambda ref, k=k: ref.at[at(flipped(place_of(), k, count), part), span])
            for k in range(1, count)
        ]

    def absorb(self, stage, arrived, kept):
        self.result = list(arrived)


class Gather:
    def __init__(self, tensor):
        self.tensor = tensor

    def moves(self, stage):
        return [
            Move(self.tensor, self.tensor.shape, "blk", k) for k in range(1, lax.axis_size("blk"))
        ]

    def absorb(self, stage, arrived, kept):
        self.result = [self.tensor] + list(arrived)


class Spread:
    def __init__(self, tensor):
        self.tensor = tensor

    def moves(self, stage):
        count = lax.axis_size("blk")
        rows, width = self.tensor.shape[0], self.tensor.shape[1] // 2
        moves, self.places = [], []
        for number in range(2):
            span = slice(number * width, (number + 1) * width)
            own = lambda ref, span=span: ref.at[:, span]
            along = []
            for k in range(2, count, 2):
                along.append(Move(self.tensor, (rows, width), "blk", k, own, number))
                self.places.append((number, k))
            moves += along
            moves.append(Move(self.tensor, (rows, width), "blk", 1, own, number + 1))
            self.places.append((number, 1))
            for one in along:
                moves.append(Move(one, (rows, width), "blk", 1, whole, number + 1))
                self.places.append((number, one.flip + 1))
        return moves

    def absorb(self, stage, arrived, kept):
        found = dict(zip(self.places, arrived))
        count = lax.axis_size("blk")
        self.result = [found[number, k] for number in range(2) for k in range(1, count)]


class Norms:
    def __init__(self, tensor):
        self.tensor = tensor

    def moves(self, stage):
        axis = "rep" if stage == "out" else "blk"
        count = lax.axis_size(axis)
        shape = self.tensor.shape
        if stage == "out":
            return [Move(self.tensor, shape, axis, k) for k in range(1, count)]
        fold = Fold(self.tensor, whole, self.arrived, shape)
        return [
            Move(fold, shape[1:], axis, k,
                 lambda ref, k=k: ref.at[flipped(place_of(), k, count)])
            for k in range(1, count)
        ]

    def absorb(self, stage, arrived, kept):
        if stage == "out":
            self.arrived = list(arrived)
        else:
            self.result = [kept[0]] + list(arrived)


VMEM = pl.BlockSpec(memory_space=pltpu.VMEM)
SMEM = pl.BlockSpec(memory_space=pltpu.SMEM)
ANY = pl.BlockSpec(memory_space=pl.ANY)


def like(*shape, kind=NARROW):
    return jax.ShapeDtypeStruct(shape, kind)


def index_of(items, item):
    return next(k for k, one in enumerate(items) if one is item)


def call(
    kernel, outs, operands, specs, scratch, flops, grid=None, out_specs=None, semaphores=0,
    moves=(), ident=None, ticking=False, lazy=(), early=(),
):
    scratch = [pltpu.VMEM(shape, kind) for shape, kind in scratch]
    if semaphores:
        scratch.append(pltpu.SemaphoreType.DMA((semaphores,)))
    out_specs = [VMEM] * len(outs) if out_specs is None else out_specs
    extra = {} if grid is None else {"grid": grid}
    params = {}
    sources, folds = [], []

    def need(array):
        if not any(array is one for one in sources):
            sources.append(array)

    for move in moves:
        if isinstance(move.source, Fold):
            if not any(move.source is one for one in folds):
                folds.append(move.source)
                for array in [move.source.own] + move.source.arrived:
                    need(array)
        elif move.late is None and not isinstance(move.source, Move):
            need(move.source)
    fixed_in, fixed_out = len(operands), len(outs)
    partners = sorted({(move.axis, move.flip) for move in moves})
    lasts = max([move.phase for move in moves], default=0)
    held_in = [k for k, spec in enumerate(specs) if spec is VMEM]
    held_out = [k for k, spec in enumerate(out_specs) if spec is VMEM]
    own_scratch = len(scratch)
    scratch += [pltpu.VMEM(operands[k].shape, operands[k].dtype) for k in held_in]
    scratch += [pltpu.VMEM(outs[k].shape, outs[k].dtype) for k in held_out]
    terms = sum(1 + len(fold.arrived) for fold in folds)
    for fold in folds:
        scratch += [pltpu.VMEM(fold.shape, NARROW)] * (1 + len(fold.arrived))
    for number in (len(held_in), len(held_out), terms, len(folds), len(moves), len(moves)):
        scratch.append(pltpu.SemaphoreType.DMA((max(number, 1),)))
    if moves:
        params = {"collective_id": ident, "has_side_effects": True}
    before = {}
    for move in moves:
        if isinstance(move.source, Move):
            number = index_of(moves, move.source)
            before[number] = min(move.phase, before.get(number, move.phase))

    def body_kernel(*refs):
        ins, refs = list(refs[:fixed_in]), refs[fixed_in:]
        sent, refs = refs[: len(sources)], refs[len(sources) :]
        results, refs = list(refs[:fixed_out]), refs[fixed_out:]
        landed, refs = refs[: len(moves)], refs[len(moves) :]
        kept, refs = refs[: len(folds)], refs[len(folds) :]
        rest, refs = refs[:own_scratch], refs[own_scratch:]
        inner, refs = refs[: len(held_in)], refs[len(held_in) :]
        outer, refs = refs[: len(held_out)], refs[len(held_out) :]
        buffers, (in_sem, out_sem, load_sem, keep_sem, send_sem, recv_sem) = refs[:terms], refs[terms:]
        fetches, stores = {}, {}
        for number, k in enumerate(held_in):
            fetches[k] = pltpu.make_async_copy(ins[k], inner[number], in_sem.at[number])
            ins[k] = inner[number]
        for number, k in enumerate(held_out):
            stores[k] = pltpu.make_async_copy(outer[number], results[k], out_sem.at[number])
            results[k] = outer[number]

        def target(axis, flip):
            return {axis: flipped(lax.axis_index(axis), flip, lax.axis_size(axis))}

        def buffers_of(fold):
            start = sum(1 + len(one.arrived) for one in folds[: index_of(folds, fold)])
            return start, buffers[start : start + 1 + len(fold.arrived)]

        def made(k):
            move = moves[k]
            if move.late is not None:
                source = results[move.late]
            elif isinstance(move.source, Fold):
                source = buffers_of(move.source)[1][0]
            elif isinstance(move.source, Move):
                source = landed[index_of(moves, move.source)]
            else:
                source = sent[index_of(sources, move.source)]
            return pltpu.make_async_remote_copy(
                src_ref=move.take(source),
                dst_ref=landed[k],
                send_sem=send_sem.at[k],
                recv_sem=recv_sem.at[k],
                device_id=target(move.axis, move.flip),
                device_id_type=pl.DeviceIdType.MESH,
            )

        def loads(fold):
            start, held = buffers_of(fold)
            return [
                pltpu.make_async_copy(
                    (fold.take if k == 0 else whole)(sent[index_of(sources, array)]),
                    held[k],
                    load_sem.at[start + k],
                )
                for k, array in enumerate([fold.own] + fold.arrived)
            ]

        def keeping(k):
            fold = folds[k]
            return pltpu.make_async_copy(
                fold.keep(buffers_of(fold)[1][0]), kept[k], keep_sem.at[k]
            )

        def add(fold):
            held = buffers_of(fold)[1]

            def one(index):
                if len(held) == 2:
                    held[0][index] = held[0][index] + held[1][index]
                elif len(held) > 2:
                    held[0][index] = functools.reduce(
                        jnp.add, [part[index].astype(SINGLE) for part in held]
                    ).astype(NARROW)

            if len(fold.shape) == 2:
                one((slice(None), slice(None)))
            else:
                loop(fold.shape[0], one)

        def begin():
            for fold in folds:
                for load in loads(fold):
                    load.start()
            for fetch in fetches.values():
                fetch.start()
            if moves:
                barrier = pltpu.get_barrier_semaphore()
                for axis, flip in partners:
                    pl.semaphore_signal(
                        barrier, inc=1, device_id=target(axis, flip),
                        device_id_type=pl.DeviceIdType.MESH,
                    )
                pl.semaphore_wait(barrier, len(partners))
            for k, move in enumerate(moves):
                if move.phase == 0 and move.late is None and not isinstance(move.source, Fold):
                    made(k).start()
            for number, fold in enumerate(folds):
                for load in loads(fold):
                    load.wait()
                add(fold)
                for k, move in enumerate(moves):
                    if move.source is fold:
                        made(k).start()
                keeping(number).start()
            for k, fetch in fetches.items():
                if k not in lazy:
                    fetch.wait()

        def launch(which):
            for k in range(len(moves)):
                if moves[k].late == which and moves[k].phase == 0:
                    made(k).start()

        def tick(phase):
            for k, needed in before.items():
                if needed == phase:
                    made(k).wait_recv()
            for k, move in enumerate(moves):
                if move.phase == phase:
                    made(k).start()

        def finish():
            for k, store in stores.items():
                if k not in early:
                    store.start()
            if not ticking:
                for phase in range(1, lasts + 1):
                    tick(phase)
            for k in range(len(moves)):
                made(k).wait_send()
                if k not in before:
                    made(k).wait_recv()
            for k in range(len(folds)):
                keeping(k).wait()
            for store in stores.values():
                store.wait()

        options = {}
        if any(move.late is not None for move in moves):
            options["launch"] = launch
        if ticking:
            options["tick"] = tick
        if lazy:
            options["ready"] = lambda k: fetches[k].wait()
        if early:
            options["flush"] = lambda k: stores[k].start()
        if grid is None:
            begin()
            kernel(*ins, *results, *rest, **options)
            finish()
        else:
            pl.when(pl.program_id(0) == 0)(begin)
            kernel(*ins, *results, *rest, **options)
            pl.when(pl.program_id(0) == pl.num_programs(0) - 1)(finish)

    result = pl.pallas_call(
        body_kernel,
        out_shape=list(outs)
        + [
            like(*m.shape, kind=m.dtype)
            for m in moves
        ]
        + [like(*fold.keep_shape) for fold in folds],
        in_specs=[ANY if spec is VMEM else spec for spec in specs] + [ANY] * len(sources),
        out_specs=[ANY if spec is VMEM else spec for spec in out_specs]
        + [ANY] * (len(moves) + len(folds)),
        scratch_shapes=scratch,
        compiler_params=pltpu.CompilerParams(vmem_limit_bytes=60 * 2**20, **params),
        cost_estimate=pl.CostEstimate(
            flops=int(flops),
            bytes_accessed=sum(o.size * o.dtype.itemsize for o in operands),
            transcendentals=0,
        ),
        **extra,
    )(*operands, *sources)
    end = fixed_out + len(moves)
    return list(result[:fixed_out]), list(result[fixed_out:end]), (folds, list(result[end:]))


def finale(kernel, outs, stages, results, scratch, ident):
    plan = []
    for stage in stages:
        for job, name in stage:
            moves = job.moves(name)
            folds = []
            for move in moves:
                known = folds + [fold for part, _ in plan for fold in part]
                if isinstance(move.source, Fold) and not any(move.source is one for one in known):
                    folds.append(move.source)
            job.absorb(name, moves, folds)
            plan.append((folds, moves))
    items = results()
    moves = [move for _, part in plan for move in part]
    folds = [fold for part, _ in plan for fold in part]
    sources, fetched = [], []

    def need(item):
        if not isinstance(item, (Fold, Move)) and not any(item is one for one in sources):
            sources.append(item)

    for fold in folds:
        for item in [fold.own] + fold.arrived:
            need(item)
            if not isinstance(item, (Fold, Move)):
                fetched.append((fold, item))
    for move in moves:
        need(move.source)
    plain_items = []
    for item in items:
        need(item)
        if not isinstance(item, (Fold, Move)):
            plain_items.append(item)
    partners = sorted({(move.axis, move.flip) for move in moves})
    shapes = [pltpu.VMEM(one.shape, one.dtype) for one in scratch]
    shapes += [pltpu.VMEM(move.shape, move.dtype) for move in moves]
    shapes += [pltpu.VMEM(fold.shape, fold.dtype) for fold in folds]
    shapes += [pltpu.VMEM(fold.shape, fold.dtype) for fold, _ in fetched]
    shapes += [pltpu.VMEM(item.shape, item.dtype) for item in plain_items]
    shapes += [pltpu.VMEM(one.shape, one.dtype) for one in outs]
    for number in (len(moves), len(moves), len(fetched), len(plain_items), len(outs)):
        shapes.append(pltpu.SemaphoreType.DMA((max(number, 1),)))

    def body_kernel(*refs):
        def take(count):
            nonlocal refs
            some, refs = refs[:count], refs[count:]
            return some

        sent, finals = take(len(sources)), take(len(outs))
        rest, landed, sums = take(len(scratch)), take(len(moves)), take(len(folds))
        brought, held, outer = take(len(fetched)), take(len(plain_items)), take(len(outs))
        send_sem, recv_sem, load_sem, item_sem, out_sem = refs
        arrived = set()

        def target(axis, flip):
            return {axis: flipped(lax.axis_index(axis), flip, lax.axis_size(axis))}

        def place(item):
            if isinstance(item, Fold):
                return sums[index_of(folds, item)]
            if isinstance(item, Move):
                return landed[index_of(moves, item)]
            return sent[index_of(sources, item)]

        def made(move):
            k = index_of(moves, move)
            source = place(move.source)
            return pltpu.make_async_remote_copy(
                src_ref=move.take(source),
                dst_ref=landed[k],
                send_sem=send_sem.at[k],
                recv_sem=recv_sem.at[k],
                device_id=target(move.axis, move.flip),
                device_id_type=pl.DeviceIdType.MESH,
            )

        def arrival(item):
            if isinstance(item, Move) and index_of(moves, item) not in arrived:
                arrived.add(index_of(moves, item))
                made(item).wait_recv()

        loads = [
            pltpu.make_async_copy(
                (fold.take if item is fold.own else whole)(place(item)), brought[k], load_sem.at[k]
            )
            for k, (fold, item) in enumerate(fetched)
        ]
        fetches = [
            pltpu.make_async_copy(place(item), held[k], item_sem.at[k])
            for k, item in enumerate(plain_items)
        ]
        stores = [
            pltpu.make_async_copy(outer[k], finals[k], out_sem.at[k]) for k in range(len(outs))
        ]
        for load in loads:
            load.start()
        barrier = pltpu.get_barrier_semaphore()
        for axis, flip in partners:
            pl.semaphore_signal(
                barrier, inc=1, device_id=target(axis, flip), device_id_type=pl.DeviceIdType.MESH
            )
        pl.semaphore_wait(barrier, len(partners))

        def total(fold):
            terms = []
            for item in [fold.own] + fold.arrived:
                if isinstance(item, (Fold, Move)):
                    arrival(item)
                    term = place(item)
                    if item is fold.own:
                        term = fold.take(item.keep(term) if isinstance(item, Fold) else term)
                else:
                    k = next(
                        k for k, (one, other) in enumerate(fetched) if one is fold and other is item
                    )
                    loads[k].wait()
                    term = brought[k]
                terms.append(term)
            goal = place(fold)

            def one(index):
                goal[index] = functools.reduce(
                    jnp.add, [term[index].astype(SINGLE) for term in terms]
                ).astype(goal.dtype)

            if len(fold.shape) == 2:
                one((slice(None), slice(None)))
            else:
                loop(fold.shape[0], one)

        for number, (some, part) in enumerate(plan):
            for fold in some:
                total(fold)
            for move in part:
                arrival(move.source)
                made(move).start()
            if number == 0:
                for fetch in fetches:
                    fetch.start()
        operands = []
        for item in items:
            if isinstance(item, (Fold, Move)):
                operands.append(place(item))
            else:
                operands.append(held[next(k for k, one in enumerate(plain_items) if one is item)])
        for fetch in fetches:
            fetch.wait()

        def ready(k):
            arrival(items[k])

        kernel(*operands, *outer, *rest, ready=ready, flush=lambda k: stores[k].start())
        for move in moves:
            made(move).wait_send()
            arrival(move)
        for store in stores:
            store.wait()

    return pl.pallas_call(
        body_kernel,
        out_shape=list(outs),
        in_specs=[ANY] * len(sources),
        out_specs=[ANY] * len(outs),
        scratch_shapes=shapes,
        compiler_params=pltpu.CompilerParams(
            vmem_limit_bytes=60 * 2**20, collective_id=ident, has_side_effects=True
        ),
    )(*sources)


class Courier:
    def __init__(self, active):
        self.active, self.waiting, self.ident = active, [], 0

    def load(self, *jobs):
        self.waiting += jobs

    def run(self, kernel, outs, operands, specs, scratch, flops, **extra):
        jobs, self.waiting = self.waiting, []
        moves, ends = [], []
        for job, stage, *late in jobs:
            added = job.moves(stage)
            for move in added:
                if late and not isinstance(move.source, Move):
                    move.late = late[0]
            moves += added
            ends.append(len(moves))
        if moves:
            self.ident += 1
        results, arrived, (folds, kept) = call(
            kernel, outs, operands, specs, scratch, flops, moves=tuple(moves), ident=self.ident, **extra
        )
        start = 0
        for (job, stage, *late), end in zip(jobs, ends):
            if late:
                job.tensor = results[late[0]]
            own = [
                kept[k]
                for k, fold in enumerate(folds)
                if any(move.source is fold for move in moves[start:end])
            ]
            job.absorb(stage, arrived[start:end], own)
            start = end
        return results


def in_halves(arrays):
    width = arrays[0].shape[1] // 2
    return (
        arrays[:1] + [one[:, :width] for one in arrays[1:]] + [one[:, width:] for one in arrays[1:]]
    )


def body(
    patches,
    queries,
    window_valid,
    answer_length,
    norm_gain,
    norm_bias,
    attn_in,
    attn_out,
    mlp_in,
    mlp_out,
    cot_patches,
    cot_queries,
):
    x, q, cot_x, cot_q = patches[0], queries[0], cot_patches[0], cot_queries[0]
    rows, features = x.shape
    count = q.shape[0]
    hidden = mlp_in.shape[2]
    blocks = lax.axis_size("blk")
    place = lax.axis_index("blk").astype(jnp.int32)
    share = features // blocks
    hidden_share = hidden // blocks
    share_rows = -(-share // 16) * 16
    hidden_rows = -(-hidden_share // 16) * 16
    part = -(-count // (blocks * 16)) * 16
    padded = part * blocks
    wide = 3 * features
    last = wide + features + features
    causal_columns = -(-last // 512) * 512
    leader = (place == 0).astype(SINGLE)
    valid = jnp.where(jnp.repeat(window_valid[0], WIN) > 0, 0.0, MASKED).astype(SINGLE)
    carried = blocks == DIRECT and lax.axis_size("rep") == 4 and share % 32 == 0
    courier = Courier(carried)

    def own_columns(tensor):
        return lax.dynamic_slice_in_dim(tensor, place * share, share, 1)

    square = 2.0 * features * features
    run = courier.run

    n0, pw, mw, x1, nx, vq, ckv = run(
        window_forward,
        [
            like(rows, features), like(rows, wide), like(rows, features),
            like(rows, features, kind=SINGLE), like(rows, features), like(rows, features),
            like(rows, 2 * features),
        ],
        [x, norm_gain, norm_bias, attn_in, attn_out],
        [VMEM, VMEM, VMEM, ANY, ANY],
        [((features, wide), NARROW), ((features, features), NARROW),
         ((features, features), NARROW), ((features, 2 * features), NARROW)],
        rows * square * 9,
        semaphores=4,
        early=(0, 1, 2, 3, 4, 5),
    )
    n1, pq, mq, q1, nq, cq, vkv, log_q = run(
        causal_forward,
        [
            like(count, features), like(count, wide), like(count, features),
            like(padded, features, kind=SINGLE), like(padded, features), like(count, features),
            like(count, 2 * features), like(16, count, kind=SINGLE),
        ],
        [q, norm_gain, norm_bias, attn_in, attn_out],
        [VMEM, VMEM, VMEM, ANY, ANY],
        [((features, wide), NARROW), ((features, features), NARROW),
         ((features, features), NARROW), ((features, 2 * features), NARROW),
         ((count, PAIR), SINGLE)],
        count * square * 15,
        semaphores=4,
        early=(0, 1, 2, 3, 4, 5),
    )
    outs, *log_pieces = run(
        functools.partial(cross_forward, blocks),
        [like(padded, features)] + [like(16, part, kind=SINGLE)] * blocks,
        [cq, ckv, valid[None, :]],
        [VMEM, VMEM, VMEM],
        [((padded, PAIR), SINGLE)],
        count * square * 6,
    )
    logs = Exchange(log_pieces)
    first_width = features // 3
    halves = [
        Pieces(outs, part, 0, first_width),
        Pieces(outs, part, first_width, features - first_width),
    ]
    if carried:
        courier.load((logs, ""), (halves[0], ""))
    mv, x2, log_v = run(
        reverse_forward,
        [like(rows, features), like(rows, features, kind=SINGLE), like(16, rows, kind=SINGLE)],
        [answer_length, vq, vkv, x1, attn_out],
        [SMEM, VMEM, VMEM, VMEM, ANY],
        [((features, features), NARROW), ((rows, PAIR), SINGLE)],
        rows * square * 8,
        semaphores=1,
        lazy=(3,),
        early=(0,),
    )
    if carried:
        courier.load((halves[1], ""))
    x3, dx2, up_x, down_x, norm_five = run(
        patch_feed_forward,
        [
            like(rows, features), like(rows, features, kind=SINGLE), like(features, hidden),
            like(hidden, features), like(8, features, kind=SINGLE),
        ],
        [x2, cot_x, norm_gain, norm_bias, mlp_in, mlp_out],
        [
            VMEM, VMEM, VMEM, VMEM,
            pl.BlockSpec((1, features, CHUNK), lambda j: (0, 0, j)),
            pl.BlockSpec((1, CHUNK, features), lambda j: (0, j, 0)),
        ],
        [((rows, features), NARROW), ((rows, CHUNK), NARROW), ((rows, CHUNK), NARROW),
         ((rows, features), SINGLE), ((rows, features), SINGLE)],
        rows * square * 24,
        grid=(hidden // CHUNK,),
        out_specs=[
            VMEM, VMEM,
            pl.BlockSpec((features, CHUNK), lambda j: (0, j)),
            pl.BlockSpec((CHUNK, features), lambda j: (j, 0)),
            VMEM,
        ],
    )
    if carried:
        merged = run(
            functools.partial(merge_blocks, blocks),
            [like(part, features), like(16, part, kind=SINGLE)],
            [outs] + logs.result + halves[0].result + halves[1].result,
            [VMEM] * (3 * blocks - 1),
            [],
            padded * square,
        )
        co_parts, log_parts = Spread(merged[0]), Gather(merged[1])
        up_x, down_x = Reduction(up_x), Reduction(down_x)
        reverse_weight = Reduction(like(blocks // 2, 2, 2, share // 2, 2 * features))
        courier.load(
            (co_parts, ""), (log_parts, ""), (up_x, "core"), (down_x, "core"),
            (reverse_weight, "core", 1),
        )
    else:
        whole_logs = jnp.stack(exchange(log_pieces))
        merged_log = jax.nn.logsumexp(whole_logs, axis=0)
        weights = jnp.transpose(jnp.exp(whole_logs - merged_log)[:, :HEADS], (0, 2, 1))
        shares = lax.all_to_all(outs.reshape(blocks, part, features), "blk", 0, 0)
        merged_out = jnp.sum(jnp.repeat(weights, HEAD, axis=2) * shares.astype(SINGLE), axis=0)
        co_parts, log_parts = Spread(None), Gather(None)
        co_parts.tensor, *co_parts.result = in_halves(gather(merged_out.astype(NARROW)))
        log_parts.result = gather(merged_log)
    folded = (blocks // 2, 2, 2, share // 2) if carried else (features,)
    dvq, reverse_grad, *kv_pieces = run(
        functools.partial(reverse_backward, blocks),
        [like(rows, features), like(*folded, 2 * features)]
        + [like(part, features)] * (2 * blocks),
        [answer_length, dx2, mv, vq, vkv, nx, log_v, attn_out],
        [SMEM, VMEM, VMEM, VMEM, VMEM, VMEM, VMEM, ANY],
        [((features, features), NARROW), ((rows, features), NARROW), ((rows, features), NARROW),
         ((16, rows), SINGLE), ((padded, 2 * features), SINGLE)],
        rows * square * 16,
        semaphores=1,
        ticking=carried,
        lazy=(3, 4, 5, 6),
    )
    k_parts, v_parts = Exchange(kv_pieces[:blocks]), Exchange(kv_pieces[blocks:])
    if carried:
        courier.load((k_parts, ""), (up_x, "x"))
    else:
        k_parts.result, v_parts.result = exchange(k_parts.pieces), exchange(v_parts.pieces)
    q3, dq2, up_q, down_q, norm_four, co = run(
        functools.partial(query_feed_forward, blocks, share, hidden_share),
        [
            like(count, features), like(count, features, kind=SINGLE), like(share_rows, hidden),
            like(hidden_rows, features), like(8, features, kind=SINGLE), like(padded, features),
        ],
        [q1, cot_q, norm_gain, norm_bias, attn_out, mlp_in, mlp_out, co_parts.tensor]
        + co_parts.result,
        [
            VMEM, VMEM, VMEM, VMEM, pl.BlockSpec((1, features, features), lambda j: (2, 0, 0)),
            pl.BlockSpec((1, features, CHUNK), lambda j: (1, 0, j)),
            pl.BlockSpec((1, CHUNK, features), lambda j: (1, j, 0)),
        ] + [ANY] * (2 * blocks - 1),
        [((count, features), SINGLE), ((count, features), NARROW), ((share_rows, count), NARROW),
         ((count, CHUNK), NARROW), ((count, CHUNK), NARROW),
         ((count, features), SINGLE), ((count, features), SINGLE)],
        count * square * 18,
        semaphores=2 * blocks - 1,
        grid=(hidden // CHUNK,),
        out_specs=[
            VMEM, VMEM,
            pl.BlockSpec((share_rows, CHUNK), lambda j: (0, j)),
            VMEM, VMEM, VMEM,
        ],
    )
    if carried:
        up_q, down_q = Reduction(up_q, 1), Reduction(down_q, 1)
        courier.load((v_parts, ""), (down_x, "x"), (up_x, "y"), (up_q, "core"), (down_q, "core"))
    dckv, cross_out_weight, *q_pieces = run(
        functools.partial(cross_backward, blocks, share),
        [like(rows, 2 * features), like(share_rows, features)] + [like(part, features)] * blocks,
        [dq2, co, cq, ckv, valid[:, None], attn_out] + log_parts.result,
        [VMEM, VMEM, VMEM, VMEM, VMEM, ANY] + [VMEM] * blocks,
        [((features, features), NARROW), ((count, features), NARROW), ((count, features), NARROW),
         ((16, count), SINGLE), ((padded, PAIR), SINGLE), ((16, count), SINGLE),
         ((padded, features), NARROW), ((rows, 2 * features), SINGLE)],
        count * square * 12,
        semaphores=1,
        lazy=(2, 3),
    )
    q_parts = Exchange(q_pieces)
    if carried:
        kv_weight = Reduction(like(blocks // 2, 2, 2, share // 2, 2 * features))
        window_weight = Reduction(like(blocks // 2, 2, 2, share // 2, 4 * features))
        courier.load(
            (q_parts, ""), (down_x, "y"), (reverse_weight, "x"), (up_q, "x"), (down_q, "x"),
            (kv_weight, "core", 0), (window_weight, "core", 1),
        )
    else:
        q_parts.result = exchange(q_pieces)
    kv_grad, window_grad, grad_x, norm_x = run(
        patch_backward,
        [
            like(*folded, 2 * features), like(*folded, 4 * features),
            like(rows, features, kind=SINGLE), like(8, features, kind=SINGLE),
        ],
        [x, dx2, x1, nx, n0, pw, mw, dvq, dckv, norm_gain, attn_in, attn_out],
        [VMEM] * 10 + [ANY, ANY],
        [((features, wide), NARROW), ((features, features), NARROW),
         ((features, features), NARROW), ((features, 2 * features), NARROW),
         ((rows, features), SINGLE), ((rows, features), NARROW), ((rows, features), NARROW),
         ((16, rows), SINGLE), ((rows, wide), NARROW)],
        rows * square * 24,
        semaphores=4,
        lazy=(0, 4, 5, 6),
        early=(0, 1),
    )
    if carried:
        share_weight = Reduction(like(blocks // 2, 2, 2, share // 2, wide))
        dq1_parts = Spread(like(part, features))
        courier.load(
            (share_weight, "core", 1), (dq1_parts, "", 0), (window_weight, "x"),
            (reverse_weight, "y"), (up_q, "back_x"), (down_q, "back_x"),
        )
    dq1_share, share_grad, norm_two = run(
        functools.partial(share_backward, blocks),
        [like(part, features), like(*folded, wide), like(8, features, kind=SINGLE)],
        [q1, nq, norm_gain, attn_in]
        + q_parts.result + k_parts.result + v_parts.result,
        [ANY, ANY, VMEM, ANY] + [VMEM] * (3 * blocks),
        [((features, features), NARROW), ((features, 2 * features), NARROW),
         ((part, wide), NARROW), ((part, features), SINGLE), ((part, features), NARROW)],
        part * square * 6,
        semaphores=4,
    )
    if carried:
        courier.load(
            (window_weight, "y"), (share_weight, "x"), (kv_weight, "x"), (down_x, "z"),
            (reverse_weight, "z"), (up_q, "back_core"), (down_q, "back_core"), (up_x, "z"),
        )
    else:
        dq1_parts = Spread(None)
        dq1_parts.tensor, *dq1_parts.result = in_halves(gather(dq1_share))
    causal_weight, grad_q, norm_one = run(
        functools.partial(causal_backward, blocks, share),
        [
            like(share_rows, causal_columns), like(count, features, kind=SINGLE),
            like(8, features, kind=SINGLE),
        ],
        [q, dq2, n1, pq, mq, log_q, cross_out_weight, norm_gain, attn_in, attn_out]
        + [dq1_parts.tensor] + dq1_parts.result,
        [VMEM] * 8 + [ANY] * (2 * blocks + 1),
        [((features, wide), NARROW), ((features, features), NARROW), ((padded, features), NARROW),
         ((count, features), SINGLE), ((count, features), NARROW), ((count, features), NARROW),
         ((16, count), SINGLE), ((count, 2 * PAIR), SINGLE), ((count, wide), NARROW)],
        count * square * 16,
        semaphores=2 * blocks + 1,
        lazy=(2, 3, 4, 5),
    )
    gains = jnp.stack(
        (norm_x[2], norm_one[0] * leader, norm_two[0], norm_x[0], norm_four[0] * leader, norm_five[0])
    )
    biases = jnp.stack(
        (norm_x[3], norm_one[1] * leader, norm_two[1], norm_x[1], norm_four[1] * leader, norm_five[1])
    )
    rest = (
        x3[None],
        own_columns(q3)[None],
        grad_x[None],
        own_columns(grad_q)[None],
    )
    if carried:
        norms = jnp.concatenate((jnp.pad(gains, ((0, 2), (0, 0))), jnp.pad(biases, ((0, 2), (0, 0)))))
        norms = jnp.transpose(norms.reshape(16, blocks, share), (1, 0, 2))
        norms = Norms(jnp.pad(norms, ((0, 0), (0, 0), (0, -share % PAIR))))
        causal_weight = Reduction(causal_weight, 1)
        sums = [
            up_x, down_x, reverse_weight, window_weight, kv_weight, share_weight, up_q, down_q,
            causal_weight,
        ]
        grads = finale(
            functools.partial(assemble, len(sums), blocks),
            [
                like(4, share, wide), like(4, share, features), like(2, share, hidden),
                like(2, hidden_share, features),
                like(6, share, kind=SINGLE), like(6, share, kind=SINGLE),
            ],
            [
                [
                    (causal_weight, "core"), (norms, "out"), (share_weight, "y"), (kv_weight, "y"),
                    (window_weight, "z"), (up_x, "back_x"), (down_x, "back_x"),
                    (reverse_weight, "back_x"),
                ],
                [
                    (causal_weight, "x"), (norms, "back"), (kv_weight, "z"), (share_weight, "z"),
                    (up_x, "back_core"), (down_x, "back_core"), (reverse_weight, "back_core"),
                    (window_weight, "back_x"),
                ],
                [
                    (causal_weight, "back_x"), (kv_weight, "back_x"), (share_weight, "back_x"),
                    (window_weight, "back_core"),
                ],
                [
                    (causal_weight, "back_core"), (kv_weight, "back_core"),
                    (share_weight, "back_core"),
                ],
            ],
            lambda: sum([one.result for one in sums], []) + norms.result,
            [like(share, 4 * features), like(share, causal_columns)],
            courier.ident + 1,
        )
        return rest + (grads[4], grads[5]) + tuple(one.astype(SINGLE) for one in grads[:4])
    up_x, down_x, reverse_weight, window_weight, kv_weight, share_weight = (
        reduce_all(one) for one in (up_x, down_x, reverse_grad, window_grad, kv_grad, share_grad)
    )
    up_q, down_q = reduce_rep(up_q[:share]), reduce_rep(down_q[:hidden_share])
    causal_weight = reduce_rep(causal_weight[:share])
    gains, biases = (
        own_columns(one) for one in lax.psum((gains, biases), ("blk", "rep"))
    )
    grad_attn_in = jnp.stack(
        (
            window_weight[:, :wide],
            causal_weight[:, :wide],
            jnp.concatenate((share_weight[:, :features], kv_weight), axis=1),
            jnp.concatenate((reverse_weight[:, :features], share_weight[:, features:]), axis=1),
        )
    )
    grad_attn_out = jnp.stack(
        (
            window_weight[:, wide:],
            causal_weight[:, wide : wide + features],
            causal_weight[:, wide + features : last],
            reverse_weight[:, features:],
        )
    )
    return rest + (
        gains,
        biases,
        grad_attn_in.astype(SINGLE),
        grad_attn_out.astype(SINGLE),
        jnp.stack((up_x, up_q)).astype(SINGLE),
        jnp.stack((down_x, down_q)).astype(SINGLE),
    )


def solution(mesh):
    placed = (
        P("rep", "blk", None),
        P("rep", None, None),
        P("rep", "blk"),
        P("rep"),
        P(),
        P(),
        P(),
        P(),
        P(),
        P(),
        P("rep", "blk", None),
        P("rep", None, None),
    )
    return jax.shard_map(
        body,
        mesh=mesh,
        in_specs=placed,
        out_specs=(
            P("rep", "blk", None),
            P("rep", None, "blk"),
            P("rep", "blk", None),
            P("rep", None, "blk"),
            P(None, "blk"),
            P(None, "blk"),
            P(None, "blk", None),
            P(None, "blk", None),
            P(None, "blk", None),
            P(None, "blk", None),
        ),
        check_vma=False,
    )
```

```python
import functools
import math

import jax
import jax.numpy as jnp
from jax import lax
from jax.experimental import pallas as pl
from jax.experimental.pallas import tpu as pltpu
from jax.sharding import PartitionSpec as P

HEADS = 12
WIN = 64
EPSILON = 1e-05
MASKED = -1e30
NARROW = jnp.bfloat16
SINGLE = jnp.float32
GROUP = 128
WINDOWS = 256
PAIR = 128
HEAD = 64
STRIP = 160
LONG = 400
CHUNK = 768


def dot(former, latter, ahead, behind, precision=None):
    return lax.dot_general(
        former,
        latter,
        (((ahead,), (behind,)), ((), ())),
        preferred_element_type=SINGLE,
        precision=precision,
    )


def plain(former, latter):
    return dot(former, latter, 1, 0)


def right_t(former, latter):
    return dot(former, latter, 1, 1)


def left_t(former, latter):
    return dot(former, latter, 0, 0)


def loop(count, action):
    def step(index, nothing):
        action(index)
        return nothing

    lax.fori_loop(0, count, step, 0)


def at(index, size):
    return pl.ds(pl.multiple_of(index * size, size), size)


def iota(shape, dim):
    return lax.broadcasted_iota(jnp.int32, shape, dim)


def statistics(tensor):
    average = jnp.mean(tensor, axis=-1, keepdims=True)
    centred = tensor - average
    spread = jnp.mean(centred * centred, axis=-1, keepdims=True)
    return centred, lax.rsqrt(spread + EPSILON)


def norm(tensor, gain, bias):
    centred, inverse = statistics(tensor)
    return centred * inverse * gain + bias


def norm_back(tensor, gain, upstream):
    centred, inverse = statistics(tensor)
    scaled = centred * inverse
    inner = upstream * gain
    grad = inverse * (
        inner
        - jnp.mean(inner, axis=-1, keepdims=True)
        - scaled * jnp.mean(inner * scaled, axis=-1, keepdims=True)
    )
    return (
        grad,
        jnp.sum(upstream * scaled, axis=0, keepdims=True),
        jnp.sum(upstream, axis=0, keepdims=True),
    )


def gelu_both(tensor):
    size = jnp.abs(tensor)
    ratio = 1.0 / (1.0 + (0.3275911 * math.sqrt(0.5)) * size)
    series = ratio * (
        0.254829592
        + ratio * (-0.284496736 + ratio * (1.421413741 + ratio * (-1.453152027 + ratio * 1.061405429)))
    )
    bell = jnp.exp(-0.5 * (tensor * tensor))
    tail = 0.5 * series * bell
    below = jnp.where(tensor >= 0, 1.0 - tail, tail)
    return tensor * below, below + tensor * bell * (1.0 / math.sqrt(2.0 * math.pi))


def half(which, value=1.0):
    return jnp.where(iota((1, PAIR), 1) // HEAD == which, value, 0.0).astype(NARROW)


def lower_lanes():
    return iota((1, PAIR), 1) < HEAD


def both(tensor, value=1.0):
    return jnp.concatenate((tensor * half(0, value), tensor * half(1, value)), axis=0)


def attend(queries, keys, values, mask):
    rows = queries.shape[0]
    scores = right_t(both(queries, 1.0 / math.sqrt(HEAD)), keys)
    weights, totals, logs = [], [], []
    for which in range(2):
        part = mask(scores[which * rows : (which + 1) * rows])
        peak = jnp.max(part, axis=-1, keepdims=True)
        part = jnp.exp(part - peak)
        total = jnp.sum(part, axis=-1, keepdims=True)
        weights.append(part.astype(NARROW))
        totals.append(1.0 / total)
        logs.append(peak + jnp.log(total))
    out = plain(jnp.concatenate(weights, axis=0), values)
    return jnp.where(lower_lanes(), out[:rows] * totals[0], out[rows:] * totals[1]), logs


def attend_back(queries, keys, values, upstream, logs, deltas, mask):
    scaled = queries * jnp.asarray(1.0 / math.sqrt(HEAD), NARROW)
    count = keys.shape[0]
    keys = both(keys)
    turned_keys = keys.T
    scores = right_t(keys, scaled)
    inner = right_t(both(values), upstream)
    weights, slopes = [], []
    for which in range(2):
        span = slice(which * count, (which + 1) * count)
        part = mask(scores[span])
        if logs is None:
            part = jnp.exp(part - jnp.max(part, axis=0, keepdims=True))
            part = part * (1.0 / jnp.sum(part, axis=0, keepdims=True))
        else:
            part = jnp.exp(part - logs[which])
        weights.append(part.astype(NARROW))
        slopes.append((part * (inner[span] - deltas[which])).astype(NARROW))
    slope = jnp.concatenate(slopes, axis=0)
    query_grad = plain(turned_keys, slope).T
    key_grad = plain(slope, scaled)
    value_grad = plain(jnp.concatenate(weights, axis=0), upstream)
    lanes = lower_lanes()
    return (
        query_grad,
        jnp.where(lanes, key_grad[:count], key_grad[count:]),
        jnp.where(lanes, value_grad[:count], value_grad[count:]),
    )


def exact_parts(tensor, count):
    parts = []
    for _ in range(count):
        parts.append(tensor.astype(NARROW))
        tensor = tensor - parts[-1].astype(SINGLE)
    return parts


def head_rows(tensor):
    features = tensor.shape[1]
    heads = 16
    chosen = jnp.where(
        iota((heads, features), 1) // HEAD == iota((heads, features), 0), 1.0, 0.0
    ).astype(NARROW)
    return functools.reduce(jnp.add, [right_t(chosen, part) for part in exact_parts(tensor, 2)])


def turn(columns):
    same = jnp.where(iota((16, columns.shape[1]), 0) == iota((16, columns.shape[1]), 1), 1.0, 0.0)
    same = same.astype(NARROW)
    return functools.reduce(jnp.add, [right_t(same, part) for part in exact_parts(columns, 3)])


def row_pair(ref, pair, span):
    tensor = ref[:, span]
    index = iota(tensor.shape, 0)
    return [
        jnp.sum(jnp.where(index == 2 * pair + which, tensor, 0.0), axis=0, keepdims=True)
        for which in range(2)
    ]


def chooser(rows, width, start, count):
    row = iota((rows, width), 0)
    hit = jnp.logical_and(iota((rows, width), 1) == row + start, row < count)
    return jnp.where(hit, 1.0, 0.0).astype(NARROW)


def spans(rows, size):
    edges = [(start, min(start + size, rows)) for start in range(0, rows, size)]
    if len(edges) > 1 and edges[-1][1] - edges[-1][0] < PAIR:
        edges[-2:] = [(edges[-2][0], rows)]
    return edges


def mark(log_ref, rows, head, value):
    log_ref[rows, :] = jnp.where(iota((1, PAIR), 1) == head, value, log_ref[rows, :])


def store_rows(ref, columns, value):
    ref[(slice(None),) * (len(ref.shape) - 1) + (columns,)] = value.astype(ref.dtype).reshape(
        ref.shape[:-1] + value.shape[1:]
    )


def nothing(*unused):
    return None


def copies(semaphores, *pairs):
    made = [
        pltpu.make_async_copy(source, target, semaphores.at[k])
        for k, (source, target) in enumerate(pairs)
    ]
    for one in made:
        one.start()
    return made


DIRECT = 8


def place_of(axis="blk"):
    return lax.axis_index(axis)


def flipped(index, mask, count):
    total, weight = 0, 1
    while weight < count:
        bit = (index // weight) % 2
        total = total + weight * ((1 - bit) if mask & weight else bit)
        weight *= 2
    return total


def piece_at(number, count):
    return flipped(place_of(), number, count) if count <= DIRECT else number


def window_forward(
    x_ref, gain_ref, bias_ref, a_in, a_out,
    n0_ref, pw_ref, mw_ref, x1_ref, nx_ref, vq_ref, ckv_ref,
    w_in, w_out, w_q, w_kv, sem,
    flush=nothing,
):
    rows, features = x_ref.shape
    loads = copies(
        sem,
        (a_in.at[0], w_in),
        (a_out.at[0], w_out),
        (a_in.at[3, :, pl.ds(0, features)], w_q),
        (a_in.at[2, :, pl.ds(features, 2 * features)], w_kv),
    )

    def first(i):
        span = at(i, GROUP)
        n0_ref[span, :] = norm(
            x_ref[span, :].astype(SINGLE), gain_ref[0:1, :], bias_ref[0:1, :]
        ).astype(NARROW)

    loop(rows // GROUP, first)
    loads[0].wait()

    def project(j):
        span = at(j, CHUNK)
        pw_ref[:, span] = plain(n0_ref[...], w_in[:, span]).astype(NARROW)

    loop(3 * features // CHUNK, project)
    flush(0)
    flush(1)
    window = jnp.where(
        iota((WINDOWS, WINDOWS), 0) // WIN == iota((WINDOWS, WINDOWS), 1) // WIN, 0.0, MASKED
    )

    def group(i):
        span = at(i, WINDOWS)
        for pair in range(features // PAIR):
            lane = pair * PAIR
            out, unused = attend(
                pw_ref[span, lane : lane + PAIR],
                pw_ref[span, features + lane : features + lane + PAIR],
                pw_ref[span, 2 * features + lane : 2 * features + lane + PAIR],
                lambda scores: scores + window,
            )
            mw_ref[span, lane : lane + PAIR] = out.astype(NARROW)

    loop(rows // WINDOWS, group)
    flush(2)
    loads[1].wait()

    def second(i):
        span = at(i, GROUP)
        total = x_ref[span, :].astype(SINGLE) + plain(mw_ref[span, :], w_out[...])
        x1_ref[span, :] = total
        nx_ref[span, :] = norm(total, gain_ref[3:4, :], bias_ref[3:4, :]).astype(NARROW)

    loop(rows // GROUP, second)
    flush(3)
    flush(4)
    loads[2].wait()
    vq_ref[...] = plain(nx_ref[...], w_q[...]).astype(NARROW)
    flush(5)
    loads[3].wait()

    def third(j):
        span = at(j, CHUNK)
        ckv_ref[:, span] = plain(nx_ref[...], w_kv[:, span]).astype(NARROW)

    loop(2 * features // CHUNK, third)


def causal_forward(
    q_ref, gain_ref, bias_ref, a_in, a_out,
    n1_ref, pq_ref, mq_ref, q1_ref, nq_ref, cq_ref, vkv_ref, log_ref,
    w_in, w_out, w_q, w_kv, logs, sem,
    flush=nothing,
):
    rows, features = q_ref.shape
    loads = copies(
        sem,
        (a_in.at[1], w_in),
        (a_out.at[1], w_out),
        (a_in.at[2, :, pl.ds(0, features)], w_q),
        (a_in.at[3, :, pl.ds(features, 2 * features)], w_kv),
    )

    def first(i):
        span = at(i, STRIP)
        n1_ref[span, :] = norm(
            q_ref[span, :].astype(SINGLE), gain_ref[1:2, :], bias_ref[1:2, :]
        ).astype(NARROW)

    loop(rows // STRIP, first)
    loads[0].wait()

    def project(j):
        span = at(j, CHUNK)
        pq_ref[:, span] = plain(n1_ref[...], w_in[:, span]).astype(NARROW)

    loop(3 * features // CHUNK, project)
    flush(0)
    flush(1)
    logs[...] = jnp.zeros_like(logs)

    def pair(p):
        for start in range(0, rows, LONG):
            end = min(start + LONG, rows)

            def mask(scores, start=start):
                shape = scores.shape
                return jnp.where(iota(shape, 1) <= iota(shape, 0) + start, scores, MASKED)

            out, sums = attend(
                pq_ref[start:end, at(p, PAIR)],
                pq_ref[0:end, at(p + features // PAIR, PAIR)],
                pq_ref[0:end, at(p + 2 * features // PAIR, PAIR)],
                mask,
            )
            mq_ref[start:end, at(p, PAIR)] = out.astype(NARROW)
            for which in range(2):
                mark(logs, slice(start, end), 2 * p + which, sums[which])

    loop(features // PAIR, pair)
    flush(2)
    log_ref[...] = turn(logs[...])
    loads[1].wait()

    def second(i):
        span = at(i, STRIP)
        total = q_ref[span, :].astype(SINGLE) + plain(mq_ref[span, :], w_out[...])
        q1_ref[span, :] = total
        nq_ref[span, :] = norm(total, gain_ref[2:3, :], bias_ref[2:3, :]).astype(NARROW)

    loop(rows // STRIP, second)
    if q1_ref.shape[0] > rows:
        q1_ref[rows:, :] = jnp.zeros_like(q1_ref[rows:, :])
        nq_ref[rows:, :] = jnp.zeros_like(nq_ref[rows:, :])
    flush(3)
    flush(4)
    loads[2].wait()
    cq_ref[...] = plain(nq_ref[0:rows, :], w_q[...]).astype(NARROW)
    flush(5)
    loads[3].wait()

    def third(j):
        span = at(j, CHUNK)
        vkv_ref[:, span] = plain(nq_ref[0:rows, :], w_kv[:, span]).astype(NARROW)

    loop(2 * features // CHUNK, third)


def cross_forward(pieces, cq_ref, ckv_ref, valid_ref, whole, *rest):
    log_refs, (logs,) = rest[:pieces], rest[pieces:]
    rows, features = cq_ref.shape
    part = log_refs[0].shape[1]
    logs[...] = jnp.zeros_like(logs)
    if whole.shape[0] > rows:
        whole[rows:, :] = jnp.zeros((whole.shape[0] - rows, features), NARROW)

    def pair(p):
        for start in range(0, rows, LONG):
            span = slice(start, min(start + LONG, rows))
            out, sums = attend(
                cq_ref[span, at(p, PAIR)],
                ckv_ref[:, at(p, PAIR)],
                ckv_ref[:, at(p + features // PAIR, PAIR)],
                lambda scores: scores + valid_ref[...],
            )
            whole[span, at(p, PAIR)] = out.astype(NARROW)
            for which in range(2):
                mark(logs, span, 2 * p + which, sums[which])

    loop(features // PAIR, pair)
    for k in range(pieces):
        log_refs[k][...] = turn(logs[at(piece_at(k, pieces), part), :])


def untwist(rows):
    same = jnp.where(iota((16, PAIR), 0) == iota((16, PAIR), 1), 1.0, 0.0).astype(NARROW)
    return functools.reduce(jnp.add, [left_t(part, same) for part in exact_parts(rows, 3)])


def merge_blocks(pieces, own_ref, *refs):
    logs, refs = refs[:pieces], refs[pieces:]
    halves, (co_ref, log_ref) = (refs[: pieces - 1], refs[pieces - 1 : -2]), refs[-2:]
    part, features = co_ref.shape
    width = features // 2
    peak = functools.reduce(jnp.maximum, [one[...] for one in logs])
    total = peak + jnp.log(functools.reduce(jnp.add, [jnp.exp(one[...] - peak) for one in logs]))
    log_ref[...] = total
    spread = jnp.where(
        iota((PAIR, features), 1) // HEAD == iota((PAIR, features), 0), 1.0, 0.0
    ).astype(NARROW)
    result = jnp.zeros(co_ref.shape, SINGLE)
    for k in range(pieces):
        weight = untwist(jnp.exp(logs[k][...] - total))
        high = weight.astype(NARROW)
        low = (weight - high.astype(SINGLE)).astype(NARROW)
        if k == 0:
            block = own_ref[at(place_of(), part), :]
        else:
            block = jnp.concatenate((halves[0][k - 1][...], halves[1][k - 1][...]), axis=1)
        result = result + (plain(high, spread) + plain(low, spread)) * block.astype(SINGLE)
    co_ref[...] = result.astype(NARROW)


def reverse_forward(
    length_ref, vq_ref, vkv_ref, x1_ref, a_out,
    mv_ref, x2_ref, log_ref,
    w_out, logs, sem,
    ready=nothing, flush=nothing,
):
    rows, features = vq_ref.shape
    keys = vkv_ref.shape[0]
    (load,) = copies(sem, (a_out.at[3], w_out))
    logs[...] = jnp.zeros_like(logs)
    bias = jnp.where(iota((1, keys), 1) < length_ref[0], 0.0, MASKED)

    def pair(p):
        for start in range(0, rows, WINDOWS):
            span = slice(start, start + WINDOWS)
            out, sums = attend(
                vq_ref[span, at(p, PAIR)],
                vkv_ref[:, at(p, PAIR)],
                vkv_ref[:, at(p + features // PAIR, PAIR)],
                lambda scores: scores + bias,
            )
            mv_ref[span, at(p, PAIR)] = out.astype(NARROW)
            for which in range(2):
                mark(logs, span, 2 * p + which, sums[which])

    loop(features // PAIR, pair)
    flush(0)
    log_ref[...] = turn(logs[...])
    load.wait()
    ready(3)

    def second(i):
        span = at(i, GROUP)
        x2_ref[span, :] = x1_ref[span, :] + plain(mv_ref[span, :], w_out[...])

    loop(rows // GROUP, second)


def feed_forward_step(block, normed, up, down, cot, hidden, slope, out, grad):
    rows = normed.shape[0]

    def strip(i):
        span = at(i, block)
        value, rise = gelu_both(plain(normed[span, :], up[...]))
        hidden[span, :] = value.astype(NARROW)
        slope[span, :] = (right_t(cot[span, :], down[...]) * rise).astype(NARROW)
        out[span, :] += plain(hidden[span, :], down[...])
        grad[span, :] += right_t(slope[span, :], up[...])

    loop(rows // block, strip)


def patch_feed_forward(
    x2_ref, cot_ref, gain_ref, bias_ref, up_ref, down_ref,
    x3_ref, dx2_ref, up_grad_ref, down_grad_ref, norm_ref,
    normed, hidden, slope, out, grad,
):
    rows = x2_ref.shape[0]
    step = pl.program_id(0)

    @pl.when(step == 0)
    def begin():
        def first(i):
            span = at(i, GROUP)
            normed[span, :] = norm(
                x2_ref[span, :], gain_ref[5:6, :], bias_ref[5:6, :]
            ).astype(NARROW)
            out[span, :] = x2_ref[span, :]
            grad[span, :] = jnp.zeros_like(grad[span, :])

        loop(rows // GROUP, first)

    feed_forward_step(
        512, normed, up_ref.at[0], down_ref.at[0], cot_ref, hidden, slope, out, grad
    )
    up_grad_ref[...] = left_t(normed[...], slope[...]).astype(NARROW)
    down_grad_ref[...] = left_t(hidden[...], cot_ref[...]).astype(NARROW)

    @pl.when(step == pl.num_programs(0) - 1)
    def finish():
        norm_ref[...] = jnp.zeros_like(norm_ref)

        def last(i):
            span = at(i, GROUP)
            x3_ref[span, :] = out[span, :].astype(NARROW)
            part, gain, bias = norm_back(x2_ref[span, :], gain_ref[5:6, :], grad[span, :])
            dx2_ref[span, :] = cot_ref[span, :].astype(SINGLE) + part
            norm_ref[0:1, :] += gain
            norm_ref[1:2, :] += bias

        loop(rows // GROUP, last)


def place_parts(ref, pieces, parts, sem):
    part, features = parts[0].shape
    width = features // 2
    pairs = [(parts[0], ref.at[at(piece_at(0, pieces), part), :])]
    for number in range(2):
        for k in range(1, pieces):
            pairs.append(
                (
                    parts[number * (pieces - 1) + k],
                    ref.at[at(piece_at(k, pieces), part), pl.ds(number * width, width)],
                )
            )
    return copies(sem, *pairs)


def query_feed_forward(
    pieces, share, hidden_share, q1_ref, cot_ref, gain_ref, bias_ref,
    w_out, up_ref, down_ref, *rest,
):
    parts, rest = rest[: 2 * pieces - 1], rest[2 * pieces - 1 :]
    (
        q3_ref, dq2_ref, up_grad_ref, down_grad_ref, norm_ref, co_ref,
        q2, normed, chosen, hidden, slope, out, grad, sem,
    ) = rest
    rows, features = cot_ref.shape
    width = up_ref.shape[2]
    step = pl.program_id(0)

    @pl.when(step == 0)
    def begin():
        for one in place_parts(co_ref, pieces, parts, sem):
            one.wait()

        def first(i):
            span = at(i, STRIP)
            total = q1_ref[span, :] + plain(co_ref[span, :], w_out[0])
            q2[span, :] = total
            out[span, :] = total
            normed[span, :] = norm(total, gain_ref[4:5, :], bias_ref[4:5, :]).astype(NARROW)
            grad[span, :] = jnp.zeros_like(grad[span, :])

        loop(rows // STRIP, first)
        chosen[...] = right_t(
            chooser(chosen.shape[0], features, place_of() * share, share), normed[...]
        ).astype(NARROW)

    feed_forward_step(
        rows, normed, up_ref.at[0], down_ref.at[0], cot_ref, hidden, slope, out, grad
    )
    up_grad_ref[...] = plain(chosen[...], slope[...]).astype(NARROW)
    begins = place_of() * hidden_share

    @pl.when(begins // width == step)
    def own_hidden():
        taken = right_t(
            chooser(down_grad_ref.shape[0], width, begins - step * width, hidden_share),
            hidden[...],
        ).astype(NARROW)
        down_grad_ref[...] = plain(taken, cot_ref[...]).astype(NARROW)

    @pl.when(step == pl.num_programs(0) - 1)
    def finish():
        norm_ref[...] = jnp.zeros_like(norm_ref)

        def last(i):
            span = at(i, STRIP)
            q3_ref[span, :] = out[span, :].astype(NARROW)
            piece, gain, bias = norm_back(q2[span, :], gain_ref[4:5, :], grad[span, :])
            dq2_ref[span, :] = cot_ref[span, :].astype(SINGLE) + piece
            norm_ref[0:1, :] += gain
            norm_ref[1:2, :] += bias

        loop(rows // STRIP, last)


def reverse_backward(
    pieces, length_ref, dx2_ref, mv_ref, vq_ref, vkv_ref, nx_ref, log_ref, a_out,
    *rest, launch=nothing, tick=nothing, ready=nothing,
):
    dvq_ref, weight_ref, rest = rest[0], rest[1], rest[2:]
    k_refs, v_refs, rest = rest[:pieces], rest[pieces : 2 * pieces], rest[2 * pieces :]
    w_out, rounded, dmv, deltas, dkv, sem = rest
    rows, features = vq_ref.shape
    keys = vkv_ref.shape[0]
    part = k_refs[0].shape[0]
    (load,) = copies(sem, (a_out.at[3], w_out))
    rounded[...] = dx2_ref[...].astype(NARROW)
    load.wait()
    dmv[...] = right_t(rounded[...], w_out[...]).astype(NARROW)
    store_rows(
        weight_ref, slice(features, 2 * features), left_t(mv_ref[...], rounded[...])
    )
    deltas[...] = head_rows(dmv[...].astype(SINGLE) * mv_ref[...].astype(SINGLE))
    if dkv.shape[0] > keys:
        dkv[keys:, :] = jnp.zeros((dkv.shape[0] - keys, 2 * features), SINGLE)
    size = 256
    for k in (3, 4, 6):
        ready(k)

    def pair(p):
        pl.when(p == 2)(lambda: tick(1))
        pl.when(p == 4)(lambda: tick(2))
        for strip in range(rows // size):
            span = slice(strip * size, (strip + 1) * size)

            def mask(scores):
                return jnp.where(iota(scores.shape, 0) < length_ref[0], scores, MASKED)

            dq, dk, dv = attend_back(
                vq_ref[span, at(p, PAIR)],
                vkv_ref[:, at(p, PAIR)],
                vkv_ref[:, at(p + features // PAIR, PAIR)],
                dmv[span, at(p, PAIR)],
                row_pair(log_ref, p, span),
                row_pair(deltas, p, span),
                mask,
            )
            dvq_ref[span, at(p, PAIR)] = (dq * (1.0 / math.sqrt(HEAD))).astype(NARROW)
            if strip == 0:
                dkv[0:keys, at(p, PAIR)] = dk
                dkv[0:keys, at(p + features // PAIR, PAIR)] = dv
            else:
                dkv[0:keys, at(p, PAIR)] += dk
                dkv[0:keys, at(p + features // PAIR, PAIR)] += dv

    loop(features // PAIR, pair)
    ready(5)
    store_rows(weight_ref, slice(0, features), left_t(nx_ref[...], dvq_ref[...]))
    launch(1)
    for k in range(pieces):
        span = at(piece_at(k, pieces), part)
        width = k_refs[k].shape[1]
        k_refs[k][...] = dkv[span, 0:width].astype(NARROW)
        v_refs[k][...] = dkv[span, width:].astype(NARROW)


def cross_backward(
    pieces, share, dq2_ref, co_ref, cq_ref, ckv_ref, valid_ref, a_out, *rest, ready=nothing
):
    log_parts, rest = rest[:pieces], rest[pieces:]
    dckv_ref, weight_ref, rest = rest[0], rest[1], rest[2:]
    q_refs, (w_out, rounded, dco, deltas, logs, turned, dq_all, dkv, sem) = (
        rest[:pieces],
        rest[pieces:],
    )
    rows, features = cq_ref.shape
    part = log_parts[0].shape[1]
    (load,) = copies(sem, (a_out.at[2], w_out))
    for k in range(pieces):
        logs[at(piece_at(k, pieces), part), :] = untwist(log_parts[k][...])
    turned[...] = turn(logs[0:rows, :])
    rounded[...] = dq2_ref[...].astype(NARROW)
    load.wait()
    dco[...] = right_t(rounded[...], w_out[...]).astype(NARROW)
    taken = right_t(
        chooser(weight_ref.shape[0], features, place_of() * share, share), co_ref[0:rows, :]
    ).astype(NARROW)
    weight_ref[...] = plain(taken, rounded[...]).astype(NARROW)
    deltas[...] = head_rows(dco[...].astype(SINGLE) * co_ref[0:rows, :].astype(SINGLE))
    if dq_all.shape[0] > rows:
        dq_all[rows:, :] = jnp.zeros((dq_all.shape[0] - rows, features), NARROW)
    edges = spans(rows, 512)
    ready(2)
    ready(3)

    def pair(p):
        for number, (start, end) in enumerate(edges):
            span = slice(start, end)
            dq, dk, dv = attend_back(
                cq_ref[span, at(p, PAIR)],
                ckv_ref[:, at(p, PAIR)],
                ckv_ref[:, at(p + features // PAIR, PAIR)],
                dco[span, at(p, PAIR)],
                row_pair(turned, p, span),
                row_pair(deltas, p, span),
                lambda scores: scores + valid_ref[...],
            )
            dq_all[span, at(p, PAIR)] = (dq * (1.0 / math.sqrt(HEAD))).astype(NARROW)
            if number == 0:
                dkv[:, at(p, PAIR)] = dk
                dkv[:, at(p + features // PAIR, PAIR)] = dv
            else:
                dkv[:, at(p, PAIR)] += dk
                dkv[:, at(p + features // PAIR, PAIR)] += dv

    loop(features // PAIR, pair)
    dckv_ref[...] = dkv[...].astype(NARROW)
    for k in range(pieces):
        q_refs[k][...] = dq_all[at(piece_at(k, pieces), part), :]


def patch_backward(
    x_ref, dx2_ref, x1_ref, nx_ref, n0_ref, pw_ref, mw_ref, dvq_ref, dckv_ref, gain_ref, a_in, a_out,
    kv_weight_ref, weight_ref, grad_ref, norm_ref,
    w_in, w_out, w_q, w_kv, dx1, rounded, dmw, deltas, dpw, sem,
    launch=nothing, ready=nothing, flush=nothing,
):
    rows, features = x_ref.shape
    loads = copies(
        sem,
        (a_in.at[3, :, pl.ds(0, features)], w_q),
        (a_in.at[2, :, pl.ds(features, 2 * features)], w_kv),
        (a_out.at[0], w_out),
        (a_in.at[0], w_in),
    )
    norm_ref[...] = jnp.zeros_like(norm_ref)
    for start in range(0, 2 * features, CHUNK):
        span = slice(start, start + CHUNK)
        store_rows(kv_weight_ref, span, left_t(nx_ref[...], dckv_ref[:, span]))
    launch(0)
    flush(0)
    loads[0].wait()
    loads[1].wait()

    def first(i):
        span = at(i, GROUP)
        upstream = right_t(dvq_ref[span, :], w_q[...]) + right_t(dckv_ref[span, :], w_kv[...])
        part, gain, bias = norm_back(x1_ref[span, :], gain_ref[3:4, :], upstream)
        total = dx2_ref[span, :] + part
        dx1[span, :] = total
        rounded[span, :] = total.astype(NARROW)
        norm_ref[0:1, :] += gain
        norm_ref[1:2, :] += bias

    loop(rows // GROUP, first)
    loads[2].wait()
    ready(6)
    dmw[...] = right_t(rounded[...], w_out[...]).astype(NARROW)
    store_rows(
        weight_ref, slice(3 * features, 4 * features), left_t(mw_ref[...], rounded[...])
    )
    deltas[...] = head_rows(dmw[...].astype(SINGLE) * mw_ref[...].astype(SINGLE))
    ready(5)
    window = jnp.where(
        iota((WINDOWS, WINDOWS), 0) // WIN == iota((WINDOWS, WINDOWS), 1) // WIN, 0.0, MASKED
    )

    def group(i):
        span = at(i, WINDOWS)
        for pair in range(features // PAIR):
            lane = pair * PAIR
            dq, dk, dv = attend_back(
                pw_ref[span, lane : lane + PAIR],
                pw_ref[span, features + lane : features + lane + PAIR],
                pw_ref[span, 2 * features + lane : 2 * features + lane + PAIR],
                dmw[span, lane : lane + PAIR],
                None,
                [deltas[2 * pair + w : 2 * pair + w + 1, span] for w in range(2)],
                lambda scores: scores + window,
            )
            dpw[span, lane : lane + PAIR] = (dq * (1.0 / math.sqrt(HEAD))).astype(NARROW)
            dpw[span, features + lane : features + lane + PAIR] = dk.astype(NARROW)
            dpw[span, 2 * features + lane : 2 * features + lane + PAIR] = dv.astype(NARROW)

    loop(rows // WINDOWS, group)
    ready(4)
    for start in range(0, 3 * features, CHUNK):
        span = slice(start, start + CHUNK)
        store_rows(weight_ref, span, left_t(n0_ref[...], dpw[:, span]))
    launch(1)
    flush(1)
    ready(0)
    loads[3].wait()

    def last(i):
        span = at(i, GROUP)
        upstream = right_t(dpw[span, :], w_in[...])
        part, gain, bias = norm_back(x_ref[span, :].astype(SINGLE), gain_ref[0:1, :], upstream)
        grad_ref[span, :] = dx1[span, :] + part
        norm_ref[2:3, :] += gain
        norm_ref[3:4, :] += bias

    loop(rows // GROUP, last)


def share_backward(
    pieces, q1, nq, gain_ref, a_in, *rest, launch=nothing
):
    parts = [rest[k * pieces : (k + 1) * pieces] for k in range(3)]
    rest = rest[3 * pieces :]
    grad_ref, weight_ref, norm_ref, w_q, w_kv, summed, q1_ref, nq_ref, sem = rest
    part, features = q1_ref.shape
    *loads, load_q, load_n = copies(
        sem,
        (a_in.at[2, :, pl.ds(0, features)], w_q),
        (a_in.at[3, :, pl.ds(features, 2 * features)], w_kv),
        (q1.at[at(place_of(), part), :], q1_ref),
        (nq.at[at(place_of(), part), :], nq_ref),
    )
    start = 0
    for k in range(3):
        width = parts[k][0].shape[1]
        total = functools.reduce(jnp.add, [one[...].astype(SINGLE) for one in parts[k]])
        summed[:, start : start + width] = total.astype(NARROW)
        start += width
    for load in loads:
        load.wait()
    upstream = right_t(summed[:, 0:features], w_q[...]) + right_t(summed[:, features:], w_kv[...])
    load_q.wait()
    piece, gain, bias = norm_back(q1_ref[...], gain_ref[2:3, :], upstream)
    grad_ref[...] = piece.astype(NARROW)
    launch(0)
    load_n.wait()
    for k in range(3):
        span = slice(k * features, (k + 1) * features)
        store_rows(weight_ref, span, left_t(nq_ref[...], summed[:, span]))
    launch(1)
    norm_ref[...] = jnp.zeros_like(norm_ref)
    norm_ref[0:1, :] = gain
    norm_ref[1:2, :] = bias


def causal_backward(
    pieces, share, q_ref, dq2_ref, n1_ref, pq_ref, mq_ref, log_ref, cross_ref, gain_ref,
    norm_x, norm_two, norm_four, norm_five, a_in, a_out, *rest, ready=nothing
):
    parts, rest = rest[: 2 * pieces - 1], rest[2 * pieces - 1 :]
    (
        weight_ref, grad_ref, norm_ref,
        w_in, w_out, gathered, dq1, rounded, dmq, deltas, dkv, dpq, norm_one, norm_all, sem,
    ) = rest
    rows, features = q_ref.shape
    placed = place_parts(gathered, pieces, parts, sem)
    loads = copies(sem.at[pl.ds(len(placed), 2)], (a_out.at[1], w_out), (a_in.at[1], w_in))
    for one in placed:
        one.wait()

    def first(i):
        span = at(i, STRIP)
        total = dq2_ref[span, :] + gathered[span, :].astype(SINGLE)
        dq1[span, :] = total
        rounded[span, :] = total.astype(NARROW)

    loop(rows // STRIP, first)
    loads[0].wait()
    dmq[...] = right_t(rounded[...], w_out[...]).astype(NARROW)
    ready(4)
    chosen = chooser(weight_ref.shape[0], features, place_of() * share, share)
    taken = right_t(chosen, mq_ref[...]).astype(NARROW)
    weight_ref[:, 3 * features : 4 * features] = plain(taken, rounded[...]).astype(NARROW)
    weight_ref[:, 4 * features : 5 * features] = cross_ref[...]
    weight_ref[:, 5 * features :] = jnp.zeros_like(weight_ref[:, 5 * features :])
    deltas[...] = head_rows(dmq[...].astype(SINGLE) * mq_ref[...].astype(SINGLE))
    edges = spans(rows, 256)
    ready(3)
    ready(5)

    def pair(p):
        for number, (start, end) in reversed(list(enumerate(edges))):
            span = slice(start, end)

            def mask(scores, start=start):
                shape = scores.shape
                return jnp.where(iota(shape, 0) <= iota(shape, 1) + start, scores, MASKED)

            dq, dk, dv = attend_back(
                pq_ref[span, at(p, PAIR)],
                pq_ref[0:end, at(p + features // PAIR, PAIR)],
                pq_ref[0:end, at(p + 2 * features // PAIR, PAIR)],
                dmq[span, at(p, PAIR)],
                row_pair(log_ref, p, span),
                row_pair(deltas, p, span),
                mask,
            )
            dpq[span, at(p, PAIR)] = (dq * (1.0 / math.sqrt(HEAD))).astype(NARROW)
            if end == rows:
                dkv[0:end, 0:PAIR] = dk
                dkv[0:end, PAIR:] = dv
            else:
                dkv[0:end, 0:PAIR] += dk
                dkv[0:end, PAIR:] += dv
        dpq[:, at(p + features // PAIR, PAIR)] = dkv[:, 0:PAIR].astype(NARROW)
        dpq[:, at(p + 2 * features // PAIR, PAIR)] = dkv[:, PAIR:].astype(NARROW)

    loop(features // PAIR, pair)
    ready(2)
    taken = right_t(chosen, n1_ref[...]).astype(NARROW)
    weight_ref[:, 0 : 3 * features] = plain(taken, dpq[...]).astype(NARROW)
    loads[1].wait()
    norm_one[...] = jnp.zeros_like(norm_one)

    def last(i):
        span = at(i, STRIP)
        upstream = right_t(dpq[span, :], w_in[...])
        piece, gain, bias = norm_back(q_ref[span, :].astype(SINGLE), gain_ref[1:2, :], upstream)
        grad_ref[span, :] = dq1[span, :] + piece
        norm_one[0:1, :] += gain
        norm_one[1:2, :] += bias

    loop(rows // STRIP, last)
    leader = jnp.where(place_of() == 0, 1.0, 0.0)
    norm_all[...] = jnp.zeros_like(norm_all)
    for row, (ref, source, scale) in enumerate(
        (
            (norm_x, 2, 1.0), (norm_one, 0, leader), (norm_two, 0, 1.0), (norm_x, 0, 1.0),
            (norm_four, 0, leader), (norm_five, 0, 1.0),
        )
    ):
        norm_all[row : row + 1, :] = ref[source : source + 1, :] * scale
        norm_all[8 + row : 9 + row, :] = ref[source + 1 : source + 2, :] * scale
    if len(norm_ref.shape) == 2:
        norm_ref[...] = norm_all[...]
    else:
        norm_ref[...] = jnp.zeros_like(norm_ref)
        for owner in range(norm_ref.shape[0]):
            norm_ref[owner, :, 0:share] = norm_all[:, owner * share : (owner + 1) * share]


def assemble(groups, count, *refs, ready=nothing, flush=nothing):
    parts, refs = refs[: 4 * groups], refs[4 * groups :]
    norms, refs = refs[:count], refs[count:]
    in_ref, out_ref, up_ref, down_ref, gain_ref, bias_ref, share, causal = refs
    features = down_ref.shape[2]
    rep = place_of("rep")

    def corners(number, write):
        for k in range(4):
            ready(4 * number + k)
            owner = flipped(rep, k, 4)
            piece = parts[4 * number + k][...]
            height, width = piece.shape[-2:]
            piece = piece.reshape(height, width)
            write(
                pl.ds(pl.multiple_of((owner % 2) * height, height), height),
                pl.multiple_of((owner // 2) * width, width), width, piece,
            )

    def into(ref, index, start=0):
        def write(rows, column, width, piece):
            ref[index, rows, pl.ds(column + start, width)] = piece

        return write

    up_x, down_x, reverse, window, kv, shared, up_q, down_q, rest = range(groups)

    def keep_causal(rows, column, width, piece):
        causal[rows, pl.ds(column, width)] = piece

    def keep_share(rows, column, width, piece):
        share[rows, pl.ds(column, width)] = piece

    corners(up_q, into(up_ref, 1))
    corners(down_q, into(down_ref, 1))
    corners(up_x, into(up_ref, 0))
    flush(2)
    corners(down_x, into(down_ref, 0))
    flush(3)
    first = 4 * groups
    for k in range(count):
        ready(first + k)
    terms = [norms[0][place_of()]] + [one[...] for one in norms[1:]]
    total = functools.reduce(jnp.add, terms)
    columns = gain_ref.shape[1]
    gain_ref[...] = total[0:6, 0:columns]
    bias_ref[...] = total[8:14, 0:columns]
    flush(4)
    flush(5)
    corners(reverse, keep_share)
    in_ref[3, :, 0:features] = share[:, 0:features]
    out_ref[3, :, :] = share[:, features : 2 * features]
    corners(window, keep_share)
    in_ref[0, :, :] = share[:, 0 : 3 * features]
    out_ref[0, :, :] = share[:, 3 * features :]
    corners(rest, keep_causal)
    in_ref[1, :, :] = causal[:, 0 : 3 * features]
    out_ref[1, :, :] = causal[:, 3 * features : 4 * features]
    out_ref[2, :, :] = causal[:, 4 * features : 5 * features]
    flush(1)
    corners(kv, into(in_ref, 2, features))
    corners(shared, keep_share)
    in_ref[2, :, 0:features] = share[:, 0:features]
    in_ref[3, :, features:] = share[:, features : 3 * features]
    flush(0)


def bits_of(count):
    return max(count - 1, 0).bit_length()


def swap(tensor, axis, mask):
    return lax.ppermute(tensor, axis, [(i, i ^ mask) for i in range(lax.axis_size(axis))])


def pick(tensor, place, dim):
    return lax.dynamic_index_in_dim(tensor, place, dim, keepdims=False)


def fold(tensor, axis, bit, dim):
    own = (lax.axis_index(axis) >> bit) & 1
    arrived = swap(pick(tensor, 1 - own, dim).astype(NARROW), axis, 1 << bit)
    return pick(tensor, own, dim).astype(SINGLE) + arrived.astype(SINGLE)


def unfold(tensor, axis, bit, dim):
    own = (lax.axis_index(axis) >> bit) & 1
    arrived = swap(tensor, axis, 1 << bit)
    return jnp.where(
        own == 0,
        jnp.stack((tensor, arrived), axis=dim),
        jnp.stack((arrived, tensor), axis=dim),
    )


def scatter_blk(tensor):
    bits = bits_of(lax.axis_size("blk"))
    tensor = tensor.reshape((2,) * bits + tensor.shape[1:])
    for bit in range(bits):
        tensor = fold(tensor, "blk", bit, bits - 1 - bit)
    return tensor


def sum_rep_scatter(tensor, dim):
    bits = bits_of(lax.axis_size("rep"))
    shape = tensor.shape
    tensor = tensor.reshape(
        shape[:dim] + (2,) * bits + (shape[dim] // 2**bits,) + shape[dim + 1 :]
    )
    for bit in range(bits):
        tensor = fold(tensor, "rep", bit, dim)
    return tensor


def gather_rep(tensor, dim):
    bits = bits_of(lax.axis_size("rep"))
    for bit in reversed(range(bits)):
        tensor = unfold(tensor, "rep", bit, dim)
    shape = tensor.shape
    return tensor.reshape(shape[:dim] + (-1,) + shape[dim + bits + 1 :])


def reduce_all(tensor):
    count = lax.axis_size("blk")
    tensor = tensor.reshape(count, tensor.shape[0] // count, tensor.shape[1])
    tensor = sum_rep_scatter(tensor, 1)
    tensor = scatter_blk(tensor).astype(NARROW)
    return gather_rep(tensor, 0)


def reduce_rep(tensor):
    return gather_rep(sum_rep_scatter(tensor, 0).astype(NARROW), 0)


def exchange(pieces):
    whole = lax.all_to_all(jnp.stack(pieces), "blk", 0, 0)
    return [whole[k] for k in range(len(pieces))]


def gather(tensor):
    count = lax.axis_size("blk")
    whole = lax.all_gather(tensor, "blk")
    return [whole[k] for k in range(count)]


def whole(ref):
    return ref


class Fold:
    def __init__(self, own, take, arrived, shape, keep=whole, keep_shape=None):
        self.own, self.take, self.arrived, self.shape = own, take, arrived, shape
        self.keep, self.keep_shape = keep, keep_shape or shape
        self.dtype = own.dtype


class Move:
    late = None

    def __init__(self, source, shape, axis, flip, take=whole, phase=0):
        self.source, self.shape, self.axis, self.flip, self.take = source, shape, axis, flip, take
        self.phase = phase
        self.dtype = source.dtype


def lanes_of(ref, start, width):
    return ref.at[(slice(None),) * (len(ref.shape) - 1) + (pl.ds(start, width),)]


class Reduction:
    def __init__(self, tensor, blocks=None):
        if blocks == 1:
            tensor = tensor.reshape(1, 1, 2, tensor.shape[0] // 2, tensor.shape[1])
        elif len(tensor.shape) == 2:
            blocks = lax.axis_size("blk")
            height = tensor.shape[0] // blocks
            tensor = tensor.reshape(blocks // 2, 2, 2, height // 2, tensor.shape[1])
        self.tensor, self.take, self.arrived, self.shape = tensor, whole, [], tensor.shape

    def fold(self, keep=whole, keep_shape=None):
        return Fold(self.tensor, self.take, self.arrived, self.shape, keep, keep_shape)

    def moves(self, stage):
        shape = self.shape
        if stage == "core":
            self.next = shape[:2] + shape[3:]
            return [
                Move(self.tensor, self.next, "rep", 1,
                     lambda ref: ref.at[:, :, 1 - place_of("rep") % 2])
            ]
        if stage == "x":
            width = shape[-1] // 2
            self.next = shape[:-1] + (width,)

            def own(ref):
                return lanes_of(ref, pl.multiple_of((place_of("rep") // 2) * width, width), width)

            def other(ref):
                start = (1 - place_of("rep") // 2) * width
                return lanes_of(ref, pl.multiple_of(start, width), width)

            return [Move(self.fold(own, self.next), self.next, "rep", 2, other)]
        if stage == "y":
            self.next = shape[:1] + shape[2:]
            fold = self.fold(lambda ref: ref.at[:, place_of() % 2], self.next)
            return [Move(fold, self.next, "blk", 1, lambda ref: ref.at[:, 1 - place_of() % 2])]
        if stage == "z":
            length = shape[0]
            self.next = shape[1:]
            fold = self.fold(lambda ref: ref.at[place_of() // 2], self.next)
            return [
                Move(fold, self.next, "blk", 2 * k,
                     lambda ref, k=k: ref.at[flipped(place_of() // 2, k, length)])
                for k in range(1, length)
            ]
        if stage == "back":
            fold = self.fold()
            return [Move(fold, shape, "rep", k) for k in range(1, 4)]
        if stage == "back_x":
            return [Move(self.fold(), shape, "rep", 2)]
        return [Move(self.tensor, shape, "rep", 1), Move(self.other, shape, "rep", 1)]

    def absorb(self, stage, arrived, kept):
        if stage == "core":
            self.take = lambda ref: ref.at[:, :, place_of("rep") % 2]
        else:
            self.take = whole
        if kept:
            self.tensor = kept[0]
        if stage in ("back", "back_x", "back_core"):
            if stage == "back_x":
                self.other = arrived[0]
                return
            if stage == "back":
                self.result = [self.tensor] + list(arrived)
            else:
                self.result = [self.tensor, arrived[0], self.other, arrived[1]]
            return
        self.shape, self.arrived = self.next, list(arrived)


class Exchange:
    def __init__(self, pieces):
        self.pieces = pieces

    def moves(self, stage):
        return [Move(one, one.shape, "blk", k) for k, one in enumerate(self.pieces) if k]

    def absorb(self, stage, arrived, kept):
        self.result = self.pieces[:1] + list(arrived)


class Pieces:
    def __init__(self, tensor, part, start, width):
        self.tensor, self.part, self.start, self.width = tensor, part, start, width

    def moves(self, stage):
        part, span = self.part, slice(self.start, self.start + self.width)
        count = lax.axis_size("blk")
        return [
            Move(self.tensor, (part, self.width), "blk", k,
                 lambda ref, k=k: ref.at[at(flipped(place_of(), k, count), part), span])
            for k in range(1, count)
        ]

    def absorb(self, stage, arrived, kept):
        self.result = list(arrived)


class Gather:
    def __init__(self, tensor):
        self.tensor = tensor

    def moves(self, stage):
        return [
            Move(self.tensor, self.tensor.shape, "blk", k) for k in range(1, lax.axis_size("blk"))
        ]

    def absorb(self, stage, arrived, kept):
        self.result = [self.tensor] + list(arrived)


class Spread:
    def __init__(self, tensor):
        self.tensor = tensor

    def moves(self, stage):
        count = lax.axis_size("blk")
        rows, width = self.tensor.shape[0], self.tensor.shape[1] // 2
        moves, self.places = [], []
        for number in range(2):
            span = slice(number * width, (number + 1) * width)
            own = lambda ref, span=span: ref.at[:, span]
            along = []
            for k in range(2, count, 2):
                along.append(Move(self.tensor, (rows, width), "blk", k, own, number))
                self.places.append((number, k))
            moves += along
            moves.append(Move(self.tensor, (rows, width), "blk", 1, own, number + 1))
            self.places.append((number, 1))
            for one in along:
                moves.append(Move(one, (rows, width), "blk", 1, whole, number + 1))
                self.places.append((number, one.flip + 1))
        return moves

    def absorb(self, stage, arrived, kept):
        found = dict(zip(self.places, arrived))
        count = lax.axis_size("blk")
        self.result = [found[number, k] for number in range(2) for k in range(1, count)]


class Norms:
    def __init__(self, tensor):
        self.tensor = tensor

    def moves(self, stage):
        axis = "rep" if stage == "out" else "blk"
        count = lax.axis_size(axis)
        shape = self.tensor.shape
        if stage == "out":
            return [Move(self.tensor, shape, axis, k) for k in range(1, count)]
        fold = Fold(self.tensor, whole, self.arrived, shape)
        return [
            Move(fold, shape[1:], axis, k,
                 lambda ref, k=k: ref.at[flipped(place_of(), k, count)])
            for k in range(1, count)
        ]

    def absorb(self, stage, arrived, kept):
        if stage == "out":
            self.arrived = list(arrived)
        else:
            self.result = [kept[0]] + list(arrived)


VMEM = pl.BlockSpec(memory_space=pltpu.VMEM)
SMEM = pl.BlockSpec(memory_space=pltpu.SMEM)
ANY = pl.BlockSpec(memory_space=pl.ANY)


def like(*shape, kind=NARROW):
    return jax.ShapeDtypeStruct(shape, kind)


def index_of(items, item):
    return next(k for k, one in enumerate(items) if one is item)


def call(
    kernel, outs, operands, specs, scratch, flops, grid=None, out_specs=None, semaphores=0,
    moves=(), ident=None, ticking=False, lazy=(), early=(),
):
    scratch = [pltpu.VMEM(shape, kind) for shape, kind in scratch]
    if semaphores:
        scratch.append(pltpu.SemaphoreType.DMA((semaphores,)))
    out_specs = [VMEM] * len(outs) if out_specs is None else out_specs
    extra = {} if grid is None else {"grid": grid}
    params = {}
    sources, folds = [], []

    def need(array):
        if not any(array is one for one in sources):
            sources.append(array)

    for move in moves:
        if isinstance(move.source, Fold):
            if not any(move.source is one for one in folds):
                folds.append(move.source)
                for array in [move.source.own] + move.source.arrived:
                    need(array)
        elif move.late is None and not isinstance(move.source, Move):
            need(move.source)
    fixed_in, fixed_out = len(operands), len(outs)
    partners = sorted({(move.axis, move.flip) for move in moves})
    lasts = max([move.phase for move in moves], default=0)
    held_in = [k for k, spec in enumerate(specs) if spec is VMEM]
    held_out = [k for k, spec in enumerate(out_specs) if spec is VMEM]
    own_scratch = len(scratch)
    scratch += [pltpu.VMEM(operands[k].shape, operands[k].dtype) for k in held_in]
    scratch += [pltpu.VMEM(outs[k].shape, outs[k].dtype) for k in held_out]
    terms = sum(1 + len(fold.arrived) for fold in folds)
    for fold in folds:
        scratch += [pltpu.VMEM(fold.shape, NARROW)] * (1 + len(fold.arrived))
    for number in (len(held_in), len(held_out), terms, len(folds), len(moves), len(moves)):
        scratch.append(pltpu.SemaphoreType.DMA((max(number, 1),)))
    if moves:
        params = {"collective_id": ident, "has_side_effects": True}
    before = {}
    for move in moves:
        if isinstance(move.source, Move):
            number = index_of(moves, move.source)
            before[number] = min(move.phase, before.get(number, move.phase))

    def body_kernel(*refs):
        ins, refs = list(refs[:fixed_in]), refs[fixed_in:]
        sent, refs = refs[: len(sources)], refs[len(sources) :]
        results, refs = list(refs[:fixed_out]), refs[fixed_out:]
        landed, refs = refs[: len(moves)], refs[len(moves) :]
        kept, refs = refs[: len(folds)], refs[len(folds) :]
        rest, refs = refs[:own_scratch], refs[own_scratch:]
        inner, refs = refs[: len(held_in)], refs[len(held_in) :]
        outer, refs = refs[: len(held_out)], refs[len(held_out) :]
        buffers, (in_sem, out_sem, load_sem, keep_sem, send_sem, recv_sem) = refs[:terms], refs[terms:]
        fetches, stores = {}, {}
        for number, k in enumerate(held_in):
            fetches[k] = pltpu.make_async_copy(ins[k], inner[number], in_sem.at[number])
            ins[k] = inner[number]
        for number, k in enumerate(held_out):
            stores[k] = pltpu.make_async_copy(outer[number], results[k], out_sem.at[number])
            results[k] = outer[number]

        def target(axis, flip):
            return {axis: flipped(lax.axis_index(axis), flip, lax.axis_size(axis))}

        def buffers_of(fold):
            start = sum(1 + len(one.arrived) for one in folds[: index_of(folds, fold)])
            return start, buffers[start : start + 1 + len(fold.arrived)]

        def made(k):
            move = moves[k]
            if move.late is not None:
                source = results[move.late]
            elif isinstance(move.source, Fold):
                source = buffers_of(move.source)[1][0]
            elif isinstance(move.source, Move):
                source = landed[index_of(moves, move.source)]
            else:
                source = sent[index_of(sources, move.source)]
            return pltpu.make_async_remote_copy(
                src_ref=move.take(source),
                dst_ref=landed[k],
                send_sem=send_sem.at[k],
                recv_sem=recv_sem.at[k],
                device_id=target(move.axis, move.flip),
                device_id_type=pl.DeviceIdType.MESH,
            )

        def loads(fold):
            start, held = buffers_of(fold)
            return [
                pltpu.make_async_copy(
                    (fold.take if k == 0 else whole)(sent[index_of(sources, array)]),
                    held[k],
                    load_sem.at[start + k],
                )
                for k, array in enumerate([fold.own] + fold.arrived)
            ]

        def keeping(k):
            fold = folds[k]
            return pltpu.make_async_copy(
                fold.keep(buffers_of(fold)[1][0]), kept[k], keep_sem.at[k]
            )

        def add(fold):
            held = buffers_of(fold)[1]

            def one(index):
                if len(held) == 2:
                    held[0][index] = held[0][index] + held[1][index]
                elif len(held) > 2:
                    held[0][index] = functools.reduce(
                        jnp.add, [part[index].astype(SINGLE) for part in held]
                    ).astype(NARROW)

            if len(fold.shape) == 2:
                one((slice(None), slice(None)))
            else:
                loop(fold.shape[0], one)

        def begin():
            for fold in folds:
                for load in loads(fold):
                    load.start()
            for fetch in fetches.values():
                fetch.start()
            if moves:
                barrier = pltpu.get_barrier_semaphore()
                for axis, flip in partners:
                    pl.semaphore_signal(
                        barrier, inc=1, device_id=target(axis, flip),
                        device_id_type=pl.DeviceIdType.MESH,
                    )
                pl.semaphore_wait(barrier, len(partners))
            for k, move in enumerate(moves):
                if move.phase == 0 and move.late is None and not isinstance(move.source, Fold):
                    made(k).start()
            for number, fold in enumerate(folds):
                for load in loads(fold):
                    load.wait()
                add(fold)
                for k, move in enumerate(moves):
                    if move.source is fold:
                        made(k).start()
                keeping(number).start()
            for k, fetch in fetches.items():
                if k not in lazy:
                    fetch.wait()

        def launch(which):
            for k in range(len(moves)):
                if moves[k].late == which and moves[k].phase == 0:
                    made(k).start()

        def tick(phase):
            for k, needed in before.items():
                if needed == phase:
                    made(k).wait_recv()
            for k, move in enumerate(moves):
                if move.phase == phase:
                    made(k).start()

        def finish():
            for k, store in stores.items():
                if k not in early:
                    store.start()
            if not ticking:
                for phase in range(1, lasts + 1):
                    tick(phase)
            for k in range(len(moves)):
                made(k).wait_send()
                if k not in before:
                    made(k).wait_recv()
            for k in range(len(folds)):
                keeping(k).wait()
            for store in stores.values():
                store.wait()

        options = {}
        if any(move.late is not None for move in moves):
            options["launch"] = launch
        if ticking:
            options["tick"] = tick
        if lazy:
            options["ready"] = lambda k: fetches[k].wait()
        if early:
            options["flush"] = lambda k: stores[k].start()
        if grid is None:
            begin()
            kernel(*ins, *results, *rest, **options)
            finish()
        else:
            pl.when(pl.program_id(0) == 0)(begin)
            kernel(*ins, *results, *rest, **options)
            pl.when(pl.program_id(0) == pl.num_programs(0) - 1)(finish)

    result = pl.pallas_call(
        body_kernel,
        out_shape=list(outs)
        + [
            like(*m.shape, kind=m.dtype)
            for m in moves
        ]
        + [like(*fold.keep_shape) for fold in folds],
        in_specs=[ANY if spec is VMEM else spec for spec in specs] + [ANY] * len(sources),
        out_specs=[ANY if spec is VMEM else spec for spec in out_specs]
        + [ANY] * (len(moves) + len(folds)),
        scratch_shapes=scratch,
        compiler_params=pltpu.CompilerParams(vmem_limit_bytes=60 * 2**20, **params),
        cost_estimate=pl.CostEstimate(
            flops=int(flops),
            bytes_accessed=sum(o.size * o.dtype.itemsize for o in operands),
            transcendentals=0,
        ),
        **extra,
    )(*operands, *sources)
    end = fixed_out + len(moves)
    return list(result[:fixed_out]), list(result[fixed_out:end]), (folds, list(result[end:]))


def finale(kernel, outs, stages, results, scratch, ident):
    plan = []
    for stage in stages:
        for job, name in stage:
            moves = job.moves(name)
            folds = []
            for move in moves:
                known = folds + [fold for part, _ in plan for fold in part]
                if isinstance(move.source, Fold) and not any(move.source is one for one in known):
                    folds.append(move.source)
            job.absorb(name, moves, folds)
            plan.append((folds, moves))
    items = results()
    moves = [move for _, part in plan for move in part]
    folds = [fold for part, _ in plan for fold in part]
    sources, fetched = [], []

    def need(item):
        if not isinstance(item, (Fold, Move)) and not any(item is one for one in sources):
            sources.append(item)

    for fold in folds:
        for item in [fold.own] + fold.arrived:
            need(item)
            if not isinstance(item, (Fold, Move)):
                fetched.append((fold, item))
    for move in moves:
        need(move.source)
    plain_items = []
    for item in items:
        need(item)
        if not isinstance(item, (Fold, Move)):
            plain_items.append(item)
    partners = sorted({(move.axis, move.flip) for move in moves})
    shapes = [pltpu.VMEM(one.shape, one.dtype) for one in scratch]
    shapes += [pltpu.VMEM(move.shape, move.dtype) for move in moves]
    shapes += [pltpu.VMEM(fold.shape, fold.dtype) for fold in folds]
    shapes += [pltpu.VMEM(fold.shape, fold.dtype) for fold, _ in fetched]
    shapes += [pltpu.VMEM(item.shape, item.dtype) for item in plain_items]
    shapes += [pltpu.VMEM(one.shape, one.dtype) for one in outs]
    for number in (len(moves), len(moves), len(fetched), len(plain_items), len(outs)):
        shapes.append(pltpu.SemaphoreType.DMA((max(number, 1),)))

    def body_kernel(*refs):
        def take(count):
            nonlocal refs
            some, refs = refs[:count], refs[count:]
            return some

        sent, finals = take(len(sources)), take(len(outs))
        rest, landed, sums = take(len(scratch)), take(len(moves)), take(len(folds))
        brought, held, outer = take(len(fetched)), take(len(plain_items)), take(len(outs))
        send_sem, recv_sem, load_sem, item_sem, out_sem = refs
        arrived = set()

        def target(axis, flip):
            return {axis: flipped(lax.axis_index(axis), flip, lax.axis_size(axis))}

        def place(item):
            if isinstance(item, Fold):
                return sums[index_of(folds, item)]
            if isinstance(item, Move):
                return landed[index_of(moves, item)]
            return sent[index_of(sources, item)]

        def made(move):
            k = index_of(moves, move)
            source = place(move.source)
            return pltpu.make_async_remote_copy(
                src_ref=move.take(source),
                dst_ref=landed[k],
                send_sem=send_sem.at[k],
                recv_sem=recv_sem.at[k],
                device_id=target(move.axis, move.flip),
                device_id_type=pl.DeviceIdType.MESH,
            )

        def arrival(item):
            if isinstance(item, Move) and index_of(moves, item) not in arrived:
                arrived.add(index_of(moves, item))
                made(item).wait_recv()

        loads = [
            pltpu.make_async_copy(
                (fold.take if item is fold.own else whole)(place(item)), brought[k], load_sem.at[k]
            )
            for k, (fold, item) in enumerate(fetched)
        ]
        fetches = [
            pltpu.make_async_copy(place(item), held[k], item_sem.at[k])
            for k, item in enumerate(plain_items)
        ]
        stores = [
            pltpu.make_async_copy(outer[k], finals[k], out_sem.at[k]) for k in range(len(outs))
        ]
        for load in loads:
            load.start()
        barrier = pltpu.get_barrier_semaphore()
        for axis, flip in partners:
            pl.semaphore_signal(
                barrier, inc=1, device_id=target(axis, flip), device_id_type=pl.DeviceIdType.MESH
            )
        pl.semaphore_wait(barrier, len(partners))

        def total(fold):
            terms = []
            for item in [fold.own] + fold.arrived:
                if isinstance(item, (Fold, Move)):
                    arrival(item)
                    term = place(item)
                    if item is fold.own:
                        term = fold.take(item.keep(term) if isinstance(item, Fold) else term)
                else:
                    k = next(
                        k for k, (one, other) in enumerate(fetched) if one is fold and other is item
                    )
                    loads[k].wait()
                    term = brought[k]
                terms.append(term)
            goal = place(fold)

            def one(index):
                goal[index] = functools.reduce(
                    jnp.add, [term[index].astype(SINGLE) for term in terms]
                ).astype(goal.dtype)

            if len(fold.shape) == 2:
                one((slice(None), slice(None)))
            else:
                loop(fold.shape[0], one)

        for number, (some, part) in enumerate(plan):
            for fold in some:
                total(fold)
            for move in part:
                arrival(move.source)
                made(move).start()
            if number == 0:
                for fetch in fetches:
                    fetch.start()
        operands = []
        for item in items:
            if isinstance(item, (Fold, Move)):
                operands.append(place(item))
            else:
                operands.append(held[next(k for k, one in enumerate(plain_items) if one is item)])
        for fetch in fetches:
            fetch.wait()

        def ready(k):
            arrival(items[k])

        kernel(*operands, *outer, *rest, ready=ready, flush=lambda k: stores[k].start())
        for move in moves:
            made(move).wait_send()
            arrival(move)
        for store in stores:
            store.wait()

    return pl.pallas_call(
        body_kernel,
        out_shape=list(outs),
        in_specs=[ANY] * len(sources),
        out_specs=[ANY] * len(outs),
        scratch_shapes=shapes,
        compiler_params=pltpu.CompilerParams(
            vmem_limit_bytes=60 * 2**20, collective_id=ident, has_side_effects=True
        ),
    )(*sources)


class Courier:
    def __init__(self, active):
        self.active, self.waiting, self.ident = active, [], 0

    def load(self, *jobs):
        self.waiting += jobs

    def run(self, kernel, outs, operands, specs, scratch, flops, **extra):
        jobs, self.waiting = self.waiting, []
        moves, ends = [], []
        for job, stage, *late in jobs:
            added = job.moves(stage)
            for move in added:
                if late and not isinstance(move.source, Move):
                    move.late = late[0]
            moves += added
            ends.append(len(moves))
        if moves:
            self.ident += 1
        results, arrived, (folds, kept) = call(
            kernel, outs, operands, specs, scratch, flops, moves=tuple(moves), ident=self.ident, **extra
        )
        start = 0
        for (job, stage, *late), end in zip(jobs, ends):
            if late:
                job.tensor = results[late[0]]
            own = [
                kept[k]
                for k, fold in enumerate(folds)
                if any(move.source is fold for move in moves[start:end])
            ]
            job.absorb(stage, arrived[start:end], own)
            start = end
        return results


def in_halves(arrays):
    width = arrays[0].shape[1] // 2
    return (
        arrays[:1] + [one[:, :width] for one in arrays[1:]] + [one[:, width:] for one in arrays[1:]]
    )


def body(
    patches,
    queries,
    window_valid,
    answer_length,
    norm_gain,
    norm_bias,
    attn_in,
    attn_out,
    mlp_in,
    mlp_out,
    cot_patches,
    cot_queries,
):
    x, q, cot_x, cot_q = patches[0], queries[0], cot_patches[0], cot_queries[0]
    rows, features = x.shape
    count = q.shape[0]
    hidden = mlp_in.shape[2]
    blocks = lax.axis_size("blk")
    place = lax.axis_index("blk").astype(jnp.int32)
    share = features // blocks
    hidden_share = hidden // blocks
    share_rows = -(-share // 16) * 16
    hidden_rows = -(-hidden_share // 16) * 16
    part = -(-count // (blocks * 16)) * 16
    padded = part * blocks
    wide = 3 * features
    last = wide + features + features
    causal_columns = -(-last // 512) * 512
    valid = jnp.where(jnp.repeat(window_valid[0], WIN) > 0, 0.0, MASKED).astype(SINGLE)
    carried = blocks == DIRECT and lax.axis_size("rep") == 4 and share % 32 == 0
    courier = Courier(carried)

    def own_columns(tensor):
        return lax.dynamic_slice_in_dim(tensor, place * share, share, 1)

    square = 2.0 * features * features
    run = courier.run

    n0, pw, mw, x1, nx, vq, ckv = run(
        window_forward,
        [
            like(rows, features), like(rows, wide), like(rows, features),
            like(rows, features, kind=SINGLE), like(rows, features), like(rows, features),
            like(rows, 2 * features),
        ],
        [x, norm_gain, norm_bias, attn_in, attn_out],
        [VMEM, VMEM, VMEM, ANY, ANY],
        [((features, wide), NARROW), ((features, features), NARROW),
         ((features, features), NARROW), ((features, 2 * features), NARROW)],
        rows * square * 9,
        semaphores=4,
        early=(0, 1, 2, 3, 4, 5),
    )
    n1, pq, mq, q1, nq, cq, vkv, log_q = run(
        causal_forward,
        [
            like(count, features), like(count, wide), like(count, features),
            like(padded, features, kind=SINGLE), like(padded, features), like(count, features),
            like(count, 2 * features), like(16, count, kind=SINGLE),
        ],
        [q, norm_gain, norm_bias, attn_in, attn_out],
        [VMEM, VMEM, VMEM, ANY, ANY],
        [((features, wide), NARROW), ((features, features), NARROW),
         ((features, features), NARROW), ((features, 2 * features), NARROW),
         ((count, PAIR), SINGLE)],
        count * square * 15,
        semaphores=4,
        early=(0, 1, 2, 3, 4, 5),
    )
    outs, *log_pieces = run(
        functools.partial(cross_forward, blocks),
        [like(padded, features)] + [like(16, part, kind=SINGLE)] * blocks,
        [cq, ckv, valid[None, :]],
        [VMEM, VMEM, VMEM],
        [((padded, PAIR), SINGLE)],
        count * square * 6,
    )
    logs = Exchange(log_pieces)
    first_width = features // 3
    halves = [
        Pieces(outs, part, 0, first_width),
        Pieces(outs, part, first_width, features - first_width),
    ]
    if carried:
        courier.load((logs, ""), (halves[0], ""))
    mv, x2, log_v = run(
        reverse_forward,
        [like(rows, features), like(rows, features, kind=SINGLE), like(16, rows, kind=SINGLE)],
        [answer_length, vq, vkv, x1, attn_out],
        [SMEM, VMEM, VMEM, VMEM, ANY],
        [((features, features), NARROW), ((rows, PAIR), SINGLE)],
        rows * square * 8,
        semaphores=1,
        lazy=(3,),
        early=(0,),
    )
    if carried:
        courier.load((halves[1], ""))
    x3, dx2, up_x, down_x, norm_five = run(
        patch_feed_forward,
        [
            like(rows, features), like(rows, features, kind=SINGLE), like(features, hidden),
            like(hidden, features), like(8, features, kind=SINGLE),
        ],
        [x2, cot_x, norm_gain, norm_bias, mlp_in, mlp_out],
        [
            VMEM, VMEM, VMEM, VMEM,
            pl.BlockSpec((1, features, CHUNK), lambda j: (0, 0, j)),
            pl.BlockSpec((1, CHUNK, features), lambda j: (0, j, 0)),
        ],
        [((rows, features), NARROW), ((rows, CHUNK), NARROW), ((rows, CHUNK), NARROW),
         ((rows, features), SINGLE), ((rows, features), SINGLE)],
        rows * square * 24,
        grid=(hidden // CHUNK,),
        out_specs=[
            VMEM, VMEM,
            pl.BlockSpec((features, CHUNK), lambda j: (0, j)),
            pl.BlockSpec((CHUNK, features), lambda j: (j, 0)),
            VMEM,
        ],
    )
    if carried:
        merged = run(
            functools.partial(merge_blocks, blocks),
            [like(part, features), like(16, part, kind=SINGLE)],
            [outs] + logs.result + halves[0].result + halves[1].result,
            [VMEM] * (3 * blocks - 1),
            [],
            padded * square,
        )
        co_parts, log_parts = Spread(merged[0]), Gather(merged[1])
        up_x, down_x = Reduction(up_x), Reduction(down_x)
        reverse_weight = Reduction(like(blocks // 2, 2, 2, share // 2, 2 * features))
        courier.load(
            (co_parts, ""), (log_parts, ""), (up_x, "core"), (down_x, "core"),
            (reverse_weight, "core", 1),
        )
    else:
        whole_logs = jnp.stack(exchange(log_pieces))
        merged_log = jax.nn.logsumexp(whole_logs, axis=0)
        weights = jnp.transpose(jnp.exp(whole_logs - merged_log)[:, :HEADS], (0, 2, 1))
        shares = lax.all_to_all(outs.reshape(blocks, part, features), "blk", 0, 0)
        merged_out = jnp.sum(jnp.repeat(weights, HEAD, axis=2) * shares.astype(SINGLE), axis=0)
        co_parts, log_parts = Spread(None), Gather(None)
        co_parts.tensor, *co_parts.result = in_halves(gather(merged_out.astype(NARROW)))
        log_parts.result = gather(merged_log)
    folded = (blocks // 2, 2, 2, share // 2) if carried else (features,)
    dvq, reverse_grad, *kv_pieces = run(
        functools.partial(reverse_backward, blocks),
        [like(rows, features), like(*folded, 2 * features)]
        + [like(part, features + PAIR)] * blocks + [like(part, features - PAIR)] * blocks,
        [answer_length, dx2, mv, vq, vkv, nx, log_v, attn_out],
        [SMEM, VMEM, VMEM, VMEM, VMEM, VMEM, VMEM, ANY],
        [((features, features), NARROW), ((rows, features), NARROW), ((rows, features), NARROW),
         ((16, rows), SINGLE), ((padded, 2 * features), SINGLE)],
        rows * square * 16,
        semaphores=1,
        ticking=carried,
        lazy=(3, 4, 5, 6),
    )
    k_parts, v_parts = Exchange(kv_pieces[:blocks]), Exchange(kv_pieces[blocks:])
    if carried:
        courier.load((k_parts, ""), (up_x, "x"))
    else:
        k_parts.result, v_parts.result = exchange(k_parts.pieces), exchange(v_parts.pieces)
    q3, dq2, up_q, down_q, norm_four, co = run(
        functools.partial(query_feed_forward, blocks, share, hidden_share),
        [
            like(count, features), like(count, features, kind=SINGLE), like(share_rows, hidden),
            like(hidden_rows, features), like(8, features, kind=SINGLE), like(padded, features),
        ],
        [q1, cot_q, norm_gain, norm_bias, attn_out, mlp_in, mlp_out, co_parts.tensor]
        + co_parts.result,
        [
            VMEM, VMEM, VMEM, VMEM, pl.BlockSpec((1, features, features), lambda j: (2, 0, 0)),
            pl.BlockSpec((1, features, CHUNK), lambda j: (1, 0, j)),
            pl.BlockSpec((1, CHUNK, features), lambda j: (1, j, 0)),
        ] + [ANY] * (2 * blocks - 1),
        [((count, features), SINGLE), ((count, features), NARROW), ((share_rows, count), NARROW),
         ((count, CHUNK), NARROW), ((count, CHUNK), NARROW),
         ((count, features), SINGLE), ((count, features), SINGLE)],
        count * square * 18,
        semaphores=2 * blocks - 1,
        grid=(hidden // CHUNK,),
        out_specs=[
            VMEM, VMEM,
            pl.BlockSpec((share_rows, CHUNK), lambda j: (0, j)),
            VMEM, VMEM, VMEM,
        ],
    )
    if carried:
        up_q, down_q = Reduction(up_q, 1), Reduction(down_q, 1)
        courier.load((v_parts, ""), (down_x, "x"), (up_x, "y"), (up_q, "core"), (down_q, "core"))
    dckv, cross_out_weight, *q_pieces = run(
        functools.partial(cross_backward, blocks, share),
        [like(rows, 2 * features), like(share_rows, features)] + [like(part, features)] * blocks,
        [dq2, co, cq, ckv, valid[:, None], attn_out] + log_parts.result,
        [VMEM, VMEM, VMEM, VMEM, VMEM, ANY] + [VMEM] * blocks,
        [((features, features), NARROW), ((count, features), NARROW), ((count, features), NARROW),
         ((16, count), SINGLE), ((padded, PAIR), SINGLE), ((16, count), SINGLE),
         ((padded, features), NARROW), ((rows, 2 * features), SINGLE)],
        count * square * 12,
        semaphores=1,
        lazy=(2, 3),
    )
    q_parts = Exchange(q_pieces)
    if carried:
        kv_weight = Reduction(like(blocks // 2, 2, 2, share // 2, 2 * features))
        window_weight = Reduction(like(blocks // 2, 2, 2, share // 2, 4 * features))
        courier.load(
            (q_parts, ""), (down_x, "y"), (reverse_weight, "x"), (up_q, "x"), (down_q, "x"),
            (kv_weight, "core", 0), (window_weight, "core", 1),
        )
    else:
        q_parts.result = exchange(q_pieces)
    kv_grad, window_grad, grad_x, norm_x = run(
        patch_backward,
        [
            like(*folded, 2 * features), like(*folded, 4 * features),
            like(rows, features, kind=SINGLE), like(8, features, kind=SINGLE),
        ],
        [x, dx2, x1, nx, n0, pw, mw, dvq, dckv, norm_gain, attn_in, attn_out],
        [VMEM] * 10 + [ANY, ANY],
        [((features, wide), NARROW), ((features, features), NARROW),
         ((features, features), NARROW), ((features, 2 * features), NARROW),
         ((rows, features), SINGLE), ((rows, features), NARROW), ((rows, features), NARROW),
         ((16, rows), SINGLE), ((rows, wide), NARROW)],
        rows * square * 24,
        semaphores=4,
        lazy=(0, 4, 5, 6),
        early=(0, 1),
    )
    if carried:
        share_weight = Reduction(like(blocks // 2, 2, 2, share // 2, wide))
        dq1_parts = Spread(like(part, features))
        courier.load(
            (share_weight, "core", 1), (dq1_parts, "", 0), (window_weight, "x"),
            (reverse_weight, "y"), (up_q, "back_x"), (down_q, "back_x"),
        )
    dq1_share, share_grad, norm_two = run(
        functools.partial(share_backward, blocks),
        [like(part, features), like(*folded, wide), like(8, features, kind=SINGLE)],
        [q1, nq, norm_gain, attn_in]
        + q_parts.result + k_parts.result + v_parts.result,
        [ANY, ANY, VMEM, ANY] + [VMEM] * (3 * blocks),
        [((features, features), NARROW), ((features, 2 * features), NARROW),
         ((part, wide), NARROW), ((part, features), SINGLE), ((part, features), NARROW)],
        part * square * 6,
        semaphores=4,
    )
    if carried:
        courier.load(
            (window_weight, "y"), (share_weight, "x"), (kv_weight, "x"), (down_x, "z"),
            (reverse_weight, "z"), (up_q, "back_core"), (down_q, "back_core"), (up_x, "z"),
        )
    else:
        dq1_parts = Spread(None)
        dq1_parts.tensor, *dq1_parts.result = in_halves(gather(dq1_share))
    causal_weight, grad_q, norms = run(
        functools.partial(causal_backward, blocks, share),
        [
            like(share_rows, causal_columns), like(count, features, kind=SINGLE),
            like(blocks, 16, -(-share // PAIR) * PAIR, kind=SINGLE)
            if carried
            else like(16, features, kind=SINGLE),
        ],
        [q, dq2, n1, pq, mq, log_q, cross_out_weight, norm_gain]
        + [norm_x, norm_two, norm_four, norm_five, attn_in, attn_out, dq1_parts.tensor]
        + dq1_parts.result,
        [VMEM] * 12 + [ANY] * (2 * blocks + 1),
        [((features, wide), NARROW), ((features, features), NARROW), ((padded, features), NARROW),
         ((count, features), SINGLE), ((count, features), NARROW), ((count, features), NARROW),
         ((16, count), SINGLE), ((count, 2 * PAIR), SINGLE), ((count, wide), NARROW),
         ((8, features), SINGLE), ((16, features), SINGLE)],
        count * square * 16,
        semaphores=2 * blocks + 1,
        lazy=(2, 3, 4, 5),
    )
    rest = (
        x3[None],
        own_columns(q3)[None],
        grad_x[None],
        own_columns(grad_q)[None],
    )
    if carried:
        norms = Norms(norms)
        causal_weight = Reduction(causal_weight, 1)
        sums = [
            up_x, down_x, reverse_weight, window_weight, kv_weight, share_weight, up_q, down_q,
            causal_weight,
        ]
        grads = finale(
            functools.partial(assemble, len(sums), blocks),
            [
                like(4, share, wide), like(4, share, features), like(2, share, hidden),
                like(2, hidden_share, features),
                like(6, share, kind=SINGLE), like(6, share, kind=SINGLE),
            ],
            [
                [
                    (causal_weight, "core"), (norms, "out"), (share_weight, "y"), (kv_weight, "y"),
                    (window_weight, "z"), (up_x, "back_x"), (down_x, "back_x"),
                    (reverse_weight, "back_x"),
                ],
                [
                    (causal_weight, "x"), (norms, "back"), (kv_weight, "z"), (share_weight, "z"),
                    (up_x, "back_core"), (down_x, "back_core"), (reverse_weight, "back_core"),
                    (window_weight, "back_x"),
                ],
                [
                    (causal_weight, "back_x"), (kv_weight, "back_x"), (share_weight, "back_x"),
                    (window_weight, "back_core"),
                ],
                [
                    (causal_weight, "back_core"), (kv_weight, "back_core"),
                    (share_weight, "back_core"),
                ],
            ],
            lambda: sum([one.result for one in sums], []) + norms.result,
            [like(share, 4 * features), like(share, causal_columns)],
            courier.ident + 1,
        )
        return rest + (grads[4], grads[5]) + tuple(one.astype(SINGLE) for one in grads[:4])
    up_x, down_x, reverse_weight, window_weight, kv_weight, share_weight = (
        reduce_all(one) for one in (up_x, down_x, reverse_grad, window_grad, kv_grad, share_grad)
    )
    up_q, down_q = reduce_rep(up_q[:share]), reduce_rep(down_q[:hidden_share])
    causal_weight = reduce_rep(causal_weight[:share])
    norms = own_columns(lax.psum(norms, ("blk", "rep")))
    gains, biases = norms[:6], norms[8:14]
    grad_attn_in = jnp.stack(
        (
            window_weight[:, :wide],
            causal_weight[:, :wide],
            jnp.concatenate((share_weight[:, :features], kv_weight), axis=1),
            jnp.concatenate((reverse_weight[:, :features], share_weight[:, features:]), axis=1),
        )
    )
    grad_attn_out = jnp.stack(
        (
            window_weight[:, wide:],
            causal_weight[:, wide : wide + features],
            causal_weight[:, wide + features : last],
            reverse_weight[:, features:],
        )
    )
    return rest + (
        gains,
        biases,
        grad_attn_in.astype(SINGLE),
        grad_attn_out.astype(SINGLE),
        jnp.stack((up_x, up_q)).astype(SINGLE),
        jnp.stack((down_x, down_q)).astype(SINGLE),
    )


def solution(mesh):
    placed = (
        P("rep", "blk", None),
        P("rep", None, None),
        P("rep", "blk"),
        P("rep"),
        P(),
        P(),
        P(),
        P(),
        P(),
        P(),
        P("rep", "blk", None),
        P("rep", None, None),
    )
    return jax.shard_map(
        body,
        mesh=mesh,
        in_specs=placed,
        out_specs=(
            P("rep", "blk", None),
            P("rep", None, "blk"),
            P("rep", "blk", None),
            P("rep", None, "blk"),
            P(None, "blk"),
            P(None, "blk"),
            P(None, "blk", None),
            P(None, "blk", None),
            P(None, "blk", None),
            P(None, "blk", None),
        ),
        check_vma=False,
    )
```

```python
import functools
import math

import jax
import jax.numpy as jnp
from jax import lax
from jax.experimental import pallas as pl
from jax.experimental.pallas import tpu as pltpu
from jax.sharding import PartitionSpec as P

HEADS = 12
WIN = 64
EPSILON = 1e-05
MASKED = -1e30
NARROW = jnp.bfloat16
SINGLE = jnp.float32
GROUP = 256
WINDOWS = 256
PAIR = 128
HEAD = 64
STRIP = 400
LONG = 400
CHUNK = 768


def dot(former, latter, ahead, behind, precision=None):
    return lax.dot_general(
        former,
        latter,
        (((ahead,), (behind,)), ((), ())),
        preferred_element_type=SINGLE,
        precision=precision,
    )


def plain(former, latter):
    return dot(former, latter, 1, 0)


def right_t(former, latter):
    return dot(former, latter, 1, 1)


def left_t(former, latter):
    return dot(former, latter, 0, 0)


def loop(count, action):
    def step(index, nothing):
        action(index)
        return nothing

    lax.fori_loop(0, count, step, 0)


def at(index, size):
    return pl.ds(pl.multiple_of(index * size, size), size)


def iota(shape, dim):
    return lax.broadcasted_iota(jnp.int32, shape, dim)


def statistics(tensor):
    average = jnp.mean(tensor, axis=-1, keepdims=True)
    centred = tensor - average
    spread = jnp.mean(centred * centred, axis=-1, keepdims=True)
    return centred, lax.rsqrt(spread + EPSILON)


def norm(tensor, gain, bias):
    centred, inverse = statistics(tensor)
    return centred * inverse * gain + bias


def norm_back(tensor, gain, upstream):
    centred, inverse = statistics(tensor)
    scaled = centred * inverse
    inner = upstream * gain
    grad = inverse * (
        inner
        - jnp.mean(inner, axis=-1, keepdims=True)
        - scaled * jnp.mean(inner * scaled, axis=-1, keepdims=True)
    )
    return (
        grad,
        jnp.sum(upstream * scaled, axis=0, keepdims=True),
        jnp.sum(upstream, axis=0, keepdims=True),
    )


def gelu_both(tensor):
    size = jnp.abs(tensor)
    ratio = 1.0 / (1.0 + (0.3275911 * math.sqrt(0.5)) * size)
    series = ratio * (
        0.254829592
        + ratio * (-0.284496736 + ratio * (1.421413741 + ratio * (-1.453152027 + ratio * 1.061405429)))
    )
    bell = jnp.exp(-0.5 * (tensor * tensor))
    tail = 0.5 * series * bell
    below = jnp.where(tensor >= 0, 1.0 - tail, tail)
    return tensor * below, below + tensor * bell * (1.0 / math.sqrt(2.0 * math.pi))


def half(which, value=1.0):
    return jnp.where(iota((1, PAIR), 1) // HEAD == which, value, 0.0).astype(NARROW)


def lower_lanes():
    return iota((1, PAIR), 1) < HEAD


def both(tensor, value=1.0):
    return jnp.concatenate((tensor * half(0, value), tensor * half(1, value)), axis=0)


def attend(queries, keys, values, mask):
    rows = queries.shape[0]
    scores = right_t(both(queries, 1.0 / math.sqrt(HEAD)), keys)
    weights, totals, logs = [], [], []
    for which in range(2):
        part = mask(scores[which * rows : (which + 1) * rows])
        peak = jnp.max(part, axis=-1, keepdims=True)
        part = jnp.exp(part - peak)
        total = jnp.sum(part, axis=-1, keepdims=True)
        weights.append(part.astype(NARROW))
        totals.append(1.0 / total)
        logs.append(peak + jnp.log(total))
    out = plain(jnp.concatenate(weights, axis=0), values)
    return jnp.where(lower_lanes(), out[:rows] * totals[0], out[rows:] * totals[1]), logs


def attend_back(queries, keys, values, upstream, logs, deltas, mask):
    scaled = queries * jnp.asarray(1.0 / math.sqrt(HEAD), NARROW)
    count = keys.shape[0]
    keys = both(keys)
    turned_keys = keys.T
    scores = right_t(keys, scaled)
    inner = right_t(both(values), upstream)
    weights, slopes = [], []
    for which in range(2):
        span = slice(which * count, (which + 1) * count)
        part = mask(scores[span])
        if logs is None:
            part = jnp.exp(part - jnp.max(part, axis=0, keepdims=True))
            part = part * (1.0 / jnp.sum(part, axis=0, keepdims=True))
        else:
            part = jnp.exp(part - logs[which])
        weights.append(part.astype(NARROW))
        slopes.append((part * (inner[span] - deltas[which])).astype(NARROW))
    slope = jnp.concatenate(slopes, axis=0)
    query_grad = plain(turned_keys, slope).T
    key_grad = plain(slope, scaled)
    value_grad = plain(jnp.concatenate(weights, axis=0), upstream)
    lanes = lower_lanes()
    return (
        query_grad,
        jnp.where(lanes, key_grad[:count], key_grad[count:]),
        jnp.where(lanes, value_grad[:count], value_grad[count:]),
    )


def exact_parts(tensor, count):
    parts = []
    for _ in range(count):
        parts.append(tensor.astype(NARROW))
        tensor = tensor - parts[-1].astype(SINGLE)
    return parts


def head_rows(tensor):
    features = tensor.shape[1]
    heads = 16
    chosen = jnp.where(
        iota((heads, features), 1) // HEAD == iota((heads, features), 0), 1.0, 0.0
    ).astype(NARROW)
    return functools.reduce(jnp.add, [right_t(chosen, part) for part in exact_parts(tensor, 2)])


def turn(columns):
    same = jnp.where(iota((16, columns.shape[1]), 0) == iota((16, columns.shape[1]), 1), 1.0, 0.0)
    same = same.astype(NARROW)
    return functools.reduce(jnp.add, [right_t(same, part) for part in exact_parts(columns, 3)])


def row_pair(ref, pair, span):
    tensor = ref[:, span]
    index = iota(tensor.shape, 0)
    return [
        jnp.sum(jnp.where(index == 2 * pair + which, tensor, 0.0), axis=0, keepdims=True)
        for which in range(2)
    ]


def chooser(rows, width, start, count):
    row = iota((rows, width), 0)
    hit = jnp.logical_and(iota((rows, width), 1) == row + start, row < count)
    return jnp.where(hit, 1.0, 0.0).astype(NARROW)


def spans(rows, size):
    edges = [(start, min(start + size, rows)) for start in range(0, rows, size)]
    if len(edges) > 1 and edges[-1][1] - edges[-1][0] < PAIR:
        edges[-2:] = [(edges[-2][0], rows)]
    return edges


def mark(log_ref, rows, head, value):
    log_ref[rows, :] = jnp.where(iota((1, PAIR), 1) == head, value, log_ref[rows, :])


def store_rows(ref, columns, value):
    ref[(slice(None),) * (len(ref.shape) - 1) + (columns,)] = value.astype(ref.dtype).reshape(
        ref.shape[:-1] + value.shape[1:]
    )


def nothing(*unused):
    return None


def copies(semaphores, *pairs):
    made = [
        pltpu.make_async_copy(source, target, semaphores.at[k])
        for k, (source, target) in enumerate(pairs)
    ]
    for one in made:
        one.start()
    return made


DIRECT = 8


def place_of(axis="blk"):
    return lax.axis_index(axis)


def flipped(index, mask, count):
    total, weight = 0, 1
    while weight < count:
        bit = (index // weight) % 2
        total = total + weight * ((1 - bit) if mask & weight else bit)
        weight *= 2
    return total


def piece_at(number, count):
    return flipped(place_of(), number, count) if count <= DIRECT else number


def window_forward(
    x_ref, gain_ref, bias_ref, a_in, a_out,
    n0_ref, pw_ref, mw_ref, x1_ref, nx_ref, vq_ref, ckv_ref,
    w_in, w_out, w_q, w_kv, sem,
    flush=nothing,
):
    rows, features = x_ref.shape
    loads = copies(
        sem,
        (a_in.at[0], w_in),
        (a_out.at[0], w_out),
        (a_in.at[3, :, pl.ds(0, features)], w_q),
        (a_in.at[2, :, pl.ds(features, 2 * features)], w_kv),
    )

    def first(i):
        span = at(i, GROUP)
        n0_ref[span, :] = norm(
            x_ref[span, :].astype(SINGLE), gain_ref[0:1, :], bias_ref[0:1, :]
        ).astype(NARROW)

    loop(rows // GROUP, first)
    loads[0].wait()

    def project(j):
        span = at(j, CHUNK)
        pw_ref[:, span] = plain(n0_ref[...], w_in[:, span]).astype(NARROW)

    loop(3 * features // CHUNK, project)
    flush(0)
    flush(1)
    window = jnp.where(
        iota((WINDOWS, WINDOWS), 0) // WIN == iota((WINDOWS, WINDOWS), 1) // WIN, 0.0, MASKED
    )

    def group(i):
        span = at(i, WINDOWS)
        for pair in range(features // PAIR):
            lane = pair * PAIR
            out, unused = attend(
                pw_ref[span, lane : lane + PAIR],
                pw_ref[span, features + lane : features + lane + PAIR],
                pw_ref[span, 2 * features + lane : 2 * features + lane + PAIR],
                lambda scores: scores + window,
            )
            mw_ref[span, lane : lane + PAIR] = out.astype(NARROW)

    loop(rows // WINDOWS, group)
    flush(2)
    loads[1].wait()

    def second(i):
        span = at(i, GROUP)
        total = x_ref[span, :].astype(SINGLE) + plain(mw_ref[span, :], w_out[...])
        x1_ref[span, :] = total
        nx_ref[span, :] = norm(total, gain_ref[3:4, :], bias_ref[3:4, :]).astype(NARROW)

    loop(rows // GROUP, second)
    flush(3)
    flush(4)
    loads[2].wait()
    vq_ref[...] = plain(nx_ref[...], w_q[...]).astype(NARROW)
    flush(5)
    loads[3].wait()

    def third(j):
        span = at(j, CHUNK)
        ckv_ref[:, span] = plain(nx_ref[...], w_kv[:, span]).astype(NARROW)

    loop(2 * features // CHUNK, third)


def causal_forward(
    q_ref, gain_ref, bias_ref, a_in, a_out,
    n1_ref, pq_ref, mq_ref, q1_ref, nq_ref, cq_ref, vkv_ref, log_ref,
    w_in, w_out, w_q, w_kv, logs, sem,
    flush=nothing,
):
    rows, features = q_ref.shape
    loads = copies(
        sem,
        (a_in.at[1], w_in),
        (a_out.at[1], w_out),
        (a_in.at[2, :, pl.ds(0, features)], w_q),
        (a_in.at[3, :, pl.ds(features, 2 * features)], w_kv),
    )

    def first(i):
        span = at(i, STRIP)
        n1_ref[span, :] = norm(
            q_ref[span, :].astype(SINGLE), gain_ref[1:2, :], bias_ref[1:2, :]
        ).astype(NARROW)

    loop(rows // STRIP, first)
    loads[0].wait()

    def project(j):
        span = at(j, CHUNK)
        pq_ref[:, span] = plain(n1_ref[...], w_in[:, span]).astype(NARROW)

    loop(3 * features // CHUNK, project)
    flush(0)
    flush(1)
    logs[...] = jnp.zeros_like(logs)

    def pair(p):
        for start in range(0, rows, LONG):
            end = min(start + LONG, rows)

            def mask(scores, start=start):
                shape = scores.shape
                return jnp.where(iota(shape, 1) <= iota(shape, 0) + start, scores, MASKED)

            out, sums = attend(
                pq_ref[start:end, at(p, PAIR)],
                pq_ref[0:end, at(p + features // PAIR, PAIR)],
                pq_ref[0:end, at(p + 2 * features // PAIR, PAIR)],
                mask,
            )
            mq_ref[start:end, at(p, PAIR)] = out.astype(NARROW)
            for which in range(2):
                mark(logs, slice(start, end), 2 * p + which, sums[which])

    loop(features // PAIR, pair)
    flush(2)
    log_ref[...] = turn(logs[...])
    loads[1].wait()

    def second(i):
        span = at(i, STRIP)
        total = q_ref[span, :].astype(SINGLE) + plain(mq_ref[span, :], w_out[...])
        q1_ref[span, :] = total
        nq_ref[span, :] = norm(total, gain_ref[2:3, :], bias_ref[2:3, :]).astype(NARROW)

    loop(rows // STRIP, second)
    if q1_ref.shape[0] > rows:
        q1_ref[rows:, :] = jnp.zeros_like(q1_ref[rows:, :])
        nq_ref[rows:, :] = jnp.zeros_like(nq_ref[rows:, :])
    flush(3)
    flush(4)
    loads[2].wait()
    cq_ref[...] = plain(nq_ref[0:rows, :], w_q[...]).astype(NARROW)
    flush(5)
    loads[3].wait()

    def third(j):
        span = at(j, CHUNK)
        vkv_ref[:, span] = plain(nq_ref[0:rows, :], w_kv[:, span]).astype(NARROW)

    loop(2 * features // CHUNK, third)


def cross_forward(pieces, cq_ref, ckv_ref, valid_ref, whole, *rest):
    log_refs, (logs,) = rest[:pieces], rest[pieces:]
    rows, features = cq_ref.shape
    part = log_refs[0].shape[1]
    logs[...] = jnp.zeros_like(logs)
    if whole.shape[0] > rows:
        whole[rows:, :] = jnp.zeros((whole.shape[0] - rows, features), NARROW)

    def pair(p):
        for start in range(0, rows, LONG):
            span = slice(start, min(start + LONG, rows))
            out, sums = attend(
                cq_ref[span, at(p, PAIR)],
                ckv_ref[:, at(p, PAIR)],
                ckv_ref[:, at(p + features // PAIR, PAIR)],
                lambda scores: scores + valid_ref[...],
            )
            whole[span, at(p, PAIR)] = out.astype(NARROW)
            for which in range(2):
                mark(logs, span, 2 * p + which, sums[which])

    loop(features // PAIR, pair)
    for k in range(pieces):
        log_refs[k][...] = turn(logs[at(piece_at(k, pieces), part), :])


def untwist(rows):
    same = jnp.where(iota((16, PAIR), 0) == iota((16, PAIR), 1), 1.0, 0.0).astype(NARROW)
    return functools.reduce(jnp.add, [left_t(part, same) for part in exact_parts(rows, 3)])


def merge_blocks(pieces, own_ref, *refs):
    logs, refs = refs[:pieces], refs[pieces:]
    halves, (co_ref, log_ref) = (refs[: pieces - 1], refs[pieces - 1 : -2]), refs[-2:]
    part, features = co_ref.shape
    width = features // 2
    peak = functools.reduce(jnp.maximum, [one[...] for one in logs])
    total = peak + jnp.log(functools.reduce(jnp.add, [jnp.exp(one[...] - peak) for one in logs]))
    log_ref[...] = total
    spread = jnp.where(
        iota((PAIR, features), 1) // HEAD == iota((PAIR, features), 0), 1.0, 0.0
    ).astype(NARROW)
    result = jnp.zeros(co_ref.shape, SINGLE)
    for k in range(pieces):
        weight = untwist(jnp.exp(logs[k][...] - total))
        high = weight.astype(NARROW)
        low = (weight - high.astype(SINGLE)).astype(NARROW)
        if k == 0:
            block = own_ref[at(place_of(), part), :]
        else:
            block = jnp.concatenate((halves[0][k - 1][...], halves[1][k - 1][...]), axis=1)
        result = result + (plain(high, spread) + plain(low, spread)) * block.astype(SINGLE)
    co_ref[...] = result.astype(NARROW)


def reverse_forward(
    length_ref, vq_ref, vkv_ref, x1_ref, a_out,
    mv_ref, x2_ref, log_ref,
    w_out, logs, sem,
    ready=nothing, flush=nothing,
):
    rows, features = vq_ref.shape
    keys = vkv_ref.shape[0]
    (load,) = copies(sem, (a_out.at[3], w_out))
    logs[...] = jnp.zeros_like(logs)
    bias = jnp.where(iota((1, keys), 1) < length_ref[0], 0.0, MASKED)

    def pair(p):
        for start in range(0, rows, WINDOWS):
            span = slice(start, start + WINDOWS)
            out, sums = attend(
                vq_ref[span, at(p, PAIR)],
                vkv_ref[:, at(p, PAIR)],
                vkv_ref[:, at(p + features // PAIR, PAIR)],
                lambda scores: scores + bias,
            )
            mv_ref[span, at(p, PAIR)] = out.astype(NARROW)
            for which in range(2):
                mark(logs, span, 2 * p + which, sums[which])

    loop(features // PAIR, pair)
    flush(0)
    log_ref[...] = turn(logs[...])
    load.wait()
    ready(3)

    def second(i):
        span = at(i, GROUP)
        x2_ref[span, :] = x1_ref[span, :] + plain(mv_ref[span, :], w_out[...])

    loop(rows // GROUP, second)


def feed_forward_step(block, normed, up, down, cot, hidden, slope, out, grad):
    rows = normed.shape[0]

    def strip(i):
        span = at(i, block)
        value, rise = gelu_both(plain(normed[span, :], up[...]))
        hidden[span, :] = value.astype(NARROW)
        slope[span, :] = (right_t(cot[span, :], down[...]) * rise).astype(NARROW)
        out[span, :] += plain(hidden[span, :], down[...])
        grad[span, :] += right_t(slope[span, :], up[...])

    loop(rows // block, strip)


def patch_feed_forward(
    x2_ref, cot_ref, gain_ref, bias_ref, up_ref, down_ref,
    x3_ref, dx2_ref, up_grad_ref, down_grad_ref, norm_ref,
    normed, hidden, slope, out, grad,
):
    rows = x2_ref.shape[0]
    step = pl.program_id(0)

    @pl.when(step == 0)
    def begin():
        def first(i):
            span = at(i, GROUP)
            normed[span, :] = norm(
                x2_ref[span, :], gain_ref[5:6, :], bias_ref[5:6, :]
            ).astype(NARROW)
            out[span, :] = x2_ref[span, :]
            grad[span, :] = jnp.zeros_like(grad[span, :])

        loop(rows // GROUP, first)

    feed_forward_step(
        512, normed, up_ref.at[0], down_ref.at[0], cot_ref, hidden, slope, out, grad
    )
    up_grad_ref[...] = left_t(normed[...], slope[...]).astype(NARROW)
    down_grad_ref[...] = left_t(hidden[...], cot_ref[...]).astype(NARROW)

    @pl.when(step == pl.num_programs(0) - 1)
    def finish():
        norm_ref[...] = jnp.zeros_like(norm_ref)

        def last(i):
            span = at(i, GROUP)
            x3_ref[span, :] = out[span, :].astype(NARROW)
            part, gain, bias = norm_back(x2_ref[span, :], gain_ref[5:6, :], grad[span, :])
            dx2_ref[span, :] = cot_ref[span, :].astype(SINGLE) + part
            norm_ref[0:1, :] += gain
            norm_ref[1:2, :] += bias

        loop(rows // GROUP, last)


def place_parts(ref, pieces, parts, sem):
    part, features = parts[0].shape
    width = features // 2
    pairs = [(parts[0], ref.at[at(piece_at(0, pieces), part), :])]
    for number in range(2):
        for k in range(1, pieces):
            pairs.append(
                (
                    parts[number * (pieces - 1) + k],
                    ref.at[at(piece_at(k, pieces), part), pl.ds(number * width, width)],
                )
            )
    return copies(sem, *pairs)


def query_feed_forward(
    pieces, share, hidden_share, q1_ref, cot_ref, gain_ref, bias_ref,
    w_out, up_ref, down_ref, *rest,
):
    parts, rest = rest[: 2 * pieces - 1], rest[2 * pieces - 1 :]
    (
        q3_ref, dq2_ref, up_grad_ref, down_grad_ref, norm_ref, co_ref,
        q2, normed, chosen, hidden, slope, out, grad, sem,
    ) = rest
    rows, features = cot_ref.shape
    width = up_ref.shape[2]
    step = pl.program_id(0)

    @pl.when(step == 0)
    def begin():
        for one in place_parts(co_ref, pieces, parts, sem):
            one.wait()

        def first(i):
            span = at(i, STRIP)
            total = q1_ref[span, :] + plain(co_ref[span, :], w_out[0])
            q2[span, :] = total
            out[span, :] = total
            normed[span, :] = norm(total, gain_ref[4:5, :], bias_ref[4:5, :]).astype(NARROW)
            grad[span, :] = jnp.zeros_like(grad[span, :])

        loop(rows // STRIP, first)
        chosen[...] = right_t(
            chooser(chosen.shape[0], features, place_of() * share, share), normed[...]
        ).astype(NARROW)

    feed_forward_step(
        rows, normed, up_ref.at[0], down_ref.at[0], cot_ref, hidden, slope, out, grad
    )
    up_grad_ref[...] = plain(chosen[...], slope[...]).astype(NARROW)
    begins = place_of() * hidden_share

    @pl.when(begins // width == step)
    def own_hidden():
        taken = right_t(
            chooser(down_grad_ref.shape[0], width, begins - step * width, hidden_share),
            hidden[...],
        ).astype(NARROW)
        down_grad_ref[...] = plain(taken, cot_ref[...]).astype(NARROW)

    @pl.when(step == pl.num_programs(0) - 1)
    def finish():
        norm_ref[...] = jnp.zeros_like(norm_ref)

        def last(i):
            span = at(i, STRIP)
            q3_ref[span, :] = out[span, :].astype(NARROW)
            piece, gain, bias = norm_back(q2[span, :], gain_ref[4:5, :], grad[span, :])
            dq2_ref[span, :] = cot_ref[span, :].astype(SINGLE) + piece
            norm_ref[0:1, :] += gain
            norm_ref[1:2, :] += bias

        loop(rows // STRIP, last)


def reverse_backward(
    pieces, length_ref, dx2_ref, mv_ref, vq_ref, vkv_ref, nx_ref, log_ref, a_out,
    *rest, launch=nothing, tick=nothing, ready=nothing,
):
    dvq_ref, weight_ref, rest = rest[0], rest[1], rest[2:]
    k_refs, v_refs, rest = rest[:pieces], rest[pieces : 2 * pieces], rest[2 * pieces :]
    w_out, rounded, dmv, deltas, dkv, sem = rest
    rows, features = vq_ref.shape
    keys = vkv_ref.shape[0]
    part = k_refs[0].shape[0]
    (load,) = copies(sem, (a_out.at[3], w_out))
    rounded[...] = dx2_ref[...].astype(NARROW)
    load.wait()
    dmv[...] = right_t(rounded[...], w_out[...]).astype(NARROW)
    store_rows(
        weight_ref, slice(features, 2 * features), left_t(mv_ref[...], rounded[...])
    )
    deltas[...] = head_rows(dmv[...].astype(SINGLE) * mv_ref[...].astype(SINGLE))
    if dkv.shape[0] > keys:
        dkv[keys:, :] = jnp.zeros((dkv.shape[0] - keys, 2 * features), SINGLE)
    size = 256
    for k in (3, 4, 6):
        ready(k)

    def pair(p):
        pl.when(p == 2)(lambda: tick(1))
        pl.when(p == 4)(lambda: tick(2))
        for strip in range(rows // size):
            span = slice(strip * size, (strip + 1) * size)

            def mask(scores):
                return jnp.where(iota(scores.shape, 0) < length_ref[0], scores, MASKED)

            dq, dk, dv = attend_back(
                vq_ref[span, at(p, PAIR)],
                vkv_ref[:, at(p, PAIR)],
                vkv_ref[:, at(p + features // PAIR, PAIR)],
                dmv[span, at(p, PAIR)],
                row_pair(log_ref, p, span),
                row_pair(deltas, p, span),
                mask,
            )
            dvq_ref[span, at(p, PAIR)] = (dq * (1.0 / math.sqrt(HEAD))).astype(NARROW)
            if strip == 0:
                dkv[0:keys, at(p, PAIR)] = dk
                dkv[0:keys, at(p + features // PAIR, PAIR)] = dv
            else:
                dkv[0:keys, at(p, PAIR)] += dk
                dkv[0:keys, at(p + features // PAIR, PAIR)] += dv

    loop(features // PAIR, pair)
    ready(5)
    store_rows(weight_ref, slice(0, features), left_t(nx_ref[...], dvq_ref[...]))
    launch(1)
    for k in range(pieces):
        span = at(piece_at(k, pieces), part)
        width = k_refs[k].shape[1]
        k_refs[k][...] = dkv[span, 0:width].astype(NARROW)
        v_refs[k][...] = dkv[span, width:].astype(NARROW)


def cross_backward(
    pieces, share, dq2_ref, co_ref, cq_ref, ckv_ref, valid_ref, a_out, *rest, ready=nothing
):
    log_parts, rest = rest[:pieces], rest[pieces:]
    dckv_ref, weight_ref, rest = rest[0], rest[1], rest[2:]
    q_refs, (w_out, rounded, dco, deltas, logs, turned, dq_all, dkv, sem) = (
        rest[:pieces],
        rest[pieces:],
    )
    rows, features = cq_ref.shape
    part = log_parts[0].shape[1]
    (load,) = copies(sem, (a_out.at[2], w_out))
    for k in range(pieces):
        logs[at(piece_at(k, pieces), part), :] = untwist(log_parts[k][...])
    turned[...] = turn(logs[0:rows, :])
    rounded[...] = dq2_ref[...].astype(NARROW)
    load.wait()
    dco[...] = right_t(rounded[...], w_out[...]).astype(NARROW)
    taken = right_t(
        chooser(weight_ref.shape[0], features, place_of() * share, share), co_ref[0:rows, :]
    ).astype(NARROW)
    weight_ref[...] = plain(taken, rounded[...]).astype(NARROW)
    deltas[...] = head_rows(dco[...].astype(SINGLE) * co_ref[0:rows, :].astype(SINGLE))
    if dq_all.shape[0] > rows:
        dq_all[rows:, :] = jnp.zeros((dq_all.shape[0] - rows, features), NARROW)
    edges = spans(rows, 512)
    ready(2)
    ready(3)

    def pair(p):
        for number, (start, end) in enumerate(edges):
            span = slice(start, end)
            dq, dk, dv = attend_back(
                cq_ref[span, at(p, PAIR)],
                ckv_ref[:, at(p, PAIR)],
                ckv_ref[:, at(p + features // PAIR, PAIR)],
                dco[span, at(p, PAIR)],
                row_pair(turned, p, span),
                row_pair(deltas, p, span),
                lambda scores: scores + valid_ref[...],
            )
            dq_all[span, at(p, PAIR)] = (dq * (1.0 / math.sqrt(HEAD))).astype(NARROW)
            if number == 0:
                dkv[:, at(p, PAIR)] = dk
                dkv[:, at(p + features // PAIR, PAIR)] = dv
            else:
                dkv[:, at(p, PAIR)] += dk
                dkv[:, at(p + features // PAIR, PAIR)] += dv

    loop(features // PAIR, pair)
    dckv_ref[...] = dkv[...].astype(NARROW)
    for k in range(pieces):
        q_refs[k][...] = dq_all[at(piece_at(k, pieces), part), :]


def patch_backward(
    x_ref, dx2_ref, x1_ref, nx_ref, n0_ref, pw_ref, mw_ref, dvq_ref, dckv_ref, gain_ref, a_in, a_out,
    kv_weight_ref, weight_ref, grad_ref, norm_ref,
    w_in, w_out, w_q, w_kv, dx1, rounded, dmw, deltas, dpw, sem,
    launch=nothing, ready=nothing, flush=nothing,
):
    rows, features = x_ref.shape
    loads = copies(
        sem,
        (a_in.at[3, :, pl.ds(0, features)], w_q),
        (a_in.at[2, :, pl.ds(features, 2 * features)], w_kv),
        (a_out.at[0], w_out),
        (a_in.at[0], w_in),
    )
    norm_ref[...] = jnp.zeros_like(norm_ref)
    for start in range(0, 2 * features, CHUNK):
        span = slice(start, start + CHUNK)
        store_rows(kv_weight_ref, span, left_t(nx_ref[...], dckv_ref[:, span]))
    launch(0)
    flush(0)
    loads[0].wait()
    loads[1].wait()

    def first(i):
        span = at(i, GROUP)
        upstream = right_t(dvq_ref[span, :], w_q[...]) + right_t(dckv_ref[span, :], w_kv[...])
        part, gain, bias = norm_back(x1_ref[span, :], gain_ref[3:4, :], upstream)
        total = dx2_ref[span, :] + part
        dx1[span, :] = total
        rounded[span, :] = total.astype(NARROW)
        norm_ref[0:1, :] += gain
        norm_ref[1:2, :] += bias

    loop(rows // GROUP, first)
    loads[2].wait()
    ready(6)
    dmw[...] = right_t(rounded[...], w_out[...]).astype(NARROW)
    store_rows(
        weight_ref, slice(3 * features, 4 * features), left_t(mw_ref[...], rounded[...])
    )
    deltas[...] = head_rows(dmw[...].astype(SINGLE) * mw_ref[...].astype(SINGLE))
    ready(5)
    window = jnp.where(
        iota((WINDOWS, WINDOWS), 0) // WIN == iota((WINDOWS, WINDOWS), 1) // WIN, 0.0, MASKED
    )

    def group(i):
        span = at(i, WINDOWS)
        for pair in range(features // PAIR):
            lane = pair * PAIR
            dq, dk, dv = attend_back(
                pw_ref[span, lane : lane + PAIR],
                pw_ref[span, features + lane : features + lane + PAIR],
                pw_ref[span, 2 * features + lane : 2 * features + lane + PAIR],
                dmw[span, lane : lane + PAIR],
                None,
                [deltas[2 * pair + w : 2 * pair + w + 1, span] for w in range(2)],
                lambda scores: scores + window,
            )
            dpw[span, lane : lane + PAIR] = (dq * (1.0 / math.sqrt(HEAD))).astype(NARROW)
            dpw[span, features + lane : features + lane + PAIR] = dk.astype(NARROW)
            dpw[span, 2 * features + lane : 2 * features + lane + PAIR] = dv.astype(NARROW)

    loop(rows // WINDOWS, group)
    ready(4)
    for start in range(0, 3 * features, CHUNK):
        span = slice(start, start + CHUNK)
        store_rows(weight_ref, span, left_t(n0_ref[...], dpw[:, span]))
    launch(1)
    flush(1)
    ready(0)
    loads[3].wait()

    def last(i):
        span = at(i, GROUP)
        upstream = right_t(dpw[span, :], w_in[...])
        part, gain, bias = norm_back(x_ref[span, :].astype(SINGLE), gain_ref[0:1, :], upstream)
        grad_ref[span, :] = dx1[span, :] + part
        norm_ref[2:3, :] += gain
        norm_ref[3:4, :] += bias

    loop(rows // GROUP, last)


def share_backward(
    pieces, q1, nq, gain_ref, a_in, *rest, launch=nothing
):
    parts = [rest[k * pieces : (k + 1) * pieces] for k in range(3)]
    rest = rest[3 * pieces :]
    grad_ref, weight_ref, norm_ref, w_q, w_kv, summed, q1_ref, nq_ref, sem = rest
    part, features = q1_ref.shape
    *loads, load_q, load_n = copies(
        sem,
        (a_in.at[2, :, pl.ds(0, features)], w_q),
        (a_in.at[3, :, pl.ds(features, 2 * features)], w_kv),
        (q1.at[at(place_of(), part), :], q1_ref),
        (nq.at[at(place_of(), part), :], nq_ref),
    )
    start = 0
    for k in range(3):
        width = parts[k][0].shape[1]
        total = functools.reduce(jnp.add, [one[...].astype(SINGLE) for one in parts[k]])
        summed[:, start : start + width] = total.astype(NARROW)
        start += width
    for load in loads:
        load.wait()
    upstream = right_t(summed[:, 0:features], w_q[...]) + right_t(summed[:, features:], w_kv[...])
    load_q.wait()
    piece, gain, bias = norm_back(q1_ref[...], gain_ref[2:3, :], upstream)
    grad_ref[...] = piece.astype(NARROW)
    launch(0)
    load_n.wait()
    for k in range(3):
        span = slice(k * features, (k + 1) * features)
        store_rows(weight_ref, span, left_t(nq_ref[...], summed[:, span]))
    launch(1)
    norm_ref[...] = jnp.zeros_like(norm_ref)
    norm_ref[0:1, :] = gain
    norm_ref[1:2, :] = bias


def causal_backward(
    pieces, share, q_ref, dq2_ref, n1_ref, pq_ref, mq_ref, log_ref, cross_ref, gain_ref,
    norm_x, norm_two, norm_four, norm_five, a_in, a_out, *rest, ready=nothing
):
    parts, rest = rest[: 2 * pieces - 1], rest[2 * pieces - 1 :]
    (
        weight_ref, grad_ref, norm_ref,
        w_in, w_out, gathered, dq1, rounded, dmq, deltas, dkv, dpq, norm_one, norm_all, sem,
    ) = rest
    rows, features = q_ref.shape
    placed = place_parts(gathered, pieces, parts, sem)
    loads = copies(sem.at[pl.ds(len(placed), 2)], (a_out.at[1], w_out), (a_in.at[1], w_in))
    for one in placed:
        one.wait()

    def first(i):
        span = at(i, STRIP)
        total = dq2_ref[span, :] + gathered[span, :].astype(SINGLE)
        dq1[span, :] = total
        rounded[span, :] = total.astype(NARROW)

    loop(rows // STRIP, first)
    loads[0].wait()
    dmq[...] = right_t(rounded[...], w_out[...]).astype(NARROW)
    ready(4)
    chosen = chooser(weight_ref.shape[0], features, place_of() * share, share)
    taken = right_t(chosen, mq_ref[...]).astype(NARROW)
    weight_ref[:, 3 * features : 4 * features] = plain(taken, rounded[...]).astype(NARROW)
    weight_ref[:, 4 * features : 5 * features] = cross_ref[...]
    weight_ref[:, 5 * features :] = jnp.zeros_like(weight_ref[:, 5 * features :])
    deltas[...] = head_rows(dmq[...].astype(SINGLE) * mq_ref[...].astype(SINGLE))
    edges = spans(rows, 256)
    ready(3)
    ready(5)

    def pair(p):
        for number, (start, end) in reversed(list(enumerate(edges))):
            span = slice(start, end)

            def mask(scores, start=start):
                shape = scores.shape
                return jnp.where(iota(shape, 0) <= iota(shape, 1) + start, scores, MASKED)

            dq, dk, dv = attend_back(
                pq_ref[span, at(p, PAIR)],
                pq_ref[0:end, at(p + features // PAIR, PAIR)],
                pq_ref[0:end, at(p + 2 * features // PAIR, PAIR)],
                dmq[span, at(p, PAIR)],
                row_pair(log_ref, p, span),
                row_pair(deltas, p, span),
                mask,
            )
            dpq[span, at(p, PAIR)] = (dq * (1.0 / math.sqrt(HEAD))).astype(NARROW)
            if end == rows:
                dkv[0:end, 0:PAIR] = dk
                dkv[0:end, PAIR:] = dv
            else:
                dkv[0:end, 0:PAIR] += dk
                dkv[0:end, PAIR:] += dv
        dpq[:, at(p + features // PAIR, PAIR)] = dkv[:, 0:PAIR].astype(NARROW)
        dpq[:, at(p + 2 * features // PAIR, PAIR)] = dkv[:, PAIR:].astype(NARROW)

    loop(features // PAIR, pair)
    ready(2)
    taken = right_t(chosen, n1_ref[...]).astype(NARROW)
    weight_ref[:, 0 : 3 * features] = plain(taken, dpq[...]).astype(NARROW)
    loads[1].wait()
    norm_one[...] = jnp.zeros_like(norm_one)

    def last(i):
        span = at(i, STRIP)
        upstream = right_t(dpq[span, :], w_in[...])
        piece, gain, bias = norm_back(q_ref[span, :].astype(SINGLE), gain_ref[1:2, :], upstream)
        grad_ref[span, :] = dq1[span, :] + piece
        norm_one[0:1, :] += gain
        norm_one[1:2, :] += bias

    loop(rows // STRIP, last)
    leader = jnp.where(place_of() == 0, 1.0, 0.0)
    norm_all[...] = jnp.zeros_like(norm_all)
    for row, (ref, source, scale) in enumerate(
        (
            (norm_x, 2, 1.0), (norm_one, 0, leader), (norm_two, 0, 1.0), (norm_x, 0, 1.0),
            (norm_four, 0, leader), (norm_five, 0, 1.0),
        )
    ):
        norm_all[row : row + 1, :] = ref[source : source + 1, :] * scale
        norm_all[8 + row : 9 + row, :] = ref[source + 1 : source + 2, :] * scale
    if len(norm_ref.shape) == 2:
        norm_ref[...] = norm_all[...]
    else:
        norm_ref[...] = jnp.zeros_like(norm_ref)
        for owner in range(norm_ref.shape[0]):
            norm_ref[owner, :, 0:share] = norm_all[:, owner * share : (owner + 1) * share]


def assemble(groups, count, *refs, ready=nothing, flush=nothing):
    parts, refs = refs[: 4 * groups], refs[4 * groups :]
    norms, refs = refs[:count], refs[count:]
    in_ref, out_ref, up_ref, down_ref, gain_ref, bias_ref, share, causal = refs
    features = down_ref.shape[2]
    rep = place_of("rep")

    def corners(number, write):
        for k in range(4):
            ready(4 * number + k)
            owner = flipped(rep, k, 4)
            piece = parts[4 * number + k][...]
            height, width = piece.shape[-2:]
            piece = piece.reshape(height, width)
            write(
                pl.ds(pl.multiple_of((owner % 2) * height, height), height),
                pl.multiple_of((owner // 2) * width, width), width, piece,
            )

    def into(ref, index, start=0):
        def write(rows, column, width, piece):
            ref[index, rows, pl.ds(column + start, width)] = piece

        return write

    up_x, down_x, reverse, window, kv, shared, up_q, down_q, rest = range(groups)

    def keep_causal(rows, column, width, piece):
        causal[rows, pl.ds(column, width)] = piece

    def keep_share(rows, column, width, piece):
        share[rows, pl.ds(column, width)] = piece

    corners(up_q, into(up_ref, 1))
    corners(down_q, into(down_ref, 1))
    corners(up_x, into(up_ref, 0))
    flush(2)
    corners(down_x, into(down_ref, 0))
    flush(3)
    first = 4 * groups
    for k in range(count):
        ready(first + k)
    terms = [norms[0][place_of()]] + [one[...] for one in norms[1:]]
    total = functools.reduce(jnp.add, terms)
    columns = gain_ref.shape[1]
    gain_ref[...] = total[0:6, 0:columns]
    bias_ref[...] = total[8:14, 0:columns]
    flush(4)
    flush(5)
    corners(reverse, keep_share)
    in_ref[3, :, 0:features] = share[:, 0:features]
    out_ref[3, :, :] = share[:, features : 2 * features]
    corners(window, keep_share)
    in_ref[0, :, :] = share[:, 0 : 3 * features]
    out_ref[0, :, :] = share[:, 3 * features :]
    corners(rest, keep_causal)
    in_ref[1, :, :] = causal[:, 0 : 3 * features]
    out_ref[1, :, :] = causal[:, 3 * features : 4 * features]
    out_ref[2, :, :] = causal[:, 4 * features : 5 * features]
    flush(1)
    corners(kv, into(in_ref, 2, features))
    corners(shared, keep_share)
    in_ref[2, :, 0:features] = share[:, 0:features]
    in_ref[3, :, features:] = share[:, features : 3 * features]
    flush(0)


def bits_of(count):
    return max(count - 1, 0).bit_length()


def swap(tensor, axis, mask):
    return lax.ppermute(tensor, axis, [(i, i ^ mask) for i in range(lax.axis_size(axis))])


def pick(tensor, place, dim):
    return lax.dynamic_index_in_dim(tensor, place, dim, keepdims=False)


def fold(tensor, axis, bit, dim):
    own = (lax.axis_index(axis) >> bit) & 1
    arrived = swap(pick(tensor, 1 - own, dim).astype(NARROW), axis, 1 << bit)
    return pick(tensor, own, dim).astype(SINGLE) + arrived.astype(SINGLE)


def unfold(tensor, axis, bit, dim):
    own = (lax.axis_index(axis) >> bit) & 1
    arrived = swap(tensor, axis, 1 << bit)
    return jnp.where(
        own == 0,
        jnp.stack((tensor, arrived), axis=dim),
        jnp.stack((arrived, tensor), axis=dim),
    )


def scatter_blk(tensor):
    bits = bits_of(lax.axis_size("blk"))
    tensor = tensor.reshape((2,) * bits + tensor.shape[1:])
    for bit in range(bits):
        tensor = fold(tensor, "blk", bit, bits - 1 - bit)
    return tensor


def sum_rep_scatter(tensor, dim):
    bits = bits_of(lax.axis_size("rep"))
    shape = tensor.shape
    tensor = tensor.reshape(
        shape[:dim] + (2,) * bits + (shape[dim] // 2**bits,) + shape[dim + 1 :]
    )
    for bit in range(bits):
        tensor = fold(tensor, "rep", bit, dim)
    return tensor


def gather_rep(tensor, dim):
    bits = bits_of(lax.axis_size("rep"))
    for bit in reversed(range(bits)):
        tensor = unfold(tensor, "rep", bit, dim)
    shape = tensor.shape
    return tensor.reshape(shape[:dim] + (-1,) + shape[dim + bits + 1 :])


def reduce_all(tensor):
    count = lax.axis_size("blk")
    tensor = tensor.reshape(count, tensor.shape[0] // count, tensor.shape[1])
    tensor = sum_rep_scatter(tensor, 1)
    tensor = scatter_blk(tensor).astype(NARROW)
    return gather_rep(tensor, 0)


def reduce_rep(tensor):
    return gather_rep(sum_rep_scatter(tensor, 0).astype(NARROW), 0)


def exchange(pieces):
    whole = lax.all_to_all(jnp.stack(pieces), "blk", 0, 0)
    return [whole[k] for k in range(len(pieces))]


def gather(tensor):
    count = lax.axis_size("blk")
    whole = lax.all_gather(tensor, "blk")
    return [whole[k] for k in range(count)]


def whole(ref):
    return ref


class Fold:
    def __init__(self, own, take, arrived, shape, keep=whole, keep_shape=None):
        self.own, self.take, self.arrived, self.shape = own, take, arrived, shape
        self.keep, self.keep_shape = keep, keep_shape or shape
        self.dtype = own.dtype


class Move:
    late = None

    def __init__(self, source, shape, axis, flip, take=whole, phase=0):
        self.source, self.shape, self.axis, self.flip, self.take = source, shape, axis, flip, take
        self.phase = phase
        self.dtype = source.dtype


def lanes_of(ref, start, width):
    return ref.at[(slice(None),) * (len(ref.shape) - 1) + (pl.ds(start, width),)]


class Reduction:
    def __init__(self, tensor, blocks=None):
        if blocks == 1:
            tensor = tensor.reshape(1, 1, 2, tensor.shape[0] // 2, tensor.shape[1])
        elif len(tensor.shape) == 2:
            blocks = lax.axis_size("blk")
            height = tensor.shape[0] // blocks
            tensor = tensor.reshape(blocks // 2, 2, 2, height // 2, tensor.shape[1])
        self.tensor, self.take, self.arrived, self.shape = tensor, whole, [], tensor.shape

    def fold(self, keep=whole, keep_shape=None):
        return Fold(self.tensor, self.take, self.arrived, self.shape, keep, keep_shape)

    def moves(self, stage):
        shape = self.shape
        if stage == "core":
            self.next = shape[:2] + shape[3:]
            return [
                Move(self.tensor, self.next, "rep", 1,
                     lambda ref: ref.at[:, :, 1 - place_of("rep") % 2])
            ]
        if stage == "x":
            width = shape[-1] // 2
            self.next = shape[:-1] + (width,)

            def own(ref):
                return lanes_of(ref, pl.multiple_of((place_of("rep") // 2) * width, width), width)

            def other(ref):
                start = (1 - place_of("rep") // 2) * width
                return lanes_of(ref, pl.multiple_of(start, width), width)

            return [Move(self.fold(own, self.next), self.next, "rep", 2, other)]
        if stage == "y":
            self.next = shape[:1] + shape[2:]
            fold = self.fold(lambda ref: ref.at[:, place_of() % 2], self.next)
            return [Move(fold, self.next, "blk", 1, lambda ref: ref.at[:, 1 - place_of() % 2])]
        if stage == "z":
            length = shape[0]
            self.next = shape[1:]
            fold = self.fold(lambda ref: ref.at[place_of() // 2], self.next)
            return [
                Move(fold, self.next, "blk", 2 * k,
                     lambda ref, k=k: ref.at[flipped(place_of() // 2, k, length)])
                for k in range(1, length)
            ]
        if stage == "back":
            fold = self.fold()
            return [Move(fold, shape, "rep", k) for k in range(1, 4)]
        if stage == "back_x":
            return [Move(self.fold(), shape, "rep", 2)]
        return [Move(self.tensor, shape, "rep", 1), Move(self.other, shape, "rep", 1)]

    def absorb(self, stage, arrived, kept):
        if stage == "core":
            self.take = lambda ref: ref.at[:, :, place_of("rep") % 2]
        else:
            self.take = whole
        if kept:
            self.tensor = kept[0]
        if stage in ("back", "back_x", "back_core"):
            if stage == "back_x":
                self.other = arrived[0]
                return
            if stage == "back":
                self.result = [self.tensor] + list(arrived)
            else:
                self.result = [self.tensor, arrived[0], self.other, arrived[1]]
            return
        self.shape, self.arrived = self.next, list(arrived)


class Exchange:
    def __init__(self, pieces):
        self.pieces = pieces

    def moves(self, stage):
        return [Move(one, one.shape, "blk", k) for k, one in enumerate(self.pieces) if k]

    def absorb(self, stage, arrived, kept):
        self.result = self.pieces[:1] + list(arrived)


class Pieces:
    def __init__(self, tensor, part, start, width):
        self.tensor, self.part, self.start, self.width = tensor, part, start, width

    def moves(self, stage):
        part, span = self.part, slice(self.start, self.start + self.width)
        count = lax.axis_size("blk")
        return [
            Move(self.tensor, (part, self.width), "blk", k,
                 lambda ref, k=k: ref.at[at(flipped(place_of(), k, count), part), span])
            for k in range(1, count)
        ]

    def absorb(self, stage, arrived, kept):
        self.result = list(arrived)


class Gather:
    def __init__(self, tensor):
        self.tensor = tensor

    def moves(self, stage):
        return [
            Move(self.tensor, self.tensor.shape, "blk", k) for k in range(1, lax.axis_size("blk"))
        ]

    def absorb(self, stage, arrived, kept):
        self.result = [self.tensor] + list(arrived)


class Spread:
    def __init__(self, tensor):
        self.tensor = tensor

    def moves(self, stage):
        count = lax.axis_size("blk")
        rows, width = self.tensor.shape[0], self.tensor.shape[1] // 2
        moves, self.places = [], []
        for number in range(2):
            span = slice(number * width, (number + 1) * width)
            own = lambda ref, span=span: ref.at[:, span]
            along = []
            for k in range(2, count, 2):
                along.append(Move(self.tensor, (rows, width), "blk", k, own, number))
                self.places.append((number, k))
            moves += along
            moves.append(Move(self.tensor, (rows, width), "blk", 1, own, number + 1))
            self.places.append((number, 1))
            for one in along:
                moves.append(Move(one, (rows, width), "blk", 1, whole, number + 1))
                self.places.append((number, one.flip + 1))
        return moves

    def absorb(self, stage, arrived, kept):
        found = dict(zip(self.places, arrived))
        count = lax.axis_size("blk")
        self.result = [found[number, k] for number in range(2) for k in range(1, count)]


class Norms:
    def __init__(self, tensor):
        self.tensor = tensor

    def moves(self, stage):
        axis = "rep" if stage == "out" else "blk"
        count = lax.axis_size(axis)
        shape = self.tensor.shape
        if stage == "out":
            return [Move(self.tensor, shape, axis, k) for k in range(1, count)]
        fold = Fold(self.tensor, whole, self.arrived, shape)
        return [
            Move(fold, shape[1:], axis, k,
                 lambda ref, k=k: ref.at[flipped(place_of(), k, count)])
            for k in range(1, count)
        ]

    def absorb(self, stage, arrived, kept):
        if stage == "out":
            self.arrived = list(arrived)
        else:
            self.result = [kept[0]] + list(arrived)


VMEM = pl.BlockSpec(memory_space=pltpu.VMEM)
SMEM = pl.BlockSpec(memory_space=pltpu.SMEM)
ANY = pl.BlockSpec(memory_space=pl.ANY)


def like(*shape, kind=NARROW):
    return jax.ShapeDtypeStruct(shape, kind)


def index_of(items, item):
    return next(k for k, one in enumerate(items) if one is item)


def call(
    kernel, outs, operands, specs, scratch, flops, grid=None, out_specs=None, semaphores=0,
    moves=(), ident=None, ticking=False, lazy=(), early=(),
):
    scratch = [pltpu.VMEM(shape, kind) for shape, kind in scratch]
    if semaphores:
        scratch.append(pltpu.SemaphoreType.DMA((semaphores,)))
    out_specs = [VMEM] * len(outs) if out_specs is None else out_specs
    extra = {} if grid is None else {"grid": grid}
    params = {}
    sources, folds = [], []

    def need(array):
        if not any(array is one for one in sources):
            sources.append(array)

    for move in moves:
        if isinstance(move.source, Fold):
            if not any(move.source is one for one in folds):
                folds.append(move.source)
                for array in [move.source.own] + move.source.arrived:
                    need(array)
        elif move.late is None and not isinstance(move.source, Move):
            need(move.source)
    fixed_in, fixed_out = len(operands), len(outs)
    partners = sorted({(move.axis, move.flip) for move in moves})
    lasts = max([move.phase for move in moves], default=0)
    held_in = [k for k, spec in enumerate(specs) if spec is VMEM]
    held_out = [k for k, spec in enumerate(out_specs) if spec is VMEM]
    own_scratch = len(scratch)
    scratch += [pltpu.VMEM(operands[k].shape, operands[k].dtype) for k in held_in]
    scratch += [pltpu.VMEM(outs[k].shape, outs[k].dtype) for k in held_out]
    terms = sum(1 + len(fold.arrived) for fold in folds)
    for fold in folds:
        scratch += [pltpu.VMEM(fold.shape, NARROW)] * (1 + len(fold.arrived))
    for number in (len(held_in), len(held_out), terms, len(folds), len(moves), len(moves)):
        scratch.append(pltpu.SemaphoreType.DMA((max(number, 1),)))
    if moves:
        params = {"collective_id": ident, "has_side_effects": True}
    before = {}
    for move in moves:
        if isinstance(move.source, Move):
            number = index_of(moves, move.source)
            before[number] = min(move.phase, before.get(number, move.phase))

    def body_kernel(*refs):
        ins, refs = list(refs[:fixed_in]), refs[fixed_in:]
        sent, refs = refs[: len(sources)], refs[len(sources) :]
        results, refs = list(refs[:fixed_out]), refs[fixed_out:]
        landed, refs = refs[: len(moves)], refs[len(moves) :]
        kept, refs = refs[: len(folds)], refs[len(folds) :]
        rest, refs = refs[:own_scratch], refs[own_scratch:]
        inner, refs = refs[: len(held_in)], refs[len(held_in) :]
        outer, refs = refs[: len(held_out)], refs[len(held_out) :]
        buffers, (in_sem, out_sem, load_sem, keep_sem, send_sem, recv_sem) = refs[:terms], refs[terms:]
        fetches, stores = {}, {}
        for number, k in enumerate(held_in):
            fetches[k] = pltpu.make_async_copy(ins[k], inner[number], in_sem.at[number])
            ins[k] = inner[number]
        for number, k in enumerate(held_out):
            stores[k] = pltpu.make_async_copy(outer[number], results[k], out_sem.at[number])
            results[k] = outer[number]

        def target(axis, flip):
            return {axis: flipped(lax.axis_index(axis), flip, lax.axis_size(axis))}

        def buffers_of(fold):
            start = sum(1 + len(one.arrived) for one in folds[: index_of(folds, fold)])
            return start, buffers[start : start + 1 + len(fold.arrived)]

        def made(k):
            move = moves[k]
            if move.late is not None:
                source = results[move.late]
            elif isinstance(move.source, Fold):
                source = buffers_of(move.source)[1][0]
            elif isinstance(move.source, Move):
                source = landed[index_of(moves, move.source)]
            else:
                source = sent[index_of(sources, move.source)]
            return pltpu.make_async_remote_copy(
                src_ref=move.take(source),
                dst_ref=landed[k],
                send_sem=send_sem.at[k],
                recv_sem=recv_sem.at[k],
                device_id=target(move.axis, move.flip),
                device_id_type=pl.DeviceIdType.MESH,
            )

        def loads(fold):
            start, held = buffers_of(fold)
            return [
                pltpu.make_async_copy(
                    (fold.take if k == 0 else whole)(sent[index_of(sources, array)]),
                    held[k],
                    load_sem.at[start + k],
                )
                for k, array in enumerate([fold.own] + fold.arrived)
            ]

        def keeping(k):
            fold = folds[k]
            return pltpu.make_async_copy(
                fold.keep(buffers_of(fold)[1][0]), kept[k], keep_sem.at[k]
            )

        def add(fold):
            held = buffers_of(fold)[1]

            def one(index):
                if len(held) == 2:
                    held[0][index] = held[0][index] + held[1][index]
                elif len(held) > 2:
                    held[0][index] = functools.reduce(
                        jnp.add, [part[index].astype(SINGLE) for part in held]
                    ).astype(NARROW)

            if len(fold.shape) == 2:
                one((slice(None), slice(None)))
            else:
                loop(fold.shape[0], one)

        def begin():
            for fold in folds:
                for load in loads(fold):
                    load.start()
            for fetch in fetches.values():
                fetch.start()
            if moves:
                barrier = pltpu.get_barrier_semaphore()
                for axis, flip in partners:
                    pl.semaphore_signal(
                        barrier, inc=1, device_id=target(axis, flip),
                        device_id_type=pl.DeviceIdType.MESH,
                    )
                pl.semaphore_wait(barrier, len(partners))
            for k, move in enumerate(moves):
                if move.phase == 0 and move.late is None and not isinstance(move.source, Fold):
                    made(k).start()
            for number, fold in enumerate(folds):
                for load in loads(fold):
                    load.wait()
                add(fold)
                for k, move in enumerate(moves):
                    if move.source is fold:
                        made(k).start()
                keeping(number).start()
            for k, fetch in fetches.items():
                if k not in lazy:
                    fetch.wait()

        def launch(which):
            for k in range(len(moves)):
                if moves[k].late == which and moves[k].phase == 0:
                    made(k).start()

        def tick(phase):
            for k, needed in before.items():
                if needed == phase:
                    made(k).wait_recv()
            for k, move in enumerate(moves):
                if move.phase == phase:
                    made(k).start()

        def finish():
            for k, store in stores.items():
                if k not in early:
                    store.start()
            if not ticking:
                for phase in range(1, lasts + 1):
                    tick(phase)
            for k in range(len(moves)):
                made(k).wait_send()
                if k not in before:
                    made(k).wait_recv()
            for k in range(len(folds)):
                keeping(k).wait()
            for store in stores.values():
                store.wait()

        options = {}
        if any(move.late is not None for move in moves):
            options["launch"] = launch
        if ticking:
            options["tick"] = tick
        if lazy:
            options["ready"] = lambda k: fetches[k].wait()
        if early:
            options["flush"] = lambda k: stores[k].start()
        if grid is None:
            begin()
            kernel(*ins, *results, *rest, **options)
            finish()
        else:
            pl.when(pl.program_id(0) == 0)(begin)
            kernel(*ins, *results, *rest, **options)
            pl.when(pl.program_id(0) == pl.num_programs(0) - 1)(finish)

    result = pl.pallas_call(
        body_kernel,
        out_shape=list(outs)
        + [
            like(*m.shape, kind=m.dtype)
            for m in moves
        ]
        + [like(*fold.keep_shape) for fold in folds],
        in_specs=[ANY if spec is VMEM else spec for spec in specs] + [ANY] * len(sources),
        out_specs=[ANY if spec is VMEM else spec for spec in out_specs]
        + [ANY] * (len(moves) + len(folds)),
        scratch_shapes=scratch,
        compiler_params=pltpu.CompilerParams(vmem_limit_bytes=60 * 2**20, **params),
        cost_estimate=pl.CostEstimate(
            flops=int(flops),
            bytes_accessed=sum(o.size * o.dtype.itemsize for o in operands),
            transcendentals=0,
        ),
        **extra,
    )(*operands, *sources)
    end = fixed_out + len(moves)
    return list(result[:fixed_out]), list(result[fixed_out:end]), (folds, list(result[end:]))


def finale(kernel, outs, stages, results, scratch, ident):
    plan = []
    for stage in stages:
        for job, name in stage:
            moves = job.moves(name)
            folds = []
            for move in moves:
                known = folds + [fold for part, _ in plan for fold in part]
                if isinstance(move.source, Fold) and not any(move.source is one for one in known):
                    folds.append(move.source)
            job.absorb(name, moves, folds)
            plan.append((folds, moves))
    items = results()
    moves = [move for _, part in plan for move in part]
    folds = [fold for part, _ in plan for fold in part]
    sources, fetched = [], []

    def need(item):
        if not isinstance(item, (Fold, Move)) and not any(item is one for one in sources):
            sources.append(item)

    for fold in folds:
        for item in [fold.own] + fold.arrived:
            need(item)
            if not isinstance(item, (Fold, Move)):
                fetched.append((fold, item))
    for move in moves:
        need(move.source)
    plain_items = []
    for item in items:
        need(item)
        if not isinstance(item, (Fold, Move)):
            plain_items.append(item)
    partners = sorted({(move.axis, move.flip) for move in moves})
    shapes = [pltpu.VMEM(one.shape, one.dtype) for one in scratch]
    shapes += [pltpu.VMEM(move.shape, move.dtype) for move in moves]
    shapes += [pltpu.VMEM(fold.shape, fold.dtype) for fold in folds]
    shapes += [pltpu.VMEM(fold.shape, fold.dtype) for fold, _ in fetched]
    shapes += [pltpu.VMEM(item.shape, item.dtype) for item in plain_items]
    shapes += [pltpu.VMEM(one.shape, one.dtype) for one in outs]
    for number in (len(moves), len(moves), len(fetched), len(plain_items), len(outs)):
        shapes.append(pltpu.SemaphoreType.DMA((max(number, 1),)))

    def body_kernel(*refs):
        def take(count):
            nonlocal refs
            some, refs = refs[:count], refs[count:]
            return some

        sent, finals = take(len(sources)), take(len(outs))
        rest, landed, sums = take(len(scratch)), take(len(moves)), take(len(folds))
        brought, held, outer = take(len(fetched)), take(len(plain_items)), take(len(outs))
        send_sem, recv_sem, load_sem, item_sem, out_sem = refs
        arrived = set()

        def target(axis, flip):
            return {axis: flipped(lax.axis_index(axis), flip, lax.axis_size(axis))}

        def place(item):
            if isinstance(item, Fold):
                return sums[index_of(folds, item)]
            if isinstance(item, Move):
                return landed[index_of(moves, item)]
            return sent[index_of(sources, item)]

        def made(move):
            k = index_of(moves, move)
            source = place(move.source)
            return pltpu.make_async_remote_copy(
                src_ref=move.take(source),
                dst_ref=landed[k],
                send_sem=send_sem.at[k],
                recv_sem=recv_sem.at[k],
                device_id=target(move.axis, move.flip),
                device_id_type=pl.DeviceIdType.MESH,
            )

        def arrival(item):
            if isinstance(item, Move) and index_of(moves, item) not in arrived:
                arrived.add(index_of(moves, item))
                made(item).wait_recv()

        loads = [
            pltpu.make_async_copy(
                (fold.take if item is fold.own else whole)(place(item)), brought[k], load_sem.at[k]
            )
            for k, (fold, item) in enumerate(fetched)
        ]
        fetches = [
            pltpu.make_async_copy(place(item), held[k], item_sem.at[k])
            for k, item in enumerate(plain_items)
        ]
        stores = [
            pltpu.make_async_copy(outer[k], finals[k], out_sem.at[k]) for k in range(len(outs))
        ]
        for load in loads:
            load.start()
        barrier = pltpu.get_barrier_semaphore()
        for axis, flip in partners:
            pl.semaphore_signal(
                barrier, inc=1, device_id=target(axis, flip), device_id_type=pl.DeviceIdType.MESH
            )
        pl.semaphore_wait(barrier, len(partners))

        def total(fold):
            terms = []
            for item in [fold.own] + fold.arrived:
                if isinstance(item, (Fold, Move)):
                    arrival(item)
                    term = place(item)
                    if item is fold.own:
                        term = fold.take(item.keep(term) if isinstance(item, Fold) else term)
                else:
                    k = next(
                        k for k, (one, other) in enumerate(fetched) if one is fold and other is item
                    )
                    loads[k].wait()
                    term = brought[k]
                terms.append(term)
            goal = place(fold)

            def one(index):
                goal[index] = functools.reduce(
                    jnp.add, [term[index].astype(SINGLE) for term in terms]
                ).astype(goal.dtype)

            if len(fold.shape) == 2:
                one((slice(None), slice(None)))
            else:
                loop(fold.shape[0], one)

        for number, (some, part) in enumerate(plan):
            for fold in some:
                total(fold)
            for move in part:
                arrival(move.source)
                made(move).start()
            if number == 0:
                for fetch in fetches:
                    fetch.start()
        operands = []
        for item in items:
            if isinstance(item, (Fold, Move)):
                operands.append(place(item))
            else:
                operands.append(held[next(k for k, one in enumerate(plain_items) if one is item)])
        for fetch in fetches:
            fetch.wait()

        def ready(k):
            arrival(items[k])

        kernel(*operands, *outer, *rest, ready=ready, flush=lambda k: stores[k].start())
        for move in moves:
            made(move).wait_send()
            arrival(move)
        for store in stores:
            store.wait()

    return pl.pallas_call(
        body_kernel,
        out_shape=list(outs),
        in_specs=[ANY] * len(sources),
        out_specs=[ANY] * len(outs),
        scratch_shapes=shapes,
        compiler_params=pltpu.CompilerParams(
            vmem_limit_bytes=60 * 2**20, collective_id=ident, has_side_effects=True
        ),
    )(*sources)


class Courier:
    def __init__(self, active):
        self.active, self.waiting, self.ident = active, [], 0

    def load(self, *jobs):
        self.waiting += jobs

    def run(self, kernel, outs, operands, specs, scratch, flops, **extra):
        jobs, self.waiting = self.waiting, []
        moves, ends = [], []
        for job, stage, *late in jobs:
            added = job.moves(stage)
            for move in added:
                if late and not isinstance(move.source, Move):
                    move.late = late[0]
            moves += added
            ends.append(len(moves))
        if moves:
            self.ident += 1
        results, arrived, (folds, kept) = call(
            kernel, outs, operands, specs, scratch, flops, moves=tuple(moves), ident=self.ident, **extra
        )
        start = 0
        for (job, stage, *late), end in zip(jobs, ends):
            if late:
                job.tensor = results[late[0]]
            own = [
                kept[k]
                for k, fold in enumerate(folds)
                if any(move.source is fold for move in moves[start:end])
            ]
            job.absorb(stage, arrived[start:end], own)
            start = end
        return results


def in_halves(arrays):
    width = arrays[0].shape[1] // 2
    return (
        arrays[:1] + [one[:, :width] for one in arrays[1:]] + [one[:, width:] for one in arrays[1:]]
    )


def body(
    patches,
    queries,
    window_valid,
    answer_length,
    norm_gain,
    norm_bias,
    attn_in,
    attn_out,
    mlp_in,
    mlp_out,
    cot_patches,
    cot_queries,
):
    x, q, cot_x, cot_q = patches[0], queries[0], cot_patches[0], cot_queries[0]
    rows, features = x.shape
    count = q.shape[0]
    hidden = mlp_in.shape[2]
    blocks = lax.axis_size("blk")
    place = lax.axis_index("blk").astype(jnp.int32)
    share = features // blocks
    hidden_share = hidden // blocks
    share_rows = -(-share // 16) * 16
    hidden_rows = -(-hidden_share // 16) * 16
    part = -(-count // (blocks * 16)) * 16
    padded = part * blocks
    wide = 3 * features
    last = wide + features + features
    causal_columns = -(-last // 512) * 512
    valid = jnp.where(jnp.repeat(window_valid[0], WIN) > 0, 0.0, MASKED).astype(SINGLE)
    carried = blocks == DIRECT and lax.axis_size("rep") == 4 and share % 32 == 0
    courier = Courier(carried)

    def own_columns(tensor):
        return lax.dynamic_slice_in_dim(tensor, place * share, share, 1)

    square = 2.0 * features * features
    run = courier.run

    n0, pw, mw, x1, nx, vq, ckv = run(
        window_forward,
        [
            like(rows, features), like(rows, wide), like(rows, features),
            like(rows, features, kind=SINGLE), like(rows, features), like(rows, features),
            like(rows, 2 * features),
        ],
        [x, norm_gain, norm_bias, attn_in, attn_out],
        [VMEM, VMEM, VMEM, ANY, ANY],
        [((features, wide), NARROW), ((features, features), NARROW),
         ((features, features), NARROW), ((features, 2 * features), NARROW)],
        rows * square * 9,
        semaphores=4,
        early=(0, 1, 2, 3, 4, 5),
    )
    n1, pq, mq, q1, nq, cq, vkv, log_q = run(
        causal_forward,
        [
            like(count, features), like(count, wide), like(count, features),
            like(padded, features, kind=SINGLE), like(padded, features), like(count, features),
            like(count, 2 * features), like(16, count, kind=SINGLE),
        ],
        [q, norm_gain, norm_bias, attn_in, attn_out],
        [VMEM, VMEM, VMEM, ANY, ANY],
        [((features, wide), NARROW), ((features, features), NARROW),
         ((features, features), NARROW), ((features, 2 * features), NARROW),
         ((count, PAIR), SINGLE)],
        count * square * 15,
        semaphores=4,
        early=(0, 1, 2, 3, 4, 5),
    )
    outs, *log_pieces = run(
        functools.partial(cross_forward, blocks),
        [like(padded, features)] + [like(16, part, kind=SINGLE)] * blocks,
        [cq, ckv, valid[None, :]],
        [VMEM, VMEM, VMEM],
        [((padded, PAIR), SINGLE)],
        count * square * 6,
    )
    logs = Exchange(log_pieces)
    first_width = features // 3
    halves = [
        Pieces(outs, part, 0, first_width),
        Pieces(outs, part, first_width, features - first_width),
    ]
    if carried:
        courier.load((logs, ""), (halves[0], ""))
    mv, x2, log_v = run(
        reverse_forward,
        [like(rows, features), like(rows, features, kind=SINGLE), like(16, rows, kind=SINGLE)],
        [answer_length, vq, vkv, x1, attn_out],
        [SMEM, VMEM, VMEM, VMEM, ANY],
        [((features, features), NARROW), ((rows, PAIR), SINGLE)],
        rows * square * 8,
        semaphores=1,
        lazy=(3,),
        early=(0,),
    )
    if carried:
        courier.load((halves[1], ""))
    x3, dx2, up_x, down_x, norm_five = run(
        patch_feed_forward,
        [
            like(rows, features), like(rows, features, kind=SINGLE), like(features, hidden),
            like(hidden, features), like(8, features, kind=SINGLE),
        ],
        [x2, cot_x, norm_gain, norm_bias, mlp_in, mlp_out],
        [
            VMEM, VMEM, VMEM, VMEM,
            pl.BlockSpec((1, features, CHUNK), lambda j: (0, 0, j)),
            pl.BlockSpec((1, CHUNK, features), lambda j: (0, j, 0)),
        ],
        [((rows, features), NARROW), ((rows, CHUNK), NARROW), ((rows, CHUNK), NARROW),
         ((rows, features), SINGLE), ((rows, features), SINGLE)],
        rows * square * 24,
        grid=(hidden // CHUNK,),
        out_specs=[
            VMEM, VMEM,
            pl.BlockSpec((features, CHUNK), lambda j: (0, j)),
            pl.BlockSpec((CHUNK, features), lambda j: (j, 0)),
            VMEM,
        ],
    )
    if carried:
        merged = run(
            functools.partial(merge_blocks, blocks),
            [like(part, features), like(16, part, kind=SINGLE)],
            [outs] + logs.result + halves[0].result + halves[1].result,
            [VMEM] * (3 * blocks - 1),
            [],
            padded * square,
        )
        co_parts, log_parts = Spread(merged[0]), Gather(merged[1])
        up_x, down_x = Reduction(up_x), Reduction(down_x)
        reverse_weight = Reduction(like(blocks // 2, 2, 2, share // 2, 2 * features))
        courier.load(
            (co_parts, ""), (log_parts, ""), (up_x, "core"), (down_x, "core"),
            (reverse_weight, "core", 1),
        )
    else:
        whole_logs = jnp.stack(exchange(log_pieces))
        merged_log = jax.nn.logsumexp(whole_logs, axis=0)
        weights = jnp.transpose(jnp.exp(whole_logs - merged_log)[:, :HEADS], (0, 2, 1))
        shares = lax.all_to_all(outs.reshape(blocks, part, features), "blk", 0, 0)
        merged_out = jnp.sum(jnp.repeat(weights, HEAD, axis=2) * shares.astype(SINGLE), axis=0)
        co_parts, log_parts = Spread(None), Gather(None)
        co_parts.tensor, *co_parts.result = in_halves(gather(merged_out.astype(NARROW)))
        log_parts.result = gather(merged_log)
    folded = (blocks // 2, 2, 2, share // 2) if carried else (features,)
    dvq, reverse_grad, *kv_pieces = run(
        functools.partial(reverse_backward, blocks),
        [like(rows, features), like(*folded, 2 * features)]
        + [like(part, features + PAIR)] * blocks + [like(part, features - PAIR)] * blocks,
        [answer_length, dx2, mv, vq, vkv, nx, log_v, attn_out],
        [SMEM, VMEM, VMEM, VMEM, VMEM, VMEM, VMEM, ANY],
        [((features, features), NARROW), ((rows, features), NARROW), ((rows, features), NARROW),
         ((16, rows), SINGLE), ((padded, 2 * features), SINGLE)],
        rows * square * 16,
        semaphores=1,
        ticking=carried,
        lazy=(3, 4, 5, 6),
    )
    k_parts, v_parts = Exchange(kv_pieces[:blocks]), Exchange(kv_pieces[blocks:])
    if carried:
        courier.load((k_parts, ""), (up_x, "x"))
    else:
        k_parts.result, v_parts.result = exchange(k_parts.pieces), exchange(v_parts.pieces)
    q3, dq2, up_q, down_q, norm_four, co = run(
        functools.partial(query_feed_forward, blocks, share, hidden_share),
        [
            like(count, features), like(count, features, kind=SINGLE), like(share_rows, hidden),
            like(hidden_rows, features), like(8, features, kind=SINGLE), like(padded, features),
        ],
        [q1, cot_q, norm_gain, norm_bias, attn_out, mlp_in, mlp_out, co_parts.tensor]
        + co_parts.result,
        [
            VMEM, VMEM, VMEM, VMEM, pl.BlockSpec((1, features, features), lambda j: (2, 0, 0)),
            pl.BlockSpec((1, features, CHUNK), lambda j: (1, 0, j)),
            pl.BlockSpec((1, CHUNK, features), lambda j: (1, j, 0)),
        ] + [ANY] * (2 * blocks - 1),
        [((count, features), SINGLE), ((count, features), NARROW), ((share_rows, count), NARROW),
         ((count, CHUNK), NARROW), ((count, CHUNK), NARROW),
         ((count, features), SINGLE), ((count, features), SINGLE)],
        count * square * 18,
        semaphores=2 * blocks - 1,
        grid=(hidden // CHUNK,),
        out_specs=[
            VMEM, VMEM,
            pl.BlockSpec((share_rows, CHUNK), lambda j: (0, j)),
            VMEM, VMEM, VMEM,
        ],
    )
    if carried:
        up_q, down_q = Reduction(up_q, 1), Reduction(down_q, 1)
        courier.load((v_parts, ""), (down_x, "x"), (up_x, "y"), (up_q, "core"), (down_q, "core"))
    dckv, cross_out_weight, *q_pieces = run(
        functools.partial(cross_backward, blocks, share),
        [like(rows, 2 * features), like(share_rows, features)] + [like(part, features)] * blocks,
        [dq2, co, cq, ckv, valid[:, None], attn_out] + log_parts.result,
        [VMEM, VMEM, VMEM, VMEM, VMEM, ANY] + [VMEM] * blocks,
        [((features, features), NARROW), ((count, features), NARROW), ((count, features), NARROW),
         ((16, count), SINGLE), ((padded, PAIR), SINGLE), ((16, count), SINGLE),
         ((padded, features), NARROW), ((rows, 2 * features), SINGLE)],
        count * square * 12,
        semaphores=1,
        lazy=(2, 3),
    )
    q_parts = Exchange(q_pieces)
    if carried:
        kv_weight = Reduction(like(blocks // 2, 2, 2, share // 2, 2 * features))
        window_weight = Reduction(like(blocks // 2, 2, 2, share // 2, 4 * features))
        courier.load(
            (q_parts, ""), (down_x, "y"), (reverse_weight, "x"), (up_q, "x"), (down_q, "x"),
            (kv_weight, "core", 0), (window_weight, "core", 1),
        )
    else:
        q_parts.result = exchange(q_pieces)
    kv_grad, window_grad, grad_x, norm_x = run(
        patch_backward,
        [
            like(*folded, 2 * features), like(*folded, 4 * features),
            like(rows, features, kind=SINGLE), like(8, features, kind=SINGLE),
        ],
        [x, dx2, x1, nx, n0, pw, mw, dvq, dckv, norm_gain, attn_in, attn_out],
        [VMEM] * 10 + [ANY, ANY],
        [((features, wide), NARROW), ((features, features), NARROW),
         ((features, features), NARROW), ((features, 2 * features), NARROW),
         ((rows, features), SINGLE), ((rows, features), NARROW), ((rows, features), NARROW),
         ((16, rows), SINGLE), ((rows, wide), NARROW)],
        rows * square * 24,
        semaphores=4,
        lazy=(0, 4, 5, 6),
        early=(0, 1),
    )
    if carried:
        share_weight = Reduction(like(blocks // 2, 2, 2, share // 2, wide))
        dq1_parts = Spread(like(part, features))
        courier.load(
            (share_weight, "core", 1), (dq1_parts, "", 0), (window_weight, "x"),
            (reverse_weight, "y"), (kv_weight, "y"), (up_q, "back_x"), (down_q, "back_x"),
        )
    dq1_share, share_grad, norm_two = run(
        functools.partial(share_backward, blocks),
        [like(part, features), like(*folded, wide), like(8, features, kind=SINGLE)],
        [q1, nq, norm_gain, attn_in]
        + q_parts.result + k_parts.result + v_parts.result,
        [ANY, ANY, VMEM, ANY] + [VMEM] * (3 * blocks),
        [((features, features), NARROW), ((features, 2 * features), NARROW),
         ((part, wide), NARROW), ((part, features), SINGLE), ((part, features), NARROW)],
        part * square * 6,
        semaphores=4,
    )
    if carried:
        courier.load(
            (window_weight, "y"), (share_weight, "x"), (kv_weight, "x"), (down_x, "z"),
            (reverse_weight, "z"), (up_q, "back_core"), (down_q, "back_core"), (up_x, "z"),
        )
    else:
        dq1_parts = Spread(None)
        dq1_parts.tensor, *dq1_parts.result = in_halves(gather(dq1_share))
    causal_weight, grad_q, norms = run(
        functools.partial(causal_backward, blocks, share),
        [
            like(share_rows, causal_columns), like(count, features, kind=SINGLE),
            like(blocks, 16, -(-share // PAIR) * PAIR, kind=SINGLE)
            if carried
            else like(16, features, kind=SINGLE),
        ],
        [q, dq2, n1, pq, mq, log_q, cross_out_weight, norm_gain]
        + [norm_x, norm_two, norm_four, norm_five, attn_in, attn_out, dq1_parts.tensor]
        + dq1_parts.result,
        [VMEM] * 12 + [ANY] * (2 * blocks + 1),
        [((features, wide), NARROW), ((features, features), NARROW), ((padded, features), NARROW),
         ((count, features), SINGLE), ((count, features), NARROW), ((count, features), NARROW),
         ((16, count), SINGLE), ((count, 2 * PAIR), SINGLE), ((count, wide), NARROW),
         ((8, features), SINGLE), ((16, features), SINGLE)],
        count * square * 16,
        semaphores=2 * blocks + 1,
        lazy=(2, 3, 4, 5),
    )
    rest = (
        x3[None],
        own_columns(q3)[None],
        grad_x[None],
        own_columns(grad_q)[None],
    )
    if carried:
        norms = Norms(norms)
        causal_weight = Reduction(causal_weight, 1)
        sums = [
            up_x, down_x, reverse_weight, window_weight, kv_weight, share_weight, up_q, down_q,
            causal_weight,
        ]
        grads = finale(
            functools.partial(assemble, len(sums), blocks),
            [
                like(4, share, wide), like(4, share, features), like(2, share, hidden),
                like(2, hidden_share, features),
                like(6, share, kind=SINGLE), like(6, share, kind=SINGLE),
            ],
            [
                [
                    (causal_weight, "core"), (norms, "out"), (share_weight, "y"), (window_weight, "z"),
                    (kv_weight, "z"), (up_x, "back_x"), (down_x, "back_x"),
                    (reverse_weight, "back_x"),
                ],
                [
                    (causal_weight, "x"), (norms, "back"), (share_weight, "z"), (kv_weight, "back_x"),
                    (up_x, "back_core"), (down_x, "back_core"), (reverse_weight, "back_core"),
                    (window_weight, "back_x"),
                ],
                [
                    (causal_weight, "back_x"), (share_weight, "back_x"),
                    (window_weight, "back_core"), (kv_weight, "back_core"),
                ],
                [
                    (causal_weight, "back_core"), (share_weight, "back_core"),
                ],
            ],
            lambda: sum([one.result for one in sums], []) + norms.result,
            [like(share, 4 * features), like(share, causal_columns)],
            courier.ident + 1,
        )
        return rest + (grads[4], grads[5]) + tuple(one.astype(SINGLE) for one in grads[:4])
    up_x, down_x, reverse_weight, window_weight, kv_weight, share_weight = (
        reduce_all(one) for one in (up_x, down_x, reverse_grad, window_grad, kv_grad, share_grad)
    )
    up_q, down_q = reduce_rep(up_q[:share]), reduce_rep(down_q[:hidden_share])
    causal_weight = reduce_rep(causal_weight[:share])
    norms = own_columns(lax.psum(norms, ("blk", "rep")))
    gains, biases = norms[:6], norms[8:14]
    grad_attn_in = jnp.stack(
        (
            window_weight[:, :wide],
            causal_weight[:, :wide],
            jnp.concatenate((share_weight[:, :features], kv_weight), axis=1),
            jnp.concatenate((reverse_weight[:, :features], share_weight[:, features:]), axis=1),
        )
    )
    grad_attn_out = jnp.stack(
        (
            window_weight[:, wide:],
            causal_weight[:, wide : wide + features],
            causal_weight[:, wide + features : last],
            reverse_weight[:, features:],
        )
    )
    return rest + (
        gains,
        biases,
        grad_attn_in.astype(SINGLE),
        grad_attn_out.astype(SINGLE),
        jnp.stack((up_x, up_q)).astype(SINGLE),
        jnp.stack((down_x, down_q)).astype(SINGLE),
    )


def solution(mesh):
    placed = (
        P("rep", "blk", None),
        P("rep", None, None),
        P("rep", "blk"),
        P("rep"),
        P(),
        P(),
        P(),
        P(),
        P(),
        P(),
        P("rep", "blk", None),
        P("rep", None, None),
    )
    return jax.shard_map(
        body,
        mesh=mesh,
        in_specs=placed,
        out_specs=(
            P("rep", "blk", None),
            P("rep", None, "blk"),
            P("rep", "blk", None),
            P("rep", None, "blk"),
            P(None, "blk"),
            P(None, "blk"),
            P(None, "blk", None),
            P(None, "blk", None),
            P(None, "blk", None),
            P(None, "blk", None),
        ),
        check_vma=False,
    )
```

```python
import functools
import math

import jax
import jax.numpy as jnp
from jax import lax
from jax.experimental import pallas as pl
from jax.experimental.pallas import tpu as pltpu
from jax.sharding import PartitionSpec as P

HEADS = 12
WIN = 64
EPSILON = 1e-05
MASKED = -1e30
NARROW = jnp.bfloat16
SINGLE = jnp.float32
GROUP = 256
WINDOWS = 256
PAIR = 128
HEAD = 64
STRIP = 400
LONG = 400
CHUNK = 768


def dot(former, latter, ahead, behind, precision=None):
    return lax.dot_general(
        former,
        latter,
        (((ahead,), (behind,)), ((), ())),
        preferred_element_type=SINGLE,
        precision=precision,
    )


def plain(former, latter):
    return dot(former, latter, 1, 0)


def right_t(former, latter):
    return dot(former, latter, 1, 1)


def left_t(former, latter):
    return dot(former, latter, 0, 0)


def loop(count, action):
    def step(index, nothing):
        action(index)
        return nothing

    lax.fori_loop(0, count, step, 0)


def at(index, size):
    return pl.ds(pl.multiple_of(index * size, size), size)


def iota(shape, dim):
    return lax.broadcasted_iota(jnp.int32, shape, dim)


def statistics(tensor):
    average = jnp.mean(tensor, axis=-1, keepdims=True)
    centred = tensor - average
    spread = jnp.mean(centred * centred, axis=-1, keepdims=True)
    return centred, lax.rsqrt(spread + EPSILON)


def norm(tensor, gain, bias):
    centred, inverse = statistics(tensor)
    return centred * inverse * gain + bias


def norm_back(tensor, gain, upstream):
    centred, inverse = statistics(tensor)
    scaled = centred * inverse
    inner = upstream * gain
    grad = inverse * (
        inner
        - jnp.mean(inner, axis=-1, keepdims=True)
        - scaled * jnp.mean(inner * scaled, axis=-1, keepdims=True)
    )
    return (
        grad,
        jnp.sum(upstream * scaled, axis=0, keepdims=True),
        jnp.sum(upstream, axis=0, keepdims=True),
    )


def gelu_both(tensor):
    size = jnp.abs(tensor)
    ratio = 1.0 / (1.0 + (0.3275911 * math.sqrt(0.5)) * size)
    series = ratio * (
        0.254829592
        + ratio * (-0.284496736 + ratio * (1.421413741 + ratio * (-1.453152027 + ratio * 1.061405429)))
    )
    bell = jnp.exp(-0.5 * (tensor * tensor))
    tail = 0.5 * series * bell
    below = jnp.where(tensor >= 0, 1.0 - tail, tail)
    return tensor * below, below + tensor * bell * (1.0 / math.sqrt(2.0 * math.pi))


def half(which, value=1.0):
    return jnp.where(iota((1, PAIR), 1) // HEAD == which, value, 0.0).astype(NARROW)


def lower_lanes():
    return iota((1, PAIR), 1) < HEAD


def both(tensor, value=1.0):
    return jnp.concatenate((tensor * half(0, value), tensor * half(1, value)), axis=0)


def attend(queries, keys, values, mask):
    rows = queries.shape[0]
    scores = right_t(both(queries, 1.0 / math.sqrt(HEAD)), keys)
    weights, totals, logs = [], [], []
    for which in range(2):
        part = mask(scores[which * rows : (which + 1) * rows])
        peak = jnp.max(part, axis=-1, keepdims=True)
        part = jnp.exp(part - peak)
        total = jnp.sum(part, axis=-1, keepdims=True)
        weights.append(part.astype(NARROW))
        totals.append(1.0 / total)
        logs.append(peak + jnp.log(total))
    out = plain(jnp.concatenate(weights, axis=0), values)
    return jnp.where(lower_lanes(), out[:rows] * totals[0], out[rows:] * totals[1]), logs


def attend_back(queries, keys, values, upstream, logs, deltas, mask):
    scaled = queries * jnp.asarray(1.0 / math.sqrt(HEAD), NARROW)
    count = keys.shape[0]
    keys = both(keys)
    turned_keys = keys.T
    scores = right_t(keys, scaled)
    inner = right_t(both(values), upstream)
    weights, slopes = [], []
    for which in range(2):
        span = slice(which * count, (which + 1) * count)
        part = mask(scores[span])
        if logs is None:
            part = jnp.exp(part - jnp.max(part, axis=0, keepdims=True))
            part = part * (1.0 / jnp.sum(part, axis=0, keepdims=True))
        else:
            part = jnp.exp(part - logs[which])
        weights.append(part.astype(NARROW))
        slopes.append((part * (inner[span] - deltas[which])).astype(NARROW))
    slope = jnp.concatenate(slopes, axis=0)
    query_grad = plain(turned_keys, slope).T
    key_grad = plain(slope, scaled)
    value_grad = plain(jnp.concatenate(weights, axis=0), upstream)
    lanes = lower_lanes()
    return (
        query_grad,
        jnp.where(lanes, key_grad[:count], key_grad[count:]),
        jnp.where(lanes, value_grad[:count], value_grad[count:]),
    )


def exact_parts(tensor, count):
    parts = []
    for _ in range(count):
        parts.append(tensor.astype(NARROW))
        tensor = tensor - parts[-1].astype(SINGLE)
    return parts


def head_rows(tensor):
    features = tensor.shape[1]
    heads = 16
    chosen = jnp.where(
        iota((heads, features), 1) // HEAD == iota((heads, features), 0), 1.0, 0.0
    ).astype(NARROW)
    return functools.reduce(jnp.add, [right_t(chosen, part) for part in exact_parts(tensor, 2)])


def turn(columns):
    same = jnp.where(iota((16, columns.shape[1]), 0) == iota((16, columns.shape[1]), 1), 1.0, 0.0)
    same = same.astype(NARROW)
    return functools.reduce(jnp.add, [right_t(same, part) for part in exact_parts(columns, 3)])


def row_pair(ref, pair, span):
    tensor = ref[:, span]
    index = iota(tensor.shape, 0)
    return [
        jnp.sum(jnp.where(index == 2 * pair + which, tensor, 0.0), axis=0, keepdims=True)
        for which in range(2)
    ]


def chooser(rows, width, start, count):
    row = iota((rows, width), 0)
    hit = jnp.logical_and(iota((rows, width), 1) == row + start, row < count)
    return jnp.where(hit, 1.0, 0.0).astype(NARROW)


def spans(rows, size):
    edges = [(start, min(start + size, rows)) for start in range(0, rows, size)]
    if len(edges) > 1 and edges[-1][1] - edges[-1][0] < PAIR:
        edges[-2:] = [(edges[-2][0], rows)]
    return edges


def mark(log_ref, rows, head, value):
    log_ref[rows, :] = jnp.where(iota((1, PAIR), 1) == head, value, log_ref[rows, :])


def store_rows(ref, columns, value):
    ref[(slice(None),) * (len(ref.shape) - 1) + (columns,)] = value.astype(ref.dtype).reshape(
        ref.shape[:-1] + value.shape[1:]
    )


def nothing(*unused):
    return None


def copies(semaphores, *pairs):
    made = [
        pltpu.make_async_copy(source, target, semaphores.at[k])
        for k, (source, target) in enumerate(pairs)
    ]
    for one in made:
        one.start()
    return made


DIRECT = 8


def place_of(axis="blk"):
    return lax.axis_index(axis)


def flipped(index, mask, count):
    total, weight = 0, 1
    while weight < count:
        bit = (index // weight) % 2
        total = total + weight * ((1 - bit) if mask & weight else bit)
        weight *= 2
    return total


def piece_at(number, count):
    return flipped(place_of(), number, count) if count <= DIRECT else number


def window_forward(
    x_ref, gain_ref, bias_ref, a_in, a_out,
    n0_ref, pw_ref, mw_ref, x1_ref, nx_ref, vq_ref, ckv_ref,
    w_in, w_out, w_q, w_kv, sem,
    flush=nothing,
):
    rows, features = x_ref.shape
    loads = copies(
        sem,
        (a_in.at[0], w_in),
        (a_out.at[0], w_out),
        (a_in.at[3, :, pl.ds(0, features)], w_q),
        (a_in.at[2, :, pl.ds(features, 2 * features)], w_kv),
    )

    def first(i):
        span = at(i, GROUP)
        n0_ref[span, :] = norm(
            x_ref[span, :].astype(SINGLE), gain_ref[0:1, :], bias_ref[0:1, :]
        ).astype(NARROW)

    loop(rows // GROUP, first)
    loads[0].wait()

    def project(j):
        span = at(j, CHUNK)
        pw_ref[:, span] = plain(n0_ref[...], w_in[:, span]).astype(NARROW)

    loop(3 * features // CHUNK, project)
    flush(0)
    flush(1)
    window = jnp.where(
        iota((WINDOWS, WINDOWS), 0) // WIN == iota((WINDOWS, WINDOWS), 1) // WIN, 0.0, MASKED
    )

    def group(i):
        span = at(i, WINDOWS)
        for pair in range(features // PAIR):
            lane = pair * PAIR
            out, unused = attend(
                pw_ref[span, lane : lane + PAIR],
                pw_ref[span, features + lane : features + lane + PAIR],
                pw_ref[span, 2 * features + lane : 2 * features + lane + PAIR],
                lambda scores: scores + window,
            )
            mw_ref[span, lane : lane + PAIR] = out.astype(NARROW)

    loop(rows // WINDOWS, group)
    flush(2)
    loads[1].wait()

    def second(i):
        span = at(i, GROUP)
        total = x_ref[span, :].astype(SINGLE) + plain(mw_ref[span, :], w_out[...])
        x1_ref[span, :] = total
        nx_ref[span, :] = norm(total, gain_ref[3:4, :], bias_ref[3:4, :]).astype(NARROW)

    loop(rows // GROUP, second)
    flush(3)
    flush(4)
    loads[2].wait()
    vq_ref[...] = plain(nx_ref[...], w_q[...]).astype(NARROW)
    flush(5)
    loads[3].wait()

    def third(j):
        span = at(j, CHUNK)
        ckv_ref[:, span] = plain(nx_ref[...], w_kv[:, span]).astype(NARROW)

    loop(2 * features // CHUNK, third)


def causal_forward(
    q_ref, gain_ref, bias_ref, a_in, a_out,
    n1_ref, pq_ref, mq_ref, q1_ref, nq_ref, cq_ref, vkv_ref, log_ref,
    w_in, w_out, w_q, w_kv, logs, sem,
    flush=nothing,
):
    rows, features = q_ref.shape
    loads = copies(
        sem,
        (a_in.at[1], w_in),
        (a_out.at[1], w_out),
        (a_in.at[2, :, pl.ds(0, features)], w_q),
        (a_in.at[3, :, pl.ds(features, 2 * features)], w_kv),
    )

    def first(i):
        span = at(i, STRIP)
        n1_ref[span, :] = norm(
            q_ref[span, :].astype(SINGLE), gain_ref[1:2, :], bias_ref[1:2, :]
        ).astype(NARROW)

    loop(rows // STRIP, first)
    loads[0].wait()

    def project(j):
        span = at(j, CHUNK)
        pq_ref[:, span] = plain(n1_ref[...], w_in[:, span]).astype(NARROW)

    loop(3 * features // CHUNK, project)
    flush(0)
    flush(1)
    logs[...] = jnp.zeros_like(logs)

    def pair(p):
        for start in range(0, rows, LONG):
            end = min(start + LONG, rows)

            def mask(scores, start=start):
                shape = scores.shape
                return jnp.where(iota(shape, 1) <= iota(shape, 0) + start, scores, MASKED)

            out, sums = attend(
                pq_ref[start:end, at(p, PAIR)],
                pq_ref[0:end, at(p + features // PAIR, PAIR)],
                pq_ref[0:end, at(p + 2 * features // PAIR, PAIR)],
                mask,
            )
            mq_ref[start:end, at(p, PAIR)] = out.astype(NARROW)
            for which in range(2):
                mark(logs, slice(start, end), 2 * p + which, sums[which])

    loop(features // PAIR, pair)
    flush(2)
    log_ref[...] = turn(logs[...])
    loads[1].wait()

    def second(i):
        span = at(i, STRIP)
        total = q_ref[span, :].astype(SINGLE) + plain(mq_ref[span, :], w_out[...])
        q1_ref[span, :] = total
        nq_ref[span, :] = norm(total, gain_ref[2:3, :], bias_ref[2:3, :]).astype(NARROW)

    loop(rows // STRIP, second)
    if q1_ref.shape[0] > rows:
        q1_ref[rows:, :] = jnp.zeros_like(q1_ref[rows:, :])
        nq_ref[rows:, :] = jnp.zeros_like(nq_ref[rows:, :])
    flush(3)
    flush(4)
    loads[2].wait()
    cq_ref[...] = plain(nq_ref[0:rows, :], w_q[...]).astype(NARROW)
    flush(5)
    loads[3].wait()

    def third(j):
        span = at(j, CHUNK)
        vkv_ref[:, span] = plain(nq_ref[0:rows, :], w_kv[:, span]).astype(NARROW)

    loop(2 * features // CHUNK, third)


def cross_forward(pieces, cq_ref, ckv_ref, valid_ref, whole, *rest):
    log_refs, (logs,) = rest[:pieces], rest[pieces:]
    rows, features = cq_ref.shape
    part = log_refs[0].shape[1]
    logs[...] = jnp.zeros_like(logs)
    if whole.shape[0] > rows:
        whole[rows:, :] = jnp.zeros((whole.shape[0] - rows, features), NARROW)

    def pair(p):
        for start in range(0, rows, LONG):
            span = slice(start, min(start + LONG, rows))
            out, sums = attend(
                cq_ref[span, at(p, PAIR)],
                ckv_ref[:, at(p, PAIR)],
                ckv_ref[:, at(p + features // PAIR, PAIR)],
                lambda scores: scores + valid_ref[...],
            )
            whole[span, at(p, PAIR)] = out.astype(NARROW)
            for which in range(2):
                mark(logs, span, 2 * p + which, sums[which])

    loop(features // PAIR, pair)
    for k in range(pieces):
        log_refs[k][...] = turn(logs[at(piece_at(k, pieces), part), :])


def untwist(rows):
    same = jnp.where(iota((16, PAIR), 0) == iota((16, PAIR), 1), 1.0, 0.0).astype(NARROW)
    return functools.reduce(jnp.add, [left_t(part, same) for part in exact_parts(rows, 3)])


def merge_blocks(pieces, own_ref, *refs):
    logs, refs = refs[:pieces], refs[pieces:]
    halves, (co_ref, log_ref) = (refs[: pieces - 1], refs[pieces - 1 : -2]), refs[-2:]
    part, features = co_ref.shape
    width = features // 2
    peak = functools.reduce(jnp.maximum, [one[...] for one in logs])
    total = peak + jnp.log(functools.reduce(jnp.add, [jnp.exp(one[...] - peak) for one in logs]))
    log_ref[...] = total
    spread = jnp.where(
        iota((PAIR, features), 1) // HEAD == iota((PAIR, features), 0), 1.0, 0.0
    ).astype(NARROW)
    result = jnp.zeros(co_ref.shape, SINGLE)
    for k in range(pieces):
        weight = untwist(jnp.exp(logs[k][...] - total))
        high = weight.astype(NARROW)
        low = (weight - high.astype(SINGLE)).astype(NARROW)
        if k == 0:
            block = own_ref[at(place_of(), part), :]
        else:
            block = jnp.concatenate((halves[0][k - 1][...], halves[1][k - 1][...]), axis=1)
        result = result + (plain(high, spread) + plain(low, spread)) * block.astype(SINGLE)
    co_ref[...] = result.astype(NARROW)


def reverse_forward(
    length_ref, vq_ref, vkv_ref, x1_ref, a_out,
    mv_ref, x2_ref, log_ref,
    w_out, logs, sem,
    ready=nothing, flush=nothing,
):
    rows, features = vq_ref.shape
    keys = vkv_ref.shape[0]
    (load,) = copies(sem, (a_out.at[3], w_out))
    logs[...] = jnp.zeros_like(logs)
    bias = jnp.where(iota((1, keys), 1) < length_ref[0], 0.0, MASKED)

    def pair(p):
        for start in range(0, rows, WINDOWS):
            span = slice(start, start + WINDOWS)
            out, sums = attend(
                vq_ref[span, at(p, PAIR)],
                vkv_ref[:, at(p, PAIR)],
                vkv_ref[:, at(p + features // PAIR, PAIR)],
                lambda scores: scores + bias,
            )
            mv_ref[span, at(p, PAIR)] = out.astype(NARROW)
            for which in range(2):
                mark(logs, span, 2 * p + which, sums[which])

    loop(features // PAIR, pair)
    flush(0)
    log_ref[...] = turn(logs[...])
    load.wait()
    ready(3)

    def second(i):
        span = at(i, GROUP)
        x2_ref[span, :] = x1_ref[span, :] + plain(mv_ref[span, :], w_out[...])

    loop(rows // GROUP, second)


def feed_forward_step(block, normed, up, down, cot, hidden, slope, out, grad):
    rows = normed.shape[0]

    def strip(i):
        span = at(i, block)
        value, rise = gelu_both(plain(normed[span, :], up[...]))
        hidden[span, :] = value.astype(NARROW)
        slope[span, :] = (right_t(cot[span, :], down[...]) * rise).astype(NARROW)
        out[span, :] += plain(hidden[span, :], down[...])
        grad[span, :] += right_t(slope[span, :], up[...])

    loop(rows // block, strip)


def patch_feed_forward(
    x2_ref, cot_ref, gain_ref, bias_ref, up_ref, down_ref,
    x3_ref, dx2_ref, up_grad_ref, down_grad_ref, norm_ref,
    normed, hidden, slope, out, grad,
):
    rows = x2_ref.shape[0]
    step = pl.program_id(0)

    @pl.when(step == 0)
    def begin():
        def first(i):
            span = at(i, GROUP)
            normed[span, :] = norm(
                x2_ref[span, :], gain_ref[5:6, :], bias_ref[5:6, :]
            ).astype(NARROW)
            out[span, :] = x2_ref[span, :]
            grad[span, :] = jnp.zeros_like(grad[span, :])

        loop(rows // GROUP, first)

    feed_forward_step(
        512, normed, up_ref.at[0], down_ref.at[0], cot_ref, hidden, slope, out, grad
    )
    up_grad_ref[...] = left_t(normed[...], slope[...]).astype(NARROW)
    down_grad_ref[...] = left_t(hidden[...], cot_ref[...]).astype(NARROW)

    @pl.when(step == pl.num_programs(0) - 1)
    def finish():
        norm_ref[...] = jnp.zeros_like(norm_ref)

        def last(i):
            span = at(i, GROUP)
            x3_ref[span, :] = out[span, :].astype(NARROW)
            part, gain, bias = norm_back(x2_ref[span, :], gain_ref[5:6, :], grad[span, :])
            dx2_ref[span, :] = cot_ref[span, :].astype(SINGLE) + part
            norm_ref[0:1, :] += gain
            norm_ref[1:2, :] += bias

        loop(rows // GROUP, last)


def place_parts(ref, pieces, parts, sem):
    part, features = parts[0].shape
    width = features // 2
    pairs = [(parts[0], ref.at[at(piece_at(0, pieces), part), :])]
    for number in range(2):
        for k in range(1, pieces):
            pairs.append(
                (
                    parts[number * (pieces - 1) + k],
                    ref.at[at(piece_at(k, pieces), part), pl.ds(number * width, width)],
                )
            )
    return copies(sem, *pairs)


def query_feed_forward(
    pieces, share, hidden_share, q1_ref, cot_ref, gain_ref, bias_ref,
    w_out, up_ref, down_ref, *rest,
):
    parts, rest = rest[: 2 * pieces - 1], rest[2 * pieces - 1 :]
    (
        q3_ref, dq2_ref, up_grad_ref, down_grad_ref, norm_ref, co_ref,
        q2, normed, chosen, hidden, slope, out, grad, sem,
    ) = rest
    rows, features = cot_ref.shape
    width = up_ref.shape[2]
    step = pl.program_id(0)

    @pl.when(step == 0)
    def begin():
        for one in place_parts(co_ref, pieces, parts, sem):
            one.wait()

        def first(i):
            span = at(i, STRIP)
            total = q1_ref[span, :] + plain(co_ref[span, :], w_out[0])
            q2[span, :] = total
            out[span, :] = total
            normed[span, :] = norm(total, gain_ref[4:5, :], bias_ref[4:5, :]).astype(NARROW)
            grad[span, :] = jnp.zeros_like(grad[span, :])

        loop(rows // STRIP, first)
        chosen[...] = right_t(
            chooser(chosen.shape[0], features, place_of() * share, share), normed[...]
        ).astype(NARROW)

    feed_forward_step(
        rows, normed, up_ref.at[0], down_ref.at[0], cot_ref, hidden, slope, out, grad
    )
    up_grad_ref[...] = plain(chosen[...], slope[...]).astype(NARROW)
    begins = place_of() * hidden_share

    @pl.when(begins // width == step)
    def own_hidden():
        taken = right_t(
            chooser(down_grad_ref.shape[0], width, begins - step * width, hidden_share),
            hidden[...],
        ).astype(NARROW)
        down_grad_ref[...] = plain(taken, cot_ref[...]).astype(NARROW)

    @pl.when(step == pl.num_programs(0) - 1)
    def finish():
        norm_ref[...] = jnp.zeros_like(norm_ref)

        def last(i):
            span = at(i, STRIP)
            q3_ref[span, :] = out[span, :].astype(NARROW)
            piece, gain, bias = norm_back(q2[span, :], gain_ref[4:5, :], grad[span, :])
            dq2_ref[span, :] = cot_ref[span, :].astype(SINGLE) + piece
            norm_ref[0:1, :] += gain
            norm_ref[1:2, :] += bias

        loop(rows // STRIP, last)


def reverse_backward(
    pieces, length_ref, dx2_ref, mv_ref, vq_ref, vkv_ref, nx_ref, log_ref, a_out,
    *rest, launch=nothing, tick=nothing, ready=nothing,
):
    dvq_ref, weight_ref, rest = rest[0], rest[1], rest[2:]
    k_refs, v_refs, rest = rest[:pieces], rest[pieces : 2 * pieces], rest[2 * pieces :]
    w_out, rounded, dmv, deltas, dkv, sem = rest
    rows, features = vq_ref.shape
    keys = vkv_ref.shape[0]
    part = k_refs[0].shape[0]
    (load,) = copies(sem, (a_out.at[3], w_out))
    rounded[...] = dx2_ref[...].astype(NARROW)
    load.wait()
    dmv[...] = right_t(rounded[...], w_out[...]).astype(NARROW)
    store_rows(
        weight_ref, slice(features, 2 * features), left_t(mv_ref[...], rounded[...])
    )
    deltas[...] = head_rows(dmv[...].astype(SINGLE) * mv_ref[...].astype(SINGLE))
    if dkv.shape[0] > keys:
        dkv[keys:, :] = jnp.zeros((dkv.shape[0] - keys, 2 * features), SINGLE)
    size = 256
    for k in (3, 4, 6):
        ready(k)

    def pair(p):
        pl.when(p == 2)(lambda: tick(1))
        pl.when(p == 4)(lambda: tick(2))
        for strip in range(rows // size):
            span = slice(strip * size, (strip + 1) * size)

            def mask(scores):
                return jnp.where(iota(scores.shape, 0) < length_ref[0], scores, MASKED)

            dq, dk, dv = attend_back(
                vq_ref[span, at(p, PAIR)],
                vkv_ref[:, at(p, PAIR)],
                vkv_ref[:, at(p + features // PAIR, PAIR)],
                dmv[span, at(p, PAIR)],
                row_pair(log_ref, p, span),
                row_pair(deltas, p, span),
                mask,
            )
            dvq_ref[span, at(p, PAIR)] = (dq * (1.0 / math.sqrt(HEAD))).astype(NARROW)
            if strip == 0:
                dkv[0:keys, at(p, PAIR)] = dk
                dkv[0:keys, at(p + features // PAIR, PAIR)] = dv
            else:
                dkv[0:keys, at(p, PAIR)] += dk
                dkv[0:keys, at(p + features // PAIR, PAIR)] += dv

    loop(features // PAIR, pair)
    ready(5)
    store_rows(weight_ref, slice(0, features), left_t(nx_ref[...], dvq_ref[...]))
    launch(1)
    for k in range(pieces):
        span = at(piece_at(k, pieces), part)
        width = k_refs[k].shape[1]
        k_refs[k][...] = dkv[span, 0:width].astype(NARROW)
        v_refs[k][...] = dkv[span, width:].astype(NARROW)


def cross_backward(
    pieces, share, dq2_ref, co_ref, cq_ref, ckv_ref, valid_ref, a_out, *rest, ready=nothing
):
    log_parts, rest = rest[:pieces], rest[pieces:]
    dckv_ref, weight_ref, rest = rest[0], rest[1], rest[2:]
    q_refs, (w_out, rounded, dco, deltas, logs, turned, dq_all, dkv, sem) = (
        rest[:pieces],
        rest[pieces:],
    )
    rows, features = cq_ref.shape
    part = log_parts[0].shape[1]
    (load,) = copies(sem, (a_out.at[2], w_out))
    for k in range(pieces):
        logs[at(piece_at(k, pieces), part), :] = untwist(log_parts[k][...])
    turned[...] = turn(logs[0:rows, :])
    rounded[...] = dq2_ref[...].astype(NARROW)
    load.wait()
    dco[...] = right_t(rounded[...], w_out[...]).astype(NARROW)
    taken = right_t(
        chooser(weight_ref.shape[0], features, place_of() * share, share), co_ref[0:rows, :]
    ).astype(NARROW)
    weight_ref[...] = plain(taken, rounded[...]).astype(NARROW)
    deltas[...] = head_rows(dco[...].astype(SINGLE) * co_ref[0:rows, :].astype(SINGLE))
    if dq_all.shape[0] > rows:
        dq_all[rows:, :] = jnp.zeros((dq_all.shape[0] - rows, features), NARROW)
    edges = spans(rows, 512)
    ready(2)
    ready(3)

    def pair(p):
        for number, (start, end) in enumerate(edges):
            span = slice(start, end)
            dq, dk, dv = attend_back(
                cq_ref[span, at(p, PAIR)],
                ckv_ref[:, at(p, PAIR)],
                ckv_ref[:, at(p + features // PAIR, PAIR)],
                dco[span, at(p, PAIR)],
                row_pair(turned, p, span),
                row_pair(deltas, p, span),
                lambda scores: scores + valid_ref[...],
            )
            dq_all[span, at(p, PAIR)] = (dq * (1.0 / math.sqrt(HEAD))).astype(NARROW)
            if number == 0:
                dkv[:, at(p, PAIR)] = dk
                dkv[:, at(p + features // PAIR, PAIR)] = dv
            else:
                dkv[:, at(p, PAIR)] += dk
                dkv[:, at(p + features // PAIR, PAIR)] += dv

    loop(features // PAIR, pair)
    dckv_ref[...] = dkv[...].astype(NARROW)
    for k in range(pieces):
        q_refs[k][...] = dq_all[at(piece_at(k, pieces), part), :]


def patch_backward(
    x_ref, dx2_ref, x1_ref, nx_ref, n0_ref, pw_ref, mw_ref, dvq_ref, dckv_ref, gain_ref, a_in, a_out,
    kv_weight_ref, weight_ref, grad_ref, norm_ref,
    w_in, w_out, w_q, w_kv, dx1, rounded, dmw, deltas, dpw, sem,
    launch=nothing, ready=nothing, flush=nothing,
):
    rows, features = x_ref.shape
    loads = copies(
        sem,
        (a_in.at[3, :, pl.ds(0, features)], w_q),
        (a_in.at[2, :, pl.ds(features, 2 * features)], w_kv),
        (a_out.at[0], w_out),
        (a_in.at[0], w_in),
    )
    norm_ref[...] = jnp.zeros_like(norm_ref)
    for start in range(0, 2 * features, CHUNK):
        span = slice(start, start + CHUNK)
        store_rows(kv_weight_ref, span, left_t(nx_ref[...], dckv_ref[:, span]))
    launch(0)
    flush(0)
    loads[0].wait()
    loads[1].wait()

    def first(i):
        span = at(i, GROUP)
        upstream = right_t(dvq_ref[span, :], w_q[...]) + right_t(dckv_ref[span, :], w_kv[...])
        part, gain, bias = norm_back(x1_ref[span, :], gain_ref[3:4, :], upstream)
        total = dx2_ref[span, :] + part
        dx1[span, :] = total
        rounded[span, :] = total.astype(NARROW)
        norm_ref[0:1, :] += gain
        norm_ref[1:2, :] += bias

    loop(rows // GROUP, first)
    loads[2].wait()
    ready(6)
    dmw[...] = right_t(rounded[...], w_out[...]).astype(NARROW)
    store_rows(
        weight_ref, slice(3 * features, 4 * features), left_t(mw_ref[...], rounded[...])
    )
    deltas[...] = head_rows(dmw[...].astype(SINGLE) * mw_ref[...].astype(SINGLE))
    ready(5)
    window = jnp.where(
        iota((WINDOWS, WINDOWS), 0) // WIN == iota((WINDOWS, WINDOWS), 1) // WIN, 0.0, MASKED
    )

    def group(i):
        span = at(i, WINDOWS)
        for pair in range(features // PAIR):
            lane = pair * PAIR
            dq, dk, dv = attend_back(
                pw_ref[span, lane : lane + PAIR],
                pw_ref[span, features + lane : features + lane + PAIR],
                pw_ref[span, 2 * features + lane : 2 * features + lane + PAIR],
                dmw[span, lane : lane + PAIR],
                None,
                [deltas[2 * pair + w : 2 * pair + w + 1, span] for w in range(2)],
                lambda scores: scores + window,
            )
            dpw[span, lane : lane + PAIR] = (dq * (1.0 / math.sqrt(HEAD))).astype(NARROW)
            dpw[span, features + lane : features + lane + PAIR] = dk.astype(NARROW)
            dpw[span, 2 * features + lane : 2 * features + lane + PAIR] = dv.astype(NARROW)

    loop(rows // WINDOWS, group)
    ready(4)
    for start in range(0, 3 * features, CHUNK):
        span = slice(start, start + CHUNK)
        store_rows(weight_ref, span, left_t(n0_ref[...], dpw[:, span]))
    launch(1)
    flush(1)
    ready(0)
    loads[3].wait()

    def last(i):
        span = at(i, GROUP)
        upstream = right_t(dpw[span, :], w_in[...])
        part, gain, bias = norm_back(x_ref[span, :].astype(SINGLE), gain_ref[0:1, :], upstream)
        grad_ref[span, :] = dx1[span, :] + part
        norm_ref[2:3, :] += gain
        norm_ref[3:4, :] += bias

    loop(rows // GROUP, last)


def share_backward(
    pieces, q1, nq, gain_ref, a_in, *rest, launch=nothing
):
    parts = [rest[k * pieces : (k + 1) * pieces] for k in range(3)]
    rest = rest[3 * pieces :]
    grad_ref, weight_ref, norm_ref, w_q, w_kv, summed, q1_ref, nq_ref, sem = rest
    part, features = q1_ref.shape
    *loads, load_q, load_n = copies(
        sem,
        (a_in.at[2, :, pl.ds(0, features)], w_q),
        (a_in.at[3, :, pl.ds(features, 2 * features)], w_kv),
        (q1.at[at(place_of(), part), :], q1_ref),
        (nq.at[at(place_of(), part), :], nq_ref),
    )
    start = 0
    for k in range(3):
        width = parts[k][0].shape[1]
        total = functools.reduce(jnp.add, [one[...].astype(SINGLE) for one in parts[k]])
        summed[:, start : start + width] = total.astype(NARROW)
        start += width
    for load in loads:
        load.wait()
    upstream = right_t(summed[:, 0:features], w_q[...]) + right_t(summed[:, features:], w_kv[...])
    load_q.wait()
    piece, gain, bias = norm_back(q1_ref[...], gain_ref[2:3, :], upstream)
    grad_ref[...] = piece.astype(NARROW)
    launch(0)
    load_n.wait()
    for k in range(3):
        span = slice(k * features, (k + 1) * features)
        store_rows(weight_ref, span, left_t(nq_ref[...], summed[:, span]))
    launch(1)
    norm_ref[...] = jnp.zeros_like(norm_ref)
    norm_ref[0:1, :] = gain
    norm_ref[1:2, :] = bias


def causal_backward(
    pieces, share, q_ref, dq2_ref, n1_ref, pq_ref, mq_ref, log_ref, cross_ref, gain_ref,
    norm_x, norm_two, norm_four, norm_five, a_in, a_out, *rest, ready=nothing
):
    parts, rest = rest[: 2 * pieces - 1], rest[2 * pieces - 1 :]
    (
        weight_ref, grad_ref, norm_ref,
        w_in, w_out, gathered, dq1, rounded, dmq, deltas, dkv, dpq, norm_one, norm_all, sem,
    ) = rest
    rows, features = q_ref.shape
    placed = place_parts(gathered, pieces, parts, sem)
    loads = copies(sem.at[pl.ds(len(placed), 2)], (a_out.at[1], w_out), (a_in.at[1], w_in))
    for one in placed:
        one.wait()

    def first(i):
        span = at(i, STRIP)
        total = dq2_ref[span, :] + gathered[span, :].astype(SINGLE)
        dq1[span, :] = total
        rounded[span, :] = total.astype(NARROW)

    loop(rows // STRIP, first)
    loads[0].wait()
    dmq[...] = right_t(rounded[...], w_out[...]).astype(NARROW)
    ready(4)
    chosen = chooser(weight_ref.shape[0], features, place_of() * share, share)
    taken = right_t(chosen, mq_ref[...]).astype(NARROW)
    weight_ref[:, 3 * features : 4 * features] = plain(taken, rounded[...]).astype(NARROW)
    weight_ref[:, 4 * features : 5 * features] = cross_ref[...]
    weight_ref[:, 5 * features :] = jnp.zeros_like(weight_ref[:, 5 * features :])
    deltas[...] = head_rows(dmq[...].astype(SINGLE) * mq_ref[...].astype(SINGLE))
    edges = spans(rows, 256)
    ready(3)
    ready(5)

    def pair(p):
        for number, (start, end) in reversed(list(enumerate(edges))):
            span = slice(start, end)

            def mask(scores, start=start):
                shape = scores.shape
                return jnp.where(iota(shape, 0) <= iota(shape, 1) + start, scores, MASKED)

            dq, dk, dv = attend_back(
                pq_ref[span, at(p, PAIR)],
                pq_ref[0:end, at(p + features // PAIR, PAIR)],
                pq_ref[0:end, at(p + 2 * features // PAIR, PAIR)],
                dmq[span, at(p, PAIR)],
                row_pair(log_ref, p, span),
                row_pair(deltas, p, span),
                mask,
            )
            dpq[span, at(p, PAIR)] = (dq * (1.0 / math.sqrt(HEAD))).astype(NARROW)
            if end == rows:
                dkv[0:end, 0:PAIR] = dk
                dkv[0:end, PAIR:] = dv
            else:
                dkv[0:end, 0:PAIR] += dk
                dkv[0:end, PAIR:] += dv
        dpq[:, at(p + features // PAIR, PAIR)] = dkv[:, 0:PAIR].astype(NARROW)
        dpq[:, at(p + 2 * features // PAIR, PAIR)] = dkv[:, PAIR:].astype(NARROW)

    loop(features // PAIR, pair)
    ready(2)
    taken = right_t(chosen, n1_ref[...]).astype(NARROW)
    weight_ref[:, 0 : 3 * features] = plain(taken, dpq[...]).astype(NARROW)
    loads[1].wait()
    norm_one[...] = jnp.zeros_like(norm_one)

    def last(i):
        span = at(i, STRIP)
        upstream = right_t(dpq[span, :], w_in[...])
        piece, gain, bias = norm_back(q_ref[span, :].astype(SINGLE), gain_ref[1:2, :], upstream)
        grad_ref[span, :] = dq1[span, :] + piece
        norm_one[0:1, :] += gain
        norm_one[1:2, :] += bias

    loop(rows // STRIP, last)
    leader = jnp.where(place_of() == 0, 1.0, 0.0)
    norm_all[...] = jnp.zeros_like(norm_all)
    for row, (ref, source, scale) in enumerate(
        (
            (norm_x, 2, 1.0), (norm_one, 0, leader), (norm_two, 0, 1.0), (norm_x, 0, 1.0),
            (norm_four, 0, leader), (norm_five, 0, 1.0),
        )
    ):
        norm_all[row : row + 1, :] = ref[source : source + 1, :] * scale
        norm_all[8 + row : 9 + row, :] = ref[source + 1 : source + 2, :] * scale
    if len(norm_ref.shape) == 2:
        norm_ref[...] = norm_all[...]
    else:
        norm_ref[...] = jnp.zeros_like(norm_ref)
        for owner in range(norm_ref.shape[0]):
            norm_ref[owner, :, 0:share] = norm_all[:, owner * share : (owner + 1) * share]


def assemble(groups, count, *refs, ready=nothing, flush=nothing):
    parts, refs = refs[: 4 * groups], refs[4 * groups :]
    norms, refs = refs[:count], refs[count:]
    in_ref, out_ref, up_ref, down_ref, gain_ref, bias_ref, share, causal = refs
    features = down_ref.shape[2]
    rep = place_of("rep")

    def corners(number, write):
        for k in range(4):
            ready(4 * number + k)
            owner = flipped(rep, k, 4)
            piece = parts[4 * number + k][...]
            height, width = piece.shape[-2:]
            piece = piece.reshape(height, width)
            write(
                pl.ds(pl.multiple_of((owner % 2) * height, height), height),
                pl.multiple_of((owner // 2) * width, width), width, piece,
            )

    def into(ref, index, start=0):
        def write(rows, column, width, piece):
            ref[index, rows, pl.ds(column + start, width)] = piece

        return write

    up_x, down_x, reverse, window, kv, shared, up_q, down_q, rest = range(groups)

    def keep_causal(rows, column, width, piece):
        causal[rows, pl.ds(column, width)] = piece

    def keep_share(rows, column, width, piece):
        share[rows, pl.ds(column, width)] = piece

    corners(up_q, into(up_ref, 1))
    corners(down_q, into(down_ref, 1))
    corners(up_x, into(up_ref, 0))
    flush(2)
    corners(down_x, into(down_ref, 0))
    flush(3)
    first = 4 * groups
    for k in range(count):
        ready(first + k)
    terms = [norms[0][place_of()]] + [one[...] for one in norms[1:]]
    total = functools.reduce(jnp.add, terms)
    columns = gain_ref.shape[1]
    gain_ref[...] = total[0:6, 0:columns]
    bias_ref[...] = total[8:14, 0:columns]
    flush(4)
    flush(5)
    corners(reverse, keep_share)
    in_ref[3, :, 0:features] = share[:, 0:features]
    out_ref[3, :, :] = share[:, features : 2 * features]
    corners(window, keep_share)
    in_ref[0, :, :] = share[:, 0 : 3 * features]
    out_ref[0, :, :] = share[:, 3 * features :]
    corners(rest, keep_causal)
    in_ref[1, :, :] = causal[:, 0 : 3 * features]
    out_ref[1, :, :] = causal[:, 3 * features : 4 * features]
    out_ref[2, :, :] = causal[:, 4 * features : 5 * features]
    flush(1)
    corners(kv, into(in_ref, 2, features))
    corners(shared, keep_share)
    in_ref[2, :, 0:features] = share[:, 0:features]
    in_ref[3, :, features:] = share[:, features : 3 * features]
    flush(0)


def bits_of(count):
    return max(count - 1, 0).bit_length()


def swap(tensor, axis, mask):
    return lax.ppermute(tensor, axis, [(i, i ^ mask) for i in range(lax.axis_size(axis))])


def pick(tensor, place, dim):
    return lax.dynamic_index_in_dim(tensor, place, dim, keepdims=False)


def fold(tensor, axis, bit, dim):
    own = (lax.axis_index(axis) >> bit) & 1
    arrived = swap(pick(tensor, 1 - own, dim).astype(NARROW), axis, 1 << bit)
    return pick(tensor, own, dim).astype(SINGLE) + arrived.astype(SINGLE)


def unfold(tensor, axis, bit, dim):
    own = (lax.axis_index(axis) >> bit) & 1
    arrived = swap(tensor, axis, 1 << bit)
    return jnp.where(
        own == 0,
        jnp.stack((tensor, arrived), axis=dim),
        jnp.stack((arrived, tensor), axis=dim),
    )


def scatter_blk(tensor):
    bits = bits_of(lax.axis_size("blk"))
    tensor = tensor.reshape((2,) * bits + tensor.shape[1:])
    for bit in range(bits):
        tensor = fold(tensor, "blk", bit, bits - 1 - bit)
    return tensor


def sum_rep_scatter(tensor, dim):
    bits = bits_of(lax.axis_size("rep"))
    shape = tensor.shape
    tensor = tensor.reshape(
        shape[:dim] + (2,) * bits + (shape[dim] // 2**bits,) + shape[dim + 1 :]
    )
    for bit in range(bits):
        tensor = fold(tensor, "rep", bit, dim)
    return tensor


def gather_rep(tensor, dim):
    bits = bits_of(lax.axis_size("rep"))
    for bit in reversed(range(bits)):
        tensor = unfold(tensor, "rep", bit, dim)
    shape = tensor.shape
    return tensor.reshape(shape[:dim] + (-1,) + shape[dim + bits + 1 :])


def reduce_all(tensor):
    count = lax.axis_size("blk")
    tensor = tensor.reshape(count, tensor.shape[0] // count, tensor.shape[1])
    tensor = sum_rep_scatter(tensor, 1)
    tensor = scatter_blk(tensor).astype(NARROW)
    return gather_rep(tensor, 0)


def reduce_rep(tensor):
    return gather_rep(sum_rep_scatter(tensor, 0).astype(NARROW), 0)


def exchange(pieces):
    whole = lax.all_to_all(jnp.stack(pieces), "blk", 0, 0)
    return [whole[k] for k in range(len(pieces))]


def gather(tensor):
    count = lax.axis_size("blk")
    whole = lax.all_gather(tensor, "blk")
    return [whole[k] for k in range(count)]


def whole(ref):
    return ref


class Fold:
    def __init__(self, own, take, arrived, shape, keep=whole, keep_shape=None):
        self.own, self.take, self.arrived, self.shape = own, take, arrived, shape
        self.keep, self.keep_shape = keep, keep_shape or shape
        self.dtype = own.dtype


class Move:
    late = None

    def __init__(self, source, shape, axis, flip, take=whole, phase=0):
        self.source, self.shape, self.axis, self.flip, self.take = source, shape, axis, flip, take
        self.phase = phase
        self.dtype = source.dtype


def lanes_of(ref, start, width):
    return ref.at[(slice(None),) * (len(ref.shape) - 1) + (pl.ds(start, width),)]


class Reduction:
    def __init__(self, tensor, blocks=None):
        if blocks == 1:
            tensor = tensor.reshape(1, 1, 2, tensor.shape[0] // 2, tensor.shape[1])
        elif len(tensor.shape) == 2:
            blocks = lax.axis_size("blk")
            height = tensor.shape[0] // blocks
            tensor = tensor.reshape(blocks // 2, 2, 2, height // 2, tensor.shape[1])
        self.tensor, self.take, self.arrived, self.shape = tensor, whole, [], tensor.shape

    def fold(self, keep=whole, keep_shape=None):
        return Fold(self.tensor, self.take, self.arrived, self.shape, keep, keep_shape)

    def moves(self, stage):
        shape = self.shape
        if stage == "core":
            self.next = shape[:2] + shape[3:]
            return [
                Move(self.tensor, self.next, "rep", 1,
                     lambda ref: ref.at[:, :, 1 - place_of("rep") % 2])
            ]
        if stage == "x":
            width = shape[-1] // 2
            self.next = shape[:-1] + (width,)

            def own(ref):
                return lanes_of(ref, pl.multiple_of((place_of("rep") // 2) * width, width), width)

            def other(ref):
                start = (1 - place_of("rep") // 2) * width
                return lanes_of(ref, pl.multiple_of(start, width), width)

            return [Move(self.fold(own, self.next), self.next, "rep", 2, other)]
        if stage == "y":
            self.next = shape[:1] + shape[2:]
            fold = self.fold(lambda ref: ref.at[:, place_of() % 2], self.next)
            return [Move(fold, self.next, "blk", 1, lambda ref: ref.at[:, 1 - place_of() % 2])]
        if stage == "z":
            length = shape[0]
            self.next = shape[1:]
            fold = self.fold(lambda ref: ref.at[place_of() // 2], self.next)
            return [
                Move(fold, self.next, "blk", 2 * k,
                     lambda ref, k=k: ref.at[flipped(place_of() // 2, k, length)])
                for k in range(1, length)
            ]
        if stage == "back":
            fold = self.fold()
            return [Move(fold, shape, "rep", k) for k in range(1, 4)]
        if stage == "back_x":
            return [Move(self.fold(), shape, "rep", 2)]
        return [Move(self.tensor, shape, "rep", 1), Move(self.other, shape, "rep", 1)]

    def absorb(self, stage, arrived, kept):
        if stage == "core":
            self.take = lambda ref: ref.at[:, :, place_of("rep") % 2]
        else:
            self.take = whole
        if kept:
            self.tensor = kept[0]
        if stage in ("back", "back_x", "back_core"):
            if stage == "back_x":
                self.other = arrived[0]
                return
            if stage == "back":
                self.result = [self.tensor] + list(arrived)
            else:
                self.result = [self.tensor, arrived[0], self.other, arrived[1]]
            return
        self.shape, self.arrived = self.next, list(arrived)


class Exchange:
    def __init__(self, pieces):
        self.pieces = pieces

    def moves(self, stage):
        return [Move(one, one.shape, "blk", k) for k, one in enumerate(self.pieces) if k]

    def absorb(self, stage, arrived, kept):
        self.result = self.pieces[:1] + list(arrived)


class Pieces:
    def __init__(self, tensor, part, start, width):
        self.tensor, self.part, self.start, self.width = tensor, part, start, width

    def moves(self, stage):
        part, span = self.part, slice(self.start, self.start + self.width)
        count = lax.axis_size("blk")
        return [
            Move(self.tensor, (part, self.width), "blk", k,
                 lambda ref, k=k: ref.at[at(flipped(place_of(), k, count), part), span])
            for k in range(1, count)
        ]

    def absorb(self, stage, arrived, kept):
        self.result = list(arrived)


class Gather:
    def __init__(self, tensor):
        self.tensor = tensor

    def moves(self, stage):
        return [
            Move(self.tensor, self.tensor.shape, "blk", k) for k in range(1, lax.axis_size("blk"))
        ]

    def absorb(self, stage, arrived, kept):
        self.result = [self.tensor] + list(arrived)


class Spread:
    def __init__(self, tensor):
        self.tensor = tensor

    def moves(self, stage):
        count = lax.axis_size("blk")
        rows, width = self.tensor.shape[0], self.tensor.shape[1] // 2
        moves, self.places = [], []
        for number in range(2):
            span = slice(number * width, (number + 1) * width)
            own = lambda ref, span=span: ref.at[:, span]
            along = []
            for k in range(2, count, 2):
                along.append(Move(self.tensor, (rows, width), "blk", k, own, number))
                self.places.append((number, k))
            moves += along
            moves.append(Move(self.tensor, (rows, width), "blk", 1, own, number + 1))
            self.places.append((number, 1))
            for one in along:
                moves.append(Move(one, (rows, width), "blk", 1, whole, number + 1))
                self.places.append((number, one.flip + 1))
        return moves

    def absorb(self, stage, arrived, kept):
        found = dict(zip(self.places, arrived))
        count = lax.axis_size("blk")
        self.result = [found[number, k] for number in range(2) for k in range(1, count)]


class Norms:
    def __init__(self, tensor):
        self.tensor = tensor

    def moves(self, stage):
        axis = "rep" if stage == "out" else "blk"
        count = lax.axis_size(axis)
        shape = self.tensor.shape
        if stage == "out":
            return [Move(self.tensor, shape, axis, k) for k in range(1, count)]
        fold = Fold(self.tensor, whole, self.arrived, shape)
        return [
            Move(fold, shape[1:], axis, k,
                 lambda ref, k=k: ref.at[flipped(place_of(), k, count)])
            for k in range(1, count)
        ]

    def absorb(self, stage, arrived, kept):
        if stage == "out":
            self.arrived = list(arrived)
        else:
            self.result = [kept[0]] + list(arrived)


VMEM = pl.BlockSpec(memory_space=pltpu.VMEM)
SMEM = pl.BlockSpec(memory_space=pltpu.SMEM)
ANY = pl.BlockSpec(memory_space=pl.ANY)


def like(*shape, kind=NARROW):
    return jax.ShapeDtypeStruct(shape, kind)


def index_of(items, item):
    return next(k for k, one in enumerate(items) if one is item)


def call(
    kernel, outs, operands, specs, scratch, flops, grid=None, out_specs=None, semaphores=0,
    moves=(), ident=None, ticking=False, lazy=(), early=(),
):
    scratch = [pltpu.VMEM(shape, kind) for shape, kind in scratch]
    if semaphores:
        scratch.append(pltpu.SemaphoreType.DMA((semaphores,)))
    out_specs = [VMEM] * len(outs) if out_specs is None else out_specs
    extra = {} if grid is None else {"grid": grid}
    params = {}
    sources, folds = [], []

    def need(array):
        if not any(array is one for one in sources):
            sources.append(array)

    for move in moves:
        if isinstance(move.source, Fold):
            if not any(move.source is one for one in folds):
                folds.append(move.source)
                for array in [move.source.own] + move.source.arrived:
                    need(array)
        elif move.late is None and not isinstance(move.source, Move):
            need(move.source)
    fixed_in, fixed_out = len(operands), len(outs)
    partners = sorted({(move.axis, move.flip) for move in moves})
    lasts = max([move.phase for move in moves], default=0)
    held_in = [k for k, spec in enumerate(specs) if spec is VMEM]
    held_out = [k for k, spec in enumerate(out_specs) if spec is VMEM]
    own_scratch = len(scratch)
    scratch += [pltpu.VMEM(operands[k].shape, operands[k].dtype) for k in held_in]
    scratch += [pltpu.VMEM(outs[k].shape, outs[k].dtype) for k in held_out]
    terms = sum(1 + len(fold.arrived) for fold in folds)
    for fold in folds:
        scratch += [pltpu.VMEM(fold.shape, NARROW)] * (1 + len(fold.arrived))
    for number in (len(held_in), len(held_out), terms, len(folds), len(moves), len(moves)):
        scratch.append(pltpu.SemaphoreType.DMA((max(number, 1),)))
    if moves:
        params = {"collective_id": ident, "has_side_effects": True}
    before = {}
    for move in moves:
        if isinstance(move.source, Move):
            number = index_of(moves, move.source)
            before[number] = min(move.phase, before.get(number, move.phase))

    def body_kernel(*refs):
        ins, refs = list(refs[:fixed_in]), refs[fixed_in:]
        sent, refs = refs[: len(sources)], refs[len(sources) :]
        results, refs = list(refs[:fixed_out]), refs[fixed_out:]
        landed, refs = refs[: len(moves)], refs[len(moves) :]
        kept, refs = refs[: len(folds)], refs[len(folds) :]
        rest, refs = refs[:own_scratch], refs[own_scratch:]
        inner, refs = refs[: len(held_in)], refs[len(held_in) :]
        outer, refs = refs[: len(held_out)], refs[len(held_out) :]
        buffers, (in_sem, out_sem, load_sem, keep_sem, send_sem, recv_sem) = refs[:terms], refs[terms:]
        fetches, stores = {}, {}
        for number, k in enumerate(held_in):
            fetches[k] = pltpu.make_async_copy(ins[k], inner[number], in_sem.at[number])
            ins[k] = inner[number]
        for number, k in enumerate(held_out):
            stores[k] = pltpu.make_async_copy(outer[number], results[k], out_sem.at[number])
            results[k] = outer[number]

        def target(axis, flip):
            return {axis: flipped(lax.axis_index(axis), flip, lax.axis_size(axis))}

        def buffers_of(fold):
            start = sum(1 + len(one.arrived) for one in folds[: index_of(folds, fold)])
            return start, buffers[start : start + 1 + len(fold.arrived)]

        def made(k):
            move = moves[k]
            if move.late is not None:
                source = results[move.late]
            elif isinstance(move.source, Fold):
                source = buffers_of(move.source)[1][0]
            elif isinstance(move.source, Move):
                source = landed[index_of(moves, move.source)]
            else:
                source = sent[index_of(sources, move.source)]
            return pltpu.make_async_remote_copy(
                src_ref=move.take(source),
                dst_ref=landed[k],
                send_sem=send_sem.at[k],
                recv_sem=recv_sem.at[k],
                device_id=target(move.axis, move.flip),
                device_id_type=pl.DeviceIdType.MESH,
            )

        def loads(fold):
            start, held = buffers_of(fold)
            return [
                pltpu.make_async_copy(
                    (fold.take if k == 0 else whole)(sent[index_of(sources, array)]),
                    held[k],
                    load_sem.at[start + k],
                )
                for k, array in enumerate([fold.own] + fold.arrived)
            ]

        def keeping(k):
            fold = folds[k]
            return pltpu.make_async_copy(
                fold.keep(buffers_of(fold)[1][0]), kept[k], keep_sem.at[k]
            )

        def add(fold):
            held = buffers_of(fold)[1]

            def one(index):
                if len(held) == 2:
                    held[0][index] = held[0][index] + held[1][index]
                elif len(held) > 2:
                    held[0][index] = functools.reduce(
                        jnp.add, [part[index].astype(SINGLE) for part in held]
                    ).astype(NARROW)

            if len(fold.shape) == 2:
                one((slice(None), slice(None)))
            else:
                loop(fold.shape[0], one)

        def begin():
            for fold in folds:
                for load in loads(fold):
                    load.start()
            for fetch in fetches.values():
                fetch.start()
            if moves:
                barrier = pltpu.get_barrier_semaphore()
                for axis, flip in partners:
                    pl.semaphore_signal(
                        barrier, inc=1, device_id=target(axis, flip),
                        device_id_type=pl.DeviceIdType.MESH,
                    )
                pl.semaphore_wait(barrier, len(partners))
            for k, move in enumerate(moves):
                if move.phase == 0 and move.late is None and not isinstance(move.source, Fold):
                    made(k).start()
            for number, fold in enumerate(folds):
                for load in loads(fold):
                    load.wait()
                add(fold)
                for k, move in enumerate(moves):
                    if move.source is fold:
                        made(k).start()
                keeping(number).start()
            for k, fetch in fetches.items():
                if k not in lazy:
                    fetch.wait()

        def launch(which):
            for k in range(len(moves)):
                if moves[k].late == which and moves[k].phase == 0:
                    made(k).start()

        def tick(phase):
            for k, needed in before.items():
                if needed == phase:
                    made(k).wait_recv()
            for k, move in enumerate(moves):
                if move.phase == phase:
                    made(k).start()

        def finish():
            for k, store in stores.items():
                if k not in early:
                    store.start()
            if not ticking:
                for phase in range(1, lasts + 1):
                    tick(phase)
            for k in range(len(moves)):
                made(k).wait_send()
                if k not in before:
                    made(k).wait_recv()
            for k in range(len(folds)):
                keeping(k).wait()
            for store in stores.values():
                store.wait()

        options = {}
        if any(move.late is not None for move in moves):
            options["launch"] = launch
        if ticking:
            options["tick"] = tick
        if lazy:
            options["ready"] = lambda k: fetches[k].wait()
        if early:
            options["flush"] = lambda k: stores[k].start()
        if grid is None:
            begin()
            kernel(*ins, *results, *rest, **options)
            finish()
        else:
            pl.when(pl.program_id(0) == 0)(begin)
            kernel(*ins, *results, *rest, **options)
            pl.when(pl.program_id(0) == pl.num_programs(0) - 1)(finish)

    result = pl.pallas_call(
        body_kernel,
        out_shape=list(outs)
        + [
            like(*m.shape, kind=m.dtype)
            for m in moves
        ]
        + [like(*fold.keep_shape) for fold in folds],
        in_specs=[ANY if spec is VMEM else spec for spec in specs] + [ANY] * len(sources),
        out_specs=[ANY if spec is VMEM else spec for spec in out_specs]
        + [ANY] * (len(moves) + len(folds)),
        scratch_shapes=scratch,
        compiler_params=pltpu.CompilerParams(vmem_limit_bytes=60 * 2**20, **params),
        cost_estimate=pl.CostEstimate(
            flops=int(flops),
            bytes_accessed=sum(o.size * o.dtype.itemsize for o in operands),
            transcendentals=0,
        ),
        **extra,
    )(*operands, *sources)
    end = fixed_out + len(moves)
    return list(result[:fixed_out]), list(result[fixed_out:end]), (folds, list(result[end:]))


def finale(kernel, outs, stages, results, scratch, ident):
    plan = []
    for stage in stages:
        for job, name in stage:
            moves = job.moves(name)
            folds = []
            for move in moves:
                known = folds + [fold for part, _ in plan for fold in part]
                if isinstance(move.source, Fold) and not any(move.source is one for one in known):
                    folds.append(move.source)
            job.absorb(name, moves, folds)
            plan.append((folds, moves))
    items = results()
    moves = [move for _, part in plan for move in part]
    folds = [fold for part, _ in plan for fold in part]
    sources, fetched = [], []

    def need(item):
        if not isinstance(item, (Fold, Move)) and not any(item is one for one in sources):
            sources.append(item)

    for fold in folds:
        for item in [fold.own] + fold.arrived:
            need(item)
            if not isinstance(item, (Fold, Move)):
                fetched.append((fold, item))
    for move in moves:
        need(move.source)
    plain_items = []
    for item in items:
        need(item)
        if not isinstance(item, (Fold, Move)):
            plain_items.append(item)
    partners = sorted({(move.axis, move.flip) for move in moves})
    shapes = [pltpu.VMEM(one.shape, one.dtype) for one in scratch]
    shapes += [pltpu.VMEM(move.shape, move.dtype) for move in moves]
    shapes += [pltpu.VMEM(fold.shape, fold.dtype) for fold in folds]
    shapes += [pltpu.VMEM(fold.shape, fold.dtype) for fold, _ in fetched]
    shapes += [pltpu.VMEM(item.shape, item.dtype) for item in plain_items]
    shapes += [pltpu.VMEM(one.shape, one.dtype) for one in outs]
    for number in (len(moves), len(moves), len(fetched), len(plain_items), len(outs)):
        shapes.append(pltpu.SemaphoreType.DMA((max(number, 1),)))

    def body_kernel(*refs):
        def take(count):
            nonlocal refs
            some, refs = refs[:count], refs[count:]
            return some

        sent, finals = take(len(sources)), take(len(outs))
        rest, landed, sums = take(len(scratch)), take(len(moves)), take(len(folds))
        brought, held, outer = take(len(fetched)), take(len(plain_items)), take(len(outs))
        send_sem, recv_sem, load_sem, item_sem, out_sem = refs
        arrived = set()

        def target(axis, flip):
            return {axis: flipped(lax.axis_index(axis), flip, lax.axis_size(axis))}

        def place(item):
            if isinstance(item, Fold):
                return sums[index_of(folds, item)]
            if isinstance(item, Move):
                return landed[index_of(moves, item)]
            return sent[index_of(sources, item)]

        def made(move):
            k = index_of(moves, move)
            source = place(move.source)
            return pltpu.make_async_remote_copy(
                src_ref=move.take(source),
                dst_ref=landed[k],
                send_sem=send_sem.at[k],
                recv_sem=recv_sem.at[k],
                device_id=target(move.axis, move.flip),
                device_id_type=pl.DeviceIdType.MESH,
            )

        def arrival(item):
            if isinstance(item, Move) and index_of(moves, item) not in arrived:
                arrived.add(index_of(moves, item))
                made(item).wait_recv()

        loads = [
            pltpu.make_async_copy(
                (fold.take if item is fold.own else whole)(place(item)), brought[k], load_sem.at[k]
            )
            for k, (fold, item) in enumerate(fetched)
        ]
        fetches = [
            pltpu.make_async_copy(place(item), held[k], item_sem.at[k])
            for k, item in enumerate(plain_items)
        ]
        stores = [
            pltpu.make_async_copy(outer[k], finals[k], out_sem.at[k]) for k in range(len(outs))
        ]
        for load in loads:
            load.start()
        barrier = pltpu.get_barrier_semaphore()
        for axis, flip in partners:
            pl.semaphore_signal(
                barrier, inc=1, device_id=target(axis, flip), device_id_type=pl.DeviceIdType.MESH
            )
        pl.semaphore_wait(barrier, len(partners))

        def total(fold):
            terms = []
            for item in [fold.own] + fold.arrived:
                if isinstance(item, (Fold, Move)):
                    arrival(item)
                    term = place(item)
                    if item is fold.own:
                        term = fold.take(item.keep(term) if isinstance(item, Fold) else term)
                else:
                    k = next(
                        k for k, (one, other) in enumerate(fetched) if one is fold and other is item
                    )
                    loads[k].wait()
                    term = brought[k]
                terms.append(term)
            goal = place(fold)

            def one(index):
                goal[index] = functools.reduce(
                    jnp.add, [term[index].astype(SINGLE) for term in terms]
                ).astype(goal.dtype)

            if len(fold.shape) == 2:
                one((slice(None), slice(None)))
            else:
                loop(fold.shape[0], one)

        for number, (some, part) in enumerate(plan):
            for fold in some:
                total(fold)
            for move in part:
                arrival(move.source)
                made(move).start()
            if number == 0:
                for fetch in fetches:
                    fetch.start()
        operands = []
        for item in items:
            if isinstance(item, (Fold, Move)):
                operands.append(place(item))
            else:
                operands.append(held[next(k for k, one in enumerate(plain_items) if one is item)])
        for fetch in fetches:
            fetch.wait()

        def ready(k):
            arrival(items[k])

        kernel(*operands, *outer, *rest, ready=ready, flush=lambda k: stores[k].start())
        for move in moves:
            made(move).wait_send()
            arrival(move)
        for store in stores:
            store.wait()

    return pl.pallas_call(
        body_kernel,
        out_shape=list(outs),
        in_specs=[ANY] * len(sources),
        out_specs=[ANY] * len(outs),
        scratch_shapes=shapes,
        compiler_params=pltpu.CompilerParams(
            vmem_limit_bytes=60 * 2**20, collective_id=ident, has_side_effects=True
        ),
    )(*sources)


class Courier:
    def __init__(self, active):
        self.active, self.waiting, self.ident = active, [], 0

    def load(self, *jobs):
        self.waiting += jobs

    def run(self, kernel, outs, operands, specs, scratch, flops, **extra):
        jobs, self.waiting = self.waiting, []
        moves, ends = [], []
        for job, stage, *late in jobs:
            added = job.moves(stage)
            for move in added:
                if late and not isinstance(move.source, Move):
                    move.late = late[0]
            moves += added
            ends.append(len(moves))
        if moves:
            self.ident += 1
        results, arrived, (folds, kept) = call(
            kernel, outs, operands, specs, scratch, flops, moves=tuple(moves), ident=self.ident, **extra
        )
        start = 0
        for (job, stage, *late), end in zip(jobs, ends):
            if late:
                job.tensor = results[late[0]]
            own = [
                kept[k]
                for k, fold in enumerate(folds)
                if any(move.source is fold for move in moves[start:end])
            ]
            job.absorb(stage, arrived[start:end], own)
            start = end
        return results


def in_halves(arrays):
    width = arrays[0].shape[1] // 2
    return (
        arrays[:1] + [one[:, :width] for one in arrays[1:]] + [one[:, width:] for one in arrays[1:]]
    )


def body(
    patches,
    queries,
    window_valid,
    answer_length,
    norm_gain,
    norm_bias,
    attn_in,
    attn_out,
    mlp_in,
    mlp_out,
    cot_patches,
    cot_queries,
):
    x, q, cot_x, cot_q = patches[0], queries[0], cot_patches[0], cot_queries[0]
    rows, features = x.shape
    count = q.shape[0]
    hidden = mlp_in.shape[2]
    blocks = lax.axis_size("blk")
    place = lax.axis_index("blk").astype(jnp.int32)
    share = features // blocks
    hidden_share = hidden // blocks
    share_rows = -(-share // 16) * 16
    hidden_rows = -(-hidden_share // 16) * 16
    part = -(-count // (blocks * 16)) * 16
    padded = part * blocks
    wide = 3 * features
    last = wide + features + features
    causal_columns = -(-last // 512) * 512
    valid = jnp.where(jnp.repeat(window_valid[0], WIN) > 0, 0.0, MASKED).astype(SINGLE)
    carried = blocks == DIRECT and lax.axis_size("rep") == 4 and share % 32 == 0
    courier = Courier(carried)

    def own_columns(tensor):
        return lax.dynamic_slice_in_dim(tensor, place * share, share, 1)

    square = 2.0 * features * features
    run = courier.run

    n0, pw, mw, x1, nx, vq, ckv = run(
        window_forward,
        [
            like(rows, features), like(rows, wide), like(rows, features),
            like(rows, features, kind=SINGLE), like(rows, features), like(rows, features),
            like(rows, 2 * features),
        ],
        [x, norm_gain, norm_bias, attn_in, attn_out],
        [VMEM, VMEM, VMEM, ANY, ANY],
        [((features, wide), NARROW), ((features, features), NARROW),
         ((features, features), NARROW), ((features, 2 * features), NARROW)],
        rows * square * 9,
        semaphores=4,
        early=(0, 1, 2, 3, 4, 5),
    )
    n1, pq, mq, q1, nq, cq, vkv, log_q = run(
        causal_forward,
        [
            like(count, features), like(count, wide), like(count, features),
            like(padded, features, kind=SINGLE), like(padded, features), like(count, features),
            like(count, 2 * features), like(16, count, kind=SINGLE),
        ],
        [q, norm_gain, norm_bias, attn_in, attn_out],
        [VMEM, VMEM, VMEM, ANY, ANY],
        [((features, wide), NARROW), ((features, features), NARROW),
         ((features, features), NARROW), ((features, 2 * features), NARROW),
         ((count, PAIR), SINGLE)],
        count * square * 15,
        semaphores=4,
        early=(0, 1, 2, 3, 4, 5),
    )
    outs, *log_pieces = run(
        functools.partial(cross_forward, blocks),
        [like(padded, features)] + [like(16, part, kind=SINGLE)] * blocks,
        [cq, ckv, valid[None, :]],
        [VMEM, VMEM, VMEM],
        [((padded, PAIR), SINGLE)],
        count * square * 6,
    )
    logs = Exchange(log_pieces)
    first_width = features // 3
    halves = [
        Pieces(outs, part, 0, first_width),
        Pieces(outs, part, first_width, features - first_width),
    ]
    if carried:
        courier.load((logs, ""), (halves[0], ""))
    mv, x2, log_v = run(
        reverse_forward,
        [like(rows, features), like(rows, features, kind=SINGLE), like(16, rows, kind=SINGLE)],
        [answer_length, vq, vkv, x1, attn_out],
        [SMEM, VMEM, VMEM, VMEM, ANY],
        [((features, features), NARROW), ((rows, PAIR), SINGLE)],
        rows * square * 8,
        semaphores=1,
        lazy=(3,),
        early=(0,),
    )
    if carried:
        courier.load((halves[1], ""))
    x3, dx2, up_x, down_x, norm_five = run(
        patch_feed_forward,
        [
            like(rows, features), like(rows, features, kind=SINGLE), like(features, hidden),
            like(hidden, features), like(8, features, kind=SINGLE),
        ],
        [x2, cot_x, norm_gain, norm_bias, mlp_in, mlp_out],
        [
            VMEM, VMEM, VMEM, VMEM,
            pl.BlockSpec((1, features, CHUNK), lambda j: (0, 0, j)),
            pl.BlockSpec((1, CHUNK, features), lambda j: (0, j, 0)),
        ],
        [((rows, features), NARROW), ((rows, CHUNK), NARROW), ((rows, CHUNK), NARROW),
         ((rows, features), SINGLE), ((rows, features), SINGLE)],
        rows * square * 24,
        grid=(hidden // CHUNK,),
        out_specs=[
            VMEM, VMEM,
            pl.BlockSpec((features, CHUNK), lambda j: (0, j)),
            pl.BlockSpec((CHUNK, features), lambda j: (j, 0)),
            VMEM,
        ],
    )
    if carried:
        merged = run(
            functools.partial(merge_blocks, blocks),
            [like(part, features), like(16, part, kind=SINGLE)],
            [outs] + logs.result + halves[0].result + halves[1].result,
            [VMEM] * (3 * blocks - 1),
            [],
            padded * square,
        )
        co_parts, log_parts = Spread(merged[0]), Gather(merged[1])
        up_x, down_x = Reduction(up_x), Reduction(down_x)
        reverse_weight = Reduction(like(blocks // 2, 2, 2, share // 2, 2 * features))
        courier.load(
            (co_parts, ""), (log_parts, ""), (up_x, "core"), (down_x, "core"),
            (reverse_weight, "core", 1),
        )
    else:
        whole_logs = jnp.stack(exchange(log_pieces))
        merged_log = jax.nn.logsumexp(whole_logs, axis=0)
        weights = jnp.transpose(jnp.exp(whole_logs - merged_log)[:, :HEADS], (0, 2, 1))
        shares = lax.all_to_all(outs.reshape(blocks, part, features), "blk", 0, 0)
        merged_out = jnp.sum(jnp.repeat(weights, HEAD, axis=2) * shares.astype(SINGLE), axis=0)
        co_parts, log_parts = Spread(None), Gather(None)
        co_parts.tensor, *co_parts.result = in_halves(gather(merged_out.astype(NARROW)))
        log_parts.result = gather(merged_log)
    folded = (blocks // 2, 2, 2, share // 2) if carried else (features,)
    dvq, reverse_grad, *kv_pieces = run(
        functools.partial(reverse_backward, blocks),
        [like(rows, features), like(*folded, 2 * features)]
        + [like(part, features + PAIR)] * blocks + [like(part, features - PAIR)] * blocks,
        [answer_length, dx2, mv, vq, vkv, nx, log_v, attn_out],
        [SMEM, VMEM, VMEM, VMEM, VMEM, VMEM, VMEM, ANY],
        [((features, features), NARROW), ((rows, features), NARROW), ((rows, features), NARROW),
         ((16, rows), SINGLE), ((padded, 2 * features), SINGLE)],
        rows * square * 16,
        semaphores=1,
        ticking=carried,
        lazy=(3, 4, 5, 6),
    )
    k_parts, v_parts = Exchange(kv_pieces[:blocks]), Exchange(kv_pieces[blocks:])
    if carried:
        courier.load((k_parts, ""), (up_x, "x"))
    else:
        k_parts.result, v_parts.result = exchange(k_parts.pieces), exchange(v_parts.pieces)
    q3, dq2, up_q, down_q, norm_four, co = run(
        functools.partial(query_feed_forward, blocks, share, hidden_share),
        [
            like(count, features), like(count, features, kind=SINGLE), like(share_rows, hidden),
            like(hidden_rows, features), like(8, features, kind=SINGLE), like(padded, features),
        ],
        [q1, cot_q, norm_gain, norm_bias, attn_out, mlp_in, mlp_out, co_parts.tensor]
        + co_parts.result,
        [
            VMEM, VMEM, VMEM, VMEM, pl.BlockSpec((1, features, features), lambda j: (2, 0, 0)),
            pl.BlockSpec((1, features, CHUNK), lambda j: (1, 0, j)),
            pl.BlockSpec((1, CHUNK, features), lambda j: (1, j, 0)),
        ] + [ANY] * (2 * blocks - 1),
        [((count, features), SINGLE), ((count, features), NARROW), ((share_rows, count), NARROW),
         ((count, CHUNK), NARROW), ((count, CHUNK), NARROW),
         ((count, features), SINGLE), ((count, features), SINGLE)],
        count * square * 18,
        semaphores=2 * blocks - 1,
        grid=(hidden // CHUNK,),
        out_specs=[
            VMEM, VMEM,
            pl.BlockSpec((share_rows, CHUNK), lambda j: (0, j)),
            VMEM, VMEM, VMEM,
        ],
    )
    if carried:
        up_q, down_q = Reduction(up_q, 1), Reduction(down_q, 1)
        courier.load((v_parts, ""), (down_x, "x"), (up_x, "y"), (up_q, "core"), (down_q, "core"))
    dckv, cross_out_weight, *q_pieces = run(
        functools.partial(cross_backward, blocks, share),
        [like(rows, 2 * features), like(share_rows, features)] + [like(part, features)] * blocks,
        [dq2, co, cq, ckv, valid[:, None], attn_out] + log_parts.result,
        [VMEM, VMEM, VMEM, VMEM, VMEM, ANY] + [VMEM] * blocks,
        [((features, features), NARROW), ((count, features), NARROW), ((count, features), NARROW),
         ((16, count), SINGLE), ((padded, PAIR), SINGLE), ((16, count), SINGLE),
         ((padded, features), NARROW), ((rows, 2 * features), SINGLE)],
        count * square * 12,
        semaphores=1,
        lazy=(2, 3),
    )
    q_parts = Exchange(q_pieces)
    if carried:
        kv_weight = Reduction(like(blocks // 2, 2, 2, share // 2, 2 * features))
        window_weight = Reduction(like(blocks // 2, 2, 2, share // 2, 4 * features))
        courier.load(
            (q_parts, ""), (down_x, "y"), (reverse_weight, "x"), (up_q, "x"), (down_q, "x"),
            (kv_weight, "core", 0), (window_weight, "core", 1),
        )
    else:
        q_parts.result = exchange(q_pieces)
    kv_grad, window_grad, grad_x, norm_x = run(
        patch_backward,
        [
            like(*folded, 2 * features), like(*folded, 4 * features),
            like(rows, features, kind=SINGLE), like(8, features, kind=SINGLE),
        ],
        [x, dx2, x1, nx, n0, pw, mw, dvq, dckv, norm_gain, attn_in, attn_out],
        [VMEM] * 10 + [ANY, ANY],
        [((features, wide), NARROW), ((features, features), NARROW),
         ((features, features), NARROW), ((features, 2 * features), NARROW),
         ((rows, features), SINGLE), ((rows, features), NARROW), ((rows, features), NARROW),
         ((16, rows), SINGLE), ((rows, wide), NARROW)],
        rows * square * 24,
        semaphores=4,
        lazy=(0, 4, 5, 6),
        early=(0, 1),
    )
    if carried:
        share_weight = Reduction(like(blocks // 2, 2, 2, share // 2, wide))
        dq1_parts = Spread(like(part, features))
        courier.load(
            (share_weight, "core", 1), (dq1_parts, "", 0), (window_weight, "x"),
            (reverse_weight, "y"), (up_q, "back_x"), (down_q, "back_x"),
        )
    dq1_share, share_grad, norm_two = run(
        functools.partial(share_backward, blocks),
        [like(part, features), like(*folded, wide), like(8, features, kind=SINGLE)],
        [q1, nq, norm_gain, attn_in]
        + q_parts.result + k_parts.result + v_parts.result,
        [ANY, ANY, VMEM, ANY] + [VMEM] * (3 * blocks),
        [((features, features), NARROW), ((features, 2 * features), NARROW),
         ((part, wide), NARROW), ((part, features), SINGLE), ((part, features), NARROW)],
        part * square * 6,
        semaphores=4,
    )
    if carried:
        courier.load(
            (window_weight, "y"), (share_weight, "x"), (kv_weight, "y"), (down_x, "z"),
            (reverse_weight, "z"), (up_q, "back_core"), (down_q, "back_core"), (up_x, "z"),
        )
    else:
        dq1_parts = Spread(None)
        dq1_parts.tensor, *dq1_parts.result = in_halves(gather(dq1_share))
    causal_weight, grad_q, norms = run(
        functools.partial(causal_backward, blocks, share),
        [
            like(share_rows, causal_columns), like(count, features, kind=SINGLE),
            like(blocks, 16, -(-share // PAIR) * PAIR, kind=SINGLE)
            if carried
            else like(16, features, kind=SINGLE),
        ],
        [q, dq2, n1, pq, mq, log_q, cross_out_weight, norm_gain]
        + [norm_x, norm_two, norm_four, norm_five, attn_in, attn_out, dq1_parts.tensor]
        + dq1_parts.result,
        [VMEM] * 12 + [ANY] * (2 * blocks + 1),
        [((features, wide), NARROW), ((features, features), NARROW), ((padded, features), NARROW),
         ((count, features), SINGLE), ((count, features), NARROW), ((count, features), NARROW),
         ((16, count), SINGLE), ((count, 2 * PAIR), SINGLE), ((count, wide), NARROW),
         ((8, features), SINGLE), ((16, features), SINGLE)],
        count * square * 16,
        semaphores=2 * blocks + 1,
        lazy=(2, 3, 4, 5),
    )
    rest = (
        x3[None],
        own_columns(q3)[None],
        grad_x[None],
        own_columns(grad_q)[None],
    )
    if carried:
        norms = Norms(norms)
        causal_weight = Reduction(causal_weight, 1)
        sums = [
            up_x, down_x, reverse_weight, window_weight, kv_weight, share_weight, up_q, down_q,
            causal_weight,
        ]
        grads = finale(
            functools.partial(assemble, len(sums), blocks),
            [
                like(4, share, wide), like(4, share, features), like(2, share, hidden),
                like(2, hidden_share, features),
                like(6, share, kind=SINGLE), like(6, share, kind=SINGLE),
            ],
            [
                [
                    (causal_weight, "core"), (norms, "out"), (kv_weight, "x"), (share_weight, "y"),
                    (window_weight, "z"), (up_x, "back_x"), (down_x, "back_x"),
                    (reverse_weight, "back_x"),
                ],
                [
                    (causal_weight, "x"), (norms, "back"), (kv_weight, "z"), (share_weight, "z"),
                    (up_x, "back_core"), (down_x, "back_core"), (reverse_weight, "back_core"),
                    (window_weight, "back_x"),
                ],
                [
                    (causal_weight, "back_x"), (kv_weight, "back_x"), (share_weight, "back_x"),
                    (window_weight, "back_core"),
                ],
                [
                    (causal_weight, "back_core"), (kv_weight, "back_core"),
                    (share_weight, "back_core"),
                ],
            ],
            lambda: sum([one.result for one in sums], []) + norms.result,
            [like(share, 4 * features), like(share, causal_columns)],
            courier.ident + 1,
        )
        return rest + (grads[4], grads[5]) + tuple(one.astype(SINGLE) for one in grads[:4])
    up_x, down_x, reverse_weight, window_weight, kv_weight, share_weight = (
        reduce_all(one) for one in (up_x, down_x, reverse_grad, window_grad, kv_grad, share_grad)
    )
    up_q, down_q = reduce_rep(up_q[:share]), reduce_rep(down_q[:hidden_share])
    causal_weight = reduce_rep(causal_weight[:share])
    norms = own_columns(lax.psum(norms, ("blk", "rep")))
    gains, biases = norms[:6], norms[8:14]
    grad_attn_in = jnp.stack(
        (
            window_weight[:, :wide],
            causal_weight[:, :wide],
            jnp.concatenate((share_weight[:, :features], kv_weight), axis=1),
            jnp.concatenate((reverse_weight[:, :features], share_weight[:, features:]), axis=1),
        )
    )
    grad_attn_out = jnp.stack(
        (
            window_weight[:, wide:],
            causal_weight[:, wide : wide + features],
            causal_weight[:, wide + features : last],
            reverse_weight[:, features:],
        )
    )
    return rest + (
        gains,
        biases,
        grad_attn_in.astype(SINGLE),
        grad_attn_out.astype(SINGLE),
        jnp.stack((up_x, up_q)).astype(SINGLE),
        jnp.stack((down_x, down_q)).astype(SINGLE),
    )


def solution(mesh):
    placed = (
        P("rep", "blk", None),
        P("rep", None, None),
        P("rep", "blk"),
        P("rep"),
        P(),
        P(),
        P(),
        P(),
        P(),
        P(),
        P("rep", "blk", None),
        P("rep", None, None),
    )
    return jax.shard_map(
        body,
        mesh=mesh,
        in_specs=placed,
        out_specs=(
            P("rep", "blk", None),
            P("rep", None, "blk"),
            P("rep", "blk", None),
            P("rep", None, "blk"),
            P(None, "blk"),
            P(None, "blk"),
            P(None, "blk", None),
            P(None, "blk", None),
            P(None, "blk", None),
            P(None, "blk", None),
        ),
        check_vma=False,
    )
```

```python
import functools
import math

import jax
import jax.numpy as jnp
from jax import lax
from jax.experimental import pallas as pl
from jax.experimental.pallas import tpu as pltpu
from jax.sharding import PartitionSpec as P

HEADS = 12
WIN = 64
EPSILON = 1e-05
MASKED = -1e30
NARROW = jnp.bfloat16
SINGLE = jnp.float32
GROUP = 256
WINDOWS = 256
PAIR = 128
HEAD = 64
STRIP = 400
LONG = 400
CHUNK = 768


def dot(former, latter, ahead, behind, precision=None):
    return lax.dot_general(
        former,
        latter,
        (((ahead,), (behind,)), ((), ())),
        preferred_element_type=SINGLE,
        precision=precision,
    )


def plain(former, latter):
    return dot(former, latter, 1, 0)


def right_t(former, latter):
    return dot(former, latter, 1, 1)


def left_t(former, latter):
    return dot(former, latter, 0, 0)


def loop(count, action):
    def step(index, nothing):
        action(index)
        return nothing

    lax.fori_loop(0, count, step, 0)


def at(index, size):
    return pl.ds(pl.multiple_of(index * size, size), size)


def iota(shape, dim):
    return lax.broadcasted_iota(jnp.int32, shape, dim)


def statistics(tensor):
    average = jnp.mean(tensor, axis=-1, keepdims=True)
    centred = tensor - average
    spread = jnp.mean(centred * centred, axis=-1, keepdims=True)
    return centred, lax.rsqrt(spread + EPSILON)


def norm(tensor, gain, bias):
    centred, inverse = statistics(tensor)
    return centred * inverse * gain + bias


def norm_back(tensor, gain, upstream):
    centred, inverse = statistics(tensor)
    scaled = centred * inverse
    inner = upstream * gain
    grad = inverse * (
        inner
        - jnp.mean(inner, axis=-1, keepdims=True)
        - scaled * jnp.mean(inner * scaled, axis=-1, keepdims=True)
    )
    return (
        grad,
        jnp.sum(upstream * scaled, axis=0, keepdims=True),
        jnp.sum(upstream, axis=0, keepdims=True),
    )


def gelu_both(tensor):
    size = jnp.abs(tensor)
    ratio = 1.0 / (1.0 + (0.3275911 * math.sqrt(0.5)) * size)
    series = ratio * (
        0.254829592
        + ratio * (-0.284496736 + ratio * (1.421413741 + ratio * (-1.453152027 + ratio * 1.061405429)))
    )
    bell = jnp.exp(-0.5 * (tensor * tensor))
    tail = 0.5 * series * bell
    below = jnp.where(tensor >= 0, 1.0 - tail, tail)
    return tensor * below, below + tensor * bell * (1.0 / math.sqrt(2.0 * math.pi))


def half(which, value=1.0):
    return jnp.where(iota((1, PAIR), 1) // HEAD == which, value, 0.0).astype(NARROW)


def lower_lanes():
    return iota((1, PAIR), 1) < HEAD


def both(tensor, value=1.0):
    return jnp.concatenate((tensor * half(0, value), tensor * half(1, value)), axis=0)


def attend(queries, keys, values, mask):
    rows = queries.shape[0]
    scores = right_t(both(queries, 1.0 / math.sqrt(HEAD)), keys)
    weights, totals, logs = [], [], []
    for which in range(2):
        part = mask(scores[which * rows : (which + 1) * rows])
        peak = jnp.max(part, axis=-1, keepdims=True)
        part = jnp.exp(part - peak)
        total = jnp.sum(part, axis=-1, keepdims=True)
        weights.append(part.astype(NARROW))
        totals.append(1.0 / total)
        logs.append(peak + jnp.log(total))
    out = plain(jnp.concatenate(weights, axis=0), values)
    return jnp.where(lower_lanes(), out[:rows] * totals[0], out[rows:] * totals[1]), logs


def attend_back(queries, keys, values, upstream, logs, deltas, mask):
    scaled = queries * jnp.asarray(1.0 / math.sqrt(HEAD), NARROW)
    count = keys.shape[0]
    keys = both(keys)
    turned_keys = keys.T
    scores = right_t(keys, scaled)
    inner = right_t(both(values), upstream)
    weights, slopes = [], []
    for which in range(2):
        span = slice(which * count, (which + 1) * count)
        part = mask(scores[span])
        if logs is None:
            part = jnp.exp(part - jnp.max(part, axis=0, keepdims=True))
            part = part * (1.0 / jnp.sum(part, axis=0, keepdims=True))
        else:
            part = jnp.exp(part - logs[which])
        weights.append(part.astype(NARROW))
        slopes.append((part * (inner[span] - deltas[which])).astype(NARROW))
    slope = jnp.concatenate(slopes, axis=0)
    query_grad = plain(turned_keys, slope).T
    key_grad = plain(slope, scaled)
    value_grad = plain(jnp.concatenate(weights, axis=0), upstream)
    lanes = lower_lanes()
    return (
        query_grad,
        jnp.where(lanes, key_grad[:count], key_grad[count:]),
        jnp.where(lanes, value_grad[:count], value_grad[count:]),
    )


def exact_parts(tensor, count):
    parts = []
    for _ in range(count):
        parts.append(tensor.astype(NARROW))
        tensor = tensor - parts[-1].astype(SINGLE)
    return parts


def head_rows(tensor):
    features = tensor.shape[1]
    heads = 16
    chosen = jnp.where(
        iota((heads, features), 1) // HEAD == iota((heads, features), 0), 1.0, 0.0
    ).astype(NARROW)
    return functools.reduce(jnp.add, [right_t(chosen, part) for part in exact_parts(tensor, 2)])


def turn(columns):
    same = jnp.where(iota((16, columns.shape[1]), 0) == iota((16, columns.shape[1]), 1), 1.0, 0.0)
    same = same.astype(NARROW)
    return functools.reduce(jnp.add, [right_t(same, part) for part in exact_parts(columns, 3)])


def row_pair(ref, pair, span):
    tensor = ref[:, span]
    index = iota(tensor.shape, 0)
    return [
        jnp.sum(jnp.where(index == 2 * pair + which, tensor, 0.0), axis=0, keepdims=True)
        for which in range(2)
    ]


def chooser(rows, width, start, count):
    row = iota((rows, width), 0)
    hit = jnp.logical_and(iota((rows, width), 1) == row + start, row < count)
    return jnp.where(hit, 1.0, 0.0).astype(NARROW)


def spans(rows, size):
    edges = [(start, min(start + size, rows)) for start in range(0, rows, size)]
    if len(edges) > 1 and edges[-1][1] - edges[-1][0] < PAIR:
        edges[-2:] = [(edges[-2][0], rows)]
    return edges


def mark(log_ref, rows, head, value):
    log_ref[rows, :] = jnp.where(iota((1, PAIR), 1) == head, value, log_ref[rows, :])


def store_rows(ref, columns, value):
    ref[(slice(None),) * (len(ref.shape) - 1) + (columns,)] = value.astype(ref.dtype).reshape(
        ref.shape[:-1] + value.shape[1:]
    )


def nothing(*unused):
    return None


def copies(semaphores, *pairs):
    made = [
        pltpu.make_async_copy(source, target, semaphores.at[k])
        for k, (source, target) in enumerate(pairs)
    ]
    for one in made:
        one.start()
    return made


DIRECT = 8


def place_of(axis="blk"):
    return lax.axis_index(axis)


def flipped(index, mask, count):
    total, weight = 0, 1
    while weight < count:
        bit = (index // weight) % 2
        total = total + weight * ((1 - bit) if mask & weight else bit)
        weight *= 2
    return total


def piece_at(number, count):
    return flipped(place_of(), number, count) if count <= DIRECT else number


def window_forward(
    x_ref, gain_ref, bias_ref, a_in, a_out,
    n0_ref, pw_ref, mw_ref, x1_ref, nx_ref, vq_ref, ckv_ref,
    w_in, w_out, w_q, w_kv, sem,
    flush=nothing,
):
    rows, features = x_ref.shape
    loads = copies(
        sem,
        (a_in.at[0], w_in),
        (a_out.at[0], w_out),
        (a_in.at[3, :, pl.ds(0, features)], w_q),
        (a_in.at[2, :, pl.ds(features, 2 * features)], w_kv),
    )

    def first(i):
        span = at(i, GROUP)
        n0_ref[span, :] = norm(
            x_ref[span, :].astype(SINGLE), gain_ref[0:1, :], bias_ref[0:1, :]
        ).astype(NARROW)

    loop(rows // GROUP, first)
    loads[0].wait()

    def project(j):
        span = at(j, CHUNK)
        pw_ref[:, span] = plain(n0_ref[...], w_in[:, span]).astype(NARROW)

    loop(3 * features // CHUNK, project)
    flush(0)
    flush(1)
    window = jnp.where(
        iota((WINDOWS, WINDOWS), 0) // WIN == iota((WINDOWS, WINDOWS), 1) // WIN, 0.0, MASKED
    )

    def group(i):
        span = at(i, WINDOWS)
        for pair in range(features // PAIR):
            lane = pair * PAIR
            out, unused = attend(
                pw_ref[span, lane : lane + PAIR],
                pw_ref[span, features + lane : features + lane + PAIR],
                pw_ref[span, 2 * features + lane : 2 * features + lane + PAIR],
                lambda scores: scores + window,
            )
            mw_ref[span, lane : lane + PAIR] = out.astype(NARROW)

    loop(rows // WINDOWS, group)
    flush(2)
    loads[1].wait()

    def second(i):
        span = at(i, GROUP)
        total = x_ref[span, :].astype(SINGLE) + plain(mw_ref[span, :], w_out[...])
        x1_ref[span, :] = total
        nx_ref[span, :] = norm(total, gain_ref[3:4, :], bias_ref[3:4, :]).astype(NARROW)

    loop(rows // GROUP, second)
    flush(3)
    flush(4)
    loads[2].wait()
    vq_ref[...] = plain(nx_ref[...], w_q[...]).astype(NARROW)
    flush(5)
    loads[3].wait()

    def third(j):
        span = at(j, CHUNK)
        ckv_ref[:, span] = plain(nx_ref[...], w_kv[:, span]).astype(NARROW)

    loop(2 * features // CHUNK, third)


def causal_forward(
    q_ref, gain_ref, bias_ref, a_in, a_out,
    n1_ref, pq_ref, mq_ref, q1_ref, nq_ref, cq_ref, vkv_ref, log_ref,
    w_in, w_out, w_q, w_kv, logs, sem,
    flush=nothing,
):
    rows, features = q_ref.shape
    loads = copies(
        sem,
        (a_in.at[1], w_in),
        (a_out.at[1], w_out),
        (a_in.at[2, :, pl.ds(0, features)], w_q),
        (a_in.at[3, :, pl.ds(features, 2 * features)], w_kv),
    )

    def first(i):
        span = at(i, STRIP)
        n1_ref[span, :] = norm(
            q_ref[span, :].astype(SINGLE), gain_ref[1:2, :], bias_ref[1:2, :]
        ).astype(NARROW)

    loop(rows // STRIP, first)
    loads[0].wait()

    def project(j):
        span = at(j, CHUNK)
        pq_ref[:, span] = plain(n1_ref[...], w_in[:, span]).astype(NARROW)

    loop(3 * features // CHUNK, project)
    flush(0)
    flush(1)
    logs[...] = jnp.zeros_like(logs)

    def pair(p):
        for start in range(0, rows, LONG):
            end = min(start + LONG, rows)

            def mask(scores, start=start):
                shape = scores.shape
                return jnp.where(iota(shape, 1) <= iota(shape, 0) + start, scores, MASKED)

            out, sums = attend(
                pq_ref[start:end, at(p, PAIR)],
                pq_ref[0:end, at(p + features // PAIR, PAIR)],
                pq_ref[0:end, at(p + 2 * features // PAIR, PAIR)],
                mask,
            )
            mq_ref[start:end, at(p, PAIR)] = out.astype(NARROW)
            for which in range(2):
                mark(logs, slice(start, end), 2 * p + which, sums[which])

    loop(features // PAIR, pair)
    flush(2)
    log_ref[...] = turn(logs[...])
    loads[1].wait()

    def second(i):
        span = at(i, STRIP)
        total = q_ref[span, :].astype(SINGLE) + plain(mq_ref[span, :], w_out[...])
        q1_ref[span, :] = total
        nq_ref[span, :] = norm(total, gain_ref[2:3, :], bias_ref[2:3, :]).astype(NARROW)

    loop(rows // STRIP, second)
    if q1_ref.shape[0] > rows:
        q1_ref[rows:, :] = jnp.zeros_like(q1_ref[rows:, :])
        nq_ref[rows:, :] = jnp.zeros_like(nq_ref[rows:, :])
    flush(3)
    flush(4)
    loads[2].wait()
    cq_ref[...] = plain(nq_ref[0:rows, :], w_q[...]).astype(NARROW)
    flush(5)
    loads[3].wait()

    def third(j):
        span = at(j, CHUNK)
        vkv_ref[:, span] = plain(nq_ref[0:rows, :], w_kv[:, span]).astype(NARROW)

    loop(2 * features // CHUNK, third)


def cross_forward(pieces, cq_ref, ckv_ref, valid_ref, whole, *rest):
    log_refs, (logs,) = rest[:pieces], rest[pieces:]
    rows, features = cq_ref.shape
    part = log_refs[0].shape[1]
    logs[...] = jnp.zeros_like(logs)
    if whole.shape[0] > rows:
        whole[rows:, :] = jnp.zeros((whole.shape[0] - rows, features), NARROW)

    def pair(p):
        for start in range(0, rows, LONG):
            span = slice(start, min(start + LONG, rows))
            out, sums = attend(
                cq_ref[span, at(p, PAIR)],
                ckv_ref[:, at(p, PAIR)],
                ckv_ref[:, at(p + features // PAIR, PAIR)],
                lambda scores: scores + valid_ref[...],
            )
            whole[span, at(p, PAIR)] = out.astype(NARROW)
            for which in range(2):
                mark(logs, span, 2 * p + which, sums[which])

    loop(features // PAIR, pair)
    for k in range(pieces):
        log_refs[k][...] = turn(logs[at(piece_at(k, pieces), part), :])


def untwist(rows):
    same = jnp.where(iota((16, PAIR), 0) == iota((16, PAIR), 1), 1.0, 0.0).astype(NARROW)
    return functools.reduce(jnp.add, [left_t(part, same) for part in exact_parts(rows, 3)])


def merge_blocks(pieces, own_ref, *refs):
    logs, refs = refs[:pieces], refs[pieces:]
    halves, (co_ref, log_ref) = (refs[: pieces - 1], refs[pieces - 1 : -2]), refs[-2:]
    part, features = co_ref.shape
    width = features // 2
    peak = functools.reduce(jnp.maximum, [one[...] for one in logs])
    total = peak + jnp.log(functools.reduce(jnp.add, [jnp.exp(one[...] - peak) for one in logs]))
    log_ref[...] = total
    spread = jnp.where(
        iota((PAIR, features), 1) // HEAD == iota((PAIR, features), 0), 1.0, 0.0
    ).astype(NARROW)
    result = jnp.zeros(co_ref.shape, SINGLE)
    for k in range(pieces):
        weight = untwist(jnp.exp(logs[k][...] - total))
        high = weight.astype(NARROW)
        low = (weight - high.astype(SINGLE)).astype(NARROW)
        if k == 0:
            block = own_ref[at(place_of(), part), :]
        else:
            block = jnp.concatenate((halves[0][k - 1][...], halves[1][k - 1][...]), axis=1)
        result = result + (plain(high, spread) + plain(low, spread)) * block.astype(SINGLE)
    co_ref[...] = result.astype(NARROW)


def reverse_forward(
    length_ref, vq_ref, vkv_ref, x1_ref, a_out,
    mv_ref, x2_ref, log_ref,
    w_out, logs, sem,
    ready=nothing, flush=nothing,
):
    rows, features = vq_ref.shape
    keys = vkv_ref.shape[0]
    (load,) = copies(sem, (a_out.at[3], w_out))
    logs[...] = jnp.zeros_like(logs)
    bias = jnp.where(iota((1, keys), 1) < length_ref[0], 0.0, MASKED)

    def pair(p):
        for start in range(0, rows, WINDOWS):
            span = slice(start, start + WINDOWS)
            out, sums = attend(
                vq_ref[span, at(p, PAIR)],
                vkv_ref[:, at(p, PAIR)],
                vkv_ref[:, at(p + features // PAIR, PAIR)],
                lambda scores: scores + bias,
            )
            mv_ref[span, at(p, PAIR)] = out.astype(NARROW)
            for which in range(2):
                mark(logs, span, 2 * p + which, sums[which])

    loop(features // PAIR, pair)
    flush(0)
    log_ref[...] = turn(logs[...])
    load.wait()
    ready(3)

    def second(i):
        span = at(i, GROUP)
        x2_ref[span, :] = x1_ref[span, :] + plain(mv_ref[span, :], w_out[...])

    loop(rows // GROUP, second)


def feed_forward_step(block, normed, up, down, cot, hidden, slope, out, grad):
    rows = normed.shape[0]

    def strip(i):
        span = at(i, block)
        value, rise = gelu_both(plain(normed[span, :], up[...]))
        hidden[span, :] = value.astype(NARROW)
        slope[span, :] = (right_t(cot[span, :], down[...]) * rise).astype(NARROW)
        out[span, :] += plain(hidden[span, :], down[...])
        grad[span, :] += right_t(slope[span, :], up[...])

    loop(rows // block, strip)


def patch_feed_forward(
    x2_ref, cot_ref, gain_ref, bias_ref, up_ref, down_ref,
    x3_ref, dx2_ref, up_grad_ref, down_grad_ref, norm_ref,
    normed, hidden, slope, out, grad,
):
    rows = x2_ref.shape[0]
    step = pl.program_id(0)

    @pl.when(step == 0)
    def begin():
        def first(i):
            span = at(i, GROUP)
            normed[span, :] = norm(
                x2_ref[span, :], gain_ref[5:6, :], bias_ref[5:6, :]
            ).astype(NARROW)
            out[span, :] = x2_ref[span, :]
            grad[span, :] = jnp.zeros_like(grad[span, :])

        loop(rows // GROUP, first)

    feed_forward_step(
        512, normed, up_ref.at[0], down_ref.at[0], cot_ref, hidden, slope, out, grad
    )
    up_grad_ref[...] = left_t(normed[...], slope[...]).astype(NARROW)
    down_grad_ref[...] = left_t(hidden[...], cot_ref[...]).astype(NARROW)

    @pl.when(step == pl.num_programs(0) - 1)
    def finish():
        norm_ref[...] = jnp.zeros_like(norm_ref)

        def last(i):
            span = at(i, GROUP)
            x3_ref[span, :] = out[span, :].astype(NARROW)
            part, gain, bias = norm_back(x2_ref[span, :], gain_ref[5:6, :], grad[span, :])
            dx2_ref[span, :] = cot_ref[span, :].astype(SINGLE) + part
            norm_ref[0:1, :] += gain
            norm_ref[1:2, :] += bias

        loop(rows // GROUP, last)


def place_parts(ref, pieces, parts, sem):
    part, features = parts[0].shape
    width = features // 2
    pairs = [(parts[0], ref.at[at(piece_at(0, pieces), part), :])]
    for number in range(2):
        for k in range(1, pieces):
            pairs.append(
                (
                    parts[number * (pieces - 1) + k],
                    ref.at[at(piece_at(k, pieces), part), pl.ds(number * width, width)],
                )
            )
    return copies(sem, *pairs)


def query_feed_forward(
    pieces, share, hidden_share, q1_ref, cot_ref, gain_ref, bias_ref,
    w_out, up_ref, down_ref, *rest,
):
    parts, rest = rest[: 2 * pieces - 1], rest[2 * pieces - 1 :]
    (
        q3_ref, dq2_ref, up_grad_ref, down_grad_ref, norm_ref, co_ref,
        q2, normed, chosen, hidden, slope, out, grad, sem,
    ) = rest
    rows, features = cot_ref.shape
    width = up_ref.shape[2]
    step = pl.program_id(0)

    @pl.when(step == 0)
    def begin():
        for one in place_parts(co_ref, pieces, parts, sem):
            one.wait()

        def first(i):
            span = at(i, STRIP)
            total = q1_ref[span, :] + plain(co_ref[span, :], w_out[0])
            q2[span, :] = total
            out[span, :] = total
            normed[span, :] = norm(total, gain_ref[4:5, :], bias_ref[4:5, :]).astype(NARROW)
            grad[span, :] = jnp.zeros_like(grad[span, :])

        loop(rows // STRIP, first)
        chosen[...] = right_t(
            chooser(chosen.shape[0], features, place_of() * share, share), normed[...]
        ).astype(NARROW)

    feed_forward_step(
        rows, normed, up_ref.at[0], down_ref.at[0], cot_ref, hidden, slope, out, grad
    )
    up_grad_ref[...] = plain(chosen[...], slope[...]).astype(NARROW)
    begins = place_of() * hidden_share

    @pl.when(begins // width == step)
    def own_hidden():
        taken = right_t(
            chooser(down_grad_ref.shape[0], width, begins - step * width, hidden_share),
            hidden[...],
        ).astype(NARROW)
        down_grad_ref[...] = plain(taken, cot_ref[...]).astype(NARROW)

    @pl.when(step == pl.num_programs(0) - 1)
    def finish():
        norm_ref[...] = jnp.zeros_like(norm_ref)

        def last(i):
            span = at(i, STRIP)
            picked = chooser(chosen.shape[0], features, place_of() * share, share)
            q3_ref[span, :] = right_t(out[span, :].astype(NARROW), picked)[:, :share].astype(NARROW)
            piece, gain, bias = norm_back(q2[span, :], gain_ref[4:5, :], grad[span, :])
            dq2_ref[span, :] = cot_ref[span, :].astype(SINGLE) + piece
            norm_ref[0:1, :] += gain
            norm_ref[1:2, :] += bias

        loop(rows // STRIP, last)


def reverse_backward(
    pieces, length_ref, dx2_ref, mv_ref, vq_ref, vkv_ref, nx_ref, log_ref, a_out,
    *rest, launch=nothing, tick=nothing, ready=nothing,
):
    dvq_ref, weight_ref, rest = rest[0], rest[1], rest[2:]
    k_refs, v_refs, rest = rest[:pieces], rest[pieces : 2 * pieces], rest[2 * pieces :]
    w_out, rounded, dmv, deltas, dkv, sem = rest
    rows, features = vq_ref.shape
    keys = vkv_ref.shape[0]
    part = k_refs[0].shape[0]
    (load,) = copies(sem, (a_out.at[3], w_out))
    rounded[...] = dx2_ref[...].astype(NARROW)
    load.wait()
    dmv[...] = right_t(rounded[...], w_out[...]).astype(NARROW)
    store_rows(
        weight_ref, slice(features, 2 * features), left_t(mv_ref[...], rounded[...])
    )
    deltas[...] = head_rows(dmv[...].astype(SINGLE) * mv_ref[...].astype(SINGLE))
    if dkv.shape[0] > keys:
        dkv[keys:, :] = jnp.zeros((dkv.shape[0] - keys, 2 * features), SINGLE)
    size = 256
    for k in (3, 4, 6):
        ready(k)

    def pair(p):
        pl.when(p == 2)(lambda: tick(1))
        pl.when(p == 4)(lambda: tick(2))
        for strip in range(rows // size):
            span = slice(strip * size, (strip + 1) * size)

            def mask(scores):
                return jnp.where(iota(scores.shape, 0) < length_ref[0], scores, MASKED)

            dq, dk, dv = attend_back(
                vq_ref[span, at(p, PAIR)],
                vkv_ref[:, at(p, PAIR)],
                vkv_ref[:, at(p + features // PAIR, PAIR)],
                dmv[span, at(p, PAIR)],
                row_pair(log_ref, p, span),
                row_pair(deltas, p, span),
                mask,
            )
            dvq_ref[span, at(p, PAIR)] = (dq * (1.0 / math.sqrt(HEAD))).astype(NARROW)
            if strip == 0:
                dkv[0:keys, at(p, PAIR)] = dk
                dkv[0:keys, at(p + features // PAIR, PAIR)] = dv
            else:
                dkv[0:keys, at(p, PAIR)] += dk
                dkv[0:keys, at(p + features // PAIR, PAIR)] += dv

    loop(features // PAIR, pair)
    ready(5)
    store_rows(weight_ref, slice(0, features), left_t(nx_ref[...], dvq_ref[...]))
    launch(1)
    for k in range(pieces):
        span = at(piece_at(k, pieces), part)
        width = k_refs[k].shape[1]
        k_refs[k][...] = dkv[span, 0:width].astype(NARROW)
        v_refs[k][...] = dkv[span, width:].astype(NARROW)


def cross_backward(
    pieces, share, dq2_ref, co_ref, cq_ref, ckv_ref, valid_ref, a_out, *rest, ready=nothing
):
    log_parts, rest = rest[:pieces], rest[pieces:]
    dckv_ref, weight_ref, rest = rest[0], rest[1], rest[2:]
    q_refs, (w_out, rounded, dco, deltas, logs, turned, dq_all, dkv, sem) = (
        rest[:pieces],
        rest[pieces:],
    )
    rows, features = cq_ref.shape
    part = log_parts[0].shape[1]
    (load,) = copies(sem, (a_out.at[2], w_out))
    for k in range(pieces):
        logs[at(piece_at(k, pieces), part), :] = untwist(log_parts[k][...])
    turned[...] = turn(logs[0:rows, :])
    rounded[...] = dq2_ref[...].astype(NARROW)
    load.wait()
    dco[...] = right_t(rounded[...], w_out[...]).astype(NARROW)
    taken = right_t(
        chooser(weight_ref.shape[0], features, place_of() * share, share), co_ref[0:rows, :]
    ).astype(NARROW)
    weight_ref[...] = plain(taken, rounded[...]).astype(NARROW)
    deltas[...] = head_rows(dco[...].astype(SINGLE) * co_ref[0:rows, :].astype(SINGLE))
    if dq_all.shape[0] > rows:
        dq_all[rows:, :] = jnp.zeros((dq_all.shape[0] - rows, features), NARROW)
    edges = spans(rows, 512)
    keys = valid_ref.shape[1]
    valid = jnp.broadcast_to(valid_ref[...], (PAIR, keys)).T[:, 0:1]
    ready(2)
    ready(3)

    def pair(p):
        for number, (start, end) in enumerate(edges):
            span = slice(start, end)
            dq, dk, dv = attend_back(
                cq_ref[span, at(p, PAIR)],
                ckv_ref[:, at(p, PAIR)],
                ckv_ref[:, at(p + features // PAIR, PAIR)],
                dco[span, at(p, PAIR)],
                row_pair(turned, p, span),
                row_pair(deltas, p, span),
                lambda scores: scores + valid,
            )
            dq_all[span, at(p, PAIR)] = (dq * (1.0 / math.sqrt(HEAD))).astype(NARROW)
            if number == 0:
                dkv[:, at(p, PAIR)] = dk
                dkv[:, at(p + features // PAIR, PAIR)] = dv
            else:
                dkv[:, at(p, PAIR)] += dk
                dkv[:, at(p + features // PAIR, PAIR)] += dv

    loop(features // PAIR, pair)
    dckv_ref[...] = dkv[...].astype(NARROW)
    for k in range(pieces):
        q_refs[k][...] = dq_all[at(piece_at(k, pieces), part), :]


def patch_backward(
    x_ref, dx2_ref, x1_ref, nx_ref, n0_ref, pw_ref, mw_ref, dvq_ref, dckv_ref, gain_ref, a_in, a_out,
    kv_weight_ref, weight_ref, grad_ref, norm_ref,
    w_in, w_out, w_q, w_kv, dx1, rounded, dmw, deltas, dpw, sem,
    launch=nothing, ready=nothing, flush=nothing,
):
    rows, features = x_ref.shape
    loads = copies(
        sem,
        (a_in.at[3, :, pl.ds(0, features)], w_q),
        (a_in.at[2, :, pl.ds(features, 2 * features)], w_kv),
        (a_out.at[0], w_out),
        (a_in.at[0], w_in),
    )
    norm_ref[...] = jnp.zeros_like(norm_ref)
    for start in range(0, 2 * features, CHUNK):
        span = slice(start, start + CHUNK)
        store_rows(kv_weight_ref, span, left_t(nx_ref[...], dckv_ref[:, span]))
    launch(0)
    flush(0)
    loads[0].wait()
    loads[1].wait()

    def first(i):
        span = at(i, GROUP)
        upstream = right_t(dvq_ref[span, :], w_q[...]) + right_t(dckv_ref[span, :], w_kv[...])
        part, gain, bias = norm_back(x1_ref[span, :], gain_ref[3:4, :], upstream)
        total = dx2_ref[span, :] + part
        dx1[span, :] = total
        rounded[span, :] = total.astype(NARROW)
        norm_ref[0:1, :] += gain
        norm_ref[1:2, :] += bias

    loop(rows // GROUP, first)
    loads[2].wait()
    ready(6)
    dmw[...] = right_t(rounded[...], w_out[...]).astype(NARROW)
    store_rows(
        weight_ref, slice(3 * features, 4 * features), left_t(mw_ref[...], rounded[...])
    )
    deltas[...] = head_rows(dmw[...].astype(SINGLE) * mw_ref[...].astype(SINGLE))
    ready(5)
    window = jnp.where(
        iota((WINDOWS, WINDOWS), 0) // WIN == iota((WINDOWS, WINDOWS), 1) // WIN, 0.0, MASKED
    )

    def group(i):
        span = at(i, WINDOWS)
        for pair in range(features // PAIR):
            lane = pair * PAIR
            dq, dk, dv = attend_back(
                pw_ref[span, lane : lane + PAIR],
                pw_ref[span, features + lane : features + lane + PAIR],
                pw_ref[span, 2 * features + lane : 2 * features + lane + PAIR],
                dmw[span, lane : lane + PAIR],
                None,
                [deltas[2 * pair + w : 2 * pair + w + 1, span] for w in range(2)],
                lambda scores: scores + window,
            )
            dpw[span, lane : lane + PAIR] = (dq * (1.0 / math.sqrt(HEAD))).astype(NARROW)
            dpw[span, features + lane : features + lane + PAIR] = dk.astype(NARROW)
            dpw[span, 2 * features + lane : 2 * features + lane + PAIR] = dv.astype(NARROW)

    loop(rows // WINDOWS, group)
    ready(4)
    for start in range(0, 3 * features, CHUNK):
        span = slice(start, start + CHUNK)
        store_rows(weight_ref, span, left_t(n0_ref[...], dpw[:, span]))
    launch(1)
    flush(1)
    ready(0)
    loads[3].wait()

    def last(i):
        span = at(i, GROUP)
        upstream = right_t(dpw[span, :], w_in[...])
        part, gain, bias = norm_back(x_ref[span, :].astype(SINGLE), gain_ref[0:1, :], upstream)
        grad_ref[span, :] = dx1[span, :] + part
        norm_ref[2:3, :] += gain
        norm_ref[3:4, :] += bias

    loop(rows // GROUP, last)


def share_backward(
    pieces, q1, nq, gain_ref, a_in, *rest, launch=nothing
):
    parts = [rest[k * pieces : (k + 1) * pieces] for k in range(3)]
    rest = rest[3 * pieces :]
    grad_ref, weight_ref, norm_ref, w_q, w_kv, summed, q1_ref, nq_ref, sem = rest
    part, features = q1_ref.shape
    *loads, load_q, load_n = copies(
        sem,
        (a_in.at[2, :, pl.ds(0, features)], w_q),
        (a_in.at[3, :, pl.ds(features, 2 * features)], w_kv),
        (q1.at[at(place_of(), part), :], q1_ref),
        (nq.at[at(place_of(), part), :], nq_ref),
    )
    start = 0
    for k in range(3):
        width = parts[k][0].shape[1]
        total = functools.reduce(jnp.add, [one[...].astype(SINGLE) for one in parts[k]])
        summed[:, start : start + width] = total.astype(NARROW)
        start += width
    for load in loads:
        load.wait()
    upstream = right_t(summed[:, 0:features], w_q[...]) + right_t(summed[:, features:], w_kv[...])
    load_q.wait()
    piece, gain, bias = norm_back(q1_ref[...], gain_ref[2:3, :], upstream)
    grad_ref[...] = piece.astype(NARROW)
    launch(0)
    load_n.wait()
    for k in range(3):
        span = slice(k * features, (k + 1) * features)
        store_rows(weight_ref, span, left_t(nq_ref[...], summed[:, span]))
    launch(1)
    norm_ref[...] = jnp.zeros_like(norm_ref)
    norm_ref[0:1, :] = gain
    norm_ref[1:2, :] = bias


def causal_backward(
    pieces, share, q_ref, dq2_ref, n1_ref, pq_ref, mq_ref, log_ref, cross_ref, gain_ref,
    norm_x, norm_two, norm_four, norm_five, a_in, a_out, *rest, ready=nothing
):
    parts, rest = rest[: 2 * pieces - 1], rest[2 * pieces - 1 :]
    (
        weight_ref, grad_ref, norm_ref,
        w_in, w_out, gathered, dq1, rounded, dmq, deltas, dkv, dpq, norm_one, norm_all, sem,
    ) = rest
    rows, features = q_ref.shape
    placed = place_parts(gathered, pieces, parts, sem)
    loads = copies(sem.at[pl.ds(len(placed), 2)], (a_out.at[1], w_out), (a_in.at[1], w_in))
    for one in placed:
        one.wait()

    def first(i):
        span = at(i, STRIP)
        total = dq2_ref[span, :] + gathered[span, :].astype(SINGLE)
        dq1[span, :] = total
        rounded[span, :] = total.astype(NARROW)

    loop(rows // STRIP, first)
    loads[0].wait()
    dmq[...] = right_t(rounded[...], w_out[...]).astype(NARROW)
    ready(4)
    chosen = chooser(weight_ref.shape[0], features, place_of() * share, share)
    taken = right_t(chosen, mq_ref[...]).astype(NARROW)
    weight_ref[:, 3 * features : 4 * features] = plain(taken, rounded[...]).astype(NARROW)
    weight_ref[:, 4 * features : 5 * features] = cross_ref[...]
    weight_ref[:, 5 * features :] = jnp.zeros_like(weight_ref[:, 5 * features :])
    deltas[...] = head_rows(dmq[...].astype(SINGLE) * mq_ref[...].astype(SINGLE))
    edges = spans(rows, 256)
    ready(3)
    ready(5)

    def pair(p):
        for number, (start, end) in reversed(list(enumerate(edges))):
            span = slice(start, end)

            def mask(scores, start=start):
                shape = scores.shape
                return jnp.where(iota(shape, 0) <= iota(shape, 1) + start, scores, MASKED)

            dq, dk, dv = attend_back(
                pq_ref[span, at(p, PAIR)],
                pq_ref[0:end, at(p + features // PAIR, PAIR)],
                pq_ref[0:end, at(p + 2 * features // PAIR, PAIR)],
                dmq[span, at(p, PAIR)],
                row_pair(log_ref, p, span),
                row_pair(deltas, p, span),
                mask,
            )
            dpq[span, at(p, PAIR)] = (dq * (1.0 / math.sqrt(HEAD))).astype(NARROW)
            if end == rows:
                dkv[0:end, 0:PAIR] = dk
                dkv[0:end, PAIR:] = dv
            else:
                dkv[0:end, 0:PAIR] += dk
                dkv[0:end, PAIR:] += dv
        dpq[:, at(p + features // PAIR, PAIR)] = dkv[:, 0:PAIR].astype(NARROW)
        dpq[:, at(p + 2 * features // PAIR, PAIR)] = dkv[:, PAIR:].astype(NARROW)

    loop(features // PAIR, pair)
    ready(2)
    taken = right_t(chosen, n1_ref[...]).astype(NARROW)
    weight_ref[:, 0 : 3 * features] = plain(taken, dpq[...]).astype(NARROW)
    loads[1].wait()
    norm_one[...] = jnp.zeros_like(norm_one)

    def last(i):
        span = at(i, STRIP)
        upstream = right_t(dpq[span, :], w_in[...])
        piece, gain, bias = norm_back(q_ref[span, :].astype(SINGLE), gain_ref[1:2, :], upstream)
        parts = [right_t(part, chosen) for part in exact_parts(dq1[span, :] + piece, 3)]
        grad_ref[span, :] = functools.reduce(jnp.add, parts)[:, :share]
        norm_one[0:1, :] += gain
        norm_one[1:2, :] += bias

    loop(rows // STRIP, last)
    leader = jnp.where(place_of() == 0, 1.0, 0.0)
    norm_all[...] = jnp.zeros_like(norm_all)
    for row, (ref, source, scale) in enumerate(
        (
            (norm_x, 2, 1.0), (norm_one, 0, leader), (norm_two, 0, 1.0), (norm_x, 0, 1.0),
            (norm_four, 0, leader), (norm_five, 0, 1.0),
        )
    ):
        norm_all[row : row + 1, :] = ref[source : source + 1, :] * scale
        norm_all[8 + row : 9 + row, :] = ref[source + 1 : source + 2, :] * scale
    if len(norm_ref.shape) == 2:
        norm_ref[...] = norm_all[...]
    else:
        norm_ref[...] = jnp.zeros_like(norm_ref)
        for owner in range(norm_ref.shape[0]):
            norm_ref[owner, :, 0:share] = norm_all[:, owner * share : (owner + 1) * share]


def assemble(groups, count, *refs, ready=nothing, flush=nothing):
    parts, refs = refs[: 4 * groups], refs[4 * groups :]
    norms, refs = refs[:count], refs[count:]
    in_ref, out_ref, up_ref, down_ref, gain_ref, bias_ref, share, causal = refs
    features = down_ref.shape[2]
    rep = place_of("rep")

    def corners(number, write):
        for k in range(4):
            ready(4 * number + k)
            owner = flipped(rep, k, 4)
            piece = parts[4 * number + k][...]
            height, width = piece.shape[-2:]
            piece = piece.reshape(height, width)
            write(
                pl.ds(pl.multiple_of((owner % 2) * height, height), height),
                pl.multiple_of((owner // 2) * width, width), width, piece,
            )

    def into(ref, index, start=0):
        def write(rows, column, width, piece):
            ref[index, rows, pl.ds(column + start, width)] = piece

        return write

    up_x, down_x, reverse, window, kv, shared, up_q, down_q, rest = range(groups)

    def keep_causal(rows, column, width, piece):
        causal[rows, pl.ds(column, width)] = piece

    def keep_share(rows, column, width, piece):
        share[rows, pl.ds(column, width)] = piece

    corners(up_q, into(up_ref, 1))
    corners(down_q, into(down_ref, 1))
    corners(up_x, into(up_ref, 0))
    flush(2)
    corners(down_x, into(down_ref, 0))
    flush(3)
    first = 4 * groups
    for k in range(count):
        ready(first + k)
    terms = [norms[0][place_of()]] + [one[...] for one in norms[1:]]
    total = functools.reduce(jnp.add, terms)
    columns = gain_ref.shape[1]
    gain_ref[...] = total[0:6, 0:columns]
    bias_ref[...] = total[8:14, 0:columns]
    flush(4)
    flush(5)
    corners(reverse, keep_share)
    in_ref[3, :, 0:features] = share[:, 0:features]
    out_ref[3, :, :] = share[:, features : 2 * features]
    corners(window, keep_share)
    in_ref[0, :, :] = share[:, 0 : 3 * features]
    out_ref[0, :, :] = share[:, 3 * features :]
    corners(rest, keep_causal)
    in_ref[1, :, :] = causal[:, 0 : 3 * features]
    out_ref[1, :, :] = causal[:, 3 * features : 4 * features]
    out_ref[2, :, :] = causal[:, 4 * features : 5 * features]
    flush(1)
    corners(kv, into(in_ref, 2, features))
    corners(shared, keep_share)
    in_ref[2, :, 0:features] = share[:, 0:features]
    in_ref[3, :, features:] = share[:, features : 3 * features]
    flush(0)


def bits_of(count):
    return max(count - 1, 0).bit_length()


def swap(tensor, axis, mask):
    return lax.ppermute(tensor, axis, [(i, i ^ mask) for i in range(lax.axis_size(axis))])


def pick(tensor, place, dim):
    return lax.dynamic_index_in_dim(tensor, place, dim, keepdims=False)


def fold(tensor, axis, bit, dim):
    own = (lax.axis_index(axis) >> bit) & 1
    arrived = swap(pick(tensor, 1 - own, dim).astype(NARROW), axis, 1 << bit)
    return pick(tensor, own, dim).astype(SINGLE) + arrived.astype(SINGLE)


def unfold(tensor, axis, bit, dim):
    own = (lax.axis_index(axis) >> bit) & 1
    arrived = swap(tensor, axis, 1 << bit)
    return jnp.where(
        own == 0,
        jnp.stack((tensor, arrived), axis=dim),
        jnp.stack((arrived, tensor), axis=dim),
    )


def scatter_blk(tensor):
    bits = bits_of(lax.axis_size("blk"))
    tensor = tensor.reshape((2,) * bits + tensor.shape[1:])
    for bit in range(bits):
        tensor = fold(tensor, "blk", bit, bits - 1 - bit)
    return tensor


def sum_rep_scatter(tensor, dim):
    bits = bits_of(lax.axis_size("rep"))
    shape = tensor.shape
    tensor = tensor.reshape(
        shape[:dim] + (2,) * bits + (shape[dim] // 2**bits,) + shape[dim + 1 :]
    )
    for bit in range(bits):
        tensor = fold(tensor, "rep", bit, dim)
    return tensor


def gather_rep(tensor, dim):
    bits = bits_of(lax.axis_size("rep"))
    for bit in reversed(range(bits)):
        tensor = unfold(tensor, "rep", bit, dim)
    shape = tensor.shape
    return tensor.reshape(shape[:dim] + (-1,) + shape[dim + bits + 1 :])


def reduce_all(tensor):
    count = lax.axis_size("blk")
    tensor = tensor.reshape(count, tensor.shape[0] // count, tensor.shape[1])
    tensor = sum_rep_scatter(tensor, 1)
    tensor = scatter_blk(tensor).astype(NARROW)
    return gather_rep(tensor, 0)


def reduce_rep(tensor):
    return gather_rep(sum_rep_scatter(tensor, 0).astype(NARROW), 0)


def exchange(pieces):
    whole = lax.all_to_all(jnp.stack(pieces), "blk", 0, 0)
    return [whole[k] for k in range(len(pieces))]


def gather(tensor):
    count = lax.axis_size("blk")
    whole = lax.all_gather(tensor, "blk")
    return [whole[k] for k in range(count)]


def whole(ref):
    return ref


class Fold:
    def __init__(self, own, take, arrived, shape, keep=whole, keep_shape=None):
        self.own, self.take, self.arrived, self.shape = own, take, arrived, shape
        self.keep, self.keep_shape = keep, keep_shape or shape
        self.dtype = own.dtype


class Move:
    late = None

    def __init__(self, source, shape, axis, flip, take=whole, phase=0):
        self.source, self.shape, self.axis, self.flip, self.take = source, shape, axis, flip, take
        self.phase = phase
        self.dtype = source.dtype


def lanes_of(ref, start, width):
    return ref.at[(slice(None),) * (len(ref.shape) - 1) + (pl.ds(start, width),)]


class Reduction:
    def __init__(self, tensor, blocks=None):
        if blocks == 1:
            tensor = tensor.reshape(1, 1, 2, tensor.shape[0] // 2, tensor.shape[1])
        elif len(tensor.shape) == 2:
            blocks = lax.axis_size("blk")
            height = tensor.shape[0] // blocks
            tensor = tensor.reshape(blocks // 2, 2, 2, height // 2, tensor.shape[1])
        self.tensor, self.take, self.arrived, self.shape = tensor, whole, [], tensor.shape

    def fold(self, keep=whole, keep_shape=None):
        return Fold(self.tensor, self.take, self.arrived, self.shape, keep, keep_shape)

    def moves(self, stage):
        shape = self.shape
        if stage == "core":
            self.next = shape[:2] + shape[3:]
            return [
                Move(self.tensor, self.next, "rep", 1,
                     lambda ref: ref.at[:, :, 1 - place_of("rep") % 2])
            ]
        if stage == "x":
            width = shape[-1] // 2
            self.next = shape[:-1] + (width,)

            def own(ref):
                return lanes_of(ref, pl.multiple_of((place_of("rep") // 2) * width, width), width)

            def other(ref):
                start = (1 - place_of("rep") // 2) * width
                return lanes_of(ref, pl.multiple_of(start, width), width)

            return [Move(self.fold(own, self.next), self.next, "rep", 2, other)]
        if stage == "y":
            self.next = shape[:1] + shape[2:]
            fold = self.fold(lambda ref: ref.at[:, place_of() % 2], self.next)
            return [Move(fold, self.next, "blk", 1, lambda ref: ref.at[:, 1 - place_of() % 2])]
        if stage == "z":
            length = shape[0]
            self.next = shape[1:]
            fold = self.fold(lambda ref: ref.at[place_of() // 2], self.next)
            return [
                Move(fold, self.next, "blk", 2 * k,
                     lambda ref, k=k: ref.at[flipped(place_of() // 2, k, length)])
                for k in range(1, length)
            ]
        if stage == "back":
            fold = self.fold()
            return [Move(fold, shape, "rep", k) for k in range(1, 4)]
        if stage == "back_x":
            return [Move(self.fold(), shape, "rep", 2)]
        return [Move(self.tensor, shape, "rep", 1), Move(self.other, shape, "rep", 1)]

    def absorb(self, stage, arrived, kept):
        if stage == "core":
            self.take = lambda ref: ref.at[:, :, place_of("rep") % 2]
        else:
            self.take = whole
        if kept:
            self.tensor = kept[0]
        if stage in ("back", "back_x", "back_core"):
            if stage == "back_x":
                self.other = arrived[0]
                return
            if stage == "back":
                self.result = [self.tensor] + list(arrived)
            else:
                self.result = [self.tensor, arrived[0], self.other, arrived[1]]
            return
        self.shape, self.arrived = self.next, list(arrived)


class Exchange:
    def __init__(self, pieces):
        self.pieces = pieces

    def moves(self, stage):
        return [Move(one, one.shape, "blk", k) for k, one in enumerate(self.pieces) if k]

    def absorb(self, stage, arrived, kept):
        self.result = self.pieces[:1] + list(arrived)


class Pieces:
    def __init__(self, tensor, part, start, width):
        self.tensor, self.part, self.start, self.width = tensor, part, start, width

    def moves(self, stage):
        part, span = self.part, slice(self.start, self.start + self.width)
        count = lax.axis_size("blk")
        return [
            Move(self.tensor, (part, self.width), "blk", k,
                 lambda ref, k=k: ref.at[at(flipped(place_of(), k, count), part), span])
            for k in range(1, count)
        ]

    def absorb(self, stage, arrived, kept):
        self.result = list(arrived)


class Gather:
    def __init__(self, tensor):
        self.tensor = tensor

    def moves(self, stage):
        return [
            Move(self.tensor, self.tensor.shape, "blk", k) for k in range(1, lax.axis_size("blk"))
        ]

    def absorb(self, stage, arrived, kept):
        self.result = [self.tensor] + list(arrived)


class Spread:
    def __init__(self, tensor):
        self.tensor = tensor

    def moves(self, stage):
        count = lax.axis_size("blk")
        rows, width = self.tensor.shape[0], self.tensor.shape[1] // 2
        moves, self.places = [], []
        for number in range(2):
            span = slice(number * width, (number + 1) * width)
            own = lambda ref, span=span: ref.at[:, span]
            along = []
            for k in range(2, count, 2):
                along.append(Move(self.tensor, (rows, width), "blk", k, own, number))
                self.places.append((number, k))
            moves += along
            moves.append(Move(self.tensor, (rows, width), "blk", 1, own, number + 1))
            self.places.append((number, 1))
            for one in along:
                moves.append(Move(one, (rows, width), "blk", 1, whole, number + 1))
                self.places.append((number, one.flip + 1))
        return moves

    def absorb(self, stage, arrived, kept):
        found = dict(zip(self.places, arrived))
        count = lax.axis_size("blk")
        self.result = [found[number, k] for number in range(2) for k in range(1, count)]


class Norms:
    def __init__(self, tensor):
        self.tensor = tensor

    def moves(self, stage):
        axis = "rep" if stage == "out" else "blk"
        count = lax.axis_size(axis)
        shape = self.tensor.shape
        if stage == "out":
            return [Move(self.tensor, shape, axis, k) for k in range(1, count)]
        fold = Fold(self.tensor, whole, self.arrived, shape)
        return [
            Move(fold, shape[1:], axis, k,
                 lambda ref, k=k: ref.at[flipped(place_of(), k, count)])
            for k in range(1, count)
        ]

    def absorb(self, stage, arrived, kept):
        if stage == "out":
            self.arrived = list(arrived)
        else:
            self.result = [kept[0]] + list(arrived)


VMEM = pl.BlockSpec(memory_space=pltpu.VMEM)
SMEM = pl.BlockSpec(memory_space=pltpu.SMEM)
ANY = pl.BlockSpec(memory_space=pl.ANY)


def like(*shape, kind=NARROW):
    return jax.ShapeDtypeStruct(shape, kind)


def index_of(items, item):
    return next(k for k, one in enumerate(items) if one is item)


def call(
    kernel, outs, operands, specs, scratch, flops, grid=None, out_specs=None, semaphores=0,
    moves=(), ident=None, ticking=False, lazy=(), early=(),
):
    scratch = [pltpu.VMEM(shape, kind) for shape, kind in scratch]
    if semaphores:
        scratch.append(pltpu.SemaphoreType.DMA((semaphores,)))
    out_specs = [VMEM] * len(outs) if out_specs is None else out_specs
    extra = {} if grid is None else {"grid": grid}
    params = {}
    sources, folds = [], []

    def need(array):
        if not any(array is one for one in sources):
            sources.append(array)

    for move in moves:
        if isinstance(move.source, Fold):
            if not any(move.source is one for one in folds):
                folds.append(move.source)
                for array in [move.source.own] + move.source.arrived:
                    need(array)
        elif move.late is None and not isinstance(move.source, Move):
            need(move.source)
    fixed_in, fixed_out = len(operands), len(outs)
    partners = sorted({(move.axis, move.flip) for move in moves})
    lasts = max([move.phase for move in moves], default=0)
    held_in = [k for k, spec in enumerate(specs) if spec is VMEM]
    held_out = [k for k, spec in enumerate(out_specs) if spec is VMEM]
    own_scratch = len(scratch)
    scratch += [pltpu.VMEM(operands[k].shape, operands[k].dtype) for k in held_in]
    scratch += [pltpu.VMEM(outs[k].shape, outs[k].dtype) for k in held_out]
    terms = sum(1 + len(fold.arrived) for fold in folds)
    for fold in folds:
        scratch += [pltpu.VMEM(fold.shape, NARROW)] * (1 + len(fold.arrived))
    for number in (len(held_in), len(held_out), terms, len(folds), len(moves), len(moves)):
        scratch.append(pltpu.SemaphoreType.DMA((max(number, 1),)))
    if moves:
        params = {"collective_id": ident, "has_side_effects": True}
    before = {}
    for move in moves:
        if isinstance(move.source, Move):
            number = index_of(moves, move.source)
            before[number] = min(move.phase, before.get(number, move.phase))

    def body_kernel(*refs):
        ins, refs = list(refs[:fixed_in]), refs[fixed_in:]
        sent, refs = refs[: len(sources)], refs[len(sources) :]
        results, refs = list(refs[:fixed_out]), refs[fixed_out:]
        landed, refs = refs[: len(moves)], refs[len(moves) :]
        kept, refs = refs[: len(folds)], refs[len(folds) :]
        rest, refs = refs[:own_scratch], refs[own_scratch:]
        inner, refs = refs[: len(held_in)], refs[len(held_in) :]
        outer, refs = refs[: len(held_out)], refs[len(held_out) :]
        buffers, (in_sem, out_sem, load_sem, keep_sem, send_sem, recv_sem) = refs[:terms], refs[terms:]
        fetches, stores = {}, {}
        for number, k in enumerate(held_in):
            fetches[k] = pltpu.make_async_copy(ins[k], inner[number], in_sem.at[number])
            ins[k] = inner[number]
        for number, k in enumerate(held_out):
            stores[k] = pltpu.make_async_copy(outer[number], results[k], out_sem.at[number])
            results[k] = outer[number]

        def target(axis, flip):
            return {axis: flipped(lax.axis_index(axis), flip, lax.axis_size(axis))}

        def buffers_of(fold):
            start = sum(1 + len(one.arrived) for one in folds[: index_of(folds, fold)])
            return start, buffers[start : start + 1 + len(fold.arrived)]

        def made(k):
            move = moves[k]
            if move.late is not None:
                source = results[move.late]
            elif isinstance(move.source, Fold):
                source = buffers_of(move.source)[1][0]
            elif isinstance(move.source, Move):
                source = landed[index_of(moves, move.source)]
            else:
                source = sent[index_of(sources, move.source)]
            return pltpu.make_async_remote_copy(
                src_ref=move.take(source),
                dst_ref=landed[k],
                send_sem=send_sem.at[k],
                recv_sem=recv_sem.at[k],
                device_id=target(move.axis, move.flip),
                device_id_type=pl.DeviceIdType.MESH,
            )

        def loads(fold):
            start, held = buffers_of(fold)
            return [
                pltpu.make_async_copy(
                    (fold.take if k == 0 else whole)(sent[index_of(sources, array)]),
                    held[k],
                    load_sem.at[start + k],
                )
                for k, array in enumerate([fold.own] + fold.arrived)
            ]

        def keeping(k):
            fold = folds[k]
            return pltpu.make_async_copy(
                fold.keep(buffers_of(fold)[1][0]), kept[k], keep_sem.at[k]
            )

        def add(fold):
            held = buffers_of(fold)[1]

            def one(index):
                if len(held) == 2:
                    held[0][index] = held[0][index] + held[1][index]
                elif len(held) > 2:
                    held[0][index] = functools.reduce(
                        jnp.add, [part[index].astype(SINGLE) for part in held]
                    ).astype(NARROW)

            if len(fold.shape) == 2:
                one((slice(None), slice(None)))
            else:
                loop(fold.shape[0], one)

        def begin():
            for fold in folds:
                for load in loads(fold):
                    load.start()
            for fetch in fetches.values():
                fetch.start()
            if moves:
                barrier = pltpu.get_barrier_semaphore()
                for axis, flip in partners:
                    pl.semaphore_signal(
                        barrier, inc=1, device_id=target(axis, flip),
                        device_id_type=pl.DeviceIdType.MESH,
                    )
                pl.semaphore_wait(barrier, len(partners))
            for k, move in enumerate(moves):
                if move.phase == 0 and move.late is None and not isinstance(move.source, Fold):
                    made(k).start()
            for number, fold in enumerate(folds):
                for load in loads(fold):
                    load.wait()
                add(fold)
                for k, move in enumerate(moves):
                    if move.source is fold:
                        made(k).start()
                keeping(number).start()
            for k, fetch in fetches.items():
                if k not in lazy:
                    fetch.wait()

        def launch(which):
            for k in range(len(moves)):
                if moves[k].late == which and moves[k].phase == 0:
                    made(k).start()

        def tick(phase):
            for k, needed in before.items():
                if needed == phase:
                    made(k).wait_recv()
            for k, move in enumerate(moves):
                if move.phase == phase:
                    made(k).start()

        def finish():
            for k, store in stores.items():
                if k not in early:
                    store.start()
            if not ticking:
                for phase in range(1, lasts + 1):
                    tick(phase)
            for k in range(len(moves)):
                made(k).wait_send()
                if k not in before:
                    made(k).wait_recv()
            for k in range(len(folds)):
                keeping(k).wait()
            for store in stores.values():
                store.wait()

        options = {}
        if any(move.late is not None for move in moves):
            options["launch"] = launch
        if ticking:
            options["tick"] = tick
        if lazy:
            options["ready"] = lambda k: fetches[k].wait()
        if early:
            options["flush"] = lambda k: stores[k].start()
        if grid is None:
            begin()
            kernel(*ins, *results, *rest, **options)
            finish()
        else:
            pl.when(pl.program_id(0) == 0)(begin)
            kernel(*ins, *results, *rest, **options)
            pl.when(pl.program_id(0) == pl.num_programs(0) - 1)(finish)

    result = pl.pallas_call(
        body_kernel,
        out_shape=list(outs)
        + [
            like(*m.shape, kind=m.dtype)
            for m in moves
        ]
        + [like(*fold.keep_shape) for fold in folds],
        in_specs=[ANY if spec is VMEM else spec for spec in specs] + [ANY] * len(sources),
        out_specs=[ANY if spec is VMEM else spec for spec in out_specs]
        + [ANY] * (len(moves) + len(folds)),
        scratch_shapes=scratch,
        compiler_params=pltpu.CompilerParams(vmem_limit_bytes=60 * 2**20, **params),
        cost_estimate=pl.CostEstimate(
            flops=int(flops),
            bytes_accessed=sum(o.size * o.dtype.itemsize for o in operands),
            transcendentals=0,
        ),
        **extra,
    )(*operands, *sources)
    end = fixed_out + len(moves)
    return list(result[:fixed_out]), list(result[fixed_out:end]), (folds, list(result[end:]))


def finale(kernel, outs, stages, results, scratch, ident):
    plan = []
    for stage in stages:
        for job, name in stage:
            moves = job.moves(name)
            folds = []
            for move in moves:
                known = folds + [fold for part, _ in plan for fold in part]
                if isinstance(move.source, Fold) and not any(move.source is one for one in known):
                    folds.append(move.source)
            job.absorb(name, moves, folds)
            plan.append((folds, moves))
    items = results()
    moves = [move for _, part in plan for move in part]
    folds = [fold for part, _ in plan for fold in part]
    sources, fetched = [], []

    def need(item):
        if not isinstance(item, (Fold, Move)) and not any(item is one for one in sources):
            sources.append(item)

    for fold in folds:
        for item in [fold.own] + fold.arrived:
            need(item)
            if not isinstance(item, (Fold, Move)):
                fetched.append((fold, item))
    for move in moves:
        need(move.source)
    plain_items = []
    for item in items:
        need(item)
        if not isinstance(item, (Fold, Move)):
            plain_items.append(item)
    partners = sorted({(move.axis, move.flip) for move in moves})
    shapes = [pltpu.VMEM(one.shape, one.dtype) for one in scratch]
    shapes += [pltpu.VMEM(move.shape, move.dtype) for move in moves]
    shapes += [pltpu.VMEM(fold.shape, fold.dtype) for fold in folds]
    shapes += [pltpu.VMEM(fold.shape, fold.dtype) for fold, _ in fetched]
    shapes += [pltpu.VMEM(item.shape, item.dtype) for item in plain_items]
    shapes += [pltpu.VMEM(one.shape, one.dtype) for one in outs]
    for number in (len(moves), len(moves), len(fetched), len(plain_items), len(outs)):
        shapes.append(pltpu.SemaphoreType.DMA((max(number, 1),)))

    def body_kernel(*refs):
        def take(count):
            nonlocal refs
            some, refs = refs[:count], refs[count:]
            return some

        sent, finals = take(len(sources)), take(len(outs))
        rest, landed, sums = take(len(scratch)), take(len(moves)), take(len(folds))
        brought, held, outer = take(len(fetched)), take(len(plain_items)), take(len(outs))
        send_sem, recv_sem, load_sem, item_sem, out_sem = refs
        arrived = set()

        def target(axis, flip):
            return {axis: flipped(lax.axis_index(axis), flip, lax.axis_size(axis))}

        def place(item):
            if isinstance(item, Fold):
                return sums[index_of(folds, item)]
            if isinstance(item, Move):
                return landed[index_of(moves, item)]
            return sent[index_of(sources, item)]

        def made(move):
            k = index_of(moves, move)
            source = place(move.source)
            return pltpu.make_async_remote_copy(
                src_ref=move.take(source),
                dst_ref=landed[k],
                send_sem=send_sem.at[k],
                recv_sem=recv_sem.at[k],
                device_id=target(move.axis, move.flip),
                device_id_type=pl.DeviceIdType.MESH,
            )

        def arrival(item):
            if isinstance(item, Move) and index_of(moves, item) not in arrived:
                arrived.add(index_of(moves, item))
                made(item).wait_recv()

        loads = [
            pltpu.make_async_copy(
                (fold.take if item is fold.own else whole)(place(item)), brought[k], load_sem.at[k]
            )
            for k, (fold, item) in enumerate(fetched)
        ]
        fetches = [
            pltpu.make_async_copy(place(item), held[k], item_sem.at[k])
            for k, item in enumerate(plain_items)
        ]
        stores = [
            pltpu.make_async_copy(outer[k], finals[k], out_sem.at[k]) for k in range(len(outs))
        ]
        for load in loads:
            load.start()
        barrier = pltpu.get_barrier_semaphore()
        for axis, flip in partners:
            pl.semaphore_signal(
                barrier, inc=1, device_id=target(axis, flip), device_id_type=pl.DeviceIdType.MESH
            )
        pl.semaphore_wait(barrier, len(partners))

        def total(fold):
            terms = []
            for item in [fold.own] + fold.arrived:
                if isinstance(item, (Fold, Move)):
                    arrival(item)
                    term = place(item)
                    if item is fold.own:
                        term = fold.take(item.keep(term) if isinstance(item, Fold) else term)
                else:
                    k = next(
                        k for k, (one, other) in enumerate(fetched) if one is fold and other is item
                    )
                    loads[k].wait()
                    term = brought[k]
                terms.append(term)
            goal = place(fold)

            def one(index):
                goal[index] = functools.reduce(
                    jnp.add, [term[index].astype(SINGLE) for term in terms]
                ).astype(goal.dtype)

            if len(fold.shape) == 2:
                one((slice(None), slice(None)))
            else:
                loop(fold.shape[0], one)

        for number, (some, part) in enumerate(plan):
            for fold in some:
                total(fold)
            for move in part:
                arrival(move.source)
                made(move).start()
            if number == 0:
                for fetch in fetches:
                    fetch.start()
        operands = []
        for item in items:
            if isinstance(item, (Fold, Move)):
                operands.append(place(item))
            else:
                operands.append(held[next(k for k, one in enumerate(plain_items) if one is item)])
        for fetch in fetches:
            fetch.wait()

        def ready(k):
            arrival(items[k])

        kernel(*operands, *outer, *rest, ready=ready, flush=lambda k: stores[k].start())
        for move in moves:
            made(move).wait_send()
            arrival(move)
        for store in stores:
            store.wait()

    return pl.pallas_call(
        body_kernel,
        out_shape=list(outs),
        in_specs=[ANY] * len(sources),
        out_specs=[ANY] * len(outs),
        scratch_shapes=shapes,
        compiler_params=pltpu.CompilerParams(
            vmem_limit_bytes=60 * 2**20, collective_id=ident, has_side_effects=True
        ),
    )(*sources)


class Courier:
    def __init__(self, active):
        self.active, self.waiting, self.ident = active, [], 0

    def load(self, *jobs):
        self.waiting += jobs

    def run(self, kernel, outs, operands, specs, scratch, flops, **extra):
        jobs, self.waiting = self.waiting, []
        moves, ends = [], []
        for job, stage, *late in jobs:
            added = job.moves(stage)
            for move in added:
                if late and not isinstance(move.source, Move):
                    move.late = late[0]
            moves += added
            ends.append(len(moves))
        if moves:
            self.ident += 1
        results, arrived, (folds, kept) = call(
            kernel, outs, operands, specs, scratch, flops, moves=tuple(moves), ident=self.ident, **extra
        )
        start = 0
        for (job, stage, *late), end in zip(jobs, ends):
            if late:
                job.tensor = results[late[0]]
            own = [
                kept[k]
                for k, fold in enumerate(folds)
                if any(move.source is fold for move in moves[start:end])
            ]
            job.absorb(stage, arrived[start:end], own)
            start = end
        return results


def in_halves(arrays):
    width = arrays[0].shape[1] // 2
    return (
        arrays[:1] + [one[:, :width] for one in arrays[1:]] + [one[:, width:] for one in arrays[1:]]
    )


def body(
    patches,
    queries,
    window_valid,
    answer_length,
    norm_gain,
    norm_bias,
    attn_in,
    attn_out,
    mlp_in,
    mlp_out,
    cot_patches,
    cot_queries,
):
    x, q, cot_x, cot_q = patches[0], queries[0], cot_patches[0], cot_queries[0]
    rows, features = x.shape
    count = q.shape[0]
    hidden = mlp_in.shape[2]
    blocks = lax.axis_size("blk")
    place = lax.axis_index("blk").astype(jnp.int32)
    share = features // blocks
    hidden_share = hidden // blocks
    share_rows = -(-share // 16) * 16
    hidden_rows = -(-hidden_share // 16) * 16
    part = -(-count // (blocks * 16)) * 16
    padded = part * blocks
    wide = 3 * features
    last = wide + features + features
    causal_columns = -(-last // 512) * 512
    valid = jnp.where(jnp.repeat(window_valid[0], WIN) > 0, 0.0, MASKED).astype(SINGLE)
    carried = blocks == DIRECT and lax.axis_size("rep") == 4 and share % 32 == 0
    courier = Courier(carried)

    def own_columns(tensor):
        return lax.dynamic_slice_in_dim(tensor, place * share, share, 1)

    square = 2.0 * features * features
    run = courier.run

    n0, pw, mw, x1, nx, vq, ckv = run(
        window_forward,
        [
            like(rows, features), like(rows, wide), like(rows, features),
            like(rows, features, kind=SINGLE), like(rows, features), like(rows, features),
            like(rows, 2 * features),
        ],
        [x, norm_gain, norm_bias, attn_in, attn_out],
        [VMEM, VMEM, VMEM, ANY, ANY],
        [((features, wide), NARROW), ((features, features), NARROW),
         ((features, features), NARROW), ((features, 2 * features), NARROW)],
        rows * square * 9,
        semaphores=4,
        early=(0, 1, 2, 3, 4, 5),
    )
    n1, pq, mq, q1, nq, cq, vkv, log_q = run(
        causal_forward,
        [
            like(count, features), like(count, wide), like(count, features),
            like(padded, features, kind=SINGLE), like(padded, features), like(count, features),
            like(count, 2 * features), like(16, count, kind=SINGLE),
        ],
        [q, norm_gain, norm_bias, attn_in, attn_out],
        [VMEM, VMEM, VMEM, ANY, ANY],
        [((features, wide), NARROW), ((features, features), NARROW),
         ((features, features), NARROW), ((features, 2 * features), NARROW),
         ((count, PAIR), SINGLE)],
        count * square * 15,
        semaphores=4,
        early=(0, 1, 2, 3, 4, 5),
    )
    outs, *log_pieces = run(
        functools.partial(cross_forward, blocks),
        [like(padded, features)] + [like(16, part, kind=SINGLE)] * blocks,
        [cq, ckv, valid[None, :]],
        [VMEM, VMEM, VMEM],
        [((padded, PAIR), SINGLE)],
        count * square * 6,
    )
    logs = Exchange(log_pieces)
    first_width = features // 3
    halves = [
        Pieces(outs, part, 0, first_width),
        Pieces(outs, part, first_width, features - first_width),
    ]
    if carried:
        courier.load((logs, ""), (halves[0], ""))
    mv, x2, log_v = run(
        reverse_forward,
        [like(rows, features), like(rows, features, kind=SINGLE), like(16, rows, kind=SINGLE)],
        [answer_length, vq, vkv, x1, attn_out],
        [SMEM, VMEM, VMEM, VMEM, ANY],
        [((features, features), NARROW), ((rows, PAIR), SINGLE)],
        rows * square * 8,
        semaphores=1,
        lazy=(3,),
        early=(0,),
    )
    if carried:
        courier.load((halves[1], ""))
    x3, dx2, up_x, down_x, norm_five = run(
        patch_feed_forward,
        [
            like(rows, features), like(rows, features, kind=SINGLE), like(features, hidden),
            like(hidden, features), like(8, features, kind=SINGLE),
        ],
        [x2, cot_x, norm_gain, norm_bias, mlp_in, mlp_out],
        [
            VMEM, VMEM, VMEM, VMEM,
            pl.BlockSpec((1, features, CHUNK), lambda j: (0, 0, j)),
            pl.BlockSpec((1, CHUNK, features), lambda j: (0, j, 0)),
        ],
        [((rows, features), NARROW), ((rows, CHUNK), NARROW), ((rows, CHUNK), NARROW),
         ((rows, features), SINGLE), ((rows, features), SINGLE)],
        rows * square * 24,
        grid=(hidden // CHUNK,),
        out_specs=[
            VMEM, VMEM,
            pl.BlockSpec((features, CHUNK), lambda j: (0, j)),
            pl.BlockSpec((CHUNK, features), lambda j: (j, 0)),
            VMEM,
        ],
    )
    if carried:
        merged = run(
            functools.partial(merge_blocks, blocks),
            [like(part, features), like(16, part, kind=SINGLE)],
            [outs] + logs.result + halves[0].result + halves[1].result,
            [VMEM] * (3 * blocks - 1),
            [],
            padded * square,
        )
        co_parts, log_parts = Spread(merged[0]), Gather(merged[1])
        up_x, down_x = Reduction(up_x), Reduction(down_x)
        reverse_weight = Reduction(like(blocks // 2, 2, 2, share // 2, 2 * features))
        courier.load(
            (co_parts, ""), (log_parts, ""), (up_x, "core"), (down_x, "core"),
            (reverse_weight, "core", 1),
        )
    else:
        whole_logs = jnp.stack(exchange(log_pieces))
        merged_log = jax.nn.logsumexp(whole_logs, axis=0)
        weights = jnp.transpose(jnp.exp(whole_logs - merged_log)[:, :HEADS], (0, 2, 1))
        shares = lax.all_to_all(outs.reshape(blocks, part, features), "blk", 0, 0)
        merged_out = jnp.sum(jnp.repeat(weights, HEAD, axis=2) * shares.astype(SINGLE), axis=0)
        co_parts, log_parts = Spread(None), Gather(None)
        co_parts.tensor, *co_parts.result = in_halves(gather(merged_out.astype(NARROW)))
        log_parts.result = gather(merged_log)
    folded = (blocks // 2, 2, 2, share // 2) if carried else (features,)
    dvq, reverse_grad, *kv_pieces = run(
        functools.partial(reverse_backward, blocks),
        [like(rows, features), like(*folded, 2 * features)]
        + [like(part, features + PAIR)] * blocks + [like(part, features - PAIR)] * blocks,
        [answer_length, dx2, mv, vq, vkv, nx, log_v, attn_out],
        [SMEM, VMEM, VMEM, VMEM, VMEM, VMEM, VMEM, ANY],
        [((features, features), NARROW), ((rows, features), NARROW), ((rows, features), NARROW),
         ((16, rows), SINGLE), ((padded, 2 * features), SINGLE)],
        rows * square * 16,
        semaphores=1,
        ticking=carried,
        lazy=(3, 4, 5, 6),
    )
    k_parts, v_parts = Exchange(kv_pieces[:blocks]), Exchange(kv_pieces[blocks:])
    if carried:
        courier.load((k_parts, ""), (up_x, "x"))
    else:
        k_parts.result, v_parts.result = exchange(k_parts.pieces), exchange(v_parts.pieces)
    q3, dq2, up_q, down_q, norm_four, co = run(
        functools.partial(query_feed_forward, blocks, share, hidden_share),
        [
            like(count, share), like(count, features, kind=SINGLE), like(share_rows, hidden),
            like(hidden_rows, features), like(8, features, kind=SINGLE), like(padded, features),
        ],
        [q1, cot_q, norm_gain, norm_bias, attn_out, mlp_in, mlp_out, co_parts.tensor]
        + co_parts.result,
        [
            VMEM, VMEM, VMEM, VMEM, pl.BlockSpec((1, features, features), lambda j: (2, 0, 0)),
            pl.BlockSpec((1, features, CHUNK), lambda j: (1, 0, j)),
            pl.BlockSpec((1, CHUNK, features), lambda j: (1, j, 0)),
        ] + [ANY] * (2 * blocks - 1),
        [((count, features), SINGLE), ((count, features), NARROW), ((share_rows, count), NARROW),
         ((count, CHUNK), NARROW), ((count, CHUNK), NARROW),
         ((count, features), SINGLE), ((count, features), SINGLE)],
        count * square * 18,
        semaphores=2 * blocks - 1,
        grid=(hidden // CHUNK,),
        out_specs=[
            VMEM, VMEM,
            pl.BlockSpec((share_rows, CHUNK), lambda j: (0, j)),
            VMEM, VMEM, VMEM,
        ],
    )
    if carried:
        up_q, down_q = Reduction(up_q, 1), Reduction(down_q, 1)
        courier.load((v_parts, ""), (down_x, "x"), (up_x, "y"), (up_q, "core"), (down_q, "core"))
    dckv, cross_out_weight, *q_pieces = run(
        functools.partial(cross_backward, blocks, share),
        [like(rows, 2 * features), like(share_rows, features)] + [like(part, features)] * blocks,
        [dq2, co, cq, ckv, valid[None, :], attn_out] + log_parts.result,
        [VMEM, VMEM, VMEM, VMEM, VMEM, ANY] + [VMEM] * blocks,
        [((features, features), NARROW), ((count, features), NARROW), ((count, features), NARROW),
         ((16, count), SINGLE), ((padded, PAIR), SINGLE), ((16, count), SINGLE),
         ((padded, features), NARROW), ((rows, 2 * features), SINGLE)],
        count * square * 12,
        semaphores=1,
        lazy=(2, 3),
    )
    q_parts = Exchange(q_pieces)
    if carried:
        kv_weight = Reduction(like(blocks // 2, 2, 2, share // 2, 2 * features))
        window_weight = Reduction(like(blocks // 2, 2, 2, share // 2, 4 * features))
        courier.load(
            (q_parts, ""), (down_x, "y"), (reverse_weight, "x"), (up_q, "x"), (down_q, "x"),
            (kv_weight, "core", 0), (window_weight, "core", 1),
        )
    else:
        q_parts.result = exchange(q_pieces)
    kv_grad, window_grad, grad_x, norm_x = run(
        patch_backward,
        [
            like(*folded, 2 * features), like(*folded, 4 * features),
            like(rows, features, kind=SINGLE), like(8, features, kind=SINGLE),
        ],
        [x, dx2, x1, nx, n0, pw, mw, dvq, dckv, norm_gain, attn_in, attn_out],
        [VMEM] * 10 + [ANY, ANY],
        [((features, wide), NARROW), ((features, features), NARROW),
         ((features, features), NARROW), ((features, 2 * features), NARROW),
         ((rows, features), SINGLE), ((rows, features), NARROW), ((rows, features), NARROW),
         ((16, rows), SINGLE), ((rows, wide), NARROW)],
        rows * square * 24,
        semaphores=4,
        lazy=(0, 4, 5, 6),
        early=(0, 1),
    )
    if carried:
        share_weight = Reduction(like(blocks // 2, 2, 2, share // 2, wide))
        dq1_parts = Spread(like(part, features))
        courier.load(
            (share_weight, "core", 1), (dq1_parts, "", 0), (window_weight, "x"),
            (reverse_weight, "y"), (up_q, "back_x"), (down_q, "back_x"),
        )
    dq1_share, share_grad, norm_two = run(
        functools.partial(share_backward, blocks),
        [like(part, features), like(*folded, wide), like(8, features, kind=SINGLE)],
        [q1, nq, norm_gain, attn_in]
        + q_parts.result + k_parts.result + v_parts.result,
        [ANY, ANY, VMEM, ANY] + [VMEM] * (3 * blocks),
        [((features, features), NARROW), ((features, 2 * features), NARROW),
         ((part, wide), NARROW), ((part, features), SINGLE), ((part, features), NARROW)],
        part * square * 6,
        semaphores=4,
    )
    if carried:
        courier.load(
            (window_weight, "y"), (share_weight, "x"), (kv_weight, "y"), (down_x, "z"),
            (reverse_weight, "z"), (up_q, "back_core"), (down_q, "back_core"), (up_x, "z"),
        )
    else:
        dq1_parts = Spread(None)
        dq1_parts.tensor, *dq1_parts.result = in_halves(gather(dq1_share))
    causal_weight, grad_q, norms = run(
        functools.partial(causal_backward, blocks, share),
        [
            like(share_rows, causal_columns), like(count, share, kind=SINGLE),
            like(blocks, 16, -(-share // PAIR) * PAIR, kind=SINGLE)
            if carried
            else like(16, features, kind=SINGLE),
        ],
        [q, dq2, n1, pq, mq, log_q, cross_out_weight, norm_gain]
        + [norm_x, norm_two, norm_four, norm_five, attn_in, attn_out, dq1_parts.tensor]
        + dq1_parts.result,
        [VMEM] * 12 + [ANY] * (2 * blocks + 1),
        [((features, wide), NARROW), ((features, features), NARROW), ((padded, features), NARROW),
         ((count, features), SINGLE), ((count, features), NARROW), ((count, features), NARROW),
         ((16, count), SINGLE), ((count, 2 * PAIR), SINGLE), ((count, wide), NARROW),
         ((8, features), SINGLE), ((16, features), SINGLE)],
        count * square * 16,
        semaphores=2 * blocks + 1,
        lazy=(2, 3, 4, 5),
    )
    rest = (
        x3[None],
        q3[None],
        grad_x[None],
        grad_q[None],
    )
    if carried:
        norms = Norms(norms)
        causal_weight = Reduction(causal_weight, 1)
        sums = [
            up_x, down_x, reverse_weight, window_weight, kv_weight, share_weight, up_q, down_q,
            causal_weight,
        ]
        grads = finale(
            functools.partial(assemble, len(sums), blocks),
            [
                like(4, share, wide), like(4, share, features), like(2, share, hidden),
                like(2, hidden_share, features),
                like(6, share, kind=SINGLE), like(6, share, kind=SINGLE),
            ],
            [
                [
                    (causal_weight, "core"), (norms, "out"), (kv_weight, "x"), (share_weight, "y"),
                    (window_weight, "z"), (up_x, "back_x"), (down_x, "back_x"),
                    (reverse_weight, "back_x"),
                ],
                [
                    (causal_weight, "x"), (norms, "back"), (kv_weight, "z"), (share_weight, "z"),
                    (up_x, "back_core"), (down_x, "back_core"), (reverse_weight, "back_core"),
                    (window_weight, "back_x"),
                ],
                [
                    (causal_weight, "back_x"), (kv_weight, "back_x"), (share_weight, "back_x"),
                    (window_weight, "back_core"),
                ],
                [
                    (causal_weight, "back_core"), (kv_weight, "back_core"),
                    (share_weight, "back_core"),
                ],
            ],
            lambda: sum([one.result for one in sums], []) + norms.result,
            [like(share, 4 * features), like(share, causal_columns)],
            courier.ident + 1,
        )
        return rest + (grads[4], grads[5]) + tuple(one.astype(SINGLE) for one in grads[:4])
    up_x, down_x, reverse_weight, window_weight, kv_weight, share_weight = (
        reduce_all(one) for one in (up_x, down_x, reverse_grad, window_grad, kv_grad, share_grad)
    )
    up_q, down_q = reduce_rep(up_q[:share]), reduce_rep(down_q[:hidden_share])
    causal_weight = reduce_rep(causal_weight[:share])
    norms = own_columns(lax.psum(norms, ("blk", "rep")))
    gains, biases = norms[:6], norms[8:14]
    grad_attn_in = jnp.stack(
        (
            window_weight[:, :wide],
            causal_weight[:, :wide],
            jnp.concatenate((share_weight[:, :features], kv_weight), axis=1),
            jnp.concatenate((reverse_weight[:, :features], share_weight[:, features:]), axis=1),
        )
    )
    grad_attn_out = jnp.stack(
        (
            window_weight[:, wide:],
            causal_weight[:, wide : wide + features],
            causal_weight[:, wide + features : last],
            reverse_weight[:, features:],
        )
    )
    return rest + (
        gains,
        biases,
        grad_attn_in.astype(SINGLE),
        grad_attn_out.astype(SINGLE),
        jnp.stack((up_x, up_q)).astype(SINGLE),
        jnp.stack((down_x, down_q)).astype(SINGLE),
    )


def solution(mesh):
    placed = (
        P("rep", "blk", None),
        P("rep", None, None),
        P("rep", "blk"),
        P("rep"),
        P(),
        P(),
        P(),
        P(),
        P(),
        P(),
        P("rep", "blk", None),
        P("rep", None, None),
    )
    return jax.shard_map(
        body,
        mesh=mesh,
        in_specs=placed,
        out_specs=(
            P("rep", "blk", None),
            P("rep", None, "blk"),
            P("rep", "blk", None),
            P("rep", None, "blk"),
            P(None, "blk"),
            P(None, "blk"),
            P(None, "blk", None),
            P(None, "blk", None),
            P(None, "blk", None),
            P(None, "blk", None),
        ),
        check_vma=False,
    )
```
